32 devices in a mesh: section: 2 (over x), tm: 4 (over y, core), mp: 4 (over z).
Axes of the slice: x: 2, y: 2, z: 4, core: 2. Of those that a mesh axis runs over, the one named last changes fastest.
Arguments:
- frame_len: int32 [4], replicated, may hold values from 64 to 256, as said below
- slot_utt: int32 [8], replicated, may hold values from -1 to 3, as said below
- enc_in: bfloat16 [256, 4, 1280], P(('section', 'tm')), may hold values from -42 to 42
- ffn_up: bfloat16 [1280, 5120], P(None, 'mp'), may hold values from -0.15625 to 0.15625
- ffn_down: bfloat16 [5120, 1280], P('mp'), may hold values from -0.078125 to 0.078125
- kv_proj: bfloat16 [1280, 1024], replicated, may hold values from -10 to 10
- hyp_state: bfloat16 [8, 8, 16, 4096], P('tm'), may hold values from -37 to 37
- hyp_tok: int32 [8, 8, 16], P('tm'), may hold values from 0 to 63999
- hyp_len: int32 [8, 8], P('tm'), may hold values from 1 to 16
- q_proj: bfloat16 [4096, 4096], P(None, ('section', 'mp')), may hold values from -0.75 to 0.75
- o_proj: bfloat16 [4096, 4096], P(('section', 'mp')), may hold values from -1 to 1
- head: bfloat16 [64000, 4096], P(('section', 'tm', 'mp')), may hold values from -45 to 45
Outputs:
- hyp_scores: float32 [8, 8], P('tm')
The draws below stay inside these ranges and needn't reach their ends.
Inputs may be any that keep to these rules, and one draw needn't show every extreme that they name: `frame_len`: one utterance in every draw has all 256 frames. `slot_utt`: every one of the 4 utterances sits in exactly one slot; slots g * 2 to (g + 1) * 2 - 1 belong to group g, and at least one group has all 2 slots filled.
All inputs are finite; a program needn't handle non-finite values.
Results may differ from the reference program's by a relative error of at most 0.005.
The reference program's roundings to bfloat16 on the way count: a program that leaves them out, or rounds other values in their place, can miss the bound.
Values may be sent and summed in bfloat16 or wider, within the bound.
No kernel may reach another device: no remote copies, remote signals or barrier semaphores. Data moves between devices by JAX's collectives and lax.ppermute only.
A program may use at most 128 MiB of HBM per device.

```python
import math
import jax
import jax.numpy as jnp
import numpy as np
from jax import lax

D = 4096
NH = 32
KVH = 4
HD = 128
V = 64000
DE = 1280
EFF = 5120
HYP = 8
HLEN = 16
UMAX = 2
U = 4
SLOTS = 8
FRAMES = 256


def log_scales(key, count, low, high):
    return jnp.exp(jax.random.uniform(key, (count,), jnp.float32, math.log(low), math.log(high)))


def draw_frame_len(key, part):
    keys = jax.random.split(jax.random.fold_in(key, 11), 2)
    lengths = jax.random.randint(keys[0], (U,), FRAMES // 4, FRAMES + 1)
    longest = jax.random.randint(keys[1], (), 0, U)
    return jnp.where(jnp.arange(U) == longest, FRAMES, lengths).astype(jnp.int32)


def draw_slot_utt(key, part):
    keys = jax.random.split(jax.random.fold_in(key, 23), 3)
    priority = jax.random.permutation(keys[0], SLOTS)
    filled = jax.random.randint(keys[1], (), 0, SLOTS // UMAX)
    slot_ids = jnp.arange(SLOTS)
    priority = jnp.where(slot_ids // UMAX == filled, -1 - slot_ids % UMAX, priority)
    ranking = jnp.argsort(jnp.argsort(priority, stable=True), stable=True)
    ordering = jax.random.permutation(keys[2], U)
    return jnp.where(ranking < U, ordering[jnp.minimum(ranking, U - 1)], -1).astype(jnp.int32)


def draw_enc_in(key, part):
    keys = jax.random.split(jax.random.fold_in(key, 101), 3)
    row_scale = log_scales(keys[0], FRAMES * U, 1.0, 3.2).reshape(FRAMES, U, 1)
    col_scale = log_scales(keys[1], DE, 1.0, 3.2)
    base = jnp.clip(jax.random.normal(keys[2], (FRAMES, U, DE), jnp.float32), -4.0, 4.0)
    return (base * row_scale * col_scale).astype(jnp.bfloat16)


def draw_hyp_state(key, part):
    keys = jax.random.split(jax.random.fold_in(key, 131), 3)
    row_scale = log_scales(keys[0], SLOTS * HYP * HLEN, 0.3, 3.0).reshape(SLOTS, HYP, HLEN, 1)
    col_scale = log_scales(keys[1], D, 0.3, 3.0)
    base = jnp.clip(jax.random.normal(keys[2], (SLOTS, HYP, HLEN, D), jnp.float32), -4.0, 4.0)
    return (base * row_scale * col_scale).astype(jnp.bfloat16)


def draw_kv_proj(key, part):
    keys = jax.random.split(jax.random.fold_in(key, 151), 1)
    columns = 2 * KVH * HD
    base = jnp.clip(jax.random.normal(keys[0], (DE, columns), jnp.float32), -4.0, 4.0)
    return (base / math.sqrt(DE)).astype(jnp.bfloat16)


def draw_head(key, part):
    keys = jax.random.split(jax.random.fold_in(key, 171), 1)
    scale = 3.5 / math.sqrt(D)
    base = jnp.clip(jax.random.normal(keys[0], (V, D), jnp.float32), -4.0, 4.0)
    return (base * scale).astype(jnp.bfloat16)


def with_ends(entries, own_key, least, top_value):
    spot = [jax.random.randint(jax.random.fold_in(own_key, axis), (), 0, length) for axis, length in enumerate(entries.shape)]
    main_axis = entries.shape.index(max(entries.shape))
    next_to = spot[:main_axis] + [(spot[main_axis] + 1) % entries.shape[main_axis]] + spot[main_axis + 1:]
    return entries.at[tuple(spot)].set(least).at[tuple(next_to)].set(top_value)


def level_of(rng, extent, pieces, low, largest):
    def one(dim, blocks):
        draws = jax.random.uniform(jax.random.fold_in(jax.random.fold_in(rng, 6), dim), (blocks,), jnp.float32, low / len(pieces), largest / len(pieces))
        return jnp.repeat(jnp.exp(draws), extent[dim] // blocks).reshape((-1,) + (1,) * (len(extent) - dim - 1))

    gain = one(*pieces[0])
    for cut in pieces[1:]:
        gain = gain * one(*cut)
    return gain


def rank_bounds(count, lean):
    weights = [(1 << 20) // math.isqrt(grade ** lean) + 1 for grade in range(1, count + 1)]
    width = 1 + sum(weights) // (1 << 30)
    return np.cumsum(np.array([max(1, weight // width) for weight in weights]))


def ranked_ids(own_key, shape, count, lean):
    listing = rank_bounds(count, lean)
    pick = jax.random.randint(jax.random.fold_in(own_key, 1), shape, 0, int(listing[count - 1]))
    rank = jnp.searchsorted(jnp.asarray(listing, jnp.int32), pick, side="right")
    return jax.random.permutation(jax.random.fold_in(own_key, 2), count)[rank].astype(jnp.int32)


def centred(own_key, extent, deviation, limit, cuts=(), held_as=jnp.bfloat16):
    values = jax.random.normal(own_key, extent, jnp.float32) * deviation
    if len(cuts) > 0:
        values = level_of(own_key, extent, cuts, -0.22, 0.18) * values
    return jnp.clip(values, min=-limit, max=limit).astype(held_as)


def setup_inputs(seed: int = 0) -> dict:
    seeds = jax.random.split(jax.random.key(seed), 13)
    frame_len = draw_frame_len(jax.random.fold_in(seeds[12], 71), 0)
    slot_utt = draw_slot_utt(jax.random.fold_in(seeds[12], 71), 0)
    enc_in = draw_enc_in(jax.random.fold_in(seeds[12], 71), 0)
    ffn_up = centred(seeds[3], (DE, EFF), DE ** -0.5, 0.15625, ((1, 4),))
    ffn_down = centred(seeds[4], (EFF, DE), EFF ** -0.5, 0.078125, ((0, 4),))
    kv_proj = draw_kv_proj(jax.random.fold_in(seeds[12], 71), 0)
    hyp_state = draw_hyp_state(jax.random.fold_in(seeds[12], 71), 0)
    hyp_tok = with_ends(ranked_ids(seeds[7], (SLOTS, HYP, HLEN), V, 2), jax.random.fold_in(seeds[7], 3), 0, V - 1).astype(jnp.int32)
    hyp_len = with_ends(jax.random.randint(seeds[8], (SLOTS, HYP), 1, HLEN + 1), jax.random.fold_in(seeds[8], 1), 1, HLEN).astype(jnp.int32)
    q_proj = centred(seeds[9], (D, NH * HD), 0.047, 0.75, ((1, 8),))
    o_proj = centred(seeds[10], (NH * HD, D), 0.0625, 1.0, ((0, 8),))
    head = draw_head(jax.random.fold_in(seeds[12], 71), 0)
    return {"frame_len": frame_len, "slot_utt": slot_utt, "enc_in": enc_in, "ffn_up": ffn_up, "ffn_down": ffn_down, "kv_proj": kv_proj, "hyp_state": hyp_state, "hyp_tok": hyp_tok, "hyp_len": hyp_len, "q_proj": q_proj, "o_proj": o_proj, "head": head}


def layer_norm(values):
    center = values - lax.optimization_barrier(jnp.mean(values, axis=-1, keepdims=True))
    spread = lax.optimization_barrier(jnp.mean(center * center, axis=-1, keepdims=True))
    return center * lax.rsqrt(spread + 1e-05)

def square_norm(values):
    return values * lax.rsqrt(lax.optimization_barrier(jnp.mean(values * values, axis=-1, keepdims=True)) + 1e-06)

def rounded(values):
    return lax.optimization_barrier(values.astype(jnp.bfloat16))

def reference(frame_len, slot_utt, enc_in, ffn_up, ffn_down, kv_proj, hyp_state, hyp_tok, hyp_len, q_proj, o_proj, head):
    enc_flat = enc_in.reshape(FRAMES * U, DE)
    enc_normed = layer_norm(enc_flat.astype(jnp.float32)).astype(jnp.bfloat16)
    enc_inner = jax.nn.gelu(jnp.dot(enc_normed, ffn_up, preferred_element_type=jnp.float32), approximate=False).astype(jnp.bfloat16)
    enc_mid = enc_flat.astype(jnp.float32) + jnp.dot(enc_inner, ffn_down, preferred_element_type=jnp.float32)
    enc_states = layer_norm(enc_mid).astype(jnp.bfloat16)
    keys_values = jnp.dot(enc_states, kv_proj, preferred_element_type=jnp.float32).astype(jnp.bfloat16)
    keys_values = keys_values.reshape(FRAMES, U, 2, KVH, HD)
    group_heads = NH // KVH

    def one_slot(inputs):
        states, tokens, lengths, utterance = inputs
        chosen = jnp.maximum(utterance, 0).astype(jnp.int32)
        slot_kv = lax.dynamic_index_in_dim(keys_values, chosen, 1, keepdims=False).astype(jnp.float32)
        dec_rows = states.reshape(HYP * HLEN, D).astype(jnp.float32)
        queries = rounded(jnp.dot(square_norm(dec_rows).astype(jnp.bfloat16), q_proj, preferred_element_type=jnp.float32))
        queries = queries.astype(jnp.float32).reshape(HYP * HLEN, KVH, group_heads, HD)
        scores = jnp.einsum('qkgd,fkd->kgqf', queries, slot_kv[:, 0]) / math.sqrt(HD)
        visible = jnp.arange(FRAMES, dtype=jnp.int32) < frame_len[chosen]
        scores = jnp.where(visible[None, None, None, :], scores, -jnp.inf)
        weights = rounded(jax.nn.softmax(scores, axis=-1)).astype(jnp.float32)
        context = rounded(jnp.einsum('kgqf,fkd->qkgd', weights, slot_kv[:, 1])).reshape(HYP * HLEN, NH * HD)
        resid = dec_rows + jnp.dot(context, o_proj, preferred_element_type=jnp.float32)
        out_normed = square_norm(resid).astype(jnp.bfloat16)
        logits = jnp.dot(out_normed, head.T, preferred_element_type=jnp.float32)
        picked = jnp.take_along_axis(logits, tokens.reshape(HYP * HLEN, 1).astype(jnp.int32), axis=1)[:, 0]
        token_logp = (picked - jax.scipy.special.logsumexp(logits, axis=1)).reshape(HYP, HLEN)
        valid = jnp.arange(HLEN, dtype=jnp.int32)[None, :] < lengths[:, None]
        summed = lax.optimization_barrier(jnp.sum(jnp.where(valid, token_logp, 0.0), axis=-1)) / lengths.astype(jnp.float32) + math.log(V)
        return jnp.where(utterance >= 0, summed, jnp.zeros_like(summed))
    return lax.map(one_slot, (hyp_state, hyp_tok, hyp_len, slot_utt))
```

```python
import math

import jax
import jax.numpy as jnp
from jax import lax
from jax.sharding import PartitionSpec as P

NH = 32
KVH = 4
HD = 128
V = 64000
ALL = ("section", "tm", "mp")


def layer_norm(values):
    center = values - jnp.mean(values, axis=-1, keepdims=True)
    spread = jnp.mean(center * center, axis=-1, keepdims=True)
    return center * lax.rsqrt(spread + 1e-05)


def square_norm(values):
    return values * lax.rsqrt(jnp.mean(values * values, axis=-1, keepdims=True) + 1e-06)


def exchange(blocks, axis):
    return lax.all_to_all(blocks, axis, split_axis=0, concat_axis=0, tiled=True)


def scatter_sum(partial, axis, count):
    blocks = partial.reshape((count, partial.shape[0] // count) + partial.shape[1:])
    return jnp.sum(exchange(blocks, axis).astype(jnp.float32), axis=0)


def per_device(
    frame_len,
    slot_utt,
    enc_in,
    ffn_up,
    ffn_down,
    kv_proj,
    hyp_state,
    hyp_tok,
    hyp_len,
    q_proj,
    o_proj,
    head,
):
    section_count = lax.axis_size("section")
    group_count = lax.axis_size("tm")
    width_count = lax.axis_size("mp")
    section_pos = lax.axis_index("section")
    group_pos = lax.axis_index("tm")
    width_pos = lax.axis_index("mp")
    head_devices = section_count * width_count
    head_pos = section_pos * width_count + width_pos
    all_devices = head_devices * group_count

    frame_rows, utterances, enc_width = enc_in.shape
    assert utterances == group_count
    slot_count, hyp_count, positions, model_width = hyp_state.shape
    slot_tokens = hyp_count * positions
    device_heads = q_proj.shape[1] // HD
    group_heads = NH // KVH
    frame_share = frame_rows // width_count
    share_rows = slot_tokens // head_devices
    here_slots = lax.dynamic_slice_in_dim(slot_utt, group_pos * slot_count, slot_count, 0)

    dec_rows = hyp_state.reshape(slot_count * slot_tokens, model_width).astype(jnp.float32)
    queries = jnp.dot(
        square_norm(dec_rows).astype(jnp.bfloat16), q_proj, preferred_element_type=jnp.float32
    ).astype(jnp.bfloat16)
    queries = queries.reshape(slot_count, slot_tokens, device_heads * HD)
    shares = lax.dynamic_slice_in_dim(
        hyp_state.reshape(slot_count, slot_tokens, model_width), head_pos * share_rows, share_rows, 1
    )

    def by_utterance(values):
        out = []
        for utterance in range(utterances):
            block = values[0]
            for slot in range(1, slot_count):
                block = jnp.where(here_slots[slot] == utterance, values[slot], block)
            out.append(block)
        return jnp.stack(out)

    own_slot = jnp.argmax(slot_utt == group_pos)
    from_group = own_slot // slot_count
    queries = lax.dynamic_index_in_dim(
        exchange(by_utterance(queries), "tm"), from_group, 0, keepdims=False
    )
    resid_rows = lax.dynamic_index_in_dim(
        exchange(by_utterance(shares), "tm"), from_group, 0, keepdims=False
    )
    slot_targets = lax.all_gather(
        hyp_tok.reshape(slot_count, slot_tokens), "tm", axis=0, tiled=True
    )
    utt_slots = jnp.argmax(slot_utt[None, :] == jnp.arange(utterances)[:, None], axis=1)
    targets = jnp.take(slot_targets, utt_slots, axis=0).reshape(utterances * slot_tokens)

    enc_flat = (
        enc_in.reshape(width_count, frame_share, utterances, enc_width)
        .transpose(0, 2, 1, 3)
        .reshape(frame_rows * utterances, enc_width)
    )
    share_count = frame_share * utterances
    enc_normed = layer_norm(enc_flat.astype(jnp.float32)).astype(jnp.bfloat16)
    enc_inner = jax.nn.gelu(
        jnp.dot(enc_normed, ffn_up, preferred_element_type=jnp.float32), approximate=False
    ).astype(jnp.bfloat16)
    enc_summed = scatter_sum(
        jnp.dot(enc_inner, ffn_down, preferred_element_type=jnp.float32).astype(jnp.bfloat16),
        "mp",
        width_count,
    )
    own_frames = lax.dynamic_slice_in_dim(enc_flat, width_pos * share_count, share_count, 0)
    enc_states = layer_norm(own_frames.astype(jnp.float32) + enc_summed).astype(jnp.bfloat16)
    keys_values = jnp.dot(enc_states, kv_proj, preferred_element_type=jnp.float32).astype(
        jnp.bfloat16
    )
    keys_values = keys_values.reshape(utterances, frame_share, 2, KVH, HD)
    sent = []
    for section in range(section_count):
        per_width = []
        for width in range(width_count):
            kv_head = (section * width_count + width) * device_heads // group_heads
            per_width.append(
                keys_values[:, :, :, kv_head].reshape(utterances, frame_share, 2 * HD)
            )
        sent.append(jnp.stack(per_width, axis=1))
    sent = jnp.stack(sent).reshape(all_devices, frame_share, 2 * HD)
    frames_all = all_devices * frame_share
    keys_values = exchange(sent, ALL).reshape(frames_all, 2 * HD)

    frame_limit = lax.dynamic_index_in_dim(frame_len, group_pos, 0, keepdims=False)
    queries = queries.reshape(slot_tokens, device_heads, HD)
    scores = jnp.einsum(
        "qhd,fd->hqf", queries, keys_values[:, :HD], preferred_element_type=jnp.float32
    ) / math.sqrt(HD)
    visible = jnp.arange(frames_all, dtype=jnp.int32) < frame_limit
    scores = jnp.where(visible[None, None, :], scores, -jnp.inf)
    weights = jax.nn.softmax(scores, axis=-1).astype(jnp.bfloat16)
    context = jnp.einsum(
        "hqf,fd->qhd", weights, keys_values[:, HD:], preferred_element_type=jnp.float32
    ).astype(jnp.bfloat16)
    partial = jnp.dot(
        context.reshape(slot_tokens, device_heads * HD), o_proj, preferred_element_type=jnp.float32
    ).astype(jnp.bfloat16)
    partial = scatter_sum(partial, "section", section_count).astype(jnp.bfloat16)
    attn_out = scatter_sum(partial, "mp", width_count)
    out_normed = square_norm(resid_rows.astype(jnp.float32) + attn_out).astype(jnp.bfloat16)

    hidden_rows = lax.all_gather(out_normed, ALL, axis=0, tiled=True)
    logits = lax.dot_general(
        hidden_rows, head, (((1,), (1,)), ((), ())), preferred_element_type=jnp.float32
    )
    vocab_rows = head.shape[0]
    vocab_start = (
        (section_pos * group_count + group_pos) * width_count + width_pos
    ) * vocab_rows
    target_rows = (
        targets.reshape(utterances, section_count, width_count, share_rows)
        .transpose(1, 0, 2, 3)
        .reshape(-1)
    )
    upper = jnp.max(logits, axis=1)
    totals = jnp.sum(jnp.exp(logits - upper[:, None]), axis=1)
    matches = (
        jnp.arange(vocab_rows, dtype=jnp.int32)[None, :] == (target_rows - vocab_start)[:, None]
    )
    target_logit = jnp.sum(jnp.where(matches, logits, 0.0), axis=1)

    stats = jnp.stack([upper, totals, target_logit])
    stats = stats.reshape(3, section_count, utterances, width_count, share_rows)
    stats = stats.transpose(2, 0, 1, 3, 4).reshape(utterances, 3, slot_tokens)
    by_slot = jnp.take(stats, jnp.maximum(slot_utt, 0), axis=0)
    by_group = by_slot.reshape(1, group_count, 1, slot_count, 3, slot_tokens)
    by_group = jnp.broadcast_to(
        by_group, (section_count, group_count, width_count, slot_count, 3, slot_tokens)
    ).reshape(all_devices, slot_count, 3, slot_tokens)
    every = exchange(by_group, ALL)
    peak = jnp.max(every[:, :, 0], axis=0)
    total = jnp.sum(every[:, :, 1] * jnp.exp(every[:, :, 0] - peak[None]), axis=0)
    picked = jnp.sum(every[:, :, 2], axis=0)
    token_logp = (picked - (peak + jnp.log(total))).reshape(slot_count, hyp_count, positions)
    valid = jnp.arange(positions, dtype=jnp.int32)[None, None, :] < hyp_len[:, :, None]
    summed = jnp.sum(jnp.where(valid, token_logp, 0.0), axis=-1) / hyp_len.astype(
        jnp.float32
    ) + math.log(V)
    return jnp.where(here_slots[:, None] >= 0, summed, 0.0)


def solution(mesh):
    in_specs = (
        P(),
        P(),
        P(("section", "tm"), None, None),
        P(None, "mp"),
        P("mp", None),
        P(),
        P("tm", None, None, None),
        P("tm", None, None),
        P("tm", None),
        P(None, ("section", "mp")),
        P(("section", "mp"), None),
        P(("section", "tm", "mp"), None),
    )
    out_specs = P("tm", None)
    return jax.shard_map(
        per_device, mesh=mesh, in_specs=in_specs, out_specs=out_specs, check_vma=False
    )
```

```python
import math

import jax
import jax.numpy as jnp
from jax import lax
from jax.sharding import PartitionSpec as P

NH = 32
KVH = 4
HD = 128
V = 64000
ALL = ("section", "tm", "mp")


def layer_norm(values):
    center = values - jnp.mean(values, axis=-1, keepdims=True)
    spread = jnp.mean(center * center, axis=-1, keepdims=True)
    return center * lax.rsqrt(spread + 1e-05)


def square_norm(values):
    return values * lax.rsqrt(jnp.mean(values * values, axis=-1, keepdims=True) + 1e-06)


def exchange(blocks, axis):
    return lax.all_to_all(blocks, axis, split_axis=0, concat_axis=0, tiled=True)


def swap(values, axis, distance):
    pairs = [(i, i ^ distance) for i in range(lax.axis_size(axis))]
    return lax.ppermute(values, axis, pairs)


def scatter_sum(partial, axis):
    count = lax.axis_size(axis)
    pos = lax.axis_index(axis)
    rows = partial.shape[0] // count
    total = None
    for distance in range(count - 1, -1, -1):
        block = lax.dynamic_slice_in_dim(partial, (pos ^ distance) * rows, rows, 0)
        if distance:
            block = swap(block, axis, distance)
        block = block.astype(jnp.float32)
        total = block if total is None else total + block
    return total


def gather_blocks(block, axis):
    blocks = [block]
    for distance in range(1, lax.axis_size(axis)):
        blocks.append(swap(block, axis, distance))
    return jnp.concatenate(blocks, axis=0)


def per_device(
    frame_len,
    slot_utt,
    enc_in,
    ffn_up,
    ffn_down,
    kv_proj,
    hyp_state,
    hyp_tok,
    hyp_len,
    q_proj,
    o_proj,
    head,
):
    section_count = lax.axis_size("section")
    group_count = lax.axis_size("tm")
    width_count = lax.axis_size("mp")
    section_pos = lax.axis_index("section")
    group_pos = lax.axis_index("tm")
    width_pos = lax.axis_index("mp")
    head_devices = section_count * width_count
    head_pos = section_pos * width_count + width_pos
    all_devices = head_devices * group_count

    frame_rows, utterances, enc_width = enc_in.shape
    assert utterances == group_count
    slot_count, hyp_count, positions, model_width = hyp_state.shape
    slot_tokens = hyp_count * positions
    device_heads = q_proj.shape[1] // HD
    group_heads = NH // KVH
    frame_share = frame_rows // width_count
    share_rows = slot_tokens // head_devices
    pieces = 2
    piece_rows = share_rows // pieces
    here_slots = lax.dynamic_slice_in_dim(slot_utt, group_pos * slot_count, slot_count, 0)

    dec_rows = hyp_state.reshape(slot_count * slot_tokens, model_width).astype(jnp.float32)
    queries = jnp.dot(
        square_norm(dec_rows).astype(jnp.bfloat16), q_proj, preferred_element_type=jnp.float32
    ).astype(jnp.bfloat16)
    queries = queries.reshape(slot_count, slot_tokens, device_heads * HD)
    shares = lax.dynamic_slice(
        hyp_state.reshape(
            slot_count, section_count, pieces, width_count, piece_rows, model_width
        ),
        (0, section_pos, 0, width_pos, 0, 0),
        (slot_count, 1, pieces, 1, piece_rows, model_width),
    ).reshape(slot_count, share_rows, model_width)

    def by_utterance(values):
        out = []
        for utterance in range(utterances):
            block = values[0]
            for slot in range(1, slot_count):
                block = jnp.where(here_slots[slot] == utterance, values[slot], block)
            out.append(block)
        return jnp.stack(out)

    own_slot = jnp.argmax(slot_utt == group_pos)
    from_group = own_slot // slot_count

    def from_owner(values):
        blocks = by_utterance(values)
        got = lax.dynamic_index_in_dim(blocks, group_pos, 0, keepdims=False)
        for distance in range(1, group_count):
            other = group_pos ^ distance
            sent = lax.dynamic_index_in_dim(blocks, other, 0, keepdims=False)
            got = jnp.where(from_group == other, swap(sent, "tm", distance), got)
        return got

    queries = from_owner(queries)
    resid_rows = from_owner(shares)
    slot_targets = gather_blocks(hyp_tok.reshape(slot_count, slot_tokens), "tm")
    slot_targets = slot_targets.reshape(-1)

    token_count = utterances * slot_tokens
    near_order = section_count == 2 and group_count == 4
    here = ((section_pos * group_count + group_pos) * width_count + width_pos) * share_rows
    here = here if near_order else 0

    def rows_of(section, utterance, width, row):
        return ((section * group_count + utterance) * width_count + width) * share_rows + row

    places = jnp.arange(token_count, dtype=jnp.int32) ^ here
    place_row = places % share_rows
    place_width = places // share_rows % width_count
    place_utt = places // (share_rows * width_count) % group_count
    place_section = places // (share_rows * width_count * group_count)
    place_token = (
        (place_section * pieces + place_row // piece_rows) * width_count + place_width
    ) * piece_rows + place_row % piece_rows
    utt_slots = jnp.argmax(slot_utt[None, :] == jnp.arange(utterances)[:, None], axis=1)
    place_slot = jnp.zeros_like(places)
    for utterance in range(utterances):
        place_slot = jnp.where(place_utt == utterance, utt_slots[utterance], place_slot)
    place_slot = place_slot ^ (group_pos * slot_count)
    targets = jnp.take(slot_targets, place_slot * slot_tokens + place_token, axis=0)

    enc_flat = (
        enc_in.reshape(width_count, frame_share, utterances, enc_width)
        .transpose(0, 2, 1, 3)
        .reshape(frame_rows * utterances, enc_width)
    )
    share_count = frame_share * utterances
    enc_normed = layer_norm(enc_flat.astype(jnp.float32)).astype(jnp.bfloat16)
    enc_inner = jax.nn.gelu(
        jnp.dot(enc_normed, ffn_up, preferred_element_type=jnp.float32), approximate=False
    ).astype(jnp.bfloat16)
    enc_summed = scatter_sum(
        jnp.dot(enc_inner, ffn_down, preferred_element_type=jnp.float32).astype(jnp.bfloat16),
        "mp",
    )
    own_frames = lax.dynamic_slice_in_dim(enc_flat, width_pos * share_count, share_count, 0)
    enc_states = layer_norm(own_frames.astype(jnp.float32) + enc_summed).astype(jnp.bfloat16)
    keys_values = jnp.dot(enc_states, kv_proj, preferred_element_type=jnp.float32).astype(
        jnp.bfloat16
    )
    keys_values = keys_values.reshape(utterances, frame_share, 2, KVH, HD)
    sent = []
    for section in range(section_count):
        per_width = []
        for width in range(width_count):
            kv_head = (section * width_count + width) * device_heads // group_heads
            per_width.append(
                keys_values[:, :, :, kv_head].reshape(utterances, frame_share, 2 * HD)
            )
        sent.append(jnp.stack(per_width, axis=1))
    sent = jnp.stack(sent).reshape(all_devices, frame_share, 2 * HD)
    frames_all = all_devices * frame_share
    keys_values = exchange(sent, ALL).reshape(frames_all, 2 * HD)

    frame_limit = lax.dynamic_index_in_dim(frame_len, group_pos, 0, keepdims=False)
    queries = queries.reshape(slot_tokens, device_heads, HD)
    scores = jnp.einsum(
        "qhd,fd->hqf", queries, keys_values[:, :HD], preferred_element_type=jnp.float32
    ) / math.sqrt(HD)
    visible = jnp.arange(frames_all, dtype=jnp.int32) < frame_limit
    scores = jnp.where(visible[None, None, :], scores, -jnp.inf)
    weights = jax.nn.softmax(scores, axis=-1).astype(jnp.bfloat16)
    context = jnp.einsum(
        "hqf,fd->qhd", weights, keys_values[:, HD:], preferred_element_type=jnp.float32
    ).astype(jnp.bfloat16)
    partial = jnp.dot(
        context.reshape(slot_tokens, device_heads * HD), o_proj, preferred_element_type=jnp.float32
    ).astype(jnp.bfloat16)
    partial = partial.reshape(section_count, pieces, width_count * piece_rows, model_width)
    attn_out = []
    for piece in range(pieces):
        section_sum = scatter_sum(partial[:, piece], "section")[0].astype(jnp.bfloat16)
        attn_out.append(scatter_sum(section_sum, "mp"))
    attn_out = jnp.concatenate(attn_out, axis=0)
    out_normed = square_norm(resid_rows.astype(jnp.float32) + attn_out).astype(jnp.bfloat16)

    if near_order:
        own = gather_blocks(out_normed, "mp")
        half = own.shape[0] // 2
        by_x = swap(own, "section", 1)
        by_y = swap(own, "tm", 2)
        across = jnp.concatenate([swap(by_x[:half], "tm", 2), swap(by_y[half:], "section", 1)])
        chunks = [jnp.concatenate([rows, swap(rows, "tm", 1)]) for rows in (own, by_y, by_x, across)]
    else:
        chunks = [lax.all_gather(out_normed, ALL, axis=0, tiled=True)]
    vocab_rows = head.shape[0]
    vocab_start = (
        (section_pos * group_count + group_pos) * width_count + width_pos
    ) * vocab_rows
    stats = []
    chunk_rows = token_count // len(chunks)
    for number, hidden_rows in enumerate(chunks):
        logits = lax.dot_general(
            hidden_rows, head, (((1,), (1,)), ((), ())), preferred_element_type=jnp.float32
        )
        target_rows = targets[number * chunk_rows : (number + 1) * chunk_rows]
        upper = jnp.max(logits, axis=1)
        totals = jnp.sum(jnp.exp(logits - upper[:, None]), axis=1)
        matches = (
            jnp.arange(vocab_rows, dtype=jnp.int32)[None, :] == (target_rows - vocab_start)[:, None]
        )
        target_logit = jnp.sum(jnp.where(matches, logits, 0.0), axis=1)
        stats.append(jnp.stack([upper, totals, target_logit]))

    stats = jnp.concatenate(stats, axis=1)
    token = jnp.arange(slot_tokens, dtype=jnp.int32)
    token_row = token // (width_count * piece_rows) % pieces * piece_rows + token % piece_rows
    wanted = rows_of(
        token[None, :] // (width_count * pieces * piece_rows),
        jnp.maximum(slot_utt, 0)[:, None],
        token[None, :] // piece_rows % width_count,
        token_row[None, :],
    )
    by_slot = jnp.take(stats, (wanted ^ here).reshape(-1), axis=1)
    by_slot = by_slot.reshape(3, slot_utt.shape[0], slot_tokens).transpose(1, 0, 2)
    by_group = by_slot.reshape(1, group_count, 1, slot_count, 3, slot_tokens)
    by_group = jnp.broadcast_to(
        by_group, (section_count, group_count, width_count, slot_count, 3, slot_tokens)
    ).reshape(all_devices, slot_count, 3, slot_tokens)
    every = exchange(by_group, ALL)
    peak = jnp.max(every[:, :, 0], axis=0)
    total = jnp.sum(every[:, :, 1] * jnp.exp(every[:, :, 0] - peak[None]), axis=0)
    picked = jnp.sum(every[:, :, 2], axis=0)
    token_logp = (picked - (peak + jnp.log(total))).reshape(slot_count, hyp_count, positions)
    valid = jnp.arange(positions, dtype=jnp.int32)[None, None, :] < hyp_len[:, :, None]
    summed = jnp.sum(jnp.where(valid, token_logp, 0.0), axis=-1) / hyp_len.astype(
        jnp.float32
    ) + math.log(V)
    return jnp.where(here_slots[:, None] >= 0, summed, 0.0)


def solution(mesh):
    in_specs = (
        P(),
        P(),
        P(("section", "tm"), None, None),
        P(None, "mp"),
        P("mp", None),
        P(),
        P("tm", None, None, None),
        P("tm", None, None),
        P("tm", None),
        P(None, ("section", "mp")),
        P(("section", "mp"), None),
        P(("section", "tm", "mp"), None),
    )
    out_specs = P("tm", None)
    return jax.shard_map(
        per_device, mesh=mesh, in_specs=in_specs, out_specs=out_specs, check_vma=False
    )
```

```python
import functools
import math

import jax
import jax.numpy as jnp
from jax import lax
from jax.experimental import pallas as pl
from jax.experimental.pallas import tpu as pltpu
from jax.sharding import PartitionSpec as P

NH = 32
KVH = 4
HD = 128
V = 64000
ALL = ("section", "tm", "mp")
LANES = 128


def layer_norm(values):
    center = values - jnp.mean(values, axis=-1, keepdims=True)
    spread = jnp.mean(center * center, axis=-1, keepdims=True)
    return center * lax.rsqrt(spread + 1e-05)


def square_norm(values):
    return values * lax.rsqrt(jnp.mean(values * values, axis=-1, keepdims=True) + 1e-06)


def exchange(blocks, axis):
    return lax.all_to_all(blocks, axis, split_axis=0, concat_axis=0, tiled=True)


def scatter_sum(partial, axis, count):
    blocks = partial.reshape((count, partial.shape[0] // count) + partial.shape[1:])
    return jnp.sum(exchange(blocks, axis).astype(jnp.float32), axis=0)


def swap(values, axis, distance):
    pairs = [(i, i ^ distance) for i in range(lax.axis_size(axis))]
    return lax.ppermute(values, axis, pairs)


def whole(shape):
    return pl.BlockSpec(shape, lambda *_: (0,) * len(shape))


SCALARS = pl.BlockSpec(memory_space=pltpu.SMEM)


def dot(left, right):
    return jnp.dot(left, right, preferred_element_type=jnp.float32)


def dot_nt(left, right):
    return lax.dot_general(
        left, right, (((1,), (1,)), ((), ())), preferred_element_type=jnp.float32
    )


def ffn_kernel(count, place_ref, x_ref, up_ref, down_ref, *refs):
    outs, own_ref, normed, total = refs[:count], refs[count], refs[count + 1], refs[count + 2]
    share = own_ref.shape[0]
    step = pl.program_id(0)
    here = place_ref[0]

    @pl.when(step == 0)
    def _():
        normed[...] = layer_norm(x_ref[...].astype(jnp.float32)).astype(jnp.bfloat16)
        own_ref[...] = x_ref[pl.ds(pl.multiple_of(here * share, share), share), :]
        total[...] = jnp.zeros_like(total)

    hidden = dot(normed[...], up_ref[...])
    inner = 0.5 * hidden * (1.0 + lax.erf(hidden * math.sqrt(0.5)))
    total[...] += dot(inner.astype(jnp.bfloat16), down_ref[...])

    @pl.when(step == pl.num_programs(0) - 1)
    def _():
        for distance in range(count):
            start = pl.multiple_of((here ^ distance) * share, share)
            outs[distance][...] = total[pl.ds(start, share), :].astype(jnp.bfloat16)


def ffn(place, rows, up, down, count):
    share = rows.shape[0] // count
    width = rows.shape[1]
    tile = 256
    block = jax.ShapeDtypeStruct((share, width), jnp.bfloat16)
    return pl.pallas_call(
        functools.partial(ffn_kernel, count),
        grid=(up.shape[1] // tile,),
        in_specs=[
            SCALARS,
            whole(rows.shape),
            pl.BlockSpec((width, tile), lambda i: (0, i)),
            pl.BlockSpec((tile, width), lambda i: (i, 0)),
        ],
        out_specs=[whole(block.shape)] * (count + 1),
        out_shape=[block] * (count + 1),
        scratch_shapes=[
            pltpu.VMEM(rows.shape, jnp.bfloat16),
            pltpu.VMEM(rows.shape, jnp.float32),
        ],
        cost_estimate=pl.CostEstimate(
            flops=4 * rows.shape[0] * width * up.shape[1],
            bytes_accessed=4 * width * up.shape[1],
            transcendentals=rows.shape[0] * up.shape[1],
        ),
        compiler_params=pltpu.CompilerParams(vmem_limit_bytes=24 << 20),
        name="encoder_ffn",
    )(place, rows, up, down)


def query_kernel(count, pick_ref, length_ref, place_ref, x_ref, tok_ref, w_ref, *refs):
    outs, normed, total, shares = refs[:count], refs[count], refs[count + 1], refs[count + 2]
    slots, tokens, width = x_ref.shape
    hyps = length_ref.shape[0] // slots
    positions = tokens // hyps
    columns = w_ref.shape[1]
    share = shares.shape[1] - 16
    step = pl.program_id(0)

    @pl.when(step == 0)
    def _():
        lane = lax.broadcasted_iota(jnp.int32, (1, tokens), 1)
        for slot in range(slots):
            order = jnp.full((1, tokens), -1, jnp.int32)
            start = jnp.int32(0)
            for hyp in range(hyps):
                length = length_ref[slot * hyps + hyp]
                inside = (lane >= hyp * positions) & (lane < hyp * positions + length)
                order = jnp.where(inside, lane - hyp * positions + start, order)
                start = start + length
            row = lax.broadcasted_iota(jnp.int32, (tokens, tokens), 0)
            move = jnp.where(order == row, 1.0, 0.0).astype(jnp.bfloat16)
            ordered = dot(move, x_ref[slot])
            normed[pl.ds(slot * tokens, tokens), :] = square_norm(ordered).astype(jnp.bfloat16)
            share_row = lax.broadcasted_iota(jnp.int32, (share, tokens), 0)
            chosen = order == share_row * (tokens // share) + place_ref[0]
            mine = dot(jnp.where(chosen, 1.0, 0.0).astype(jnp.bfloat16), x_ref[slot])
            shares[slot, :share, :] = mine.astype(jnp.bfloat16)
            target = jnp.sum(
                jnp.where(chosen, tok_ref[slot], 0), axis=1, keepdims=True, dtype=jnp.int32
            )
            coarse = target // 256
            cell = lax.broadcasted_iota(jnp.int32, (share, width), 1)
            packed = jnp.where(cell == 0, coarse, jnp.where(cell == 1, target - coarse * 256, 0))
            shares[slot, share:, :] = packed.astype(jnp.float32).astype(jnp.bfloat16)
        total[...] = jnp.zeros_like(total)

    depth = w_ref.shape[0]
    part = normed[:, pl.ds(pl.multiple_of(step * depth, depth), depth)]
    total[...] += dot(part, w_ref[...])

    @pl.when(step == pl.num_programs(0) - 1)
    def _():
        for distance in range(count):
            slot = pick_ref[distance]
            out = outs[distance]
            start = pl.multiple_of(slot * tokens, tokens)
            out[:tokens, :] = total[pl.ds(start, tokens), :].astype(jnp.bfloat16)
            for part in range(width // columns):
                out[pl.ds(tokens + part * share, share), :] = shares[
                    slot, :share, part * columns : (part + 1) * columns
                ]
            out[pl.ds(tokens + width // columns * share, share), :] = shares[slot, share:, :columns]


def queries_of(pick, lengths, place, states, targets, weights, count, share):
    slots, tokens, width = states.shape
    columns = weights.shape[1]
    depth = 1024
    rows = tokens + width // columns * share + share
    block = jax.ShapeDtypeStruct((rows, columns), jnp.bfloat16)
    return pl.pallas_call(
        functools.partial(query_kernel, count),
        grid=(width // depth,),
        in_specs=[
            SCALARS,
            SCALARS,
            SCALARS,
            whole(states.shape),
            whole(targets.shape),
            pl.BlockSpec((depth, columns), lambda i: (i, 0)),
        ],
        out_specs=[whole(block.shape)] * count,
        out_shape=[block] * count,
        scratch_shapes=[
            pltpu.VMEM((slots * tokens, width), jnp.bfloat16),
            pltpu.VMEM((slots * tokens, columns), jnp.float32),
            pltpu.VMEM((slots, share + 16, width), jnp.bfloat16),
        ],
        cost_estimate=pl.CostEstimate(
            flops=2 * slots * tokens * width * columns,
            bytes_accessed=2 * width * (columns + slots * tokens),
            transcendentals=0,
        ),
        compiler_params=pltpu.CompilerParams(vmem_limit_bytes=32 << 20),
        name="hypothesis_queries",
    )(pick, lengths, place, states, targets, weights)


def kv_kernel(sections, utterances, widths, *refs):
    parts, own_ref, w_ref, out_ref = refs[:-3], refs[-3], refs[-2], refs[-1]
    rows = own_ref.shape[0]
    frames = rows // utterances
    total = own_ref[...].astype(jnp.float32)
    summed = parts[0][...].astype(jnp.float32)
    for part in parts[1:]:
        summed += part[...].astype(jnp.float32)
    states = layer_norm(total + summed).astype(jnp.bfloat16)
    to = lax.broadcasted_iota(jnp.int32, (rows, rows), 0)
    come = lax.broadcasted_iota(jnp.int32, (rows, rows), 1)
    move = jnp.where(come == to % frames * utterances + to // frames, 1.0, 0.0)
    states = dot(move.astype(jnp.bfloat16), states).astype(jnp.bfloat16)
    both = dot(states, w_ref[...])
    half = KVH * HD
    per_kv = sections * widths // KVH
    for section in range(sections):
        for utterance in range(utterances):
            for width in range(0, widths, per_kv):
                kv_head = (section * widths + width) // per_kv
                take = slice(utterance * frames, (utterance + 1) * frames)
                block = jnp.concatenate(
                    [
                        both[take, kv_head * HD : (kv_head + 1) * HD],
                        both[take, half + kv_head * HD : half + (kv_head + 1) * HD],
                    ],
                    axis=1,
                )
                start = ((section * utterances + utterance) * widths + width) * frames
                block = jnp.concatenate([block] * per_kv, axis=0).astype(jnp.bfloat16)
                out_ref[start : start + per_kv * frames, :] = block


def keys_values_of(parts, own, weights, sections, utterances, widths):
    rows = sections * widths * own.shape[0]
    return pl.pallas_call(
        functools.partial(kv_kernel, sections, utterances, widths),
        out_shape=jax.ShapeDtypeStruct((rows, 2 * HD), jnp.bfloat16),
        cost_estimate=pl.CostEstimate(
            flops=2 * own.shape[0] * weights.shape[0] * weights.shape[1],
            bytes_accessed=2 * weights.shape[0] * weights.shape[1],
            transcendentals=0,
        ),
        compiler_params=pltpu.CompilerParams(vmem_limit_bytes=24 << 20),
        name="frame_keys_values",
    )(*parts, own, weights)


def attention_kernel(count, capacity, pieces, sections, widths, info_ref, *refs):
    payloads = refs[:count]
    kv_ref, w_ref = refs[count : count + 2]
    outs = refs[count + 2 : count + 2 + 2 * len(pieces)]
    resid_ref, context, picked = refs[count + 2 + 2 * len(pieces) :]
    tokens, columns = kv_ref.shape[1] // 2, w_ref.shape[0]
    tokens = capacity
    source, frame_limit, section_pos = info_ref[0], info_ref[1], info_ref[2]
    step = pl.program_id(0)

    @pl.when(step == 0)
    def _():
        for distance in range(count):

            @pl.when(source == distance)
            def _(payload=payloads[distance]):
                picked[...] = payload[...]

        keys = kv_ref[:, :HD]
        values = kv_ref[:, HD:]
        frames = kv_ref.shape[0]
        visible = lax.broadcasted_iota(jnp.int32, (tokens, frames), 1) < frame_limit
        for head in range(columns // HD):
            query = picked[:tokens, head * HD : (head + 1) * HD]
            scores = dot_nt(query, keys) * (1.0 / math.sqrt(HD))
            scores = jnp.where(visible, scores, -jnp.inf)
            raised = jnp.exp(scores - jnp.max(scores, axis=1, keepdims=True))
            weights = (raised / jnp.sum(raised, axis=1, keepdims=True)).astype(jnp.bfloat16)
            context[:, head * HD : (head + 1) * HD] = dot(weights, values).astype(jnp.bfloat16)
        to = lax.broadcasted_iota(jnp.int32, (tokens, tokens), 0)
        come = lax.broadcasted_iota(jnp.int32, (tokens, tokens), 1)
        half = tokens // sections
        section = jnp.where(to < half, 1 - section_pos, section_pos)
        inside = to % half
        row = jnp.zeros_like(to)
        width = jnp.zeros_like(to)
        first = 0
        for piece in pieces:
            at = inside - first * widths
            here = (at >= 0) & (at < piece * widths)
            row = jnp.where(here, first + at % piece, row)
            width = jnp.where(here, at // piece, width)
            first += piece
        move = come == (row * sections + section) * widths + width
        context[...] = dot(jnp.where(move, 1.0, 0.0).astype(jnp.bfloat16), context[...]).astype(
            jnp.bfloat16
        )
        share = resid_ref.shape[0]
        first_row = payloads[0].shape[0] - share * (1 + (resid_ref.shape[1] - LANES) // columns)
        for part in range((resid_ref.shape[1] - LANES) // columns):
            resid_ref[:, part * columns : (part + 1) * columns] = picked[
                first_row + part * share : first_row + (part + 1) * share, :
            ]
        resid_ref[:, resid_ref.shape[1] - LANES :] = picked[
            payloads[0].shape[0] - share :, :LANES
        ]

    product = dot(context[...], w_ref[...])
    first = 0
    for number, out in enumerate(outs):
        rows = out.shape[0]
        out[...] = product[first : first + rows, :].astype(jnp.bfloat16)
        first += rows


def attend(info, payloads, keys_values, weights, capacity, pieces, sections, widths, share):
    count = len(payloads)
    columns, width = weights.shape
    tile = 1024
    shapes = [jax.ShapeDtypeStruct((piece * widths, width), jnp.bfloat16) for piece in pieces]
    shapes = shapes + shapes
    resid = jax.ShapeDtypeStruct((share, width + LANES), jnp.bfloat16)
    return pl.pallas_call(
        functools.partial(attention_kernel, count, capacity, pieces, sections, widths),
        grid=(width // tile,),
        in_specs=[SCALARS]
        + [whole(payloads[0].shape)] * count
        + [whole(keys_values.shape), pl.BlockSpec((columns, tile), lambda i: (0, i))],
        out_specs=[pl.BlockSpec((s.shape[0], tile), lambda i: (0, i)) for s in shapes]
        + [whole(resid.shape)],
        out_shape=shapes + [resid],
        scratch_shapes=[
            pltpu.VMEM((capacity, columns), jnp.bfloat16),
            pltpu.VMEM(payloads[0].shape, jnp.bfloat16),
        ],
        cost_estimate=pl.CostEstimate(
            flops=2 * capacity * columns * (width + 2 * keys_values.shape[0]),
            bytes_accessed=2 * columns * width + 2 * capacity * width,
            transcendentals=capacity * keys_values.shape[0] * columns // HD,
        ),
        compiler_params=pltpu.CompilerParams(vmem_limit_bytes=24 << 20),
        name="attention_projection",
    )(info, *payloads, keys_values, weights)


def near_device(
    frame_len,
    slot_utt,
    enc_in,
    ffn_up,
    ffn_down,
    kv_proj,
    hyp_state,
    hyp_tok,
    hyp_len,
    q_proj,
    o_proj,
    head,
):
    section_count = lax.axis_size("section")
    group_count = lax.axis_size("tm")
    width_count = lax.axis_size("mp")
    section_pos = lax.axis_index("section")
    group_pos = lax.axis_index("tm")
    width_pos = lax.axis_index("mp")
    head_devices = section_count * width_count
    head_pos = section_pos * width_count + width_pos
    all_devices = head_devices * group_count

    frame_rows, utterances, enc_width = enc_in.shape
    slot_count, hyp_count, positions, model_width = hyp_state.shape
    slot_tokens = hyp_count * positions
    share_rows = slot_tokens // head_devices
    here_slots = lax.dynamic_slice_in_dim(slot_utt, group_pos * slot_count, slot_count, 0)
    own_slot = jnp.argmax(slot_utt == group_pos).astype(jnp.int32)
    source = (own_slot // slot_count) ^ group_pos

    parts = ffn(
        width_pos.astype(jnp.int32).reshape(1),
        enc_in.reshape(frame_rows * utterances, enc_width),
        ffn_up,
        ffn_down,
        width_count,
    )
    own_frames = parts[width_count]
    parts = [parts[0]] + [
        swap(parts[distance], "mp", distance) for distance in range(1, width_count)
    ]

    wanted = group_pos ^ jnp.arange(group_count)
    pick = jnp.argmax(here_slots[None, :] == wanted[:, None], axis=1).astype(jnp.int32)
    payloads = queries_of(
        pick,
        hyp_len.reshape(-1),
        head_pos.astype(jnp.int32).reshape(1),
        hyp_state.reshape(slot_count, slot_tokens, model_width),
        hyp_tok.reshape(slot_count, 1, slot_tokens),
        q_proj,
        group_count,
        share_rows,
    )
    payloads = [payloads[0]] + [
        swap(payloads[distance], "tm", distance) for distance in range(1, group_count)
    ]

    sent = keys_values_of(parts, own_frames, kv_proj, section_count, utterances, width_count)
    frames_all = all_devices * (frame_rows // width_count)
    keys_values = exchange(sent.reshape(all_devices, -1, 2 * HD), ALL).reshape(frames_all, 2 * HD)
    frame_limit = lax.dynamic_index_in_dim(frame_len, group_pos, 0, keepdims=False)
    info = jnp.stack([source, frame_limit, section_pos.astype(jnp.int32)])

    pieces = (share_rows // 2, share_rows - share_rows // 2)
    capacity = sum(pieces) * head_devices
    *projected, resid = attend(
        info,
        payloads,
        keys_values,
        o_proj,
        capacity,
        pieces,
        section_count,
        width_count,
        share_rows,
    )
    attn_out = []
    for number, piece in enumerate(pieces):
        other = swap(projected[number], "section", 1)
        section_sum = (
            projected[len(pieces) + number].astype(jnp.float32) + other.astype(jnp.float32)
        ).astype(jnp.bfloat16)
        total = None
        for distance in range(width_count - 1, -1, -1):
            block = lax.dynamic_slice_in_dim(
                section_sum, (width_pos ^ distance) * piece, piece, 0
            )
            if distance:
                block = swap(block, "mp", distance)
            block = block.astype(jnp.float32)
            total = block if total is None else total + block
        attn_out.append(total)
    attn_out = jnp.concatenate(attn_out, axis=0)
    out_normed = square_norm(resid[:, :model_width].astype(jnp.float32) + attn_out)
    out_rows = jnp.concatenate(
        [out_normed.astype(jnp.bfloat16), resid[:, model_width:]], axis=1
    )

    share = out_rows.shape[0]
    own = jnp.zeros((width_count * share, out_rows.shape[1]), jnp.bfloat16)
    for distance in range(width_count):
        block = swap(out_rows, "mp", distance) if distance else out_rows
        own = lax.dynamic_update_slice_in_dim(own, block, (width_pos ^ distance) * share, 0)
    half = own.shape[0] // 2
    by_x = swap(own, "section", 1)
    by_y = swap(own, "tm", 2)
    across = jnp.concatenate([swap(by_x[:half], "tm", 2), swap(by_y[half:], "section", 1)])
    vocab_rows = head.shape[0]
    vocab_start = (
        (section_pos * group_count + group_pos) * width_count + width_pos
    ) * vocab_rows
    stats = []
    for rows in (own, by_y, by_x, across):
        chunk = jnp.concatenate([rows, swap(rows, "tm", 1)])
        logits = dot_nt(chunk[:, :model_width], head)
        target = chunk[:, model_width : model_width + 2].astype(jnp.int32)
        target = target[:, 0] * 256 + target[:, 1] - vocab_start
        upper = jnp.max(logits, axis=1)
        totals = jnp.sum(jnp.exp(logits - upper[:, None]), axis=1)
        matches = jnp.arange(vocab_rows, dtype=jnp.int32)[None, :] == target[:, None]
        target_logit = jnp.sum(jnp.where(matches, logits, 0.0), axis=1)
        stats.append(jnp.stack([upper, totals, target_logit]).reshape(3, 2, -1))

    stats = jnp.stack(stats).transpose(0, 2, 1, 3).reshape(head_devices, -1)
    slots = slot_utt.shape[0]
    place = (
        (jnp.arange(section_count)[None, :] ^ section_pos) * group_count
        + (jnp.maximum(slot_utt, 0)[:, None] ^ group_pos)
    ).reshape(-1)
    by_slot = jnp.take(stats, place, axis=0, mode="clip")
    by_group = by_slot.reshape(1, group_count, 1, -1)
    by_group = jnp.broadcast_to(
        by_group, (section_count, group_count, width_count, by_group.shape[-1])
    ).reshape(all_devices, slot_count, section_count, 3, width_count, share)
    every = exchange(by_group, ALL)
    peak = jnp.max(every[:, :, :, 0], axis=0)
    total = jnp.sum(every[:, :, :, 1] * jnp.exp(every[:, :, :, 0] - peak[None]), axis=0)
    picked = jnp.sum(every[:, :, :, 2], axis=0)
    token_logp = picked - (peak + jnp.log(total))
    shape = (1, 1, section_count, width_count, share)
    order = (
        lax.broadcasted_iota(jnp.int32, shape, 4) * head_devices
        + lax.broadcasted_iota(jnp.int32, shape, 2) * width_count
        + lax.broadcasted_iota(jnp.int32, shape, 3)
    )
    ends = jnp.cumsum(hyp_len, axis=1)[:, :, None, None, None]
    starts = ends - hyp_len[:, :, None, None, None]
    valid = (order >= starts) & (order < ends)
    summed = jnp.sum(
        jnp.where(valid, token_logp[:, None], 0.0), axis=(2, 3, 4)
    ) / hyp_len.astype(jnp.float32) + math.log(V)
    return jnp.where(here_slots[:, None] >= 0, summed, 0.0)


def general(
    frame_len,
    slot_utt,
    enc_in,
    ffn_up,
    ffn_down,
    kv_proj,
    hyp_state,
    hyp_tok,
    hyp_len,
    q_proj,
    o_proj,
    head,
):
    section_count = lax.axis_size("section")
    group_count = lax.axis_size("tm")
    width_count = lax.axis_size("mp")
    section_pos = lax.axis_index("section")
    group_pos = lax.axis_index("tm")
    width_pos = lax.axis_index("mp")
    head_devices = section_count * width_count
    head_pos = section_pos * width_count + width_pos
    all_devices = head_devices * group_count

    frame_rows, utterances, enc_width = enc_in.shape
    assert utterances == group_count
    slot_count, hyp_count, positions, model_width = hyp_state.shape
    slot_tokens = hyp_count * positions
    device_heads = q_proj.shape[1] // HD
    group_heads = NH // KVH
    frame_share = frame_rows // width_count
    share_rows = slot_tokens // head_devices
    here_slots = lax.dynamic_slice_in_dim(slot_utt, group_pos * slot_count, slot_count, 0)

    dec_rows = hyp_state.reshape(slot_count * slot_tokens, model_width).astype(jnp.float32)
    queries = jnp.dot(
        square_norm(dec_rows).astype(jnp.bfloat16), q_proj, preferred_element_type=jnp.float32
    ).astype(jnp.bfloat16)
    queries = queries.reshape(slot_count, slot_tokens, device_heads * HD)
    shares = lax.dynamic_slice_in_dim(
        hyp_state.reshape(slot_count, slot_tokens, model_width), head_pos * share_rows, share_rows, 1
    )

    def by_utterance(values):
        out = []
        for utterance in range(utterances):
            block = values[0]
            for slot in range(1, slot_count):
                block = jnp.where(here_slots[slot] == utterance, values[slot], block)
            out.append(block)
        return jnp.stack(out)

    own_slot = jnp.argmax(slot_utt == group_pos)
    from_group = own_slot // slot_count
    queries = lax.dynamic_index_in_dim(
        exchange(by_utterance(queries), "tm"), from_group, 0, keepdims=False
    )
    resid_rows = lax.dynamic_index_in_dim(
        exchange(by_utterance(shares), "tm"), from_group, 0, keepdims=False
    )
    slot_targets = lax.all_gather(
        hyp_tok.reshape(slot_count, slot_tokens), "tm", axis=0, tiled=True
    )
    utt_slots = jnp.argmax(slot_utt[None, :] == jnp.arange(utterances)[:, None], axis=1)
    targets = jnp.take(slot_targets, utt_slots, axis=0).reshape(utterances * slot_tokens)

    enc_flat = (
        enc_in.reshape(width_count, frame_share, utterances, enc_width)
        .transpose(0, 2, 1, 3)
        .reshape(frame_rows * utterances, enc_width)
    )
    share_count = frame_share * utterances
    enc_normed = layer_norm(enc_flat.astype(jnp.float32)).astype(jnp.bfloat16)
    enc_inner = jax.nn.gelu(
        jnp.dot(enc_normed, ffn_up, preferred_element_type=jnp.float32), approximate=False
    ).astype(jnp.bfloat16)
    enc_summed = scatter_sum(
        jnp.dot(enc_inner, ffn_down, preferred_element_type=jnp.float32).astype(jnp.bfloat16),
        "mp",
        width_count,
    )
    own_frames = lax.dynamic_slice_in_dim(enc_flat, width_pos * share_count, share_count, 0)
    enc_states = layer_norm(own_frames.astype(jnp.float32) + enc_summed).astype(jnp.bfloat16)
    keys_values = jnp.dot(enc_states, kv_proj, preferred_element_type=jnp.float32).astype(
        jnp.bfloat16
    )
    keys_values = keys_values.reshape(utterances, frame_share, 2, KVH, HD)
    sent = []
    for section in range(section_count):
        per_width = []
        for width in range(width_count):
            kv_head = (section * width_count + width) * device_heads // group_heads
            per_width.append(
                keys_values[:, :, :, kv_head].reshape(utterances, frame_share, 2 * HD)
            )
        sent.append(jnp.stack(per_width, axis=1))
    sent = jnp.stack(sent).reshape(all_devices, frame_share, 2 * HD)
    frames_all = all_devices * frame_share
    keys_values = exchange(sent, ALL).reshape(frames_all, 2 * HD)

    frame_limit = lax.dynamic_index_in_dim(frame_len, group_pos, 0, keepdims=False)
    queries = queries.reshape(slot_tokens, device_heads, HD)
    scores = jnp.einsum(
        "qhd,fd->hqf", queries, keys_values[:, :HD], preferred_element_type=jnp.float32
    ) / math.sqrt(HD)
    visible = jnp.arange(frames_all, dtype=jnp.int32) < frame_limit
    scores = jnp.where(visible[None, None, :], scores, -jnp.inf)
    weights = jax.nn.softmax(scores, axis=-1).astype(jnp.bfloat16)
    context = jnp.einsum(
        "hqf,fd->qhd", weights, keys_values[:, HD:], preferred_element_type=jnp.float32
    ).astype(jnp.bfloat16)
    partial = jnp.dot(
        context.reshape(slot_tokens, device_heads * HD), o_proj, preferred_element_type=jnp.float32
    ).astype(jnp.bfloat16)
    partial = scatter_sum(partial, "section", section_count).astype(jnp.bfloat16)
    attn_out = scatter_sum(partial, "mp", width_count)
    out_normed = square_norm(resid_rows.astype(jnp.float32) + attn_out).astype(jnp.bfloat16)

    hidden_rows = lax.all_gather(out_normed, ALL, axis=0, tiled=True)
    logits = lax.dot_general(
        hidden_rows, head, (((1,), (1,)), ((), ())), preferred_element_type=jnp.float32
    )
    vocab_rows = head.shape[0]
    vocab_start = (
        (section_pos * group_count + group_pos) * width_count + width_pos
    ) * vocab_rows
    target_rows = (
        targets.reshape(utterances, section_count, width_count, share_rows)
        .transpose(1, 0, 2, 3)
        .reshape(-1)
    )
    upper = jnp.max(logits, axis=1)
    totals = jnp.sum(jnp.exp(logits - upper[:, None]), axis=1)
    matches = (
        jnp.arange(vocab_rows, dtype=jnp.int32)[None, :] == (target_rows - vocab_start)[:, None]
    )
    target_logit = jnp.sum(jnp.where(matches, logits, 0.0), axis=1)

    stats = jnp.stack([upper, totals, target_logit])
    stats = stats.reshape(3, section_count, utterances, width_count, share_rows)
    stats = stats.transpose(2, 0, 1, 3, 4).reshape(utterances, 3, slot_tokens)
    by_slot = jnp.take(stats, jnp.maximum(slot_utt, 0), axis=0)
    by_group = by_slot.reshape(1, group_count, 1, slot_count, 3, slot_tokens)
    by_group = jnp.broadcast_to(
        by_group, (section_count, group_count, width_count, slot_count, 3, slot_tokens)
    ).reshape(all_devices, slot_count, 3, slot_tokens)
    every = exchange(by_group, ALL)
    peak = jnp.max(every[:, :, 0], axis=0)
    total = jnp.sum(every[:, :, 1] * jnp.exp(every[:, :, 0] - peak[None]), axis=0)
    picked = jnp.sum(every[:, :, 2], axis=0)
    token_logp = (picked - (peak + jnp.log(total))).reshape(slot_count, hyp_count, positions)
    valid = jnp.arange(positions, dtype=jnp.int32)[None, None, :] < hyp_len[:, :, None]
    summed = jnp.sum(jnp.where(valid, token_logp, 0.0), axis=-1) / hyp_len.astype(
        jnp.float32
    ) + math.log(V)
    return jnp.where(here_slots[:, None] >= 0, summed, 0.0)


def solution(mesh):
    in_specs = (
        P(),
        P(),
        P(("section", "tm"), None, None),
        P(None, "mp"),
        P("mp", None),
        P(),
        P("tm", None, None, None),
        P("tm", None, None),
        P("tm", None),
        P(None, ("section", "mp")),
        P(("section", "mp"), None),
        P(("section", "tm", "mp"), None),
    )
    out_specs = P("tm", None)
    near = dict(mesh.shape) == {"section": 2, "tm": 4, "mp": 4}
    per_device = near_device if near else general
    return jax.shard_map(
        per_device, mesh=mesh, in_specs=in_specs, out_specs=out_specs, check_vma=False
    )
```

```python
import functools
import math

import jax
import jax.numpy as jnp
from jax import lax
from jax.experimental import pallas as pl
from jax.experimental.pallas import tpu as pltpu
from jax.sharding import PartitionSpec as P

NH = 32
KVH = 4
HD = 128
V = 64000
ALL = ("section", "tm", "mp")
LANES = 128


def layer_norm(values):
    center = values - jnp.mean(values, axis=-1, keepdims=True)
    spread = jnp.mean(center * center, axis=-1, keepdims=True)
    return center * lax.rsqrt(spread + 1e-05)


def square_norm(values):
    return values * lax.rsqrt(jnp.mean(values * values, axis=-1, keepdims=True) + 1e-06)


def exchange(blocks, axis):
    return lax.all_to_all(blocks, axis, split_axis=0, concat_axis=0, tiled=True)


def scatter_sum(partial, axis, count):
    blocks = partial.reshape((count, partial.shape[0] // count) + partial.shape[1:])
    return jnp.sum(exchange(blocks, axis).astype(jnp.float32), axis=0)


def swap(values, axis, distance):
    pairs = [(i, i ^ distance) for i in range(lax.axis_size(axis))]
    return lax.ppermute(values, axis, pairs)


def whole(shape):
    return pl.BlockSpec(shape, lambda *_: (0,) * len(shape))


SCALARS = pl.BlockSpec(memory_space=pltpu.SMEM)


def dot(left, right):
    return jnp.dot(left, right, preferred_element_type=jnp.float32)


def dot_nt(left, right):
    return lax.dot_general(
        left, right, (((1,), (1,)), ((), ())), preferred_element_type=jnp.float32
    )


def start_copies(source_of, target_of, semaphores, count):
    copies = []
    for number in range(count):
        copy = pltpu.make_async_copy(
            source_of(number), target_of(number), semaphores.at[number]
        )
        copy.start()
        copies.append(copy)
    return copies


def ffn_kernel(count, tile, place_ref, x_ref, up_ref, down_ref, *refs):
    outs, (own_ref, total, up, down, up_sem, down_sem) = refs[:count], refs[count:]
    share = own_ref.shape[0]
    tiles = up_ref.shape[1] // tile
    up_copies = start_copies(
        lambda i: up_ref.at[:, pl.ds(i * tile, tile)], lambda i: up.at[i], up_sem, tiles
    )
    down_copies = start_copies(
        lambda i: down_ref.at[pl.ds(i * tile, tile), :], lambda i: down.at[i], down_sem, tiles
    )
    here = place_ref[2]
    own_ref[...] = x_ref[pl.ds(pl.multiple_of(here * share, share), share), :]
    normed = layer_norm(x_ref[...].astype(jnp.float32)).astype(jnp.bfloat16)
    for number in range(tiles):
        up_copies[number].wait()
        hidden = dot(normed, up[number])
        inner = 0.5 * hidden * (1.0 + lax.erf(hidden * math.sqrt(0.5)))
        down_copies[number].wait()
        product = dot(inner.astype(jnp.bfloat16), down[number])
        if number == 0:
            total[...] = product
        else:
            total[...] += product
    for distance in range(count):
        start = pl.multiple_of((here ^ distance) * share, share)
        outs[distance][...] = total[pl.ds(start, share), :].astype(jnp.bfloat16)


def in_hbm(values):
    return pltpu.with_memory_space_constraint(values, pltpu.HBM)


ANYWHERE = pl.BlockSpec(memory_space=pl.ANY)
INSIDE = pl.BlockSpec(memory_space=pltpu.VMEM)


def ffn(place, rows, up, down, count):
    share = rows.shape[0] // count
    width = rows.shape[1]
    tile = 256
    tiles = up.shape[1] // tile
    block = jax.ShapeDtypeStruct((share, width), jnp.bfloat16)
    return pl.pallas_call(
        functools.partial(ffn_kernel, count, tile),
        in_specs=[SCALARS, INSIDE, ANYWHERE, ANYWHERE],
        out_specs=[INSIDE] * (count + 1),
        out_shape=[block] * (count + 1),
        scratch_shapes=[
            pltpu.VMEM(rows.shape, jnp.float32),
            pltpu.VMEM((tiles, width, tile), jnp.bfloat16),
            pltpu.VMEM((tiles, tile, width), jnp.bfloat16),
            pltpu.SemaphoreType.DMA((tiles,)),
            pltpu.SemaphoreType.DMA((tiles,)),
        ],
        cost_estimate=pl.CostEstimate(
            flops=4 * rows.shape[0] * width * up.shape[1],
            bytes_accessed=4 * width * up.shape[1],
            transcendentals=rows.shape[0] * up.shape[1],
        ),
        compiler_params=pltpu.CompilerParams(vmem_limit_bytes=24 << 20),
        name="encoder_ffn",
    )(place, rows, in_hbm(up), in_hbm(down))


def query_kernel(count, depth, place_ref, slot_ref, length_ref, x_ref, tok_ref, w_ref, *refs):
    outs, shares_out = refs[:count], refs[count : 2 * count]
    states, weights, normed, total, shares, x_sem, w_sem = refs[2 * count :]
    slots, tokens, width = x_ref.shape
    hyps = length_ref.shape[0] // slots
    positions = tokens // hyps
    columns = w_ref.shape[1]
    share = shares.shape[1] // 2
    parts = width // columns
    x_copies = start_copies(lambda i: x_ref.at[i], lambda i: states.at[i], x_sem, slots)
    w_copies = start_copies(
        lambda i: w_ref.at[pl.ds(i * depth, depth), :],
        lambda i: weights.at[i],
        w_sem,
        width // depth,
    )
    head_pos = place_ref[4]
    lane = lax.broadcasted_iota(jnp.int32, (1, tokens), 1)
    for slot in range(slots):
        order = jnp.full((1, tokens), -1, jnp.int32)
        start = jnp.int32(0)
        for hyp in range(hyps):
            length = length_ref[slot * hyps + hyp]
            inside = (lane >= hyp * positions) & (lane < hyp * positions + length)
            order = jnp.where(inside, lane - hyp * positions + start, order)
            start = start + length
        row = lax.broadcasted_iota(jnp.int32, (tokens, tokens), 0)
        move = jnp.where(order == row, 1.0, 0.0).astype(jnp.bfloat16)
        x_copies[slot].wait()
        ordered = dot(move, states[slot])
        normed[slot * tokens : (slot + 1) * tokens, :] = square_norm(ordered).astype(jnp.bfloat16)
        share_row = lax.broadcasted_iota(jnp.int32, (share, tokens), 0)
        chosen = order == share_row * (tokens // share) + head_pos
        mine = dot(jnp.where(chosen, 1.0, 0.0).astype(jnp.bfloat16), states[slot])
        shares[slot, :share, :] = mine.astype(jnp.bfloat16)
        target = jnp.sum(
            jnp.where(chosen, tok_ref[slot], 0), axis=1, keepdims=True, dtype=jnp.int32
        )
        coarse = target // 256
        cell = lax.broadcasted_iota(jnp.int32, (share, columns), 1)
        packed = jnp.where(cell == 0, coarse, jnp.where(cell == 1, target - coarse * 256, 0))
        shares[slot, share:, :columns] = packed.astype(jnp.float32).astype(jnp.bfloat16)
    for number in range(width // depth):
        w_copies[number].wait()
        product = dot(normed[:, number * depth : (number + 1) * depth], weights[number])
        if number == 0:
            total[...] = product
        else:
            total[...] += product
    group = place_ref[1]
    for distance in range(count):
        slot = jnp.int32(0)
        for candidate in range(1, slots):
            holds = slot_ref[group * slots + candidate] == group ^ distance
            slot = jnp.where(holds, candidate, slot)
        start = pl.multiple_of(slot * tokens, tokens)
        outs[distance][...] = total[pl.ds(start, tokens), :].astype(jnp.bfloat16)
        out = shares_out[distance]
        for part in range(parts):
            out[part * share : (part + 1) * share, :] = shares[
                slot, :share, part * columns : (part + 1) * columns
            ]
        out[parts * share :, :] = shares[slot, share:, :columns]


def queries_of(place, slot_utt, lengths, states, targets, weights, count, share):
    slots, tokens, width = states.shape
    columns = weights.shape[1]
    depth = 1024
    block = jax.ShapeDtypeStruct((tokens, columns), jnp.bfloat16)
    rows = jax.ShapeDtypeStruct(((width // columns + 1) * share, columns), jnp.bfloat16)
    return pl.pallas_call(
        functools.partial(query_kernel, count, depth),
        in_specs=[SCALARS] * 3 + [ANYWHERE, INSIDE, ANYWHERE],
        out_specs=[INSIDE] * (2 * count),
        out_shape=[block] * count + [rows] * count,
        scratch_shapes=[
            pltpu.VMEM(states.shape, jnp.bfloat16),
            pltpu.VMEM((width // depth, depth, columns), jnp.bfloat16),
            pltpu.VMEM((slots * tokens, width), jnp.bfloat16),
            pltpu.VMEM((slots * tokens, columns), jnp.float32),
            pltpu.VMEM((slots, 2 * share, width), jnp.bfloat16),
            pltpu.SemaphoreType.DMA((slots,)),
            pltpu.SemaphoreType.DMA((width // depth,)),
        ],
        cost_estimate=pl.CostEstimate(
            flops=2 * slots * tokens * width * columns,
            bytes_accessed=2 * width * (columns + slots * tokens),
            transcendentals=0,
        ),
        compiler_params=pltpu.CompilerParams(vmem_limit_bytes=32 << 20),
        name="hypothesis_queries",
    )(place, slot_utt, lengths, in_hbm(states), targets, in_hbm(weights))


def kv_kernel(sections, utterances, widths, *refs):
    parts, own_ref, w_ref, out_ref = refs[:-3], refs[-3], refs[-2], refs[-1]
    rows = own_ref.shape[0]
    frames = rows // utterances
    total = own_ref[...].astype(jnp.float32)
    summed = parts[0][...].astype(jnp.float32)
    for part in parts[1:]:
        summed += part[...].astype(jnp.float32)
    states = layer_norm(total + summed).astype(jnp.bfloat16)
    to = lax.broadcasted_iota(jnp.int32, (rows, rows), 0)
    come = lax.broadcasted_iota(jnp.int32, (rows, rows), 1)
    move = jnp.where(come == to % frames * utterances + to // frames, 1.0, 0.0)
    states = dot(move.astype(jnp.bfloat16), states).astype(jnp.bfloat16)
    both = dot(states, w_ref[...])
    half = KVH * HD
    per_kv = sections * widths // KVH
    for section in range(sections):
        for utterance in range(utterances):
            for width in range(0, widths, per_kv):
                kv_head = (section * widths + width) // per_kv
                take = slice(utterance * frames, (utterance + 1) * frames)
                block = jnp.concatenate(
                    [
                        both[take, kv_head * HD : (kv_head + 1) * HD],
                        both[take, half + kv_head * HD : half + (kv_head + 1) * HD],
                    ],
                    axis=1,
                )
                start = ((section * utterances + utterance) * widths + width) * frames
                block = jnp.concatenate([block] * per_kv, axis=0).astype(jnp.bfloat16)
                out_ref[start : start + per_kv * frames, :] = block


def keys_values_of(parts, own, weights, sections, utterances, widths):
    rows = sections * widths * own.shape[0]
    return pl.pallas_call(
        functools.partial(kv_kernel, sections, utterances, widths),
        out_shape=jax.ShapeDtypeStruct((rows, 2 * HD), jnp.bfloat16),
        cost_estimate=pl.CostEstimate(
            flops=2 * own.shape[0] * weights.shape[0] * weights.shape[1],
            bytes_accessed=2 * weights.shape[0] * weights.shape[1],
            transcendentals=0,
        ),
        compiler_params=pltpu.CompilerParams(vmem_limit_bytes=24 << 20),
        name="frame_keys_values",
    )(*parts, own, weights)


def distance_of_slot(place_ref, slot_ref, slots):
    group = place_ref[1]
    source = jnp.int32(0)
    for slot in range(slot_ref.shape[0]):
        source = jnp.where(slot_ref[slot] == group, slot // slots, source)
    return source ^ group


def attention_kernel(count, capacity, pieces, sections, widths, tile, *refs):
    place_ref, slot_ref, frame_ref = refs[:3]
    payloads, (kv_ref, w_ref) = refs[3 : 3 + count], refs[3 + count : 5 + count]
    outs = refs[5 + count : 5 + count + 2 * len(pieces)]
    weights, picked, context, w_sem = refs[5 + count + 2 * len(pieces) :]
    tokens, columns = capacity, w_ref.shape[0]
    tiles = w_ref.shape[1] // tile
    w_copies = start_copies(
        lambda i: w_ref.at[:, pl.ds(i * tile, tile)], lambda i: weights.at[i], w_sem, tiles
    )
    source = distance_of_slot(place_ref, slot_ref, slot_ref.shape[0] // count)
    section_pos = place_ref[0]
    frame_limit = frame_ref[place_ref[1]]
    for distance in range(count):

        @pl.when(source == distance)
        def _(payload=payloads[distance]):
            picked[...] = payload[:tokens, :]

    keys = kv_ref[:, :HD]
    values = kv_ref[:, HD:]
    frames = kv_ref.shape[0]
    visible = lax.broadcasted_iota(jnp.int32, (tokens, frames), 1) < frame_limit
    for head in range(columns // HD):
        scores = dot_nt(picked[:, head * HD : (head + 1) * HD], keys) * (1.0 / math.sqrt(HD))
        scores = jnp.where(visible, scores, -jnp.inf)
        raised = jnp.exp(scores - jnp.max(scores, axis=1, keepdims=True))
        chances = (raised / jnp.sum(raised, axis=1, keepdims=True)).astype(jnp.bfloat16)
        context[:, head * HD : (head + 1) * HD] = dot(chances, values).astype(jnp.bfloat16)
    to = lax.broadcasted_iota(jnp.int32, (tokens, tokens), 0)
    come = lax.broadcasted_iota(jnp.int32, (tokens, tokens), 1)
    half = tokens // sections
    section = jnp.where(to < half, 1 - section_pos, section_pos)
    inside = to % half
    row = jnp.zeros_like(to)
    width = jnp.zeros_like(to)
    first = 0
    for piece in pieces:
        at = inside - first * widths
        here = (at >= 0) & (at < piece * widths)
        row = jnp.where(here, first + at % piece, row)
        width = jnp.where(here, at // piece, width)
        first += piece
    move = come == (row * sections + section) * widths + width
    ordered = dot(jnp.where(move, 1.0, 0.0).astype(jnp.bfloat16), context[...])
    ordered = ordered.astype(jnp.bfloat16)
    for number in range(tiles):
        w_copies[number].wait()
        product = dot(ordered, weights[number]).astype(jnp.bfloat16)
        first = 0
        for out in outs:
            out[:, number * tile : (number + 1) * tile] = product[first : first + out.shape[0], :]
            first += out.shape[0]


def attend(place, slot_utt, frame_len, payloads, keys_values, weights, pieces, sections, widths):
    count = len(payloads)
    columns, width = weights.shape
    capacity = sum(pieces) * sections * widths
    tile = 1024
    tiles = width // tile
    shapes = [jax.ShapeDtypeStruct((piece * widths, width), jnp.bfloat16) for piece in pieces]
    shapes = shapes + shapes
    return pl.pallas_call(
        functools.partial(attention_kernel, count, capacity, pieces, sections, widths, tile),
        in_specs=[SCALARS] * 3 + [INSIDE] * (count + 1) + [ANYWHERE],
        out_specs=[INSIDE] * len(shapes),
        out_shape=shapes,
        scratch_shapes=[
            pltpu.VMEM((tiles, columns, tile), jnp.bfloat16),
            pltpu.VMEM((capacity, columns), jnp.bfloat16),
            pltpu.VMEM((capacity, columns), jnp.bfloat16),
            pltpu.SemaphoreType.DMA((tiles,)),
        ],
        cost_estimate=pl.CostEstimate(
            flops=2 * capacity * columns * (width + 2 * keys_values.shape[0]),
            bytes_accessed=2 * columns * width + 2 * capacity * width,
            transcendentals=capacity * keys_values.shape[0] * columns // HD,
        ),
        compiler_params=pltpu.CompilerParams(vmem_limit_bytes=24 << 20),
        name="attention_projection",
    )(place, slot_utt, frame_len, *payloads, keys_values, in_hbm(weights))


def norm_kernel(count, pieces, widths, place_ref, slot_ref, *refs):
    payloads, blocks = refs[:count], refs[count : count + len(pieces) * widths]
    out_ref, picked, total = refs[count + len(pieces) * widths :]
    rows, width = total.shape
    columns = picked.shape[1]
    share = picked.shape[0] // (width // columns + 1)
    source = distance_of_slot(place_ref, slot_ref, slot_ref.shape[0] // count)
    for distance in range(count):

        @pl.when(source == distance)
        def _(payload=payloads[distance]):
            picked[...] = payload[...]

    first = 0
    for number, piece in enumerate(pieces):
        mine = blocks[number * widths : (number + 1) * widths]
        summed = mine[0][...].astype(jnp.float32)
        for block in mine[1:]:
            summed += block[...].astype(jnp.float32)
        total[first : first + piece, :] = summed
        first += piece
    for part in range(width // columns):
        take = slice(part * columns, (part + 1) * columns)
        total[:, take] += picked[part * share : part * share + rows, :].astype(jnp.float32)
    out_ref[:, :width] = square_norm(total[...]).astype(jnp.bfloat16)
    last = width // columns * share
    out_ref[:, width:] = picked[last : last + rows, :LANES]


def normed_rows(place, slot_utt, payloads, blocks, pieces, widths):
    width = blocks[0].shape[1]
    rows = sum(pieces)
    return pl.pallas_call(
        functools.partial(norm_kernel, len(payloads), pieces, widths),
        in_specs=[SCALARS] * 2 + [INSIDE] * (len(payloads) + len(blocks)),
        out_specs=INSIDE,
        out_shape=jax.ShapeDtypeStruct((rows, width + LANES), jnp.bfloat16),
        scratch_shapes=[
            pltpu.VMEM(payloads[0].shape, jnp.bfloat16),
            pltpu.VMEM((rows, width), jnp.float32),
        ],
        compiler_params=pltpu.CompilerParams(vmem_limit_bytes=16 << 20),
        name="token_rows",
    )(place, slot_utt, *payloads, *blocks)


def vocabulary_kernel(tile, first_ref, *refs):
    sets, (head_ref, out_ref, rows_ref, stat) = refs[:-4], refs[-4:]
    vocab_rows, width = head_ref.shape
    share = sets[0].shape[0]
    tokens = share * len(sets)
    cell = lax.broadcasted_iota(jnp.int32, (8, LANES), 1)
    take = jnp.where(cell == 0, 256.0, jnp.where(cell == 1, 1.0, 0.0)).astype(jnp.bfloat16)
    for number, rows in enumerate(sets):
        rows_ref[number * share : (number + 1) * share, :] = rows[...]
    target = dot_nt(take, rows_ref[:, width:])[0:1, :].astype(jnp.int32) - first_ref[3]
    stat[0:1, :] = jnp.full((1, tokens), -jnp.inf, jnp.float32)
    stat[8:9, :] = jnp.zeros((1, tokens), jnp.float32)
    stat[16:17, :] = jnp.zeros((1, tokens), jnp.float32)

    @pl.loop(0, vocab_rows // tile)
    def _(step):
        start = pl.multiple_of(step * tile, tile)
        logits = dot_nt(head_ref[pl.ds(start, tile), :], rows_ref[:, :width])
        vocab = lax.broadcasted_iota(jnp.int32, logits.shape, 0) + start
        before = stat[0:1, :]
        upper = jnp.maximum(before, jnp.max(logits, axis=0, keepdims=True))
        stat[8:9, :] = stat[8:9, :] * jnp.exp(before - upper) + jnp.sum(
            jnp.exp(logits - upper), axis=0, keepdims=True
        )
        stat[16:17, :] += jnp.sum(jnp.where(vocab == target, logits, 0.0), axis=0, keepdims=True)
        stat[0:1, :] = upper

    for number in range(len(sets)):
        for row in range(3):
            out_ref[number, row : row + 1, :] = stat[
                8 * row : 8 * row + 1, number * share : (number + 1) * share
            ]


def vocabulary_stats(place, sets, head):
    share = sets[0].shape[0]
    count = len(sets)
    width = head.shape[1]
    tokens = share * count
    return pl.pallas_call(
        functools.partial(vocabulary_kernel, head.shape[0] // 2),
        in_specs=[SCALARS] + [INSIDE] * (count + 1),
        out_specs=INSIDE,
        out_shape=jax.ShapeDtypeStruct((count, 8, share), jnp.float32),
        scratch_shapes=[
            pltpu.VMEM((tokens, width + LANES), jnp.bfloat16),
            pltpu.VMEM((24, tokens), jnp.float32),
        ],
        cost_estimate=pl.CostEstimate(
            flops=3 * tokens * head.shape[0] * width,
            bytes_accessed=2 * tokens * width,
            transcendentals=tokens * head.shape[0],
        ),
        compiler_params=pltpu.CompilerParams(vmem_limit_bytes=16 << 20),
        name="vocabulary_scores",
    )(place, *sets, pltpu.with_memory_space_constraint(head, pltpu.VMEM))


def spread_kernel(sections, groups, widths, place_ref, slot_ref, *refs):
    stats, (out_ref, table, block) = refs[:-3], refs[-3:]
    share = table.shape[2]
    first = 0
    for stat in stats:
        table[first : first + stat.shape[0]] = stat[...]
        first += stat.shape[0]
    slots = slot_ref.shape[0] // groups
    block[...] = jnp.zeros_like(block)
    for group in range(groups):
        for slot in range(slots):
            utterance = jnp.maximum(slot_ref[group * slots + slot], 0)
            for section in range(sections):
                at = (section ^ place_ref[0]) * groups + (utterance ^ place_ref[1])
                block[group, 3 * slot : 3 * slot + 3, section * share : (section + 1) * share] = (
                    table[at][0:3, :]
                )
    for section in range(sections):
        for group in range(groups):
            for width in range(widths):
                out_ref[(section * groups + group) * widths + width] = block[group]


def spread_stats(place, slot_utt, stats, sections, groups, widths):
    share = stats[0].shape[2]
    assert 3 * slot_utt.shape[0] // groups <= 8
    return pl.pallas_call(
        functools.partial(spread_kernel, sections, groups, widths),
        in_specs=[SCALARS] * 2 + [INSIDE] * len(stats),
        out_specs=INSIDE,
        out_shape=jax.ShapeDtypeStruct(
            (sections * groups * widths, 8, sections * share), jnp.float32
        ),
        scratch_shapes=[
            pltpu.VMEM((sections * groups, 8, share), jnp.float32),
            pltpu.VMEM((groups, 8, sections * share), jnp.float32),
        ],
        compiler_params=pltpu.CompilerParams(vmem_limit_bytes=16 << 20),
        name="statistics_by_group",
    )(place, slot_utt, *stats)


def score_kernel(sections, widths, place_ref, slot_ref, length_ref, every_ref, out_ref):
    slots, hyps = out_ref.shape
    lanes = every_ref.shape[2]
    share = lanes // sections // widths
    lane = lax.broadcasted_iota(jnp.int32, (1, lanes), 1)
    order = lane % share * (sections * widths) + lane // share
    column = lax.broadcasted_iota(jnp.int32, (1, hyps), 1)
    for slot in range(slots):
        upper = every_ref[:, 3 * slot, :]
        peak = jnp.max(upper, axis=0, keepdims=True)
        total = jnp.sum(
            every_ref[:, 3 * slot + 1, :] * jnp.exp(upper - peak), axis=0, keepdims=True
        )
        picked = jnp.sum(every_ref[:, 3 * slot + 2, :], axis=0, keepdims=True)
        logp = picked - (peak + jnp.log(total))
        scores = jnp.zeros((1, hyps), jnp.float32)
        start = jnp.int32(0)
        for hyp in range(hyps):
            length = length_ref[slot * hyps + hyp]
            valid = (order >= start) & (order < start + length)
            summed = jnp.sum(jnp.where(valid, logp, 0.0), axis=1, keepdims=True)
            mean = summed / jnp.full((1, 1), length, jnp.int32).astype(jnp.float32)
            scores = jnp.where(column == hyp, mean + math.log(V), scores)
            start = start + length
        filled = slot_ref[place_ref[1] * slots + slot] >= 0
        out_ref[slot : slot + 1, :] = jnp.where(filled, scores, 0.0)


def hypothesis_scores(place, slot_utt, lengths, every, slots, hyps, sections, widths):
    return pl.pallas_call(
        functools.partial(score_kernel, sections, widths),
        in_specs=[SCALARS] * 3 + [INSIDE],
        out_specs=INSIDE,
        out_shape=jax.ShapeDtypeStruct((slots, hyps), jnp.float32),
        compiler_params=pltpu.CompilerParams(vmem_limit_bytes=16 << 20),
        name="hypothesis_scores",
    )(place, slot_utt, lengths, every)


def near_device(
    frame_len,
    slot_utt,
    enc_in,
    ffn_up,
    ffn_down,
    kv_proj,
    hyp_state,
    hyp_tok,
    hyp_len,
    q_proj,
    o_proj,
    head,
):
    section_count = lax.axis_size("section")
    group_count = lax.axis_size("tm")
    width_count = lax.axis_size("mp")
    section_pos = lax.axis_index("section")
    group_pos = lax.axis_index("tm")
    width_pos = lax.axis_index("mp")
    head_devices = section_count * width_count
    all_devices = head_devices * group_count

    frame_rows, utterances, enc_width = enc_in.shape
    slot_count, hyp_count, positions, model_width = hyp_state.shape
    slot_tokens = hyp_count * positions
    share_rows = slot_tokens // head_devices
    vocab_start = (
        (section_pos * group_count + group_pos) * width_count + width_pos
    ) * head.shape[0]
    head_pos = section_pos * width_count + width_pos
    place = jnp.stack([section_pos, group_pos, width_pos, vocab_start, head_pos])
    place = place.astype(jnp.int32)
    lengths = hyp_len.reshape(-1)

    parts = ffn(
        place, enc_in.reshape(frame_rows * utterances, enc_width), ffn_up, ffn_down, width_count
    )
    own_frames = parts[width_count]
    parts = [parts[0]] + [
        swap(parts[distance], "mp", distance) for distance in range(1, width_count)
    ]

    blocks = queries_of(
        place,
        slot_utt,
        lengths,
        hyp_state.reshape(slot_count, slot_tokens, model_width),
        hyp_tok.reshape(slot_count, 1, slot_tokens),
        q_proj,
        group_count,
        share_rows,
    )
    payloads = [blocks[0]] + [
        swap(blocks[distance], "tm", distance) for distance in range(1, group_count)
    ]
    shares = blocks[group_count:]

    sent = keys_values_of(parts, own_frames, kv_proj, section_count, utterances, width_count)
    frames_all = all_devices * (frame_rows // width_count)
    keys_values = exchange(sent.reshape(all_devices, -1, 2 * HD), ALL).reshape(frames_all, 2 * HD)
    keys_values, *shares = lax.optimization_barrier((keys_values, *shares))
    shares = [shares[0]] + [
        swap(shares[distance], "tm", distance) for distance in range(1, group_count)
    ]

    pieces = (share_rows // 2, share_rows - share_rows // 2)
    projected = attend(
        place,
        slot_utt,
        frame_len,
        payloads,
        keys_values,
        o_proj,
        pieces,
        section_count,
        width_count,
    )
    sums = []
    for number, piece in enumerate(pieces):
        other = swap(projected[number], "section", 1)
        section_sum = (
            projected[len(pieces) + number].astype(jnp.float32) + other.astype(jnp.float32)
        ).astype(jnp.bfloat16)
        for distance in range(width_count):
            block = lax.dynamic_slice_in_dim(
                section_sum, (width_pos ^ distance) * piece, piece, 0
            )
            sums.append(swap(block, "mp", distance) if distance else block)
    out_rows = normed_rows(place, slot_utt, shares, sums, pieces, width_count)

    share = out_rows.shape[0]
    own = jnp.zeros((width_count * share, out_rows.shape[1]), jnp.bfloat16)
    for distance in range(width_count):
        block = swap(out_rows, "mp", distance) if distance else out_rows
        own = lax.dynamic_update_slice_in_dim(own, block, (width_pos ^ distance) * share, 0)
    half = own.shape[0] // 2
    by_x = swap(own, "section", 1)
    by_y = swap(own, "tm", 2)
    across = jnp.concatenate([swap(by_x[:half], "tm", 2), swap(by_y[half:], "section", 1)])
    stats = [
        vocabulary_stats(place, [own, swap(own, "tm", 1)], head),
        vocabulary_stats(place, [by_y, swap(by_y, "tm", 1), by_x, swap(by_x, "tm", 1)], head),
        vocabulary_stats(place, [across, swap(across, "tm", 1)], head),
    ]

    every = exchange(
        spread_stats(place, slot_utt, stats, section_count, group_count, width_count), ALL
    )
    return hypothesis_scores(
        place, slot_utt, lengths, every, slot_count, hyp_count, section_count, width_count
    )


def general(
    frame_len,
    slot_utt,
    enc_in,
    ffn_up,
    ffn_down,
    kv_proj,
    hyp_state,
    hyp_tok,
    hyp_len,
    q_proj,
    o_proj,
    head,
):
    section_count = lax.axis_size("section")
    group_count = lax.axis_size("tm")
    width_count = lax.axis_size("mp")
    section_pos = lax.axis_index("section")
    group_pos = lax.axis_index("tm")
    width_pos = lax.axis_index("mp")
    head_devices = section_count * width_count
    head_pos = section_pos * width_count + width_pos
    all_devices = head_devices * group_count

    frame_rows, utterances, enc_width = enc_in.shape
    assert utterances == group_count
    slot_count, hyp_count, positions, model_width = hyp_state.shape
    slot_tokens = hyp_count * positions
    device_heads = q_proj.shape[1] // HD
    group_heads = NH // KVH
    frame_share = frame_rows // width_count
    share_rows = slot_tokens // head_devices
    here_slots = lax.dynamic_slice_in_dim(slot_utt, group_pos * slot_count, slot_count, 0)

    dec_rows = hyp_state.reshape(slot_count * slot_tokens, model_width).astype(jnp.float32)
    queries = jnp.dot(
        square_norm(dec_rows).astype(jnp.bfloat16), q_proj, preferred_element_type=jnp.float32
    ).astype(jnp.bfloat16)
    queries = queries.reshape(slot_count, slot_tokens, device_heads * HD)
    shares = lax.dynamic_slice_in_dim(
        hyp_state.reshape(slot_count, slot_tokens, model_width), head_pos * share_rows, share_rows, 1
    )

    def by_utterance(values):
        out = []
        for utterance in range(utterances):
            block = values[0]
            for slot in range(1, slot_count):
                block = jnp.where(here_slots[slot] == utterance, values[slot], block)
            out.append(block)
        return jnp.stack(out)

    own_slot = jnp.argmax(slot_utt == group_pos)
    from_group = own_slot // slot_count
    queries = lax.dynamic_index_in_dim(
        exchange(by_utterance(queries), "tm"), from_group, 0, keepdims=False
    )
    resid_rows = lax.dynamic_index_in_dim(
        exchange(by_utterance(shares), "tm"), from_group, 0, keepdims=False
    )
    slot_targets = lax.all_gather(
        hyp_tok.reshape(slot_count, slot_tokens), "tm", axis=0, tiled=True
    )
    utt_slots = jnp.argmax(slot_utt[None, :] == jnp.arange(utterances)[:, None], axis=1)
    targets = jnp.take(slot_targets, utt_slots, axis=0).reshape(utterances * slot_tokens)

    enc_flat = (
        enc_in.reshape(width_count, frame_share, utterances, enc_width)
        .transpose(0, 2, 1, 3)
        .reshape(frame_rows * utterances, enc_width)
    )
    share_count = frame_share * utterances
    enc_normed = layer_norm(enc_flat.astype(jnp.float32)).astype(jnp.bfloat16)
    enc_inner = jax.nn.gelu(
        jnp.dot(enc_normed, ffn_up, preferred_element_type=jnp.float32), approximate=False
    ).astype(jnp.bfloat16)
    enc_summed = scatter_sum(
        jnp.dot(enc_inner, ffn_down, preferred_element_type=jnp.float32).astype(jnp.bfloat16),
        "mp",
        width_count,
    )
    own_frames = lax.dynamic_slice_in_dim(enc_flat, width_pos * share_count, share_count, 0)
    enc_states = layer_norm(own_frames.astype(jnp.float32) + enc_summed).astype(jnp.bfloat16)
    keys_values = jnp.dot(enc_states, kv_proj, preferred_element_type=jnp.float32).astype(
        jnp.bfloat16
    )
    keys_values = keys_values.reshape(utterances, frame_share, 2, KVH, HD)
    sent = []
    for section in range(section_count):
        per_width = []
        for width in range(width_count):
            kv_head = (section * width_count + width) * device_heads // group_heads
            per_width.append(
                keys_values[:, :, :, kv_head].reshape(utterances, frame_share, 2 * HD)
            )
        sent.append(jnp.stack(per_width, axis=1))
    sent = jnp.stack(sent).reshape(all_devices, frame_share, 2 * HD)
    frames_all = all_devices * frame_share
    keys_values = exchange(sent, ALL).reshape(frames_all, 2 * HD)

    frame_limit = lax.dynamic_index_in_dim(frame_len, group_pos, 0, keepdims=False)
    queries = queries.reshape(slot_tokens, device_heads, HD)
    scores = jnp.einsum(
        "qhd,fd->hqf", queries, keys_values[:, :HD], preferred_element_type=jnp.float32
    ) / math.sqrt(HD)
    visible = jnp.arange(frames_all, dtype=jnp.int32) < frame_limit
    scores = jnp.where(visible[None, None, :], scores, -jnp.inf)
    weights = jax.nn.softmax(scores, axis=-1).astype(jnp.bfloat16)
    context = jnp.einsum(
        "hqf,fd->qhd", weights, keys_values[:, HD:], preferred_element_type=jnp.float32
    ).astype(jnp.bfloat16)
    partial = jnp.dot(
        context.reshape(slot_tokens, device_heads * HD), o_proj, preferred_element_type=jnp.float32
    ).astype(jnp.bfloat16)
    partial = scatter_sum(partial, "section", section_count).astype(jnp.bfloat16)
    attn_out = scatter_sum(partial, "mp", width_count)
    out_normed = square_norm(resid_rows.astype(jnp.float32) + attn_out).astype(jnp.bfloat16)

    hidden_rows = lax.all_gather(out_normed, ALL, axis=0, tiled=True)
    logits = lax.dot_general(
        hidden_rows, head, (((1,), (1,)), ((), ())), preferred_element_type=jnp.float32
    )
    vocab_rows = head.shape[0]
    vocab_start = (
        (section_pos * group_count + group_pos) * width_count + width_pos
    ) * vocab_rows
    target_rows = (
        targets.reshape(utterances, section_count, width_count, share_rows)
        .transpose(1, 0, 2, 3)
        .reshape(-1)
    )
    upper = jnp.max(logits, axis=1)
    totals = jnp.sum(jnp.exp(logits - upper[:, None]), axis=1)
    matches = (
        jnp.arange(vocab_rows, dtype=jnp.int32)[None, :] == (target_rows - vocab_start)[:, None]
    )
    target_logit = jnp.sum(jnp.where(matches, logits, 0.0), axis=1)

    stats = jnp.stack([upper, totals, target_logit])
    stats = stats.reshape(3, section_count, utterances, width_count, share_rows)
    stats = stats.transpose(2, 0, 1, 3, 4).reshape(utterances, 3, slot_tokens)
    by_slot = jnp.take(stats, jnp.maximum(slot_utt, 0), axis=0)
    by_group = by_slot.reshape(1, group_count, 1, slot_count, 3, slot_tokens)
    by_group = jnp.broadcast_to(
        by_group, (section_count, group_count, width_count, slot_count, 3, slot_tokens)
    ).reshape(all_devices, slot_count, 3, slot_tokens)
    every = exchange(by_group, ALL)
    peak = jnp.max(every[:, :, 0], axis=0)
    total = jnp.sum(every[:, :, 1] * jnp.exp(every[:, :, 0] - peak[None]), axis=0)
    picked = jnp.sum(every[:, :, 2], axis=0)
    token_logp = (picked - (peak + jnp.log(total))).reshape(slot_count, hyp_count, positions)
    valid = jnp.arange(positions, dtype=jnp.int32)[None, None, :] < hyp_len[:, :, None]
    summed = jnp.sum(jnp.where(valid, token_logp, 0.0), axis=-1) / hyp_len.astype(
        jnp.float32
    ) + math.log(V)
    return jnp.where(here_slots[:, None] >= 0, summed, 0.0)


def solution(mesh):
    in_specs = (
        P(),
        P(),
        P(("section", "tm"), None, None),
        P(None, "mp"),
        P("mp", None),
        P(),
        P("tm", None, None, None),
        P("tm", None, None),
        P("tm", None),
        P(None, ("section", "mp")),
        P(("section", "mp"), None),
        P(("section", "tm", "mp"), None),
    )
    out_specs = P("tm", None)
    near = dict(mesh.shape) == {"section": 2, "tm": 4, "mp": 4}
    per_device = near_device if near else general
    return jax.shard_map(
        per_device, mesh=mesh, in_specs=in_specs, out_specs=out_specs, check_vma=False
    )
```

```python
import functools
import math

import jax
import jax.numpy as jnp
from jax import lax
from jax.experimental import pallas as pl
from jax.experimental.pallas import tpu as pltpu
from jax.sharding import PartitionSpec as P

NH = 32
KVH = 4
HD = 128
V = 64000
ALL = ("section", "tm", "mp")
LANES = 128


def layer_norm(values):
    center = values - jnp.mean(values, axis=-1, keepdims=True)
    spread = jnp.mean(center * center, axis=-1, keepdims=True)
    return center * lax.rsqrt(spread + 1e-05)


def square_norm(values):
    return values * lax.rsqrt(jnp.mean(values * values, axis=-1, keepdims=True) + 1e-06)


def exchange(blocks, axis):
    return lax.all_to_all(blocks, axis, split_axis=0, concat_axis=0, tiled=True)


def scatter_sum(partial, axis, count):
    blocks = partial.reshape((count, partial.shape[0] // count) + partial.shape[1:])
    return jnp.sum(exchange(blocks, axis).astype(jnp.float32), axis=0)


def swap(values, axis, distance):
    pairs = [(i, i ^ distance) for i in range(lax.axis_size(axis))]
    return lax.ppermute(values, axis, pairs)


def whole(shape):
    return pl.BlockSpec(shape, lambda *_: (0,) * len(shape))


SCALARS = pl.BlockSpec(memory_space=pltpu.SMEM)


def dot(left, right):
    return jnp.dot(left, right, preferred_element_type=jnp.float32)


def dot_nt(left, right):
    return lax.dot_general(
        left, right, (((1,), (1,)), ((), ())), preferred_element_type=jnp.float32
    )


def start_copies(source_of, target_of, semaphores, count):
    copies = []
    for number in range(count):
        copy = pltpu.make_async_copy(
            source_of(number), target_of(number), semaphores.at[number]
        )
        copy.start()
        copies.append(copy)
    return copies


def ffn_kernel(count, tile, place_ref, x_ref, up_ref, down_ref, *refs):
    outs, (own_ref, total, up, down, up_sem, down_sem) = refs[:count], refs[count:]
    share = own_ref.shape[0]
    tiles = up_ref.shape[1] // tile
    up_copies = start_copies(
        lambda i: up_ref.at[:, pl.ds(i * tile, tile)], lambda i: up.at[i], up_sem, tiles
    )
    down_copies = start_copies(
        lambda i: down_ref.at[pl.ds(i * tile, tile), :], lambda i: down.at[i], down_sem, tiles
    )
    here = place_ref[2]
    own_ref[...] = x_ref[pl.ds(pl.multiple_of(here * share, share), share), :]
    normed = layer_norm(x_ref[...].astype(jnp.float32)).astype(jnp.bfloat16)
    for number in range(tiles):
        up_copies[number].wait()
        hidden = dot(normed, up[number])
        inner = 0.5 * hidden * (1.0 + lax.erf(hidden * math.sqrt(0.5)))
        down_copies[number].wait()
        product = dot(inner.astype(jnp.bfloat16), down[number])
        if number == 0:
            total[...] = product
        else:
            total[...] += product
    for distance in range(count):
        start = pl.multiple_of((here ^ distance) * share, share)
        outs[distance][...] = total[pl.ds(start, share), :].astype(jnp.bfloat16)


def in_hbm(values):
    return pltpu.with_memory_space_constraint(values, pltpu.HBM)


ANYWHERE = pl.BlockSpec(memory_space=pl.ANY)
INSIDE = pl.BlockSpec(memory_space=pltpu.VMEM)


def ffn(place, rows, up, down, count):
    share = rows.shape[0] // count
    width = rows.shape[1]
    tile = 256
    tiles = up.shape[1] // tile
    block = jax.ShapeDtypeStruct((share, width), jnp.bfloat16)
    return pl.pallas_call(
        functools.partial(ffn_kernel, count, tile),
        in_specs=[SCALARS, INSIDE, ANYWHERE, ANYWHERE],
        out_specs=[INSIDE] * (count + 1),
        out_shape=[block] * (count + 1),
        scratch_shapes=[
            pltpu.VMEM(rows.shape, jnp.float32),
            pltpu.VMEM((tiles, width, tile), jnp.bfloat16),
            pltpu.VMEM((tiles, tile, width), jnp.bfloat16),
            pltpu.SemaphoreType.DMA((tiles,)),
            pltpu.SemaphoreType.DMA((tiles,)),
        ],
        cost_estimate=pl.CostEstimate(
            flops=4 * rows.shape[0] * width * up.shape[1],
            bytes_accessed=4 * width * up.shape[1],
            transcendentals=rows.shape[0] * up.shape[1],
        ),
        compiler_params=pltpu.CompilerParams(vmem_limit_bytes=24 << 20),
        name="encoder_ffn",
    )(place, rows, in_hbm(up), in_hbm(down))


def query_kernel(
    count, depth, place_ref, slot_ref, length_ref, after_ref, x_ref, tok_ref, w_ref, *refs
):
    outs, (states, weights, normed, total, shares, x_sem, w_sem) = refs[:count], refs[count:]
    slots, tokens, width = x_ref.shape
    hyps = length_ref.shape[0] // slots
    positions = tokens // hyps
    columns = w_ref.shape[1]
    share = shares.shape[1] // 2
    parts = width // columns
    x_copies = start_copies(lambda i: x_ref.at[i], lambda i: states.at[i], x_sem, slots)
    w_copies = start_copies(
        lambda i: w_ref.at[pl.ds(i * depth, depth), :],
        lambda i: weights.at[i],
        w_sem,
        width // depth,
    )
    head_pos = place_ref[4]
    lane = lax.broadcasted_iota(jnp.int32, (1, tokens), 1)
    for slot in range(slots):
        order = jnp.full((1, tokens), -1, jnp.int32)
        start = jnp.int32(0)
        for hyp in range(hyps):
            length = length_ref[slot * hyps + hyp]
            inside = (lane >= hyp * positions) & (lane < hyp * positions + length)
            order = jnp.where(inside, lane - hyp * positions + start, order)
            start = start + length
        row = lax.broadcasted_iota(jnp.int32, (tokens, tokens), 0)
        move = jnp.where(order == row, 1.0, 0.0).astype(jnp.bfloat16)
        x_copies[slot].wait()
        ordered = dot(move, states[slot])
        normed[slot * tokens : (slot + 1) * tokens, :] = square_norm(ordered).astype(jnp.bfloat16)
        share_row = lax.broadcasted_iota(jnp.int32, (share, tokens), 0)
        chosen = order == share_row * (tokens // share) + head_pos
        mine = dot(jnp.where(chosen, 1.0, 0.0).astype(jnp.bfloat16), states[slot])
        shares[slot, :share, :] = mine.astype(jnp.bfloat16)
        target = jnp.sum(
            jnp.where(chosen, tok_ref[slot], 0), axis=1, keepdims=True, dtype=jnp.int32
        )
        coarse = target // 256
        cell = lax.broadcasted_iota(jnp.int32, (share, columns), 1)
        packed = jnp.where(cell == 0, coarse, jnp.where(cell == 1, target - coarse * 256, 0))
        shares[slot, share:, :columns] = packed.astype(jnp.float32).astype(jnp.bfloat16)
    for number in range(width // depth):
        w_copies[number].wait()
        product = dot(normed[:, number * depth : (number + 1) * depth], weights[number])
        if number == 0:
            total[...] = product
        else:
            total[...] += product
    group = place_ref[1]
    for distance in range(count):
        slot = jnp.int32(0)
        for candidate in range(1, slots):
            holds = slot_ref[group * slots + candidate] == group ^ distance
            slot = jnp.where(holds, candidate, slot)
        start = pl.multiple_of(slot * tokens, tokens)
        out = outs[distance]
        out[:tokens, :] = total[pl.ds(start, tokens), :].astype(jnp.bfloat16)
        for part in range(parts):
            first = tokens + part * share
            out[first : first + share, :] = shares[
                slot, :share, part * columns : (part + 1) * columns
            ]
        out[tokens + parts * share :, :] = shares[slot, share:, :columns]


def queries_of(place, slot_utt, lengths, after, states, targets, weights, count, share):
    slots, tokens, width = states.shape
    columns = weights.shape[1]
    depth = 1024
    rows = tokens + (width // columns + 1) * share
    block = jax.ShapeDtypeStruct((rows, columns), jnp.bfloat16)
    return pl.pallas_call(
        functools.partial(query_kernel, count, depth),
        in_specs=[SCALARS] * 3 + [ANYWHERE, ANYWHERE, INSIDE, ANYWHERE],
        out_specs=[INSIDE] * count,
        out_shape=[block] * count,
        scratch_shapes=[
            pltpu.VMEM(states.shape, jnp.bfloat16),
            pltpu.VMEM((width // depth, depth, columns), jnp.bfloat16),
            pltpu.VMEM((slots * tokens, width), jnp.bfloat16),
            pltpu.VMEM((slots * tokens, columns), jnp.float32),
            pltpu.VMEM((slots, 2 * share, width), jnp.bfloat16),
            pltpu.SemaphoreType.DMA((slots,)),
            pltpu.SemaphoreType.DMA((width // depth,)),
        ],
        cost_estimate=pl.CostEstimate(
            flops=2 * slots * tokens * width * columns,
            bytes_accessed=2 * width * (columns + slots * tokens),
            transcendentals=0,
        ),
        compiler_params=pltpu.CompilerParams(vmem_limit_bytes=32 << 20),
        name="hypothesis_queries",
    )(place, slot_utt, lengths, after, in_hbm(states), targets, in_hbm(weights))


def kv_kernel(sections, utterances, widths, *refs):
    parts, (own_ref, w_ref, after_ref, out_ref) = refs[:-4], refs[-4:]
    rows = own_ref.shape[0]
    frames = rows // utterances
    total = own_ref[...].astype(jnp.float32)
    summed = parts[0][...].astype(jnp.float32)
    for part in parts[1:]:
        summed += part[...].astype(jnp.float32)
    states = layer_norm(total + summed).astype(jnp.bfloat16)
    to = lax.broadcasted_iota(jnp.int32, (rows, rows), 0)
    come = lax.broadcasted_iota(jnp.int32, (rows, rows), 1)
    move = jnp.where(come == to % frames * utterances + to // frames, 1.0, 0.0)
    states = dot(move.astype(jnp.bfloat16), states).astype(jnp.bfloat16)
    both = dot(states, w_ref[...])
    half = KVH * HD
    per_kv = sections * widths // KVH
    for section in range(sections):
        for utterance in range(utterances):
            for width in range(0, widths, per_kv):
                kv_head = (section * widths + width) // per_kv
                take = slice(utterance * frames, (utterance + 1) * frames)
                block = jnp.concatenate(
                    [
                        both[take, kv_head * HD : (kv_head + 1) * HD],
                        both[take, half + kv_head * HD : half + (kv_head + 1) * HD],
                    ],
                    axis=1,
                )
                start = ((section * utterances + utterance) * widths + width) * frames
                block = jnp.concatenate([block] * per_kv, axis=0).astype(jnp.bfloat16)
                out_ref[start : start + per_kv * frames, :] = block


def keys_values_of(parts, own, weights, after, sections, utterances, widths):
    rows = sections * widths * own.shape[0]
    return pl.pallas_call(
        functools.partial(kv_kernel, sections, utterances, widths),
        in_specs=[INSIDE] * (len(parts) + 2) + [ANYWHERE],
        out_specs=INSIDE,
        out_shape=jax.ShapeDtypeStruct((rows, 2 * HD), jnp.bfloat16),
        cost_estimate=pl.CostEstimate(
            flops=2 * own.shape[0] * weights.shape[0] * weights.shape[1],
            bytes_accessed=2 * weights.shape[0] * weights.shape[1],
            transcendentals=0,
        ),
        compiler_params=pltpu.CompilerParams(vmem_limit_bytes=24 << 20),
        name="frame_keys_values",
    )(*parts, own, weights, after)


def choice_of_payload(place_ref, slot_ref, slots):
    group = place_ref[1]
    source = jnp.int32(0)
    for slot in range(slot_ref.shape[0]):
        source = jnp.where(slot_ref[slot] == group, slot // slots, source)
    return jnp.minimum(source ^ group, 2)


def attention_kernel(count, slots, capacity, pieces, sections, widths, tile, *refs):
    place_ref, slot_ref, frame_ref = refs[:3]
    payloads, (kv_ref, w_ref) = refs[3 : 3 + count], refs[3 + count : 5 + count]
    outs = refs[5 + count : 5 + count + 2 * len(pieces)]
    weights, picked, context, w_sem = refs[5 + count + 2 * len(pieces) :]
    tokens, columns = capacity, w_ref.shape[0]
    tiles = w_ref.shape[1] // tile
    w_copies = start_copies(
        lambda i: w_ref.at[:, pl.ds(i * tile, tile)], lambda i: weights.at[i], w_sem, tiles
    )
    source = choice_of_payload(place_ref, slot_ref, slots)
    section_pos = place_ref[0]
    frame_limit = frame_ref[place_ref[1]]
    for distance in range(count):

        @pl.when(source == distance)
        def _(payload=payloads[distance]):
            picked[...] = payload[:tokens, :]

    keys = kv_ref[:, :HD]
    values = kv_ref[:, HD:]
    frames = kv_ref.shape[0]
    visible = lax.broadcasted_iota(jnp.int32, (tokens, frames), 1) < frame_limit
    for head in range(columns // HD):
        scores = dot_nt(picked[:, head * HD : (head + 1) * HD], keys) * (1.0 / math.sqrt(HD))
        scores = jnp.where(visible, scores, -jnp.inf)
        raised = jnp.exp(scores - jnp.max(scores, axis=1, keepdims=True))
        chances = (raised / jnp.sum(raised, axis=1, keepdims=True)).astype(jnp.bfloat16)
        context[:, head * HD : (head + 1) * HD] = dot(chances, values).astype(jnp.bfloat16)
    to = lax.broadcasted_iota(jnp.int32, (tokens, tokens), 0)
    come = lax.broadcasted_iota(jnp.int32, (tokens, tokens), 1)
    half = tokens // sections
    section = jnp.where(to < half, 1 - section_pos, section_pos)
    inside = to % half
    row = jnp.zeros_like(to)
    width = jnp.zeros_like(to)
    first = 0
    for piece in pieces:
        at = inside - first * widths
        here = (at >= 0) & (at < piece * widths)
        row = jnp.where(here, first + at % piece, row)
        block = at // piece
        width = jnp.where(here, block % 2 * (widths // 2) + block // 2, width)
        first += piece
    move = come == (row * sections + section) * widths + width
    ordered = dot(jnp.where(move, 1.0, 0.0).astype(jnp.bfloat16), context[...])
    ordered = ordered.astype(jnp.bfloat16)
    for number in range(tiles):
        w_copies[number].wait()
        product = dot(ordered, weights[number]).astype(jnp.bfloat16)
        first = 0
        for out in outs:
            out[:, number * tile : (number + 1) * tile] = product[first : first + out.shape[0], :]
            first += out.shape[0]


def attend(place, slot_utt, frame_len, payloads, keys_values, weights, pieces, sections, widths, slots):
    count = len(payloads)
    columns, width = weights.shape
    capacity = sum(pieces) * sections * widths
    tile = 1024
    tiles = width // tile
    shapes = [jax.ShapeDtypeStruct((piece * widths, width), jnp.bfloat16) for piece in pieces]
    shapes = shapes + shapes
    return pl.pallas_call(
        functools.partial(
            attention_kernel, count, slots, capacity, pieces, sections, widths, tile
        ),
        in_specs=[SCALARS] * 3 + [INSIDE] * (count + 1) + [ANYWHERE],
        out_specs=[INSIDE] * len(shapes),
        out_shape=shapes,
        scratch_shapes=[
            pltpu.VMEM((tiles, columns, tile), jnp.bfloat16),
            pltpu.VMEM((capacity, columns), jnp.bfloat16),
            pltpu.VMEM((capacity, columns), jnp.bfloat16),
            pltpu.SemaphoreType.DMA((tiles,)),
        ],
        cost_estimate=pl.CostEstimate(
            flops=2 * capacity * columns * (width + 2 * keys_values.shape[0]),
            bytes_accessed=2 * columns * width + 2 * capacity * width,
            transcendentals=capacity * keys_values.shape[0] * columns // HD,
        ),
        compiler_params=pltpu.CompilerParams(vmem_limit_bytes=24 << 20),
        name="attention_projection",
    )(place, slot_utt, frame_len, *payloads, keys_values, in_hbm(weights))


def norm_kernel(count, slots, tokens, pieces, place_ref, slot_ref, after_ref, *refs):
    payloads, blocks = refs[:count], refs[count : count + 2 * len(pieces)]
    out_ref, picked, total = refs[count + 2 * len(pieces) :]
    rows, width = total.shape
    columns = picked.shape[1]
    share = picked.shape[0] // (width // columns + 1)
    source = choice_of_payload(place_ref, slot_ref, slots)
    for choice in range(count):

        @pl.when(source == choice)
        def _(payload=payloads[choice]):
            picked[...] = payload[tokens:, :]

    first = 0
    for number, piece in enumerate(pieces):
        kept, other = blocks[2 * number : 2 * number + 2]
        total[first : first + piece, :] = kept[...] + other[...].astype(jnp.float32)
        first += piece
    for part in range(width // columns):
        take = slice(part * columns, (part + 1) * columns)
        total[:, take] += picked[part * share : part * share + rows, :].astype(jnp.float32)
    out_ref[:, :width] = square_norm(total[...]).astype(jnp.bfloat16)
    last = width // columns * share
    out_ref[:, width:] = picked[last : last + rows, :LANES]


def normed_rows(place, slot_utt, after, payloads, blocks, pieces, tokens, slots):
    width = blocks[0].shape[1]
    rows = sum(pieces)
    columns = payloads[0].shape[1]
    return pl.pallas_call(
        functools.partial(norm_kernel, len(payloads), slots, tokens, pieces),
        in_specs=[SCALARS] * 2 + [ANYWHERE] + [INSIDE] * (len(payloads) + len(blocks)),
        out_specs=INSIDE,
        out_shape=jax.ShapeDtypeStruct((rows, width + LANES), jnp.bfloat16),
        scratch_shapes=[
            pltpu.VMEM((payloads[0].shape[0] - tokens, columns), jnp.bfloat16),
            pltpu.VMEM((rows, width), jnp.float32),
        ],
        compiler_params=pltpu.CompilerParams(vmem_limit_bytes=16 << 20),
        name="token_rows",
    )(place, slot_utt, after, *payloads, *blocks)


def load_kernel(rows, after_ref, head_ref, out_ref, token_ref, semaphores):
    count = head_ref.shape[0] // rows
    copies = start_copies(
        lambda i: head_ref.at[pl.ds(i * rows, rows), :],
        lambda i: out_ref.at[pl.ds(i * rows, rows), :],
        semaphores,
        count,
    )
    token_ref[...] = jnp.zeros_like(token_ref)
    for copy in copies:
        copy.wait()


def load_head(after, head):
    rows = head.shape[0] // 5
    return pl.pallas_call(
        functools.partial(load_kernel, rows),
        in_specs=[ANYWHERE, ANYWHERE],
        out_specs=[INSIDE, INSIDE],
        out_shape=[
            pltpu.VMEM(head.shape, head.dtype),
            jax.ShapeDtypeStruct((8, LANES), jnp.float32),
        ],
        scratch_shapes=[pltpu.SemaphoreType.DMA((5,))],
        cost_estimate=pl.CostEstimate(
            flops=0, bytes_accessed=2 * head.size, transcendentals=0
        ),
        compiler_params=pltpu.CompilerParams(vmem_limit_bytes=20 << 20),
        name="vocabulary_rows",
    )(after, in_hbm(head))


def vocabulary_kernel(tile, first_ref, *refs):
    sets, (head_ref, out_ref, rows_ref, stat) = refs[:-4], refs[-4:]
    vocab_rows, width = head_ref.shape
    share = sets[0].shape[0]
    tokens = share * len(sets)
    cell = lax.broadcasted_iota(jnp.int32, (8, LANES), 1)
    take = jnp.where(cell == 0, 256.0, jnp.where(cell == 1, 1.0, 0.0)).astype(jnp.bfloat16)
    for number, rows in enumerate(sets):
        rows_ref[number * share : (number + 1) * share, :] = rows[...]
    target = dot_nt(take, rows_ref[:, width:])[0:1, :].astype(jnp.int32) - first_ref[3]
    stat[0:1, :] = jnp.full((1, tokens), -jnp.inf, jnp.float32)
    stat[8:9, :] = jnp.zeros((1, tokens), jnp.float32)
    stat[16:17, :] = jnp.zeros((1, tokens), jnp.float32)

    @pl.loop(0, vocab_rows // tile)
    def _(step):
        start = pl.multiple_of(step * tile, tile)
        logits = dot_nt(head_ref[pl.ds(start, tile), :], rows_ref[:, :width])
        vocab = lax.broadcasted_iota(jnp.int32, logits.shape, 0) + start
        before = stat[0:1, :]
        upper = jnp.maximum(before, jnp.max(logits, axis=0, keepdims=True))
        stat[8:9, :] = stat[8:9, :] * jnp.exp(before - upper) + jnp.sum(
            jnp.exp(logits - upper), axis=0, keepdims=True
        )
        stat[16:17, :] += jnp.sum(jnp.where(vocab == target, logits, 0.0), axis=0, keepdims=True)
        stat[0:1, :] = upper

    for number in range(len(sets)):
        for row in range(3):
            out_ref[number, row : row + 1, :] = stat[
                8 * row : 8 * row + 1, number * share : (number + 1) * share
            ]


def vocabulary_stats(place, sets, head):
    share = sets[0].shape[0]
    count = len(sets)
    width = head.shape[1]
    tokens = share * count
    return pl.pallas_call(
        functools.partial(vocabulary_kernel, head.shape[0] // 2),
        in_specs=[SCALARS] + [INSIDE] * (count + 1),
        out_specs=INSIDE,
        out_shape=jax.ShapeDtypeStruct((count, 8, share), jnp.float32),
        scratch_shapes=[
            pltpu.VMEM((tokens, width + LANES), jnp.bfloat16),
            pltpu.VMEM((24, tokens), jnp.float32),
        ],
        cost_estimate=pl.CostEstimate(
            flops=3 * tokens * head.shape[0] * width,
            bytes_accessed=2 * tokens * width,
            transcendentals=tokens * head.shape[0],
        ),
        compiler_params=pltpu.CompilerParams(vmem_limit_bytes=16 << 20),
        name="vocabulary_scores",
    )(place, *sets, pltpu.with_memory_space_constraint(head, pltpu.VMEM))


def spread_kernel(sections, groups, widths, place_ref, slot_ref, *refs):
    stats, (out_ref, table, block) = refs[:-3], refs[-3:]
    share = table.shape[2]
    first = 0
    for stat in stats:
        table[first : first + stat.shape[0]] = stat[...]
        first += stat.shape[0]
    slots = slot_ref.shape[0] // groups
    block[...] = jnp.zeros_like(block)
    for group in range(groups):
        for slot in range(slots):
            utterance = jnp.maximum(slot_ref[group * slots + slot], 0)
            for section in range(sections):
                at = (section ^ place_ref[0]) * groups + (utterance ^ place_ref[1])
                block[group, 3 * slot : 3 * slot + 3, section * share : (section + 1) * share] = (
                    table[at][0:3, :]
                )
    for section in range(sections):
        for group in range(groups):
            for width in range(widths):
                out_ref[(section * groups + group) * widths + width] = block[group]


def spread_stats(place, slot_utt, stats, sections, groups, widths):
    share = stats[0].shape[2]
    assert 3 * slot_utt.shape[0] // groups <= 8
    return pl.pallas_call(
        functools.partial(spread_kernel, sections, groups, widths),
        in_specs=[SCALARS] * 2 + [INSIDE] * len(stats),
        out_specs=INSIDE,
        out_shape=jax.ShapeDtypeStruct(
            (sections * groups * widths, 8, sections * share), jnp.float32
        ),
        scratch_shapes=[
            pltpu.VMEM((sections * groups, 8, share), jnp.float32),
            pltpu.VMEM((groups, 8, sections * share), jnp.float32),
        ],
        compiler_params=pltpu.CompilerParams(vmem_limit_bytes=16 << 20),
        name="statistics_by_group",
    )(place, slot_utt, *stats)


def score_kernel(sections, widths, place_ref, slot_ref, length_ref, every_ref, out_ref):
    slots, hyps = out_ref.shape
    lanes = every_ref.shape[2]
    share = lanes // sections // widths
    lane = lax.broadcasted_iota(jnp.int32, (1, lanes), 1)
    order = lane % share * (sections * widths) + lane // share
    column = lax.broadcasted_iota(jnp.int32, (1, hyps), 1)
    for slot in range(slots):
        upper = every_ref[:, 3 * slot, :]
        peak = jnp.max(upper, axis=0, keepdims=True)
        total = jnp.sum(
            every_ref[:, 3 * slot + 1, :] * jnp.exp(upper - peak), axis=0, keepdims=True
        )
        picked = jnp.sum(every_ref[:, 3 * slot + 2, :], axis=0, keepdims=True)
        logp = picked - (peak + jnp.log(total))
        scores = jnp.zeros((1, hyps), jnp.float32)
        start = jnp.int32(0)
        for hyp in range(hyps):
            length = length_ref[slot * hyps + hyp]
            valid = (order >= start) & (order < start + length)
            summed = jnp.sum(jnp.where(valid, logp, 0.0), axis=1, keepdims=True)
            mean = summed / jnp.full((1, 1), length, jnp.int32).astype(jnp.float32)
            scores = jnp.where(column == hyp, mean + math.log(V), scores)
            start = start + length
        filled = slot_ref[place_ref[1] * slots + slot] >= 0
        out_ref[slot : slot + 1, :] = jnp.where(filled, scores, 0.0)


def hypothesis_scores(place, slot_utt, lengths, every, slots, hyps, sections, widths):
    return pl.pallas_call(
        functools.partial(score_kernel, sections, widths),
        in_specs=[SCALARS] * 3 + [INSIDE],
        out_specs=INSIDE,
        out_shape=jax.ShapeDtypeStruct((slots, hyps), jnp.float32),
        compiler_params=pltpu.CompilerParams(vmem_limit_bytes=16 << 20),
        name="hypothesis_scores",
    )(place, slot_utt, lengths, every)


def near_device(
    frame_len,
    slot_utt,
    enc_in,
    ffn_up,
    ffn_down,
    kv_proj,
    hyp_state,
    hyp_tok,
    hyp_len,
    q_proj,
    o_proj,
    head,
):
    section_count = lax.axis_size("section")
    group_count = lax.axis_size("tm")
    width_count = lax.axis_size("mp")
    section_pos = lax.axis_index("section")
    group_pos = lax.axis_index("tm")
    width_pos = lax.axis_index("mp")
    head_devices = section_count * width_count
    all_devices = head_devices * group_count

    frame_rows, utterances, enc_width = enc_in.shape
    slot_count, hyp_count, positions, model_width = hyp_state.shape
    slot_tokens = hyp_count * positions
    share_rows = slot_tokens // head_devices
    vocab_start = (
        (section_pos * group_count + group_pos) * width_count + width_pos
    ) * head.shape[0]
    head_pos = section_pos * width_count + width_pos
    place = jnp.stack([section_pos, group_pos, width_pos, vocab_start, head_pos])
    place = place.astype(jnp.int32)
    lengths = hyp_len.reshape(-1)

    parts = ffn(
        place, enc_in.reshape(frame_rows * utterances, enc_width), ffn_up, ffn_down, width_count
    )
    own_frames = parts[width_count]
    parts = [parts[0]] + [
        swap(parts[distance], "mp", distance) for distance in range(1, width_count)
    ]

    blocks = queries_of(
        place,
        slot_utt,
        lengths,
        parts[1],
        hyp_state.reshape(slot_count, slot_tokens, model_width),
        hyp_tok.reshape(slot_count, 1, slot_tokens),
        q_proj,
        group_count,
        share_rows,
    )
    beside = group_pos ^ 1
    beside_slots = lax.dynamic_slice_in_dim(slot_utt, beside * slot_count, slot_count, 0)
    beside_has = jnp.any(beside_slots == group_pos ^ 2)
    crossing = jnp.where(beside_has, swap(blocks[3], "tm", 1), blocks[2])
    payloads = [blocks[0], swap(blocks[1], "tm", 1), swap(crossing, "tm", 2)]

    sent = keys_values_of(
        parts, own_frames, kv_proj, blocks[0], section_count, utterances, width_count
    )
    frames_all = all_devices * (frame_rows // width_count)
    keys_values = exchange(sent.reshape(all_devices, -1, 2 * HD), ALL).reshape(frames_all, 2 * HD)

    pieces = (share_rows // 2, share_rows - share_rows // 2)
    projected = attend(
        place,
        slot_utt,
        frame_len,
        payloads,
        keys_values,
        o_proj,
        pieces,
        section_count,
        width_count,
        slot_count,
    )
    others = [swap(projected[number], "section", 1) for number in range(len(pieces))]
    head, token = load_head(projected[len(pieces)], head)
    sums = []
    for number, piece in enumerate(pieces):
        total = projected[len(pieces) + number].astype(jnp.float32) + others[number].astype(
            jnp.float32
        )
        for distance in (1, 2):
            half = total.shape[0] // 2
            side = width_pos // distance % 2
            kept = lax.dynamic_slice_in_dim(total, side * half, half, 0)
            sent = lax.dynamic_slice_in_dim(total, (1 - side) * half, half, 0)
            came = swap(sent.astype(jnp.bfloat16), "mp", distance)
            if distance == 1:
                total = kept + came.astype(jnp.float32)
        sums += [kept, came]
    out_rows = normed_rows(
        place, slot_utt, token, payloads, sums, pieces, slot_tokens, slot_count
    )

    share = out_rows.shape[0]
    own = jnp.zeros((width_count * share, out_rows.shape[1]), jnp.bfloat16)
    for distance in range(width_count):
        block = swap(out_rows, "mp", distance) if distance else out_rows
        own = lax.dynamic_update_slice_in_dim(own, block, (width_pos ^ distance) * share, 0)
    half = own.shape[0] // 2
    by_x = swap(own, "section", 1)
    by_y = swap(own, "tm", 2)
    stats = [vocabulary_stats(place, [own, swap(own, "tm", 1)], head)]
    by_x, by_y, stats[0] = lax.optimization_barrier((by_x, by_y, stats[0]))
    across = [swap(by_x[:half], "tm", 2), swap(by_y[half:], "section", 1)]
    stats.append(
        vocabulary_stats(place, [by_y, swap(by_y, "tm", 1), by_x, swap(by_x, "tm", 1)], head)
    )
    *across, stats[1] = lax.optimization_barrier((*across, stats[1]))
    across = jnp.concatenate(across)
    stats.append(vocabulary_stats(place, [across, swap(across, "tm", 1)], head))

    every = exchange(
        spread_stats(place, slot_utt, stats, section_count, group_count, width_count), ALL
    )
    return hypothesis_scores(
        place, slot_utt, lengths, every, slot_count, hyp_count, section_count, width_count
    )


def general(
    frame_len,
    slot_utt,
    enc_in,
    ffn_up,
    ffn_down,
    kv_proj,
    hyp_state,
    hyp_tok,
    hyp_len,
    q_proj,
    o_proj,
    head,
):
    section_count = lax.axis_size("section")
    group_count = lax.axis_size("tm")
    width_count = lax.axis_size("mp")
    section_pos = lax.axis_index("section")
    group_pos = lax.axis_index("tm")
    width_pos = lax.axis_index("mp")
    head_devices = section_count * width_count
    head_pos = section_pos * width_count + width_pos
    all_devices = head_devices * group_count

    frame_rows, utterances, enc_width = enc_in.shape
    assert utterances == group_count
    slot_count, hyp_count, positions, model_width = hyp_state.shape
    slot_tokens = hyp_count * positions
    device_heads = q_proj.shape[1] // HD
    group_heads = NH // KVH
    frame_share = frame_rows // width_count
    share_rows = slot_tokens // head_devices
    here_slots = lax.dynamic_slice_in_dim(slot_utt, group_pos * slot_count, slot_count, 0)

    dec_rows = hyp_state.reshape(slot_count * slot_tokens, model_width).astype(jnp.float32)
    queries = jnp.dot(
        square_norm(dec_rows).astype(jnp.bfloat16), q_proj, preferred_element_type=jnp.float32
    ).astype(jnp.bfloat16)
    queries = queries.reshape(slot_count, slot_tokens, device_heads * HD)
    shares = lax.dynamic_slice_in_dim(
        hyp_state.reshape(slot_count, slot_tokens, model_width), head_pos * share_rows, share_rows, 1
    )

    def by_utterance(values):
        out = []
        for utterance in range(utterances):
            block = values[0]
            for slot in range(1, slot_count):
                block = jnp.where(here_slots[slot] == utterance, values[slot], block)
            out.append(block)
        return jnp.stack(out)

    own_slot = jnp.argmax(slot_utt == group_pos)
    from_group = own_slot // slot_count
    queries = lax.dynamic_index_in_dim(
        exchange(by_utterance(queries), "tm"), from_group, 0, keepdims=False
    )
    resid_rows = lax.dynamic_index_in_dim(
        exchange(by_utterance(shares), "tm"), from_group, 0, keepdims=False
    )
    slot_targets = lax.all_gather(
        hyp_tok.reshape(slot_count, slot_tokens), "tm", axis=0, tiled=True
    )
    utt_slots = jnp.argmax(slot_utt[None, :] == jnp.arange(utterances)[:, None], axis=1)
    targets = jnp.take(slot_targets, utt_slots, axis=0).reshape(utterances * slot_tokens)

    enc_flat = (
        enc_in.reshape(width_count, frame_share, utterances, enc_width)
        .transpose(0, 2, 1, 3)
        .reshape(frame_rows * utterances, enc_width)
    )
    share_count = frame_share * utterances
    enc_normed = layer_norm(enc_flat.astype(jnp.float32)).astype(jnp.bfloat16)
    enc_inner = jax.nn.gelu(
        jnp.dot(enc_normed, ffn_up, preferred_element_type=jnp.float32), approximate=False
    ).astype(jnp.bfloat16)
    enc_summed = scatter_sum(
        jnp.dot(enc_inner, ffn_down, preferred_element_type=jnp.float32).astype(jnp.bfloat16),
        "mp",
        width_count,
    )
    own_frames = lax.dynamic_slice_in_dim(enc_flat, width_pos * share_count, share_count, 0)
    enc_states = layer_norm(own_frames.astype(jnp.float32) + enc_summed).astype(jnp.bfloat16)
    keys_values = jnp.dot(enc_states, kv_proj, preferred_element_type=jnp.float32).astype(
        jnp.bfloat16
    )
    keys_values = keys_values.reshape(utterances, frame_share, 2, KVH, HD)
    sent = []
    for section in range(section_count):
        per_width = []
        for width in range(width_count):
            kv_head = (section * width_count + width) * device_heads // group_heads
            per_width.append(
                keys_values[:, :, :, kv_head].reshape(utterances, frame_share, 2 * HD)
            )
        sent.append(jnp.stack(per_width, axis=1))
    sent = jnp.stack(sent).reshape(all_devices, frame_share, 2 * HD)
    frames_all = all_devices * frame_share
    keys_values = exchange(sent, ALL).reshape(frames_all, 2 * HD)

    frame_limit = lax.dynamic_index_in_dim(frame_len, group_pos, 0, keepdims=False)
    queries = queries.reshape(slot_tokens, device_heads, HD)
    scores = jnp.einsum(
        "qhd,fd->hqf", queries, keys_values[:, :HD], preferred_element_type=jnp.float32
    ) / math.sqrt(HD)
    visible = jnp.arange(frames_all, dtype=jnp.int32) < frame_limit
    scores = jnp.where(visible[None, None, :], scores, -jnp.inf)
    weights = jax.nn.softmax(scores, axis=-1).astype(jnp.bfloat16)
    context = jnp.einsum(
        "hqf,fd->qhd", weights, keys_values[:, HD:], preferred_element_type=jnp.float32
    ).astype(jnp.bfloat16)
    partial = jnp.dot(
        context.reshape(slot_tokens, device_heads * HD), o_proj, preferred_element_type=jnp.float32
    ).astype(jnp.bfloat16)
    partial = scatter_sum(partial, "section", section_count).astype(jnp.bfloat16)
    attn_out = scatter_sum(partial, "mp", width_count)
    out_normed = square_norm(resid_rows.astype(jnp.float32) + attn_out).astype(jnp.bfloat16)

    hidden_rows = lax.all_gather(out_normed, ALL, axis=0, tiled=True)
    logits = lax.dot_general(
        hidden_rows, head, (((1,), (1,)), ((), ())), preferred_element_type=jnp.float32
    )
    vocab_rows = head.shape[0]
    vocab_start = (
        (section_pos * group_count + group_pos) * width_count + width_pos
    ) * vocab_rows
    target_rows = (
        targets.reshape(utterances, section_count, width_count, share_rows)
        .transpose(1, 0, 2, 3)
        .reshape(-1)
    )
    upper = jnp.max(logits, axis=1)
    totals = jnp.sum(jnp.exp(logits - upper[:, None]), axis=1)
    matches = (
        jnp.arange(vocab_rows, dtype=jnp.int32)[None, :] == (target_rows - vocab_start)[:, None]
    )
    target_logit = jnp.sum(jnp.where(matches, logits, 0.0), axis=1)

    stats = jnp.stack([upper, totals, target_logit])
    stats = stats.reshape(3, section_count, utterances, width_count, share_rows)
    stats = stats.transpose(2, 0, 1, 3, 4).reshape(utterances, 3, slot_tokens)
    by_slot = jnp.take(stats, jnp.maximum(slot_utt, 0), axis=0)
    by_group = by_slot.reshape(1, group_count, 1, slot_count, 3, slot_tokens)
    by_group = jnp.broadcast_to(
        by_group, (section_count, group_count, width_count, slot_count, 3, slot_tokens)
    ).reshape(all_devices, slot_count, 3, slot_tokens)
    every = exchange(by_group, ALL)
    peak = jnp.max(every[:, :, 0], axis=0)
    total = jnp.sum(every[:, :, 1] * jnp.exp(every[:, :, 0] - peak[None]), axis=0)
    picked = jnp.sum(every[:, :, 2], axis=0)
    token_logp = (picked - (peak + jnp.log(total))).reshape(slot_count, hyp_count, positions)
    valid = jnp.arange(positions, dtype=jnp.int32)[None, None, :] < hyp_len[:, :, None]
    summed = jnp.sum(jnp.where(valid, token_logp, 0.0), axis=-1) / hyp_len.astype(
        jnp.float32
    ) + math.log(V)
    return jnp.where(here_slots[:, None] >= 0, summed, 0.0)


def solution(mesh):
    in_specs = (
        P(),
        P(),
        P(("section", "tm"), None, None),
        P(None, "mp"),
        P("mp", None),
        P(),
        P("tm", None, None, None),
        P("tm", None, None),
        P("tm", None),
        P(None, ("section", "mp")),
        P(("section", "mp"), None),
        P(("section", "tm", "mp"), None),
    )
    out_specs = P("tm", None)
    near = dict(mesh.shape) == {"section": 2, "tm": 4, "mp": 4}
    per_device = near_device if near else general
    return jax.shard_map(
        per_device, mesh=mesh, in_specs=in_specs, out_specs=out_specs, check_vma=False
    )
```

```python
import functools
import math

import jax
import jax.numpy as jnp
from jax import lax
from jax.experimental import pallas as pl
from jax.experimental.pallas import tpu as pltpu
from jax.sharding import PartitionSpec as P

NH = 32
KVH = 4
HD = 128
V = 64000
ALL = ("section", "tm", "mp")
LANES = 128


def layer_norm(values):
    center = values - jnp.mean(values, axis=-1, keepdims=True)
    spread = jnp.mean(center * center, axis=-1, keepdims=True)
    return center * lax.rsqrt(spread + 1e-05)


def square_norm(values):
    return values * lax.rsqrt(jnp.mean(values * values, axis=-1, keepdims=True) + 1e-06)


def exchange(blocks, axis):
    return lax.all_to_all(blocks, axis, split_axis=0, concat_axis=0, tiled=True)


def scatter_sum(partial, axis, count):
    blocks = partial.reshape((count, partial.shape[0] // count) + partial.shape[1:])
    return jnp.sum(exchange(blocks, axis).astype(jnp.float32), axis=0)


def swap(values, axis, distance):
    pairs = [(i, i ^ distance) for i in range(lax.axis_size(axis))]
    return lax.ppermute(values, axis, pairs)


def whole(shape):
    return pl.BlockSpec(shape, lambda *_: (0,) * len(shape))


SCALARS = pl.BlockSpec(memory_space=pltpu.SMEM)


def dot(left, right):
    return jnp.dot(left, right, preferred_element_type=jnp.float32)


def dot_nt(left, right):
    return lax.dot_general(
        left, right, (((1,), (1,)), ((), ())), preferred_element_type=jnp.float32
    )


def start_copies(source_of, target_of, semaphores, count):
    copies = []
    for number in range(count):
        copy = pltpu.make_async_copy(
            source_of(number), target_of(number), semaphores.at[number]
        )
        copy.start()
        copies.append(copy)
    return copies


def ffn_kernel(count, tile, place_ref, x_ref, up_ref, down_ref, *refs):
    outs, (own_ref, total, up, down, up_sem, down_sem) = refs[:count], refs[count:]
    share = own_ref.shape[0]
    tiles = up_ref.shape[1] // tile
    up_copies = start_copies(
        lambda i: up_ref.at[:, pl.ds(i * tile, tile)], lambda i: up.at[i], up_sem, tiles
    )
    down_copies = start_copies(
        lambda i: down_ref.at[pl.ds(i * tile, tile), :], lambda i: down.at[i], down_sem, tiles
    )
    here = place_ref[2]
    own_ref[...] = x_ref[pl.ds(pl.multiple_of(here * share, share), share), :]
    normed = layer_norm(x_ref[...].astype(jnp.float32)).astype(jnp.bfloat16)
    for number in range(tiles):
        up_copies[number].wait()
        hidden = dot(normed, up[number])
        inner = 0.5 * hidden * (1.0 + lax.erf(hidden * math.sqrt(0.5)))
        down_copies[number].wait()
        product = dot(inner.astype(jnp.bfloat16), down[number])
        if number == 0:
            total[...] = product
        else:
            total[...] += product
    for distance in range(count):
        start = pl.multiple_of((here ^ distance) * share, share)
        outs[distance][...] = total[pl.ds(start, share), :].astype(jnp.bfloat16)


def in_hbm(values):
    return pltpu.with_memory_space_constraint(values, pltpu.HBM)


ANYWHERE = pl.BlockSpec(memory_space=pl.ANY)
INSIDE = pl.BlockSpec(memory_space=pltpu.VMEM)


def ffn(place, rows, up, down, count):
    share = rows.shape[0] // count
    width = rows.shape[1]
    tile = 256
    tiles = up.shape[1] // tile
    block = jax.ShapeDtypeStruct((share, width), jnp.bfloat16)
    return pl.pallas_call(
        functools.partial(ffn_kernel, count, tile),
        in_specs=[SCALARS, INSIDE, ANYWHERE, ANYWHERE],
        out_specs=[INSIDE] * (count + 1),
        out_shape=[block] * (count + 1),
        scratch_shapes=[
            pltpu.VMEM(rows.shape, jnp.float32),
            pltpu.VMEM((tiles, width, tile), jnp.bfloat16),
            pltpu.VMEM((tiles, tile, width), jnp.bfloat16),
            pltpu.SemaphoreType.DMA((tiles,)),
            pltpu.SemaphoreType.DMA((tiles,)),
        ],
        cost_estimate=pl.CostEstimate(
            flops=4 * rows.shape[0] * width * up.shape[1],
            bytes_accessed=4 * width * up.shape[1],
            transcendentals=rows.shape[0] * up.shape[1],
        ),
        compiler_params=pltpu.CompilerParams(vmem_limit_bytes=24 << 20),
        name="encoder_ffn",
    )(place, rows, in_hbm(up), in_hbm(down))


def query_kernel(
    count, depth, place_ref, slot_ref, length_ref, after_ref, x_ref, tok_ref, w_ref, *refs
):
    outs, (states, weights, normed, total, shares, x_sem, w_sem) = refs[:count], refs[count:]
    slots, tokens, width = x_ref.shape
    hyps = length_ref.shape[0] // slots
    positions = tokens // hyps
    columns = w_ref.shape[1]
    share = shares.shape[1] // 2
    parts = width // columns
    x_copies = start_copies(lambda i: x_ref.at[i], lambda i: states.at[i], x_sem, slots)
    w_copies = start_copies(
        lambda i: w_ref.at[pl.ds(i * depth, depth), :],
        lambda i: weights.at[i],
        w_sem,
        width // depth,
    )
    head_pos = place_ref[4]
    lane = lax.broadcasted_iota(jnp.int32, (1, tokens), 1)
    for slot in range(slots):
        order = jnp.full((1, tokens), -1, jnp.int32)
        start = jnp.int32(0)
        for hyp in range(hyps):
            length = length_ref[slot * hyps + hyp]
            inside = (lane >= hyp * positions) & (lane < hyp * positions + length)
            order = jnp.where(inside, lane - hyp * positions + start, order)
            start = start + length
        row = lax.broadcasted_iota(jnp.int32, (tokens, tokens), 0)
        move = jnp.where(order == row, 1.0, 0.0).astype(jnp.bfloat16)
        x_copies[slot].wait()
        ordered = dot(move, states[slot])
        normed[slot * tokens : (slot + 1) * tokens, :] = square_norm(ordered).astype(jnp.bfloat16)
        share_row = lax.broadcasted_iota(jnp.int32, (share, tokens), 0)
        chosen = order == share_row * (tokens // share) + head_pos
        mine = dot(jnp.where(chosen, 1.0, 0.0).astype(jnp.bfloat16), states[slot])
        shares[slot, :share, :] = mine.astype(jnp.bfloat16)
        target = jnp.sum(
            jnp.where(chosen, tok_ref[slot], 0), axis=1, keepdims=True, dtype=jnp.int32
        )
        coarse = target // 256
        cell = lax.broadcasted_iota(jnp.int32, (share, columns), 1)
        packed = jnp.where(cell == 0, coarse, jnp.where(cell == 1, target - coarse * 256, 0))
        shares[slot, share:, :columns] = packed.astype(jnp.float32).astype(jnp.bfloat16)
    for number in range(width // depth):
        w_copies[number].wait()
        product = dot(normed[:, number * depth : (number + 1) * depth], weights[number])
        if number == 0:
            total[...] = product
        else:
            total[...] += product
    group = place_ref[1]
    for distance in range(count):
        slot = jnp.int32(-1)
        for candidate in range(slots):
            holds = slot_ref[group * slots + candidate] == group ^ distance
            slot = jnp.where(holds, candidate, slot)
        out = outs[distance]

        @pl.when(slot < 0)
        def _(out=out):
            out[...] = jnp.zeros_like(out)

        @pl.when(slot >= 0)
        def _(out=out, slot=slot):
            start = pl.multiple_of(slot * tokens, tokens)
            out[:tokens, :] = total[pl.ds(start, tokens), :].astype(jnp.bfloat16)
            for part in range(parts):
                first = tokens + part * share
                out[first : first + share, :] = shares[
                    slot, :share, part * columns : (part + 1) * columns
                ]
            out[tokens + parts * share :, :] = shares[slot, share:, :columns]


def queries_of(place, slot_utt, lengths, after, states, targets, weights, count, share):
    slots, tokens, width = states.shape
    columns = weights.shape[1]
    depth = 1024
    rows = tokens + (width // columns + 1) * share
    block = jax.ShapeDtypeStruct((rows, columns), jnp.bfloat16)
    return pl.pallas_call(
        functools.partial(query_kernel, count, depth),
        in_specs=[SCALARS] * 3 + [ANYWHERE, ANYWHERE, INSIDE, ANYWHERE],
        out_specs=[INSIDE] * count,
        out_shape=[block] * count,
        scratch_shapes=[
            pltpu.VMEM(states.shape, jnp.bfloat16),
            pltpu.VMEM((width // depth, depth, columns), jnp.bfloat16),
            pltpu.VMEM((slots * tokens, width), jnp.bfloat16),
            pltpu.VMEM((slots * tokens, columns), jnp.float32),
            pltpu.VMEM((slots, 2 * share, width), jnp.bfloat16),
            pltpu.SemaphoreType.DMA((slots,)),
            pltpu.SemaphoreType.DMA((width // depth,)),
        ],
        cost_estimate=pl.CostEstimate(
            flops=2 * slots * tokens * width * columns,
            bytes_accessed=2 * width * (columns + slots * tokens),
            transcendentals=0,
        ),
        compiler_params=pltpu.CompilerParams(vmem_limit_bytes=32 << 20),
        name="hypothesis_queries",
    )(place, slot_utt, lengths, after, in_hbm(states), targets, in_hbm(weights))


def kv_kernel(sections, utterances, widths, *refs):
    parts, (own_ref, w_ref, after_ref, out_ref) = refs[:-4], refs[-4:]
    rows = own_ref.shape[0]
    frames = rows // utterances
    total = own_ref[...].astype(jnp.float32)
    summed = parts[0][...].astype(jnp.float32)
    for part in parts[1:]:
        summed += part[...].astype(jnp.float32)
    states = layer_norm(total + summed).astype(jnp.bfloat16)
    to = lax.broadcasted_iota(jnp.int32, (rows, rows), 0)
    come = lax.broadcasted_iota(jnp.int32, (rows, rows), 1)
    move = jnp.where(come == to % frames * utterances + to // frames, 1.0, 0.0)
    states = dot(move.astype(jnp.bfloat16), states).astype(jnp.bfloat16)
    both = dot(states, w_ref[...])
    half = KVH * HD
    per_kv = sections * widths // KVH
    for section in range(sections):
        for utterance in range(utterances):
            for width in range(0, widths, per_kv):
                kv_head = (section * widths + width) // per_kv
                take = slice(utterance * frames, (utterance + 1) * frames)
                block = jnp.concatenate(
                    [
                        both[take, kv_head * HD : (kv_head + 1) * HD],
                        both[take, half + kv_head * HD : half + (kv_head + 1) * HD],
                    ],
                    axis=1,
                )
                start = ((section * utterances + utterance) * widths + width) * frames
                block = jnp.concatenate([block] * per_kv, axis=0).astype(jnp.bfloat16)
                out_ref[start : start + per_kv * frames, :] = block


def keys_values_of(parts, own, weights, after, sections, utterances, widths):
    rows = sections * widths * own.shape[0]
    return pl.pallas_call(
        functools.partial(kv_kernel, sections, utterances, widths),
        in_specs=[INSIDE] * (len(parts) + 2) + [ANYWHERE],
        out_specs=INSIDE,
        out_shape=jax.ShapeDtypeStruct((rows, 2 * HD), jnp.bfloat16),
        cost_estimate=pl.CostEstimate(
            flops=2 * own.shape[0] * weights.shape[0] * weights.shape[1],
            bytes_accessed=2 * weights.shape[0] * weights.shape[1],
            transcendentals=0,
        ),
        compiler_params=pltpu.CompilerParams(vmem_limit_bytes=24 << 20),
        name="frame_keys_values",
    )(*parts, own, weights, after)


def choice_of_payload(place_ref, slot_ref, slots):
    group = place_ref[1]
    source = jnp.int32(0)
    for slot in range(slot_ref.shape[0]):
        source = jnp.where(slot_ref[slot] == group, slot // slots, source)
    return jnp.minimum(source ^ group, 2)


def attention_kernel(count, slots, capacity, pieces, sections, widths, tile, *refs):
    place_ref, slot_ref, frame_ref = refs[:3]
    payloads, (kv_ref, w_ref) = refs[3 : 3 + count], refs[3 + count : 5 + count]
    outs = refs[5 + count : 5 + count + 2 * len(pieces)]
    weights, picked, context, w_sem = refs[5 + count + 2 * len(pieces) :]
    tokens, columns = capacity, w_ref.shape[0]
    tiles = w_ref.shape[1] // tile
    w_copies = start_copies(
        lambda i: w_ref.at[:, pl.ds(i * tile, tile)], lambda i: weights.at[i], w_sem, tiles
    )
    source = choice_of_payload(place_ref, slot_ref, slots)
    section_pos = place_ref[0]
    frame_limit = frame_ref[place_ref[1]]
    for distance in range(count):

        @pl.when(source == distance)
        def _(payload=payloads[distance]):
            picked[...] = payload[:tokens, :]

    keys = kv_ref[:, :HD]
    values = kv_ref[:, HD:]
    frames = kv_ref.shape[0]
    visible = lax.broadcasted_iota(jnp.int32, (tokens, frames), 1) < frame_limit
    for head in range(columns // HD):
        scores = dot_nt(picked[:, head * HD : (head + 1) * HD], keys) * (1.0 / math.sqrt(HD))
        scores = jnp.where(visible, scores, -jnp.inf)
        raised = jnp.exp(scores - jnp.max(scores, axis=1, keepdims=True))
        chances = (raised / jnp.sum(raised, axis=1, keepdims=True)).astype(jnp.bfloat16)
        context[:, head * HD : (head + 1) * HD] = dot(chances, values).astype(jnp.bfloat16)
    to = lax.broadcasted_iota(jnp.int32, (tokens, tokens), 0)
    come = lax.broadcasted_iota(jnp.int32, (tokens, tokens), 1)
    low_bit = place_ref[2] % 2
    size = widths * pieces[0]
    block = to % size // pieces[0]
    section = jnp.where(to < size, 1 - section_pos, section_pos)
    first_order = (to % pieces[0] * sections + section) * widths + block % 2 * 2 + block // 2
    at = to - 2 * size
    size = widths * pieces[1]
    block = at % size // pieces[1]
    low = jnp.where(at < size, 1 - low_bit, low_bit)
    row = pieces[0] + at % pieces[1]
    second_order = (row * sections + block % 2) * widths + block // 2 * 2 + low
    move = come == jnp.where(at < 0, first_order, second_order)
    ordered = dot(jnp.where(move, 1.0, 0.0).astype(jnp.bfloat16), context[...])
    ordered = ordered.astype(jnp.bfloat16)
    for number in range(tiles):
        w_copies[number].wait()
        product = dot(ordered, weights[number]).astype(jnp.bfloat16)
        first = 0
        for out in outs:
            out[:, number * tile : (number + 1) * tile] = product[first : first + out.shape[0], :]
            first += out.shape[0]


def attend(place, slot_utt, frame_len, payloads, keys_values, weights, pieces, sections, widths, slots):
    count = len(payloads)
    columns, width = weights.shape
    capacity = sum(pieces) * sections * widths
    tile = 1024
    tiles = width // tile
    shapes = [
        jax.ShapeDtypeStruct((piece * widths, width), jnp.bfloat16)
        for piece in pieces
        for _ in range(2)
    ]
    return pl.pallas_call(
        functools.partial(
            attention_kernel, count, slots, capacity, pieces, sections, widths, tile
        ),
        in_specs=[SCALARS] * 3 + [INSIDE] * (count + 1) + [ANYWHERE],
        out_specs=[INSIDE] * len(shapes),
        out_shape=shapes,
        scratch_shapes=[
            pltpu.VMEM((tiles, columns, tile), jnp.bfloat16),
            pltpu.VMEM((capacity, columns), jnp.bfloat16),
            pltpu.VMEM((capacity, columns), jnp.bfloat16),
            pltpu.SemaphoreType.DMA((tiles,)),
        ],
        cost_estimate=pl.CostEstimate(
            flops=2 * capacity * columns * (width + 2 * keys_values.shape[0]),
            bytes_accessed=2 * columns * width + 2 * capacity * width,
            transcendentals=capacity * keys_values.shape[0] * columns // HD,
        ),
        compiler_params=pltpu.CompilerParams(vmem_limit_bytes=24 << 20),
        name="attention_projection",
    )(place, slot_utt, frame_len, *payloads, keys_values, in_hbm(weights))


def norm_kernel(count, slots, tokens, pieces, place_ref, slot_ref, after_ref, *refs):
    payloads, blocks = refs[:count], refs[count : count + 2 * len(pieces)]
    out_ref, picked, total = refs[count + 2 * len(pieces) :]
    rows, width = total.shape
    columns = picked.shape[1]
    share = picked.shape[0] // (width // columns + 1)
    source = choice_of_payload(place_ref, slot_ref, slots)
    for choice in range(count):

        @pl.when(source == choice)
        def _(payload=payloads[choice]):
            picked[...] = payload[tokens:, :]

    first = 0
    for number, piece in enumerate(pieces):
        kept, other = blocks[2 * number : 2 * number + 2]
        total[first : first + piece, :] = kept[...] + other[...].astype(jnp.float32)
        first += piece
    for part in range(width // columns):
        take = slice(part * columns, (part + 1) * columns)
        total[:, take] += picked[part * share : part * share + rows, :].astype(jnp.float32)
    out_ref[:, :width] = square_norm(total[...]).astype(jnp.bfloat16)
    last = width // columns * share
    out_ref[:, width:] = picked[last : last + rows, :LANES]


def normed_rows(place, slot_utt, after, payloads, blocks, pieces, tokens, slots):
    width = blocks[0].shape[1]
    rows = sum(pieces)
    columns = payloads[0].shape[1]
    return pl.pallas_call(
        functools.partial(norm_kernel, len(payloads), slots, tokens, pieces),
        in_specs=[SCALARS] * 2 + [ANYWHERE] + [INSIDE] * (len(payloads) + len(blocks)),
        out_specs=INSIDE,
        out_shape=jax.ShapeDtypeStruct((rows, width + LANES), jnp.bfloat16),
        scratch_shapes=[
            pltpu.VMEM((payloads[0].shape[0] - tokens, columns), jnp.bfloat16),
            pltpu.VMEM((rows, width), jnp.float32),
        ],
        compiler_params=pltpu.CompilerParams(vmem_limit_bytes=16 << 20),
        name="token_rows",
    )(place, slot_utt, after, *payloads, *blocks)


def load_kernel(rows, after_ref, head_ref, out_ref, token_ref, semaphores):
    count = head_ref.shape[0] // rows
    copies = start_copies(
        lambda i: head_ref.at[pl.ds(i * rows, rows), :],
        lambda i: out_ref.at[pl.ds(i * rows, rows), :],
        semaphores,
        count,
    )
    token_ref[...] = jnp.zeros_like(token_ref)
    for copy in copies:
        copy.wait()


def load_head(after, head):
    rows = head.shape[0] // 5
    return pl.pallas_call(
        functools.partial(load_kernel, rows),
        in_specs=[ANYWHERE, ANYWHERE],
        out_specs=[INSIDE, INSIDE],
        out_shape=[
            pltpu.VMEM(head.shape, head.dtype),
            jax.ShapeDtypeStruct((8, LANES), jnp.float32),
        ],
        scratch_shapes=[pltpu.SemaphoreType.DMA((5,))],
        cost_estimate=pl.CostEstimate(
            flops=0, bytes_accessed=2 * head.size, transcendentals=0
        ),
        compiler_params=pltpu.CompilerParams(vmem_limit_bytes=20 << 20),
        name="vocabulary_rows",
    )(after, in_hbm(head))


def vocabulary_kernel(tile, first_ref, *refs):
    sets, (head_ref, out_ref, rows_ref, stat) = refs[:-4], refs[-4:]
    vocab_rows, width = head_ref.shape
    share = sets[0].shape[0]
    tokens = share * len(sets)
    cell = lax.broadcasted_iota(jnp.int32, (8, LANES), 1)
    take = jnp.where(cell == 0, 256.0, jnp.where(cell == 1, 1.0, 0.0)).astype(jnp.bfloat16)
    for number, rows in enumerate(sets):
        rows_ref[number * share : (number + 1) * share, :] = rows[...]
    target = dot_nt(take, rows_ref[:, width:])[0:1, :].astype(jnp.int32) - first_ref[3]
    stat[0:1, :] = jnp.full((1, tokens), -jnp.inf, jnp.float32)
    stat[8:9, :] = jnp.zeros((1, tokens), jnp.float32)
    stat[16:17, :] = jnp.zeros((1, tokens), jnp.float32)

    @pl.loop(0, vocab_rows // tile)
    def _(step):
        start = pl.multiple_of(step * tile, tile)
        logits = dot_nt(head_ref[pl.ds(start, tile), :], rows_ref[:, :width])
        vocab = lax.broadcasted_iota(jnp.int32, logits.shape, 0) + start
        before = stat[0:1, :]
        upper = jnp.maximum(before, jnp.max(logits, axis=0, keepdims=True))
        stat[8:9, :] = stat[8:9, :] * jnp.exp(before - upper) + jnp.sum(
            jnp.exp(logits - upper), axis=0, keepdims=True
        )
        stat[16:17, :] += jnp.sum(jnp.where(vocab == target, logits, 0.0), axis=0, keepdims=True)
        stat[0:1, :] = upper

    for number in range(len(sets)):
        for row in range(3):
            out_ref[number, row : row + 1, :] = stat[
                8 * row : 8 * row + 1, number * share : (number + 1) * share
            ]


def vocabulary_stats(place, sets, head):
    share = sets[0].shape[0]
    count = len(sets)
    width = head.shape[1]
    tokens = share * count
    return pl.pallas_call(
        functools.partial(vocabulary_kernel, head.shape[0] // 2),
        in_specs=[SCALARS] + [INSIDE] * (count + 1),
        out_specs=INSIDE,
        out_shape=jax.ShapeDtypeStruct((count, 8, share), jnp.float32),
        scratch_shapes=[
            pltpu.VMEM((tokens, width + LANES), jnp.bfloat16),
            pltpu.VMEM((24, tokens), jnp.float32),
        ],
        cost_estimate=pl.CostEstimate(
            flops=3 * tokens * head.shape[0] * width,
            bytes_accessed=2 * tokens * width,
            transcendentals=tokens * head.shape[0],
        ),
        compiler_params=pltpu.CompilerParams(vmem_limit_bytes=16 << 20),
        name="vocabulary_scores",
    )(place, *sets, pltpu.with_memory_space_constraint(head, pltpu.VMEM))


def spread_kernel(sections, groups, widths, place_ref, slot_ref, *refs):
    stats, (out_ref, table, block) = refs[:-3], refs[-3:]
    share = table.shape[2]
    first = 0
    for stat in stats:
        table[first : first + stat.shape[0]] = stat[...]
        first += stat.shape[0]
    slots = slot_ref.shape[0] // groups
    block[...] = jnp.zeros_like(block)
    for group in range(groups):
        for slot in range(slots):
            utterance = jnp.maximum(slot_ref[group * slots + slot], 0)
            for section in range(sections):
                at = (section ^ place_ref[0]) * groups + (utterance ^ place_ref[1])
                block[group, 3 * slot : 3 * slot + 3, section * share : (section + 1) * share] = (
                    table[at][0:3, :]
                )
    for section in range(sections):
        for group in range(groups):
            for width in range(widths):
                out_ref[(section * groups + group) * widths + width] = block[group]


def spread_stats(place, slot_utt, stats, sections, groups, widths):
    share = stats[0].shape[2]
    assert 3 * slot_utt.shape[0] // groups <= 8
    return pl.pallas_call(
        functools.partial(spread_kernel, sections, groups, widths),
        in_specs=[SCALARS] * 2 + [INSIDE] * len(stats),
        out_specs=INSIDE,
        out_shape=jax.ShapeDtypeStruct(
            (sections * groups * widths, 8, sections * share), jnp.float32
        ),
        scratch_shapes=[
            pltpu.VMEM((sections * groups, 8, share), jnp.float32),
            pltpu.VMEM((groups, 8, sections * share), jnp.float32),
        ],
        compiler_params=pltpu.CompilerParams(vmem_limit_bytes=16 << 20),
        name="statistics_by_group",
    )(place, slot_utt, *stats)


def score_kernel(sections, widths, place_ref, slot_ref, length_ref, every_ref, out_ref):
    slots, hyps = out_ref.shape
    lanes = every_ref.shape[2]
    share = lanes // sections // widths
    lane = lax.broadcasted_iota(jnp.int32, (1, lanes), 1)
    order = lane % share * (sections * widths) + lane // share
    column = lax.broadcasted_iota(jnp.int32, (1, hyps), 1)
    for slot in range(slots):
        upper = every_ref[:, 3 * slot, :]
        peak = jnp.max(upper, axis=0, keepdims=True)
        total = jnp.sum(
            every_ref[:, 3 * slot + 1, :] * jnp.exp(upper - peak), axis=0, keepdims=True
        )
        picked = jnp.sum(every_ref[:, 3 * slot + 2, :], axis=0, keepdims=True)
        logp = picked - (peak + jnp.log(total))
        scores = jnp.zeros((1, hyps), jnp.float32)
        start = jnp.int32(0)
        for hyp in range(hyps):
            length = length_ref[slot * hyps + hyp]
            valid = (order >= start) & (order < start + length)
            summed = jnp.sum(jnp.where(valid, logp, 0.0), axis=1, keepdims=True)
            mean = summed / jnp.full((1, 1), length, jnp.int32).astype(jnp.float32)
            scores = jnp.where(column == hyp, mean + math.log(V), scores)
            start = start + length
        filled = slot_ref[place_ref[1] * slots + slot] >= 0
        out_ref[slot : slot + 1, :] = jnp.where(filled, scores, 0.0)


def hypothesis_scores(place, slot_utt, lengths, every, slots, hyps, sections, widths):
    return pl.pallas_call(
        functools.partial(score_kernel, sections, widths),
        in_specs=[SCALARS] * 3 + [INSIDE],
        out_specs=INSIDE,
        out_shape=jax.ShapeDtypeStruct((slots, hyps), jnp.float32),
        compiler_params=pltpu.CompilerParams(vmem_limit_bytes=16 << 20),
        name="hypothesis_scores",
    )(place, slot_utt, lengths, every)


def near_device(
    frame_len,
    slot_utt,
    enc_in,
    ffn_up,
    ffn_down,
    kv_proj,
    hyp_state,
    hyp_tok,
    hyp_len,
    q_proj,
    o_proj,
    head,
):
    section_count = lax.axis_size("section")
    group_count = lax.axis_size("tm")
    width_count = lax.axis_size("mp")
    section_pos = lax.axis_index("section")
    group_pos = lax.axis_index("tm")
    width_pos = lax.axis_index("mp")
    head_devices = section_count * width_count
    all_devices = head_devices * group_count

    frame_rows, utterances, enc_width = enc_in.shape
    slot_count, hyp_count, positions, model_width = hyp_state.shape
    slot_tokens = hyp_count * positions
    share_rows = slot_tokens // head_devices
    vocab_start = (
        (section_pos * group_count + group_pos) * width_count + width_pos
    ) * head.shape[0]
    head_pos = section_pos * width_count + width_pos
    place = jnp.stack([section_pos, group_pos, width_pos, vocab_start, head_pos])
    place = place.astype(jnp.int32)
    lengths = hyp_len.reshape(-1)

    parts = ffn(
        place, enc_in.reshape(frame_rows * utterances, enc_width), ffn_up, ffn_down, width_count
    )
    own_frames = parts[width_count]
    parts = [parts[0]] + [
        swap(parts[distance], "mp", distance) for distance in range(1, width_count)
    ]

    blocks = queries_of(
        place,
        slot_utt,
        lengths,
        own_frames,
        hyp_state.reshape(slot_count, slot_tokens, model_width),
        hyp_tok.reshape(slot_count, 1, slot_tokens),
        q_proj,
        group_count,
        share_rows,
    )
    crossing = blocks[2] + swap(blocks[3], "tm", 1)
    payloads = [blocks[0], swap(blocks[1], "tm", 1), swap(crossing, "tm", 2)]

    sent = keys_values_of(
        parts, own_frames, kv_proj, blocks[0], section_count, utterances, width_count
    )
    frames_all = all_devices * (frame_rows // width_count)
    keys_values = exchange(sent.reshape(all_devices, -1, 2 * HD), ALL).reshape(frames_all, 2 * HD)

    pieces = (share_rows // 2, share_rows - share_rows // 2)
    projected = attend(
        place,
        slot_utt,
        frame_len,
        payloads,
        keys_values,
        o_proj,
        pieces,
        section_count,
        width_count,
        slot_count,
    )
    head, token = load_head(projected[1], head)

    def halve(total, came, axis, distance, side):
        if came is not None:
            total = total + came.astype(jnp.float32)
        half = total.shape[0] // 2
        kept = lax.dynamic_slice_in_dim(total, side * half, half, 0)
        sent = lax.dynamic_slice_in_dim(total, (1 - side) * half, half, 0)
        return kept, swap(sent.astype(jnp.bfloat16), axis, distance)

    low, high = width_pos % 2, width_pos // 2
    first = projected[1].astype(jnp.float32), swap(projected[0], "section", 1)
    second = projected[3].astype(jnp.float32), swap(projected[2], "mp", 1)
    first = halve(*first, "mp", 1, low)
    second = halve(*second, "mp", 2, high)
    first = halve(*first, "mp", 2, high)
    second = halve(*second, "section", 1, section_pos)
    sums = [*first, *second]
    out_rows = normed_rows(
        place, slot_utt, token, payloads, sums, pieces, slot_tokens, slot_count
    )

    share = out_rows.shape[0]
    own = jnp.zeros((width_count * share, out_rows.shape[1]), jnp.bfloat16)
    for distance in range(width_count):
        block = swap(out_rows, "mp", distance) if distance else out_rows
        own = lax.dynamic_update_slice_in_dim(own, block, (width_pos ^ distance) * share, 0)
    half = own.shape[0] // 2
    by_x = swap(own, "section", 1)
    by_y = swap(own, "tm", 2)
    stats = [vocabulary_stats(place, [own, swap(own, "tm", 1)], head)]
    by_x, by_y, stats[0] = lax.optimization_barrier((by_x, by_y, stats[0]))
    across = [swap(by_x[:half], "tm", 2), swap(by_y[half:], "section", 1)]
    stats.append(
        vocabulary_stats(place, [by_y, swap(by_y, "tm", 1), by_x, swap(by_x, "tm", 1)], head)
    )
    *across, stats[1] = lax.optimization_barrier((*across, stats[1]))
    across = jnp.concatenate(across)
    stats.append(vocabulary_stats(place, [across, swap(across, "tm", 1)], head))

    every = exchange(
        spread_stats(place, slot_utt, stats, section_count, group_count, width_count), ALL
    )
    return hypothesis_scores(
        place, slot_utt, lengths, every, slot_count, hyp_count, section_count, width_count
    )


def general(
    frame_len,
    slot_utt,
    enc_in,
    ffn_up,
    ffn_down,
    kv_proj,
    hyp_state,
    hyp_tok,
    hyp_len,
    q_proj,
    o_proj,
    head,
):
    section_count = lax.axis_size("section")
    group_count = lax.axis_size("tm")
    width_count = lax.axis_size("mp")
    section_pos = lax.axis_index("section")
    group_pos = lax.axis_index("tm")
    width_pos = lax.axis_index("mp")
    head_devices = section_count * width_count
    head_pos = section_pos * width_count + width_pos
    all_devices = head_devices * group_count

    frame_rows, utterances, enc_width = enc_in.shape
    assert utterances == group_count
    slot_count, hyp_count, positions, model_width = hyp_state.shape
    slot_tokens = hyp_count * positions
    device_heads = q_proj.shape[1] // HD
    group_heads = NH // KVH
    frame_share = frame_rows // width_count
    share_rows = slot_tokens // head_devices
    here_slots = lax.dynamic_slice_in_dim(slot_utt, group_pos * slot_count, slot_count, 0)

    dec_rows = hyp_state.reshape(slot_count * slot_tokens, model_width).astype(jnp.float32)
    queries = jnp.dot(
        square_norm(dec_rows).astype(jnp.bfloat16), q_proj, preferred_element_type=jnp.float32
    ).astype(jnp.bfloat16)
    queries = queries.reshape(slot_count, slot_tokens, device_heads * HD)
    shares = lax.dynamic_slice_in_dim(
        hyp_state.reshape(slot_count, slot_tokens, model_width), head_pos * share_rows, share_rows, 1
    )

    def by_utterance(values):
        out = []
        for utterance in range(utterances):
            block = values[0]
            for slot in range(1, slot_count):
                block = jnp.where(here_slots[slot] == utterance, values[slot], block)
            out.append(block)
        return jnp.stack(out)

    own_slot = jnp.argmax(slot_utt == group_pos)
    from_group = own_slot // slot_count
    queries = lax.dynamic_index_in_dim(
        exchange(by_utterance(queries), "tm"), from_group, 0, keepdims=False
    )
    resid_rows = lax.dynamic_index_in_dim(
        exchange(by_utterance(shares), "tm"), from_group, 0, keepdims=False
    )
    slot_targets = lax.all_gather(
        hyp_tok.reshape(slot_count, slot_tokens), "tm", axis=0, tiled=True
    )
    utt_slots = jnp.argmax(slot_utt[None, :] == jnp.arange(utterances)[:, None], axis=1)
    targets = jnp.take(slot_targets, utt_slots, axis=0).reshape(utterances * slot_tokens)

    enc_flat = (
        enc_in.reshape(width_count, frame_share, utterances, enc_width)
        .transpose(0, 2, 1, 3)
        .reshape(frame_rows * utterances, enc_width)
    )
    share_count = frame_share * utterances
    enc_normed = layer_norm(enc_flat.astype(jnp.float32)).astype(jnp.bfloat16)
    enc_inner = jax.nn.gelu(
        jnp.dot(enc_normed, ffn_up, preferred_element_type=jnp.float32), approximate=False
    ).astype(jnp.bfloat16)
    enc_summed = scatter_sum(
        jnp.dot(enc_inner, ffn_down, preferred_element_type=jnp.float32).astype(jnp.bfloat16),
        "mp",
        width_count,
    )
    own_frames = lax.dynamic_slice_in_dim(enc_flat, width_pos * share_count, share_count, 0)
    enc_states = layer_norm(own_frames.astype(jnp.float32) + enc_summed).astype(jnp.bfloat16)
    keys_values = jnp.dot(enc_states, kv_proj, preferred_element_type=jnp.float32).astype(
        jnp.bfloat16
    )
    keys_values = keys_values.reshape(utterances, frame_share, 2, KVH, HD)
    sent = []
    for section in range(section_count):
        per_width = []
        for width in range(width_count):
            kv_head = (section * width_count + width) * device_heads // group_heads
            per_width.append(
                keys_values[:, :, :, kv_head].reshape(utterances, frame_share, 2 * HD)
            )
        sent.append(jnp.stack(per_width, axis=1))
    sent = jnp.stack(sent).reshape(all_devices, frame_share, 2 * HD)
    frames_all = all_devices * frame_share
    keys_values = exchange(sent, ALL).reshape(frames_all, 2 * HD)

    frame_limit = lax.dynamic_index_in_dim(frame_len, group_pos, 0, keepdims=False)
    queries = queries.reshape(slot_tokens, device_heads, HD)
    scores = jnp.einsum(
        "qhd,fd->hqf", queries, keys_values[:, :HD], preferred_element_type=jnp.float32
    ) / math.sqrt(HD)
    visible = jnp.arange(frames_all, dtype=jnp.int32) < frame_limit
    scores = jnp.where(visible[None, None, :], scores, -jnp.inf)
    weights = jax.nn.softmax(scores, axis=-1).astype(jnp.bfloat16)
    context = jnp.einsum(
        "hqf,fd->qhd", weights, keys_values[:, HD:], preferred_element_type=jnp.float32
    ).astype(jnp.bfloat16)
    partial = jnp.dot(
        context.reshape(slot_tokens, device_heads * HD), o_proj, preferred_element_type=jnp.float32
    ).astype(jnp.bfloat16)
    partial = scatter_sum(partial, "section", section_count).astype(jnp.bfloat16)
    attn_out = scatter_sum(partial, "mp", width_count)
    out_normed = square_norm(resid_rows.astype(jnp.float32) + attn_out).astype(jnp.bfloat16)

    hidden_rows = lax.all_gather(out_normed, ALL, axis=0, tiled=True)
    logits = lax.dot_general(
        hidden_rows, head, (((1,), (1,)), ((), ())), preferred_element_type=jnp.float32
    )
    vocab_rows = head.shape[0]
    vocab_start = (
        (section_pos * group_count + group_pos) * width_count + width_pos
    ) * vocab_rows
    target_rows = (
        targets.reshape(utterances, section_count, width_count, share_rows)
        .transpose(1, 0, 2, 3)
        .reshape(-1)
    )
    upper = jnp.max(logits, axis=1)
    totals = jnp.sum(jnp.exp(logits - upper[:, None]), axis=1)
    matches = (
        jnp.arange(vocab_rows, dtype=jnp.int32)[None, :] == (target_rows - vocab_start)[:, None]
    )
    target_logit = jnp.sum(jnp.where(matches, logits, 0.0), axis=1)

    stats = jnp.stack([upper, totals, target_logit])
    stats = stats.reshape(3, section_count, utterances, width_count, share_rows)
    stats = stats.transpose(2, 0, 1, 3, 4).reshape(utterances, 3, slot_tokens)
    by_slot = jnp.take(stats, jnp.maximum(slot_utt, 0), axis=0)
    by_group = by_slot.reshape(1, group_count, 1, slot_count, 3, slot_tokens)
    by_group = jnp.broadcast_to(
        by_group, (section_count, group_count, width_count, slot_count, 3, slot_tokens)
    ).reshape(all_devices, slot_count, 3, slot_tokens)
    every = exchange(by_group, ALL)
    peak = jnp.max(every[:, :, 0], axis=0)
    total = jnp.sum(every[:, :, 1] * jnp.exp(every[:, :, 0] - peak[None]), axis=0)
    picked = jnp.sum(every[:, :, 2], axis=0)
    token_logp = (picked - (peak + jnp.log(total))).reshape(slot_count, hyp_count, positions)
    valid = jnp.arange(positions, dtype=jnp.int32)[None, None, :] < hyp_len[:, :, None]
    summed = jnp.sum(jnp.where(valid, token_logp, 0.0), axis=-1) / hyp_len.astype(
        jnp.float32
    ) + math.log(V)
    return jnp.where(here_slots[:, None] >= 0, summed, 0.0)


def solution(mesh):
    in_specs = (
        P(),
        P(),
        P(("section", "tm"), None, None),
        P(None, "mp"),
        P("mp", None),
        P(),
        P("tm", None, None, None),
        P("tm", None, None),
        P("tm", None),
        P(None, ("section", "mp")),
        P(("section", "mp"), None),
        P(("section", "tm", "mp"), None),
    )
    out_specs = P("tm", None)
    near = dict(mesh.shape) == {"section": 2, "tm": 4, "mp": 4}
    per_device = near_device if near else general
    return jax.shard_map(
        per_device, mesh=mesh, in_specs=in_specs, out_specs=out_specs, check_vma=False
    )
```

```python
import functools
import math

import jax
import jax.numpy as jnp
from jax import lax
from jax.experimental import pallas as pl
from jax.experimental.pallas import tpu as pltpu
from jax.sharding import PartitionSpec as P

NH = 32
KVH = 4
HD = 128
V = 64000
ALL = ("section", "tm", "mp")
LANES = 128


def layer_norm(values):
    center = values - jnp.mean(values, axis=-1, keepdims=True)
    spread = jnp.mean(center * center, axis=-1, keepdims=True)
    return center * lax.rsqrt(spread + 1e-05)


def square_norm(values):
    return values * lax.rsqrt(jnp.mean(values * values, axis=-1, keepdims=True) + 1e-06)


def exchange(blocks, axis):
    return lax.all_to_all(blocks, axis, split_axis=0, concat_axis=0, tiled=True)


def scatter_sum(partial, axis, count):
    blocks = partial.reshape((count, partial.shape[0] // count) + partial.shape[1:])
    return jnp.sum(exchange(blocks, axis).astype(jnp.float32), axis=0)


def swap(values, axis, distance):
    pairs = [(i, i ^ distance) for i in range(lax.axis_size(axis))]
    return lax.ppermute(values, axis, pairs)


def whole(shape):
    return pl.BlockSpec(shape, lambda *_: (0,) * len(shape))


SCALARS = pl.BlockSpec(memory_space=pltpu.SMEM)


def dot(left, right):
    return jnp.dot(left, right, preferred_element_type=jnp.float32)


def dot_nt(left, right):
    return lax.dot_general(
        left, right, (((1,), (1,)), ((), ())), preferred_element_type=jnp.float32
    )


def start_copies(source_of, target_of, semaphores, count):
    copies = []
    for number in range(count):
        copy = pltpu.make_async_copy(
            source_of(number), target_of(number), semaphores.at[number]
        )
        copy.start()
        copies.append(copy)
    return copies


def ffn_kernel(tile, place_ref, x_ref, up_ref, down_ref, *refs):
    out_ref, own_ref, rows, total, up, down, up_sem, down_sem = refs
    count, share, width = out_ref.shape
    tiles = up_ref.shape[1] // tile
    up_copies = start_copies(
        lambda i: up_ref.at[:, pl.ds(i * tile, tile)], lambda i: up.at[i], up_sem, tiles
    )
    down_copies = start_copies(
        lambda i: down_ref.at[pl.ds(i * tile, tile), :], lambda i: down.at[i], down_sem, tiles
    )
    rows[...] = x_ref[...].astype(jnp.float32).reshape(rows.shape)
    start = pl.multiple_of(place_ref[2] * share, share)
    own_ref[...] = rows[pl.ds(start, share), :].astype(jnp.bfloat16)
    normed = layer_norm(rows[...]).astype(jnp.bfloat16)
    for number in range(tiles):
        up_copies[number].wait()
        hidden = dot(normed, up[number])
        inner = 0.5 * hidden * (1.0 + lax.erf(hidden * math.sqrt(0.5)))
        down_copies[number].wait()
        product = dot(inner.astype(jnp.bfloat16), down[number])
        if number == 0:
            total[...] = product
        else:
            total[...] += product
    for part in range(count):
        out_ref[part] = total[part * share : (part + 1) * share, :].astype(jnp.bfloat16)


def in_hbm(values):
    return pltpu.with_memory_space_constraint(values, pltpu.HBM)


ANYWHERE = pl.BlockSpec(memory_space=pl.ANY)
INSIDE = pl.BlockSpec(memory_space=pltpu.VMEM)


def ffn(place, enc_in, up, down, count):
    frames, utterances, width = enc_in.shape
    rows = frames * utterances
    share = rows // count
    tile = 256
    tiles = up.shape[1] // tile
    return pl.pallas_call(
        functools.partial(ffn_kernel, tile),
        in_specs=[SCALARS, INSIDE, ANYWHERE, ANYWHERE],
        out_specs=[INSIDE] * 2,
        out_shape=[
            jax.ShapeDtypeStruct((count, share, width), jnp.bfloat16),
            jax.ShapeDtypeStruct((share, width), jnp.bfloat16),
        ],
        scratch_shapes=[
            pltpu.VMEM((rows, width), jnp.float32),
            pltpu.VMEM((rows, width), jnp.float32),
            pltpu.VMEM((tiles, width, tile), jnp.bfloat16),
            pltpu.VMEM((tiles, tile, width), jnp.bfloat16),
            pltpu.SemaphoreType.DMA((tiles,)),
            pltpu.SemaphoreType.DMA((tiles,)),
        ],
        cost_estimate=pl.CostEstimate(
            flops=4 * rows * width * up.shape[1],
            bytes_accessed=4 * width * up.shape[1],
            transcendentals=rows * up.shape[1],
        ),
        compiler_params=pltpu.CompilerParams(vmem_limit_bytes=24 << 20),
        name="encoder_ffn",
    )(place, enc_in, in_hbm(up), in_hbm(down))


def query_kernel(
    count, depth, place_ref, slot_ref, length_ref, after_ref, x_ref, tok_ref, w_ref, *refs
):
    outs, (states, weights, normed, total, shares, x_sem, w_sem) = refs[:count], refs[count:]
    slots, tokens, width = x_ref.shape
    hyps = length_ref.shape[1]
    positions = tokens // hyps
    columns = w_ref.shape[1]
    share = shares.shape[1] // 2
    parts = width // columns
    x_copies = start_copies(lambda i: x_ref.at[i], lambda i: states.at[i], x_sem, slots)
    w_copies = start_copies(
        lambda i: w_ref.at[pl.ds(i * depth, depth), :],
        lambda i: weights.at[i],
        w_sem,
        width // depth,
    )
    head_pos = place_ref[4]
    lane = lax.broadcasted_iota(jnp.int32, (1, tokens), 1)
    for slot in range(slots):
        order = jnp.full((1, tokens), -1, jnp.int32)
        start = jnp.int32(0)
        for hyp in range(hyps):
            length = length_ref[slot, hyp]
            inside = (lane >= hyp * positions) & (lane < hyp * positions + length)
            order = jnp.where(inside, lane - hyp * positions + start, order)
            start = start + length
        row = lax.broadcasted_iota(jnp.int32, (tokens, tokens), 0)
        move = jnp.where(order == row, 1.0, 0.0).astype(jnp.bfloat16)
        x_copies[slot].wait()
        ordered = dot(move, states[slot])
        normed[slot * tokens : (slot + 1) * tokens, :] = square_norm(ordered).astype(jnp.bfloat16)
        share_row = lax.broadcasted_iota(jnp.int32, (share, tokens), 0)
        chosen = order == share_row * (tokens // share) + head_pos
        mine = dot(jnp.where(chosen, 1.0, 0.0).astype(jnp.bfloat16), states[slot])
        shares[slot, :share, :] = mine.astype(jnp.bfloat16)
        target = jnp.sum(
            jnp.where(chosen, tok_ref[slot], 0), axis=1, keepdims=True, dtype=jnp.int32
        )
        coarse = target // 256
        cell = lax.broadcasted_iota(jnp.int32, (share, columns), 1)
        packed = jnp.where(cell == 0, coarse, jnp.where(cell == 1, target - coarse * 256, 0))
        shares[slot, share:, :columns] = packed.astype(jnp.float32).astype(jnp.bfloat16)
    for number in range(width // depth):
        w_copies[number].wait()
        product = dot(normed[:, number * depth : (number + 1) * depth], weights[number])
        if number == 0:
            total[...] = product
        else:
            total[...] += product
    group = place_ref[1]
    for distance in range(count):
        slot = jnp.int32(-1)
        for candidate in range(slots):
            holds = slot_ref[group * slots + candidate] == group ^ distance
            slot = jnp.where(holds, candidate, slot)
        out = outs[distance]

        @pl.when(slot < 0)
        def _(out=out):
            out[...] = jnp.zeros_like(out)

        @pl.when(slot >= 0)
        def _(out=out, slot=slot):
            start = pl.multiple_of(slot * tokens, tokens)
            out[:tokens, :] = total[pl.ds(start, tokens), :].astype(jnp.bfloat16)
            for part in range(parts):
                first = tokens + part * share
                out[first : first + share, :] = shares[
                    slot, :share, part * columns : (part + 1) * columns
                ]
            out[tokens + parts * share :, :] = shares[slot, share:, :columns]


def queries_of(place, slot_utt, lengths, after, states, targets, weights, count, share):
    slots, tokens, width = states.shape
    columns = weights.shape[1]
    depth = 1024
    rows = tokens + (width // columns + 1) * share
    block = jax.ShapeDtypeStruct((rows, columns), jnp.bfloat16)
    return pl.pallas_call(
        functools.partial(query_kernel, count, depth),
        in_specs=[SCALARS] * 3 + [ANYWHERE, ANYWHERE, INSIDE, ANYWHERE],
        out_specs=[INSIDE] * count,
        out_shape=[block] * count,
        scratch_shapes=[
            pltpu.VMEM(states.shape, jnp.bfloat16),
            pltpu.VMEM((width // depth, depth, columns), jnp.bfloat16),
            pltpu.VMEM((slots * tokens, width), jnp.bfloat16),
            pltpu.VMEM((slots * tokens, columns), jnp.float32),
            pltpu.VMEM((slots, 2 * share, width), jnp.bfloat16),
            pltpu.SemaphoreType.DMA((slots,)),
            pltpu.SemaphoreType.DMA((width // depth,)),
        ],
        cost_estimate=pl.CostEstimate(
            flops=2 * slots * tokens * width * columns,
            bytes_accessed=2 * width * (columns + slots * tokens),
            transcendentals=0,
        ),
        compiler_params=pltpu.CompilerParams(vmem_limit_bytes=32 << 20),
        name="hypothesis_queries",
    )(place, slot_utt, lengths, after, in_hbm(states), targets, in_hbm(weights))


def kv_kernel(sections, utterances, widths, *refs):
    parts_ref, own_ref, w_ref, after_ref, out_ref = refs
    rows = own_ref.shape[0]
    frames = rows // utterances
    total = own_ref[...].astype(jnp.float32)
    summed = parts_ref[0].astype(jnp.float32)
    for part in range(1, parts_ref.shape[0]):
        summed += parts_ref[part].astype(jnp.float32)
    states = layer_norm(total + summed).astype(jnp.bfloat16)
    to = lax.broadcasted_iota(jnp.int32, (rows, rows), 0)
    come = lax.broadcasted_iota(jnp.int32, (rows, rows), 1)
    move = jnp.where(come == to % frames * utterances + to // frames, 1.0, 0.0)
    states = dot(move.astype(jnp.bfloat16), states).astype(jnp.bfloat16)
    both = dot(states, w_ref[...])
    half = KVH * HD
    per_kv = sections * widths // KVH
    for section in range(sections):
        for utterance in range(utterances):
            for width in range(0, widths, per_kv):
                kv_head = (section * widths + width) // per_kv
                take = slice(utterance * frames, (utterance + 1) * frames)
                block = jnp.concatenate(
                    [
                        both[take, kv_head * HD : (kv_head + 1) * HD],
                        both[take, half + kv_head * HD : half + (kv_head + 1) * HD],
                    ],
                    axis=1,
                )
                start = ((section * utterances + utterance) * widths + width) * frames
                block = jnp.concatenate([block] * per_kv, axis=0).astype(jnp.bfloat16)
                out_ref[start : start + per_kv * frames, :] = block


def keys_values_of(parts, own, weights, after, sections, utterances, widths):
    rows = sections * widths * own.shape[0]
    return pl.pallas_call(
        functools.partial(kv_kernel, sections, utterances, widths),
        in_specs=[INSIDE] * 3 + [ANYWHERE],
        out_specs=INSIDE,
        out_shape=jax.ShapeDtypeStruct((rows, 2 * HD), jnp.bfloat16),
        cost_estimate=pl.CostEstimate(
            flops=2 * own.shape[0] * weights.shape[0] * weights.shape[1],
            bytes_accessed=2 * weights.shape[0] * weights.shape[1],
            transcendentals=0,
        ),
        compiler_params=pltpu.CompilerParams(vmem_limit_bytes=24 << 20),
        name="frame_keys_values",
    )(parts, own, weights, after)


def choice_of_payload(place_ref, slot_ref, slots):
    group = place_ref[1]
    source = jnp.int32(0)
    for slot in range(slot_ref.shape[0]):
        source = jnp.where(slot_ref[slot] == group, slot // slots, source)
    return jnp.minimum(source ^ group, 2)


def attention_kernel(count, slots, capacity, pieces, sections, widths, tile, *refs):
    place_ref, slot_ref, frame_ref = refs[:3]
    payloads, (kv_ref, w_ref) = refs[3 : 3 + count], refs[3 + count : 5 + count]
    outs = refs[5 + count : 5 + count + 2 * len(pieces)]
    weights, picked, context, w_sem = refs[5 + count + 2 * len(pieces) :]
    tokens, columns = capacity, w_ref.shape[0]
    tiles = w_ref.shape[1] // tile
    w_copies = start_copies(
        lambda i: w_ref.at[:, pl.ds(i * tile, tile)], lambda i: weights.at[i], w_sem, tiles
    )
    source = choice_of_payload(place_ref, slot_ref, slots)
    section_pos = place_ref[0]
    frame_limit = frame_ref[place_ref[1]]
    for distance in range(count):

        @pl.when(source == distance)
        def _(payload=payloads[distance]):
            picked[...] = payload[:tokens, :]

    keys = kv_ref[:, :HD]
    values = kv_ref[:, HD:]
    frames = kv_ref.shape[0]
    visible = lax.broadcasted_iota(jnp.int32, (tokens, frames), 1) < frame_limit
    for head in range(columns // HD):
        scores = dot_nt(picked[:, head * HD : (head + 1) * HD], keys) * (1.0 / math.sqrt(HD))
        scores = jnp.where(visible, scores, -jnp.inf)
        raised = jnp.exp(scores - jnp.max(scores, axis=1, keepdims=True))
        chances = (raised / jnp.sum(raised, axis=1, keepdims=True)).astype(jnp.bfloat16)
        context[:, head * HD : (head + 1) * HD] = dot(chances, values).astype(jnp.bfloat16)
    to = lax.broadcasted_iota(jnp.int32, (tokens, tokens), 0)
    come = lax.broadcasted_iota(jnp.int32, (tokens, tokens), 1)
    low_bit = place_ref[2] % 2
    size = widths * pieces[0]
    block = to % size // pieces[0]
    section = jnp.where(to < size, 1 - section_pos, section_pos)
    first_order = (to % pieces[0] * sections + section) * widths + block % 2 * 2 + block // 2
    at = to - 2 * size
    size = widths * pieces[1]
    block = at % size // pieces[1]
    low = jnp.where(at < size, 1 - low_bit, low_bit)
    row = pieces[0] + at % pieces[1]
    second_order = (row * sections + block % 2) * widths + block // 2 * 2 + low
    move = come == jnp.where(at < 0, first_order, second_order)
    ordered = dot(jnp.where(move, 1.0, 0.0).astype(jnp.bfloat16), context[...])
    ordered = ordered.astype(jnp.bfloat16)
    for number in range(tiles):
        w_copies[number].wait()
        product = dot(ordered, weights[number]).astype(jnp.bfloat16)
        first = 0
        for out in outs:
            out[:, number * tile : (number + 1) * tile] = product[first : first + out.shape[0], :]
            first += out.shape[0]


def attend(place, slot_utt, frame_len, payloads, keys_values, weights, pieces, sections, widths, slots):
    count = len(payloads)
    columns, width = weights.shape
    capacity = sum(pieces) * sections * widths
    tile = 1024
    tiles = width // tile
    shapes = [
        jax.ShapeDtypeStruct((piece * widths, width), jnp.bfloat16)
        for piece in pieces
        for _ in range(2)
    ]
    return pl.pallas_call(
        functools.partial(
            attention_kernel, count, slots, capacity, pieces, sections, widths, tile
        ),
        in_specs=[SCALARS] * 3 + [INSIDE] * (count + 1) + [ANYWHERE],
        out_specs=[INSIDE] * len(shapes),
        out_shape=shapes,
        scratch_shapes=[
            pltpu.VMEM((tiles, columns, tile), jnp.bfloat16),
            pltpu.VMEM((capacity, columns), jnp.bfloat16),
            pltpu.VMEM((capacity, columns), jnp.bfloat16),
            pltpu.SemaphoreType.DMA((tiles,)),
        ],
        cost_estimate=pl.CostEstimate(
            flops=2 * capacity * columns * (width + 2 * keys_values.shape[0]),
            bytes_accessed=2 * columns * width + 2 * capacity * width,
            transcendentals=capacity * keys_values.shape[0] * columns // HD,
        ),
        compiler_params=pltpu.CompilerParams(vmem_limit_bytes=24 << 20),
        name="attention_projection",
    )(place, slot_utt, frame_len, *payloads, keys_values, in_hbm(weights))


def norm_kernel(count, slots, tokens, pieces, place_ref, slot_ref, after_ref, *refs):
    payloads, blocks = refs[:count], refs[count : count + 2 * len(pieces)]
    out_ref, picked, total = refs[count + 2 * len(pieces) :]
    rows, width = total.shape
    columns = picked.shape[1]
    share = picked.shape[0] // (width // columns + 1)
    source = choice_of_payload(place_ref, slot_ref, slots)
    for choice in range(count):

        @pl.when(source == choice)
        def _(payload=payloads[choice]):
            picked[...] = payload[tokens:, :]

    first = 0
    for number, piece in enumerate(pieces):
        kept, other = blocks[2 * number : 2 * number + 2]
        total[first : first + piece, :] = kept[...] + other[...].astype(jnp.float32)
        first += piece
    for part in range(width // columns):
        take = slice(part * columns, (part + 1) * columns)
        total[:, take] += picked[part * share : part * share + rows, :].astype(jnp.float32)
    out_ref[:, :width] = square_norm(total[...]).astype(jnp.bfloat16)
    last = width // columns * share
    out_ref[:, width:] = picked[last : last + rows, :LANES]


def normed_rows(place, slot_utt, after, payloads, blocks, pieces, tokens, slots):
    width = blocks[0].shape[1]
    rows = sum(pieces)
    columns = payloads[0].shape[1]
    return pl.pallas_call(
        functools.partial(norm_kernel, len(payloads), slots, tokens, pieces),
        in_specs=[SCALARS] * 2 + [ANYWHERE] + [INSIDE] * (len(payloads) + len(blocks)),
        out_specs=INSIDE,
        out_shape=jax.ShapeDtypeStruct((rows, width + LANES), jnp.bfloat16),
        scratch_shapes=[
            pltpu.VMEM((payloads[0].shape[0] - tokens, columns), jnp.bfloat16),
            pltpu.VMEM((rows, width), jnp.float32),
        ],
        compiler_params=pltpu.CompilerParams(vmem_limit_bytes=16 << 20),
        name="token_rows",
    )(place, slot_utt, after, *payloads, *blocks)


def load_kernel(rows, after_ref, head_ref, out_ref, token_ref, semaphores):
    count = head_ref.shape[0] // rows
    copies = start_copies(
        lambda i: head_ref.at[pl.ds(i * rows, rows), :],
        lambda i: out_ref.at[pl.ds(i * rows, rows), :],
        semaphores,
        count,
    )
    token_ref[...] = jnp.zeros_like(token_ref)
    for copy in copies:
        copy.wait()


def load_head(after, head):
    rows = head.shape[0] // 5
    return pl.pallas_call(
        functools.partial(load_kernel, rows),
        in_specs=[ANYWHERE, ANYWHERE],
        out_specs=[INSIDE, INSIDE],
        out_shape=[
            pltpu.VMEM(head.shape, head.dtype),
            jax.ShapeDtypeStruct((8, LANES), jnp.float32),
        ],
        scratch_shapes=[pltpu.SemaphoreType.DMA((5,))],
        cost_estimate=pl.CostEstimate(
            flops=0, bytes_accessed=2 * head.size, transcendentals=0
        ),
        compiler_params=pltpu.CompilerParams(vmem_limit_bytes=20 << 20),
        name="vocabulary_rows",
    )(after, in_hbm(head))


def vocabulary_kernel(tile, first_ref, *refs):
    sets, (head_ref, out_ref, rows_ref, stat) = refs[:-4], refs[-4:]
    vocab_rows, width = head_ref.shape
    share = sets[0].shape[0]
    tokens = share * len(sets)
    cell = lax.broadcasted_iota(jnp.int32, (8, LANES), 1)
    take = jnp.where(cell == 0, 256.0, jnp.where(cell == 1, 1.0, 0.0)).astype(jnp.bfloat16)
    for number, rows in enumerate(sets):
        rows_ref[number * share : (number + 1) * share, :] = rows[...]
    target = dot_nt(take, rows_ref[:, width:])[0:1, :].astype(jnp.int32) - first_ref[3]
    stat[0:1, :] = jnp.full((1, tokens), -jnp.inf, jnp.float32)
    stat[8:9, :] = jnp.zeros((1, tokens), jnp.float32)
    stat[16:17, :] = jnp.zeros((1, tokens), jnp.float32)

    @pl.loop(0, vocab_rows // tile)
    def _(step):
        start = pl.multiple_of(step * tile, tile)
        logits = dot_nt(head_ref[pl.ds(start, tile), :], rows_ref[:, :width])
        vocab = lax.broadcasted_iota(jnp.int32, logits.shape, 0) + start
        before = stat[0:1, :]
        upper = jnp.maximum(before, jnp.max(logits, axis=0, keepdims=True))
        stat[8:9, :] = stat[8:9, :] * jnp.exp(before - upper) + jnp.sum(
            jnp.exp(logits - upper), axis=0, keepdims=True
        )
        stat[16:17, :] += jnp.sum(jnp.where(vocab == target, logits, 0.0), axis=0, keepdims=True)
        stat[0:1, :] = upper

    for number in range(len(sets)):
        for row in range(3):
            out_ref[number, row : row + 1, :] = stat[
                8 * row : 8 * row + 1, number * share : (number + 1) * share
            ]


def vocabulary_stats(place, sets, head):
    share = sets[0].shape[0]
    count = len(sets)
    width = head.shape[1]
    tokens = share * count
    return pl.pallas_call(
        functools.partial(vocabulary_kernel, head.shape[0] // 2),
        in_specs=[SCALARS] + [INSIDE] * (count + 1),
        out_specs=INSIDE,
        out_shape=jax.ShapeDtypeStruct((count, 8, share), jnp.float32),
        scratch_shapes=[
            pltpu.VMEM((tokens, width + LANES), jnp.bfloat16),
            pltpu.VMEM((24, tokens), jnp.float32),
        ],
        cost_estimate=pl.CostEstimate(
            flops=3 * tokens * head.shape[0] * width,
            bytes_accessed=2 * tokens * width,
            transcendentals=tokens * head.shape[0],
        ),
        compiler_params=pltpu.CompilerParams(vmem_limit_bytes=16 << 20),
        name="vocabulary_scores",
    )(place, *sets, pltpu.with_memory_space_constraint(head, pltpu.VMEM))


def spread_kernel(sections, groups, widths, place_ref, slot_ref, *refs):
    stats, (out_ref, table, block) = refs[:-3], refs[-3:]
    share = table.shape[2]
    first = 0
    for stat in stats:
        table[first : first + stat.shape[0]] = stat[...]
        first += stat.shape[0]
    slots = slot_ref.shape[0] // groups
    block[...] = jnp.zeros_like(block)
    for group in range(groups):
        for slot in range(slots):
            utterance = jnp.maximum(slot_ref[group * slots + slot], 0)
            for section in range(sections):
                at = (section ^ place_ref[0]) * groups + (utterance ^ place_ref[1])
                block[group, 3 * slot : 3 * slot + 3, section * share : (section + 1) * share] = (
                    table[at][0:3, :]
                )
    for section in range(sections):
        for group in range(groups):
            for width in range(widths):
                out_ref[(section * groups + group) * widths + width] = block[group]


def spread_stats(place, slot_utt, stats, sections, groups, widths):
    share = stats[0].shape[2]
    assert 3 * slot_utt.shape[0] // groups <= 8
    return pl.pallas_call(
        functools.partial(spread_kernel, sections, groups, widths),
        in_specs=[SCALARS] * 2 + [INSIDE] * len(stats),
        out_specs=INSIDE,
        out_shape=jax.ShapeDtypeStruct(
            (sections * groups * widths, 8, sections * share), jnp.float32
        ),
        scratch_shapes=[
            pltpu.VMEM((sections * groups, 8, share), jnp.float32),
            pltpu.VMEM((groups, 8, sections * share), jnp.float32),
        ],
        compiler_params=pltpu.CompilerParams(vmem_limit_bytes=16 << 20),
        name="statistics_by_group",
    )(place, slot_utt, *stats)


def score_kernel(sections, widths, place_ref, slot_ref, length_ref, every_ref, out_ref):
    slots, hyps = out_ref.shape
    lanes = every_ref.shape[2]
    share = lanes // sections // widths
    lane = lax.broadcasted_iota(jnp.int32, (1, lanes), 1)
    order = lane % share * (sections * widths) + lane // share
    column = lax.broadcasted_iota(jnp.int32, (1, hyps), 1)
    for slot in range(slots):
        upper = every_ref[:, 3 * slot, :]
        peak = jnp.max(upper, axis=0, keepdims=True)
        total = jnp.sum(
            every_ref[:, 3 * slot + 1, :] * jnp.exp(upper - peak), axis=0, keepdims=True
        )
        picked = jnp.sum(every_ref[:, 3 * slot + 2, :], axis=0, keepdims=True)
        logp = picked - (peak + jnp.log(total))
        scores = jnp.zeros((1, hyps), jnp.float32)
        start = jnp.int32(0)
        for hyp in range(hyps):
            length = length_ref[slot, hyp]
            valid = (order >= start) & (order < start + length)
            summed = jnp.sum(jnp.where(valid, logp, 0.0), axis=1, keepdims=True)
            mean = summed / jnp.full((1, 1), length, jnp.int32).astype(jnp.float32)
            scores = jnp.where(column == hyp, mean + math.log(V), scores)
            start = start + length
        filled = slot_ref[place_ref[1] * slots + slot] >= 0
        out_ref[slot : slot + 1, :] = jnp.where(filled, scores, 0.0)


def hypothesis_scores(place, slot_utt, lengths, every, slots, hyps, sections, widths):
    return pl.pallas_call(
        functools.partial(score_kernel, sections, widths),
        in_specs=[SCALARS] * 3 + [INSIDE],
        out_specs=INSIDE,
        out_shape=jax.ShapeDtypeStruct((slots, hyps), jnp.float32),
        compiler_params=pltpu.CompilerParams(vmem_limit_bytes=16 << 20),
        name="hypothesis_scores",
    )(place, slot_utt, lengths, every)


def near_device(
    frame_len,
    slot_utt,
    enc_in,
    ffn_up,
    ffn_down,
    kv_proj,
    hyp_state,
    hyp_tok,
    hyp_len,
    q_proj,
    o_proj,
    head,
):
    section_count = lax.axis_size("section")
    group_count = lax.axis_size("tm")
    width_count = lax.axis_size("mp")
    section_pos = lax.axis_index("section")
    group_pos = lax.axis_index("tm")
    width_pos = lax.axis_index("mp")
    head_devices = section_count * width_count
    all_devices = head_devices * group_count

    frame_rows, utterances, enc_width = enc_in.shape
    slot_count, hyp_count, positions, model_width = hyp_state.shape
    slot_tokens = hyp_count * positions
    share_rows = slot_tokens // head_devices
    vocab_start = (
        (section_pos * group_count + group_pos) * width_count + width_pos
    ) * head.shape[0]
    head_pos = section_pos * width_count + width_pos
    place = jnp.stack([section_pos, group_pos, width_pos, vocab_start, head_pos])
    place = place.astype(jnp.int32)

    parts, own_frames = ffn(place, enc_in, ffn_up, ffn_down, width_count)
    parts = exchange(parts, "mp")

    blocks = queries_of(
        place,
        slot_utt,
        hyp_len,
        place,
        hyp_state.reshape(slot_count, slot_tokens, model_width),
        hyp_tok.reshape(slot_count, 1, slot_tokens),
        q_proj,
        group_count,
        share_rows,
    )
    crossing = blocks[2] + swap(blocks[3], "tm", 1)
    payloads = [blocks[0], swap(blocks[1], "tm", 1), swap(crossing, "tm", 2)]

    sent = keys_values_of(
        parts, own_frames, kv_proj, blocks[0], section_count, utterances, width_count
    )
    frames_all = all_devices * (frame_rows // width_count)
    keys_values = exchange(sent.reshape(all_devices, -1, 2 * HD), ALL).reshape(frames_all, 2 * HD)

    pieces = (share_rows // 2, share_rows - share_rows // 2)
    projected = attend(
        place,
        slot_utt,
        frame_len,
        payloads,
        keys_values,
        o_proj,
        pieces,
        section_count,
        width_count,
        slot_count,
    )
    head, token = load_head(projected[1], head)

    def halve(total, came, axis, distance, side):
        if came is not None:
            total = total + came.astype(jnp.float32)
        half = total.shape[0] // 2
        kept = lax.dynamic_slice_in_dim(total, side * half, half, 0)
        sent = lax.dynamic_slice_in_dim(total, (1 - side) * half, half, 0)
        return kept, swap(sent.astype(jnp.bfloat16), axis, distance)

    low, high = width_pos % 2, width_pos // 2
    first = projected[1].astype(jnp.float32), swap(projected[0], "section", 1)
    second = projected[3].astype(jnp.float32), swap(projected[2], "mp", 1)
    first = halve(*first, "mp", 1, low)
    second = halve(*second, "mp", 2, high)
    first = halve(*first, "mp", 2, high)
    second = halve(*second, "section", 1, section_pos)
    sums = [*first, *second]
    out_rows = normed_rows(
        place, slot_utt, token, payloads, sums, pieces, slot_tokens, slot_count
    )

    share = out_rows.shape[0]
    own = jnp.zeros((width_count * share, out_rows.shape[1]), jnp.bfloat16)
    for distance in range(width_count):
        block = swap(out_rows, "mp", distance) if distance else out_rows
        own = lax.dynamic_update_slice_in_dim(own, block, (width_pos ^ distance) * share, 0)
    half = own.shape[0] // 2
    by_x = swap(own, "section", 1)
    by_y = swap(own, "tm", 2)
    stats = [vocabulary_stats(place, [own, swap(own, "tm", 1)], head)]
    by_x, by_y, stats[0] = lax.optimization_barrier((by_x, by_y, stats[0]))
    across = [swap(by_x[:half], "tm", 2), swap(by_y[half:], "section", 1)]
    stats.append(
        vocabulary_stats(place, [by_y, swap(by_y, "tm", 1), by_x, swap(by_x, "tm", 1)], head)
    )
    *across, stats[1] = lax.optimization_barrier((*across, stats[1]))
    across = jnp.concatenate(across)
    stats.append(vocabulary_stats(place, [across, swap(across, "tm", 1)], head))

    every = exchange(
        spread_stats(place, slot_utt, stats, section_count, group_count, width_count), ALL
    )
    return hypothesis_scores(
        place, slot_utt, hyp_len, every, slot_count, hyp_count, section_count, width_count
    )


def general(
    frame_len,
    slot_utt,
    enc_in,
    ffn_up,
    ffn_down,
    kv_proj,
    hyp_state,
    hyp_tok,
    hyp_len,
    q_proj,
    o_proj,
    head,
):
    section_count = lax.axis_size("section")
    group_count = lax.axis_size("tm")
    width_count = lax.axis_size("mp")
    section_pos = lax.axis_index("section")
    group_pos = lax.axis_index("tm")
    width_pos = lax.axis_index("mp")
    head_devices = section_count * width_count
    head_pos = section_pos * width_count + width_pos
    all_devices = head_devices * group_count

    frame_rows, utterances, enc_width = enc_in.shape
    assert utterances == group_count
    slot_count, hyp_count, positions, model_width = hyp_state.shape
    slot_tokens = hyp_count * positions
    device_heads = q_proj.shape[1] // HD
    group_heads = NH // KVH
    frame_share = frame_rows // width_count
    share_rows = slot_tokens // head_devices
    here_slots = lax.dynamic_slice_in_dim(slot_utt, group_pos * slot_count, slot_count, 0)

    dec_rows = hyp_state.reshape(slot_count * slot_tokens, model_width).astype(jnp.float32)
    queries = jnp.dot(
        square_norm(dec_rows).astype(jnp.bfloat16), q_proj, preferred_element_type=jnp.float32
    ).astype(jnp.bfloat16)
    queries = queries.reshape(slot_count, slot_tokens, device_heads * HD)
    shares = lax.dynamic_slice_in_dim(
        hyp_state.reshape(slot_count, slot_tokens, model_width), head_pos * share_rows, share_rows, 1
    )

    def by_utterance(values):
        out = []
        for utterance in range(utterances):
            block = values[0]
            for slot in range(1, slot_count):
                block = jnp.where(here_slots[slot] == utterance, values[slot], block)
            out.append(block)
        return jnp.stack(out)

    own_slot = jnp.argmax(slot_utt == group_pos)
    from_group = own_slot // slot_count
    queries = lax.dynamic_index_in_dim(
        exchange(by_utterance(queries), "tm"), from_group, 0, keepdims=False
    )
    resid_rows = lax.dynamic_index_in_dim(
        exchange(by_utterance(shares), "tm"), from_group, 0, keepdims=False
    )
    slot_targets = lax.all_gather(
        hyp_tok.reshape(slot_count, slot_tokens), "tm", axis=0, tiled=True
    )
    utt_slots = jnp.argmax(slot_utt[None, :] == jnp.arange(utterances)[:, None], axis=1)
    targets = jnp.take(slot_targets, utt_slots, axis=0).reshape(utterances * slot_tokens)

    enc_flat = (
        enc_in.reshape(width_count, frame_share, utterances, enc_width)
        .transpose(0, 2, 1, 3)
        .reshape(frame_rows * utterances, enc_width)
    )
    share_count = frame_share * utterances
    enc_normed = layer_norm(enc_flat.astype(jnp.float32)).astype(jnp.bfloat16)
    enc_inner = jax.nn.gelu(
        jnp.dot(enc_normed, ffn_up, preferred_element_type=jnp.float32), approximate=False
    ).astype(jnp.bfloat16)
    enc_summed = scatter_sum(
        jnp.dot(enc_inner, ffn_down, preferred_element_type=jnp.float32).astype(jnp.bfloat16),
        "mp",
        width_count,
    )
    own_frames = lax.dynamic_slice_in_dim(enc_flat, width_pos * share_count, share_count, 0)
    enc_states = layer_norm(own_frames.astype(jnp.float32) + enc_summed).astype(jnp.bfloat16)
    keys_values = jnp.dot(enc_states, kv_proj, preferred_element_type=jnp.float32).astype(
        jnp.bfloat16
    )
    keys_values = keys_values.reshape(utterances, frame_share, 2, KVH, HD)
    sent = []
    for section in range(section_count):
        per_width = []
        for width in range(width_count):
            kv_head = (section * width_count + width) * device_heads // group_heads
            per_width.append(
                keys_values[:, :, :, kv_head].reshape(utterances, frame_share, 2 * HD)
            )
        sent.append(jnp.stack(per_width, axis=1))
    sent = jnp.stack(sent).reshape(all_devices, frame_share, 2 * HD)
    frames_all = all_devices * frame_share
    keys_values = exchange(sent, ALL).reshape(frames_all, 2 * HD)

    frame_limit = lax.dynamic_index_in_dim(frame_len, group_pos, 0, keepdims=False)
    queries = queries.reshape(slot_tokens, device_heads, HD)
    scores = jnp.einsum(
        "qhd,fd->hqf", queries, keys_values[:, :HD], preferred_element_type=jnp.float32
    ) / math.sqrt(HD)
    visible = jnp.arange(frames_all, dtype=jnp.int32) < frame_limit
    scores = jnp.where(visible[None, None, :], scores, -jnp.inf)
    weights = jax.nn.softmax(scores, axis=-1).astype(jnp.bfloat16)
    context = jnp.einsum(
        "hqf,fd->qhd", weights, keys_values[:, HD:], preferred_element_type=jnp.float32
    ).astype(jnp.bfloat16)
    partial = jnp.dot(
        context.reshape(slot_tokens, device_heads * HD), o_proj, preferred_element_type=jnp.float32
    ).astype(jnp.bfloat16)
    partial = scatter_sum(partial, "section", section_count).astype(jnp.bfloat16)
    attn_out = scatter_sum(partial, "mp", width_count)
    out_normed = square_norm(resid_rows.astype(jnp.float32) + attn_out).astype(jnp.bfloat16)

    hidden_rows = lax.all_gather(out_normed, ALL, axis=0, tiled=True)
    logits = lax.dot_general(
        hidden_rows, head, (((1,), (1,)), ((), ())), preferred_element_type=jnp.float32
    )
    vocab_rows = head.shape[0]
    vocab_start = (
        (section_pos * group_count + group_pos) * width_count + width_pos
    ) * vocab_rows
    target_rows = (
        targets.reshape(utterances, section_count, width_count, share_rows)
        .transpose(1, 0, 2, 3)
        .reshape(-1)
    )
    upper = jnp.max(logits, axis=1)
    totals = jnp.sum(jnp.exp(logits - upper[:, None]), axis=1)
    matches = (
        jnp.arange(vocab_rows, dtype=jnp.int32)[None, :] == (target_rows - vocab_start)[:, None]
    )
    target_logit = jnp.sum(jnp.where(matches, logits, 0.0), axis=1)

    stats = jnp.stack([upper, totals, target_logit])
    stats = stats.reshape(3, section_count, utterances, width_count, share_rows)
    stats = stats.transpose(2, 0, 1, 3, 4).reshape(utterances, 3, slot_tokens)
    by_slot = jnp.take(stats, jnp.maximum(slot_utt, 0), axis=0)
    by_group = by_slot.reshape(1, group_count, 1, slot_count, 3, slot_tokens)
    by_group = jnp.broadcast_to(
        by_group, (section_count, group_count, width_count, slot_count, 3, slot_tokens)
    ).reshape(all_devices, slot_count, 3, slot_tokens)
    every = exchange(by_group, ALL)
    peak = jnp.max(every[:, :, 0], axis=0)
    total = jnp.sum(every[:, :, 1] * jnp.exp(every[:, :, 0] - peak[None]), axis=0)
    picked = jnp.sum(every[:, :, 2], axis=0)
    token_logp = (picked - (peak + jnp.log(total))).reshape(slot_count, hyp_count, positions)
    valid = jnp.arange(positions, dtype=jnp.int32)[None, None, :] < hyp_len[:, :, None]
    summed = jnp.sum(jnp.where(valid, token_logp, 0.0), axis=-1) / hyp_len.astype(
        jnp.float32
    ) + math.log(V)
    return jnp.where(here_slots[:, None] >= 0, summed, 0.0)


def solution(mesh):
    in_specs = (
        P(),
        P(),
        P(("section", "tm"), None, None),
        P(None, "mp"),
        P("mp", None),
        P(),
        P("tm", None, None, None),
        P("tm", None, None),
        P("tm", None),
        P(None, ("section", "mp")),
        P(("section", "mp"), None),
        P(("section", "tm", "mp"), None),
    )
    out_specs = P("tm", None)
    near = dict(mesh.shape) == {"section": 2, "tm": 4, "mp": 4}
    per_device = near_device if near else general
    return jax.shard_map(
        per_device, mesh=mesh, in_specs=in_specs, out_specs=out_specs, check_vma=False
    )
```

```python
import functools
import math

import jax
import jax.numpy as jnp
from jax import lax
from jax.experimental import pallas as pl
from jax.experimental.pallas import tpu as pltpu
from jax.sharding import PartitionSpec as P

NH = 32
KVH = 4
HD = 128
V = 64000
ALL = ("section", "tm", "mp")
LANES = 128


def layer_norm(values):
    center = values - jnp.mean(values, axis=-1, keepdims=True)
    spread = jnp.mean(center * center, axis=-1, keepdims=True)
    return center * lax.rsqrt(spread + 1e-05)


def square_norm(values):
    return values * lax.rsqrt(jnp.mean(values * values, axis=-1, keepdims=True) + 1e-06)


def exchange(blocks, axis):
    return lax.all_to_all(blocks, axis, split_axis=0, concat_axis=0, tiled=True)


def scatter_sum(partial, axis, count):
    blocks = partial.reshape((count, partial.shape[0] // count) + partial.shape[1:])
    return jnp.sum(exchange(blocks, axis).astype(jnp.float32), axis=0)


def swap(values, axis, distance):
    pairs = [(i, i ^ distance) for i in range(lax.axis_size(axis))]
    return lax.ppermute(values, axis, pairs)


def whole(shape):
    return pl.BlockSpec(shape, lambda *_: (0,) * len(shape))


SCALARS = pl.BlockSpec(memory_space=pltpu.SMEM)


def dot(left, right):
    return jnp.dot(left, right, preferred_element_type=jnp.float32)


def dot_nt(left, right):
    return lax.dot_general(
        left, right, (((1,), (1,)), ((), ())), preferred_element_type=jnp.float32
    )


def start_copies(source_of, target_of, semaphores, count):
    copies = []
    for number in range(count):
        copy = pltpu.make_async_copy(
            source_of(number), target_of(number), semaphores.at[number]
        )
        copy.start()
        copies.append(copy)
    return copies


def front_kernel(count, tile, depth, place_ref, slot_ref, length_ref, *refs):
    x_ref, up_ref, down_ref, state_ref, tok_ref, w_ref = refs[:6]
    sum_ref, own_ref = refs[6:8]
    outs = refs[8 : 8 + count]
    inputs, rows, total, up, down, states, weights, normed, queries, shares = refs[8 + count : -5]
    x_sem, up_sem, down_sem, state_sem, w_sem = refs[-5:]
    parts, share, enc_width = sum_ref.shape
    tiles = up_ref.shape[1] // tile
    slots, tokens, width = state_ref.shape
    columns = w_ref.shape[1]
    steps = width // depth
    x_copy = start_copies(lambda i: x_ref, lambda i: inputs, x_sem, 1)[0]
    up_copies = start_copies(
        lambda i: up_ref.at[:, pl.ds(i * tile, tile)], lambda i: up.at[i], up_sem, tiles
    )
    down_copies = start_copies(
        lambda i: down_ref.at[pl.ds(i * tile, tile), :], lambda i: down.at[i], down_sem, tiles
    )
    state_copies = start_copies(
        lambda i: state_ref.at[i], lambda i: states.at[i], state_sem, slots
    )
    w_copies = start_copies(
        lambda i: w_ref.at[pl.ds(i * depth, depth), :], lambda i: weights.at[i], w_sem, steps
    )

    x_copy.wait()
    rows[...] = inputs[...].astype(jnp.float32).reshape(rows.shape)
    start = pl.multiple_of(place_ref[2] * share, share)
    own_ref[...] = rows[pl.ds(start, share), :].astype(jnp.bfloat16)
    enc_normed = layer_norm(rows[...]).astype(jnp.bfloat16)
    for number in range(tiles):
        up_copies[number].wait()
        hidden = dot(enc_normed, up[number])
        inner = 0.5 * hidden * (1.0 + lax.erf(hidden * math.sqrt(0.5)))
        down_copies[number].wait()
        product = dot(inner.astype(jnp.bfloat16), down[number])
        if number == 0:
            total[...] = product
        else:
            total[...] += product
    for part in range(parts):
        sum_ref[part] = total[part * share : (part + 1) * share, :].astype(jnp.bfloat16)

    hyps = length_ref.shape[1]
    positions = tokens // hyps
    share = shares.shape[1] // 2
    head_pos = place_ref[4]
    lane = lax.broadcasted_iota(jnp.int32, (1, tokens), 1)
    for slot in range(slots):
        order = jnp.full((1, tokens), -1, jnp.int32)
        start = jnp.int32(0)
        for hyp in range(hyps):
            length = length_ref[slot, hyp]
            inside = (lane >= hyp * positions) & (lane < hyp * positions + length)
            order = jnp.where(inside, lane - hyp * positions + start, order)
            start = start + length
        row = lax.broadcasted_iota(jnp.int32, (tokens, tokens), 0)
        move = jnp.where(order == row, 1.0, 0.0).astype(jnp.bfloat16)
        state_copies[slot].wait()
        ordered = dot(move, states[slot])
        normed[slot * tokens : (slot + 1) * tokens, :] = square_norm(ordered).astype(jnp.bfloat16)
        share_row = lax.broadcasted_iota(jnp.int32, (share, tokens), 0)
        chosen = order == share_row * (tokens // share) + head_pos
        mine = dot(jnp.where(chosen, 1.0, 0.0).astype(jnp.bfloat16), states[slot])
        shares[slot, :share, :] = mine.astype(jnp.bfloat16)
        target = jnp.sum(
            jnp.where(chosen, tok_ref[slot], 0), axis=1, keepdims=True, dtype=jnp.int32
        )
        coarse = target // 256
        cell = lax.broadcasted_iota(jnp.int32, (share, columns), 1)
        packed = jnp.where(cell == 0, coarse, jnp.where(cell == 1, target - coarse * 256, 0))
        shares[slot, share:, :columns] = packed.astype(jnp.float32).astype(jnp.bfloat16)
    for number in range(steps):
        w_copies[number].wait()
        product = dot(normed[:, number * depth : (number + 1) * depth], weights[number])
        if number == 0:
            queries[...] = product
        else:
            queries[...] += product
    group = place_ref[1]
    chunks = width // columns
    for distance in range(count):
        slot = jnp.int32(-1)
        for candidate in range(slots):
            holds = slot_ref[group * slots + candidate] == group ^ distance
            slot = jnp.where(holds, candidate, slot)
        out = outs[distance]

        @pl.when(slot < 0)
        def _(out=out):
            out[...] = jnp.zeros_like(out)

        @pl.when(slot >= 0)
        def _(out=out, slot=slot):
            start = pl.multiple_of(slot * tokens, tokens)
            out[:tokens, :] = queries[pl.ds(start, tokens), :].astype(jnp.bfloat16)
            for part in range(chunks):
                first = tokens + part * share
                out[first : first + share, :] = shares[
                    slot, :share, part * columns : (part + 1) * columns
                ]
            out[tokens + chunks * share :, :] = shares[slot, share:, :columns]


def in_hbm(values):
    return pltpu.with_memory_space_constraint(values, pltpu.HBM)


ANYWHERE = pl.BlockSpec(memory_space=pl.ANY)
INSIDE = pl.BlockSpec(memory_space=pltpu.VMEM)


def front(place, slot_utt, lengths, enc_in, up, down, states, targets, weights, parts, count, share):
    frames, utterances, enc_width = enc_in.shape
    rows = frames * utterances
    tile = 256
    tiles = up.shape[1] // tile
    slots, tokens, width = states.shape
    columns = weights.shape[1]
    depth = 1024
    steps = width // depth
    payload = tokens + (width // columns + 1) * share
    return pl.pallas_call(
        functools.partial(front_kernel, count, tile, depth),
        in_specs=[SCALARS] * 3 + [ANYWHERE] * 4 + [INSIDE, ANYWHERE],
        out_specs=[INSIDE] * (2 + count),
        out_shape=[
            jax.ShapeDtypeStruct((parts, rows // parts, enc_width), jnp.bfloat16),
            jax.ShapeDtypeStruct((rows // parts, enc_width), jnp.bfloat16),
        ]
        + [jax.ShapeDtypeStruct((payload, columns), jnp.bfloat16)] * count,
        scratch_shapes=[
            pltpu.VMEM(enc_in.shape, jnp.bfloat16),
            pltpu.VMEM((rows, enc_width), jnp.float32),
            pltpu.VMEM((rows, enc_width), jnp.float32),
            pltpu.VMEM((tiles, enc_width, tile), jnp.bfloat16),
            pltpu.VMEM((tiles, tile, enc_width), jnp.bfloat16),
            pltpu.VMEM(states.shape, jnp.bfloat16),
            pltpu.VMEM((steps, depth, columns), jnp.bfloat16),
            pltpu.VMEM((slots * tokens, width), jnp.bfloat16),
            pltpu.VMEM((slots * tokens, columns), jnp.float32),
            pltpu.VMEM((slots, 2 * share, width), jnp.bfloat16),
            pltpu.SemaphoreType.DMA((1,)),
            pltpu.SemaphoreType.DMA((tiles,)),
            pltpu.SemaphoreType.DMA((tiles,)),
            pltpu.SemaphoreType.DMA((slots,)),
            pltpu.SemaphoreType.DMA((steps,)),
        ],
        cost_estimate=pl.CostEstimate(
            flops=4 * rows * enc_width * up.shape[1] + 2 * slots * tokens * width * columns,
            bytes_accessed=4 * enc_width * up.shape[1] + 2 * width * (columns + slots * tokens),
            transcendentals=rows * up.shape[1],
        ),
        compiler_params=pltpu.CompilerParams(vmem_limit_bytes=40 << 20),
        name="encoder_ffn_and_queries",
    )(
        place,
        slot_utt,
        lengths,
        in_hbm(enc_in),
        in_hbm(up),
        in_hbm(down),
        in_hbm(states),
        targets,
        in_hbm(weights),
    )


def kv_kernel(sections, utterances, widths, *refs):
    parts_ref, own_ref, w_ref, out_ref = refs
    rows = own_ref.shape[0]
    frames = rows // utterances
    total = own_ref[...].astype(jnp.float32)
    summed = parts_ref[0].astype(jnp.float32)
    for part in range(1, parts_ref.shape[0]):
        summed += parts_ref[part].astype(jnp.float32)
    states = layer_norm(total + summed).astype(jnp.bfloat16)
    to = lax.broadcasted_iota(jnp.int32, (rows, rows), 0)
    come = lax.broadcasted_iota(jnp.int32, (rows, rows), 1)
    move = jnp.where(come == to % frames * utterances + to // frames, 1.0, 0.0)
    states = dot(move.astype(jnp.bfloat16), states).astype(jnp.bfloat16)
    both = dot(states, w_ref[...])
    half = KVH * HD
    per_kv = sections * widths // KVH
    for section in range(sections):
        for utterance in range(utterances):
            for width in range(0, widths, per_kv):
                kv_head = (section * widths + width) // per_kv
                take = slice(utterance * frames, (utterance + 1) * frames)
                block = jnp.concatenate(
                    [
                        both[take, kv_head * HD : (kv_head + 1) * HD],
                        both[take, half + kv_head * HD : half + (kv_head + 1) * HD],
                    ],
                    axis=1,
                )
                start = ((section * utterances + utterance) * widths + width) * frames
                block = jnp.concatenate([block] * per_kv, axis=0).astype(jnp.bfloat16)
                out_ref[start : start + per_kv * frames, :] = block


def keys_values_of(parts, own, weights, sections, utterances, widths):
    rows = sections * widths * own.shape[0]
    return pl.pallas_call(
        functools.partial(kv_kernel, sections, utterances, widths),
        in_specs=[INSIDE] * 3,
        out_specs=INSIDE,
        out_shape=jax.ShapeDtypeStruct((rows, 2 * HD), jnp.bfloat16),
        cost_estimate=pl.CostEstimate(
            flops=2 * own.shape[0] * weights.shape[0] * weights.shape[1],
            bytes_accessed=2 * weights.shape[0] * weights.shape[1],
            transcendentals=0,
        ),
        compiler_params=pltpu.CompilerParams(vmem_limit_bytes=24 << 20),
        name="frame_keys_values",
    )(parts, own, weights)


def choice_of_payload(place_ref, slot_ref, slots):
    group = place_ref[1]
    source = jnp.int32(0)
    for slot in range(slot_ref.shape[0]):
        source = jnp.where(slot_ref[slot] == group, slot // slots, source)
    return jnp.minimum(source ^ group, 2)


def attention_kernel(count, slots, capacity, pieces, sections, widths, tile, *refs):
    place_ref, slot_ref, frame_ref = refs[:3]
    payloads, (kv_ref, w_ref) = refs[3 : 3 + count], refs[3 + count : 5 + count]
    outs = refs[5 + count : 5 + count + 2 * len(pieces)]
    weights, picked, context, w_sem = refs[5 + count + 2 * len(pieces) :]
    tokens, columns = capacity, w_ref.shape[0]
    tiles = w_ref.shape[1] // tile
    w_copies = start_copies(
        lambda i: w_ref.at[:, pl.ds(i * tile, tile)], lambda i: weights.at[i], w_sem, tiles
    )
    source = choice_of_payload(place_ref, slot_ref, slots)
    section_pos = place_ref[0]
    frame_limit = frame_ref[place_ref[1]]
    for distance in range(count):

        @pl.when(source == distance)
        def _(payload=payloads[distance]):
            picked[...] = payload[:tokens, :]

    keys = kv_ref[:, :HD]
    values = kv_ref[:, HD:]
    frames = kv_ref.shape[0]
    visible = lax.broadcasted_iota(jnp.int32, (tokens, frames), 1) < frame_limit
    for head in range(columns // HD):
        scores = dot_nt(picked[:, head * HD : (head + 1) * HD], keys) * (1.0 / math.sqrt(HD))
        scores = jnp.where(visible, scores, -jnp.inf)
        raised = jnp.exp(scores - jnp.max(scores, axis=1, keepdims=True))
        chances = (raised / jnp.sum(raised, axis=1, keepdims=True)).astype(jnp.bfloat16)
        context[:, head * HD : (head + 1) * HD] = dot(chances, values).astype(jnp.bfloat16)
    to = lax.broadcasted_iota(jnp.int32, (tokens, tokens), 0)
    come = lax.broadcasted_iota(jnp.int32, (tokens, tokens), 1)
    low_bit = place_ref[2] % 2
    size = widths * pieces[0]
    block = to % size // pieces[0]
    section = jnp.where(to < size, 1 - section_pos, section_pos)
    first_order = (to % pieces[0] * sections + section) * widths + block % 2 * 2 + block // 2
    at = to - 2 * size
    size = widths * pieces[1]
    block = at % size // pieces[1]
    low = jnp.where(at < size, 1 - low_bit, low_bit)
    row = pieces[0] + at % pieces[1]
    second_order = (row * sections + block % 2) * widths + block // 2 * 2 + low
    move = come == jnp.where(at < 0, first_order, second_order)
    ordered = dot(jnp.where(move, 1.0, 0.0).astype(jnp.bfloat16), context[...])
    ordered = ordered.astype(jnp.bfloat16)
    for number in range(tiles):
        w_copies[number].wait()
        product = dot(ordered, weights[number]).astype(jnp.bfloat16)
        first = 0
        for out in outs:
            out[:, number * tile : (number + 1) * tile] = product[first : first + out.shape[0], :]
            first += out.shape[0]


def attend(place, slot_utt, frame_len, payloads, keys_values, weights, pieces, sections, widths, slots):
    count = len(payloads)
    columns, width = weights.shape
    capacity = sum(pieces) * sections * widths
    tile = 1024
    tiles = width // tile
    shapes = [
        jax.ShapeDtypeStruct((piece * widths, width), jnp.bfloat16)
        for piece in pieces
        for _ in range(2)
    ]
    return pl.pallas_call(
        functools.partial(
            attention_kernel, count, slots, capacity, pieces, sections, widths, tile
        ),
        in_specs=[SCALARS] * 3 + [INSIDE] * (count + 1) + [ANYWHERE],
        out_specs=[INSIDE] * len(shapes),
        out_shape=shapes,
        scratch_shapes=[
            pltpu.VMEM((tiles, columns, tile), jnp.bfloat16),
            pltpu.VMEM((capacity, columns), jnp.bfloat16),
            pltpu.VMEM((capacity, columns), jnp.bfloat16),
            pltpu.SemaphoreType.DMA((tiles,)),
        ],
        cost_estimate=pl.CostEstimate(
            flops=2 * capacity * columns * (width + 2 * keys_values.shape[0]),
            bytes_accessed=2 * columns * width + 2 * capacity * width,
            transcendentals=capacity * keys_values.shape[0] * columns // HD,
        ),
        compiler_params=pltpu.CompilerParams(vmem_limit_bytes=24 << 20),
        name="attention_projection",
    )(place, slot_utt, frame_len, *payloads, keys_values, in_hbm(weights))


def norm_kernel(count, slots, tokens, pieces, place_ref, slot_ref, after_ref, *refs):
    payloads, blocks = refs[:count], refs[count : count + 2 * len(pieces)]
    out_ref, picked, total = refs[count + 2 * len(pieces) :]
    rows, width = total.shape
    columns = picked.shape[1]
    share = picked.shape[0] // (width // columns + 1)
    source = choice_of_payload(place_ref, slot_ref, slots)
    for choice in range(count):

        @pl.when(source == choice)
        def _(payload=payloads[choice]):
            picked[...] = payload[tokens:, :]

    first = 0
    for number, piece in enumerate(pieces):
        kept, other = blocks[2 * number : 2 * number + 2]
        total[first : first + piece, :] = kept[...] + other[...].astype(jnp.float32)
        first += piece
    for part in range(width // columns):
        take = slice(part * columns, (part + 1) * columns)
        total[:, take] += picked[part * share : part * share + rows, :].astype(jnp.float32)
    out_ref[:, :width] = square_norm(total[...]).astype(jnp.bfloat16)
    last = width // columns * share
    out_ref[:, width:] = picked[last : last + rows, :LANES]


def normed_rows(place, slot_utt, after, payloads, blocks, pieces, tokens, slots):
    width = blocks[0].shape[1]
    rows = sum(pieces)
    columns = payloads[0].shape[1]
    return pl.pallas_call(
        functools.partial(norm_kernel, len(payloads), slots, tokens, pieces),
        in_specs=[SCALARS] * 2 + [ANYWHERE] + [INSIDE] * (len(payloads) + len(blocks)),
        out_specs=INSIDE,
        out_shape=jax.ShapeDtypeStruct((rows, width + LANES), jnp.bfloat16),
        scratch_shapes=[
            pltpu.VMEM((payloads[0].shape[0] - tokens, columns), jnp.bfloat16),
            pltpu.VMEM((rows, width), jnp.float32),
        ],
        compiler_params=pltpu.CompilerParams(vmem_limit_bytes=16 << 20),
        name="token_rows",
    )(place, slot_utt, after, *payloads, *blocks)


def load_kernel(rows, after_ref, head_ref, out_ref, token_ref, semaphores):
    count = head_ref.shape[0] // rows
    copies = start_copies(
        lambda i: head_ref.at[pl.ds(i * rows, rows), :],
        lambda i: out_ref.at[pl.ds(i * rows, rows), :],
        semaphores,
        count,
    )
    token_ref[...] = jnp.zeros_like(token_ref)
    for copy in copies:
        copy.wait()


def load_head(after, head):
    rows = head.shape[0] // 5
    return pl.pallas_call(
        functools.partial(load_kernel, rows),
        in_specs=[ANYWHERE, ANYWHERE],
        out_specs=[INSIDE, INSIDE],
        out_shape=[
            pltpu.VMEM(head.shape, head.dtype),
            jax.ShapeDtypeStruct((8, LANES), jnp.float32),
        ],
        scratch_shapes=[pltpu.SemaphoreType.DMA((5,))],
        cost_estimate=pl.CostEstimate(
            flops=0, bytes_accessed=2 * head.size, transcendentals=0
        ),
        compiler_params=pltpu.CompilerParams(vmem_limit_bytes=20 << 20),
        name="vocabulary_rows",
    )(after, in_hbm(head))


def vocabulary_kernel(tile, first_ref, *refs):
    sets, (head_ref, out_ref, rows_ref, stat) = refs[:-4], refs[-4:]
    vocab_rows, width = head_ref.shape
    share = sets[0].shape[0]
    tokens = share * len(sets)
    cell = lax.broadcasted_iota(jnp.int32, (8, LANES), 1)
    take = jnp.where(cell == 0, 256.0, jnp.where(cell == 1, 1.0, 0.0)).astype(jnp.bfloat16)
    for number, rows in enumerate(sets):
        rows_ref[number * share : (number + 1) * share, :] = rows[...]
    target = dot_nt(take, rows_ref[:, width:])[0:1, :].astype(jnp.int32) - first_ref[3]
    stat[0:1, :] = jnp.full((1, tokens), -jnp.inf, jnp.float32)
    stat[8:9, :] = jnp.zeros((1, tokens), jnp.float32)
    stat[16:17, :] = jnp.zeros((1, tokens), jnp.float32)

    @pl.loop(0, vocab_rows // tile)
    def _(step):
        start = pl.multiple_of(step * tile, tile)
        logits = dot_nt(head_ref[pl.ds(start, tile), :], rows_ref[:, :width])
        vocab = lax.broadcasted_iota(jnp.int32, logits.shape, 0) + start
        before = stat[0:1, :]
        upper = jnp.maximum(before, jnp.max(logits, axis=0, keepdims=True))
        stat[8:9, :] = stat[8:9, :] * jnp.exp(before - upper) + jnp.sum(
            jnp.exp(logits - upper), axis=0, keepdims=True
        )
        stat[16:17, :] += jnp.sum(jnp.where(vocab == target, logits, 0.0), axis=0, keepdims=True)
        stat[0:1, :] = upper

    for number in range(len(sets)):
        for row in range(3):
            out_ref[number, row : row + 1, :] = stat[
                8 * row : 8 * row + 1, number * share : (number + 1) * share
            ]


def vocabulary_stats(place, sets, head):
    share = sets[0].shape[0]
    count = len(sets)
    width = head.shape[1]
    tokens = share * count
    return pl.pallas_call(
        functools.partial(vocabulary_kernel, head.shape[0] // 2),
        in_specs=[SCALARS] + [INSIDE] * (count + 1),
        out_specs=INSIDE,
        out_shape=jax.ShapeDtypeStruct((count, 8, share), jnp.float32),
        scratch_shapes=[
            pltpu.VMEM((tokens, width + LANES), jnp.bfloat16),
            pltpu.VMEM((24, tokens), jnp.float32),
        ],
        cost_estimate=pl.CostEstimate(
            flops=3 * tokens * head.shape[0] * width,
            bytes_accessed=2 * tokens * width,
            transcendentals=tokens * head.shape[0],
        ),
        compiler_params=pltpu.CompilerParams(vmem_limit_bytes=16 << 20),
        name="vocabulary_scores",
    )(place, *sets, pltpu.with_memory_space_constraint(head, pltpu.VMEM))


def spread_kernel(sections, groups, widths, place_ref, slot_ref, *refs):
    stats, (out_ref, table, block) = refs[:-3], refs[-3:]
    share = table.shape[2]
    first = 0
    for stat in stats:
        table[first : first + stat.shape[0]] = stat[...]
        first += stat.shape[0]
    slots = slot_ref.shape[0] // groups
    block[...] = jnp.zeros_like(block)
    for group in range(groups):
        for slot in range(slots):
            utterance = jnp.maximum(slot_ref[group * slots + slot], 0)
            for section in range(sections):
                at = (section ^ place_ref[0]) * groups + (utterance ^ place_ref[1])
                block[group, 3 * slot : 3 * slot + 3, section * share : (section + 1) * share] = (
                    table[at][0:3, :]
                )
    for section in range(sections):
        for group in range(groups):
            for width in range(widths):
                out_ref[(section * groups + group) * widths + width] = block[group]


def spread_stats(place, slot_utt, stats, sections, groups, widths):
    share = stats[0].shape[2]
    assert 3 * slot_utt.shape[0] // groups <= 8
    return pl.pallas_call(
        functools.partial(spread_kernel, sections, groups, widths),
        in_specs=[SCALARS] * 2 + [INSIDE] * len(stats),
        out_specs=INSIDE,
        out_shape=jax.ShapeDtypeStruct(
            (sections * groups * widths, 8, sections * share), jnp.float32
        ),
        scratch_shapes=[
            pltpu.VMEM((sections * groups, 8, share), jnp.float32),
            pltpu.VMEM((groups, 8, sections * share), jnp.float32),
        ],
        compiler_params=pltpu.CompilerParams(vmem_limit_bytes=16 << 20),
        name="statistics_by_group",
    )(place, slot_utt, *stats)


def score_kernel(sections, widths, place_ref, slot_ref, length_ref, every_ref, out_ref):
    slots, hyps = out_ref.shape
    lanes = every_ref.shape[2]
    share = lanes // sections // widths
    lane = lax.broadcasted_iota(jnp.int32, (1, lanes), 1)
    order = lane % share * (sections * widths) + lane // share
    column = lax.broadcasted_iota(jnp.int32, (1, hyps), 1)
    for slot in range(slots):
        upper = every_ref[:, 3 * slot, :]
        peak = jnp.max(upper, axis=0, keepdims=True)
        total = jnp.sum(
            every_ref[:, 3 * slot + 1, :] * jnp.exp(upper - peak), axis=0, keepdims=True
        )
        picked = jnp.sum(every_ref[:, 3 * slot + 2, :], axis=0, keepdims=True)
        logp = picked - (peak + jnp.log(total))
        scores = jnp.zeros((1, hyps), jnp.float32)
        start = jnp.int32(0)
        for hyp in range(hyps):
            length = length_ref[slot, hyp]
            valid = (order >= start) & (order < start + length)
            summed = jnp.sum(jnp.where(valid, logp, 0.0), axis=1, keepdims=True)
            mean = summed / jnp.full((1, 1), length, jnp.int32).astype(jnp.float32)
            scores = jnp.where(column == hyp, mean + math.log(V), scores)
            start = start + length
        filled = slot_ref[place_ref[1] * slots + slot] >= 0
        out_ref[slot : slot + 1, :] = jnp.where(filled, scores, 0.0)


def hypothesis_scores(place, slot_utt, lengths, every, slots, hyps, sections, widths):
    return pl.pallas_call(
        functools.partial(score_kernel, sections, widths),
        in_specs=[SCALARS] * 3 + [INSIDE],
        out_specs=INSIDE,
        out_shape=jax.ShapeDtypeStruct((slots, hyps), jnp.float32),
        compiler_params=pltpu.CompilerParams(vmem_limit_bytes=16 << 20),
        name="hypothesis_scores",
    )(place, slot_utt, lengths, every)


def near_device(
    frame_len,
    slot_utt,
    enc_in,
    ffn_up,
    ffn_down,
    kv_proj,
    hyp_state,
    hyp_tok,
    hyp_len,
    q_proj,
    o_proj,
    head,
):
    section_count = lax.axis_size("section")
    group_count = lax.axis_size("tm")
    width_count = lax.axis_size("mp")
    section_pos = lax.axis_index("section")
    group_pos = lax.axis_index("tm")
    width_pos = lax.axis_index("mp")
    head_devices = section_count * width_count
    all_devices = head_devices * group_count

    frame_rows, utterances, enc_width = enc_in.shape
    slot_count, hyp_count, positions, model_width = hyp_state.shape
    slot_tokens = hyp_count * positions
    share_rows = slot_tokens // head_devices
    vocab_start = (
        (section_pos * group_count + group_pos) * width_count + width_pos
    ) * head.shape[0]
    head_pos = section_pos * width_count + width_pos
    place = jnp.stack([section_pos, group_pos, width_pos, vocab_start, head_pos])
    place = place.astype(jnp.int32)

    parts, own_frames, *blocks = front(
        place,
        slot_utt,
        hyp_len,
        enc_in,
        ffn_up,
        ffn_down,
        hyp_state.reshape(slot_count, slot_tokens, model_width),
        hyp_tok.reshape(slot_count, 1, slot_tokens),
        q_proj,
        width_count,
        group_count,
        share_rows,
    )
    parts = exchange(parts, "mp")
    crossing = blocks[2] + swap(blocks[3], "tm", 1)
    payloads = [blocks[0], swap(blocks[1], "tm", 1), swap(crossing, "tm", 2)]

    sent = keys_values_of(parts, own_frames, kv_proj, section_count, utterances, width_count)
    frames_all = all_devices * (frame_rows // width_count)
    keys_values = exchange(sent.reshape(all_devices, -1, 2 * HD), ALL).reshape(frames_all, 2 * HD)

    pieces = (share_rows // 2, share_rows - share_rows // 2)
    projected = attend(
        place,
        slot_utt,
        frame_len,
        payloads,
        keys_values,
        o_proj,
        pieces,
        section_count,
        width_count,
        slot_count,
    )
    head, token = load_head(projected[1], head)

    def halve(total, came, axis, distance, side):
        if came is not None:
            total = total + came.astype(jnp.float32)
        half = total.shape[0] // 2
        kept = lax.dynamic_slice_in_dim(total, side * half, half, 0)
        sent = lax.dynamic_slice_in_dim(total, (1 - side) * half, half, 0)
        return kept, swap(sent.astype(jnp.bfloat16), axis, distance)

    low, high = width_pos % 2, width_pos // 2
    first = projected[1].astype(jnp.float32), swap(projected[0], "section", 1)
    second = projected[3].astype(jnp.float32), swap(projected[2], "mp", 1)
    first = halve(*first, "mp", 1, low)
    second = halve(*second, "mp", 2, high)
    first = halve(*first, "mp", 2, high)
    second = halve(*second, "section", 1, section_pos)
    sums = [*first, *second]
    out_rows = normed_rows(
        place, slot_utt, token, payloads, sums, pieces, slot_tokens, slot_count
    )

    share = out_rows.shape[0]
    own = jnp.zeros((width_count * share, out_rows.shape[1]), jnp.bfloat16)
    for distance in range(width_count):
        block = swap(out_rows, "mp", distance) if distance else out_rows
        own = lax.dynamic_update_slice_in_dim(own, block, (width_pos ^ distance) * share, 0)
    half = own.shape[0] // 2
    by_x = swap(own, "section", 1)
    by_y = swap(own, "tm", 2)
    stats = [vocabulary_stats(place, [own, swap(own, "tm", 1)], head)]
    by_x, by_y, stats[0] = lax.optimization_barrier((by_x, by_y, stats[0]))
    across = [swap(by_x[:half], "tm", 2), swap(by_y[half:], "section", 1)]
    stats.append(
        vocabulary_stats(place, [by_y, swap(by_y, "tm", 1), by_x, swap(by_x, "tm", 1)], head)
    )
    *across, stats[1] = lax.optimization_barrier((*across, stats[1]))
    across = jnp.concatenate(across)
    stats.append(vocabulary_stats(place, [across, swap(across, "tm", 1)], head))

    every = exchange(
        spread_stats(place, slot_utt, stats, section_count, group_count, width_count), ALL
    )
    return hypothesis_scores(
        place, slot_utt, hyp_len, every, slot_count, hyp_count, section_count, width_count
    )


def general(
    frame_len,
    slot_utt,
    enc_in,
    ffn_up,
    ffn_down,
    kv_proj,
    hyp_state,
    hyp_tok,
    hyp_len,
    q_proj,
    o_proj,
    head,
):
    section_count = lax.axis_size("section")
    group_count = lax.axis_size("tm")
    width_count = lax.axis_size("mp")
    section_pos = lax.axis_index("section")
    group_pos = lax.axis_index("tm")
    width_pos = lax.axis_index("mp")
    head_devices = section_count * width_count
    head_pos = section_pos * width_count + width_pos
    all_devices = head_devices * group_count

    frame_rows, utterances, enc_width = enc_in.shape
    assert utterances == group_count
    slot_count, hyp_count, positions, model_width = hyp_state.shape
    slot_tokens = hyp_count * positions
    device_heads = q_proj.shape[1] // HD
    group_heads = NH // KVH
    frame_share = frame_rows // width_count
    share_rows = slot_tokens // head_devices
    here_slots = lax.dynamic_slice_in_dim(slot_utt, group_pos * slot_count, slot_count, 0)

    dec_rows = hyp_state.reshape(slot_count * slot_tokens, model_width).astype(jnp.float32)
    queries = jnp.dot(
        square_norm(dec_rows).astype(jnp.bfloat16), q_proj, preferred_element_type=jnp.float32
    ).astype(jnp.bfloat16)
    queries = queries.reshape(slot_count, slot_tokens, device_heads * HD)
    shares = lax.dynamic_slice_in_dim(
        hyp_state.reshape(slot_count, slot_tokens, model_width), head_pos * share_rows, share_rows, 1
    )

    def by_utterance(values):
        out = []
        for utterance in range(utterances):
            block = values[0]
            for slot in range(1, slot_count):
                block = jnp.where(here_slots[slot] == utterance, values[slot], block)
            out.append(block)
        return jnp.stack(out)

    own_slot = jnp.argmax(slot_utt == group_pos)
    from_group = own_slot // slot_count
    queries = lax.dynamic_index_in_dim(
        exchange(by_utterance(queries), "tm"), from_group, 0, keepdims=False
    )
    resid_rows = lax.dynamic_index_in_dim(
        exchange(by_utterance(shares), "tm"), from_group, 0, keepdims=False
    )
    slot_targets = lax.all_gather(
        hyp_tok.reshape(slot_count, slot_tokens), "tm", axis=0, tiled=True
    )
    utt_slots = jnp.argmax(slot_utt[None, :] == jnp.arange(utterances)[:, None], axis=1)
    targets = jnp.take(slot_targets, utt_slots, axis=0).reshape(utterances * slot_tokens)

    enc_flat = (
        enc_in.reshape(width_count, frame_share, utterances, enc_width)
        .transpose(0, 2, 1, 3)
        .reshape(frame_rows * utterances, enc_width)
    )
    share_count = frame_share * utterances
    enc_normed = layer_norm(enc_flat.astype(jnp.float32)).astype(jnp.bfloat16)
    enc_inner = jax.nn.gelu(
        jnp.dot(enc_normed, ffn_up, preferred_element_type=jnp.float32), approximate=False
    ).astype(jnp.bfloat16)
    enc_summed = scatter_sum(
        jnp.dot(enc_inner, ffn_down, preferred_element_type=jnp.float32).astype(jnp.bfloat16),
        "mp",
        width_count,
    )
    own_frames = lax.dynamic_slice_in_dim(enc_flat, width_pos * share_count, share_count, 0)
    enc_states = layer_norm(own_frames.astype(jnp.float32) + enc_summed).astype(jnp.bfloat16)
    keys_values = jnp.dot(enc_states, kv_proj, preferred_element_type=jnp.float32).astype(
        jnp.bfloat16
    )
    keys_values = keys_values.reshape(utterances, frame_share, 2, KVH, HD)
    sent = []
    for section in range(section_count):
        per_width = []
        for width in range(width_count):
            kv_head = (section * width_count + width) * device_heads // group_heads
            per_width.append(
                keys_values[:, :, :, kv_head].reshape(utterances, frame_share, 2 * HD)
            )
        sent.append(jnp.stack(per_width, axis=1))
    sent = jnp.stack(sent).reshape(all_devices, frame_share, 2 * HD)
    frames_all = all_devices * frame_share
    keys_values = exchange(sent, ALL).reshape(frames_all, 2 * HD)

    frame_limit = lax.dynamic_index_in_dim(frame_len, group_pos, 0, keepdims=False)
    queries = queries.reshape(slot_tokens, device_heads, HD)
    scores = jnp.einsum(
        "qhd,fd->hqf", queries, keys_values[:, :HD], preferred_element_type=jnp.float32
    ) / math.sqrt(HD)
    visible = jnp.arange(frames_all, dtype=jnp.int32) < frame_limit
    scores = jnp.where(visible[None, None, :], scores, -jnp.inf)
    weights = jax.nn.softmax(scores, axis=-1).astype(jnp.bfloat16)
    context = jnp.einsum(
        "hqf,fd->qhd", weights, keys_values[:, HD:], preferred_element_type=jnp.float32
    ).astype(jnp.bfloat16)
    partial = jnp.dot(
        context.reshape(slot_tokens, device_heads * HD), o_proj, preferred_element_type=jnp.float32
    ).astype(jnp.bfloat16)
    partial = scatter_sum(partial, "section", section_count).astype(jnp.bfloat16)
    attn_out = scatter_sum(partial, "mp", width_count)
    out_normed = square_norm(resid_rows.astype(jnp.float32) + attn_out).astype(jnp.bfloat16)

    hidden_rows = lax.all_gather(out_normed, ALL, axis=0, tiled=True)
    logits = lax.dot_general(
        hidden_rows, head, (((1,), (1,)), ((), ())), preferred_element_type=jnp.float32
    )
    vocab_rows = head.shape[0]
    vocab_start = (
        (section_pos * group_count + group_pos) * width_count + width_pos
    ) * vocab_rows
    target_rows = (
        targets.reshape(utterances, section_count, width_count, share_rows)
        .transpose(1, 0, 2, 3)
        .reshape(-1)
    )
    upper = jnp.max(logits, axis=1)
    totals = jnp.sum(jnp.exp(logits - upper[:, None]), axis=1)
    matches = (
        jnp.arange(vocab_rows, dtype=jnp.int32)[None, :] == (target_rows - vocab_start)[:, None]
    )
    target_logit = jnp.sum(jnp.where(matches, logits, 0.0), axis=1)

    stats = jnp.stack([upper, totals, target_logit])
    stats = stats.reshape(3, section_count, utterances, width_count, share_rows)
    stats = stats.transpose(2, 0, 1, 3, 4).reshape(utterances, 3, slot_tokens)
    by_slot = jnp.take(stats, jnp.maximum(slot_utt, 0), axis=0)
    by_group = by_slot.reshape(1, group_count, 1, slot_count, 3, slot_tokens)
    by_group = jnp.broadcast_to(
        by_group, (section_count, group_count, width_count, slot_count, 3, slot_tokens)
    ).reshape(all_devices, slot_count, 3, slot_tokens)
    every = exchange(by_group, ALL)
    peak = jnp.max(every[:, :, 0], axis=0)
    total = jnp.sum(every[:, :, 1] * jnp.exp(every[:, :, 0] - peak[None]), axis=0)
    picked = jnp.sum(every[:, :, 2], axis=0)
    token_logp = (picked - (peak + jnp.log(total))).reshape(slot_count, hyp_count, positions)
    valid = jnp.arange(positions, dtype=jnp.int32)[None, None, :] < hyp_len[:, :, None]
    summed = jnp.sum(jnp.where(valid, token_logp, 0.0), axis=-1) / hyp_len.astype(
        jnp.float32
    ) + math.log(V)
    return jnp.where(here_slots[:, None] >= 0, summed, 0.0)


def solution(mesh):
    in_specs = (
        P(),
        P(),
        P(("section", "tm"), None, None),
        P(None, "mp"),
        P("mp", None),
        P(),
        P("tm", None, None, None),
        P("tm", None, None),
        P("tm", None),
        P(None, ("section", "mp")),
        P(("section", "mp"), None),
        P(("section", "tm", "mp"), None),
    )
    out_specs = P("tm", None)
    near = dict(mesh.shape) == {"section": 2, "tm": 4, "mp": 4}
    per_device = near_device if near else general
    return jax.shard_map(
        per_device, mesh=mesh, in_specs=in_specs, out_specs=out_specs, check_vma=False
    )
```

```python
import functools
import math

import jax
import jax.numpy as jnp
from jax import lax
from jax.experimental import pallas as pl
from jax.experimental.pallas import tpu as pltpu
from jax.sharding import PartitionSpec as P

NH = 32
KVH = 4
HD = 128
V = 64000
ALL = ("section", "tm", "mp")
LANES = 128


def layer_norm(values):
    center = values - jnp.mean(values, axis=-1, keepdims=True)
    spread = jnp.mean(center * center, axis=-1, keepdims=True)
    return center * lax.rsqrt(spread + 1e-05)


def square_norm(values):
    return values * lax.rsqrt(jnp.mean(values * values, axis=-1, keepdims=True) + 1e-06)


def exchange(blocks, axis):
    return lax.all_to_all(blocks, axis, split_axis=0, concat_axis=0, tiled=True)


def scatter_sum(partial, axis, count):
    blocks = partial.reshape((count, partial.shape[0] // count) + partial.shape[1:])
    return jnp.sum(exchange(blocks, axis).astype(jnp.float32), axis=0)


def swap(values, axis, distance):
    pairs = [(i, i ^ distance) for i in range(lax.axis_size(axis))]
    return lax.ppermute(values, axis, pairs)


def whole(shape):
    return pl.BlockSpec(shape, lambda *_: (0,) * len(shape))


SCALARS = pl.BlockSpec(memory_space=pltpu.SMEM)


def dot(left, right):
    return jnp.dot(left, right, preferred_element_type=jnp.float32)


def dot_nt(left, right):
    return lax.dot_general(
        left, right, (((1,), (1,)), ((), ())), preferred_element_type=jnp.float32
    )


def start_copies(source_of, target_of, semaphores, count):
    copies = []
    for number in range(count):
        copy = pltpu.make_async_copy(
            source_of(number), target_of(number), semaphores.at[number]
        )
        copy.start()
        copies.append(copy)
    return copies


def ffn_kernel(tile, place_ref, after_ref, x_ref, up_ref, down_ref, *refs):
    out_ref, own_ref, rows, total = refs
    count, share, width = out_ref.shape
    tiles = up_ref.shape[1] // tile
    rows[...] = x_ref[...].astype(jnp.float32).reshape(rows.shape)
    start = pl.multiple_of(place_ref[2] * share, share)
    own_ref[...] = rows[pl.ds(start, share), :].astype(jnp.bfloat16)
    normed = layer_norm(rows[...]).astype(jnp.bfloat16)
    for number in range(tiles):
        hidden = dot(normed, up_ref[:, number * tile : (number + 1) * tile])
        inner = 0.5 * hidden * (1.0 + lax.erf(hidden * math.sqrt(0.5)))
        product = dot(inner.astype(jnp.bfloat16), down_ref[number * tile : (number + 1) * tile, :])
        if number == 0:
            total[...] = product
        else:
            total[...] += product
    for part in range(count):
        out_ref[part] = total[part * share : (part + 1) * share, :].astype(jnp.bfloat16)


def in_hbm(values):
    return pltpu.with_memory_space_constraint(values, pltpu.HBM)


ANYWHERE = pl.BlockSpec(memory_space=pl.ANY)
INSIDE = pl.BlockSpec(memory_space=pltpu.VMEM)


def ffn(place, after, enc_in, up, down, count):
    frames, utterances, width = enc_in.shape
    rows = frames * utterances
    share = rows // count
    tile = 256
    return pl.pallas_call(
        functools.partial(ffn_kernel, tile),
        in_specs=[SCALARS, ANYWHERE, INSIDE, INSIDE, INSIDE],
        out_specs=[INSIDE] * 2,
        out_shape=[
            jax.ShapeDtypeStruct((count, share, width), jnp.bfloat16),
            jax.ShapeDtypeStruct((share, width), jnp.bfloat16),
        ],
        scratch_shapes=[
            pltpu.VMEM((rows, width), jnp.float32),
            pltpu.VMEM((rows, width), jnp.float32),
        ],
        cost_estimate=pl.CostEstimate(
            flops=4 * rows * width * up.shape[1],
            bytes_accessed=4 * width * up.shape[1],
            transcendentals=rows * up.shape[1],
        ),
        compiler_params=pltpu.CompilerParams(vmem_limit_bytes=24 << 20),
        name="encoder_ffn",
    )(place, after, enc_in, up, down)


def query_kernel(count, depth, place_ref, slot_ref, length_ref, x_ref, tok_ref, w_ref, *refs):
    outs, (states, weights, total, ordered, shares, x_sem, w_sem) = refs[:count], refs[count:]
    slots, tokens, width = x_ref.shape
    hyps, positions = tok_ref.shape[1:]
    columns = w_ref.shape[1]
    share = shares.shape[1] // 2
    parts = width // columns
    steps = width // depth
    x_copies = start_copies(lambda i: x_ref.at[i], lambda i: states.at[i], x_sem, slots)
    w_copies = start_copies(
        lambda i: w_ref.at[pl.ds(i * depth, depth), :], lambda i: weights.at[i], w_sem, steps
    )
    scales = []
    for slot in range(slots):
        x_copies[slot].wait()
        squares = jnp.zeros((tokens, depth), jnp.float32)
        for number in range(steps):
            part = states[slot, :, number * depth : (number + 1) * depth].astype(jnp.float32)
            squares += part * part
        mean = jnp.sum(squares, axis=1, keepdims=True) * (1.0 / width)
        scales.append(lax.rsqrt(mean + 1e-06))
    for number in range(steps):
        w_copies[number].wait()
        for slot in range(slots):
            part = states[slot, :, number * depth : (number + 1) * depth].astype(jnp.float32)
            product = dot((part * scales[slot]).astype(jnp.bfloat16), weights[number])
            if number == 0:
                total[slot] = product
            else:
                total[slot] += product
    head_pos = place_ref[4]
    lane = lax.broadcasted_iota(jnp.int32, (1, tokens), 1)
    position = lax.broadcasted_iota(jnp.int32, (1, positions), 1)
    share_place = (
        lax.broadcasted_iota(jnp.int32, (share, 1), 0) * (tokens // share) + head_pos
    )
    for slot in range(slots):
        order = jnp.full((1, tokens), -1, jnp.int32)
        target = jnp.zeros((share, positions), jnp.int32)
        start = jnp.int32(0)
        for hyp in range(hyps):
            length = length_ref[slot, hyp]
            inside = (lane >= hyp * positions) & (lane < hyp * positions + length)
            order = jnp.where(inside, lane - hyp * positions + start, order)
            here = jnp.where(position < length, position + start, -1)
            target = jnp.where(here == share_place, tok_ref[slot, hyp : hyp + 1, :], target)
            start = start + length
        row = lax.broadcasted_iota(jnp.int32, (tokens, tokens), 0)
        move = jnp.where(order == row, 1.0, 0.0).astype(jnp.bfloat16)
        ordered[slot] = dot(move, total[slot].astype(jnp.bfloat16)).astype(jnp.bfloat16)
        mine = jnp.where(order == share_place, 1.0, 0.0).astype(jnp.bfloat16)
        shares[slot, :share, :] = dot(mine, states[slot]).astype(jnp.bfloat16)
        target = jnp.sum(target, axis=1, keepdims=True, dtype=jnp.int32)
        coarse = target // 256
        cell = lax.broadcasted_iota(jnp.int32, (share, columns), 1)
        packed = jnp.where(cell == 0, coarse, jnp.where(cell == 1, target - coarse * 256, 0))
        shares[slot, share:, :columns] = packed.astype(jnp.float32).astype(jnp.bfloat16)
    group = place_ref[1]
    for distance in range(count):
        slot = jnp.int32(-1)
        for candidate in range(slots):
            holds = slot_ref[group * slots + candidate] == group ^ distance
            slot = jnp.where(holds, candidate, slot)
        out = outs[distance]

        @pl.when(slot < 0)
        def _(out=out):
            out[...] = jnp.zeros_like(out)

        @pl.when(slot >= 0)
        def _(out=out, slot=slot):
            out[:tokens, :] = ordered[slot]
            for part in range(parts):
                first = tokens + part * share
                out[first : first + share, :] = shares[
                    slot, :share, part * columns : (part + 1) * columns
                ]
            out[tokens + parts * share :, :] = shares[slot, share:, :columns]


def queries_of(place, slot_utt, lengths, states, targets, weights, count, share):
    slots, tokens, width = states.shape
    columns = weights.shape[1]
    depth = 1024
    rows = tokens + (width // columns + 1) * share
    block = jax.ShapeDtypeStruct((rows, columns), jnp.bfloat16)
    return pl.pallas_call(
        functools.partial(query_kernel, count, depth),
        in_specs=[SCALARS] * 3 + [ANYWHERE, INSIDE, ANYWHERE],
        out_specs=[INSIDE] * count,
        out_shape=[block] * count,
        scratch_shapes=[
            pltpu.VMEM(states.shape, jnp.bfloat16),
            pltpu.VMEM((width // depth, depth, columns), jnp.bfloat16),
            pltpu.VMEM((slots, tokens, columns), jnp.float32),
            pltpu.VMEM((slots, tokens, columns), jnp.bfloat16),
            pltpu.VMEM((slots, 2 * share, width), jnp.bfloat16),
            pltpu.SemaphoreType.DMA((slots,)),
            pltpu.SemaphoreType.DMA((width // depth,)),
        ],
        cost_estimate=pl.CostEstimate(
            flops=2 * slots * tokens * width * columns,
            bytes_accessed=2 * width * (columns + slots * tokens),
            transcendentals=0,
        ),
        compiler_params=pltpu.CompilerParams(vmem_limit_bytes=20 << 20),
        name="hypothesis_queries",
    )(place, slot_utt, lengths, in_hbm(states), targets, in_hbm(weights))


def kv_kernel(sections, utterances, widths, *refs):
    parts_ref, own_ref, w_ref, out_ref = refs
    rows = own_ref.shape[0]
    frames = rows // utterances
    total = own_ref[...].astype(jnp.float32)
    summed = parts_ref[0].astype(jnp.float32)
    for part in range(1, parts_ref.shape[0]):
        summed += parts_ref[part].astype(jnp.float32)
    states = layer_norm(total + summed).astype(jnp.bfloat16)
    to = lax.broadcasted_iota(jnp.int32, (rows, rows), 0)
    come = lax.broadcasted_iota(jnp.int32, (rows, rows), 1)
    move = jnp.where(come == to % frames * utterances + to // frames, 1.0, 0.0)
    states = dot(move.astype(jnp.bfloat16), states).astype(jnp.bfloat16)
    both = dot(states, w_ref[...])
    half = KVH * HD
    per_kv = sections * widths // KVH
    for section in range(sections):
        for utterance in range(utterances):
            for width in range(0, widths, per_kv):
                kv_head = (section * widths + width) // per_kv
                take = slice(utterance * frames, (utterance + 1) * frames)
                block = jnp.concatenate(
                    [
                        both[take, kv_head * HD : (kv_head + 1) * HD],
                        both[take, half + kv_head * HD : half + (kv_head + 1) * HD],
                    ],
                    axis=1,
                )
                start = ((section * utterances + utterance) * widths + width) * frames
                block = jnp.concatenate([block] * per_kv, axis=0).astype(jnp.bfloat16)
                out_ref[start : start + per_kv * frames, :] = block


def keys_values_of(parts, own, weights, sections, utterances, widths):
    rows = sections * widths * own.shape[0]
    return pl.pallas_call(
        functools.partial(kv_kernel, sections, utterances, widths),
        in_specs=[INSIDE] * 3,
        out_specs=INSIDE,
        out_shape=jax.ShapeDtypeStruct((rows, 2 * HD), jnp.bfloat16),
        cost_estimate=pl.CostEstimate(
            flops=2 * own.shape[0] * weights.shape[0] * weights.shape[1],
            bytes_accessed=2 * weights.shape[0] * weights.shape[1],
            transcendentals=0,
        ),
        compiler_params=pltpu.CompilerParams(vmem_limit_bytes=24 << 20),
        name="frame_keys_values",
    )(parts, own, weights)


def choice_of_payload(place_ref, slot_ref, slots):
    group = place_ref[1]
    source = jnp.int32(0)
    for slot in range(slot_ref.shape[0]):
        source = jnp.where(slot_ref[slot] == group, slot // slots, source)
    return jnp.minimum(source ^ group, 2)


def attention_kernel(count, slots, capacity, pieces, sections, widths, tile, *refs):
    place_ref, slot_ref, frame_ref = refs[:3]
    payloads, (kv_ref, w_ref) = refs[3 : 3 + count], refs[3 + count : 5 + count]
    outs = refs[5 + count : 5 + count + 2 * len(pieces)]
    weights, picked, context, w_sem = refs[5 + count + 2 * len(pieces) :]
    tokens, columns = capacity, w_ref.shape[0]
    tiles = w_ref.shape[1] // tile
    w_copies = start_copies(
        lambda i: w_ref.at[:, pl.ds(i * tile, tile)], lambda i: weights.at[i], w_sem, tiles
    )
    source = choice_of_payload(place_ref, slot_ref, slots)
    section_pos = place_ref[0]
    frame_limit = frame_ref[place_ref[1]]
    for distance in range(count):

        @pl.when(source == distance)
        def _(payload=payloads[distance]):
            picked[...] = payload[:tokens, :]

    keys = kv_ref[:, :HD]
    values = kv_ref[:, HD:]
    frames = kv_ref.shape[0]
    visible = lax.broadcasted_iota(jnp.int32, (tokens, frames), 1) < frame_limit
    for head in range(columns // HD):
        scores = dot_nt(picked[:, head * HD : (head + 1) * HD], keys) * (1.0 / math.sqrt(HD))
        scores = jnp.where(visible, scores, -jnp.inf)
        raised = jnp.exp(scores - jnp.max(scores, axis=1, keepdims=True))
        chances = (raised / jnp.sum(raised, axis=1, keepdims=True)).astype(jnp.bfloat16)
        context[:, head * HD : (head + 1) * HD] = dot(chances, values).astype(jnp.bfloat16)
    to = lax.broadcasted_iota(jnp.int32, (tokens, tokens), 0)
    come = lax.broadcasted_iota(jnp.int32, (tokens, tokens), 1)
    low_bit = place_ref[2] % 2
    size = widths * pieces[0]
    block = to % size // pieces[0]
    section = jnp.where(to < size, 1 - section_pos, section_pos)
    first_order = (to % pieces[0] * sections + section) * widths + block % 2 * 2 + block // 2
    at = to - 2 * size
    size = widths * pieces[1]
    block = at % size // pieces[1]
    low = jnp.where(at < size, 1 - low_bit, low_bit)
    row = pieces[0] + at % pieces[1]
    second_order = (row * sections + block % 2) * widths + block // 2 * 2 + low
    move = come == jnp.where(at < 0, first_order, second_order)
    ordered = dot(jnp.where(move, 1.0, 0.0).astype(jnp.bfloat16), context[...])
    ordered = ordered.astype(jnp.bfloat16)
    for number in range(tiles):
        w_copies[number].wait()
        product = dot(ordered, weights[number]).astype(jnp.bfloat16)
        first = 0
        for out in outs:
            out[:, number * tile : (number + 1) * tile] = product[first : first + out.shape[0], :]
            first += out.shape[0]


def attend(place, slot_utt, frame_len, payloads, keys_values, weights, pieces, sections, widths, slots):
    count = len(payloads)
    columns, width = weights.shape
    capacity = sum(pieces) * sections * widths
    tile = 1024
    tiles = width // tile
    shapes = [
        jax.ShapeDtypeStruct((piece * widths, width), jnp.bfloat16)
        for piece in pieces
        for _ in range(2)
    ]
    return pl.pallas_call(
        functools.partial(
            attention_kernel, count, slots, capacity, pieces, sections, widths, tile
        ),
        in_specs=[SCALARS] * 3 + [INSIDE] * (count + 1) + [ANYWHERE],
        out_specs=[INSIDE] * len(shapes),
        out_shape=shapes,
        scratch_shapes=[
            pltpu.VMEM((tiles, columns, tile), jnp.bfloat16),
            pltpu.VMEM((capacity, columns), jnp.bfloat16),
            pltpu.VMEM((capacity, columns), jnp.bfloat16),
            pltpu.SemaphoreType.DMA((tiles,)),
        ],
        cost_estimate=pl.CostEstimate(
            flops=2 * capacity * columns * (width + 2 * keys_values.shape[0]),
            bytes_accessed=2 * columns * width + 2 * capacity * width,
            transcendentals=capacity * keys_values.shape[0] * columns // HD,
        ),
        compiler_params=pltpu.CompilerParams(vmem_limit_bytes=24 << 20),
        name="attention_projection",
    )(place, slot_utt, frame_len, *payloads, keys_values, in_hbm(weights))


def norm_kernel(count, slots, tokens, pieces, place_ref, slot_ref, after_ref, *refs):
    payloads, blocks = refs[:count], refs[count : count + 2 * len(pieces)]
    out_ref, picked, total = refs[count + 2 * len(pieces) :]
    rows, width = total.shape
    columns = picked.shape[1]
    share = picked.shape[0] // (width // columns + 1)
    source = choice_of_payload(place_ref, slot_ref, slots)
    for choice in range(count):

        @pl.when(source == choice)
        def _(payload=payloads[choice]):
            picked[...] = payload[tokens:, :]

    first = 0
    for number, piece in enumerate(pieces):
        kept, other = blocks[2 * number : 2 * number + 2]
        total[first : first + piece, :] = kept[...] + other[...].astype(jnp.float32)
        first += piece
    for part in range(width // columns):
        take = slice(part * columns, (part + 1) * columns)
        total[:, take] += picked[part * share : part * share + rows, :].astype(jnp.float32)
    out_ref[:, :width] = square_norm(total[...]).astype(jnp.bfloat16)
    last = width // columns * share
    out_ref[:, width:] = picked[last : last + rows, :LANES]


def normed_rows(place, slot_utt, after, payloads, blocks, pieces, tokens, slots):
    width = blocks[0].shape[1]
    rows = sum(pieces)
    columns = payloads[0].shape[1]
    return pl.pallas_call(
        functools.partial(norm_kernel, len(payloads), slots, tokens, pieces),
        in_specs=[SCALARS] * 2 + [ANYWHERE] + [INSIDE] * (len(payloads) + len(blocks)),
        out_specs=INSIDE,
        out_shape=jax.ShapeDtypeStruct((rows, width + LANES), jnp.bfloat16),
        scratch_shapes=[
            pltpu.VMEM((payloads[0].shape[0] - tokens, columns), jnp.bfloat16),
            pltpu.VMEM((rows, width), jnp.float32),
        ],
        compiler_params=pltpu.CompilerParams(vmem_limit_bytes=16 << 20),
        name="token_rows",
    )(place, slot_utt, after, *payloads, *blocks)


def load_kernel(rows, after_ref, head_ref, out_ref, token_ref, semaphores):
    count = head_ref.shape[0] // rows
    copies = start_copies(
        lambda i: head_ref.at[pl.ds(i * rows, rows), :],
        lambda i: out_ref.at[pl.ds(i * rows, rows), :],
        semaphores,
        count,
    )
    token_ref[...] = jnp.zeros_like(token_ref)
    for copy in copies:
        copy.wait()


def load_head(after, head):
    rows = head.shape[0] // 5
    return pl.pallas_call(
        functools.partial(load_kernel, rows),
        in_specs=[ANYWHERE, ANYWHERE],
        out_specs=[INSIDE, INSIDE],
        out_shape=[
            pltpu.VMEM(head.shape, head.dtype),
            jax.ShapeDtypeStruct((8, LANES), jnp.float32),
        ],
        scratch_shapes=[pltpu.SemaphoreType.DMA((5,))],
        cost_estimate=pl.CostEstimate(
            flops=0, bytes_accessed=2 * head.size, transcendentals=0
        ),
        compiler_params=pltpu.CompilerParams(vmem_limit_bytes=20 << 20),
        name="vocabulary_rows",
    )(after, in_hbm(head))


def vocabulary_kernel(tile, first_ref, *refs):
    sets, (head_ref, out_ref, rows_ref, stat) = refs[:-4], refs[-4:]
    vocab_rows, width = head_ref.shape
    share = sets[0].shape[0]
    tokens = share * len(sets)
    cell = lax.broadcasted_iota(jnp.int32, (8, LANES), 1)
    take = jnp.where(cell == 0, 256.0, jnp.where(cell == 1, 1.0, 0.0)).astype(jnp.bfloat16)
    for number, rows in enumerate(sets):
        rows_ref[number * share : (number + 1) * share, :] = rows[...]
    target = dot_nt(take, rows_ref[:, width:])[0:1, :].astype(jnp.int32) - first_ref[3]
    stat[0:1, :] = jnp.full((1, tokens), -jnp.inf, jnp.float32)
    stat[8:9, :] = jnp.zeros((1, tokens), jnp.float32)
    stat[16:17, :] = jnp.zeros((1, tokens), jnp.float32)

    @pl.loop(0, vocab_rows // tile)
    def _(step):
        start = pl.multiple_of(step * tile, tile)
        logits = dot_nt(head_ref[pl.ds(start, tile), :], rows_ref[:, :width])
        vocab = lax.broadcasted_iota(jnp.int32, logits.shape, 0) + start
        before = stat[0:1, :]
        upper = jnp.maximum(before, jnp.max(logits, axis=0, keepdims=True))
        stat[8:9, :] = stat[8:9, :] * jnp.exp(before - upper) + jnp.sum(
            jnp.exp(logits - upper), axis=0, keepdims=True
        )
        stat[16:17, :] += jnp.sum(jnp.where(vocab == target, logits, 0.0), axis=0, keepdims=True)
        stat[0:1, :] = upper

    for number in range(len(sets)):
        for row in range(3):
            out_ref[number, row : row + 1, :] = stat[
                8 * row : 8 * row + 1, number * share : (number + 1) * share
            ]


def vocabulary_stats(place, sets, head):
    share = sets[0].shape[0]
    count = len(sets)
    width = head.shape[1]
    tokens = share * count
    return pl.pallas_call(
        functools.partial(vocabulary_kernel, head.shape[0] // 2),
        in_specs=[SCALARS] + [INSIDE] * (count + 1),
        out_specs=INSIDE,
        out_shape=jax.ShapeDtypeStruct((count, 8, share), jnp.float32),
        scratch_shapes=[
            pltpu.VMEM((tokens, width + LANES), jnp.bfloat16),
            pltpu.VMEM((24, tokens), jnp.float32),
        ],
        cost_estimate=pl.CostEstimate(
            flops=3 * tokens * head.shape[0] * width,
            bytes_accessed=2 * tokens * width,
            transcendentals=tokens * head.shape[0],
        ),
        compiler_params=pltpu.CompilerParams(vmem_limit_bytes=16 << 20),
        name="vocabulary_scores",
    )(place, *sets, pltpu.with_memory_space_constraint(head, pltpu.VMEM))


def spread_kernel(sections, groups, widths, place_ref, slot_ref, *refs):
    stats, (out_ref, table, block) = refs[:-3], refs[-3:]
    share = table.shape[2]
    first = 0
    for stat in stats:
        table[first : first + stat.shape[0]] = stat[...]
        first += stat.shape[0]
    slots = slot_ref.shape[0] // groups
    block[...] = jnp.zeros_like(block)
    for group in range(groups):
        for slot in range(slots):
            utterance = jnp.maximum(slot_ref[group * slots + slot], 0)
            for section in range(sections):
                at = (section ^ place_ref[0]) * groups + (utterance ^ place_ref[1])
                block[group, 3 * slot : 3 * slot + 3, section * share : (section + 1) * share] = (
                    table[at][0:3, :]
                )
    for section in range(sections):
        for group in range(groups):
            for width in range(widths):
                out_ref[(section * groups + group) * widths + width] = block[group]


def spread_stats(place, slot_utt, stats, sections, groups, widths):
    share = stats[0].shape[2]
    assert 3 * slot_utt.shape[0] // groups <= 8
    return pl.pallas_call(
        functools.partial(spread_kernel, sections, groups, widths),
        in_specs=[SCALARS] * 2 + [INSIDE] * len(stats),
        out_specs=INSIDE,
        out_shape=jax.ShapeDtypeStruct(
            (sections * groups * widths, 8, sections * share), jnp.float32
        ),
        scratch_shapes=[
            pltpu.VMEM((sections * groups, 8, share), jnp.float32),
            pltpu.VMEM((groups, 8, sections * share), jnp.float32),
        ],
        compiler_params=pltpu.CompilerParams(vmem_limit_bytes=16 << 20),
        name="statistics_by_group",
    )(place, slot_utt, *stats)


def score_kernel(sections, widths, place_ref, slot_ref, length_ref, every_ref, out_ref):
    slots, hyps = out_ref.shape
    lanes = every_ref.shape[2]
    share = lanes // sections // widths
    lane = lax.broadcasted_iota(jnp.int32, (1, lanes), 1)
    order = lane % share * (sections * widths) + lane // share
    column = lax.broadcasted_iota(jnp.int32, (1, hyps), 1)
    for slot in range(slots):
        upper = every_ref[:, 3 * slot, :]
        peak = jnp.max(upper, axis=0, keepdims=True)
        total = jnp.sum(
            every_ref[:, 3 * slot + 1, :] * jnp.exp(upper - peak), axis=0, keepdims=True
        )
        picked = jnp.sum(every_ref[:, 3 * slot + 2, :], axis=0, keepdims=True)
        logp = picked - (peak + jnp.log(total))
        scores = jnp.zeros((1, hyps), jnp.float32)
        start = jnp.int32(0)
        for hyp in range(hyps):
            length = length_ref[slot, hyp]
            valid = (order >= start) & (order < start + length)
            summed = jnp.sum(jnp.where(valid, logp, 0.0), axis=1, keepdims=True)
            mean = summed / jnp.full((1, 1), length, jnp.int32).astype(jnp.float32)
            scores = jnp.where(column == hyp, mean + math.log(V), scores)
            start = start + length
        filled = slot_ref[place_ref[1] * slots + slot] >= 0
        out_ref[slot : slot + 1, :] = jnp.where(filled, scores, 0.0)


def hypothesis_scores(place, slot_utt, lengths, every, slots, hyps, sections, widths):
    return pl.pallas_call(
        functools.partial(score_kernel, sections, widths),
        in_specs=[SCALARS] * 3 + [INSIDE],
        out_specs=INSIDE,
        out_shape=jax.ShapeDtypeStruct((slots, hyps), jnp.float32),
        compiler_params=pltpu.CompilerParams(vmem_limit_bytes=16 << 20),
        name="hypothesis_scores",
    )(place, slot_utt, lengths, every)


def near_device(
    frame_len,
    slot_utt,
    enc_in,
    ffn_up,
    ffn_down,
    kv_proj,
    hyp_state,
    hyp_tok,
    hyp_len,
    q_proj,
    o_proj,
    head,
):
    section_count = lax.axis_size("section")
    group_count = lax.axis_size("tm")
    width_count = lax.axis_size("mp")
    section_pos = lax.axis_index("section")
    group_pos = lax.axis_index("tm")
    width_pos = lax.axis_index("mp")
    head_devices = section_count * width_count
    all_devices = head_devices * group_count

    frame_rows, utterances, enc_width = enc_in.shape
    slot_count, hyp_count, positions, model_width = hyp_state.shape
    slot_tokens = hyp_count * positions
    share_rows = slot_tokens // head_devices
    vocab_start = (
        (section_pos * group_count + group_pos) * width_count + width_pos
    ) * head.shape[0]
    head_pos = section_pos * width_count + width_pos
    place = jnp.stack([section_pos, group_pos, width_pos, vocab_start, head_pos])
    place = place.astype(jnp.int32)

    blocks = queries_of(
        place,
        slot_utt,
        hyp_len,
        hyp_state.reshape(slot_count, slot_tokens, model_width),
        hyp_tok,
        q_proj,
        group_count,
        share_rows,
    )
    crossing = blocks[2] + swap(blocks[3], "tm", 1)
    payloads = [blocks[0], swap(blocks[1], "tm", 1), swap(crossing, "tm", 2)]

    parts, own_frames = ffn(place, blocks[0], enc_in, ffn_up, ffn_down, width_count)
    parts = exchange(parts, "mp")
    sent = keys_values_of(parts, own_frames, kv_proj, section_count, utterances, width_count)
    frames_all = all_devices * (frame_rows // width_count)
    keys_values = exchange(sent.reshape(all_devices, -1, 2 * HD), ALL).reshape(frames_all, 2 * HD)

    pieces = (share_rows // 2, share_rows - share_rows // 2)
    projected = attend(
        place,
        slot_utt,
        frame_len,
        payloads,
        keys_values,
        o_proj,
        pieces,
        section_count,
        width_count,
        slot_count,
    )
    head, token = load_head(projected[1], head)

    def halve(total, came, axis, distance, side):
        if came is not None:
            total = total + came.astype(jnp.float32)
        half = total.shape[0] // 2
        kept = lax.dynamic_slice_in_dim(total, side * half, half, 0)
        sent = lax.dynamic_slice_in_dim(total, (1 - side) * half, half, 0)
        return kept, swap(sent.astype(jnp.bfloat16), axis, distance)

    low, high = width_pos % 2, width_pos // 2
    first = projected[1].astype(jnp.float32), swap(projected[0], "section", 1)
    second = projected[3].astype(jnp.float32), swap(projected[2], "mp", 1)
    first = halve(*first, "mp", 1, low)
    second = halve(*second, "mp", 2, high)
    first = halve(*first, "mp", 2, high)
    second = halve(*second, "section", 1, section_pos)
    sums = [*first, *second]
    out_rows = normed_rows(
        place, slot_utt, token, payloads, sums, pieces, slot_tokens, slot_count
    )

    share = out_rows.shape[0]
    own = jnp.zeros((width_count * share, out_rows.shape[1]), jnp.bfloat16)
    for distance in range(width_count):
        block = swap(out_rows, "mp", distance) if distance else out_rows
        own = lax.dynamic_update_slice_in_dim(own, block, (width_pos ^ distance) * share, 0)
    half = own.shape[0] // 2
    by_x = swap(own, "section", 1)
    by_y = swap(own, "tm", 2)
    stats = [vocabulary_stats(place, [own, swap(own, "tm", 1)], head)]
    by_x, by_y, stats[0] = lax.optimization_barrier((by_x, by_y, stats[0]))
    across = [swap(by_x[:half], "tm", 2), swap(by_y[half:], "section", 1)]
    stats.append(
        vocabulary_stats(place, [by_y, swap(by_y, "tm", 1), by_x, swap(by_x, "tm", 1)], head)
    )
    *across, stats[1] = lax.optimization_barrier((*across, stats[1]))
    across = jnp.concatenate(across)
    stats.append(vocabulary_stats(place, [across, swap(across, "tm", 1)], head))

    every = exchange(
        spread_stats(place, slot_utt, stats, section_count, group_count, width_count), ALL
    )
    return hypothesis_scores(
        place, slot_utt, hyp_len, every, slot_count, hyp_count, section_count, width_count
    )


def general(
    frame_len,
    slot_utt,
    enc_in,
    ffn_up,
    ffn_down,
    kv_proj,
    hyp_state,
    hyp_tok,
    hyp_len,
    q_proj,
    o_proj,
    head,
):
    section_count = lax.axis_size("section")
    group_count = lax.axis_size("tm")
    width_count = lax.axis_size("mp")
    section_pos = lax.axis_index("section")
    group_pos = lax.axis_index("tm")
    width_pos = lax.axis_index("mp")
    head_devices = section_count * width_count
    head_pos = section_pos * width_count + width_pos
    all_devices = head_devices * group_count

    frame_rows, utterances, enc_width = enc_in.shape
    assert utterances == group_count
    slot_count, hyp_count, positions, model_width = hyp_state.shape
    slot_tokens = hyp_count * positions
    device_heads = q_proj.shape[1] // HD
    group_heads = NH // KVH
    frame_share = frame_rows // width_count
    share_rows = slot_tokens // head_devices
    here_slots = lax.dynamic_slice_in_dim(slot_utt, group_pos * slot_count, slot_count, 0)

    dec_rows = hyp_state.reshape(slot_count * slot_tokens, model_width).astype(jnp.float32)
    queries = jnp.dot(
        square_norm(dec_rows).astype(jnp.bfloat16), q_proj, preferred_element_type=jnp.float32
    ).astype(jnp.bfloat16)
    queries = queries.reshape(slot_count, slot_tokens, device_heads * HD)
    shares = lax.dynamic_slice_in_dim(
        hyp_state.reshape(slot_count, slot_tokens, model_width), head_pos * share_rows, share_rows, 1
    )

    def by_utterance(values):
        out = []
        for utterance in range(utterances):
            block = values[0]
            for slot in range(1, slot_count):
                block = jnp.where(here_slots[slot] == utterance, values[slot], block)
            out.append(block)
        return jnp.stack(out)

    own_slot = jnp.argmax(slot_utt == group_pos)
    from_group = own_slot // slot_count
    queries = lax.dynamic_index_in_dim(
        exchange(by_utterance(queries), "tm"), from_group, 0, keepdims=False
    )
    resid_rows = lax.dynamic_index_in_dim(
        exchange(by_utterance(shares), "tm"), from_group, 0, keepdims=False
    )
    slot_targets = lax.all_gather(
        hyp_tok.reshape(slot_count, slot_tokens), "tm", axis=0, tiled=True
    )
    utt_slots = jnp.argmax(slot_utt[None, :] == jnp.arange(utterances)[:, None], axis=1)
    targets = jnp.take(slot_targets, utt_slots, axis=0).reshape(utterances * slot_tokens)

    enc_flat = (
        enc_in.reshape(width_count, frame_share, utterances, enc_width)
        .transpose(0, 2, 1, 3)
        .reshape(frame_rows * utterances, enc_width)
    )
    share_count = frame_share * utterances
    enc_normed = layer_norm(enc_flat.astype(jnp.float32)).astype(jnp.bfloat16)
    enc_inner = jax.nn.gelu(
        jnp.dot(enc_normed, ffn_up, preferred_element_type=jnp.float32), approximate=False
    ).astype(jnp.bfloat16)
    enc_summed = scatter_sum(
        jnp.dot(enc_inner, ffn_down, preferred_element_type=jnp.float32).astype(jnp.bfloat16),
        "mp",
        width_count,
    )
    own_frames = lax.dynamic_slice_in_dim(enc_flat, width_pos * share_count, share_count, 0)
    enc_states = layer_norm(own_frames.astype(jnp.float32) + enc_summed).astype(jnp.bfloat16)
    keys_values = jnp.dot(enc_states, kv_proj, preferred_element_type=jnp.float32).astype(
        jnp.bfloat16
    )
    keys_values = keys_values.reshape(utterances, frame_share, 2, KVH, HD)
    sent = []
    for section in range(section_count):
        per_width = []
        for width in range(width_count):
            kv_head = (section * width_count + width) * device_heads // group_heads
            per_width.append(
                keys_values[:, :, :, kv_head].reshape(utterances, frame_share, 2 * HD)
            )
        sent.append(jnp.stack(per_width, axis=1))
    sent = jnp.stack(sent).reshape(all_devices, frame_share, 2 * HD)
    frames_all = all_devices * frame_share
    keys_values = exchange(sent, ALL).reshape(frames_all, 2 * HD)

    frame_limit = lax.dynamic_index_in_dim(frame_len, group_pos, 0, keepdims=False)
    queries = queries.reshape(slot_tokens, device_heads, HD)
    scores = jnp.einsum(
        "qhd,fd->hqf", queries, keys_values[:, :HD], preferred_element_type=jnp.float32
    ) / math.sqrt(HD)
    visible = jnp.arange(frames_all, dtype=jnp.int32) < frame_limit
    scores = jnp.where(visible[None, None, :], scores, -jnp.inf)
    weights = jax.nn.softmax(scores, axis=-1).astype(jnp.bfloat16)
    context = jnp.einsum(
        "hqf,fd->qhd", weights, keys_values[:, HD:], preferred_element_type=jnp.float32
    ).astype(jnp.bfloat16)
    partial = jnp.dot(
        context.reshape(slot_tokens, device_heads * HD), o_proj, preferred_element_type=jnp.float32
    ).astype(jnp.bfloat16)
    partial = scatter_sum(partial, "section", section_count).astype(jnp.bfloat16)
    attn_out = scatter_sum(partial, "mp", width_count)
    out_normed = square_norm(resid_rows.astype(jnp.float32) + attn_out).astype(jnp.bfloat16)

    hidden_rows = lax.all_gather(out_normed, ALL, axis=0, tiled=True)
    logits = lax.dot_general(
        hidden_rows, head, (((1,), (1,)), ((), ())), preferred_element_type=jnp.float32
    )
    vocab_rows = head.shape[0]
    vocab_start = (
        (section_pos * group_count + group_pos) * width_count + width_pos
    ) * vocab_rows
    target_rows = (
        targets.reshape(utterances, section_count, width_count, share_rows)
        .transpose(1, 0, 2, 3)
        .reshape(-1)
    )
    upper = jnp.max(logits, axis=1)
    totals = jnp.sum(jnp.exp(logits - upper[:, None]), axis=1)
    matches = (
        jnp.arange(vocab_rows, dtype=jnp.int32)[None, :] == (target_rows - vocab_start)[:, None]
    )
    target_logit = jnp.sum(jnp.where(matches, logits, 0.0), axis=1)

    stats = jnp.stack([upper, totals, target_logit])
    stats = stats.reshape(3, section_count, utterances, width_count, share_rows)
    stats = stats.transpose(2, 0, 1, 3, 4).reshape(utterances, 3, slot_tokens)
    by_slot = jnp.take(stats, jnp.maximum(slot_utt, 0), axis=0)
    by_group = by_slot.reshape(1, group_count, 1, slot_count, 3, slot_tokens)
    by_group = jnp.broadcast_to(
        by_group, (section_count, group_count, width_count, slot_count, 3, slot_tokens)
    ).reshape(all_devices, slot_count, 3, slot_tokens)
    every = exchange(by_group, ALL)
    peak = jnp.max(every[:, :, 0], axis=0)
    total = jnp.sum(every[:, :, 1] * jnp.exp(every[:, :, 0] - peak[None]), axis=0)
    picked = jnp.sum(every[:, :, 2], axis=0)
    token_logp = (picked - (peak + jnp.log(total))).reshape(slot_count, hyp_count, positions)
    valid = jnp.arange(positions, dtype=jnp.int32)[None, None, :] < hyp_len[:, :, None]
    summed = jnp.sum(jnp.where(valid, token_logp, 0.0), axis=-1) / hyp_len.astype(
        jnp.float32
    ) + math.log(V)
    return jnp.where(here_slots[:, None] >= 0, summed, 0.0)


def solution(mesh):
    in_specs = (
        P(),
        P(),
        P(("section", "tm"), None, None),
        P(None, "mp"),
        P("mp", None),
        P(),
        P("tm", None, None, None),
        P("tm", None, None),
        P("tm", None),
        P(None, ("section", "mp")),
        P(("section", "mp"), None),
        P(("section", "tm", "mp"), None),
    )
    out_specs = P("tm", None)
    near = dict(mesh.shape) == {"section": 2, "tm": 4, "mp": 4}
    per_device = near_device if near else general
    return jax.shard_map(
        per_device, mesh=mesh, in_specs=in_specs, out_specs=out_specs, check_vma=False
    )
```

```python
import functools
import math

import jax
import jax.numpy as jnp
from jax import lax
from jax.experimental import pallas as pl
from jax.experimental.pallas import tpu as pltpu
from jax.sharding import PartitionSpec as P

NH = 32
KVH = 4
HD = 128
V = 64000
ALL = ("section", "tm", "mp")
LANES = 128


def layer_norm(values):
    center = values - jnp.mean(values, axis=-1, keepdims=True)
    spread = jnp.mean(center * center, axis=-1, keepdims=True)
    return center * lax.rsqrt(spread + 1e-05)


def square_norm(values):
    return values * lax.rsqrt(jnp.mean(values * values, axis=-1, keepdims=True) + 1e-06)


def exchange(blocks, axis):
    return lax.all_to_all(blocks, axis, split_axis=0, concat_axis=0, tiled=True)


def scatter_sum(partial, axis, count):
    blocks = partial.reshape((count, partial.shape[0] // count) + partial.shape[1:])
    return jnp.sum(exchange(blocks, axis).astype(jnp.float32), axis=0)


def swap(values, axis, distance):
    pairs = [(i, i ^ distance) for i in range(lax.axis_size(axis))]
    return lax.ppermute(values, axis, pairs)


def whole(shape):
    return pl.BlockSpec(shape, lambda *_: (0,) * len(shape))


SCALARS = pl.BlockSpec(memory_space=pltpu.SMEM)
PLACES = 5


class Scalars:
    def __init__(self, ref, slots, utterances, hyps):
        self.ref = ref
        self.slots = slots
        self.frames_at = PLACES + slots
        self.lengths_at = self.frames_at + utterances
        self.hyps = hyps

    def place(self, number):
        return self.ref[number]

    def slot(self, number):
        return self.ref[PLACES + number]

    def frames(self, utterance):
        return self.ref[self.frames_at + utterance]

    def length(self, slot, hyp):
        return self.ref[self.lengths_at + slot * self.hyps + hyp]


def dot(left, right):
    return jnp.dot(left, right, preferred_element_type=jnp.float32)


def dot_nt(left, right):
    return lax.dot_general(
        left, right, (((1,), (1,)), ((), ())), preferred_element_type=jnp.float32
    )


def start_copies(source_of, target_of, semaphores, count):
    copies = []
    for number in range(count):
        copy = pltpu.make_async_copy(
            source_of(number), target_of(number), semaphores.at[number]
        )
        copy.start()
        copies.append(copy)
    return copies


def ffn_kernel(steps, view, info_ref, after_ref, x_ref, up_ref, down_ref, *refs):
    out_ref, own_ref, inputs, rows, up, down, x_sem, up_sem, down_sem = refs
    count, share, width = out_ref.shape
    hidden_units = up_ref.shape[1]
    up_rows, down_rows = width // steps, hidden_units // steps
    x_copy = start_copies(lambda i: x_ref, lambda i: inputs, x_sem, 1)[0]
    up_copies = start_copies(
        lambda i: up_ref.at[pl.ds(i * up_rows, up_rows), :], lambda i: up.at[i], up_sem, steps
    )
    down_copies = start_copies(
        lambda i: down_ref.at[pl.ds(i * down_rows, down_rows), :],
        lambda i: down.at[i],
        down_sem,
        steps,
    )
    x_copy.wait()
    rows[...] = inputs[...].astype(jnp.float32).reshape(rows.shape)
    start = pl.multiple_of(view(info_ref).place(2) * share, share)
    own_ref[...] = rows[pl.ds(start, share), :].astype(jnp.bfloat16)
    normed = layer_norm(rows[...]).astype(jnp.bfloat16)
    hidden = None
    for number in range(steps):
        up_copies[number].wait()
        product = dot(normed[:, number * up_rows : (number + 1) * up_rows], up[number])
        hidden = product if hidden is None else hidden + product
    inner = (0.5 * hidden * (1.0 + lax.erf(hidden * math.sqrt(0.5)))).astype(jnp.bfloat16)
    total = None
    for number in range(steps):
        down_copies[number].wait()
        product = dot(inner[:, number * down_rows : (number + 1) * down_rows], down[number])
        total = product if total is None else total + product
    for part in range(count):
        out_ref[part] = total[part * share : (part + 1) * share, :].astype(jnp.bfloat16)


def in_hbm(values):
    return pltpu.with_memory_space_constraint(values, pltpu.HBM)


ANYWHERE = pl.BlockSpec(memory_space=pl.ANY)
INSIDE = pl.BlockSpec(memory_space=pltpu.VMEM)


def ffn(view, info, after, enc_in, up, down, count):
    frames, utterances, width = enc_in.shape
    rows = frames * utterances
    share = rows // count
    steps = 5
    return pl.pallas_call(
        functools.partial(ffn_kernel, steps, view),
        in_specs=[SCALARS] + [ANYWHERE] * 4,
        out_specs=[INSIDE] * 2,
        out_shape=[
            pltpu.HBM((count, share, width), jnp.bfloat16),
            jax.ShapeDtypeStruct((share, width), jnp.bfloat16),
        ],
        scratch_shapes=[
            pltpu.VMEM(enc_in.shape, jnp.bfloat16),
            pltpu.VMEM((rows, width), jnp.float32),
            pltpu.VMEM((steps, width // steps, up.shape[1]), jnp.bfloat16),
            pltpu.VMEM((steps, up.shape[1] // steps, width), jnp.bfloat16),
            pltpu.SemaphoreType.DMA((1,)),
            pltpu.SemaphoreType.DMA((steps,)),
            pltpu.SemaphoreType.DMA((steps,)),
        ],
        cost_estimate=pl.CostEstimate(
            flops=4 * rows * width * up.shape[1],
            bytes_accessed=4 * width * up.shape[1],
            transcendentals=rows * up.shape[1],
        ),
        compiler_params=pltpu.CompilerParams(vmem_limit_bytes=24 << 20),
        name="encoder_ffn",
    )(info, after, in_hbm(enc_in), in_hbm(up), in_hbm(down))


def query_kernel(count, depth, view, info_ref, x_ref, tok_ref, w_ref, *refs):
    outs, (states, weights, total, ordered, shares, x_sem, w_sem) = refs[:count], refs[count:]
    slots, tokens, width = x_ref.shape
    hyps, positions = tok_ref.shape[1:]
    columns = w_ref.shape[1]
    share = shares.shape[1] // 2
    parts = width // columns
    steps = width // depth
    x_copies = start_copies(lambda i: x_ref.at[i], lambda i: states.at[i], x_sem, slots)
    w_copies = start_copies(
        lambda i: w_ref.at[pl.ds(i * depth, depth), :], lambda i: weights.at[i], w_sem, steps
    )
    scales = []
    for slot in range(slots):
        x_copies[slot].wait()
        squares = jnp.zeros((tokens, depth), jnp.float32)
        for number in range(steps):
            part = states[slot, :, number * depth : (number + 1) * depth].astype(jnp.float32)
            squares += part * part
        mean = jnp.sum(squares, axis=1, keepdims=True) * (1.0 / width)
        scales.append(lax.rsqrt(mean + 1e-06))
    for number in range(steps):
        w_copies[number].wait()
        for slot in range(slots):
            part = states[slot, :, number * depth : (number + 1) * depth].astype(jnp.float32)
            product = dot((part * scales[slot]).astype(jnp.bfloat16), weights[number])
            if number == 0:
                total[slot] = product
            else:
                total[slot] += product
    info = view(info_ref)
    head_pos = info.place(4)
    lane = lax.broadcasted_iota(jnp.int32, (1, tokens), 1)
    position = lax.broadcasted_iota(jnp.int32, (1, positions), 1)
    share_place = (
        lax.broadcasted_iota(jnp.int32, (share, 1), 0) * (tokens // share) + head_pos
    )
    for slot in range(slots):
        order = jnp.full((1, tokens), -1, jnp.int32)
        target = jnp.zeros((share, positions), jnp.int32)
        start = jnp.int32(0)
        for hyp in range(hyps):
            length = info.length(slot, hyp)
            inside = (lane >= hyp * positions) & (lane < hyp * positions + length)
            order = jnp.where(inside, lane - hyp * positions + start, order)
            here = jnp.where(position < length, position + start, -1)
            target = jnp.where(here == share_place, tok_ref[slot, hyp : hyp + 1, :], target)
            start = start + length
        row = lax.broadcasted_iota(jnp.int32, (tokens, tokens), 0)
        move = jnp.where(order == row, 1.0, 0.0).astype(jnp.bfloat16)
        ordered[slot] = dot(move, total[slot].astype(jnp.bfloat16)).astype(jnp.bfloat16)
        mine = jnp.where(order == share_place, 1.0, 0.0).astype(jnp.bfloat16)
        shares[slot, :share, :] = dot(mine, states[slot]).astype(jnp.bfloat16)
        target = jnp.sum(target, axis=1, keepdims=True, dtype=jnp.int32)
        coarse = target // 256
        cell = lax.broadcasted_iota(jnp.int32, (share, columns), 1)
        packed = jnp.where(cell == 0, coarse, jnp.where(cell == 1, target - coarse * 256, 0))
        shares[slot, share:, :columns] = packed.astype(jnp.float32).astype(jnp.bfloat16)
    group = info.place(1)
    for distance in range(count):
        slot = jnp.int32(-1)
        for candidate in range(slots):
            holds = info.slot(group * slots + candidate) == group ^ distance
            slot = jnp.where(holds, candidate, slot)
        out = outs[distance]

        @pl.when(slot < 0)
        def _(out=out):
            out[...] = jnp.zeros_like(out)

        @pl.when(slot >= 0)
        def _(out=out, slot=slot):
            out[:tokens, :] = ordered[slot]
            for part in range(parts):
                first = tokens + part * share
                out[first : first + share, :] = shares[
                    slot, :share, part * columns : (part + 1) * columns
                ]
            out[tokens + parts * share :, :] = shares[slot, share:, :columns]


def queries_of(view, info, states, targets, weights, count, share):
    slots, tokens, width = states.shape
    columns = weights.shape[1]
    depth = 1024
    rows = tokens + (width // columns + 1) * share
    block = pltpu.HBM((rows, columns), jnp.bfloat16)
    return pl.pallas_call(
        functools.partial(query_kernel, count, depth, view),
        in_specs=[SCALARS, ANYWHERE, INSIDE, ANYWHERE],
        out_specs=[INSIDE] * count,
        out_shape=[block] * count,
        scratch_shapes=[
            pltpu.VMEM(states.shape, jnp.bfloat16),
            pltpu.VMEM((width // depth, depth, columns), jnp.bfloat16),
            pltpu.VMEM((slots, tokens, columns), jnp.float32),
            pltpu.VMEM((slots, tokens, columns), jnp.bfloat16),
            pltpu.VMEM((slots, 2 * share, width), jnp.bfloat16),
            pltpu.SemaphoreType.DMA((slots,)),
            pltpu.SemaphoreType.DMA((width // depth,)),
        ],
        cost_estimate=pl.CostEstimate(
            flops=2 * slots * tokens * width * columns,
            bytes_accessed=2 * width * (columns + slots * tokens),
            transcendentals=0,
        ),
        compiler_params=pltpu.CompilerParams(vmem_limit_bytes=20 << 20),
        name="hypothesis_queries",
    )(info, in_hbm(states), in_hbm(targets), in_hbm(weights))


def kv_kernel(sections, utterances, widths, *refs):
    parts_ref, own_ref, w_ref, out_ref = refs
    rows = own_ref.shape[0]
    frames = rows // utterances
    total = own_ref[...].astype(jnp.float32)
    summed = parts_ref[0].astype(jnp.float32)
    for part in range(1, parts_ref.shape[0]):
        summed += parts_ref[part].astype(jnp.float32)
    states = layer_norm(total + summed).astype(jnp.bfloat16)
    to = lax.broadcasted_iota(jnp.int32, (rows, rows), 0)
    come = lax.broadcasted_iota(jnp.int32, (rows, rows), 1)
    move = jnp.where(come == to % frames * utterances + to // frames, 1.0, 0.0)
    states = dot(move.astype(jnp.bfloat16), states).astype(jnp.bfloat16)
    both = dot(states, w_ref[...])
    half = KVH * HD
    per_kv = sections * widths // KVH
    for section in range(sections):
        for utterance in range(utterances):
            for width in range(0, widths, per_kv):
                kv_head = (section * widths + width) // per_kv
                take = slice(utterance * frames, (utterance + 1) * frames)
                block = jnp.concatenate(
                    [
                        both[take, kv_head * HD : (kv_head + 1) * HD],
                        both[take, half + kv_head * HD : half + (kv_head + 1) * HD],
                    ],
                    axis=1,
                )
                start = ((section * utterances + utterance) * widths + width) * frames
                block = jnp.concatenate([block] * per_kv, axis=0).astype(jnp.bfloat16)
                out_ref[start : start + per_kv * frames, :] = block


def keys_values_of(parts, own, weights, sections, utterances, widths):
    rows = sections * widths * own.shape[0]
    return pl.pallas_call(
        functools.partial(kv_kernel, sections, utterances, widths),
        in_specs=[INSIDE] * 3,
        out_specs=INSIDE,
        out_shape=pltpu.HBM((rows, 2 * HD), jnp.bfloat16),
        cost_estimate=pl.CostEstimate(
            flops=2 * own.shape[0] * weights.shape[0] * weights.shape[1],
            bytes_accessed=2 * weights.shape[0] * weights.shape[1],
            transcendentals=0,
        ),
        compiler_params=pltpu.CompilerParams(vmem_limit_bytes=24 << 20),
        name="frame_keys_values",
    )(parts, own, weights)


def choice_of_payload(info, slots):
    group = info.place(1)
    source = jnp.int32(0)
    for slot in range(info.slots):
        source = jnp.where(info.slot(slot) == group, slot // slots, source)
    return jnp.minimum(source ^ group, 2)


def attention_kernel(count, slots, capacity, pieces, sections, widths, tile, view, info_ref, *refs):
    info = view(info_ref)
    payloads, (kv_ref, w_ref) = refs[:count], refs[count : 2 + count]
    outs = refs[2 + count : 2 + count + 2 * len(pieces)]
    weights, picked, context, w_sem = refs[2 + count + 2 * len(pieces) :]
    tokens, columns = capacity, w_ref.shape[0]
    tiles = w_ref.shape[1] // tile
    w_copies = start_copies(
        lambda i: w_ref.at[:, pl.ds(i * tile, tile)], lambda i: weights.at[i], w_sem, tiles
    )
    source = choice_of_payload(info, slots)
    section_pos = info.place(0)
    frame_limit = info.frames(info.place(1))
    for distance in range(count):

        @pl.when(source == distance)
        def _(payload=payloads[distance]):
            picked[...] = payload[:tokens, :]

    keys = kv_ref[:, :HD]
    values = kv_ref[:, HD:]
    frames = kv_ref.shape[0]
    visible = lax.broadcasted_iota(jnp.int32, (tokens, frames), 1) < frame_limit
    for head in range(columns // HD):
        scores = dot_nt(picked[:, head * HD : (head + 1) * HD], keys) * (1.0 / math.sqrt(HD))
        scores = jnp.where(visible, scores, -jnp.inf)
        raised = jnp.exp(scores - jnp.max(scores, axis=1, keepdims=True))
        chances = (raised / jnp.sum(raised, axis=1, keepdims=True)).astype(jnp.bfloat16)
        context[:, head * HD : (head + 1) * HD] = dot(chances, values).astype(jnp.bfloat16)
    to = lax.broadcasted_iota(jnp.int32, (tokens, tokens), 0)
    come = lax.broadcasted_iota(jnp.int32, (tokens, tokens), 1)
    low_bit = info.place(2) % 2
    size = widths * pieces[0]
    block = to % size // pieces[0]
    section = jnp.where(to < size, 1 - section_pos, section_pos)
    first_order = (to % pieces[0] * sections + section) * widths + block % 2 * 2 + block // 2
    at = to - 2 * size
    size = widths * pieces[1]
    block = at % size // pieces[1]
    low = jnp.where(at < size, 1 - low_bit, low_bit)
    row = pieces[0] + at % pieces[1]
    second_order = (row * sections + block % 2) * widths + block // 2 * 2 + low
    move = come == jnp.where(at < 0, first_order, second_order)
    ordered = dot(jnp.where(move, 1.0, 0.0).astype(jnp.bfloat16), context[...])
    ordered = ordered.astype(jnp.bfloat16)
    for number in range(tiles):
        w_copies[number].wait()
        product = dot(ordered, weights[number]).astype(jnp.bfloat16)
        first = 0
        for out in outs:
            out[:, number * tile : (number + 1) * tile] = product[first : first + out.shape[0], :]
            first += out.shape[0]


def attend(view, info, payloads, keys_values, weights, pieces, sections, widths, slots):
    count = len(payloads)
    columns, width = weights.shape
    capacity = sum(pieces) * sections * widths
    tile = 1024
    tiles = width // tile
    shapes = [
        kind((piece * widths, width), jnp.bfloat16)
        for piece in pieces
        for kind in (pltpu.HBM, jax.ShapeDtypeStruct)
    ]
    return pl.pallas_call(
        functools.partial(
            attention_kernel, count, slots, capacity, pieces, sections, widths, tile, view
        ),
        in_specs=[SCALARS] + [INSIDE] * (count + 1) + [ANYWHERE],
        out_specs=[INSIDE] * len(shapes),
        out_shape=shapes,
        scratch_shapes=[
            pltpu.VMEM((tiles, columns, tile), jnp.bfloat16),
            pltpu.VMEM((capacity, columns), jnp.bfloat16),
            pltpu.VMEM((capacity, columns), jnp.bfloat16),
            pltpu.SemaphoreType.DMA((tiles,)),
        ],
        cost_estimate=pl.CostEstimate(
            flops=2 * capacity * columns * (width + 2 * keys_values.shape[0]),
            bytes_accessed=2 * columns * width + 2 * capacity * width,
            transcendentals=capacity * keys_values.shape[0] * columns // HD,
        ),
        compiler_params=pltpu.CompilerParams(vmem_limit_bytes=24 << 20),
        name="attention_projection",
    )(info, *payloads, keys_values, in_hbm(weights))


def norm_kernel(count, slots, tokens, pieces, view, info_ref, after_ref, *refs):
    payloads, blocks = refs[:count], refs[count : count + 2 * len(pieces)]
    out_ref, picked, total = refs[count + 2 * len(pieces) :]
    rows, width = total.shape
    columns = picked.shape[1]
    share = picked.shape[0] // (width // columns + 1)
    source = choice_of_payload(view(info_ref), slots)
    for choice in range(count):

        @pl.when(source == choice)
        def _(payload=payloads[choice]):
            picked[...] = payload[tokens:, :]

    first = 0
    for number, piece in enumerate(pieces):
        kept, other = blocks[2 * number : 2 * number + 2]
        total[first : first + piece, :] = kept[...] + other[...].astype(jnp.float32)
        first += piece
    for part in range(width // columns):
        take = slice(part * columns, (part + 1) * columns)
        total[:, take] += picked[part * share : part * share + rows, :].astype(jnp.float32)
    out_ref[:, :width] = square_norm(total[...]).astype(jnp.bfloat16)
    last = width // columns * share
    out_ref[:, width:] = picked[last : last + rows, :LANES]


def normed_rows(view, info, after, payloads, blocks, pieces, tokens, slots):
    width = blocks[0].shape[1]
    rows = sum(pieces)
    columns = payloads[0].shape[1]
    return pl.pallas_call(
        functools.partial(norm_kernel, len(payloads), slots, tokens, pieces, view),
        in_specs=[SCALARS, ANYWHERE] + [INSIDE] * (len(payloads) + len(blocks)),
        out_specs=INSIDE,
        out_shape=pltpu.HBM((rows, width + LANES), jnp.bfloat16),
        scratch_shapes=[
            pltpu.VMEM((payloads[0].shape[0] - tokens, columns), jnp.bfloat16),
            pltpu.VMEM((rows, width), jnp.float32),
        ],
        compiler_params=pltpu.CompilerParams(vmem_limit_bytes=16 << 20),
        name="token_rows",
    )(info, after, *payloads, *blocks)


def load_kernel(rows, after_ref, head_ref, out_ref, token_ref, semaphores):
    count = head_ref.shape[0] // rows
    copies = start_copies(
        lambda i: head_ref.at[pl.ds(i * rows, rows), :],
        lambda i: out_ref.at[pl.ds(i * rows, rows), :],
        semaphores,
        count,
    )
    token_ref[...] = jnp.zeros_like(token_ref)
    for copy in copies:
        copy.wait()


def load_head(after, head):
    rows = head.shape[0] // 5
    return pl.pallas_call(
        functools.partial(load_kernel, rows),
        in_specs=[ANYWHERE, ANYWHERE],
        out_specs=[INSIDE, INSIDE],
        out_shape=[
            pltpu.VMEM(head.shape, head.dtype),
            jax.ShapeDtypeStruct((8, LANES), jnp.float32),
        ],
        scratch_shapes=[pltpu.SemaphoreType.DMA((5,))],
        cost_estimate=pl.CostEstimate(
            flops=0, bytes_accessed=2 * head.size, transcendentals=0
        ),
        compiler_params=pltpu.CompilerParams(vmem_limit_bytes=20 << 20),
        name="vocabulary_rows",
    )(after, in_hbm(head))


def vocabulary_kernel(tile, first_ref, *refs):
    sets, (head_ref, out_ref, rows_ref, stat) = refs[:-4], refs[-4:]
    vocab_rows, width = head_ref.shape
    share = sets[0].shape[0]
    tokens = share * len(sets)
    cell = lax.broadcasted_iota(jnp.int32, (8, LANES), 1)
    take = jnp.where(cell == 0, 256.0, jnp.where(cell == 1, 1.0, 0.0)).astype(jnp.bfloat16)
    for number, rows in enumerate(sets):
        rows_ref[number * share : (number + 1) * share, :] = rows[...]
    target = dot_nt(take, rows_ref[:, width:])[0:1, :].astype(jnp.int32) - first_ref[3]
    stat[0:1, :] = jnp.full((1, tokens), -jnp.inf, jnp.float32)
    stat[8:9, :] = jnp.zeros((1, tokens), jnp.float32)
    stat[16:17, :] = jnp.zeros((1, tokens), jnp.float32)

    @pl.loop(0, vocab_rows // tile)
    def _(step):
        start = pl.multiple_of(step * tile, tile)
        logits = dot_nt(head_ref[pl.ds(start, tile), :], rows_ref[:, :width])
        vocab = lax.broadcasted_iota(jnp.int32, logits.shape, 0) + start
        before = stat[0:1, :]
        upper = jnp.maximum(before, jnp.max(logits, axis=0, keepdims=True))
        stat[8:9, :] = stat[8:9, :] * jnp.exp(before - upper) + jnp.sum(
            jnp.exp(logits - upper), axis=0, keepdims=True
        )
        stat[16:17, :] += jnp.sum(jnp.where(vocab == target, logits, 0.0), axis=0, keepdims=True)
        stat[0:1, :] = upper

    for number in range(len(sets)):
        for row in range(3):
            out_ref[number, row : row + 1, :] = stat[
                8 * row : 8 * row + 1, number * share : (number + 1) * share
            ]


def vocabulary_stats(info, sets, head):
    share = sets[0].shape[0]
    count = len(sets)
    width = head.shape[1]
    tokens = share * count
    return pl.pallas_call(
        functools.partial(vocabulary_kernel, head.shape[0] // 2),
        in_specs=[SCALARS] + [INSIDE] * (count + 1),
        out_specs=INSIDE,
        out_shape=jax.ShapeDtypeStruct((count, 8, share), jnp.float32),
        scratch_shapes=[
            pltpu.VMEM((tokens, width + LANES), jnp.bfloat16),
            pltpu.VMEM((24, tokens), jnp.float32),
        ],
        cost_estimate=pl.CostEstimate(
            flops=3 * tokens * head.shape[0] * width,
            bytes_accessed=2 * tokens * width,
            transcendentals=tokens * head.shape[0],
        ),
        compiler_params=pltpu.CompilerParams(vmem_limit_bytes=16 << 20),
        name="vocabulary_scores",
    )(info, *sets, pltpu.with_memory_space_constraint(head, pltpu.VMEM))


def spread_kernel(sections, groups, widths, view, info_ref, *refs):
    info = view(info_ref)
    stats, (out_ref, table, block) = refs[:-3], refs[-3:]
    share = table.shape[2]
    first = 0
    for stat in stats:
        table[first : first + stat.shape[0]] = stat[...]
        first += stat.shape[0]
    slots = info.slots // groups
    block[...] = jnp.zeros_like(block)
    for group in range(groups):
        for slot in range(slots):
            utterance = jnp.maximum(info.slot(group * slots + slot), 0)
            for section in range(sections):
                at = (section ^ info.place(0)) * groups + (utterance ^ info.place(1))
                block[group, 3 * slot : 3 * slot + 3, section * share : (section + 1) * share] = (
                    table[at][0:3, :]
                )
    for section in range(sections):
        for group in range(groups):
            for width in range(widths):
                out_ref[(section * groups + group) * widths + width] = block[group]


def spread_stats(view, info, stats, slots, sections, groups, widths):
    share = stats[0].shape[2]
    assert 3 * slots <= 8
    return pl.pallas_call(
        functools.partial(spread_kernel, sections, groups, widths, view),
        in_specs=[SCALARS] + [INSIDE] * len(stats),
        out_specs=INSIDE,
        out_shape=pltpu.HBM((sections * groups * widths, 8, sections * share), jnp.float32),
        scratch_shapes=[
            pltpu.VMEM((sections * groups, 8, share), jnp.float32),
            pltpu.VMEM((groups, 8, sections * share), jnp.float32),
        ],
        compiler_params=pltpu.CompilerParams(vmem_limit_bytes=16 << 20),
        name="statistics_by_group",
    )(info, *stats)


def score_kernel(sections, widths, view, info_ref, every_ref, out_ref):
    info = view(info_ref)
    slots, hyps = out_ref.shape
    lanes = every_ref.shape[2]
    share = lanes // sections // widths
    lane = lax.broadcasted_iota(jnp.int32, (1, lanes), 1)
    order = lane % share * (sections * widths) + lane // share
    column = lax.broadcasted_iota(jnp.int32, (1, hyps), 1)
    for slot in range(slots):
        upper = every_ref[:, 3 * slot, :]
        peak = jnp.max(upper, axis=0, keepdims=True)
        total = jnp.sum(
            every_ref[:, 3 * slot + 1, :] * jnp.exp(upper - peak), axis=0, keepdims=True
        )
        picked = jnp.sum(every_ref[:, 3 * slot + 2, :], axis=0, keepdims=True)
        logp = picked - (peak + jnp.log(total))
        scores = jnp.zeros((1, hyps), jnp.float32)
        start = jnp.int32(0)
        for hyp in range(hyps):
            length = info.length(slot, hyp)
            valid = (order >= start) & (order < start + length)
            summed = jnp.sum(jnp.where(valid, logp, 0.0), axis=1, keepdims=True)
            mean = summed / jnp.full((1, 1), length, jnp.int32).astype(jnp.float32)
            scores = jnp.where(column == hyp, mean + math.log(V), scores)
            start = start + length
        filled = info.slot(info.place(1) * slots + slot) >= 0
        out_ref[slot : slot + 1, :] = jnp.where(filled, scores, 0.0)


def hypothesis_scores(view, info, every, slots, hyps, sections, widths):
    return pl.pallas_call(
        functools.partial(score_kernel, sections, widths, view),
        in_specs=[SCALARS, INSIDE],
        out_specs=INSIDE,
        out_shape=jax.ShapeDtypeStruct((slots, hyps), jnp.float32),
        compiler_params=pltpu.CompilerParams(vmem_limit_bytes=16 << 20),
        name="hypothesis_scores",
    )(info, every)


def near_device(
    frame_len,
    slot_utt,
    enc_in,
    ffn_up,
    ffn_down,
    kv_proj,
    hyp_state,
    hyp_tok,
    hyp_len,
    q_proj,
    o_proj,
    head,
):
    section_count = lax.axis_size("section")
    group_count = lax.axis_size("tm")
    width_count = lax.axis_size("mp")
    section_pos = lax.axis_index("section")
    group_pos = lax.axis_index("tm")
    width_pos = lax.axis_index("mp")
    head_devices = section_count * width_count
    all_devices = head_devices * group_count

    frame_rows, utterances, enc_width = enc_in.shape
    slot_count, hyp_count, positions, model_width = hyp_state.shape
    slot_tokens = hyp_count * positions
    share_rows = slot_tokens // head_devices
    vocab_start = (
        (section_pos * group_count + group_pos) * width_count + width_pos
    ) * head.shape[0]
    head_pos = section_pos * width_count + width_pos
    place = jnp.stack([section_pos, group_pos, width_pos, vocab_start, head_pos])
    info = jnp.concatenate([place.astype(jnp.int32), slot_utt, frame_len, hyp_len.reshape(-1)])
    view = functools.partial(
        Scalars, slots=slot_utt.shape[0], utterances=utterances, hyps=hyp_count
    )

    blocks = queries_of(
        view,
        info,
        hyp_state.reshape(slot_count, slot_tokens, model_width),
        hyp_tok,
        q_proj,
        group_count,
        share_rows,
    )
    crossing = blocks[2] + swap(blocks[3], "tm", 1)
    payloads = [blocks[0], swap(blocks[1], "tm", 1), swap(crossing, "tm", 2)]

    parts, own_frames = ffn(view, info, crossing, enc_in, ffn_up, ffn_down, width_count)
    parts = exchange(parts, "mp")
    sent = keys_values_of(parts, own_frames, kv_proj, section_count, utterances, width_count)
    frames_all = all_devices * (frame_rows // width_count)
    keys_values = exchange(sent.reshape(all_devices, -1, 2 * HD), ALL).reshape(frames_all, 2 * HD)

    pieces = (share_rows // 2, share_rows - share_rows // 2)
    projected = attend(
        view,
        info,
        payloads,
        keys_values,
        o_proj,
        pieces,
        section_count,
        width_count,
        slot_count,
    )
    head, token = load_head(projected[1], head)

    def halve(total, came, axis, distance, side):
        if came is not None:
            total = total + came.astype(jnp.float32)
        half = total.shape[0] // 2
        kept = lax.dynamic_slice_in_dim(total, side * half, half, 0)
        sent = lax.dynamic_slice_in_dim(total, (1 - side) * half, half, 0)
        return kept, swap(sent.astype(jnp.bfloat16), axis, distance)

    low, high = width_pos % 2, width_pos // 2
    first = projected[1].astype(jnp.float32), swap(projected[0], "section", 1)
    second = projected[3].astype(jnp.float32), swap(projected[2], "mp", 1)
    first = halve(*first, "mp", 1, low)
    second = halve(*second, "mp", 2, high)
    first = halve(*first, "mp", 2, high)
    second = halve(*second, "section", 1, section_pos)
    sums = [*first, *second]
    out_rows = normed_rows(
        view, info, token, payloads, sums, pieces, slot_tokens, slot_count
    )

    share = out_rows.shape[0]
    own = jnp.zeros((width_count * share, out_rows.shape[1]), jnp.bfloat16)
    for distance in range(width_count):
        block = swap(out_rows, "mp", distance) if distance else out_rows
        own = lax.dynamic_update_slice_in_dim(own, block, (width_pos ^ distance) * share, 0)
    half = own.shape[0] // 2
    by_x = swap(own, "section", 1)
    by_y = swap(own, "tm", 2)
    stats = [vocabulary_stats(info, [own, swap(own, "tm", 1)], head)]
    by_x, by_y, stats[0] = lax.optimization_barrier((by_x, by_y, stats[0]))
    across = [swap(by_x[:half], "tm", 2), swap(by_y[half:], "section", 1)]
    stats.append(
        vocabulary_stats(info, [by_y, swap(by_y, "tm", 1), by_x, swap(by_x, "tm", 1)], head)
    )
    *across, stats[1] = lax.optimization_barrier((*across, stats[1]))
    across = jnp.concatenate(across)
    stats.append(vocabulary_stats(info, [across, swap(across, "tm", 1)], head))

    every = exchange(
        spread_stats(
            view, info, stats, slot_count, section_count, group_count, width_count
        ),
        ALL,
    )
    return hypothesis_scores(
        view, info, every, slot_count, hyp_count, section_count, width_count
    )


def general(
    frame_len,
    slot_utt,
    enc_in,
    ffn_up,
    ffn_down,
    kv_proj,
    hyp_state,
    hyp_tok,
    hyp_len,
    q_proj,
    o_proj,
    head,
):
    section_count = lax.axis_size("section")
    group_count = lax.axis_size("tm")
    width_count = lax.axis_size("mp")
    section_pos = lax.axis_index("section")
    group_pos = lax.axis_index("tm")
    width_pos = lax.axis_index("mp")
    head_devices = section_count * width_count
    head_pos = section_pos * width_count + width_pos
    all_devices = head_devices * group_count

    frame_rows, utterances, enc_width = enc_in.shape
    assert utterances == group_count
    slot_count, hyp_count, positions, model_width = hyp_state.shape
    slot_tokens = hyp_count * positions
    device_heads = q_proj.shape[1] // HD
    group_heads = NH // KVH
    frame_share = frame_rows // width_count
    share_rows = slot_tokens // head_devices
    here_slots = lax.dynamic_slice_in_dim(slot_utt, group_pos * slot_count, slot_count, 0)

    dec_rows = hyp_state.reshape(slot_count * slot_tokens, model_width).astype(jnp.float32)
    queries = jnp.dot(
        square_norm(dec_rows).astype(jnp.bfloat16), q_proj, preferred_element_type=jnp.float32
    ).astype(jnp.bfloat16)
    queries = queries.reshape(slot_count, slot_tokens, device_heads * HD)
    shares = lax.dynamic_slice_in_dim(
        hyp_state.reshape(slot_count, slot_tokens, model_width), head_pos * share_rows, share_rows, 1
    )

    def by_utterance(values):
        out = []
        for utterance in range(utterances):
            block = values[0]
            for slot in range(1, slot_count):
                block = jnp.where(here_slots[slot] == utterance, values[slot], block)
            out.append(block)
        return jnp.stack(out)

    own_slot = jnp.argmax(slot_utt == group_pos)
    from_group = own_slot // slot_count
    queries = lax.dynamic_index_in_dim(
        exchange(by_utterance(queries), "tm"), from_group, 0, keepdims=False
    )
    resid_rows = lax.dynamic_index_in_dim(
        exchange(by_utterance(shares), "tm"), from_group, 0, keepdims=False
    )
    slot_targets = lax.all_gather(
        hyp_tok.reshape(slot_count, slot_tokens), "tm", axis=0, tiled=True
    )
    utt_slots = jnp.argmax(slot_utt[None, :] == jnp.arange(utterances)[:, None], axis=1)
    targets = jnp.take(slot_targets, utt_slots, axis=0).reshape(utterances * slot_tokens)

    enc_flat = (
        enc_in.reshape(width_count, frame_share, utterances, enc_width)
        .transpose(0, 2, 1, 3)
        .reshape(frame_rows * utterances, enc_width)
    )
    share_count = frame_share * utterances
    enc_normed = layer_norm(enc_flat.astype(jnp.float32)).astype(jnp.bfloat16)
    enc_inner = jax.nn.gelu(
        jnp.dot(enc_normed, ffn_up, preferred_element_type=jnp.float32), approximate=False
    ).astype(jnp.bfloat16)
    enc_summed = scatter_sum(
        jnp.dot(enc_inner, ffn_down, preferred_element_type=jnp.float32).astype(jnp.bfloat16),
        "mp",
        width_count,
    )
    own_frames = lax.dynamic_slice_in_dim(enc_flat, width_pos * share_count, share_count, 0)
    enc_states = layer_norm(own_frames.astype(jnp.float32) + enc_summed).astype(jnp.bfloat16)
    keys_values = jnp.dot(enc_states, kv_proj, preferred_element_type=jnp.float32).astype(
        jnp.bfloat16
    )
    keys_values = keys_values.reshape(utterances, frame_share, 2, KVH, HD)
    sent = []
    for section in range(section_count):
        per_width = []
        for width in range(width_count):
            kv_head = (section * width_count + width) * device_heads // group_heads
            per_width.append(
                keys_values[:, :, :, kv_head].reshape(utterances, frame_share, 2 * HD)
            )
        sent.append(jnp.stack(per_width, axis=1))
    sent = jnp.stack(sent).reshape(all_devices, frame_share, 2 * HD)
    frames_all = all_devices * frame_share
    keys_values = exchange(sent, ALL).reshape(frames_all, 2 * HD)

    frame_limit = lax.dynamic_index_in_dim(frame_len, group_pos, 0, keepdims=False)
    queries = queries.reshape(slot_tokens, device_heads, HD)
    scores = jnp.einsum(
        "qhd,fd->hqf", queries, keys_values[:, :HD], preferred_element_type=jnp.float32
    ) / math.sqrt(HD)
    visible = jnp.arange(frames_all, dtype=jnp.int32) < frame_limit
    scores = jnp.where(visible[None, None, :], scores, -jnp.inf)
    weights = jax.nn.softmax(scores, axis=-1).astype(jnp.bfloat16)
    context = jnp.einsum(
        "hqf,fd->qhd", weights, keys_values[:, HD:], preferred_element_type=jnp.float32
    ).astype(jnp.bfloat16)
    partial = jnp.dot(
        context.reshape(slot_tokens, device_heads * HD), o_proj, preferred_element_type=jnp.float32
    ).astype(jnp.bfloat16)
    partial = scatter_sum(partial, "section", section_count).astype(jnp.bfloat16)
    attn_out = scatter_sum(partial, "mp", width_count)
    out_normed = square_norm(resid_rows.astype(jnp.float32) + attn_out).astype(jnp.bfloat16)

    hidden_rows = lax.all_gather(out_normed, ALL, axis=0, tiled=True)
    logits = lax.dot_general(
        hidden_rows, head, (((1,), (1,)), ((), ())), preferred_element_type=jnp.float32
    )
    vocab_rows = head.shape[0]
    vocab_start = (
        (section_pos * group_count + group_pos) * width_count + width_pos
    ) * vocab_rows
    target_rows = (
        targets.reshape(utterances, section_count, width_count, share_rows)
        .transpose(1, 0, 2, 3)
        .reshape(-1)
    )
    upper = jnp.max(logits, axis=1)
    totals = jnp.sum(jnp.exp(logits - upper[:, None]), axis=1)
    matches = (
        jnp.arange(vocab_rows, dtype=jnp.int32)[None, :] == (target_rows - vocab_start)[:, None]
    )
    target_logit = jnp.sum(jnp.where(matches, logits, 0.0), axis=1)

    stats = jnp.stack([upper, totals, target_logit])
    stats = stats.reshape(3, section_count, utterances, width_count, share_rows)
    stats = stats.transpose(2, 0, 1, 3, 4).reshape(utterances, 3, slot_tokens)
    by_slot = jnp.take(stats, jnp.maximum(slot_utt, 0), axis=0)
    by_group = by_slot.reshape(1, group_count, 1, slot_count, 3, slot_tokens)
    by_group = jnp.broadcast_to(
        by_group, (section_count, group_count, width_count, slot_count, 3, slot_tokens)
    ).reshape(all_devices, slot_count, 3, slot_tokens)
    every = exchange(by_group, ALL)
    peak = jnp.max(every[:, :, 0], axis=0)
    total = jnp.sum(every[:, :, 1] * jnp.exp(every[:, :, 0] - peak[None]), axis=0)
    picked = jnp.sum(every[:, :, 2], axis=0)
    token_logp = (picked - (peak + jnp.log(total))).reshape(slot_count, hyp_count, positions)
    valid = jnp.arange(positions, dtype=jnp.int32)[None, None, :] < hyp_len[:, :, None]
    summed = jnp.sum(jnp.where(valid, token_logp, 0.0), axis=-1) / hyp_len.astype(
        jnp.float32
    ) + math.log(V)
    return jnp.where(here_slots[:, None] >= 0, summed, 0.0)


def solution(mesh):
    in_specs = (
        P(),
        P(),
        P(("section", "tm"), None, None),
        P(None, "mp"),
        P("mp", None),
        P(),
        P("tm", None, None, None),
        P("tm", None, None),
        P("tm", None),
        P(None, ("section", "mp")),
        P(("section", "mp"), None),
        P(("section", "tm", "mp"), None),
    )
    out_specs = P("tm", None)
    near = dict(mesh.shape) == {"section": 2, "tm": 4, "mp": 4}
    per_device = near_device if near else general
    return jax.shard_map(
        per_device, mesh=mesh, in_specs=in_specs, out_specs=out_specs, check_vma=False
    )
```

```python
import functools
import math

import jax
import jax.numpy as jnp
from jax import lax
from jax.experimental import pallas as pl
from jax.experimental.pallas import tpu as pltpu
from jax.sharding import PartitionSpec as P

NH = 32
KVH = 4
HD = 128
V = 64000
ALL = ("section", "tm", "mp")
LANES = 128
FOLD = 4


def layer_norm(values):
    center = values - jnp.mean(values, axis=-1, keepdims=True)
    spread = jnp.mean(center * center, axis=-1, keepdims=True)
    return center * lax.rsqrt(spread + 1e-05)


def square_norm(values):
    return values * lax.rsqrt(jnp.mean(values * values, axis=-1, keepdims=True) + 1e-06)


def exchange(blocks, axis):
    return lax.all_to_all(blocks, axis, split_axis=0, concat_axis=0, tiled=True)


def scatter_sum(partial, axis, count):
    blocks = partial.reshape((count, partial.shape[0] // count) + partial.shape[1:])
    return jnp.sum(exchange(blocks, axis).astype(jnp.float32), axis=0)


def swap(values, axis, distance):
    pairs = [(i, i ^ distance) for i in range(lax.axis_size(axis))]
    return lax.ppermute(values, axis, pairs)


def whole(shape):
    return pl.BlockSpec(shape, lambda *_: (0,) * len(shape))


SCALARS = pl.BlockSpec(memory_space=pltpu.SMEM)


def dot(left, right):
    return jnp.dot(left, right, preferred_element_type=jnp.float32)


def dot_nt(left, right):
    return lax.dot_general(
        left, right, (((1,), (1,)), ((), ())), preferred_element_type=jnp.float32
    )


def start_copies(source_of, target_of, semaphores, count):
    copies = []
    for number in range(count):
        copy = pltpu.make_async_copy(
            source_of(number), target_of(number), semaphores.at[number]
        )
        copy.start()
        copies.append(copy)
    return copies


def ffn_kernel(tile, place_ref, x_ref, up_ref, down_ref, *refs):
    out_ref, own_ref, rows, total, up, down, up_sem, down_sem = refs
    count, share, width = out_ref.shape
    tiles = up_ref.shape[1] // tile
    up_copies = start_copies(
        lambda i: up_ref.at[:, pl.ds(i * tile, tile)], lambda i: up.at[i], up_sem, tiles
    )
    down_copies = start_copies(
        lambda i: down_ref.at[pl.ds(i * tile, tile), :], lambda i: down.at[i], down_sem, tiles
    )
    rows[...] = x_ref[...].astype(jnp.float32).reshape(rows.shape)
    start = pl.multiple_of(place_ref[2] * share, share)
    own_ref[...] = rows[pl.ds(start, share), :].astype(jnp.bfloat16)
    normed = layer_norm(rows[...]).astype(jnp.bfloat16)
    for number in range(tiles):
        up_copies[number].wait()
        hidden = dot(normed, up[number])
        inner = 0.5 * hidden * (1.0 + lax.erf(hidden * math.sqrt(0.5)))
        down_copies[number].wait()
        product = dot(inner.astype(jnp.bfloat16), down[number])
        if number == 0:
            total[...] = product
        else:
            total[...] += product
    for part in range(count):
        out_ref[part] = total[part * share : (part + 1) * share, :].astype(jnp.bfloat16)


def in_hbm(values):
    return pltpu.with_memory_space_constraint(values, pltpu.HBM)


ANYWHERE = pl.BlockSpec(memory_space=pl.ANY)
INSIDE = pl.BlockSpec(memory_space=pltpu.VMEM)


def ffn(place, enc_in, up, down, count):
    frames, utterances, width = enc_in.shape
    rows = frames * utterances
    share = rows // count
    tile = 256
    tiles = up.shape[1] // tile
    return pl.pallas_call(
        functools.partial(ffn_kernel, tile),
        in_specs=[SCALARS, INSIDE, ANYWHERE, ANYWHERE],
        out_specs=[INSIDE] * 2,
        out_shape=[
            jax.ShapeDtypeStruct((count, share, width), jnp.bfloat16),
            jax.ShapeDtypeStruct((share, width), jnp.bfloat16),
        ],
        scratch_shapes=[
            pltpu.VMEM((rows, width), jnp.float32),
            pltpu.VMEM((rows, width), jnp.float32),
            pltpu.VMEM((tiles, width, tile), jnp.bfloat16),
            pltpu.VMEM((tiles, tile, width), jnp.bfloat16),
            pltpu.SemaphoreType.DMA((tiles,)),
            pltpu.SemaphoreType.DMA((tiles,)),
        ],
        cost_estimate=pl.CostEstimate(
            flops=4 * rows * width * up.shape[1],
            bytes_accessed=4 * width * up.shape[1],
            transcendentals=rows * up.shape[1],
        ),
        compiler_params=pltpu.CompilerParams(vmem_limit_bytes=24 << 20),
        name="encoder_ffn",
    )(place, enc_in, in_hbm(up), in_hbm(down))


def query_kernel(
    count, depth, place_ref, slot_ref, length_ref, after_ref, x_ref, tok_ref, w_ref, *refs
):
    outs, (states, weights, normed, total, shares, x_sem, w_sem) = refs[:count], refs[count:]
    slots, tokens, width = x_ref.shape
    hyps = length_ref.shape[1]
    positions = tokens // hyps
    columns = w_ref.shape[1]
    share = shares.shape[1] // 2
    parts = width // columns
    x_copies = start_copies(lambda i: x_ref.at[i], lambda i: states.at[i], x_sem, slots)
    w_copies = start_copies(
        lambda i: w_ref.at[pl.ds(i * depth, depth), :],
        lambda i: weights.at[i],
        w_sem,
        width // depth,
    )
    head_pos = place_ref[4]
    lane = lax.broadcasted_iota(jnp.int32, (1, tokens), 1)
    for slot in range(slots):
        order = jnp.full((1, tokens), -1, jnp.int32)
        start = jnp.int32(0)
        for hyp in range(hyps):
            length = length_ref[slot, hyp]
            inside = (lane >= hyp * positions) & (lane < hyp * positions + length)
            order = jnp.where(inside, lane - hyp * positions + start, order)
            start = start + length
        row = lax.broadcasted_iota(jnp.int32, (tokens, tokens), 0)
        move = jnp.where(order == row, 1.0, 0.0).astype(jnp.bfloat16)
        x_copies[slot].wait()
        ordered = dot(move, states[slot])
        normed[slot * tokens : (slot + 1) * tokens, :] = square_norm(ordered).astype(jnp.bfloat16)
        share_row = lax.broadcasted_iota(jnp.int32, (share, tokens), 0)
        chosen = order == share_row * (tokens // share) + head_pos
        mine = dot(jnp.where(chosen, 1.0, 0.0).astype(jnp.bfloat16), states[slot])
        shares[slot, :share, :] = mine.astype(jnp.bfloat16)
        target = jnp.sum(
            jnp.where(chosen, tok_ref[slot], 0), axis=1, keepdims=True, dtype=jnp.int32
        )
        coarse = target // 256
        cell = lax.broadcasted_iota(jnp.int32, (share, columns), 1)
        packed = jnp.where(cell == 0, coarse, jnp.where(cell == 1, target - coarse * 256, 0))
        shares[slot, share:, :columns] = packed.astype(jnp.float32).astype(jnp.bfloat16)
    for number in range(width // depth):
        w_copies[number].wait()
        product = dot(normed[:, number * depth : (number + 1) * depth], weights[number])
        if number == 0:
            total[...] = product
        else:
            total[...] += product
    group = place_ref[1]
    for distance in range(count):
        slot = jnp.int32(-1)
        for candidate in range(slots):
            holds = slot_ref[group * slots + candidate] == group ^ distance
            slot = jnp.where(holds, candidate, slot)
        out = outs[distance]

        @pl.when(slot < 0)
        def _(out=out):
            out[...] = jnp.zeros_like(out)

        @pl.when(slot >= 0)
        def _(out=out, slot=slot):
            start = pl.multiple_of(slot * tokens, tokens)
            out[:tokens, :] = total[pl.ds(start, tokens), :].astype(jnp.bfloat16)
            for part in range(parts):
                first = tokens + part * share
                out[first : first + share, :] = shares[
                    slot, :share, part * columns : (part + 1) * columns
                ]
            out[tokens + parts * share :, :] = shares[slot, share:, :columns]


def queries_of(place, slot_utt, lengths, after, states, targets, weights, count, share):
    slots, tokens, width = states.shape
    columns = weights.shape[1]
    depth = 1024
    rows = tokens + (width // columns + 1) * share
    block = jax.ShapeDtypeStruct((rows, columns), jnp.bfloat16)
    return pl.pallas_call(
        functools.partial(query_kernel, count, depth),
        in_specs=[SCALARS] * 3 + [ANYWHERE, ANYWHERE, INSIDE, ANYWHERE],
        out_specs=[INSIDE] * count,
        out_shape=[block] * count,
        scratch_shapes=[
            pltpu.VMEM(states.shape, jnp.bfloat16),
            pltpu.VMEM((width // depth, depth, columns), jnp.bfloat16),
            pltpu.VMEM((slots * tokens, width), jnp.bfloat16),
            pltpu.VMEM((slots * tokens, columns), jnp.float32),
            pltpu.VMEM((slots, 2 * share, width), jnp.bfloat16),
            pltpu.SemaphoreType.DMA((slots,)),
            pltpu.SemaphoreType.DMA((width // depth,)),
        ],
        cost_estimate=pl.CostEstimate(
            flops=2 * slots * tokens * width * columns,
            bytes_accessed=2 * width * (columns + slots * tokens),
            transcendentals=0,
        ),
        compiler_params=pltpu.CompilerParams(vmem_limit_bytes=32 << 20),
        name="hypothesis_queries",
    )(place, slot_utt, lengths, after, in_hbm(states), targets, in_hbm(weights))


def kv_kernel(sections, utterances, widths, *refs):
    parts_ref, own_ref, w_ref, after_ref, out_ref = refs
    rows = own_ref.shape[0]
    frames = rows // utterances
    total = own_ref[...].astype(jnp.float32)
    summed = parts_ref[0].astype(jnp.float32)
    for part in range(1, parts_ref.shape[0]):
        summed += parts_ref[part].astype(jnp.float32)
    states = layer_norm(total + summed).astype(jnp.bfloat16)
    to = lax.broadcasted_iota(jnp.int32, (rows, rows), 0)
    come = lax.broadcasted_iota(jnp.int32, (rows, rows), 1)
    move = jnp.where(come == to % frames * utterances + to // frames, 1.0, 0.0)
    states = dot(move.astype(jnp.bfloat16), states).astype(jnp.bfloat16)
    both = dot(states, w_ref[...])
    half = KVH * HD
    per_kv = sections * widths // KVH
    for section in range(sections):
        for utterance in range(utterances):
            for width in range(0, widths, per_kv):
                kv_head = (section * widths + width) // per_kv
                take = slice(utterance * frames, (utterance + 1) * frames)
                block = jnp.concatenate(
                    [
                        both[take, kv_head * HD : (kv_head + 1) * HD],
                        both[take, half + kv_head * HD : half + (kv_head + 1) * HD],
                    ],
                    axis=1,
                )
                start = ((section * utterances + utterance) * widths + width) * frames
                block = jnp.concatenate([block] * per_kv, axis=0).astype(jnp.bfloat16)
                out_ref[start : start + per_kv * frames, :] = block


def keys_values_of(parts, own, weights, after, sections, utterances, widths):
    rows = sections * widths * own.shape[0]
    return pl.pallas_call(
        functools.partial(kv_kernel, sections, utterances, widths),
        in_specs=[INSIDE] * 3 + [ANYWHERE],
        out_specs=INSIDE,
        out_shape=jax.ShapeDtypeStruct((rows, 2 * HD), jnp.bfloat16),
        cost_estimate=pl.CostEstimate(
            flops=2 * own.shape[0] * weights.shape[0] * weights.shape[1],
            bytes_accessed=2 * weights.shape[0] * weights.shape[1],
            transcendentals=0,
        ),
        compiler_params=pltpu.CompilerParams(vmem_limit_bytes=24 << 20),
        name="frame_keys_values",
    )(parts, own, weights, after)


def choice_of_payload(place_ref, slot_ref, slots):
    group = place_ref[1]
    source = jnp.int32(0)
    for slot in range(slot_ref.shape[0]):
        source = jnp.where(slot_ref[slot] == group, slot // slots, source)
    return jnp.minimum(source ^ group, 2)


def attention_kernel(count, slots, capacity, pieces, sections, widths, tile, *refs):
    place_ref, slot_ref, frame_ref = refs[:3]
    payloads, (kv_ref, w_ref) = refs[3 : 3 + count], refs[3 + count : 5 + count]
    outs = refs[5 + count : 5 + count + 2 * len(pieces)]
    weights, picked, context, w_sem = refs[5 + count + 2 * len(pieces) :]
    tokens, columns = capacity, w_ref.shape[0]
    tiles = w_ref.shape[1] // tile
    w_copies = start_copies(
        lambda i: w_ref.at[:, pl.ds(i * tile, tile)], lambda i: weights.at[i], w_sem, tiles
    )
    source = choice_of_payload(place_ref, slot_ref, slots)
    section_pos = place_ref[0]
    frame_limit = frame_ref[place_ref[1]]
    for distance in range(count):

        @pl.when(source == distance)
        def _(payload=payloads[distance]):
            picked[...] = payload[:tokens, :]

    keys = kv_ref[:, :HD]
    values = kv_ref[:, HD:]
    frames = kv_ref.shape[0]
    visible = lax.broadcasted_iota(jnp.int32, (tokens, frames), 1) < frame_limit
    for head in range(columns // HD):
        scores = dot_nt(picked[:, head * HD : (head + 1) * HD], keys) * (1.0 / math.sqrt(HD))
        scores = jnp.where(visible, scores, -jnp.inf)
        raised = jnp.exp(scores - jnp.max(scores, axis=1, keepdims=True))
        chances = (raised / jnp.sum(raised, axis=1, keepdims=True)).astype(jnp.bfloat16)
        context[:, head * HD : (head + 1) * HD] = dot(chances, values).astype(jnp.bfloat16)
    to = lax.broadcasted_iota(jnp.int32, (tokens, tokens), 0)
    come = lax.broadcasted_iota(jnp.int32, (tokens, tokens), 1)
    low_bit = place_ref[2] % 2
    size = widths * pieces[0]
    block = to % size // pieces[0]
    section = jnp.where(to < size, 1 - section_pos, section_pos)
    first_order = (to % pieces[0] * sections + section) * widths + block % 2 * 2 + block // 2
    at = to - 2 * size
    size = widths * pieces[1]
    block = at % size // pieces[1]
    low = jnp.where(at < size, 1 - low_bit, low_bit)
    row = pieces[0] + at % pieces[1]
    second_order = (row * sections + block % 2) * widths + block // 2 * 2 + low
    move = come == jnp.where(at < 0, first_order, second_order)
    ordered = dot(jnp.where(move, 1.0, 0.0).astype(jnp.bfloat16), context[...])
    ordered = ordered.astype(jnp.bfloat16)
    for number in range(tiles):
        w_copies[number].wait()
        product = dot(ordered, weights[number]).astype(jnp.bfloat16)
        first = 0
        for out in outs:
            out[:, number * tile : (number + 1) * tile] = product[first : first + out.shape[0], :]
            first += out.shape[0]


def attend(place, slot_utt, frame_len, payloads, keys_values, weights, pieces, sections, widths, slots):
    count = len(payloads)
    columns, width = weights.shape
    capacity = sum(pieces) * sections * widths
    tile = 1024
    tiles = width // tile
    shapes = [
        jax.ShapeDtypeStruct((piece * widths, width), jnp.bfloat16)
        for piece in pieces
        for _ in range(2)
    ]
    return pl.pallas_call(
        functools.partial(
            attention_kernel, count, slots, capacity, pieces, sections, widths, tile
        ),
        in_specs=[SCALARS] * 3 + [INSIDE] * (count + 1) + [ANYWHERE],
        out_specs=[INSIDE] * len(shapes),
        out_shape=shapes,
        scratch_shapes=[
            pltpu.VMEM((tiles, columns, tile), jnp.bfloat16),
            pltpu.VMEM((capacity, columns), jnp.bfloat16),
            pltpu.VMEM((capacity, columns), jnp.bfloat16),
            pltpu.SemaphoreType.DMA((tiles,)),
        ],
        cost_estimate=pl.CostEstimate(
            flops=2 * capacity * columns * (width + 2 * keys_values.shape[0]),
            bytes_accessed=2 * columns * width + 2 * capacity * width,
            transcendentals=capacity * keys_values.shape[0] * columns // HD,
        ),
        compiler_params=pltpu.CompilerParams(vmem_limit_bytes=24 << 20),
        name="attention_projection",
    )(place, slot_utt, frame_len, *payloads, keys_values, in_hbm(weights))


def norm_kernel(count, slots, tokens, pieces, place_ref, slot_ref, after_ref, *refs):
    payloads, blocks = refs[:count], refs[count : count + 2 * len(pieces)]
    out_ref, picked, total = refs[count + 2 * len(pieces) :]
    rows, width = total.shape
    columns = picked.shape[1]
    share = picked.shape[0] // (width // columns + 1)
    source = choice_of_payload(place_ref, slot_ref, slots)
    for choice in range(count):

        @pl.when(source == choice)
        def _(payload=payloads[choice]):
            picked[...] = payload[tokens:, :]

    first = 0
    for number, piece in enumerate(pieces):
        kept, other = blocks[2 * number : 2 * number + 2]
        total[first : first + piece, :] = kept[...] + other[...].astype(jnp.float32)
        first += piece
    for part in range(width // columns):
        take = slice(part * columns, (part + 1) * columns)
        total[:, take] += picked[part * share : part * share + rows, :].astype(jnp.float32)
    shape = out_ref.shape[:2]
    normed = square_norm(total[...]).reshape(*shape, width)
    out_ref[:, :, :width] = normed.astype(jnp.bfloat16)
    last = width // columns * share
    target = picked[last : last + rows, :LANES].astype(jnp.float32).reshape(*shape, LANES)
    out_ref[:, :, width:] = target.astype(jnp.bfloat16)


def normed_rows(place, slot_utt, after, payloads, blocks, pieces, tokens, slots):
    width = blocks[0].shape[1]
    rows = sum(pieces)
    columns = payloads[0].shape[1]
    return pl.pallas_call(
        functools.partial(norm_kernel, len(payloads), slots, tokens, pieces),
        in_specs=[SCALARS] * 2 + [ANYWHERE] + [INSIDE] * (len(payloads) + len(blocks)),
        out_specs=INSIDE,
        out_shape=jax.ShapeDtypeStruct((rows // FOLD, FOLD, width + LANES), jnp.bfloat16),
        scratch_shapes=[
            pltpu.VMEM((payloads[0].shape[0] - tokens, columns), jnp.bfloat16),
            pltpu.VMEM((rows, width), jnp.float32),
        ],
        compiler_params=pltpu.CompilerParams(vmem_limit_bytes=16 << 20),
        name="token_rows",
    )(place, slot_utt, after, *payloads, *blocks)


def load_kernel(rows, after_ref, head_ref, out_ref, token_ref, semaphores):
    count = head_ref.shape[0] // rows
    copies = start_copies(
        lambda i: head_ref.at[pl.ds(i * rows, rows), :],
        lambda i: out_ref.at[pl.ds(i * rows, rows), :],
        semaphores,
        count,
    )
    token_ref[...] = jnp.zeros_like(token_ref)
    for copy in copies:
        copy.wait()


def load_head(after, head):
    rows = head.shape[0] // 5
    return pl.pallas_call(
        functools.partial(load_kernel, rows),
        in_specs=[ANYWHERE, ANYWHERE],
        out_specs=[INSIDE, INSIDE],
        out_shape=[
            pltpu.VMEM(head.shape, head.dtype),
            jax.ShapeDtypeStruct((8, LANES), jnp.float32),
        ],
        scratch_shapes=[pltpu.SemaphoreType.DMA((5,))],
        cost_estimate=pl.CostEstimate(
            flops=0, bytes_accessed=2 * head.size, transcendentals=0
        ),
        compiler_params=pltpu.CompilerParams(vmem_limit_bytes=20 << 20),
        name="vocabulary_rows",
    )(after, in_hbm(head))


def vocabulary_kernel(tile, first_ref, *refs):
    sets, (head_ref, out_ref, rows_ref, stat) = refs[:-4], refs[-4:]
    vocab_rows, width = head_ref.shape
    share = sets[0].shape[0] * FOLD
    tokens = share * len(sets)
    cell = lax.broadcasted_iota(jnp.int32, (8, LANES), 1)
    take = jnp.where(cell == 0, 256.0, jnp.where(cell == 1, 1.0, 0.0)).astype(jnp.bfloat16)
    for number, rows in enumerate(sets):
        flat = rows[...].astype(jnp.float32).reshape(share, width + LANES)
        rows_ref[number * share : (number + 1) * share, :] = flat.astype(jnp.bfloat16)
    target = dot_nt(take, rows_ref[:, width:])[0:1, :].astype(jnp.int32) - first_ref[3]
    stat[0:1, :] = jnp.full((1, tokens), -jnp.inf, jnp.float32)
    stat[8:9, :] = jnp.zeros((1, tokens), jnp.float32)
    stat[16:17, :] = jnp.zeros((1, tokens), jnp.float32)

    @pl.loop(0, vocab_rows // tile)
    def _(step):
        start = pl.multiple_of(step * tile, tile)
        logits = dot_nt(head_ref[pl.ds(start, tile), :], rows_ref[:, :width])
        vocab = lax.broadcasted_iota(jnp.int32, logits.shape, 0) + start
        before = stat[0:1, :]
        upper = jnp.maximum(before, jnp.max(logits, axis=0, keepdims=True))
        stat[8:9, :] = stat[8:9, :] * jnp.exp(before - upper) + jnp.sum(
            jnp.exp(logits - upper), axis=0, keepdims=True
        )
        stat[16:17, :] += jnp.sum(jnp.where(vocab == target, logits, 0.0), axis=0, keepdims=True)
        stat[0:1, :] = upper

    for number in range(len(sets)):
        for row in range(3):
            out_ref[number, row : row + 1, :] = stat[
                8 * row : 8 * row + 1, number * share : (number + 1) * share
            ]


def vocabulary_stats(place, sets, head):
    share = sets[0].shape[0] * FOLD
    count = len(sets)
    width = head.shape[1]
    tokens = share * count
    return pl.pallas_call(
        functools.partial(vocabulary_kernel, head.shape[0] // 2),
        in_specs=[SCALARS] + [INSIDE] * (count + 1),
        out_specs=INSIDE,
        out_shape=jax.ShapeDtypeStruct((count, 8, share), jnp.float32),
        scratch_shapes=[
            pltpu.VMEM((tokens, width + LANES), jnp.bfloat16),
            pltpu.VMEM((24, tokens), jnp.float32),
        ],
        cost_estimate=pl.CostEstimate(
            flops=3 * tokens * head.shape[0] * width,
            bytes_accessed=2 * tokens * width,
            transcendentals=tokens * head.shape[0],
        ),
        compiler_params=pltpu.CompilerParams(vmem_limit_bytes=16 << 20),
        name="vocabulary_scores",
    )(place, *sets, pltpu.with_memory_space_constraint(head, pltpu.VMEM))


def spread_kernel(sections, groups, widths, place_ref, slot_ref, *refs):
    stats, (out_ref, table, block) = refs[:-3], refs[-3:]
    share = table.shape[2]
    first = 0
    for stat in stats:
        table[first : first + stat.shape[0]] = stat[...]
        first += stat.shape[0]
    slots = slot_ref.shape[0] // groups
    block[...] = jnp.zeros_like(block)
    for group in range(groups):
        for slot in range(slots):
            utterance = jnp.maximum(slot_ref[group * slots + slot], 0)
            for section in range(sections):
                at = (section ^ place_ref[0]) * groups + (utterance ^ place_ref[1])
                block[group, 3 * slot : 3 * slot + 3, section * share : (section + 1) * share] = (
                    table[at][0:3, :]
                )
    for section in range(sections):
        for group in range(groups):
            for width in range(widths):
                out_ref[(section * groups + group) * widths + width] = block[group]


def spread_stats(place, slot_utt, stats, sections, groups, widths):
    share = stats[0].shape[2]
    assert 3 * slot_utt.shape[0] // groups <= 8
    return pl.pallas_call(
        functools.partial(spread_kernel, sections, groups, widths),
        in_specs=[SCALARS] * 2 + [INSIDE] * len(stats),
        out_specs=INSIDE,
        out_shape=jax.ShapeDtypeStruct(
            (sections * groups * widths, 8, sections * share), jnp.float32
        ),
        scratch_shapes=[
            pltpu.VMEM((sections * groups, 8, share), jnp.float32),
            pltpu.VMEM((groups, 8, sections * share), jnp.float32),
        ],
        compiler_params=pltpu.CompilerParams(vmem_limit_bytes=16 << 20),
        name="statistics_by_group",
    )(place, slot_utt, *stats)


def score_kernel(sections, widths, place_ref, slot_ref, length_ref, every_ref, out_ref):
    slots, hyps = out_ref.shape
    lanes = every_ref.shape[2]
    share = lanes // sections // widths
    lane = lax.broadcasted_iota(jnp.int32, (1, lanes), 1)
    order = lane % share * (sections * widths) + lane // share
    column = lax.broadcasted_iota(jnp.int32, (1, hyps), 1)
    for slot in range(slots):
        upper = every_ref[:, 3 * slot, :]
        peak = jnp.max(upper, axis=0, keepdims=True)
        total = jnp.sum(
            every_ref[:, 3 * slot + 1, :] * jnp.exp(upper - peak), axis=0, keepdims=True
        )
        picked = jnp.sum(every_ref[:, 3 * slot + 2, :], axis=0, keepdims=True)
        logp = picked - (peak + jnp.log(total))
        scores = jnp.zeros((1, hyps), jnp.float32)
        start = jnp.int32(0)
        for hyp in range(hyps):
            length = length_ref[slot, hyp]
            valid = (order >= start) & (order < start + length)
            summed = jnp.sum(jnp.where(valid, logp, 0.0), axis=1, keepdims=True)
            mean = summed / jnp.full((1, 1), length, jnp.int32).astype(jnp.float32)
            scores = jnp.where(column == hyp, mean + math.log(V), scores)
            start = start + length
        filled = slot_ref[place_ref[1] * slots + slot] >= 0
        out_ref[slot : slot + 1, :] = jnp.where(filled, scores, 0.0)


def hypothesis_scores(place, slot_utt, lengths, every, slots, hyps, sections, widths):
    return pl.pallas_call(
        functools.partial(score_kernel, sections, widths),
        in_specs=[SCALARS] * 3 + [INSIDE],
        out_specs=INSIDE,
        out_shape=jax.ShapeDtypeStruct((slots, hyps), jnp.float32),
        compiler_params=pltpu.CompilerParams(vmem_limit_bytes=16 << 20),
        name="hypothesis_scores",
    )(place, slot_utt, lengths, every)


def rest(pieces, slot_tokens, place, slot_utt, frame_len, hyp_len, payloads, keys_values, o_proj, head):
    section_count = lax.axis_size("section")
    group_count = lax.axis_size("tm")
    width_count = lax.axis_size("mp")
    section_pos = lax.axis_index("section")
    width_pos = lax.axis_index("mp")
    slot_count, hyp_count = hyp_len.shape
    projected = attend(
        place,
        slot_utt,
        frame_len,
        payloads,
        keys_values,
        o_proj,
        pieces,
        section_count,
        width_count,
        slot_count,
    )
    head, token = load_head(projected[1], head)

    def halve(total, came, axis, distance, side):
        if came is not None:
            total = total + came.astype(jnp.float32)
        half = total.shape[0] // 2
        kept = lax.dynamic_slice_in_dim(total, side * half, half, 0)
        sent = lax.dynamic_slice_in_dim(total, (1 - side) * half, half, 0)
        return kept, swap(sent.astype(jnp.bfloat16), axis, distance)

    low, high = width_pos % 2, width_pos // 2
    first = projected[1].astype(jnp.float32), swap(projected[0], "section", 1)
    second = projected[3].astype(jnp.float32), swap(projected[2], "mp", 1)
    first = halve(*first, "mp", 1, low)
    second = halve(*second, "mp", 2, high)
    first = halve(*first, "mp", 2, high)
    second = halve(*second, "section", 1, section_pos)
    sums = [*first, *second]
    out_rows = normed_rows(
        place, slot_utt, token, payloads, sums, pieces, slot_tokens, slot_count
    )

    own = jnp.zeros((width_count, *out_rows.shape), jnp.bfloat16)
    for distance in range(width_count):
        block = swap(out_rows, "mp", distance) if distance else out_rows
        own = lax.dynamic_update_index_in_dim(own, block, width_pos ^ distance, 0)
    own = own.reshape(-1, *out_rows.shape[1:])
    half = own.shape[0] // 2
    by_x = swap(own, "section", 1)
    by_y = swap(own, "tm", 2)
    stats = [vocabulary_stats(place, [own, swap(own, "tm", 1)], head)]
    by_x, by_y, stats[0] = lax.optimization_barrier((by_x, by_y, stats[0]))
    across = [swap(by_x[:half], "tm", 2), swap(by_y[half:], "section", 1)]
    stats.append(
        vocabulary_stats(place, [by_y, swap(by_y, "tm", 1), by_x, swap(by_x, "tm", 1)], head)
    )
    *across, stats[1] = lax.optimization_barrier((*across, stats[1]))
    across = jnp.concatenate(across)
    stats.append(vocabulary_stats(place, [across, swap(across, "tm", 1)], head))

    every = exchange(
        spread_stats(place, slot_utt, stats, section_count, group_count, width_count), ALL
    )
    return hypothesis_scores(
        place, slot_utt, hyp_len, every, slot_count, hyp_count, section_count, width_count
    )


def near_device(
    frame_len,
    slot_utt,
    enc_in,
    ffn_up,
    ffn_down,
    kv_proj,
    hyp_state,
    hyp_tok,
    hyp_len,
    q_proj,
    o_proj,
    head,
):
    section_count = lax.axis_size("section")
    group_count = lax.axis_size("tm")
    width_count = lax.axis_size("mp")
    section_pos = lax.axis_index("section")
    group_pos = lax.axis_index("tm")
    width_pos = lax.axis_index("mp")
    head_devices = section_count * width_count
    all_devices = head_devices * group_count

    frame_rows, utterances, enc_width = enc_in.shape
    slot_count, hyp_count, positions, model_width = hyp_state.shape
    slot_tokens = hyp_count * positions
    share_rows = slot_tokens // head_devices
    vocab_start = (
        (section_pos * group_count + group_pos) * width_count + width_pos
    ) * head.shape[0]
    head_pos = section_pos * width_count + width_pos
    place = jnp.stack([section_pos, group_pos, width_pos, vocab_start, head_pos])
    place = place.astype(jnp.int32)

    parts, own_frames = ffn(place, enc_in, ffn_up, ffn_down, width_count)
    parts = exchange(parts, "mp")

    blocks = queries_of(
        place,
        slot_utt,
        hyp_len,
        place,
        hyp_state.reshape(slot_count, slot_tokens, model_width),
        hyp_tok.reshape(slot_count, 1, slot_tokens),
        q_proj,
        group_count,
        share_rows,
    )
    crossing = blocks[2] + swap(blocks[3], "tm", 1)
    payloads = [blocks[0], swap(blocks[1], "tm", 1), swap(crossing, "tm", 2)]

    sent = keys_values_of(
        parts, own_frames, kv_proj, blocks[0], section_count, utterances, width_count
    )
    frames_all = all_devices * (frame_rows // width_count)
    keys_values = exchange(sent.reshape(all_devices, -1, 2 * HD), ALL).reshape(frames_all, 2 * HD)

    here_slots = lax.dynamic_slice_in_dim(slot_utt, group_pos * slot_count, slot_count, 0)
    filled = jnp.where(here_slots >= 0, jnp.sum(hyp_len, axis=1), 0)
    most = jnp.max(filled).reshape(1)
    for distance in (1, 2):
        most = jnp.maximum(most, swap(most, "tm", distance))
    operands = (place, slot_utt, frame_len, hyp_len, payloads, keys_values, o_proj, head)
    few = share_rows * 3 // 4
    return lax.cond(
        most[0] <= few * head_devices,
        functools.partial(rest, (few - few // 3, few // 3), slot_tokens),
        functools.partial(rest, (share_rows // 2, share_rows - share_rows // 2), slot_tokens),
        *operands,
    )


def general(
    frame_len,
    slot_utt,
    enc_in,
    ffn_up,
    ffn_down,
    kv_proj,
    hyp_state,
    hyp_tok,
    hyp_len,
    q_proj,
    o_proj,
    head,
):
    section_count = lax.axis_size("section")
    group_count = lax.axis_size("tm")
    width_count = lax.axis_size("mp")
    section_pos = lax.axis_index("section")
    group_pos = lax.axis_index("tm")
    width_pos = lax.axis_index("mp")
    head_devices = section_count * width_count
    head_pos = section_pos * width_count + width_pos
    all_devices = head_devices * group_count

    frame_rows, utterances, enc_width = enc_in.shape
    assert utterances == group_count
    slot_count, hyp_count, positions, model_width = hyp_state.shape
    slot_tokens = hyp_count * positions
    device_heads = q_proj.shape[1] // HD
    group_heads = NH // KVH
    frame_share = frame_rows // width_count
    share_rows = slot_tokens // head_devices
    here_slots = lax.dynamic_slice_in_dim(slot_utt, group_pos * slot_count, slot_count, 0)

    dec_rows = hyp_state.reshape(slot_count * slot_tokens, model_width).astype(jnp.float32)
    queries = jnp.dot(
        square_norm(dec_rows).astype(jnp.bfloat16), q_proj, preferred_element_type=jnp.float32
    ).astype(jnp.bfloat16)
    queries = queries.reshape(slot_count, slot_tokens, device_heads * HD)
    shares = lax.dynamic_slice_in_dim(
        hyp_state.reshape(slot_count, slot_tokens, model_width), head_pos * share_rows, share_rows, 1
    )

    def by_utterance(values):
        out = []
        for utterance in range(utterances):
            block = values[0]
            for slot in range(1, slot_count):
                block = jnp.where(here_slots[slot] == utterance, values[slot], block)
            out.append(block)
        return jnp.stack(out)

    own_slot = jnp.argmax(slot_utt == group_pos)
    from_group = own_slot // slot_count
    queries = lax.dynamic_index_in_dim(
        exchange(by_utterance(queries), "tm"), from_group, 0, keepdims=False
    )
    resid_rows = lax.dynamic_index_in_dim(
        exchange(by_utterance(shares), "tm"), from_group, 0, keepdims=False
    )
    slot_targets = lax.all_gather(
        hyp_tok.reshape(slot_count, slot_tokens), "tm", axis=0, tiled=True
    )
    utt_slots = jnp.argmax(slot_utt[None, :] == jnp.arange(utterances)[:, None], axis=1)
    targets = jnp.take(slot_targets, utt_slots, axis=0).reshape(utterances * slot_tokens)

    enc_flat = (
        enc_in.reshape(width_count, frame_share, utterances, enc_width)
        .transpose(0, 2, 1, 3)
        .reshape(frame_rows * utterances, enc_width)
    )
    share_count = frame_share * utterances
    enc_normed = layer_norm(enc_flat.astype(jnp.float32)).astype(jnp.bfloat16)
    enc_inner = jax.nn.gelu(
        jnp.dot(enc_normed, ffn_up, preferred_element_type=jnp.float32), approximate=False
    ).astype(jnp.bfloat16)
    enc_summed = scatter_sum(
        jnp.dot(enc_inner, ffn_down, preferred_element_type=jnp.float32).astype(jnp.bfloat16),
        "mp",
        width_count,
    )
    own_frames = lax.dynamic_slice_in_dim(enc_flat, width_pos * share_count, share_count, 0)
    enc_states = layer_norm(own_frames.astype(jnp.float32) + enc_summed).astype(jnp.bfloat16)
    keys_values = jnp.dot(enc_states, kv_proj, preferred_element_type=jnp.float32).astype(
        jnp.bfloat16
    )
    keys_values = keys_values.reshape(utterances, frame_share, 2, KVH, HD)
    sent = []
    for section in range(section_count):
        per_width = []
        for width in range(width_count):
            kv_head = (section * width_count + width) * device_heads // group_heads
            per_width.append(
                keys_values[:, :, :, kv_head].reshape(utterances, frame_share, 2 * HD)
            )
        sent.append(jnp.stack(per_width, axis=1))
    sent = jnp.stack(sent).reshape(all_devices, frame_share, 2 * HD)
    frames_all = all_devices * frame_share
    keys_values = exchange(sent, ALL).reshape(frames_all, 2 * HD)

    frame_limit = lax.dynamic_index_in_dim(frame_len, group_pos, 0, keepdims=False)
    queries = queries.reshape(slot_tokens, device_heads, HD)
    scores = jnp.einsum(
        "qhd,fd->hqf", queries, keys_values[:, :HD], preferred_element_type=jnp.float32
    ) / math.sqrt(HD)
    visible = jnp.arange(frames_all, dtype=jnp.int32) < frame_limit
    scores = jnp.where(visible[None, None, :], scores, -jnp.inf)
    weights = jax.nn.softmax(scores, axis=-1).astype(jnp.bfloat16)
    context = jnp.einsum(
        "hqf,fd->qhd", weights, keys_values[:, HD:], preferred_element_type=jnp.float32
    ).astype(jnp.bfloat16)
    partial = jnp.dot(
        context.reshape(slot_tokens, device_heads * HD), o_proj, preferred_element_type=jnp.float32
    ).astype(jnp.bfloat16)
    partial = scatter_sum(partial, "section", section_count).astype(jnp.bfloat16)
    attn_out = scatter_sum(partial, "mp", width_count)
    out_normed = square_norm(resid_rows.astype(jnp.float32) + attn_out).astype(jnp.bfloat16)

    hidden_rows = lax.all_gather(out_normed, ALL, axis=0, tiled=True)
    logits = lax.dot_general(
        hidden_rows, head, (((1,), (1,)), ((), ())), preferred_element_type=jnp.float32
    )
    vocab_rows = head.shape[0]
    vocab_start = (
        (section_pos * group_count + group_pos) * width_count + width_pos
    ) * vocab_rows
    target_rows = (
        targets.reshape(utterances, section_count, width_count, share_rows)
        .transpose(1, 0, 2, 3)
        .reshape(-1)
    )
    upper = jnp.max(logits, axis=1)
    totals = jnp.sum(jnp.exp(logits - upper[:, None]), axis=1)
    matches = (
        jnp.arange(vocab_rows, dtype=jnp.int32)[None, :] == (target_rows - vocab_start)[:, None]
    )
    target_logit = jnp.sum(jnp.where(matches, logits, 0.0), axis=1)

    stats = jnp.stack([upper, totals, target_logit])
    stats = stats.reshape(3, section_count, utterances, width_count, share_rows)
    stats = stats.transpose(2, 0, 1, 3, 4).reshape(utterances, 3, slot_tokens)
    by_slot = jnp.take(stats, jnp.maximum(slot_utt, 0), axis=0)
    by_group = by_slot.reshape(1, group_count, 1, slot_count, 3, slot_tokens)
    by_group = jnp.broadcast_to(
        by_group, (section_count, group_count, width_count, slot_count, 3, slot_tokens)
    ).reshape(all_devices, slot_count, 3, slot_tokens)
    every = exchange(by_group, ALL)
    peak = jnp.max(every[:, :, 0], axis=0)
    total = jnp.sum(every[:, :, 1] * jnp.exp(every[:, :, 0] - peak[None]), axis=0)
    picked = jnp.sum(every[:, :, 2], axis=0)
    token_logp = (picked - (peak + jnp.log(total))).reshape(slot_count, hyp_count, positions)
    valid = jnp.arange(positions, dtype=jnp.int32)[None, None, :] < hyp_len[:, :, None]
    summed = jnp.sum(jnp.where(valid, token_logp, 0.0), axis=-1) / hyp_len.astype(
        jnp.float32
    ) + math.log(V)
    return jnp.where(here_slots[:, None] >= 0, summed, 0.0)


def solution(mesh):
    in_specs = (
        P(),
        P(),
        P(("section", "tm"), None, None),
        P(None, "mp"),
        P("mp", None),
        P(),
        P("tm", None, None, None),
        P("tm", None, None),
        P("tm", None),
        P(None, ("section", "mp")),
        P(("section", "mp"), None),
        P(("section", "tm", "mp"), None),
    )
    out_specs = P("tm", None)
    near = dict(mesh.shape) == {"section": 2, "tm": 4, "mp": 4}
    per_device = near_device if near else general
    return jax.shard_map(
        per_device, mesh=mesh, in_specs=in_specs, out_specs=out_specs, check_vma=False
    )
```

```python
import functools
import math

import jax
import jax.numpy as jnp
from jax import lax
from jax.experimental import pallas as pl
from jax.experimental.pallas import tpu as pltpu
from jax.sharding import PartitionSpec as P

NH = 32
KVH = 4
HD = 128
V = 64000
ALL = ("section", "tm", "mp")
LANES = 128
FOLD = 4


def layer_norm(values):
    center = values - jnp.mean(values, axis=-1, keepdims=True)
    spread = jnp.mean(center * center, axis=-1, keepdims=True)
    return center * lax.rsqrt(spread + 1e-05)


def square_norm(values):
    return values * lax.rsqrt(jnp.mean(values * values, axis=-1, keepdims=True) + 1e-06)


def exchange(blocks, axis):
    return lax.all_to_all(blocks, axis, split_axis=0, concat_axis=0, tiled=True)


def scatter_sum(partial, axis, count):
    blocks = partial.reshape((count, partial.shape[0] // count) + partial.shape[1:])
    return jnp.sum(exchange(blocks, axis).astype(jnp.float32), axis=0)


def swap(values, axis, distance):
    pairs = [(i, i ^ distance) for i in range(lax.axis_size(axis))]
    return lax.ppermute(values, axis, pairs)


def whole(shape):
    return pl.BlockSpec(shape, lambda *_: (0,) * len(shape))


SCALARS = pl.BlockSpec(memory_space=pltpu.SMEM)


def dot(left, right):
    return jnp.dot(left, right, preferred_element_type=jnp.float32)


def dot_nt(left, right):
    return lax.dot_general(
        left, right, (((1,), (1,)), ((), ())), preferred_element_type=jnp.float32
    )


def start_copies(source_of, target_of, semaphores, count):
    copies = []
    for number in range(count):
        copy = pltpu.make_async_copy(
            source_of(number), target_of(number), semaphores.at[number]
        )
        copy.start()
        copies.append(copy)
    return copies


def ffn_kernel(tile, place_ref, x_ref, up_ref, down_ref, *refs):
    out_ref, own_ref, rows, total, up, down, up_sem, down_sem = refs
    count, share, width = out_ref.shape
    tiles = up_ref.shape[1] // tile
    up_copies = start_copies(
        lambda i: up_ref.at[:, pl.ds(i * tile, tile)], lambda i: up.at[i], up_sem, tiles
    )
    down_copies = start_copies(
        lambda i: down_ref.at[pl.ds(i * tile, tile), :], lambda i: down.at[i], down_sem, tiles
    )
    rows[...] = x_ref[...].astype(jnp.float32).reshape(rows.shape)
    start = pl.multiple_of(place_ref[2] * share, share)
    own_ref[...] = rows[pl.ds(start, share), :].astype(jnp.bfloat16)
    normed = layer_norm(rows[...]).astype(jnp.bfloat16)
    for number in range(tiles):
        up_copies[number].wait()
        hidden = dot(normed, up[number])
        inner = 0.5 * hidden * (1.0 + lax.erf(hidden * math.sqrt(0.5)))
        down_copies[number].wait()
        product = dot(inner.astype(jnp.bfloat16), down[number])
        if number == 0:
            total[...] = product
        else:
            total[...] += product
    for part in range(count):
        out_ref[part] = total[part * share : (part + 1) * share, :].astype(jnp.bfloat16)


def in_hbm(values):
    return pltpu.with_memory_space_constraint(values, pltpu.HBM)


ANYWHERE = pl.BlockSpec(memory_space=pl.ANY)
INSIDE = pl.BlockSpec(memory_space=pltpu.VMEM)


def ffn(place, enc_in, up, down, count):
    frames, utterances, width = enc_in.shape
    rows = frames * utterances
    share = rows // count
    tile = 256
    tiles = up.shape[1] // tile
    return pl.pallas_call(
        functools.partial(ffn_kernel, tile),
        in_specs=[SCALARS, INSIDE, ANYWHERE, ANYWHERE],
        out_specs=[INSIDE] * 2,
        out_shape=[
            jax.ShapeDtypeStruct((count, share, width), jnp.bfloat16),
            jax.ShapeDtypeStruct((share, width), jnp.bfloat16),
        ],
        scratch_shapes=[
            pltpu.VMEM((rows, width), jnp.float32),
            pltpu.VMEM((rows, width), jnp.float32),
            pltpu.VMEM((tiles, width, tile), jnp.bfloat16),
            pltpu.VMEM((tiles, tile, width), jnp.bfloat16),
            pltpu.SemaphoreType.DMA((tiles,)),
            pltpu.SemaphoreType.DMA((tiles,)),
        ],
        cost_estimate=pl.CostEstimate(
            flops=4 * rows * width * up.shape[1],
            bytes_accessed=4 * width * up.shape[1],
            transcendentals=rows * up.shape[1],
        ),
        compiler_params=pltpu.CompilerParams(vmem_limit_bytes=24 << 20),
        name="encoder_ffn",
    )(place, enc_in, in_hbm(up), in_hbm(down))


def query_kernel(
    count, depth, place_ref, slot_ref, length_ref, after_ref, x_ref, tok_ref, w_ref, *refs
):
    outs, (states, weights, normed, total, shares, x_sem, w_sem) = refs[:count], refs[count:]
    slots, tokens, width = x_ref.shape
    hyps = length_ref.shape[1]
    positions = tokens // hyps
    columns = w_ref.shape[1]
    share = shares.shape[1] // 2
    parts = width // columns
    x_copies = start_copies(lambda i: x_ref.at[i], lambda i: states.at[i], x_sem, slots)
    w_copies = start_copies(
        lambda i: w_ref.at[pl.ds(i * depth, depth), :],
        lambda i: weights.at[i],
        w_sem,
        width // depth,
    )
    head_pos = place_ref[4]
    lane = lax.broadcasted_iota(jnp.int32, (1, tokens), 1)
    for slot in range(slots):
        order = jnp.full((1, tokens), -1, jnp.int32)
        start = jnp.int32(0)
        for hyp in range(hyps):
            length = length_ref[slot, hyp]
            inside = (lane >= hyp * positions) & (lane < hyp * positions + length)
            order = jnp.where(inside, lane - hyp * positions + start, order)
            start = start + length
        row = lax.broadcasted_iota(jnp.int32, (tokens, tokens), 0)
        move = jnp.where(order == row, 1.0, 0.0).astype(jnp.bfloat16)
        x_copies[slot].wait()
        ordered = dot(move, states[slot])
        normed[slot * tokens : (slot + 1) * tokens, :] = square_norm(ordered).astype(jnp.bfloat16)
        share_row = lax.broadcasted_iota(jnp.int32, (share, tokens), 0)
        chosen = order == share_row * (tokens // share) + head_pos
        mine = dot(jnp.where(chosen, 1.0, 0.0).astype(jnp.bfloat16), states[slot])
        shares[slot, :share, :] = mine.astype(jnp.bfloat16)
        target = jnp.sum(
            jnp.where(chosen, tok_ref[slot], 0), axis=1, keepdims=True, dtype=jnp.int32
        )
        coarse = target // 256
        cell = lax.broadcasted_iota(jnp.int32, (share, columns), 1)
        packed = jnp.where(cell == 0, coarse, jnp.where(cell == 1, target - coarse * 256, 0))
        shares[slot, share:, :columns] = packed.astype(jnp.float32).astype(jnp.bfloat16)
    for number in range(width // depth):
        w_copies[number].wait()
        product = dot(normed[:, number * depth : (number + 1) * depth], weights[number])
        if number == 0:
            total[...] = product
        else:
            total[...] += product
    group = place_ref[1]
    for distance in range(count):
        slot = jnp.int32(-1)
        for candidate in range(slots):
            holds = slot_ref[group * slots + candidate] == group ^ distance
            slot = jnp.where(holds, candidate, slot)
        out = outs[distance]

        @pl.when(slot < 0)
        def _(out=out):
            out[...] = jnp.zeros_like(out)

        @pl.when(slot >= 0)
        def _(out=out, slot=slot):
            start = pl.multiple_of(slot * tokens, tokens)
            out[:tokens, :] = total[pl.ds(start, tokens), :].astype(jnp.bfloat16)
            for part in range(parts):
                first = tokens + part * share
                out[first : first + share, :] = shares[
                    slot, :share, part * columns : (part + 1) * columns
                ]
            out[tokens + parts * share :, :] = shares[slot, share:, :columns]


def queries_of(place, slot_utt, lengths, after, states, targets, weights, count, share):
    slots, tokens, width = states.shape
    columns = weights.shape[1]
    depth = 1024
    rows = tokens + (width // columns + 1) * share
    block = jax.ShapeDtypeStruct((rows, columns), jnp.bfloat16)
    return pl.pallas_call(
        functools.partial(query_kernel, count, depth),
        in_specs=[SCALARS] * 3 + [ANYWHERE, ANYWHERE, INSIDE, ANYWHERE],
        out_specs=[INSIDE] * count,
        out_shape=[block] * count,
        scratch_shapes=[
            pltpu.VMEM(states.shape, jnp.bfloat16),
            pltpu.VMEM((width // depth, depth, columns), jnp.bfloat16),
            pltpu.VMEM((slots * tokens, width), jnp.bfloat16),
            pltpu.VMEM((slots * tokens, columns), jnp.float32),
            pltpu.VMEM((slots, 2 * share, width), jnp.bfloat16),
            pltpu.SemaphoreType.DMA((slots,)),
            pltpu.SemaphoreType.DMA((width // depth,)),
        ],
        cost_estimate=pl.CostEstimate(
            flops=2 * slots * tokens * width * columns,
            bytes_accessed=2 * width * (columns + slots * tokens),
            transcendentals=0,
        ),
        compiler_params=pltpu.CompilerParams(vmem_limit_bytes=32 << 20),
        name="hypothesis_queries",
    )(place, slot_utt, lengths, after, in_hbm(states), targets, in_hbm(weights))


def kv_kernel(sections, utterances, widths, *refs):
    parts_ref, own_ref, w_ref, after_ref, out_ref = refs
    rows = own_ref.shape[0]
    frames = rows // utterances
    total = own_ref[...].astype(jnp.float32)
    summed = parts_ref[0].astype(jnp.float32)
    for part in range(1, parts_ref.shape[0]):
        summed += parts_ref[part].astype(jnp.float32)
    states = layer_norm(total + summed).astype(jnp.bfloat16)
    to = lax.broadcasted_iota(jnp.int32, (rows, rows), 0)
    come = lax.broadcasted_iota(jnp.int32, (rows, rows), 1)
    move = jnp.where(come == to % frames * utterances + to // frames, 1.0, 0.0)
    states = dot(move.astype(jnp.bfloat16), states).astype(jnp.bfloat16)
    both = dot(states, w_ref[...])
    half = KVH * HD
    per_kv = sections * widths // KVH
    for section in range(sections):
        for utterance in range(utterances):
            for width in range(0, widths, per_kv):
                kv_head = (section * widths + width) // per_kv
                take = slice(utterance * frames, (utterance + 1) * frames)
                block = jnp.concatenate(
                    [
                        both[take, kv_head * HD : (kv_head + 1) * HD],
                        both[take, half + kv_head * HD : half + (kv_head + 1) * HD],
                    ],
                    axis=1,
                )
                start = ((section * utterances + utterance) * widths + width) * frames
                block = jnp.concatenate([block] * per_kv, axis=0).astype(jnp.bfloat16)
                out_ref[start : start + per_kv * frames, :] = block


def keys_values_of(parts, own, weights, after, sections, utterances, widths):
    rows = sections * widths * own.shape[0]
    return pl.pallas_call(
        functools.partial(kv_kernel, sections, utterances, widths),
        in_specs=[INSIDE] * 3 + [ANYWHERE],
        out_specs=INSIDE,
        out_shape=jax.ShapeDtypeStruct((rows, 2 * HD), jnp.bfloat16),
        cost_estimate=pl.CostEstimate(
            flops=2 * own.shape[0] * weights.shape[0] * weights.shape[1],
            bytes_accessed=2 * weights.shape[0] * weights.shape[1],
            transcendentals=0,
        ),
        compiler_params=pltpu.CompilerParams(vmem_limit_bytes=24 << 20),
        name="frame_keys_values",
    )(parts, own, weights, after)


def choice_of_payload(place_ref, slot_ref, slots):
    group = place_ref[1]
    source = jnp.int32(0)
    for slot in range(slot_ref.shape[0]):
        source = jnp.where(slot_ref[slot] == group, slot // slots, source)
    return jnp.minimum(source ^ group, 2)


def attention_kernel(count, slots, capacity, pieces, sections, widths, tile, *refs):
    place_ref, slot_ref, frame_ref = refs[:3]
    payloads, (kv_ref, w_ref) = refs[3 : 3 + count], refs[3 + count : 5 + count]
    outs = refs[5 + count : 5 + count + 2 * len(pieces)]
    weights, picked, context, w_sem = refs[5 + count + 2 * len(pieces) :]
    tokens, columns = capacity, w_ref.shape[0]
    tiles = w_ref.shape[1] // tile
    w_copies = start_copies(
        lambda i: w_ref.at[:, pl.ds(i * tile, tile)], lambda i: weights.at[i], w_sem, tiles
    )
    source = choice_of_payload(place_ref, slot_ref, slots)
    section_pos = place_ref[0]
    frame_limit = frame_ref[place_ref[1]]
    for distance in range(count):

        @pl.when(source == distance)
        def _(payload=payloads[distance]):
            picked[...] = payload[:tokens, :]

    keys = kv_ref[:, :HD]
    values = kv_ref[:, HD:]
    frames = kv_ref.shape[0]
    visible = lax.broadcasted_iota(jnp.int32, (tokens, frames), 1) < frame_limit
    for head in range(columns // HD):
        scores = dot_nt(picked[:, head * HD : (head + 1) * HD], keys) * (1.0 / math.sqrt(HD))
        scores = jnp.where(visible, scores, -jnp.inf)
        raised = jnp.exp(scores - jnp.max(scores, axis=1, keepdims=True))
        chances = (raised / jnp.sum(raised, axis=1, keepdims=True)).astype(jnp.bfloat16)
        context[:, head * HD : (head + 1) * HD] = dot(chances, values).astype(jnp.bfloat16)
    to = lax.broadcasted_iota(jnp.int32, (tokens, tokens), 0)
    come = lax.broadcasted_iota(jnp.int32, (tokens, tokens), 1)
    low_bit = place_ref[2] % 2
    size = widths * pieces[0]
    block = to % size // pieces[0]
    section = jnp.where(to < size, 1 - section_pos, section_pos)
    first_order = (to % pieces[0] * sections + section) * widths + block % 2 * 2 + block // 2
    at = to - 2 * size
    size = widths * pieces[1]
    block = at % size // pieces[1]
    low = jnp.where(at < size, 1 - low_bit, low_bit)
    row = pieces[0] + at % pieces[1]
    second_order = (row * sections + block % 2) * widths + block // 2 * 2 + low
    move = come == jnp.where(at < 0, first_order, second_order)
    ordered = dot(jnp.where(move, 1.0, 0.0).astype(jnp.bfloat16), context[...])
    ordered = ordered.astype(jnp.bfloat16)
    for number in range(tiles):
        w_copies[number].wait()
        product = dot(ordered, weights[number]).astype(jnp.bfloat16)
        first = 0
        for out in outs:
            out[:, number * tile : (number + 1) * tile] = product[first : first + out.shape[0], :]
            first += out.shape[0]


def attend(place, slot_utt, frame_len, payloads, keys_values, weights, pieces, sections, widths, slots):
    count = len(payloads)
    columns, width = weights.shape
    capacity = sum(pieces) * sections * widths
    tile = 1024
    tiles = width // tile
    shapes = [
        jax.ShapeDtypeStruct((piece * widths, width), jnp.bfloat16)
        for piece in pieces
        for _ in range(2)
    ]
    return pl.pallas_call(
        functools.partial(
            attention_kernel, count, slots, capacity, pieces, sections, widths, tile
        ),
        in_specs=[SCALARS] * 3 + [INSIDE] * (count + 1) + [ANYWHERE],
        out_specs=[INSIDE] * len(shapes),
        out_shape=shapes,
        scratch_shapes=[
            pltpu.VMEM((tiles, columns, tile), jnp.bfloat16),
            pltpu.VMEM((capacity, columns), jnp.bfloat16),
            pltpu.VMEM((capacity, columns), jnp.bfloat16),
            pltpu.SemaphoreType.DMA((tiles,)),
        ],
        cost_estimate=pl.CostEstimate(
            flops=2 * capacity * columns * (width + 2 * keys_values.shape[0]),
            bytes_accessed=2 * columns * width + 2 * capacity * width,
            transcendentals=capacity * keys_values.shape[0] * columns // HD,
        ),
        compiler_params=pltpu.CompilerParams(vmem_limit_bytes=24 << 20),
        name="attention_projection",
    )(place, slot_utt, frame_len, *payloads, keys_values, in_hbm(weights))


def norm_kernel(count, slots, tokens, pieces, place_ref, slot_ref, *refs):
    payloads, blocks = refs[:count], refs[count : count + 2 * len(pieces)]
    out_ref, picked, total = refs[count + 2 * len(pieces) :]
    rows, width = total.shape
    columns = picked.shape[1]
    share = picked.shape[0] // (width // columns + 1)
    source = choice_of_payload(place_ref, slot_ref, slots)
    for choice in range(count):

        @pl.when(source == choice)
        def _(payload=payloads[choice]):
            picked[...] = payload[tokens:, :]

    first = 0
    for number, piece in enumerate(pieces):
        kept, other = blocks[2 * number : 2 * number + 2]
        total[first : first + piece, :] = kept[...] + other[...].astype(jnp.float32)
        first += piece
    for part in range(width // columns):
        take = slice(part * columns, (part + 1) * columns)
        total[:, take] += picked[part * share : part * share + rows, :].astype(jnp.float32)
    shape = out_ref.shape[:2]
    normed = square_norm(total[...]).reshape(*shape, width)
    out_ref[:, :, :width] = normed.astype(jnp.bfloat16)
    last = width // columns * share
    target = picked[last : last + rows, :LANES].astype(jnp.float32).reshape(*shape, LANES)
    out_ref[:, :, width:] = target.astype(jnp.bfloat16)


def normed_rows(place, slot_utt, payloads, blocks, pieces, tokens, slots):
    width = blocks[0].shape[1]
    rows = sum(pieces)
    columns = payloads[0].shape[1]
    return pl.pallas_call(
        functools.partial(norm_kernel, len(payloads), slots, tokens, pieces),
        in_specs=[SCALARS] * 2 + [INSIDE] * (len(payloads) + len(blocks)),
        out_specs=INSIDE,
        out_shape=jax.ShapeDtypeStruct((rows // FOLD, FOLD, width + LANES), jnp.bfloat16),
        scratch_shapes=[
            pltpu.VMEM((payloads[0].shape[0] - tokens, columns), jnp.bfloat16),
            pltpu.VMEM((rows, width), jnp.float32),
        ],
        compiler_params=pltpu.CompilerParams(vmem_limit_bytes=16 << 20),
        name="token_rows",
    )(place, slot_utt, *payloads, *blocks)


def vocabulary_kernel(tile, first_ref, *refs):
    sets, (head_ref, out_ref, rows_ref, stat) = refs[:-4], refs[-4:]
    vocab_rows, width = head_ref.shape
    share = sets[0].shape[0] * FOLD
    tokens = share * len(sets)
    cell = lax.broadcasted_iota(jnp.int32, (8, LANES), 1)
    take = jnp.where(cell == 0, 256.0, jnp.where(cell == 1, 1.0, 0.0)).astype(jnp.bfloat16)
    for number, rows in enumerate(sets):
        flat = rows[...].astype(jnp.float32).reshape(share, width + LANES)
        rows_ref[number * share : (number + 1) * share, :] = flat.astype(jnp.bfloat16)
    target = dot_nt(take, rows_ref[:, width:])[0:1, :].astype(jnp.int32) - first_ref[3]
    stat[0:1, :] = jnp.full((1, tokens), -jnp.inf, jnp.float32)
    stat[8:9, :] = jnp.zeros((1, tokens), jnp.float32)
    stat[16:17, :] = jnp.zeros((1, tokens), jnp.float32)

    @pl.loop(0, vocab_rows // tile)
    def _(step):
        start = pl.multiple_of(step * tile, tile)
        logits = dot_nt(head_ref[pl.ds(start, tile), :], rows_ref[:, :width])
        vocab = lax.broadcasted_iota(jnp.int32, logits.shape, 0) + start
        before = stat[0:1, :]
        upper = jnp.maximum(before, jnp.max(logits, axis=0, keepdims=True))
        stat[8:9, :] = stat[8:9, :] * jnp.exp(before - upper) + jnp.sum(
            jnp.exp(logits - upper), axis=0, keepdims=True
        )
        stat[16:17, :] += jnp.sum(jnp.where(vocab == target, logits, 0.0), axis=0, keepdims=True)
        stat[0:1, :] = upper

    for number in range(len(sets)):
        for row in range(3):
            out_ref[number, row : row + 1, :] = stat[
                8 * row : 8 * row + 1, number * share : (number + 1) * share
            ]


def vocabulary_stats(place, sets, head):
    share = sets[0].shape[0] * FOLD
    count = len(sets)
    width = head.shape[1]
    tokens = share * count
    return pl.pallas_call(
        functools.partial(vocabulary_kernel, head.shape[0] // 2),
        in_specs=[SCALARS] + [INSIDE] * (count + 1),
        out_specs=INSIDE,
        out_shape=jax.ShapeDtypeStruct((count, 8, share), jnp.float32),
        scratch_shapes=[
            pltpu.VMEM((tokens, width + LANES), jnp.bfloat16),
            pltpu.VMEM((24, tokens), jnp.float32),
        ],
        cost_estimate=pl.CostEstimate(
            flops=3 * tokens * head.shape[0] * width,
            bytes_accessed=2 * tokens * width,
            transcendentals=tokens * head.shape[0],
        ),
        compiler_params=pltpu.CompilerParams(vmem_limit_bytes=16 << 20),
        name="vocabulary_scores",
    )(place, *sets, pltpu.with_memory_space_constraint(head, pltpu.VMEM))


def spread_kernel(sections, groups, widths, place_ref, slot_ref, *refs):
    stats, (out_ref, table, block) = refs[:-3], refs[-3:]
    share = table.shape[2]
    first = 0
    for stat in stats:
        table[first : first + stat.shape[0]] = stat[...]
        first += stat.shape[0]
    slots = slot_ref.shape[0] // groups
    block[...] = jnp.zeros_like(block)
    for group in range(groups):
        for slot in range(slots):
            utterance = jnp.maximum(slot_ref[group * slots + slot], 0)
            for section in range(sections):
                at = (section ^ place_ref[0]) * groups + (utterance ^ place_ref[1])
                block[group, 3 * slot : 3 * slot + 3, section * share : (section + 1) * share] = (
                    table[at][0:3, :]
                )
    for section in range(sections):
        for group in range(groups):
            for width in range(widths):
                out_ref[(section * groups + group) * widths + width] = block[group]


def spread_stats(place, slot_utt, stats, sections, groups, widths):
    share = stats[0].shape[2]
    assert 3 * slot_utt.shape[0] // groups <= 8
    return pl.pallas_call(
        functools.partial(spread_kernel, sections, groups, widths),
        in_specs=[SCALARS] * 2 + [INSIDE] * len(stats),
        out_specs=INSIDE,
        out_shape=jax.ShapeDtypeStruct(
            (sections * groups * widths, 8, sections * share), jnp.float32
        ),
        scratch_shapes=[
            pltpu.VMEM((sections * groups, 8, share), jnp.float32),
            pltpu.VMEM((groups, 8, sections * share), jnp.float32),
        ],
        compiler_params=pltpu.CompilerParams(vmem_limit_bytes=16 << 20),
        name="statistics_by_group",
    )(place, slot_utt, *stats)


def score_kernel(sections, widths, place_ref, slot_ref, length_ref, every_ref, out_ref):
    slots, hyps = out_ref.shape
    lanes = every_ref.shape[2]
    share = lanes // sections // widths
    lane = lax.broadcasted_iota(jnp.int32, (1, lanes), 1)
    order = lane % share * (sections * widths) + lane // share
    column = lax.broadcasted_iota(jnp.int32, (1, hyps), 1)
    for slot in range(slots):
        upper = every_ref[:, 3 * slot, :]
        peak = jnp.max(upper, axis=0, keepdims=True)
        total = jnp.sum(
            every_ref[:, 3 * slot + 1, :] * jnp.exp(upper - peak), axis=0, keepdims=True
        )
        picked = jnp.sum(every_ref[:, 3 * slot + 2, :], axis=0, keepdims=True)
        logp = picked - (peak + jnp.log(total))
        scores = jnp.zeros((1, hyps), jnp.float32)
        start = jnp.int32(0)
        for hyp in range(hyps):
            length = length_ref[slot, hyp]
            valid = (order >= start) & (order < start + length)
            summed = jnp.sum(jnp.where(valid, logp, 0.0), axis=1, keepdims=True)
            mean = summed / jnp.full((1, 1), length, jnp.int32).astype(jnp.float32)
            scores = jnp.where(column == hyp, mean + math.log(V), scores)
            start = start + length
        filled = slot_ref[place_ref[1] * slots + slot] >= 0
        out_ref[slot : slot + 1, :] = jnp.where(filled, scores, 0.0)


def hypothesis_scores(place, slot_utt, lengths, every, slots, hyps, sections, widths):
    return pl.pallas_call(
        functools.partial(score_kernel, sections, widths),
        in_specs=[SCALARS] * 3 + [INSIDE],
        out_specs=INSIDE,
        out_shape=jax.ShapeDtypeStruct((slots, hyps), jnp.float32),
        compiler_params=pltpu.CompilerParams(vmem_limit_bytes=16 << 20),
        name="hypothesis_scores",
    )(place, slot_utt, lengths, every)


def rest(pieces, slot_tokens, place, slot_utt, frame_len, hyp_len, payloads, keys_values, o_proj, head):
    section_count = lax.axis_size("section")
    group_count = lax.axis_size("tm")
    width_count = lax.axis_size("mp")
    section_pos = lax.axis_index("section")
    width_pos = lax.axis_index("mp")
    slot_count, hyp_count = hyp_len.shape
    projected = attend(
        place,
        slot_utt,
        frame_len,
        payloads,
        keys_values,
        o_proj,
        pieces,
        section_count,
        width_count,
        slot_count,
    )

    def halve(total, came, axis, distance, side):
        if came is not None:
            total = total + came.astype(jnp.float32)
        half = total.shape[0] // 2
        kept = lax.dynamic_slice_in_dim(total, side * half, half, 0)
        sent = lax.dynamic_slice_in_dim(total, (1 - side) * half, half, 0)
        return kept, swap(sent.astype(jnp.bfloat16), axis, distance)

    low, high = width_pos % 2, width_pos // 2
    first = projected[1].astype(jnp.float32), swap(projected[0], "section", 1)
    second = projected[3].astype(jnp.float32), swap(projected[2], "mp", 1)
    first = halve(*first, "mp", 1, low)
    second = halve(*second, "mp", 2, high)
    first = halve(*first, "mp", 2, high)
    second = halve(*second, "section", 1, section_pos)
    sums = [*first, *second]
    out_rows = normed_rows(
        place, slot_utt, payloads, sums, pieces, slot_tokens, slot_count
    )

    own = jnp.zeros((width_count, *out_rows.shape), jnp.bfloat16)
    for distance in range(width_count):
        block = swap(out_rows, "mp", distance) if distance else out_rows
        own = lax.dynamic_update_index_in_dim(own, block, width_pos ^ distance, 0)
    own = own.reshape(-1, *out_rows.shape[1:])
    half = own.shape[0] // 2
    by_x = swap(own, "section", 1)
    by_y = swap(own, "tm", 2)
    stats = [vocabulary_stats(place, [own, swap(own, "tm", 1)], head)]
    by_x, by_y, stats[0] = lax.optimization_barrier((by_x, by_y, stats[0]))
    across = [swap(by_x[:half], "tm", 2), swap(by_y[half:], "section", 1)]
    stats.append(
        vocabulary_stats(place, [by_y, swap(by_y, "tm", 1), by_x, swap(by_x, "tm", 1)], head)
    )
    *across, stats[1] = lax.optimization_barrier((*across, stats[1]))
    across = jnp.concatenate(across)
    stats.append(vocabulary_stats(place, [across, swap(across, "tm", 1)], head))

    every = exchange(
        spread_stats(place, slot_utt, stats, section_count, group_count, width_count), ALL
    )
    return hypothesis_scores(
        place, slot_utt, hyp_len, every, slot_count, hyp_count, section_count, width_count
    )


def near_device(
    frame_len,
    slot_utt,
    enc_in,
    ffn_up,
    ffn_down,
    kv_proj,
    hyp_state,
    hyp_tok,
    hyp_len,
    q_proj,
    o_proj,
    head,
):
    section_count = lax.axis_size("section")
    group_count = lax.axis_size("tm")
    width_count = lax.axis_size("mp")
    section_pos = lax.axis_index("section")
    group_pos = lax.axis_index("tm")
    width_pos = lax.axis_index("mp")
    head_devices = section_count * width_count
    all_devices = head_devices * group_count

    frame_rows, utterances, enc_width = enc_in.shape
    slot_count, hyp_count, positions, model_width = hyp_state.shape
    slot_tokens = hyp_count * positions
    share_rows = slot_tokens // head_devices
    vocab_start = (
        (section_pos * group_count + group_pos) * width_count + width_pos
    ) * head.shape[0]
    head_pos = section_pos * width_count + width_pos
    place = jnp.stack([section_pos, group_pos, width_pos, vocab_start, head_pos])
    place = place.astype(jnp.int32)

    parts, own_frames = ffn(place, enc_in, ffn_up, ffn_down, width_count)
    parts = exchange(parts, "mp")

    blocks = queries_of(
        place,
        slot_utt,
        hyp_len,
        place,
        hyp_state.reshape(slot_count, slot_tokens, model_width),
        hyp_tok.reshape(slot_count, 1, slot_tokens),
        q_proj,
        group_count,
        share_rows,
    )
    crossing = blocks[2] + swap(blocks[3], "tm", 1)
    payloads = [blocks[0], swap(blocks[1], "tm", 1), swap(crossing, "tm", 2)]

    sent = keys_values_of(
        parts, own_frames, kv_proj, blocks[0], section_count, utterances, width_count
    )
    frames_all = all_devices * (frame_rows // width_count)
    keys_values = exchange(sent.reshape(all_devices, -1, 2 * HD), ALL).reshape(frames_all, 2 * HD)

    here_slots = lax.dynamic_slice_in_dim(slot_utt, group_pos * slot_count, slot_count, 0)
    filled = jnp.where(here_slots >= 0, jnp.sum(hyp_len, axis=1), 0)
    most = jnp.max(filled).reshape(1)
    for distance in (1, 2):
        most = jnp.maximum(most, swap(most, "tm", distance))
    operands = (place, slot_utt, frame_len, hyp_len, payloads, keys_values, o_proj, head)
    few = share_rows * 3 // 4
    return lax.cond(
        most[0] <= few * head_devices,
        functools.partial(rest, (few - few // 3, few // 3), slot_tokens),
        functools.partial(rest, (share_rows // 2, share_rows - share_rows // 2), slot_tokens),
        *operands,
    )


def general(
    frame_len,
    slot_utt,
    enc_in,
    ffn_up,
    ffn_down,
    kv_proj,
    hyp_state,
    hyp_tok,
    hyp_len,
    q_proj,
    o_proj,
    head,
):
    section_count = lax.axis_size("section")
    group_count = lax.axis_size("tm")
    width_count = lax.axis_size("mp")
    section_pos = lax.axis_index("section")
    group_pos = lax.axis_index("tm")
    width_pos = lax.axis_index("mp")
    head_devices = section_count * width_count
    head_pos = section_pos * width_count + width_pos
    all_devices = head_devices * group_count

    frame_rows, utterances, enc_width = enc_in.shape
    assert utterances == group_count
    slot_count, hyp_count, positions, model_width = hyp_state.shape
    slot_tokens = hyp_count * positions
    device_heads = q_proj.shape[1] // HD
    group_heads = NH // KVH
    frame_share = frame_rows // width_count
    share_rows = slot_tokens // head_devices
    here_slots = lax.dynamic_slice_in_dim(slot_utt, group_pos * slot_count, slot_count, 0)

    dec_rows = hyp_state.reshape(slot_count * slot_tokens, model_width).astype(jnp.float32)
    queries = jnp.dot(
        square_norm(dec_rows).astype(jnp.bfloat16), q_proj, preferred_element_type=jnp.float32
    ).astype(jnp.bfloat16)
    queries = queries.reshape(slot_count, slot_tokens, device_heads * HD)
    shares = lax.dynamic_slice_in_dim(
        hyp_state.reshape(slot_count, slot_tokens, model_width), head_pos * share_rows, share_rows, 1
    )

    def by_utterance(values):
        out = []
        for utterance in range(utterances):
            block = values[0]
            for slot in range(1, slot_count):
                block = jnp.where(here_slots[slot] == utterance, values[slot], block)
            out.append(block)
        return jnp.stack(out)

    own_slot = jnp.argmax(slot_utt == group_pos)
    from_group = own_slot // slot_count
    queries = lax.dynamic_index_in_dim(
        exchange(by_utterance(queries), "tm"), from_group, 0, keepdims=False
    )
    resid_rows = lax.dynamic_index_in_dim(
        exchange(by_utterance(shares), "tm"), from_group, 0, keepdims=False
    )
    slot_targets = lax.all_gather(
        hyp_tok.reshape(slot_count, slot_tokens), "tm", axis=0, tiled=True
    )
    utt_slots = jnp.argmax(slot_utt[None, :] == jnp.arange(utterances)[:, None], axis=1)
    targets = jnp.take(slot_targets, utt_slots, axis=0).reshape(utterances * slot_tokens)

    enc_flat = (
        enc_in.reshape(width_count, frame_share, utterances, enc_width)
        .transpose(0, 2, 1, 3)
        .reshape(frame_rows * utterances, enc_width)
    )
    share_count = frame_share * utterances
    enc_normed = layer_norm(enc_flat.astype(jnp.float32)).astype(jnp.bfloat16)
    enc_inner = jax.nn.gelu(
        jnp.dot(enc_normed, ffn_up, preferred_element_type=jnp.float32), approximate=False
    ).astype(jnp.bfloat16)
    enc_summed = scatter_sum(
        jnp.dot(enc_inner, ffn_down, preferred_element_type=jnp.float32).astype(jnp.bfloat16),
        "mp",
        width_count,
    )
    own_frames = lax.dynamic_slice_in_dim(enc_flat, width_pos * share_count, share_count, 0)
    enc_states = layer_norm(own_frames.astype(jnp.float32) + enc_summed).astype(jnp.bfloat16)
    keys_values = jnp.dot(enc_states, kv_proj, preferred_element_type=jnp.float32).astype(
        jnp.bfloat16
    )
    keys_values = keys_values.reshape(utterances, frame_share, 2, KVH, HD)
    sent = []
    for section in range(section_count):
        per_width = []
        for width in range(width_count):
            kv_head = (section * width_count + width) * device_heads // group_heads
            per_width.append(
                keys_values[:, :, :, kv_head].reshape(utterances, frame_share, 2 * HD)
            )
        sent.append(jnp.stack(per_width, axis=1))
    sent = jnp.stack(sent).reshape(all_devices, frame_share, 2 * HD)
    frames_all = all_devices * frame_share
    keys_values = exchange(sent, ALL).reshape(frames_all, 2 * HD)

    frame_limit = lax.dynamic_index_in_dim(frame_len, group_pos, 0, keepdims=False)
    queries = queries.reshape(slot_tokens, device_heads, HD)
    scores = jnp.einsum(
        "qhd,fd->hqf", queries, keys_values[:, :HD], preferred_element_type=jnp.float32
    ) / math.sqrt(HD)
    visible = jnp.arange(frames_all, dtype=jnp.int32) < frame_limit
    scores = jnp.where(visible[None, None, :], scores, -jnp.inf)
    weights = jax.nn.softmax(scores, axis=-1).astype(jnp.bfloat16)
    context = jnp.einsum(
        "hqf,fd->qhd", weights, keys_values[:, HD:], preferred_element_type=jnp.float32
    ).astype(jnp.bfloat16)
    partial = jnp.dot(
        context.reshape(slot_tokens, device_heads * HD), o_proj, preferred_element_type=jnp.float32
    ).astype(jnp.bfloat16)
    partial = scatter_sum(partial, "section", section_count).astype(jnp.bfloat16)
    attn_out = scatter_sum(partial, "mp", width_count)
    out_normed = square_norm(resid_rows.astype(jnp.float32) + attn_out).astype(jnp.bfloat16)

    hidden_rows = lax.all_gather(out_normed, ALL, axis=0, tiled=True)
    logits = lax.dot_general(
        hidden_rows, head, (((1,), (1,)), ((), ())), preferred_element_type=jnp.float32
    )
    vocab_rows = head.shape[0]
    vocab_start = (
        (section_pos * group_count + group_pos) * width_count + width_pos
    ) * vocab_rows
    target_rows = (
        targets.reshape(utterances, section_count, width_count, share_rows)
        .transpose(1, 0, 2, 3)
        .reshape(-1)
    )
    upper = jnp.max(logits, axis=1)
    totals = jnp.sum(jnp.exp(logits - upper[:, None]), axis=1)
    matches = (
        jnp.arange(vocab_rows, dtype=jnp.int32)[None, :] == (target_rows - vocab_start)[:, None]
    )
    target_logit = jnp.sum(jnp.where(matches, logits, 0.0), axis=1)

    stats = jnp.stack([upper, totals, target_logit])
    stats = stats.reshape(3, section_count, utterances, width_count, share_rows)
    stats = stats.transpose(2, 0, 1, 3, 4).reshape(utterances, 3, slot_tokens)
    by_slot = jnp.take(stats, jnp.maximum(slot_utt, 0), axis=0)
    by_group = by_slot.reshape(1, group_count, 1, slot_count, 3, slot_tokens)
    by_group = jnp.broadcast_to(
        by_group, (section_count, group_count, width_count, slot_count, 3, slot_tokens)
    ).reshape(all_devices, slot_count, 3, slot_tokens)
    every = exchange(by_group, ALL)
    peak = jnp.max(every[:, :, 0], axis=0)
    total = jnp.sum(every[:, :, 1] * jnp.exp(every[:, :, 0] - peak[None]), axis=0)
    picked = jnp.sum(every[:, :, 2], axis=0)
    token_logp = (picked - (peak + jnp.log(total))).reshape(slot_count, hyp_count, positions)
    valid = jnp.arange(positions, dtype=jnp.int32)[None, None, :] < hyp_len[:, :, None]
    summed = jnp.sum(jnp.where(valid, token_logp, 0.0), axis=-1) / hyp_len.astype(
        jnp.float32
    ) + math.log(V)
    return jnp.where(here_slots[:, None] >= 0, summed, 0.0)


def solution(mesh):
    in_specs = (
        P(),
        P(),
        P(("section", "tm"), None, None),
        P(None, "mp"),
        P("mp", None),
        P(),
        P("tm", None, None, None),
        P("tm", None, None),
        P("tm", None),
        P(None, ("section", "mp")),
        P(("section", "mp"), None),
        P(("section", "tm", "mp"), None),
    )
    out_specs = P("tm", None)
    near = dict(mesh.shape) == {"section": 2, "tm": 4, "mp": 4}
    per_device = near_device if near else general
    return jax.shard_map(
        per_device, mesh=mesh, in_specs=in_specs, out_specs=out_specs, check_vma=False
    )
```

```python
import functools
import math

import jax
import jax.numpy as jnp
from jax import lax
from jax.experimental import pallas as pl
from jax.experimental.pallas import tpu as pltpu
from jax.sharding import PartitionSpec as P

NH = 32
KVH = 4
HD = 128
V = 64000
ALL = ("section", "tm", "mp")
LANES = 128
FOLD = 4


def layer_norm(values):
    center = values - jnp.mean(values, axis=-1, keepdims=True)
    spread = jnp.mean(center * center, axis=-1, keepdims=True)
    return center * lax.rsqrt(spread + 1e-05)


def square_norm(values):
    return values * lax.rsqrt(jnp.mean(values * values, axis=-1, keepdims=True) + 1e-06)


def exchange(blocks, axis):
    return lax.all_to_all(blocks, axis, split_axis=0, concat_axis=0, tiled=True)


def scatter_sum(partial, axis, count):
    blocks = partial.reshape((count, partial.shape[0] // count) + partial.shape[1:])
    return jnp.sum(exchange(blocks, axis).astype(jnp.float32), axis=0)


def swap(values, axis, distance):
    pairs = [(i, i ^ distance) for i in range(lax.axis_size(axis))]
    return lax.ppermute(values, axis, pairs)


def whole(shape):
    return pl.BlockSpec(shape, lambda *_: (0,) * len(shape))


SCALARS = pl.BlockSpec(memory_space=pltpu.SMEM)


def dot(left, right):
    return jnp.dot(left, right, preferred_element_type=jnp.float32)


def dot_nt(left, right):
    return lax.dot_general(
        left, right, (((1,), (1,)), ((), ())), preferred_element_type=jnp.float32
    )


def start_copies(source_of, target_of, semaphores, count):
    copies = []
    for number in range(count):
        copy = pltpu.make_async_copy(
            source_of(number), target_of(number), semaphores.at[number]
        )
        copy.start()
        copies.append(copy)
    return copies


def ffn_kernel(tile, place_ref, x_ref, up_ref, down_ref, *refs):
    out_ref, own_ref, rows, total, up, down, up_sem, down_sem = refs
    count, share, width = out_ref.shape
    tiles = up_ref.shape[1] // tile
    up_copies = start_copies(
        lambda i: up_ref.at[:, pl.ds(i * tile, tile)], lambda i: up.at[i], up_sem, tiles
    )
    down_copies = start_copies(
        lambda i: down_ref.at[pl.ds(i * tile, tile), :], lambda i: down.at[i], down_sem, tiles
    )
    rows[...] = x_ref[...].astype(jnp.float32).reshape(rows.shape)
    start = pl.multiple_of(place_ref[2] * share, share)
    own_ref[...] = rows[pl.ds(start, share), :].astype(jnp.bfloat16)
    normed = layer_norm(rows[...]).astype(jnp.bfloat16)
    for number in range(tiles):
        up_copies[number].wait()
        hidden = dot(normed, up[number])
        inner = 0.5 * hidden * (1.0 + lax.erf(hidden * math.sqrt(0.5)))
        down_copies[number].wait()
        product = dot(inner.astype(jnp.bfloat16), down[number])
        if number == 0:
            total[...] = product
        else:
            total[...] += product
    for part in range(count):
        out_ref[part] = total[part * share : (part + 1) * share, :].astype(jnp.bfloat16)


def in_hbm(values):
    return pltpu.with_memory_space_constraint(values, pltpu.HBM)


ANYWHERE = pl.BlockSpec(memory_space=pl.ANY)
INSIDE = pl.BlockSpec(memory_space=pltpu.VMEM)


def ffn(place, enc_in, up, down, count):
    frames, utterances, width = enc_in.shape
    rows = frames * utterances
    share = rows // count
    tile = 256
    tiles = up.shape[1] // tile
    return pl.pallas_call(
        functools.partial(ffn_kernel, tile),
        in_specs=[SCALARS, INSIDE, ANYWHERE, ANYWHERE],
        out_specs=[INSIDE] * 2,
        out_shape=[
            jax.ShapeDtypeStruct((count, share, width), jnp.bfloat16),
            jax.ShapeDtypeStruct((share, width), jnp.bfloat16),
        ],
        scratch_shapes=[
            pltpu.VMEM((rows, width), jnp.float32),
            pltpu.VMEM((rows, width), jnp.float32),
            pltpu.VMEM((tiles, width, tile), jnp.bfloat16),
            pltpu.VMEM((tiles, tile, width), jnp.bfloat16),
            pltpu.SemaphoreType.DMA((tiles,)),
            pltpu.SemaphoreType.DMA((tiles,)),
        ],
        cost_estimate=pl.CostEstimate(
            flops=4 * rows * width * up.shape[1],
            bytes_accessed=4 * width * up.shape[1],
            transcendentals=rows * up.shape[1],
        ),
        compiler_params=pltpu.CompilerParams(vmem_limit_bytes=24 << 20),
        name="encoder_ffn",
    )(place, enc_in, in_hbm(up), in_hbm(down))


def query_kernel(
    count, depth, place_ref, slot_ref, length_ref, after_ref, x_ref, tok_ref, w_ref, *refs
):
    outs, (states, weights, normed, total, shares, x_sem, w_sem) = refs[:count], refs[count:]
    slots, tokens, width = x_ref.shape
    hyps = length_ref.shape[1]
    positions = tokens // hyps
    columns = w_ref.shape[1]
    share = shares.shape[1] // 2
    parts = width // columns
    x_copies = start_copies(lambda i: x_ref.at[i], lambda i: states.at[i], x_sem, slots)
    w_copies = start_copies(
        lambda i: w_ref.at[pl.ds(i * depth, depth), :],
        lambda i: weights.at[i],
        w_sem,
        width // depth,
    )
    head_pos = place_ref[4]
    lane = lax.broadcasted_iota(jnp.int32, (1, tokens), 1)
    for slot in range(slots):
        order = jnp.full((1, tokens), -1, jnp.int32)
        start = jnp.int32(0)
        for hyp in range(hyps):
            length = length_ref[slot, hyp]
            inside = (lane >= hyp * positions) & (lane < hyp * positions + length)
            order = jnp.where(inside, lane - hyp * positions + start, order)
            start = start + length
        row = lax.broadcasted_iota(jnp.int32, (tokens, tokens), 0)
        move = jnp.where(order == row, 1.0, 0.0).astype(jnp.bfloat16)
        x_copies[slot].wait()
        ordered = dot(move, states[slot])
        normed[slot * tokens : (slot + 1) * tokens, :] = square_norm(ordered).astype(jnp.bfloat16)
        share_row = lax.broadcasted_iota(jnp.int32, (share, tokens), 0)
        chosen = order == share_row * (tokens // share) + head_pos
        mine = dot(jnp.where(chosen, 1.0, 0.0).astype(jnp.bfloat16), states[slot])
        shares[slot, :share, :] = mine.astype(jnp.bfloat16)
        target = jnp.sum(
            jnp.where(chosen, tok_ref[slot], 0), axis=1, keepdims=True, dtype=jnp.int32
        )
        coarse = target // 256
        cell = lax.broadcasted_iota(jnp.int32, (share, columns), 1)
        packed = jnp.where(cell == 0, coarse, jnp.where(cell == 1, target - coarse * 256, 0))
        shares[slot, share:, :columns] = packed.astype(jnp.float32).astype(jnp.bfloat16)
    for number in range(width // depth):
        w_copies[number].wait()
        product = dot(normed[:, number * depth : (number + 1) * depth], weights[number])
        if number == 0:
            total[...] = product
        else:
            total[...] += product
    group = place_ref[1]
    for distance in range(count):
        slot = jnp.int32(-1)
        for candidate in range(slots):
            holds = slot_ref[group * slots + candidate] == group ^ distance
            slot = jnp.where(holds, candidate, slot)
        out = outs[distance]

        @pl.when(slot < 0)
        def _(out=out):
            out[...] = jnp.zeros_like(out)

        @pl.when(slot >= 0)
        def _(out=out, slot=slot):
            start = pl.multiple_of(slot * tokens, tokens)
            out[:tokens, :] = total[pl.ds(start, tokens), :].astype(jnp.bfloat16)
            for part in range(parts):
                first = tokens + part * share
                out[first : first + share, :] = shares[
                    slot, :share, part * columns : (part + 1) * columns
                ]
            out[tokens + parts * share :, :] = shares[slot, share:, :columns]


def queries_of(place, slot_utt, lengths, after, states, targets, weights, count, share):
    slots, tokens, width = states.shape
    columns = weights.shape[1]
    depth = 1024
    rows = tokens + (width // columns + 1) * share
    block = jax.ShapeDtypeStruct((rows, columns), jnp.bfloat16)
    return pl.pallas_call(
        functools.partial(query_kernel, count, depth),
        in_specs=[SCALARS] * 3 + [ANYWHERE, ANYWHERE, INSIDE, ANYWHERE],
        out_specs=[INSIDE] * count,
        out_shape=[block] * count,
        scratch_shapes=[
            pltpu.VMEM(states.shape, jnp.bfloat16),
            pltpu.VMEM((width // depth, depth, columns), jnp.bfloat16),
            pltpu.VMEM((slots * tokens, width), jnp.bfloat16),
            pltpu.VMEM((slots * tokens, columns), jnp.float32),
            pltpu.VMEM((slots, 2 * share, width), jnp.bfloat16),
            pltpu.SemaphoreType.DMA((slots,)),
            pltpu.SemaphoreType.DMA((width // depth,)),
        ],
        cost_estimate=pl.CostEstimate(
            flops=2 * slots * tokens * width * columns,
            bytes_accessed=2 * width * (columns + slots * tokens),
            transcendentals=0,
        ),
        compiler_params=pltpu.CompilerParams(vmem_limit_bytes=32 << 20),
        name="hypothesis_queries",
    )(place, slot_utt, lengths, after, in_hbm(states), targets, in_hbm(weights))


def kv_kernel(sections, utterances, widths, *refs):
    parts_ref, own_ref, w_ref, after_ref, out_ref = refs
    rows = own_ref.shape[0]
    frames = rows // utterances
    total = own_ref[...].astype(jnp.float32)
    summed = parts_ref[0].astype(jnp.float32)
    for part in range(1, parts_ref.shape[0]):
        summed += parts_ref[part].astype(jnp.float32)
    states = layer_norm(total + summed).astype(jnp.bfloat16)
    to = lax.broadcasted_iota(jnp.int32, (rows, rows), 0)
    come = lax.broadcasted_iota(jnp.int32, (rows, rows), 1)
    move = jnp.where(come == to % frames * utterances + to // frames, 1.0, 0.0)
    states = dot(move.astype(jnp.bfloat16), states).astype(jnp.bfloat16)
    both = dot(states, w_ref[...])
    half = KVH * HD
    per_kv = sections * widths // KVH
    for section in range(sections):
        for utterance in range(utterances):
            for width in range(0, widths, per_kv):
                kv_head = (section * widths + width) // per_kv
                take = slice(utterance * frames, (utterance + 1) * frames)
                block = jnp.concatenate(
                    [
                        both[take, kv_head * HD : (kv_head + 1) * HD],
                        both[take, half + kv_head * HD : half + (kv_head + 1) * HD],
                    ],
                    axis=1,
                )
                start = ((section * utterances + utterance) * widths + width) * frames
                block = jnp.concatenate([block] * per_kv, axis=0).astype(jnp.bfloat16)
                out_ref[start : start + per_kv * frames, :] = block


def keys_values_of(parts, own, weights, after, sections, utterances, widths):
    rows = sections * widths * own.shape[0]
    return pl.pallas_call(
        functools.partial(kv_kernel, sections, utterances, widths),
        in_specs=[INSIDE] * 3 + [ANYWHERE],
        out_specs=INSIDE,
        out_shape=jax.ShapeDtypeStruct((rows, 2 * HD), jnp.bfloat16),
        cost_estimate=pl.CostEstimate(
            flops=2 * own.shape[0] * weights.shape[0] * weights.shape[1],
            bytes_accessed=2 * weights.shape[0] * weights.shape[1],
            transcendentals=0,
        ),
        compiler_params=pltpu.CompilerParams(vmem_limit_bytes=24 << 20),
        name="frame_keys_values",
    )(parts, own, weights, after)


def choice_of_payload(place_ref, slot_ref, slots):
    group = place_ref[1]
    source = jnp.int32(0)
    for slot in range(slot_ref.shape[0]):
        source = jnp.where(slot_ref[slot] == group, slot // slots, source)
    return jnp.minimum(source ^ group, 2)


def attention_kernel(count, slots, capacity, pieces, sections, widths, tile, *refs):
    place_ref, slot_ref, frame_ref = refs[:3]
    payloads, (kv_ref, w_ref) = refs[3 : 3 + count], refs[3 + count : 5 + count]
    outs = refs[5 + count : 5 + count + 2 * len(pieces)]
    weights, picked, context, w_sem = refs[5 + count + 2 * len(pieces) :]
    tokens, columns = capacity, w_ref.shape[0]
    tiles = w_ref.shape[1] // tile
    w_copies = start_copies(
        lambda i: w_ref.at[:, pl.ds(i * tile, tile)], lambda i: weights.at[i], w_sem, tiles
    )
    source = choice_of_payload(place_ref, slot_ref, slots)
    section_pos = place_ref[0]
    frame_limit = frame_ref[place_ref[1]]
    for distance in range(count):

        @pl.when(source == distance)
        def _(payload=payloads[distance]):
            picked[...] = payload[:tokens, :]

    keys = kv_ref[:, :HD]
    values = kv_ref[:, HD:]
    frames = kv_ref.shape[0]
    visible = lax.broadcasted_iota(jnp.int32, (tokens, frames), 1) < frame_limit
    for head in range(columns // HD):
        scores = dot_nt(picked[:, head * HD : (head + 1) * HD], keys) * (1.0 / math.sqrt(HD))
        scores = jnp.where(visible, scores, -jnp.inf)
        raised = jnp.exp(scores - jnp.max(scores, axis=1, keepdims=True))
        chances = (raised / jnp.sum(raised, axis=1, keepdims=True)).astype(jnp.bfloat16)
        context[:, head * HD : (head + 1) * HD] = dot(chances, values).astype(jnp.bfloat16)
    to = lax.broadcasted_iota(jnp.int32, (tokens, tokens), 0)
    come = lax.broadcasted_iota(jnp.int32, (tokens, tokens), 1)
    low_bit = place_ref[2] % 2
    size = widths * pieces[0]
    block = to % size // pieces[0]
    section = jnp.where(to < size, 1 - section_pos, section_pos)
    first_order = (to % pieces[0] * sections + section) * widths + block % 2 * 2 + block // 2
    at = to - 2 * size
    size = widths * pieces[1]
    block = at % size // pieces[1]
    low = jnp.where(at < size, 1 - low_bit, low_bit)
    row = pieces[0] + at % pieces[1]
    second_order = (row * sections + block // 2) * widths + block % 2 * 2 + low
    move = come == jnp.where(at < 0, first_order, second_order)
    ordered = dot(jnp.where(move, 1.0, 0.0).astype(jnp.bfloat16), context[...])
    ordered = ordered.astype(jnp.bfloat16)
    for number in range(tiles):
        w_copies[number].wait()
        product = dot(ordered, weights[number]).astype(jnp.bfloat16)
        first = 0
        for out in outs:
            out[:, number * tile : (number + 1) * tile] = product[first : first + out.shape[0], :]
            first += out.shape[0]


def attend(place, slot_utt, frame_len, payloads, keys_values, weights, pieces, sections, widths, slots):
    count = len(payloads)
    columns, width = weights.shape
    capacity = sum(pieces) * sections * widths
    tile = 1024
    tiles = width // tile
    shapes = [
        jax.ShapeDtypeStruct((piece * widths, width), jnp.bfloat16)
        for piece in pieces
        for _ in range(2)
    ]
    return pl.pallas_call(
        functools.partial(
            attention_kernel, count, slots, capacity, pieces, sections, widths, tile
        ),
        in_specs=[SCALARS] * 3 + [INSIDE] * (count + 1) + [ANYWHERE],
        out_specs=[INSIDE] * len(shapes),
        out_shape=shapes,
        scratch_shapes=[
            pltpu.VMEM((tiles, columns, tile), jnp.bfloat16),
            pltpu.VMEM((capacity, columns), jnp.bfloat16),
            pltpu.VMEM((capacity, columns), jnp.bfloat16),
            pltpu.SemaphoreType.DMA((tiles,)),
        ],
        cost_estimate=pl.CostEstimate(
            flops=2 * capacity * columns * (width + 2 * keys_values.shape[0]),
            bytes_accessed=2 * columns * width + 2 * capacity * width,
            transcendentals=capacity * keys_values.shape[0] * columns // HD,
        ),
        compiler_params=pltpu.CompilerParams(vmem_limit_bytes=24 << 20),
        name="attention_projection",
    )(place, slot_utt, frame_len, *payloads, keys_values, in_hbm(weights))


def fold_kernel(sides, joined, place_ref, *refs):
    count = len(sides)
    parts, outs = refs[: 2 * count], refs[2 * count :]
    first = 0
    for number, side in enumerate(sides):
        kept_ref, came_ref = parts[2 * number : 2 * number + 2]
        total = kept_ref[...].astype(jnp.float32) + came_ref[...].astype(jnp.float32)
        half = total.shape[0] // 2
        top, bottom = total[:half], total[half:]
        upper = side(place_ref) == 0
        kept = jnp.where(upper, top, bottom)
        sent = jnp.where(upper, bottom, top).astype(jnp.bfloat16)
        if joined:
            outs[0][first : first + half, :] = kept
            outs[1][first : first + half, :] = sent
            first += half
        else:
            outs[2 * number][...] = kept
            outs[2 * number + 1][...] = sent


def fold(place, parts, sides, joined):
    width = parts[0].shape[1]
    halves = [part.shape[0] // 2 for part in parts[::2]]
    if joined:
        halves = [sum(halves)]
    shapes = [
        jax.ShapeDtypeStruct((half, width), kind)
        for half in halves
        for kind in (jnp.float32, jnp.bfloat16)
    ]
    return pl.pallas_call(
        functools.partial(fold_kernel, sides, joined),
        in_specs=[SCALARS] + [INSIDE] * len(parts),
        out_specs=[INSIDE] * len(shapes),
        out_shape=shapes,
        compiler_params=pltpu.CompilerParams(vmem_limit_bytes=24 << 20),
        name="sum_phase",
    )(place, *parts)


def section_side(place_ref):
    return place_ref[0]


def low_side(place_ref):
    return place_ref[2] % 2


def high_side(place_ref):
    return place_ref[2] // 2


def norm_kernel(count, slots, tokens, place_ref, slot_ref, *refs):
    payloads, (kept, other) = refs[:count], refs[count : count + 2]
    out_ref, picked, total = refs[count + 2 :]
    rows, width = total.shape
    columns = picked.shape[1]
    share = picked.shape[0] // (width // columns + 1)
    source = choice_of_payload(place_ref, slot_ref, slots)
    for choice in range(count):

        @pl.when(source == choice)
        def _(payload=payloads[choice]):
            picked[...] = payload[tokens:, :]

    total[...] = kept[...] + other[...].astype(jnp.float32)
    for part in range(width // columns):
        take = slice(part * columns, (part + 1) * columns)
        total[:, take] += picked[part * share : part * share + rows, :].astype(jnp.float32)
    shape = out_ref.shape[:2]
    normed = square_norm(total[...]).reshape(*shape, width)
    out_ref[:, :, :width] = normed.astype(jnp.bfloat16)
    last = width // columns * share
    target = picked[last : last + rows, :LANES].astype(jnp.float32).reshape(*shape, LANES)
    out_ref[:, :, width:] = target.astype(jnp.bfloat16)


def normed_rows(place, slot_utt, payloads, blocks, tokens, slots):
    width = blocks[0].shape[1]
    rows = blocks[0].shape[0]
    columns = payloads[0].shape[1]
    return pl.pallas_call(
        functools.partial(norm_kernel, len(payloads), slots, tokens),
        in_specs=[SCALARS] * 2 + [INSIDE] * (len(payloads) + len(blocks)),
        out_specs=INSIDE,
        out_shape=jax.ShapeDtypeStruct((rows // FOLD, FOLD, width + LANES), jnp.bfloat16),
        scratch_shapes=[
            pltpu.VMEM((payloads[0].shape[0] - tokens, columns), jnp.bfloat16),
            pltpu.VMEM((rows, width), jnp.float32),
        ],
        compiler_params=pltpu.CompilerParams(vmem_limit_bytes=16 << 20),
        name="token_rows",
    )(place, slot_utt, *payloads, *blocks)


def vocabulary_kernel(tile, count, first_ref, *refs):
    sets, head_ref, out_ref = refs[:count], refs[count], refs[count + 1]
    loaded_ref, semaphores = (refs[count + 2], refs[-1]) if len(refs) > count + 4 else (None, None)
    rows_ref, stat = refs[-3:-1] if loaded_ref is not None else refs[-2:]
    vocab_rows, width = head_ref.shape
    share = sets[0].shape[0] * FOLD
    tokens = share * len(sets)
    tiles = vocab_rows // tile
    if loaded_ref is not None:
        copies = start_copies(
            lambda i: head_ref.at[pl.ds(i * tile, tile), :],
            lambda i: loaded_ref.at[pl.ds(i * tile, tile), :],
            semaphores,
            tiles,
        )
    cell = lax.broadcasted_iota(jnp.int32, (8, LANES), 1)
    take = jnp.where(cell == 0, 256.0, jnp.where(cell == 1, 1.0, 0.0)).astype(jnp.bfloat16)
    for number, rows in enumerate(sets):
        flat = rows[...].astype(jnp.float32).reshape(share, width + LANES)
        rows_ref[number * share : (number + 1) * share, :] = flat.astype(jnp.bfloat16)
    target = dot_nt(take, rows_ref[:, width:])[0:1, :].astype(jnp.int32) - first_ref[3]
    stat[0:1, :] = jnp.full((1, tokens), -jnp.inf, jnp.float32)
    stat[8:9, :] = jnp.zeros((1, tokens), jnp.float32)
    stat[16:17, :] = jnp.zeros((1, tokens), jnp.float32)

    def one_tile(start, block):
        logits = dot_nt(block, rows_ref[:, :width])
        vocab = lax.broadcasted_iota(jnp.int32, logits.shape, 0) + start
        before = stat[0:1, :]
        upper = jnp.maximum(before, jnp.max(logits, axis=0, keepdims=True))
        stat[8:9, :] = stat[8:9, :] * jnp.exp(before - upper) + jnp.sum(
            jnp.exp(logits - upper), axis=0, keepdims=True
        )
        stat[16:17, :] += jnp.sum(jnp.where(vocab == target, logits, 0.0), axis=0, keepdims=True)
        stat[0:1, :] = upper

    if loaded_ref is not None:
        for number in range(tiles):
            copies[number].wait()
            one_tile(number * tile, loaded_ref[number * tile : (number + 1) * tile, :])
    else:

        @pl.loop(0, tiles)
        def _(step):
            start = pl.multiple_of(step * tile, tile)
            one_tile(start, head_ref[pl.ds(start, tile), :])

    for number in range(len(sets)):
        for row in range(3):
            out_ref[number, row : row + 1, :] = stat[
                8 * row : 8 * row + 1, number * share : (number + 1) * share
            ]


def vocabulary_stats(place, sets, head, load=False):
    share = sets[0].shape[0] * FOLD
    count = len(sets)
    width = head.shape[1]
    tokens = share * count
    tile = head.shape[0] // (5 if load else 2)
    stats = jax.ShapeDtypeStruct((count, 8, share), jnp.float32)
    return pl.pallas_call(
        functools.partial(vocabulary_kernel, tile, count),
        in_specs=[SCALARS] + [INSIDE] * count + [ANYWHERE if load else INSIDE],
        out_specs=[INSIDE] * 2 if load else INSIDE,
        out_shape=[stats, pltpu.VMEM(head.shape, head.dtype)] if load else stats,
        scratch_shapes=[
            pltpu.VMEM((tokens, width + LANES), jnp.bfloat16),
            pltpu.VMEM((24, tokens), jnp.float32),
        ]
        + ([pltpu.SemaphoreType.DMA((5,))] if load else []),
        cost_estimate=pl.CostEstimate(
            flops=3 * tokens * head.shape[0] * width,
            bytes_accessed=2 * tokens * width,
            transcendentals=tokens * head.shape[0],
        ),
        compiler_params=pltpu.CompilerParams(vmem_limit_bytes=(36 if load else 16) << 20),
        name="vocabulary_scores",
    )(
        place,
        *sets,
        in_hbm(head) if load else pltpu.with_memory_space_constraint(head, pltpu.VMEM),
    )


def spread_kernel(sections, groups, widths, place_ref, slot_ref, *refs):
    stats, (out_ref, table, block) = refs[:-3], refs[-3:]
    share = table.shape[2]
    first = 0
    for stat in stats:
        table[first : first + stat.shape[0]] = stat[...]
        first += stat.shape[0]
    slots = slot_ref.shape[0] // groups
    block[...] = jnp.zeros_like(block)
    for group in range(groups):
        for slot in range(slots):
            utterance = jnp.maximum(slot_ref[group * slots + slot], 0)
            for section in range(sections):
                at = (section ^ place_ref[0]) * groups + (utterance ^ place_ref[1])
                block[group, 3 * slot : 3 * slot + 3, section * share : (section + 1) * share] = (
                    table[at][0:3, :]
                )
    for section in range(sections):
        for group in range(groups):
            for width in range(widths):
                out_ref[(section * groups + group) * widths + width] = block[group]


def spread_stats(place, slot_utt, stats, sections, groups, widths):
    share = stats[0].shape[2]
    assert 3 * slot_utt.shape[0] // groups <= 8
    return pl.pallas_call(
        functools.partial(spread_kernel, sections, groups, widths),
        in_specs=[SCALARS] * 2 + [INSIDE] * len(stats),
        out_specs=INSIDE,
        out_shape=jax.ShapeDtypeStruct(
            (sections * groups * widths, 8, sections * share), jnp.float32
        ),
        scratch_shapes=[
            pltpu.VMEM((sections * groups, 8, share), jnp.float32),
            pltpu.VMEM((groups, 8, sections * share), jnp.float32),
        ],
        compiler_params=pltpu.CompilerParams(vmem_limit_bytes=16 << 20),
        name="statistics_by_group",
    )(place, slot_utt, *stats)


def score_kernel(sections, widths, place_ref, slot_ref, length_ref, every_ref, out_ref):
    slots, hyps = out_ref.shape
    lanes = every_ref.shape[2]
    share = lanes // sections // widths
    lane = lax.broadcasted_iota(jnp.int32, (1, lanes), 1)
    order = lane % share * (sections * widths) + lane // share
    column = lax.broadcasted_iota(jnp.int32, (1, hyps), 1)
    for slot in range(slots):
        upper = every_ref[:, 3 * slot, :]
        peak = jnp.max(upper, axis=0, keepdims=True)
        total = jnp.sum(
            every_ref[:, 3 * slot + 1, :] * jnp.exp(upper - peak), axis=0, keepdims=True
        )
        picked = jnp.sum(every_ref[:, 3 * slot + 2, :], axis=0, keepdims=True)
        logp = picked - (peak + jnp.log(total))
        scores = jnp.zeros((1, hyps), jnp.float32)
        start = jnp.int32(0)
        for hyp in range(hyps):
            length = length_ref[slot, hyp]
            valid = (order >= start) & (order < start + length)
            summed = jnp.sum(jnp.where(valid, logp, 0.0), axis=1, keepdims=True)
            mean = summed / jnp.full((1, 1), length, jnp.int32).astype(jnp.float32)
            scores = jnp.where(column == hyp, mean + math.log(V), scores)
            start = start + length
        filled = slot_ref[place_ref[1] * slots + slot] >= 0
        out_ref[slot : slot + 1, :] = jnp.where(filled, scores, 0.0)


def hypothesis_scores(place, slot_utt, lengths, every, slots, hyps, sections, widths):
    return pl.pallas_call(
        functools.partial(score_kernel, sections, widths),
        in_specs=[SCALARS] * 3 + [INSIDE],
        out_specs=INSIDE,
        out_shape=jax.ShapeDtypeStruct((slots, hyps), jnp.float32),
        compiler_params=pltpu.CompilerParams(vmem_limit_bytes=16 << 20),
        name="hypothesis_scores",
    )(place, slot_utt, lengths, every)


def rest(pieces, slot_tokens, place, slot_utt, frame_len, hyp_len, payloads, keys_values, o_proj, head):
    section_count = lax.axis_size("section")
    group_count = lax.axis_size("tm")
    width_count = lax.axis_size("mp")
    section_pos = lax.axis_index("section")
    width_pos = lax.axis_index("mp")
    slot_count, hyp_count = hyp_len.shape
    projected = attend(
        place,
        slot_utt,
        frame_len,
        payloads,
        keys_values,
        o_proj,
        pieces,
        section_count,
        width_count,
        slot_count,
    )

    kept, sent, other_kept, other_sent = fold(
        place,
        [projected[1], swap(projected[0], "section", 1), projected[3], swap(projected[2], "mp", 1)],
        [low_side, section_side],
        False,
    )
    kept, sent = fold(
        place,
        [kept, swap(sent, "mp", 1), other_kept, swap(other_sent, "section", 1)],
        [high_side, high_side],
        True,
    )
    out_rows = normed_rows(
        place, slot_utt, payloads, [kept, swap(sent, "mp", 2)], slot_tokens, slot_count
    )

    own = jnp.zeros((width_count, *out_rows.shape), jnp.bfloat16)
    for distance in range(width_count):
        block = swap(out_rows, "mp", distance) if distance else out_rows
        own = lax.dynamic_update_index_in_dim(own, block, width_pos ^ distance, 0)
    own = own.reshape(-1, *out_rows.shape[1:])
    half = own.shape[0] // 2
    by_x = swap(own, "section", 1)
    by_y = swap(own, "tm", 2)
    stats, head = vocabulary_stats(place, [own, swap(own, "tm", 1)], head, load=True)
    stats = [stats]
    across = [swap(by_x[:half], "tm", 2), swap(by_y[half:], "section", 1)]
    stats.append(
        vocabulary_stats(place, [by_y, swap(by_y, "tm", 1), by_x, swap(by_x, "tm", 1)], head)
    )
    across = jnp.concatenate(across)
    stats.append(vocabulary_stats(place, [across, swap(across, "tm", 1)], head))

    every = exchange(
        spread_stats(place, slot_utt, stats, section_count, group_count, width_count), ALL
    )
    return hypothesis_scores(
        place, slot_utt, hyp_len, every, slot_count, hyp_count, section_count, width_count
    )


def near_device(
    frame_len,
    slot_utt,
    enc_in,
    ffn_up,
    ffn_down,
    kv_proj,
    hyp_state,
    hyp_tok,
    hyp_len,
    q_proj,
    o_proj,
    head,
):
    section_count = lax.axis_size("section")
    group_count = lax.axis_size("tm")
    width_count = lax.axis_size("mp")
    section_pos = lax.axis_index("section")
    group_pos = lax.axis_index("tm")
    width_pos = lax.axis_index("mp")
    head_devices = section_count * width_count
    all_devices = head_devices * group_count

    frame_rows, utterances, enc_width = enc_in.shape
    slot_count, hyp_count, positions, model_width = hyp_state.shape
    slot_tokens = hyp_count * positions
    share_rows = slot_tokens // head_devices
    vocab_start = (
        (section_pos * group_count + group_pos) * width_count + width_pos
    ) * head.shape[0]
    head_pos = section_pos * width_count + width_pos
    place = jnp.stack([section_pos, group_pos, width_pos, vocab_start, head_pos])
    place = place.astype(jnp.int32)

    parts, own_frames = ffn(place, enc_in, ffn_up, ffn_down, width_count)
    parts = exchange(parts, "mp")

    blocks = queries_of(
        place,
        slot_utt,
        hyp_len,
        place,
        hyp_state.reshape(slot_count, slot_tokens, model_width),
        hyp_tok.reshape(slot_count, 1, slot_tokens),
        q_proj,
        group_count,
        share_rows,
    )
    crossing = blocks[2] + swap(blocks[3], "tm", 1)
    payloads = [blocks[0], swap(blocks[1], "tm", 1), swap(crossing, "tm", 2)]

    sent = keys_values_of(
        parts, own_frames, kv_proj, blocks[0], section_count, utterances, width_count
    )
    frames_all = all_devices * (frame_rows // width_count)
    keys_values = exchange(sent.reshape(all_devices, -1, 2 * HD), ALL).reshape(frames_all, 2 * HD)

    here_slots = lax.dynamic_slice_in_dim(slot_utt, group_pos * slot_count, slot_count, 0)
    filled = jnp.where(here_slots >= 0, jnp.sum(hyp_len, axis=1), 0)
    most = jnp.max(filled).reshape(1)
    for distance in (1, 2):
        most = jnp.maximum(most, swap(most, "tm", distance))
    operands = (place, slot_utt, frame_len, hyp_len, payloads, keys_values, o_proj, head)
    few = share_rows * 3 // 4
    return lax.cond(
        most[0] <= few * head_devices,
        functools.partial(rest, (few - few // 3, few // 3), slot_tokens),
        functools.partial(rest, (share_rows // 2, share_rows - share_rows // 2), slot_tokens),
        *operands,
    )


def general(
    frame_len,
    slot_utt,
    enc_in,
    ffn_up,
    ffn_down,
    kv_proj,
    hyp_state,
    hyp_tok,
    hyp_len,
    q_proj,
    o_proj,
    head,
):
    section_count = lax.axis_size("section")
    group_count = lax.axis_size("tm")
    width_count = lax.axis_size("mp")
    section_pos = lax.axis_index("section")
    group_pos = lax.axis_index("tm")
    width_pos = lax.axis_index("mp")
    head_devices = section_count * width_count
    head_pos = section_pos * width_count + width_pos
    all_devices = head_devices * group_count

    frame_rows, utterances, enc_width = enc_in.shape
    assert utterances == group_count
    slot_count, hyp_count, positions, model_width = hyp_state.shape
    slot_tokens = hyp_count * positions
    device_heads = q_proj.shape[1] // HD
    group_heads = NH // KVH
    frame_share = frame_rows // width_count
    share_rows = slot_tokens // head_devices
    here_slots = lax.dynamic_slice_in_dim(slot_utt, group_pos * slot_count, slot_count, 0)

    dec_rows = hyp_state.reshape(slot_count * slot_tokens, model_width).astype(jnp.float32)
    queries = jnp.dot(
        square_norm(dec_rows).astype(jnp.bfloat16), q_proj, preferred_element_type=jnp.float32
    ).astype(jnp.bfloat16)
    queries = queries.reshape(slot_count, slot_tokens, device_heads * HD)
    shares = lax.dynamic_slice_in_dim(
        hyp_state.reshape(slot_count, slot_tokens, model_width), head_pos * share_rows, share_rows, 1
    )

    def by_utterance(values):
        out = []
        for utterance in range(utterances):
            block = values[0]
            for slot in range(1, slot_count):
                block = jnp.where(here_slots[slot] == utterance, values[slot], block)
            out.append(block)
        return jnp.stack(out)

    own_slot = jnp.argmax(slot_utt == group_pos)
    from_group = own_slot // slot_count
    queries = lax.dynamic_index_in_dim(
        exchange(by_utterance(queries), "tm"), from_group, 0, keepdims=False
    )
    resid_rows = lax.dynamic_index_in_dim(
        exchange(by_utterance(shares), "tm"), from_group, 0, keepdims=False
    )
    slot_targets = lax.all_gather(
        hyp_tok.reshape(slot_count, slot_tokens), "tm", axis=0, tiled=True
    )
    utt_slots = jnp.argmax(slot_utt[None, :] == jnp.arange(utterances)[:, None], axis=1)
    targets = jnp.take(slot_targets, utt_slots, axis=0).reshape(utterances * slot_tokens)

    enc_flat = (
        enc_in.reshape(width_count, frame_share, utterances, enc_width)
        .transpose(0, 2, 1, 3)
        .reshape(frame_rows * utterances, enc_width)
    )
    share_count = frame_share * utterances
    enc_normed = layer_norm(enc_flat.astype(jnp.float32)).astype(jnp.bfloat16)
    enc_inner = jax.nn.gelu(
        jnp.dot(enc_normed, ffn_up, preferred_element_type=jnp.float32), approximate=False
    ).astype(jnp.bfloat16)
    enc_summed = scatter_sum(
        jnp.dot(enc_inner, ffn_down, preferred_element_type=jnp.float32).astype(jnp.bfloat16),
        "mp",
        width_count,
    )
    own_frames = lax.dynamic_slice_in_dim(enc_flat, width_pos * share_count, share_count, 0)
    enc_states = layer_norm(own_frames.astype(jnp.float32) + enc_summed).astype(jnp.bfloat16)
    keys_values = jnp.dot(enc_states, kv_proj, preferred_element_type=jnp.float32).astype(
        jnp.bfloat16
    )
    keys_values = keys_values.reshape(utterances, frame_share, 2, KVH, HD)
    sent = []
    for section in range(section_count):
        per_width = []
        for width in range(width_count):
            kv_head = (section * width_count + width) * device_heads // group_heads
            per_width.append(
                keys_values[:, :, :, kv_head].reshape(utterances, frame_share, 2 * HD)
            )
        sent.append(jnp.stack(per_width, axis=1))
    sent = jnp.stack(sent).reshape(all_devices, frame_share, 2 * HD)
    frames_all = all_devices * frame_share
    keys_values = exchange(sent, ALL).reshape(frames_all, 2 * HD)

    frame_limit = lax.dynamic_index_in_dim(frame_len, group_pos, 0, keepdims=False)
    queries = queries.reshape(slot_tokens, device_heads, HD)
    scores = jnp.einsum(
        "qhd,fd->hqf", queries, keys_values[:, :HD], preferred_element_type=jnp.float32
    ) / math.sqrt(HD)
    visible = jnp.arange(frames_all, dtype=jnp.int32) < frame_limit
    scores = jnp.where(visible[None, None, :], scores, -jnp.inf)
    weights = jax.nn.softmax(scores, axis=-1).astype(jnp.bfloat16)
    context = jnp.einsum(
        "hqf,fd->qhd", weights, keys_values[:, HD:], preferred_element_type=jnp.float32
    ).astype(jnp.bfloat16)
    partial = jnp.dot(
        context.reshape(slot_tokens, device_heads * HD), o_proj, preferred_element_type=jnp.float32
    ).astype(jnp.bfloat16)
    partial = scatter_sum(partial, "section", section_count).astype(jnp.bfloat16)
    attn_out = scatter_sum(partial, "mp", width_count)
    out_normed = square_norm(resid_rows.astype(jnp.float32) + attn_out).astype(jnp.bfloat16)

    hidden_rows = lax.all_gather(out_normed, ALL, axis=0, tiled=True)
    logits = lax.dot_general(
        hidden_rows, head, (((1,), (1,)), ((), ())), preferred_element_type=jnp.float32
    )
    vocab_rows = head.shape[0]
    vocab_start = (
        (section_pos * group_count + group_pos) * width_count + width_pos
    ) * vocab_rows
    target_rows = (
        targets.reshape(utterances, section_count, width_count, share_rows)
        .transpose(1, 0, 2, 3)
        .reshape(-1)
    )
    upper = jnp.max(logits, axis=1)
    totals = jnp.sum(jnp.exp(logits - upper[:, None]), axis=1)
    matches = (
        jnp.arange(vocab_rows, dtype=jnp.int32)[None, :] == (target_rows - vocab_start)[:, None]
    )
    target_logit = jnp.sum(jnp.where(matches, logits, 0.0), axis=1)

    stats = jnp.stack([upper, totals, target_logit])
    stats = stats.reshape(3, section_count, utterances, width_count, share_rows)
    stats = stats.transpose(2, 0, 1, 3, 4).reshape(utterances, 3, slot_tokens)
    by_slot = jnp.take(stats, jnp.maximum(slot_utt, 0), axis=0)
    by_group = by_slot.reshape(1, group_count, 1, slot_count, 3, slot_tokens)
    by_group = jnp.broadcast_to(
        by_group, (section_count, group_count, width_count, slot_count, 3, slot_tokens)
    ).reshape(all_devices, slot_count, 3, slot_tokens)
    every = exchange(by_group, ALL)
    peak = jnp.max(every[:, :, 0], axis=0)
    total = jnp.sum(every[:, :, 1] * jnp.exp(every[:, :, 0] - peak[None]), axis=0)
    picked = jnp.sum(every[:, :, 2], axis=0)
    token_logp = (picked - (peak + jnp.log(total))).reshape(slot_count, hyp_count, positions)
    valid = jnp.arange(positions, dtype=jnp.int32)[None, None, :] < hyp_len[:, :, None]
    summed = jnp.sum(jnp.where(valid, token_logp, 0.0), axis=-1) / hyp_len.astype(
        jnp.float32
    ) + math.log(V)
    return jnp.where(here_slots[:, None] >= 0, summed, 0.0)


def solution(mesh):
    in_specs = (
        P(),
        P(),
        P(("section", "tm"), None, None),
        P(None, "mp"),
        P("mp", None),
        P(),
        P("tm", None, None, None),
        P("tm", None, None),
        P("tm", None),
        P(None, ("section", "mp")),
        P(("section", "mp"), None),
        P(("section", "tm", "mp"), None),
    )
    out_specs = P("tm", None)
    near = dict(mesh.shape) == {"section": 2, "tm": 4, "mp": 4}
    per_device = near_device if near else general
    return jax.shard_map(
        per_device, mesh=mesh, in_specs=in_specs, out_specs=out_specs, check_vma=False
    )
```

```python
import functools
import math

import jax
import jax.numpy as jnp
from jax import lax
from jax.experimental import pallas as pl
from jax.experimental.pallas import tpu as pltpu
from jax.sharding import PartitionSpec as P

NH = 32
KVH = 4
HD = 128
V = 64000
ALL = ("section", "tm", "mp")
LANES = 128
FOLD = 4


def layer_norm(values):
    center = values - jnp.mean(values, axis=-1, keepdims=True)
    spread = jnp.mean(center * center, axis=-1, keepdims=True)
    return center * lax.rsqrt(spread + 1e-05)


def square_norm(values):
    return values * lax.rsqrt(jnp.mean(values * values, axis=-1, keepdims=True) + 1e-06)


def exchange(blocks, axis):
    return lax.all_to_all(blocks, axis, split_axis=0, concat_axis=0, tiled=True)


def scatter_sum(partial, axis, count):
    blocks = partial.reshape((count, partial.shape[0] // count) + partial.shape[1:])
    return jnp.sum(exchange(blocks, axis).astype(jnp.float32), axis=0)


def swap(values, axis, distance):
    pairs = [(i, i ^ distance) for i in range(lax.axis_size(axis))]
    return lax.ppermute(values, axis, pairs)


def whole(shape):
    return pl.BlockSpec(shape, lambda *_: (0,) * len(shape))


SCALARS = pl.BlockSpec(memory_space=pltpu.SMEM)


def dot(left, right):
    return jnp.dot(left, right, preferred_element_type=jnp.float32)


def dot_nt(left, right):
    return lax.dot_general(
        left, right, (((1,), (1,)), ((), ())), preferred_element_type=jnp.float32
    )


def start_copies(source_of, target_of, semaphores, count):
    copies = []
    for number in range(count):
        copy = pltpu.make_async_copy(
            source_of(number), target_of(number), semaphores.at[number]
        )
        copy.start()
        copies.append(copy)
    return copies


def ffn_kernel(tile, place_ref, x_ref, up_ref, down_ref, *refs):
    out_ref, own_ref, inputs, rows, up, down, x_sem, up_sem, down_sem = refs
    count, share, width = out_ref.shape
    tiles = up_ref.shape[1] // tile
    x_copy = start_copies(lambda i: x_ref, lambda i: inputs, x_sem, 1)[0]
    up_copies = start_copies(
        lambda i: up_ref.at[:, pl.ds(i * tile, tile)], lambda i: up.at[i], up_sem, tiles
    )
    x_copy.wait()
    rows[...] = inputs[...].astype(jnp.float32).reshape(rows.shape)
    start = pl.multiple_of(place_ref[2] * share, share)
    own_ref[...] = rows[pl.ds(start, share), :].astype(jnp.bfloat16)
    normed = layer_norm(rows[...]).astype(jnp.bfloat16)
    inner = []
    for number in range(tiles):
        up_copies[number].wait()
        if number == 0:
            down_copies = start_copies(
                lambda i: down_ref.at[pl.ds(i * tile, tile), :],
                lambda i: down.at[i],
                down_sem,
                tiles,
            )
        hidden = dot(normed, up[number])
        hidden = 0.5 * hidden * (1.0 + lax.erf(hidden * math.sqrt(0.5)))
        inner.append(hidden.astype(jnp.bfloat16))
    total = None
    for number in range(tiles):
        down_copies[number].wait()
        product = dot(inner[number], down[number])
        total = product if total is None else total + product
    for part in range(count):
        out_ref[part] = total[part * share : (part + 1) * share, :].astype(jnp.bfloat16)


def in_hbm(values):
    return pltpu.with_memory_space_constraint(values, pltpu.HBM)


ANYWHERE = pl.BlockSpec(memory_space=pl.ANY)
INSIDE = pl.BlockSpec(memory_space=pltpu.VMEM)


def ffn(place, enc_in, up, down, count):
    frames, utterances, width = enc_in.shape
    rows = frames * utterances
    share = rows // count
    tile = 256
    tiles = up.shape[1] // tile
    return pl.pallas_call(
        functools.partial(ffn_kernel, tile),
        in_specs=[SCALARS] + [ANYWHERE] * 3,
        out_specs=[INSIDE] * 2,
        out_shape=[
            jax.ShapeDtypeStruct((count, share, width), jnp.bfloat16),
            jax.ShapeDtypeStruct((share, width), jnp.bfloat16),
        ],
        scratch_shapes=[
            pltpu.VMEM(enc_in.shape, jnp.bfloat16),
            pltpu.VMEM((rows, width), jnp.float32),
            pltpu.VMEM((tiles, width, tile), jnp.bfloat16),
            pltpu.VMEM((tiles, tile, width), jnp.bfloat16),
            pltpu.SemaphoreType.DMA((1,)),
            pltpu.SemaphoreType.DMA((tiles,)),
            pltpu.SemaphoreType.DMA((tiles,)),
        ],
        cost_estimate=pl.CostEstimate(
            flops=4 * rows * width * up.shape[1],
            bytes_accessed=4 * width * up.shape[1],
            transcendentals=rows * up.shape[1],
        ),
        compiler_params=pltpu.CompilerParams(vmem_limit_bytes=24 << 20),
        name="encoder_ffn",
    )(place, in_hbm(enc_in), in_hbm(up), in_hbm(down))


def query_kernel(
    count, depth, place_ref, slot_ref, length_ref, after_ref, x_ref, tok_ref, w_ref, *refs
):
    outs, (states, weights, normed, total, shares, x_sem, w_sem) = refs[:count], refs[count:]
    slots, tokens, width = x_ref.shape
    hyps = length_ref.shape[1]
    positions = tokens // hyps
    columns = w_ref.shape[1]
    share = shares.shape[1] // 2
    parts = width // columns
    x_copies = start_copies(lambda i: x_ref.at[i], lambda i: states.at[i], x_sem, slots)
    w_copies = start_copies(
        lambda i: w_ref.at[pl.ds(i * depth, depth), :],
        lambda i: weights.at[i],
        w_sem,
        width // depth,
    )
    head_pos = place_ref[4]
    lane = lax.broadcasted_iota(jnp.int32, (1, tokens), 1)
    for slot in range(slots):
        order = jnp.full((1, tokens), -1, jnp.int32)
        start = jnp.int32(0)
        for hyp in range(hyps):
            length = length_ref[slot, hyp]
            inside = (lane >= hyp * positions) & (lane < hyp * positions + length)
            order = jnp.where(inside, lane - hyp * positions + start, order)
            start = start + length
        row = lax.broadcasted_iota(jnp.int32, (tokens, tokens), 0)
        move = jnp.where(order == row, 1.0, 0.0).astype(jnp.bfloat16)
        x_copies[slot].wait()
        ordered = dot(move, states[slot])
        normed[slot * tokens : (slot + 1) * tokens, :] = square_norm(ordered).astype(jnp.bfloat16)
        share_row = lax.broadcasted_iota(jnp.int32, (share, tokens), 0)
        chosen = order == share_row * (tokens // share) + head_pos
        mine = dot(jnp.where(chosen, 1.0, 0.0).astype(jnp.bfloat16), states[slot])
        shares[slot, :share, :] = mine.astype(jnp.bfloat16)
        target = jnp.sum(
            jnp.where(chosen, tok_ref[slot], 0), axis=1, keepdims=True, dtype=jnp.int32
        )
        coarse = target // 256
        cell = lax.broadcasted_iota(jnp.int32, (share, columns), 1)
        packed = jnp.where(cell == 0, coarse, jnp.where(cell == 1, target - coarse * 256, 0))
        shares[slot, share:, :columns] = packed.astype(jnp.float32).astype(jnp.bfloat16)
    for number in range(width // depth):
        w_copies[number].wait()
        product = dot(normed[:, number * depth : (number + 1) * depth], weights[number])
        if number == 0:
            total[...] = product
        else:
            total[...] += product
    group = place_ref[1]
    for distance in range(count):
        slot = jnp.int32(-1)
        for candidate in range(slots):
            holds = slot_ref[group * slots + candidate] == group ^ distance
            slot = jnp.where(holds, candidate, slot)
        out = outs[distance]

        @pl.when(slot < 0)
        def _(out=out):
            out[...] = jnp.zeros_like(out)

        @pl.when(slot >= 0)
        def _(out=out, slot=slot):
            start = pl.multiple_of(slot * tokens, tokens)
            out[:tokens, :] = total[pl.ds(start, tokens), :].astype(jnp.bfloat16)
            for part in range(parts):
                first = tokens + part * share
                out[first : first + share, :] = shares[
                    slot, :share, part * columns : (part + 1) * columns
                ]
            out[tokens + parts * share :, :] = shares[slot, share:, :columns]


def queries_of(place, slot_utt, lengths, after, states, targets, weights, count, share):
    slots, tokens, width = states.shape
    columns = weights.shape[1]
    depth = 1024
    rows = tokens + (width // columns + 1) * share
    block = jax.ShapeDtypeStruct((rows, columns), jnp.bfloat16)
    return pl.pallas_call(
        functools.partial(query_kernel, count, depth),
        in_specs=[SCALARS] * 3 + [ANYWHERE, ANYWHERE, INSIDE, ANYWHERE],
        out_specs=[INSIDE] * count,
        out_shape=[block] * count,
        scratch_shapes=[
            pltpu.VMEM(states.shape, jnp.bfloat16),
            pltpu.VMEM((width // depth, depth, columns), jnp.bfloat16),
            pltpu.VMEM((slots * tokens, width), jnp.bfloat16),
            pltpu.VMEM((slots * tokens, columns), jnp.float32),
            pltpu.VMEM((slots, 2 * share, width), jnp.bfloat16),
            pltpu.SemaphoreType.DMA((slots,)),
            pltpu.SemaphoreType.DMA((width // depth,)),
        ],
        cost_estimate=pl.CostEstimate(
            flops=2 * slots * tokens * width * columns,
            bytes_accessed=2 * width * (columns + slots * tokens),
            transcendentals=0,
        ),
        compiler_params=pltpu.CompilerParams(vmem_limit_bytes=32 << 20),
        name="hypothesis_queries",
    )(place, slot_utt, lengths, after, in_hbm(states), targets, in_hbm(weights))


def kv_kernel(sections, utterances, widths, *refs):
    parts_ref, own_ref, w_ref, after_ref, out_ref = refs
    rows = own_ref.shape[0]
    frames = rows // utterances
    total = own_ref[...].astype(jnp.float32)
    summed = parts_ref[0].astype(jnp.float32)
    for part in range(1, parts_ref.shape[0]):
        summed += parts_ref[part].astype(jnp.float32)
    states = layer_norm(total + summed).astype(jnp.bfloat16)
    to = lax.broadcasted_iota(jnp.int32, (rows, rows), 0)
    come = lax.broadcasted_iota(jnp.int32, (rows, rows), 1)
    move = jnp.where(come == to % frames * utterances + to // frames, 1.0, 0.0)
    states = dot(move.astype(jnp.bfloat16), states).astype(jnp.bfloat16)
    both = dot(states, w_ref[...])
    half = KVH * HD
    per_kv = sections * widths // KVH
    for section in range(sections):
        for utterance in range(utterances):
            for width in range(0, widths, per_kv):
                kv_head = (section * widths + width) // per_kv
                take = slice(utterance * frames, (utterance + 1) * frames)
                block = jnp.concatenate(
                    [
                        both[take, kv_head * HD : (kv_head + 1) * HD],
                        both[take, half + kv_head * HD : half + (kv_head + 1) * HD],
                    ],
                    axis=1,
                )
                start = ((section * utterances + utterance) * widths + width) * frames
                block = jnp.concatenate([block] * per_kv, axis=0).astype(jnp.bfloat16)
                out_ref[start : start + per_kv * frames, :] = block


def keys_values_of(parts, own, weights, after, sections, utterances, widths):
    rows = sections * widths * own.shape[0]
    return pl.pallas_call(
        functools.partial(kv_kernel, sections, utterances, widths),
        in_specs=[INSIDE] * 3 + [ANYWHERE],
        out_specs=INSIDE,
        out_shape=jax.ShapeDtypeStruct((rows, 2 * HD), jnp.bfloat16),
        cost_estimate=pl.CostEstimate(
            flops=2 * own.shape[0] * weights.shape[0] * weights.shape[1],
            bytes_accessed=2 * weights.shape[0] * weights.shape[1],
            transcendentals=0,
        ),
        compiler_params=pltpu.CompilerParams(vmem_limit_bytes=24 << 20),
        name="frame_keys_values",
    )(parts, own, weights, after)


def choice_of_payload(place_ref, slot_ref, slots):
    group = place_ref[1]
    source = jnp.int32(0)
    for slot in range(slot_ref.shape[0]):
        source = jnp.where(slot_ref[slot] == group, slot // slots, source)
    return jnp.minimum(source ^ group, 2)


def attention_kernel(count, slots, capacity, pieces, sections, widths, tile, *refs):
    place_ref, slot_ref, frame_ref = refs[:3]
    payloads, (kv_ref, w_ref) = refs[3 : 3 + count], refs[3 + count : 5 + count]
    outs = refs[5 + count : 5 + count + 2 * len(pieces)]
    weights, picked, context, w_sem = refs[5 + count + 2 * len(pieces) :]
    tokens, columns = capacity, w_ref.shape[0]
    tiles = w_ref.shape[1] // tile
    w_copies = start_copies(
        lambda i: w_ref.at[:, pl.ds(i * tile, tile)], lambda i: weights.at[i], w_sem, tiles
    )
    source = choice_of_payload(place_ref, slot_ref, slots)
    section_pos = place_ref[0]
    frame_limit = frame_ref[place_ref[1]]
    for distance in range(count):

        @pl.when(source == distance)
        def _(payload=payloads[distance]):
            picked[...] = payload[:tokens, :]

    keys = kv_ref[:, :HD]
    values = kv_ref[:, HD:]
    frames = kv_ref.shape[0]
    visible = lax.broadcasted_iota(jnp.int32, (tokens, frames), 1) < frame_limit
    for head in range(columns // HD):
        scores = dot_nt(picked[:, head * HD : (head + 1) * HD], keys) * (1.0 / math.sqrt(HD))
        scores = jnp.where(visible, scores, -jnp.inf)
        raised = jnp.exp(scores - jnp.max(scores, axis=1, keepdims=True))
        chances = (raised / jnp.sum(raised, axis=1, keepdims=True)).astype(jnp.bfloat16)
        context[:, head * HD : (head + 1) * HD] = dot(chances, values).astype(jnp.bfloat16)
    to = lax.broadcasted_iota(jnp.int32, (tokens, tokens), 0)
    come = lax.broadcasted_iota(jnp.int32, (tokens, tokens), 1)
    low_bit = place_ref[2] % 2
    size = widths * pieces[0]
    block = to % size // pieces[0]
    section = jnp.where(to < size, 1 - section_pos, section_pos)
    first_order = (to % pieces[0] * sections + section) * widths + block % 2 * 2 + block // 2
    at = to - 2 * size
    size = widths * pieces[1]
    block = at % size // pieces[1]
    low = jnp.where(at < size, 1 - low_bit, low_bit)
    row = pieces[0] + at % pieces[1]
    second_order = (row * sections + block // 2) * widths + block % 2 * 2 + low
    move = come == jnp.where(at < 0, first_order, second_order)
    ordered = dot(jnp.where(move, 1.0, 0.0).astype(jnp.bfloat16), context[...])
    ordered = ordered.astype(jnp.bfloat16)
    for number in range(tiles):
        w_copies[number].wait()
        product = dot(ordered, weights[number]).astype(jnp.bfloat16)
        first = 0
        for out in outs:
            out[:, number * tile : (number + 1) * tile] = product[first : first + out.shape[0], :]
            first += out.shape[0]


def attend(place, slot_utt, frame_len, payloads, keys_values, weights, pieces, sections, widths, slots):
    count = len(payloads)
    columns, width = weights.shape
    capacity = sum(pieces) * sections * widths
    tile = 1024
    tiles = width // tile
    shapes = [
        jax.ShapeDtypeStruct((piece * widths, width), jnp.bfloat16)
        for piece in pieces
        for _ in range(2)
    ]
    return pl.pallas_call(
        functools.partial(
            attention_kernel, count, slots, capacity, pieces, sections, widths, tile
        ),
        in_specs=[SCALARS] * 3 + [INSIDE] * (count + 1) + [ANYWHERE],
        out_specs=[INSIDE] * len(shapes),
        out_shape=shapes,
        scratch_shapes=[
            pltpu.VMEM((tiles, columns, tile), jnp.bfloat16),
            pltpu.VMEM((capacity, columns), jnp.bfloat16),
            pltpu.VMEM((capacity, columns), jnp.bfloat16),
            pltpu.SemaphoreType.DMA((tiles,)),
        ],
        cost_estimate=pl.CostEstimate(
            flops=2 * capacity * columns * (width + 2 * keys_values.shape[0]),
            bytes_accessed=2 * columns * width + 2 * capacity * width,
            transcendentals=capacity * keys_values.shape[0] * columns // HD,
        ),
        compiler_params=pltpu.CompilerParams(vmem_limit_bytes=24 << 20),
        name="attention_projection",
    )(place, slot_utt, frame_len, *payloads, keys_values, in_hbm(weights))


def fold_kernel(sides, joined, place_ref, *refs):
    count = len(sides)
    parts, outs = refs[: 2 * count], refs[2 * count :]
    first = 0
    for number, side in enumerate(sides):
        kept_ref, came_ref = parts[2 * number : 2 * number + 2]
        total = kept_ref[...].astype(jnp.float32) + came_ref[...].astype(jnp.float32)
        half = total.shape[0] // 2
        top, bottom = total[:half], total[half:]
        upper = side(place_ref) == 0
        kept = jnp.where(upper, top, bottom)
        sent = jnp.where(upper, bottom, top).astype(jnp.bfloat16)
        if joined:
            outs[0][first : first + half, :] = kept
            outs[1][first : first + half, :] = sent
            first += half
        else:
            outs[2 * number][...] = kept
            outs[2 * number + 1][...] = sent


def fold(place, parts, sides, joined):
    width = parts[0].shape[1]
    halves = [part.shape[0] // 2 for part in parts[::2]]
    if joined:
        halves = [sum(halves)]
    shapes = [
        jax.ShapeDtypeStruct((half, width), kind)
        for half in halves
        for kind in (jnp.float32, jnp.bfloat16)
    ]
    return pl.pallas_call(
        functools.partial(fold_kernel, sides, joined),
        in_specs=[SCALARS] + [INSIDE] * len(parts),
        out_specs=[INSIDE] * len(shapes),
        out_shape=shapes,
        compiler_params=pltpu.CompilerParams(vmem_limit_bytes=24 << 20),
        name="sum_phase",
    )(place, *parts)


def section_side(place_ref):
    return place_ref[0]


def low_side(place_ref):
    return place_ref[2] % 2


def high_side(place_ref):
    return place_ref[2] // 2


def norm_kernel(count, slots, tokens, place_ref, slot_ref, *refs):
    payloads, (kept, other) = refs[:count], refs[count : count + 2]
    out_ref, picked, total = refs[count + 2 :]
    rows, width = total.shape
    columns = picked.shape[1]
    share = picked.shape[0] // (width // columns + 1)
    source = choice_of_payload(place_ref, slot_ref, slots)
    for choice in range(count):

        @pl.when(source == choice)
        def _(payload=payloads[choice]):
            picked[...] = payload[tokens:, :]

    total[...] = kept[...] + other[...].astype(jnp.float32)
    for part in range(width // columns):
        take = slice(part * columns, (part + 1) * columns)
        total[:, take] += picked[part * share : part * share + rows, :].astype(jnp.float32)
    shape = out_ref.shape[:2]
    normed = square_norm(total[...]).reshape(*shape, width)
    out_ref[:, :, :width] = normed.astype(jnp.bfloat16)
    last = width // columns * share
    target = picked[last : last + rows, :LANES].astype(jnp.float32).reshape(*shape, LANES)
    out_ref[:, :, width:] = target.astype(jnp.bfloat16)


def normed_rows(place, slot_utt, payloads, blocks, tokens, slots):
    width = blocks[0].shape[1]
    rows = blocks[0].shape[0]
    columns = payloads[0].shape[1]
    return pl.pallas_call(
        functools.partial(norm_kernel, len(payloads), slots, tokens),
        in_specs=[SCALARS] * 2 + [INSIDE] * (len(payloads) + len(blocks)),
        out_specs=INSIDE,
        out_shape=jax.ShapeDtypeStruct((rows // FOLD, FOLD, width + LANES), jnp.bfloat16),
        scratch_shapes=[
            pltpu.VMEM((payloads[0].shape[0] - tokens, columns), jnp.bfloat16),
            pltpu.VMEM((rows, width), jnp.float32),
        ],
        compiler_params=pltpu.CompilerParams(vmem_limit_bytes=16 << 20),
        name="token_rows",
    )(place, slot_utt, *payloads, *blocks)


def vocabulary_kernel(tile, count, first_ref, *refs):
    sets, head_ref, out_ref = refs[:count], refs[count], refs[count + 1]
    loads = len(refs) > count + 4
    if loads:
        loaded_ref, zero_ref, rows_ref, stat, semaphores = refs[count + 2 :]
        zero_ref[0] = 0
    else:
        rows_ref, stat = refs[count + 2 :]
    vocab_rows, width = head_ref.shape
    share = sets[0].shape[0] * FOLD
    tokens = share * len(sets)
    tiles = vocab_rows // tile
    pieces = 5

    def load(number):
        size = tile // pieces
        place = lambda i: pl.ds(number * tile + i * size, size)
        return start_copies(
            lambda i: head_ref.at[place(i), :],
            lambda i: loaded_ref.at[place(i), :],
            semaphores.at[number],
            pieces,
        )

    if loads:
        copies = [load(0), load(1)]
    cell = lax.broadcasted_iota(jnp.int32, (8, LANES), 1)
    take = jnp.where(cell == 0, 256.0, jnp.where(cell == 1, 1.0, 0.0)).astype(jnp.bfloat16)
    for number, rows in enumerate(sets):
        flat = rows[...].astype(jnp.float32).reshape(share, width + LANES)
        rows_ref[number * share : (number + 1) * share, :] = flat.astype(jnp.bfloat16)
    target = dot_nt(take, rows_ref[:, width:])[0:1, :].astype(jnp.int32) - first_ref[3]
    stat[0:1, :] = jnp.full((1, tokens), -jnp.inf, jnp.float32)
    stat[8:9, :] = jnp.zeros((1, tokens), jnp.float32)
    stat[16:17, :] = jnp.zeros((1, tokens), jnp.float32)

    def one_tile(start, block):
        logits = dot_nt(block, rows_ref[:, :width])
        vocab = lax.broadcasted_iota(jnp.int32, logits.shape, 0) + start
        before = stat[0:1, :]
        upper = jnp.maximum(before, jnp.max(logits, axis=0, keepdims=True))
        stat[8:9, :] = stat[8:9, :] * jnp.exp(before - upper) + jnp.sum(
            jnp.exp(logits - upper), axis=0, keepdims=True
        )
        stat[16:17, :] += jnp.sum(jnp.where(vocab == target, logits, 0.0), axis=0, keepdims=True)
        stat[0:1, :] = upper

    if loads:
        for number in range(tiles):
            for copy in copies[number]:
                copy.wait()
            if number + 2 < tiles:
                copies.append(load(number + 2))
            one_tile(number * tile, loaded_ref[number * tile : (number + 1) * tile, :])
    else:

        @pl.loop(0, tiles)
        def _(step):
            start = pl.multiple_of(step * tile, tile)
            one_tile(start, head_ref[pl.ds(start, tile), :])

    for number in range(len(sets)):
        for row in range(3):
            out_ref[number, row : row + 1, :] = stat[
                8 * row : 8 * row + 1, number * share : (number + 1) * share
            ]


def vocabulary_stats(place, sets, head, load=False):
    share = sets[0].shape[0] * FOLD
    count = len(sets)
    width = head.shape[1]
    tokens = share * count
    tile = head.shape[0] // (5 if load else 2)
    stats = jax.ShapeDtypeStruct((count, 8, share), jnp.float32)
    return pl.pallas_call(
        functools.partial(vocabulary_kernel, tile, count),
        in_specs=[SCALARS] + [INSIDE] * count + [ANYWHERE if load else INSIDE],
        out_specs=[INSIDE, INSIDE, SCALARS] if load else INSIDE,
        out_shape=[
            stats,
            pltpu.VMEM(head.shape, head.dtype),
            jax.ShapeDtypeStruct((1,), jnp.int32),
        ]
        if load
        else stats,
        scratch_shapes=[
            pltpu.VMEM((tokens, width + LANES), jnp.bfloat16),
            pltpu.VMEM((24, tokens), jnp.float32),
        ]
        + ([pltpu.SemaphoreType.DMA((5, 5))] if load else []),
        cost_estimate=pl.CostEstimate(
            flops=3 * tokens * head.shape[0] * width,
            bytes_accessed=2 * tokens * width,
            transcendentals=tokens * head.shape[0],
        ),
        compiler_params=pltpu.CompilerParams(vmem_limit_bytes=(36 if load else 16) << 20),
        name="vocabulary_scores",
    )(
        place,
        *sets,
        in_hbm(head) if load else pltpu.with_memory_space_constraint(head, pltpu.VMEM),
    )


def spread_kernel(sections, groups, widths, place_ref, slot_ref, *refs):
    stats, (out_ref, table, block) = refs[:-3], refs[-3:]
    share = table.shape[2]
    first = 0
    for stat in stats:
        table[first : first + stat.shape[0]] = stat[...]
        first += stat.shape[0]
    slots = slot_ref.shape[0] // groups
    block[...] = jnp.zeros_like(block)
    for group in range(groups):
        for slot in range(slots):
            utterance = jnp.maximum(slot_ref[group * slots + slot], 0)
            for section in range(sections):
                at = (section ^ place_ref[0]) * groups + (utterance ^ place_ref[1])
                block[group, 3 * slot : 3 * slot + 3, section * share : (section + 1) * share] = (
                    table[at][0:3, :]
                )
    for section in range(sections):
        for group in range(groups):
            for width in range(widths):
                out_ref[(section * groups + group) * widths + width] = block[group]


def spread_stats(place, slot_utt, stats, sections, groups, widths):
    share = stats[0].shape[2]
    assert 3 * slot_utt.shape[0] // groups <= 8
    return pl.pallas_call(
        functools.partial(spread_kernel, sections, groups, widths),
        in_specs=[SCALARS] * 2 + [INSIDE] * len(stats),
        out_specs=INSIDE,
        out_shape=jax.ShapeDtypeStruct(
            (sections * groups * widths, 8, sections * share), jnp.float32
        ),
        scratch_shapes=[
            pltpu.VMEM((sections * groups, 8, share), jnp.float32),
            pltpu.VMEM((groups, 8, sections * share), jnp.float32),
        ],
        compiler_params=pltpu.CompilerParams(vmem_limit_bytes=16 << 20),
        name="statistics_by_group",
    )(place, slot_utt, *stats)


def score_kernel(sections, widths, place_ref, slot_ref, length_ref, every_ref, out_ref):
    slots, hyps = out_ref.shape
    lanes = every_ref.shape[2]
    share = lanes // sections // widths
    lane = lax.broadcasted_iota(jnp.int32, (1, lanes), 1)
    order = lane % share * (sections * widths) + lane // share
    column = lax.broadcasted_iota(jnp.int32, (1, hyps), 1)
    for slot in range(slots):
        upper = every_ref[:, 3 * slot, :]
        peak = jnp.max(upper, axis=0, keepdims=True)
        total = jnp.sum(
            every_ref[:, 3 * slot + 1, :] * jnp.exp(upper - peak), axis=0, keepdims=True
        )
        picked = jnp.sum(every_ref[:, 3 * slot + 2, :], axis=0, keepdims=True)
        logp = picked - (peak + jnp.log(total))
        scores = jnp.zeros((1, hyps), jnp.float32)
        start = jnp.int32(0)
        for hyp in range(hyps):
            length = length_ref[slot, hyp]
            valid = (order >= start) & (order < start + length)
            summed = jnp.sum(jnp.where(valid, logp, 0.0), axis=1, keepdims=True)
            mean = summed / jnp.full((1, 1), length, jnp.int32).astype(jnp.float32)
            scores = jnp.where(column == hyp, mean + math.log(V), scores)
            start = start + length
        filled = slot_ref[place_ref[1] * slots + slot] >= 0
        out_ref[slot : slot + 1, :] = jnp.where(filled, scores, 0.0)


def hypothesis_scores(place, slot_utt, lengths, every, slots, hyps, sections, widths):
    return pl.pallas_call(
        functools.partial(score_kernel, sections, widths),
        in_specs=[SCALARS] * 3 + [INSIDE],
        out_specs=INSIDE,
        out_shape=jax.ShapeDtypeStruct((slots, hyps), jnp.float32),
        compiler_params=pltpu.CompilerParams(vmem_limit_bytes=16 << 20),
        name="hypothesis_scores",
    )(place, slot_utt, lengths, every)


def rest(pieces, slot_tokens, place, slot_utt, frame_len, hyp_len, payloads, keys_values, o_proj, head):
    section_count = lax.axis_size("section")
    group_count = lax.axis_size("tm")
    width_count = lax.axis_size("mp")
    section_pos = lax.axis_index("section")
    width_pos = lax.axis_index("mp")
    slot_count, hyp_count = hyp_len.shape
    projected = attend(
        place,
        slot_utt,
        frame_len,
        payloads,
        keys_values,
        o_proj,
        pieces,
        section_count,
        width_count,
        slot_count,
    )

    kept, sent, other_kept, other_sent = fold(
        place,
        [projected[1], swap(projected[0], "section", 1), projected[3], swap(projected[2], "mp", 1)],
        [low_side, section_side],
        False,
    )
    kept, sent = fold(
        place,
        [kept, swap(sent, "mp", 1), other_kept, swap(other_sent, "section", 1)],
        [high_side, high_side],
        True,
    )
    out_rows = normed_rows(
        place, slot_utt, payloads, [kept, swap(sent, "mp", 2)], slot_tokens, slot_count
    )

    own = jnp.zeros((width_count, *out_rows.shape), jnp.bfloat16)
    for distance in range(width_count):
        block = swap(out_rows, "mp", distance) if distance else out_rows
        own = lax.dynamic_update_index_in_dim(own, block, width_pos ^ distance, 0)
    own = own.reshape(-1, *out_rows.shape[1:])
    half = own.shape[0] // 2
    by_x = swap(own, "section", 1)
    by_y = swap(own, "tm", 2)
    stats, head, zero = vocabulary_stats(place, [own, swap(own, "tm", 1)], head, load=True)
    stats = [stats]
    across = [
        swap(lax.dynamic_slice_in_dim(by_x, zero[0], half, 0), "tm", 2),
        swap(lax.dynamic_slice_in_dim(by_y, zero[0] + half, half, 0), "section", 1),
    ]
    stats.append(
        vocabulary_stats(place, [by_y, swap(by_y, "tm", 1), by_x, swap(by_x, "tm", 1)], head)
    )
    across = jnp.concatenate(across)
    stats.append(vocabulary_stats(place, [across, swap(across, "tm", 1)], head))

    every = exchange(
        spread_stats(place, slot_utt, stats, section_count, group_count, width_count), ALL
    )
    return hypothesis_scores(
        place, slot_utt, hyp_len, every, slot_count, hyp_count, section_count, width_count
    )


def near_device(
    frame_len,
    slot_utt,
    enc_in,
    ffn_up,
    ffn_down,
    kv_proj,
    hyp_state,
    hyp_tok,
    hyp_len,
    q_proj,
    o_proj,
    head,
):
    section_count = lax.axis_size("section")
    group_count = lax.axis_size("tm")
    width_count = lax.axis_size("mp")
    section_pos = lax.axis_index("section")
    group_pos = lax.axis_index("tm")
    width_pos = lax.axis_index("mp")
    head_devices = section_count * width_count
    all_devices = head_devices * group_count

    frame_rows, utterances, enc_width = enc_in.shape
    slot_count, hyp_count, positions, model_width = hyp_state.shape
    slot_tokens = hyp_count * positions
    share_rows = slot_tokens // head_devices
    vocab_start = (
        (section_pos * group_count + group_pos) * width_count + width_pos
    ) * head.shape[0]
    head_pos = section_pos * width_count + width_pos
    place = jnp.stack([section_pos, group_pos, width_pos, vocab_start, head_pos])
    place = place.astype(jnp.int32)

    parts, own_frames = ffn(place, enc_in, ffn_up, ffn_down, width_count)
    parts = exchange(parts, "mp")

    blocks = queries_of(
        place,
        slot_utt,
        hyp_len,
        place,
        hyp_state.reshape(slot_count, slot_tokens, model_width),
        hyp_tok.reshape(slot_count, 1, slot_tokens),
        q_proj,
        group_count,
        share_rows,
    )
    crossing = blocks[2] + swap(blocks[3], "tm", 1)
    payloads = [blocks[0], swap(blocks[1], "tm", 1), swap(crossing, "tm", 2)]

    sent = keys_values_of(
        parts, own_frames, kv_proj, blocks[0], section_count, utterances, width_count
    )
    frames_all = all_devices * (frame_rows // width_count)
    keys_values = exchange(sent.reshape(all_devices, -1, 2 * HD), ALL).reshape(frames_all, 2 * HD)

    here_slots = lax.dynamic_slice_in_dim(slot_utt, group_pos * slot_count, slot_count, 0)
    filled = jnp.where(here_slots >= 0, jnp.sum(hyp_len, axis=1), 0)
    count = jnp.max(filled).reshape(1)
    most = count
    for distance in range(1, group_count):
        most = jnp.maximum(most, swap(count, "tm", distance))
    operands = (place, slot_utt, frame_len, hyp_len, payloads, keys_values, o_proj, head)
    few = share_rows * 3 // 4
    return lax.cond(
        most[0] <= few * head_devices,
        functools.partial(rest, (few - few // 3, few // 3), slot_tokens),
        functools.partial(rest, (share_rows // 2, share_rows - share_rows // 2), slot_tokens),
        *operands,
    )


def general(
    frame_len,
    slot_utt,
    enc_in,
    ffn_up,
    ffn_down,
    kv_proj,
    hyp_state,
    hyp_tok,
    hyp_len,
    q_proj,
    o_proj,
    head,
):
    section_count = lax.axis_size("section")
    group_count = lax.axis_size("tm")
    width_count = lax.axis_size("mp")
    section_pos = lax.axis_index("section")
    group_pos = lax.axis_index("tm")
    width_pos = lax.axis_index("mp")
    head_devices = section_count * width_count
    head_pos = section_pos * width_count + width_pos
    all_devices = head_devices * group_count

    frame_rows, utterances, enc_width = enc_in.shape
    assert utterances == group_count
    slot_count, hyp_count, positions, model_width = hyp_state.shape
    slot_tokens = hyp_count * positions
    device_heads = q_proj.shape[1] // HD
    group_heads = NH // KVH
    frame_share = frame_rows // width_count
    share_rows = slot_tokens // head_devices
    here_slots = lax.dynamic_slice_in_dim(slot_utt, group_pos * slot_count, slot_count, 0)

    dec_rows = hyp_state.reshape(slot_count * slot_tokens, model_width).astype(jnp.float32)
    queries = jnp.dot(
        square_norm(dec_rows).astype(jnp.bfloat16), q_proj, preferred_element_type=jnp.float32
    ).astype(jnp.bfloat16)
    queries = queries.reshape(slot_count, slot_tokens, device_heads * HD)
    shares = lax.dynamic_slice_in_dim(
        hyp_state.reshape(slot_count, slot_tokens, model_width), head_pos * share_rows, share_rows, 1
    )

    def by_utterance(values):
        out = []
        for utterance in range(utterances):
            block = values[0]
            for slot in range(1, slot_count):
                block = jnp.where(here_slots[slot] == utterance, values[slot], block)
            out.append(block)
        return jnp.stack(out)

    own_slot = jnp.argmax(slot_utt == group_pos)
    from_group = own_slot // slot_count
    queries = lax.dynamic_index_in_dim(
        exchange(by_utterance(queries), "tm"), from_group, 0, keepdims=False
    )
    resid_rows = lax.dynamic_index_in_dim(
        exchange(by_utterance(shares), "tm"), from_group, 0, keepdims=False
    )
    slot_targets = lax.all_gather(
        hyp_tok.reshape(slot_count, slot_tokens), "tm", axis=0, tiled=True
    )
    utt_slots = jnp.argmax(slot_utt[None, :] == jnp.arange(utterances)[:, None], axis=1)
    targets = jnp.take(slot_targets, utt_slots, axis=0).reshape(utterances * slot_tokens)

    enc_flat = (
        enc_in.reshape(width_count, frame_share, utterances, enc_width)
        .transpose(0, 2, 1, 3)
        .reshape(frame_rows * utterances, enc_width)
    )
    share_count = frame_share * utterances
    enc_normed = layer_norm(enc_flat.astype(jnp.float32)).astype(jnp.bfloat16)
    enc_inner = jax.nn.gelu(
        jnp.dot(enc_normed, ffn_up, preferred_element_type=jnp.float32), approximate=False
    ).astype(jnp.bfloat16)
    enc_summed = scatter_sum(
        jnp.dot(enc_inner, ffn_down, preferred_element_type=jnp.float32).astype(jnp.bfloat16),
        "mp",
        width_count,
    )
    own_frames = lax.dynamic_slice_in_dim(enc_flat, width_pos * share_count, share_count, 0)
    enc_states = layer_norm(own_frames.astype(jnp.float32) + enc_summed).astype(jnp.bfloat16)
    keys_values = jnp.dot(enc_states, kv_proj, preferred_element_type=jnp.float32).astype(
        jnp.bfloat16
    )
    keys_values = keys_values.reshape(utterances, frame_share, 2, KVH, HD)
    sent = []
    for section in range(section_count):
        per_width = []
        for width in range(width_count):
            kv_head = (section * width_count + width) * device_heads // group_heads
            per_width.append(
                keys_values[:, :, :, kv_head].reshape(utterances, frame_share, 2 * HD)
            )
        sent.append(jnp.stack(per_width, axis=1))
    sent = jnp.stack(sent).reshape(all_devices, frame_share, 2 * HD)
    frames_all = all_devices * frame_share
    keys_values = exchange(sent, ALL).reshape(frames_all, 2 * HD)

    frame_limit = lax.dynamic_index_in_dim(frame_len, group_pos, 0, keepdims=False)
    queries = queries.reshape(slot_tokens, device_heads, HD)
    scores = jnp.einsum(
        "qhd,fd->hqf", queries, keys_values[:, :HD], preferred_element_type=jnp.float32
    ) / math.sqrt(HD)
    visible = jnp.arange(frames_all, dtype=jnp.int32) < frame_limit
    scores = jnp.where(visible[None, None, :], scores, -jnp.inf)
    weights = jax.nn.softmax(scores, axis=-1).astype(jnp.bfloat16)
    context = jnp.einsum(
        "hqf,fd->qhd", weights, keys_values[:, HD:], preferred_element_type=jnp.float32
    ).astype(jnp.bfloat16)
    partial = jnp.dot(
        context.reshape(slot_tokens, device_heads * HD), o_proj, preferred_element_type=jnp.float32
    ).astype(jnp.bfloat16)
    partial = scatter_sum(partial, "section", section_count).astype(jnp.bfloat16)
    attn_out = scatter_sum(partial, "mp", width_count)
    out_normed = square_norm(resid_rows.astype(jnp.float32) + attn_out).astype(jnp.bfloat16)

    hidden_rows = lax.all_gather(out_normed, ALL, axis=0, tiled=True)
    logits = lax.dot_general(
        hidden_rows, head, (((1,), (1,)), ((), ())), preferred_element_type=jnp.float32
    )
    vocab_rows = head.shape[0]
    vocab_start = (
        (section_pos * group_count + group_pos) * width_count + width_pos
    ) * vocab_rows
    target_rows = (
        targets.reshape(utterances, section_count, width_count, share_rows)
        .transpose(1, 0, 2, 3)
        .reshape(-1)
    )
    upper = jnp.max(logits, axis=1)
    totals = jnp.sum(jnp.exp(logits - upper[:, None]), axis=1)
    matches = (
        jnp.arange(vocab_rows, dtype=jnp.int32)[None, :] == (target_rows - vocab_start)[:, None]
    )
    target_logit = jnp.sum(jnp.where(matches, logits, 0.0), axis=1)

    stats = jnp.stack([upper, totals, target_logit])
    stats = stats.reshape(3, section_count, utterances, width_count, share_rows)
    stats = stats.transpose(2, 0, 1, 3, 4).reshape(utterances, 3, slot_tokens)
    by_slot = jnp.take(stats, jnp.maximum(slot_utt, 0), axis=0)
    by_group = by_slot.reshape(1, group_count, 1, slot_count, 3, slot_tokens)
    by_group = jnp.broadcast_to(
        by_group, (section_count, group_count, width_count, slot_count, 3, slot_tokens)
    ).reshape(all_devices, slot_count, 3, slot_tokens)
    every = exchange(by_group, ALL)
    peak = jnp.max(every[:, :, 0], axis=0)
    total = jnp.sum(every[:, :, 1] * jnp.exp(every[:, :, 0] - peak[None]), axis=0)
    picked = jnp.sum(every[:, :, 2], axis=0)
    token_logp = (picked - (peak + jnp.log(total))).reshape(slot_count, hyp_count, positions)
    valid = jnp.arange(positions, dtype=jnp.int32)[None, None, :] < hyp_len[:, :, None]
    summed = jnp.sum(jnp.where(valid, token_logp, 0.0), axis=-1) / hyp_len.astype(
        jnp.float32
    ) + math.log(V)
    return jnp.where(here_slots[:, None] >= 0, summed, 0.0)


def solution(mesh):
    in_specs = (
        P(),
        P(),
        P(("section", "tm"), None, None),
        P(None, "mp"),
        P("mp", None),
        P(),
        P("tm", None, None, None),
        P("tm", None, None),
        P("tm", None),
        P(None, ("section", "mp")),
        P(("section", "mp"), None),
        P(("section", "tm", "mp"), None),
    )
    out_specs = P("tm", None)
    near = dict(mesh.shape) == {"section": 2, "tm": 4, "mp": 4}
    per_device = near_device if near else general
    return jax.shard_map(
        per_device, mesh=mesh, in_specs=in_specs, out_specs=out_specs, check_vma=False
    )
```

```python
import functools
import math

import jax
import jax.numpy as jnp
from jax import lax
from jax.experimental import pallas as pl
from jax.experimental.pallas import tpu as pltpu
from jax.sharding import PartitionSpec as P

NH = 32
KVH = 4
HD = 128
V = 64000
ALL = ("section", "tm", "mp")
LANES = 128
FOLD = 4


def layer_norm(values):
    center = values - jnp.mean(values, axis=-1, keepdims=True)
    spread = jnp.mean(center * center, axis=-1, keepdims=True)
    return center * lax.rsqrt(spread + 1e-05)


def square_norm(values):
    return values * lax.rsqrt(jnp.mean(values * values, axis=-1, keepdims=True) + 1e-06)


def exchange(blocks, axis):
    return lax.all_to_all(blocks, axis, split_axis=0, concat_axis=0, tiled=True)


def scatter_sum(partial, axis, count):
    blocks = partial.reshape((count, partial.shape[0] // count) + partial.shape[1:])
    return jnp.sum(exchange(blocks, axis).astype(jnp.float32), axis=0)


def swap(values, axis, distance):
    pairs = [(i, i ^ distance) for i in range(lax.axis_size(axis))]
    return lax.ppermute(values, axis, pairs)


def whole(shape):
    return pl.BlockSpec(shape, lambda *_: (0,) * len(shape))


SCALARS = pl.BlockSpec(memory_space=pltpu.SMEM)


def dot(left, right):
    return jnp.dot(left, right, preferred_element_type=jnp.float32)


def dot_nt(left, right):
    return lax.dot_general(
        left, right, (((1,), (1,)), ((), ())), preferred_element_type=jnp.float32
    )


def start_copies(source_of, target_of, semaphores, count):
    copies = []
    for number in range(count):
        copy = pltpu.make_async_copy(
            source_of(number), target_of(number), semaphores.at[number]
        )
        copy.start()
        copies.append(copy)
    return copies


def ffn_kernel(tile, place_ref, x_ref, up_ref, down_ref, *refs):
    out_ref, own_ref, inputs, rows, up, down, x_sem, up_sem, down_sem = refs
    count, share, width = out_ref.shape
    tiles = up_ref.shape[1] // tile
    x_copy = start_copies(lambda i: x_ref, lambda i: inputs, x_sem, 1)[0]
    up_copies = start_copies(
        lambda i: up_ref.at[:, pl.ds(i * tile, tile)], lambda i: up.at[i], up_sem, tiles
    )
    x_copy.wait()
    rows[...] = inputs[...].astype(jnp.float32).reshape(rows.shape)
    start = pl.multiple_of(place_ref[2] * share, share)
    own_ref[...] = rows[pl.ds(start, share), :].astype(jnp.bfloat16)
    normed = layer_norm(rows[...]).astype(jnp.bfloat16)
    inner = []
    for number in range(tiles):
        up_copies[number].wait()
        if number == 0:
            down_copies = start_copies(
                lambda i: down_ref.at[pl.ds(i * tile, tile), :],
                lambda i: down.at[i],
                down_sem,
                tiles,
            )
        hidden = dot(normed, up[number])
        hidden = 0.5 * hidden * (1.0 + lax.erf(hidden * math.sqrt(0.5)))
        inner.append(hidden.astype(jnp.bfloat16))
    total = None
    for number in range(tiles):
        down_copies[number].wait()
        product = dot(inner[number], down[number])
        total = product if total is None else total + product
    for part in range(count):
        out_ref[part] = total[part * share : (part + 1) * share, :].astype(jnp.bfloat16)


def in_hbm(values):
    return pltpu.with_memory_space_constraint(values, pltpu.HBM)


ANYWHERE = pl.BlockSpec(memory_space=pl.ANY)
INSIDE = pl.BlockSpec(memory_space=pltpu.VMEM)


def ffn(place, enc_in, up, down, count):
    frames, utterances, width = enc_in.shape
    rows = frames * utterances
    share = rows // count
    tile = 256
    tiles = up.shape[1] // tile
    return pl.pallas_call(
        functools.partial(ffn_kernel, tile),
        in_specs=[SCALARS] + [ANYWHERE] * 3,
        out_specs=[INSIDE] * 2,
        out_shape=[
            jax.ShapeDtypeStruct((count, share, width), jnp.bfloat16),
            jax.ShapeDtypeStruct((share, width), jnp.bfloat16),
        ],
        scratch_shapes=[
            pltpu.VMEM(enc_in.shape, jnp.bfloat16),
            pltpu.VMEM((rows, width), jnp.float32),
            pltpu.VMEM((tiles, width, tile), jnp.bfloat16),
            pltpu.VMEM((tiles, tile, width), jnp.bfloat16),
            pltpu.SemaphoreType.DMA((1,)),
            pltpu.SemaphoreType.DMA((tiles,)),
            pltpu.SemaphoreType.DMA((tiles,)),
        ],
        cost_estimate=pl.CostEstimate(
            flops=4 * rows * width * up.shape[1],
            bytes_accessed=4 * width * up.shape[1],
            transcendentals=rows * up.shape[1],
        ),
        compiler_params=pltpu.CompilerParams(vmem_limit_bytes=24 << 20),
        name="encoder_ffn",
    )(place, in_hbm(enc_in), in_hbm(up), in_hbm(down))


def query_kernel(
    count, depth, place_ref, slot_ref, length_ref, after_ref, x_ref, tok_ref, w_ref, *refs
):
    outs, (states, weights, normed, total, shares, x_sem, w_sem) = refs[:count], refs[count:]
    slots, tokens, width = x_ref.shape
    hyps = length_ref.shape[1]
    positions = tokens // hyps
    columns = w_ref.shape[1]
    share = shares.shape[1] // 2
    parts = width // columns
    x_copies = start_copies(lambda i: x_ref.at[i], lambda i: states.at[i], x_sem, slots)
    w_copies = start_copies(
        lambda i: w_ref.at[pl.ds(i * depth, depth), :],
        lambda i: weights.at[i],
        w_sem,
        width // depth,
    )
    head_pos = place_ref[4]
    lane = lax.broadcasted_iota(jnp.int32, (1, tokens), 1)
    for slot in range(slots):
        order = jnp.full((1, tokens), -1, jnp.int32)
        start = jnp.int32(0)
        for hyp in range(hyps):
            length = length_ref[slot, hyp]
            inside = (lane >= hyp * positions) & (lane < hyp * positions + length)
            order = jnp.where(inside, lane - hyp * positions + start, order)
            start = start + length
        row = lax.broadcasted_iota(jnp.int32, (tokens, tokens), 0)
        move = jnp.where(order == row, 1.0, 0.0).astype(jnp.bfloat16)
        x_copies[slot].wait()
        ordered = dot(move, states[slot])
        normed[slot * tokens : (slot + 1) * tokens, :] = square_norm(ordered).astype(jnp.bfloat16)
        share_row = lax.broadcasted_iota(jnp.int32, (share, tokens), 0)
        chosen = order == share_row * (tokens // share) + head_pos
        mine = dot(jnp.where(chosen, 1.0, 0.0).astype(jnp.bfloat16), states[slot])
        shares[slot, :share, :] = mine.astype(jnp.bfloat16)
        target = jnp.sum(
            jnp.where(chosen, tok_ref[slot], 0), axis=1, keepdims=True, dtype=jnp.int32
        )
        coarse = target // 256
        cell = lax.broadcasted_iota(jnp.int32, (share, columns), 1)
        packed = jnp.where(cell == 0, coarse, jnp.where(cell == 1, target - coarse * 256, 0))
        shares[slot, share:, :columns] = packed.astype(jnp.float32).astype(jnp.bfloat16)
    for number in range(width // depth):
        w_copies[number].wait()
        product = dot(normed[:, number * depth : (number + 1) * depth], weights[number])
        if number == 0:
            total[...] = product
        else:
            total[...] += product
    group = place_ref[1]
    for distance in range(count):
        slot = jnp.int32(-1)
        for candidate in range(slots):
            holds = slot_ref[group * slots + candidate] == group ^ distance
            slot = jnp.where(holds, candidate, slot)
        out = outs[distance]

        @pl.when(slot < 0)
        def _(out=out):
            out[...] = jnp.zeros_like(out)

        @pl.when(slot >= 0)
        def _(out=out, slot=slot):
            start = pl.multiple_of(slot * tokens, tokens)
            out[:tokens, :] = total[pl.ds(start, tokens), :].astype(jnp.bfloat16)
            for part in range(parts):
                first = tokens + part * share
                out[first : first + share, :] = shares[
                    slot, :share, part * columns : (part + 1) * columns
                ]
            out[tokens + parts * share :, :] = shares[slot, share:, :columns]


def queries_of(place, slot_utt, lengths, after, states, targets, weights, count, share):
    slots, tokens, width = states.shape
    columns = weights.shape[1]
    depth = 1024
    rows = tokens + (width // columns + 1) * share
    block = jax.ShapeDtypeStruct((rows, columns), jnp.bfloat16)
    return pl.pallas_call(
        functools.partial(query_kernel, count, depth),
        in_specs=[SCALARS] * 3 + [ANYWHERE, ANYWHERE, INSIDE, ANYWHERE],
        out_specs=[INSIDE] * count,
        out_shape=[block] * count,
        scratch_shapes=[
            pltpu.VMEM(states.shape, jnp.bfloat16),
            pltpu.VMEM((width // depth, depth, columns), jnp.bfloat16),
            pltpu.VMEM((slots * tokens, width), jnp.bfloat16),
            pltpu.VMEM((slots * tokens, columns), jnp.float32),
            pltpu.VMEM((slots, 2 * share, width), jnp.bfloat16),
            pltpu.SemaphoreType.DMA((slots,)),
            pltpu.SemaphoreType.DMA((width // depth,)),
        ],
        cost_estimate=pl.CostEstimate(
            flops=2 * slots * tokens * width * columns,
            bytes_accessed=2 * width * (columns + slots * tokens),
            transcendentals=0,
        ),
        compiler_params=pltpu.CompilerParams(vmem_limit_bytes=32 << 20),
        name="hypothesis_queries",
    )(place, slot_utt, lengths, after, in_hbm(states), targets, in_hbm(weights))


def kv_kernel(sections, utterances, widths, *refs):
    parts_ref, own_ref, w_ref, after_ref, out_ref = refs
    rows = own_ref.shape[0]
    frames = rows // utterances
    total = own_ref[...].astype(jnp.float32)
    summed = parts_ref[0].astype(jnp.float32)
    for part in range(1, parts_ref.shape[0]):
        summed += parts_ref[part].astype(jnp.float32)
    states = layer_norm(total + summed).astype(jnp.bfloat16)
    to = lax.broadcasted_iota(jnp.int32, (rows, rows), 0)
    come = lax.broadcasted_iota(jnp.int32, (rows, rows), 1)
    move = jnp.where(come == to % frames * utterances + to // frames, 1.0, 0.0)
    states = dot(move.astype(jnp.bfloat16), states).astype(jnp.bfloat16)
    both = dot(states, w_ref[...])
    half = KVH * HD
    per_kv = sections * widths // KVH
    for section in range(sections):
        for utterance in range(utterances):
            for width in range(0, widths, per_kv):
                kv_head = (section * widths + width) // per_kv
                take = slice(utterance * frames, (utterance + 1) * frames)
                block = jnp.concatenate(
                    [
                        both[take, kv_head * HD : (kv_head + 1) * HD],
                        both[take, half + kv_head * HD : half + (kv_head + 1) * HD],
                    ],
                    axis=1,
                )
                start = ((section * utterances + utterance) * widths + width) * frames
                block = jnp.concatenate([block] * per_kv, axis=0).astype(jnp.bfloat16)
                out_ref[start : start + per_kv * frames, :] = block


def keys_values_of(parts, own, weights, after, sections, utterances, widths):
    rows = sections * widths * own.shape[0]
    return pl.pallas_call(
        functools.partial(kv_kernel, sections, utterances, widths),
        in_specs=[INSIDE] * 3 + [ANYWHERE],
        out_specs=INSIDE,
        out_shape=jax.ShapeDtypeStruct((rows, 2 * HD), jnp.bfloat16),
        cost_estimate=pl.CostEstimate(
            flops=2 * own.shape[0] * weights.shape[0] * weights.shape[1],
            bytes_accessed=2 * weights.shape[0] * weights.shape[1],
            transcendentals=0,
        ),
        compiler_params=pltpu.CompilerParams(vmem_limit_bytes=24 << 20),
        name="frame_keys_values",
    )(parts, own, weights, after)


def choice_of_payload(place_ref, slot_ref, slots):
    group = place_ref[1]
    source = jnp.int32(0)
    for slot in range(slot_ref.shape[0]):
        source = jnp.where(slot_ref[slot] == group, slot // slots, source)
    return jnp.minimum(source ^ group, 2)


def attention_kernel(count, slots, capacity, pieces, sections, widths, tile, *refs):
    place_ref, slot_ref, frame_ref = refs[:3]
    payloads, (kv_ref, w_ref) = refs[3 : 3 + count], refs[3 + count : 5 + count]
    outs = refs[5 + count : 5 + count + 2 * len(pieces)]
    weights, picked, context, w_sem = refs[5 + count + 2 * len(pieces) :]
    tokens, columns = capacity, w_ref.shape[0]
    tiles = w_ref.shape[1] // tile
    w_copies = start_copies(
        lambda i: w_ref.at[:, pl.ds(i * tile, tile)], lambda i: weights.at[i], w_sem, tiles
    )
    source = choice_of_payload(place_ref, slot_ref, slots)
    section_pos = place_ref[0]
    frame_limit = frame_ref[place_ref[1]]
    for distance in range(count):

        @pl.when(source == distance)
        def _(payload=payloads[distance]):
            picked[...] = payload[:tokens, :]

    keys = kv_ref[:, :HD]
    values = kv_ref[:, HD:]
    frames = kv_ref.shape[0]
    visible = lax.broadcasted_iota(jnp.int32, (tokens, frames), 1) < frame_limit
    for head in range(columns // HD):
        scores = dot_nt(picked[:, head * HD : (head + 1) * HD], keys) * (1.0 / math.sqrt(HD))
        scores = jnp.where(visible, scores, -jnp.inf)
        raised = jnp.exp(scores - jnp.max(scores, axis=1, keepdims=True))
        chances = (raised / jnp.sum(raised, axis=1, keepdims=True)).astype(jnp.bfloat16)
        context[:, head * HD : (head + 1) * HD] = dot(chances, values).astype(jnp.bfloat16)
    to = lax.broadcasted_iota(jnp.int32, (tokens, tokens), 0)
    come = lax.broadcasted_iota(jnp.int32, (tokens, tokens), 1)
    low_bit = place_ref[2] % 2
    size = widths * pieces[0]
    block = to % size // pieces[0]
    section = jnp.where(to < size, 1 - section_pos, section_pos)
    first_order = (to % pieces[0] * sections + section) * widths + block % 2 * 2 + block // 2
    at = to - 2 * size
    size = widths * pieces[1]
    block = at % size // pieces[1]
    low = jnp.where(at < size, 1 - low_bit, low_bit)
    row = pieces[0] + at % pieces[1]
    second_order = (row * sections + block // 2) * widths + block % 2 * 2 + low
    move = come == jnp.where(at < 0, first_order, second_order)
    ordered = dot(jnp.where(move, 1.0, 0.0).astype(jnp.bfloat16), context[...])
    ordered = ordered.astype(jnp.bfloat16)
    for number in range(tiles):
        w_copies[number].wait()
        product = dot(ordered, weights[number]).astype(jnp.bfloat16)
        first = 0
        for out in outs:
            out[:, number * tile : (number + 1) * tile] = product[first : first + out.shape[0], :]
            first += out.shape[0]


def attend(place, slot_utt, frame_len, payloads, keys_values, weights, pieces, sections, widths, slots):
    count = len(payloads)
    columns, width = weights.shape
    capacity = sum(pieces) * sections * widths
    tile = 1024
    tiles = width // tile
    shapes = [
        jax.ShapeDtypeStruct((piece * widths, width), jnp.bfloat16)
        for piece in pieces
        for _ in range(2)
    ]
    return pl.pallas_call(
        functools.partial(
            attention_kernel, count, slots, capacity, pieces, sections, widths, tile
        ),
        in_specs=[SCALARS] * 3 + [INSIDE] * (count + 1) + [ANYWHERE],
        out_specs=[INSIDE] * len(shapes),
        out_shape=shapes,
        scratch_shapes=[
            pltpu.VMEM((tiles, columns, tile), jnp.bfloat16),
            pltpu.VMEM((capacity, columns), jnp.bfloat16),
            pltpu.VMEM((capacity, columns), jnp.bfloat16),
            pltpu.SemaphoreType.DMA((tiles,)),
        ],
        cost_estimate=pl.CostEstimate(
            flops=2 * capacity * columns * (width + 2 * keys_values.shape[0]),
            bytes_accessed=2 * columns * width + 2 * capacity * width,
            transcendentals=capacity * keys_values.shape[0] * columns // HD,
        ),
        compiler_params=pltpu.CompilerParams(vmem_limit_bytes=24 << 20),
        name="attention_projection",
    )(place, slot_utt, frame_len, *payloads, keys_values, in_hbm(weights))


def fold_kernel(sides, joined, place_ref, *refs):
    count = len(sides)
    parts, outs = refs[: 2 * count], refs[2 * count :]
    first = 0
    for number, side in enumerate(sides):
        kept_ref, came_ref = parts[2 * number : 2 * number + 2]
        total = kept_ref[...].astype(jnp.float32) + came_ref[...].astype(jnp.float32)
        half = total.shape[0] // 2
        top, bottom = total[:half], total[half:]
        upper = side(place_ref) == 0
        kept = jnp.where(upper, top, bottom)
        sent = jnp.where(upper, bottom, top).astype(jnp.bfloat16)
        if joined:
            outs[0][first : first + half, :] = kept
            outs[1][first : first + half, :] = sent
            first += half
        else:
            outs[2 * number][...] = kept
            outs[2 * number + 1][...] = sent


def fold(place, parts, sides, joined):
    width = parts[0].shape[1]
    halves = [part.shape[0] // 2 for part in parts[::2]]
    if joined:
        halves = [sum(halves)]
    shapes = [
        jax.ShapeDtypeStruct((half, width), kind)
        for half in halves
        for kind in (jnp.float32, jnp.bfloat16)
    ]
    return pl.pallas_call(
        functools.partial(fold_kernel, sides, joined),
        in_specs=[SCALARS] + [INSIDE] * len(parts),
        out_specs=[INSIDE] * len(shapes),
        out_shape=shapes,
        compiler_params=pltpu.CompilerParams(vmem_limit_bytes=24 << 20),
        name="sum_phase",
    )(place, *parts)


def section_side(place_ref):
    return place_ref[0]


def low_side(place_ref):
    return place_ref[2] % 2


def high_side(place_ref):
    return place_ref[2] // 2


def norm_kernel(count, slots, tokens, place_ref, slot_ref, *refs):
    payloads, (kept, other) = refs[:count], refs[count : count + 2]
    out_ref, picked, total = refs[count + 2 :]
    rows, width = total.shape
    columns = picked.shape[1]
    share = picked.shape[0] // (width // columns + 1)
    source = choice_of_payload(place_ref, slot_ref, slots)
    for choice in range(count):

        @pl.when(source == choice)
        def _(payload=payloads[choice]):
            picked[...] = payload[tokens:, :]

    total[...] = kept[...] + other[...].astype(jnp.float32)
    for part in range(width // columns):
        take = slice(part * columns, (part + 1) * columns)
        total[:, take] += picked[part * share : part * share + rows, :].astype(jnp.float32)
    shape = out_ref.shape[:2]
    normed = square_norm(total[...]).reshape(*shape, width)
    out_ref[:, :, :width] = normed.astype(jnp.bfloat16)
    last = width // columns * share
    target = picked[last : last + rows, :LANES].astype(jnp.float32).reshape(*shape, LANES)
    out_ref[:, :, width:] = target.astype(jnp.bfloat16)


def normed_rows(place, slot_utt, payloads, blocks, tokens, slots):
    width = blocks[0].shape[1]
    rows = blocks[0].shape[0]
    columns = payloads[0].shape[1]
    return pl.pallas_call(
        functools.partial(norm_kernel, len(payloads), slots, tokens),
        in_specs=[SCALARS] * 2 + [INSIDE] * (len(payloads) + len(blocks)),
        out_specs=INSIDE,
        out_shape=jax.ShapeDtypeStruct((rows // FOLD, FOLD, width + LANES), jnp.bfloat16),
        scratch_shapes=[
            pltpu.VMEM((payloads[0].shape[0] - tokens, columns), jnp.bfloat16),
            pltpu.VMEM((rows, width), jnp.float32),
        ],
        compiler_params=pltpu.CompilerParams(vmem_limit_bytes=16 << 20),
        name="token_rows",
    )(place, slot_utt, *payloads, *blocks)


def vocabulary_kernel(tile, count, first_ref, *refs):
    sets, (head_ref, out_ref, rows_ref, stat) = refs[:count], refs[count:]
    vocab_rows, width = head_ref.shape
    share = sets[0].shape[0] * FOLD
    tokens = share * len(sets)
    cell = lax.broadcasted_iota(jnp.int32, (8, LANES), 1)
    take = jnp.where(cell == 0, 256.0, jnp.where(cell == 1, 1.0, 0.0)).astype(jnp.bfloat16)
    for number, rows in enumerate(sets):
        flat = rows[...].astype(jnp.float32).reshape(share, width + LANES)
        rows_ref[number * share : (number + 1) * share, :] = flat.astype(jnp.bfloat16)
    target = dot_nt(take, rows_ref[:, width:])[0:1, :].astype(jnp.int32) - first_ref[3]
    stat[0:1, :] = jnp.full((1, tokens), -jnp.inf, jnp.float32)
    stat[8:9, :] = jnp.zeros((1, tokens), jnp.float32)
    stat[16:17, :] = jnp.zeros((1, tokens), jnp.float32)

    @pl.loop(0, vocab_rows // tile)
    def _(step):
        start = pl.multiple_of(step * tile, tile)
        logits = dot_nt(head_ref[pl.ds(start, tile), :], rows_ref[:, :width])
        vocab = lax.broadcasted_iota(jnp.int32, logits.shape, 0) + start
        before = stat[0:1, :]
        upper = jnp.maximum(before, jnp.max(logits, axis=0, keepdims=True))
        stat[8:9, :] = stat[8:9, :] * jnp.exp(before - upper) + jnp.sum(
            jnp.exp(logits - upper), axis=0, keepdims=True
        )
        stat[16:17, :] += jnp.sum(jnp.where(vocab == target, logits, 0.0), axis=0, keepdims=True)
        stat[0:1, :] = upper

    for number in range(len(sets)):
        for row in range(3):
            out_ref[number, row : row + 1, :] = stat[
                8 * row : 8 * row + 1, number * share : (number + 1) * share
            ]


def vocabulary_stats(place, sets, head):
    share = sets[0].shape[0] * FOLD
    count = len(sets)
    width = head.shape[1]
    tokens = share * count
    return pl.pallas_call(
        functools.partial(vocabulary_kernel, head.shape[0] // 2, count),
        in_specs=[SCALARS] + [INSIDE] * (count + 1),
        out_specs=INSIDE,
        out_shape=jax.ShapeDtypeStruct((count, 8, share), jnp.float32),
        scratch_shapes=[
            pltpu.VMEM((tokens, width + LANES), jnp.bfloat16),
            pltpu.VMEM((24, tokens), jnp.float32),
        ],
        cost_estimate=pl.CostEstimate(
            flops=3 * tokens * head.shape[0] * width,
            bytes_accessed=2 * tokens * width,
            transcendentals=tokens * head.shape[0],
        ),
        compiler_params=pltpu.CompilerParams(vmem_limit_bytes=16 << 20),
        name="vocabulary_scores",
    )(place, *sets, pltpu.with_memory_space_constraint(head, pltpu.VMEM))


def zero_kernel(after_ref, head_ref, out_ref):
    out_ref[0] = 0


def zero_after(after, head):
    return pl.pallas_call(
        zero_kernel,
        in_specs=[ANYWHERE, INSIDE],
        out_specs=SCALARS,
        out_shape=jax.ShapeDtypeStruct((1,), jnp.int32),
        compiler_params=pltpu.CompilerParams(vmem_limit_bytes=16 << 20),
        name="vocabulary_rows",
    )(after, pltpu.with_memory_space_constraint(head, pltpu.VMEM))


def spread_kernel(sections, groups, widths, place_ref, slot_ref, *refs):
    stats, (out_ref, table, block) = refs[:-3], refs[-3:]
    share = table.shape[2]
    first = 0
    for stat in stats:
        table[first : first + stat.shape[0]] = stat[...]
        first += stat.shape[0]
    slots = slot_ref.shape[0] // groups
    block[...] = jnp.zeros_like(block)
    for group in range(groups):
        for slot in range(slots):
            utterance = jnp.maximum(slot_ref[group * slots + slot], 0)
            for section in range(sections):
                at = (section ^ place_ref[0]) * groups + (utterance ^ place_ref[1])
                block[group, 3 * slot : 3 * slot + 3, section * share : (section + 1) * share] = (
                    table[at][0:3, :]
                )
    for section in range(sections):
        for group in range(groups):
            for width in range(widths):
                out_ref[(section * groups + group) * widths + width] = block[group]


def spread_stats(place, slot_utt, stats, sections, groups, widths):
    share = stats[0].shape[2]
    assert 3 * slot_utt.shape[0] // groups <= 8
    return pl.pallas_call(
        functools.partial(spread_kernel, sections, groups, widths),
        in_specs=[SCALARS] * 2 + [INSIDE] * len(stats),
        out_specs=INSIDE,
        out_shape=jax.ShapeDtypeStruct(
            (sections * groups * widths, 8, sections * share), jnp.float32
        ),
        scratch_shapes=[
            pltpu.VMEM((sections * groups, 8, share), jnp.float32),
            pltpu.VMEM((groups, 8, sections * share), jnp.float32),
        ],
        compiler_params=pltpu.CompilerParams(vmem_limit_bytes=16 << 20),
        name="statistics_by_group",
    )(place, slot_utt, *stats)


def score_kernel(sections, widths, place_ref, slot_ref, length_ref, every_ref, out_ref):
    slots, hyps = out_ref.shape
    lanes = every_ref.shape[2]
    share = lanes // sections // widths
    lane = lax.broadcasted_iota(jnp.int32, (1, lanes), 1)
    order = lane % share * (sections * widths) + lane // share
    column = lax.broadcasted_iota(jnp.int32, (1, hyps), 1)
    for slot in range(slots):
        upper = every_ref[:, 3 * slot, :]
        peak = jnp.max(upper, axis=0, keepdims=True)
        total = jnp.sum(
            every_ref[:, 3 * slot + 1, :] * jnp.exp(upper - peak), axis=0, keepdims=True
        )
        picked = jnp.sum(every_ref[:, 3 * slot + 2, :], axis=0, keepdims=True)
        logp = picked - (peak + jnp.log(total))
        scores = jnp.zeros((1, hyps), jnp.float32)
        start = jnp.int32(0)
        for hyp in range(hyps):
            length = length_ref[slot, hyp]
            valid = (order >= start) & (order < start + length)
            summed = jnp.sum(jnp.where(valid, logp, 0.0), axis=1, keepdims=True)
            mean = summed / jnp.full((1, 1), length, jnp.int32).astype(jnp.float32)
            scores = jnp.where(column == hyp, mean + math.log(V), scores)
            start = start + length
        filled = slot_ref[place_ref[1] * slots + slot] >= 0
        out_ref[slot : slot + 1, :] = jnp.where(filled, scores, 0.0)


def hypothesis_scores(place, slot_utt, lengths, every, slots, hyps, sections, widths):
    return pl.pallas_call(
        functools.partial(score_kernel, sections, widths),
        in_specs=[SCALARS] * 3 + [INSIDE],
        out_specs=INSIDE,
        out_shape=jax.ShapeDtypeStruct((slots, hyps), jnp.float32),
        compiler_params=pltpu.CompilerParams(vmem_limit_bytes=16 << 20),
        name="hypothesis_scores",
    )(place, slot_utt, lengths, every)


def rest(pieces, slot_tokens, place, slot_utt, frame_len, hyp_len, payloads, keys_values, o_proj, head):
    section_count = lax.axis_size("section")
    group_count = lax.axis_size("tm")
    width_count = lax.axis_size("mp")
    section_pos = lax.axis_index("section")
    width_pos = lax.axis_index("mp")
    slot_count, hyp_count = hyp_len.shape
    projected = attend(
        place,
        slot_utt,
        frame_len,
        payloads,
        keys_values,
        o_proj,
        pieces,
        section_count,
        width_count,
        slot_count,
    )

    kept, sent, other_kept, other_sent = fold(
        place,
        [projected[1], swap(projected[0], "section", 1), projected[3], swap(projected[2], "mp", 1)],
        [low_side, section_side],
        False,
    )
    kept, sent = fold(
        place,
        [kept, swap(sent, "mp", 1), other_kept, swap(other_sent, "section", 1)],
        [high_side, high_side],
        True,
    )
    out_rows = normed_rows(
        place, slot_utt, payloads, [kept, swap(sent, "mp", 2)], slot_tokens, slot_count
    )

    own = jnp.zeros((width_count, *out_rows.shape), jnp.bfloat16)
    for distance in range(width_count):
        block = swap(out_rows, "mp", distance) if distance else out_rows
        own = lax.dynamic_update_index_in_dim(own, block, width_pos ^ distance, 0)
    own = own.reshape(-1, *out_rows.shape[1:])
    half = own.shape[0] // 2
    by_x = swap(own, "section", 1)
    by_y = swap(own, "tm", 2)
    zero = zero_after(own, head)
    across = [
        swap(lax.dynamic_slice_in_dim(by_x, zero[0], half, 0), "tm", 2),
        swap(lax.dynamic_slice_in_dim(by_y, zero[0] + half, half, 0), "section", 1),
    ]
    stats = [
        vocabulary_stats(place, [own, swap(own, "tm", 1), by_y, swap(by_y, "tm", 1)], head)
    ]
    across = jnp.concatenate(across)
    stats.append(
        vocabulary_stats(place, [by_x, swap(by_x, "tm", 1), across, swap(across, "tm", 1)], head)
    )

    every = exchange(
        spread_stats(place, slot_utt, stats, section_count, group_count, width_count), ALL
    )
    return hypothesis_scores(
        place, slot_utt, hyp_len, every, slot_count, hyp_count, section_count, width_count
    )


def near_device(
    frame_len,
    slot_utt,
    enc_in,
    ffn_up,
    ffn_down,
    kv_proj,
    hyp_state,
    hyp_tok,
    hyp_len,
    q_proj,
    o_proj,
    head,
):
    section_count = lax.axis_size("section")
    group_count = lax.axis_size("tm")
    width_count = lax.axis_size("mp")
    section_pos = lax.axis_index("section")
    group_pos = lax.axis_index("tm")
    width_pos = lax.axis_index("mp")
    head_devices = section_count * width_count
    all_devices = head_devices * group_count

    frame_rows, utterances, enc_width = enc_in.shape
    slot_count, hyp_count, positions, model_width = hyp_state.shape
    slot_tokens = hyp_count * positions
    share_rows = slot_tokens // head_devices
    vocab_start = (
        (section_pos * group_count + group_pos) * width_count + width_pos
    ) * head.shape[0]
    head_pos = section_pos * width_count + width_pos
    place = jnp.stack([section_pos, group_pos, width_pos, vocab_start, head_pos])
    place = place.astype(jnp.int32)

    parts, own_frames = ffn(place, enc_in, ffn_up, ffn_down, width_count)
    parts = exchange(parts, "mp")

    blocks = queries_of(
        place,
        slot_utt,
        hyp_len,
        place,
        hyp_state.reshape(slot_count, slot_tokens, model_width),
        hyp_tok.reshape(slot_count, 1, slot_tokens),
        q_proj,
        group_count,
        share_rows,
    )
    crossing = blocks[2] + swap(blocks[3], "tm", 1)
    payloads = [blocks[0], swap(blocks[1], "tm", 1), swap(crossing, "tm", 2)]

    sent = keys_values_of(
        parts, own_frames, kv_proj, blocks[0], section_count, utterances, width_count
    )
    frames_all = all_devices * (frame_rows // width_count)
    keys_values = exchange(sent.reshape(all_devices, -1, 2 * HD), ALL).reshape(frames_all, 2 * HD)

    here_slots = lax.dynamic_slice_in_dim(slot_utt, group_pos * slot_count, slot_count, 0)
    filled = jnp.where(here_slots >= 0, jnp.sum(hyp_len, axis=1), 0)
    count = jnp.max(filled).reshape(1)
    most = count
    for distance in range(1, group_count):
        most = jnp.maximum(most, swap(count, "tm", distance))
    operands = (place, slot_utt, frame_len, hyp_len, payloads, keys_values, o_proj, head)
    few = share_rows * 3 // 4
    return lax.cond(
        most[0] <= few * head_devices,
        functools.partial(rest, (few - few // 3, few // 3), slot_tokens),
        functools.partial(rest, (share_rows // 2, share_rows - share_rows // 2), slot_tokens),
        *operands,
    )


def general(
    frame_len,
    slot_utt,
    enc_in,
    ffn_up,
    ffn_down,
    kv_proj,
    hyp_state,
    hyp_tok,
    hyp_len,
    q_proj,
    o_proj,
    head,
):
    section_count = lax.axis_size("section")
    group_count = lax.axis_size("tm")
    width_count = lax.axis_size("mp")
    section_pos = lax.axis_index("section")
    group_pos = lax.axis_index("tm")
    width_pos = lax.axis_index("mp")
    head_devices = section_count * width_count
    head_pos = section_pos * width_count + width_pos
    all_devices = head_devices * group_count

    frame_rows, utterances, enc_width = enc_in.shape
    assert utterances == group_count
    slot_count, hyp_count, positions, model_width = hyp_state.shape
    slot_tokens = hyp_count * positions
    device_heads = q_proj.shape[1] // HD
    group_heads = NH // KVH
    frame_share = frame_rows // width_count
    share_rows = slot_tokens // head_devices
    here_slots = lax.dynamic_slice_in_dim(slot_utt, group_pos * slot_count, slot_count, 0)

    dec_rows = hyp_state.reshape(slot_count * slot_tokens, model_width).astype(jnp.float32)
    queries = jnp.dot(
        square_norm(dec_rows).astype(jnp.bfloat16), q_proj, preferred_element_type=jnp.float32
    ).astype(jnp.bfloat16)
    queries = queries.reshape(slot_count, slot_tokens, device_heads * HD)
    shares = lax.dynamic_slice_in_dim(
        hyp_state.reshape(slot_count, slot_tokens, model_width), head_pos * share_rows, share_rows, 1
    )

    def by_utterance(values):
        out = []
        for utterance in range(utterances):
            block = values[0]
            for slot in range(1, slot_count):
                block = jnp.where(here_slots[slot] == utterance, values[slot], block)
            out.append(block)
        return jnp.stack(out)

    own_slot = jnp.argmax(slot_utt == group_pos)
    from_group = own_slot // slot_count
    queries = lax.dynamic_index_in_dim(
        exchange(by_utterance(queries), "tm"), from_group, 0, keepdims=False
    )
    resid_rows = lax.dynamic_index_in_dim(
        exchange(by_utterance(shares), "tm"), from_group, 0, keepdims=False
    )
    slot_targets = lax.all_gather(
        hyp_tok.reshape(slot_count, slot_tokens), "tm", axis=0, tiled=True
    )
    utt_slots = jnp.argmax(slot_utt[None, :] == jnp.arange(utterances)[:, None], axis=1)
    targets = jnp.take(slot_targets, utt_slots, axis=0).reshape(utterances * slot_tokens)

    enc_flat = (
        enc_in.reshape(width_count, frame_share, utterances, enc_width)
        .transpose(0, 2, 1, 3)
        .reshape(frame_rows * utterances, enc_width)
    )
    share_count = frame_share * utterances
    enc_normed = layer_norm(enc_flat.astype(jnp.float32)).astype(jnp.bfloat16)
    enc_inner = jax.nn.gelu(
        jnp.dot(enc_normed, ffn_up, preferred_element_type=jnp.float32), approximate=False
    ).astype(jnp.bfloat16)
    enc_summed = scatter_sum(
        jnp.dot(enc_inner, ffn_down, preferred_element_type=jnp.float32).astype(jnp.bfloat16),
        "mp",
        width_count,
    )
    own_frames = lax.dynamic_slice_in_dim(enc_flat, width_pos * share_count, share_count, 0)
    enc_states = layer_norm(own_frames.astype(jnp.float32) + enc_summed).astype(jnp.bfloat16)
    keys_values = jnp.dot(enc_states, kv_proj, preferred_element_type=jnp.float32).astype(
        jnp.bfloat16
    )
    keys_values = keys_values.reshape(utterances, frame_share, 2, KVH, HD)
    sent = []
    for section in range(section_count):
        per_width = []
        for width in range(width_count):
            kv_head = (section * width_count + width) * device_heads // group_heads
            per_width.append(
                keys_values[:, :, :, kv_head].reshape(utterances, frame_share, 2 * HD)
            )
        sent.append(jnp.stack(per_width, axis=1))
    sent = jnp.stack(sent).reshape(all_devices, frame_share, 2 * HD)
    frames_all = all_devices * frame_share
    keys_values = exchange(sent, ALL).reshape(frames_all, 2 * HD)

    frame_limit = lax.dynamic_index_in_dim(frame_len, group_pos, 0, keepdims=False)
    queries = queries.reshape(slot_tokens, device_heads, HD)
    scores = jnp.einsum(
        "qhd,fd->hqf", queries, keys_values[:, :HD], preferred_element_type=jnp.float32
    ) / math.sqrt(HD)
    visible = jnp.arange(frames_all, dtype=jnp.int32) < frame_limit
    scores = jnp.where(visible[None, None, :], scores, -jnp.inf)
    weights = jax.nn.softmax(scores, axis=-1).astype(jnp.bfloat16)
    context = jnp.einsum(
        "hqf,fd->qhd", weights, keys_values[:, HD:], preferred_element_type=jnp.float32
    ).astype(jnp.bfloat16)
    partial = jnp.dot(
        context.reshape(slot_tokens, device_heads * HD), o_proj, preferred_element_type=jnp.float32
    ).astype(jnp.bfloat16)
    partial = scatter_sum(partial, "section", section_count).astype(jnp.bfloat16)
    attn_out = scatter_sum(partial, "mp", width_count)
    out_normed = square_norm(resid_rows.astype(jnp.float32) + attn_out).astype(jnp.bfloat16)

    hidden_rows = lax.all_gather(out_normed, ALL, axis=0, tiled=True)
    logits = lax.dot_general(
        hidden_rows, head, (((1,), (1,)), ((), ())), preferred_element_type=jnp.float32
    )
    vocab_rows = head.shape[0]
    vocab_start = (
        (section_pos * group_count + group_pos) * width_count + width_pos
    ) * vocab_rows
    target_rows = (
        targets.reshape(utterances, section_count, width_count, share_rows)
        .transpose(1, 0, 2, 3)
        .reshape(-1)
    )
    upper = jnp.max(logits, axis=1)
    totals = jnp.sum(jnp.exp(logits - upper[:, None]), axis=1)
    matches = (
        jnp.arange(vocab_rows, dtype=jnp.int32)[None, :] == (target_rows - vocab_start)[:, None]
    )
    target_logit = jnp.sum(jnp.where(matches, logits, 0.0), axis=1)

    stats = jnp.stack([upper, totals, target_logit])
    stats = stats.reshape(3, section_count, utterances, width_count, share_rows)
    stats = stats.transpose(2, 0, 1, 3, 4).reshape(utterances, 3, slot_tokens)
    by_slot = jnp.take(stats, jnp.maximum(slot_utt, 0), axis=0)
    by_group = by_slot.reshape(1, group_count, 1, slot_count, 3, slot_tokens)
    by_group = jnp.broadcast_to(
        by_group, (section_count, group_count, width_count, slot_count, 3, slot_tokens)
    ).reshape(all_devices, slot_count, 3, slot_tokens)
    every = exchange(by_group, ALL)
    peak = jnp.max(every[:, :, 0], axis=0)
    total = jnp.sum(every[:, :, 1] * jnp.exp(every[:, :, 0] - peak[None]), axis=0)
    picked = jnp.sum(every[:, :, 2], axis=0)
    token_logp = (picked - (peak + jnp.log(total))).reshape(slot_count, hyp_count, positions)
    valid = jnp.arange(positions, dtype=jnp.int32)[None, None, :] < hyp_len[:, :, None]
    summed = jnp.sum(jnp.where(valid, token_logp, 0.0), axis=-1) / hyp_len.astype(
        jnp.float32
    ) + math.log(V)
    return jnp.where(here_slots[:, None] >= 0, summed, 0.0)


def solution(mesh):
    in_specs = (
        P(),
        P(),
        P(("section", "tm"), None, None),
        P(None, "mp"),
        P("mp", None),
        P(),
        P("tm", None, None, None),
        P("tm", None, None),
        P("tm", None),
        P(None, ("section", "mp")),
        P(("section", "mp"), None),
        P(("section", "tm", "mp"), None),
    )
    out_specs = P("tm", None)
    near = dict(mesh.shape) == {"section": 2, "tm": 4, "mp": 4}
    per_device = near_device if near else general
    return jax.shard_map(
        per_device, mesh=mesh, in_specs=in_specs, out_specs=out_specs, check_vma=False
    )
```

```python
import functools
import math

import jax
import jax.numpy as jnp
from jax import lax
from jax.experimental import pallas as pl
from jax.experimental.pallas import tpu as pltpu
from jax.sharding import PartitionSpec as P

NH = 32
KVH = 4
HD = 128
V = 64000
ALL = ("section", "tm", "mp")
LANES = 128
FOLD = 4


def layer_norm(values):
    center = values - jnp.mean(values, axis=-1, keepdims=True)
    spread = jnp.mean(center * center, axis=-1, keepdims=True)
    return center * lax.rsqrt(spread + 1e-05)


def square_norm(values):
    return values * lax.rsqrt(jnp.mean(values * values, axis=-1, keepdims=True) + 1e-06)


def exchange(blocks, axis):
    return lax.all_to_all(blocks, axis, split_axis=0, concat_axis=0, tiled=True)


def scatter_sum(partial, axis, count):
    blocks = partial.reshape((count, partial.shape[0] // count) + partial.shape[1:])
    return jnp.sum(exchange(blocks, axis).astype(jnp.float32), axis=0)


def swap(values, axis, distance):
    pairs = [(i, i ^ distance) for i in range(lax.axis_size(axis))]
    return lax.ppermute(values, axis, pairs)


def whole(shape):
    return pl.BlockSpec(shape, lambda *_: (0,) * len(shape))


SCALARS = pl.BlockSpec(memory_space=pltpu.SMEM)


def dot(left, right):
    return jnp.dot(left, right, preferred_element_type=jnp.float32)


def dot_nt(left, right):
    return lax.dot_general(
        left, right, (((1,), (1,)), ((), ())), preferred_element_type=jnp.float32
    )


def start_copies(source_of, target_of, semaphores, count):
    copies = []
    for number in range(count):
        copy = pltpu.make_async_copy(
            source_of(number), target_of(number), semaphores.at[number]
        )
        copy.start()
        copies.append(copy)
    return copies


def ffn_kernel(tile, place_ref, x_ref, up_ref, down_ref, *refs):
    out_ref, own_ref, inputs, rows, up, down, x_sem, up_sem, down_sem = refs
    count, share, width = out_ref.shape
    tiles = up_ref.shape[1] // tile
    x_copy = start_copies(lambda i: x_ref, lambda i: inputs, x_sem, 1)[0]
    up_copies = start_copies(
        lambda i: up_ref.at[:, pl.ds(i * tile, tile)], lambda i: up.at[i], up_sem, tiles
    )
    x_copy.wait()
    rows[...] = inputs[...].astype(jnp.float32).reshape(rows.shape)
    start = pl.multiple_of(place_ref[2] * share, share)
    own_ref[...] = rows[pl.ds(start, share), :].astype(jnp.bfloat16)
    normed = layer_norm(rows[...]).astype(jnp.bfloat16)
    inner = []
    for number in range(tiles):
        up_copies[number].wait()
        if number == 0:
            down_copies = start_copies(
                lambda i: down_ref.at[pl.ds(i * tile, tile), :],
                lambda i: down.at[i],
                down_sem,
                tiles,
            )
        hidden = dot(normed, up[number])
        hidden = 0.5 * hidden * (1.0 + lax.erf(hidden * math.sqrt(0.5)))
        inner.append(hidden.astype(jnp.bfloat16))
    total = None
    for number in range(tiles):
        down_copies[number].wait()
        product = dot(inner[number], down[number])
        total = product if total is None else total + product
    for part in range(count):
        out_ref[part] = total[part * share : (part + 1) * share, :].astype(jnp.bfloat16)


def in_hbm(values):
    return pltpu.with_memory_space_constraint(values, pltpu.HBM)


ANYWHERE = pl.BlockSpec(memory_space=pl.ANY)
INSIDE = pl.BlockSpec(memory_space=pltpu.VMEM)


def ffn(place, enc_in, up, down, count):
    frames, utterances, width = enc_in.shape
    rows = frames * utterances
    share = rows // count
    tile = 256
    tiles = up.shape[1] // tile
    return pl.pallas_call(
        functools.partial(ffn_kernel, tile),
        in_specs=[SCALARS] + [ANYWHERE] * 3,
        out_specs=[INSIDE] * 2,
        out_shape=[
            jax.ShapeDtypeStruct((count, share, width), jnp.bfloat16),
            jax.ShapeDtypeStruct((share, width), jnp.bfloat16),
        ],
        scratch_shapes=[
            pltpu.VMEM(enc_in.shape, jnp.bfloat16),
            pltpu.VMEM((rows, width), jnp.float32),
            pltpu.VMEM((tiles, width, tile), jnp.bfloat16),
            pltpu.VMEM((tiles, tile, width), jnp.bfloat16),
            pltpu.SemaphoreType.DMA((1,)),
            pltpu.SemaphoreType.DMA((tiles,)),
            pltpu.SemaphoreType.DMA((tiles,)),
        ],
        cost_estimate=pl.CostEstimate(
            flops=4 * rows * width * up.shape[1],
            bytes_accessed=4 * width * up.shape[1],
            transcendentals=rows * up.shape[1],
        ),
        compiler_params=pltpu.CompilerParams(vmem_limit_bytes=24 << 20),
        name="encoder_ffn",
    )(place, in_hbm(enc_in), in_hbm(up), in_hbm(down))


def query_kernel(
    count, depth, place_ref, slot_ref, length_ref, after_ref, x_ref, tok_ref, w_ref, *refs
):
    outs, (states, weights, normed, total, shares, x_sem, w_sem) = refs[:count], refs[count:]
    slots, tokens, width = x_ref.shape
    hyps = length_ref.shape[1]
    positions = tokens // hyps
    columns = w_ref.shape[1]
    share = shares.shape[1] // 2
    parts = width // columns
    x_copies = start_copies(lambda i: x_ref.at[i], lambda i: states.at[i], x_sem, slots)
    w_copies = start_copies(
        lambda i: w_ref.at[pl.ds(i * depth, depth), :],
        lambda i: weights.at[i],
        w_sem,
        width // depth,
    )
    head_pos = place_ref[4]
    lane = lax.broadcasted_iota(jnp.int32, (1, tokens), 1)
    for slot in range(slots):
        order = jnp.full((1, tokens), -1, jnp.int32)
        start = jnp.int32(0)
        for hyp in range(hyps):
            length = length_ref[slot, hyp]
            inside = (lane >= hyp * positions) & (lane < hyp * positions + length)
            order = jnp.where(inside, lane - hyp * positions + start, order)
            start = start + length
        row = lax.broadcasted_iota(jnp.int32, (tokens, tokens), 0)
        move = jnp.where(order == row, 1.0, 0.0).astype(jnp.bfloat16)
        x_copies[slot].wait()
        ordered = dot(move, states[slot])
        normed[slot * tokens : (slot + 1) * tokens, :] = square_norm(ordered).astype(jnp.bfloat16)
        share_row = lax.broadcasted_iota(jnp.int32, (share, tokens), 0)
        chosen = order == share_row * (tokens // share) + head_pos
        mine = dot(jnp.where(chosen, 1.0, 0.0).astype(jnp.bfloat16), states[slot])
        shares[slot, :share, :] = mine.astype(jnp.bfloat16)
        target = jnp.sum(
            jnp.where(chosen, tok_ref[slot], 0), axis=1, keepdims=True, dtype=jnp.int32
        )
        coarse = target // 256
        cell = lax.broadcasted_iota(jnp.int32, (share, columns), 1)
        packed = jnp.where(cell == 0, coarse, jnp.where(cell == 1, target - coarse * 256, 0))
        shares[slot, share:, :columns] = packed.astype(jnp.float32).astype(jnp.bfloat16)
    for number in range(width // depth):
        w_copies[number].wait()
        product = dot(normed[:, number * depth : (number + 1) * depth], weights[number])
        if number == 0:
            total[...] = product
        else:
            total[...] += product
    group = place_ref[1]
    for distance in range(count):
        slot = jnp.int32(-1)
        for candidate in range(slots):
            holds = slot_ref[group * slots + candidate] == group ^ distance
            slot = jnp.where(holds, candidate, slot)
        out = outs[distance]

        @pl.when(slot < 0)
        def _(out=out):
            out[...] = jnp.zeros_like(out)

        @pl.when(slot >= 0)
        def _(out=out, slot=slot):
            start = pl.multiple_of(slot * tokens, tokens)
            out[:tokens, :] = total[pl.ds(start, tokens), :].astype(jnp.bfloat16)
            for part in range(parts):
                first = tokens + part * share
                out[first : first + share, :] = shares[
                    slot, :share, part * columns : (part + 1) * columns
                ]
            out[tokens + parts * share :, :] = shares[slot, share:, :columns]


def queries_of(place, slot_utt, lengths, after, states, targets, weights, count, share):
    slots, tokens, width = states.shape
    columns = weights.shape[1]
    depth = 1024
    rows = tokens + (width // columns + 1) * share
    block = jax.ShapeDtypeStruct((rows, columns), jnp.bfloat16)
    return pl.pallas_call(
        functools.partial(query_kernel, count, depth),
        in_specs=[SCALARS] * 3 + [ANYWHERE, ANYWHERE, INSIDE, ANYWHERE],
        out_specs=[INSIDE] * count,
        out_shape=[block] * count,
        scratch_shapes=[
            pltpu.VMEM(states.shape, jnp.bfloat16),
            pltpu.VMEM((width // depth, depth, columns), jnp.bfloat16),
            pltpu.VMEM((slots * tokens, width), jnp.bfloat16),
            pltpu.VMEM((slots * tokens, columns), jnp.float32),
            pltpu.VMEM((slots, 2 * share, width), jnp.bfloat16),
            pltpu.SemaphoreType.DMA((slots,)),
            pltpu.SemaphoreType.DMA((width // depth,)),
        ],
        cost_estimate=pl.CostEstimate(
            flops=2 * slots * tokens * width * columns,
            bytes_accessed=2 * width * (columns + slots * tokens),
            transcendentals=0,
        ),
        compiler_params=pltpu.CompilerParams(vmem_limit_bytes=32 << 20),
        name="hypothesis_queries",
    )(place, slot_utt, lengths, after, in_hbm(states), targets, in_hbm(weights))


def kv_kernel(sections, utterances, widths, *refs):
    parts_ref, own_ref, w_ref, after_ref, out_ref = refs
    rows = own_ref.shape[0]
    frames = rows // utterances
    total = own_ref[...].astype(jnp.float32)
    summed = parts_ref[0].astype(jnp.float32)
    for part in range(1, parts_ref.shape[0]):
        summed += parts_ref[part].astype(jnp.float32)
    states = layer_norm(total + summed).astype(jnp.bfloat16)
    to = lax.broadcasted_iota(jnp.int32, (rows, rows), 0)
    come = lax.broadcasted_iota(jnp.int32, (rows, rows), 1)
    move = jnp.where(come == to % frames * utterances + to // frames, 1.0, 0.0)
    states = dot(move.astype(jnp.bfloat16), states).astype(jnp.bfloat16)
    both = dot(states, w_ref[...])
    half = KVH * HD
    per_kv = sections * widths // KVH
    for section in range(sections):
        for utterance in range(utterances):
            for width in range(0, widths, per_kv):
                kv_head = (section * widths + width) // per_kv
                take = slice(utterance * frames, (utterance + 1) * frames)
                block = jnp.concatenate(
                    [
                        both[take, kv_head * HD : (kv_head + 1) * HD],
                        both[take, half + kv_head * HD : half + (kv_head + 1) * HD],
                    ],
                    axis=1,
                )
                start = ((section * utterances + utterance) * widths + width) * frames
                block = jnp.concatenate([block] * per_kv, axis=0).astype(jnp.bfloat16)
                out_ref[start : start + per_kv * frames, :] = block


def keys_values_of(parts, own, weights, after, sections, utterances, widths):
    rows = sections * widths * own.shape[0]
    return pl.pallas_call(
        functools.partial(kv_kernel, sections, utterances, widths),
        in_specs=[INSIDE] * 3 + [ANYWHERE],
        out_specs=INSIDE,
        out_shape=jax.ShapeDtypeStruct((rows, 2 * HD), jnp.bfloat16),
        cost_estimate=pl.CostEstimate(
            flops=2 * own.shape[0] * weights.shape[0] * weights.shape[1],
            bytes_accessed=2 * weights.shape[0] * weights.shape[1],
            transcendentals=0,
        ),
        compiler_params=pltpu.CompilerParams(vmem_limit_bytes=24 << 20),
        name="frame_keys_values",
    )(parts, own, weights, after)


def choice_of_payload(place_ref, slot_ref, slots):
    group = place_ref[1]
    source = jnp.int32(0)
    for slot in range(slot_ref.shape[0]):
        source = jnp.where(slot_ref[slot] == group, slot // slots, source)
    return jnp.minimum(source ^ group, 2)


def attention_kernel(count, slots, capacity, pieces, sections, widths, tile, *refs):
    place_ref, slot_ref, frame_ref = refs[:3]
    payloads, (kv_ref, w_ref) = refs[3 : 3 + count], refs[3 + count : 5 + count]
    outs = refs[5 + count : 5 + count + 2 * len(pieces)]
    weights, picked, context, w_sem = refs[5 + count + 2 * len(pieces) :]
    tokens, columns = capacity, w_ref.shape[0]
    tiles = w_ref.shape[1] // tile
    w_copies = start_copies(
        lambda i: w_ref.at[:, pl.ds(i * tile, tile)], lambda i: weights.at[i], w_sem, tiles
    )
    source = choice_of_payload(place_ref, slot_ref, slots)
    section_pos = place_ref[0]
    frame_limit = frame_ref[place_ref[1]]
    for distance in range(count):

        @pl.when(source == distance)
        def _(payload=payloads[distance]):
            picked[...] = payload[:tokens, :]

    keys = kv_ref[:, :HD]
    values = kv_ref[:, HD:]
    frames = kv_ref.shape[0]
    visible = lax.broadcasted_iota(jnp.int32, (tokens, frames), 1) < frame_limit
    for head in range(columns // HD):
        scores = dot_nt(picked[:, head * HD : (head + 1) * HD], keys) * (1.0 / math.sqrt(HD))
        scores = jnp.where(visible, scores, -jnp.inf)
        raised = jnp.exp(scores - jnp.max(scores, axis=1, keepdims=True))
        chances = (raised / jnp.sum(raised, axis=1, keepdims=True)).astype(jnp.bfloat16)
        context[:, head * HD : (head + 1) * HD] = dot(chances, values).astype(jnp.bfloat16)
    to = lax.broadcasted_iota(jnp.int32, (tokens, tokens), 0)
    come = lax.broadcasted_iota(jnp.int32, (tokens, tokens), 1)
    low_bit = place_ref[2] % 2
    size = widths * pieces[0]
    block = to % size // pieces[0]
    section = jnp.where(to < size, 1 - section_pos, section_pos)
    first_order = (to % pieces[0] * sections + section) * widths + block % 2 * 2 + block // 2
    at = to - 2 * size
    size = widths * pieces[1]
    block = at % size // pieces[1]
    low = jnp.where(at < size, 1 - low_bit, low_bit)
    row = pieces[0] + at % pieces[1]
    second_order = (row * sections + block // 2) * widths + block % 2 * 2 + low
    move = come == jnp.where(at < 0, first_order, second_order)
    ordered = dot(jnp.where(move, 1.0, 0.0).astype(jnp.bfloat16), context[...])
    ordered = ordered.astype(jnp.bfloat16)
    for number in range(tiles):
        w_copies[number].wait()
        product = dot(ordered, weights[number]).astype(jnp.bfloat16)
        first = 0
        for out in outs:
            out[:, number * tile : (number + 1) * tile] = product[first : first + out.shape[0], :]
            first += out.shape[0]


def attend(place, slot_utt, frame_len, payloads, keys_values, weights, pieces, sections, widths, slots):
    count = len(payloads)
    columns, width = weights.shape
    capacity = sum(pieces) * sections * widths
    tile = 1024
    tiles = width // tile
    shapes = [
        jax.ShapeDtypeStruct((piece * widths, width), jnp.bfloat16)
        for piece in pieces
        for _ in range(2)
    ]
    return pl.pallas_call(
        functools.partial(
            attention_kernel, count, slots, capacity, pieces, sections, widths, tile
        ),
        in_specs=[SCALARS] * 3 + [INSIDE] * (count + 1) + [ANYWHERE],
        out_specs=[INSIDE] * len(shapes),
        out_shape=shapes,
        scratch_shapes=[
            pltpu.VMEM((tiles, columns, tile), jnp.bfloat16),
            pltpu.VMEM((capacity, columns), jnp.bfloat16),
            pltpu.VMEM((capacity, columns), jnp.bfloat16),
            pltpu.SemaphoreType.DMA((tiles,)),
        ],
        cost_estimate=pl.CostEstimate(
            flops=2 * capacity * columns * (width + 2 * keys_values.shape[0]),
            bytes_accessed=2 * columns * width + 2 * capacity * width,
            transcendentals=capacity * keys_values.shape[0] * columns // HD,
        ),
        compiler_params=pltpu.CompilerParams(vmem_limit_bytes=24 << 20),
        name="attention_projection",
    )(place, slot_utt, frame_len, *payloads, keys_values, in_hbm(weights))


def fold_kernel(sides, joined, place_ref, *refs):
    count = len(sides)
    parts, outs = refs[: 2 * count], refs[2 * count :]
    first = 0
    for number, side in enumerate(sides):
        kept_ref, came_ref = parts[2 * number : 2 * number + 2]
        total = kept_ref[...].astype(jnp.float32) + came_ref[...].astype(jnp.float32)
        half = total.shape[0] // 2
        top, bottom = total[:half], total[half:]
        upper = side(place_ref) == 0
        kept = jnp.where(upper, top, bottom)
        sent = jnp.where(upper, bottom, top).astype(jnp.bfloat16)
        if joined:
            outs[0][first : first + half, :] = kept
            outs[1][first : first + half, :] = sent
            first += half
        else:
            outs[2 * number][...] = kept
            outs[2 * number + 1][...] = sent


def fold(place, parts, sides, joined):
    width = parts[0].shape[1]
    halves = [part.shape[0] // 2 for part in parts[::2]]
    if joined:
        halves = [sum(halves)]
    shapes = [
        jax.ShapeDtypeStruct((half, width), kind)
        for half in halves
        for kind in (jnp.float32, jnp.bfloat16)
    ]
    return pl.pallas_call(
        functools.partial(fold_kernel, sides, joined),
        in_specs=[SCALARS] + [INSIDE] * len(parts),
        out_specs=[INSIDE] * len(shapes),
        out_shape=shapes,
        compiler_params=pltpu.CompilerParams(vmem_limit_bytes=24 << 20),
        name="sum_phase",
    )(place, *parts)


def section_side(place_ref):
    return place_ref[0]


def low_side(place_ref):
    return place_ref[2] % 2


def high_side(place_ref):
    return place_ref[2] // 2


def norm_kernel(count, slots, tokens, place_ref, slot_ref, *refs):
    payloads, (kept, other) = refs[:count], refs[count : count + 2]
    out_ref, picked, total = refs[count + 2 :]
    rows, width = total.shape
    columns = picked.shape[1]
    share = picked.shape[0] // (width // columns + 1)
    source = choice_of_payload(place_ref, slot_ref, slots)
    for choice in range(count):

        @pl.when(source == choice)
        def _(payload=payloads[choice]):
            picked[...] = payload[tokens:, :]

    total[...] = kept[...] + other[...].astype(jnp.float32)
    for part in range(width // columns):
        take = slice(part * columns, (part + 1) * columns)
        total[:, take] += picked[part * share : part * share + rows, :].astype(jnp.float32)
    shape = out_ref.shape[:2]
    normed = square_norm(total[...]).reshape(*shape, width)
    out_ref[:, :, :width] = normed.astype(jnp.bfloat16)
    last = width // columns * share
    target = picked[last : last + rows, :LANES].astype(jnp.float32).reshape(*shape, LANES)
    out_ref[:, :, width:] = target.astype(jnp.bfloat16)


def normed_rows(place, slot_utt, payloads, blocks, tokens, slots):
    width = blocks[0].shape[1]
    rows = blocks[0].shape[0]
    columns = payloads[0].shape[1]
    return pl.pallas_call(
        functools.partial(norm_kernel, len(payloads), slots, tokens),
        in_specs=[SCALARS] * 2 + [INSIDE] * (len(payloads) + len(blocks)),
        out_specs=INSIDE,
        out_shape=jax.ShapeDtypeStruct((rows // FOLD, FOLD, width + LANES), jnp.bfloat16),
        scratch_shapes=[
            pltpu.VMEM((payloads[0].shape[0] - tokens, columns), jnp.bfloat16),
            pltpu.VMEM((rows, width), jnp.float32),
        ],
        compiler_params=pltpu.CompilerParams(vmem_limit_bytes=16 << 20),
        name="token_rows",
    )(place, slot_utt, *payloads, *blocks)


def vocabulary_kernel(tile, count, first_ref, *refs):
    sets, (head_ref, out_ref, zero_ref, rows_ref, stat) = refs[:count], refs[count:]
    zero_ref[0] = 0
    vocab_rows, width = head_ref.shape
    share = sets[0].shape[0] * FOLD
    tokens = share * len(sets)
    cell = lax.broadcasted_iota(jnp.int32, (8, LANES), 1)
    take = jnp.where(cell == 0, 256.0, jnp.where(cell == 1, 1.0, 0.0)).astype(jnp.bfloat16)
    for number, rows in enumerate(sets):
        flat = rows[...].astype(jnp.float32).reshape(share, width + LANES)
        rows_ref[number * share : (number + 1) * share, :] = flat.astype(jnp.bfloat16)
    target = dot_nt(take, rows_ref[:, width:])[0:1, :].astype(jnp.int32) - first_ref[3]
    stat[0:1, :] = jnp.full((1, tokens), -jnp.inf, jnp.float32)
    stat[8:9, :] = jnp.zeros((1, tokens), jnp.float32)
    stat[16:17, :] = jnp.zeros((1, tokens), jnp.float32)

    @pl.loop(0, vocab_rows // tile)
    def _(step):
        start = pl.multiple_of(step * tile, tile)
        logits = dot_nt(head_ref[pl.ds(start, tile), :], rows_ref[:, :width])
        vocab = lax.broadcasted_iota(jnp.int32, logits.shape, 0) + start
        before = stat[0:1, :]
        upper = jnp.maximum(before, jnp.max(logits, axis=0, keepdims=True))
        stat[8:9, :] = stat[8:9, :] * jnp.exp(before - upper) + jnp.sum(
            jnp.exp(logits - upper), axis=0, keepdims=True
        )
        stat[16:17, :] += jnp.sum(jnp.where(vocab == target, logits, 0.0), axis=0, keepdims=True)
        stat[0:1, :] = upper

    for number in range(len(sets)):
        for row in range(3):
            out_ref[number, row : row + 1, :] = stat[
                8 * row : 8 * row + 1, number * share : (number + 1) * share
            ]


def vocabulary_stats(place, sets, head):
    share = sets[0].shape[0] * FOLD
    count = len(sets)
    width = head.shape[1]
    tokens = share * count
    return pl.pallas_call(
        functools.partial(vocabulary_kernel, head.shape[0] // 2, count),
        in_specs=[SCALARS] + [INSIDE] * (count + 1),
        out_specs=[INSIDE, SCALARS],
        out_shape=[
            jax.ShapeDtypeStruct((count, 8, share), jnp.float32),
            jax.ShapeDtypeStruct((1,), jnp.int32),
        ],
        scratch_shapes=[
            pltpu.VMEM((tokens, width + LANES), jnp.bfloat16),
            pltpu.VMEM((24, tokens), jnp.float32),
        ],
        cost_estimate=pl.CostEstimate(
            flops=3 * tokens * head.shape[0] * width,
            bytes_accessed=2 * tokens * width,
            transcendentals=tokens * head.shape[0],
        ),
        compiler_params=pltpu.CompilerParams(vmem_limit_bytes=16 << 20),
        name="vocabulary_scores",
    )(place, *sets, pltpu.with_memory_space_constraint(head, pltpu.VMEM))


def spread_kernel(sections, groups, widths, place_ref, slot_ref, *refs):
    stats, (out_ref, table, block) = refs[:-3], refs[-3:]
    share = table.shape[2]
    first = 0
    for stat in stats:
        table[first : first + stat.shape[0]] = stat[...]
        first += stat.shape[0]
    slots = slot_ref.shape[0] // groups
    block[...] = jnp.zeros_like(block)
    for group in range(groups):
        for slot in range(slots):
            utterance = jnp.maximum(slot_ref[group * slots + slot], 0)
            for section in range(sections):
                at = (section ^ place_ref[0]) * groups + (utterance ^ place_ref[1])
                block[group, 3 * slot : 3 * slot + 3, section * share : (section + 1) * share] = (
                    table[at][0:3, :]
                )
    for section in range(sections):
        for group in range(groups):
            for width in range(widths):
                out_ref[(section * groups + group) * widths + width] = block[group]


def spread_stats(place, slot_utt, stats, sections, groups, widths):
    share = stats[0].shape[2]
    assert 3 * slot_utt.shape[0] // groups <= 8
    return pl.pallas_call(
        functools.partial(spread_kernel, sections, groups, widths),
        in_specs=[SCALARS] * 2 + [INSIDE] * len(stats),
        out_specs=INSIDE,
        out_shape=jax.ShapeDtypeStruct(
            (sections * groups * widths, 8, sections * share), jnp.float32
        ),
        scratch_shapes=[
            pltpu.VMEM((sections * groups, 8, share), jnp.float32),
            pltpu.VMEM((groups, 8, sections * share), jnp.float32),
        ],
        compiler_params=pltpu.CompilerParams(vmem_limit_bytes=16 << 20),
        name="statistics_by_group",
    )(place, slot_utt, *stats)


def score_kernel(sections, widths, place_ref, slot_ref, length_ref, every_ref, out_ref):
    slots, hyps = out_ref.shape
    lanes = every_ref.shape[2]
    share = lanes // sections // widths
    lane = lax.broadcasted_iota(jnp.int32, (1, lanes), 1)
    order = lane % share * (sections * widths) + lane // share
    column = lax.broadcasted_iota(jnp.int32, (1, hyps), 1)
    for slot in range(slots):
        upper = every_ref[:, 3 * slot, :]
        peak = jnp.max(upper, axis=0, keepdims=True)
        total = jnp.sum(
            every_ref[:, 3 * slot + 1, :] * jnp.exp(upper - peak), axis=0, keepdims=True
        )
        picked = jnp.sum(every_ref[:, 3 * slot + 2, :], axis=0, keepdims=True)
        logp = picked - (peak + jnp.log(total))
        scores = jnp.zeros((1, hyps), jnp.float32)
        start = jnp.int32(0)
        for hyp in range(hyps):
            length = length_ref[slot, hyp]
            valid = (order >= start) & (order < start + length)
            summed = jnp.sum(jnp.where(valid, logp, 0.0), axis=1, keepdims=True)
            mean = summed / jnp.full((1, 1), length, jnp.int32).astype(jnp.float32)
            scores = jnp.where(column == hyp, mean + math.log(V), scores)
            start = start + length
        filled = slot_ref[place_ref[1] * slots + slot] >= 0
        out_ref[slot : slot + 1, :] = jnp.where(filled, scores, 0.0)


def hypothesis_scores(place, slot_utt, lengths, every, slots, hyps, sections, widths):
    return pl.pallas_call(
        functools.partial(score_kernel, sections, widths),
        in_specs=[SCALARS] * 3 + [INSIDE],
        out_specs=INSIDE,
        out_shape=jax.ShapeDtypeStruct((slots, hyps), jnp.float32),
        compiler_params=pltpu.CompilerParams(vmem_limit_bytes=16 << 20),
        name="hypothesis_scores",
    )(place, slot_utt, lengths, every)


def rest(pieces, slot_tokens, place, slot_utt, frame_len, hyp_len, payloads, keys_values, o_proj, head):
    section_count = lax.axis_size("section")
    group_count = lax.axis_size("tm")
    width_count = lax.axis_size("mp")
    section_pos = lax.axis_index("section")
    width_pos = lax.axis_index("mp")
    slot_count, hyp_count = hyp_len.shape
    projected = attend(
        place,
        slot_utt,
        frame_len,
        payloads,
        keys_values,
        o_proj,
        pieces,
        section_count,
        width_count,
        slot_count,
    )

    kept, sent, other_kept, other_sent = fold(
        place,
        [projected[1], swap(projected[0], "section", 1), projected[3], swap(projected[2], "mp", 1)],
        [low_side, section_side],
        False,
    )
    kept, sent = fold(
        place,
        [kept, swap(sent, "mp", 1), other_kept, swap(other_sent, "section", 1)],
        [high_side, high_side],
        True,
    )
    out_rows = normed_rows(
        place, slot_utt, payloads, [kept, swap(sent, "mp", 2)], slot_tokens, slot_count
    )

    own = jnp.zeros((width_count, *out_rows.shape), jnp.bfloat16)
    for distance in range(width_count):
        block = swap(out_rows, "mp", distance) if distance else out_rows
        own = lax.dynamic_update_index_in_dim(own, block, width_pos ^ distance, 0)
    own = own.reshape(-1, *out_rows.shape[1:])
    half = own.shape[0] // 2
    by_x = swap(own, "section", 1)
    by_y = swap(own, "tm", 2)
    first, zero = vocabulary_stats(place, [own, swap(own, "tm", 1)], head)
    across = [
        swap(lax.dynamic_slice_in_dim(by_x, zero[0], half, 0), "tm", 2),
        swap(lax.dynamic_slice_in_dim(by_y, zero[0] + half, half, 0), "section", 1),
    ]
    second, _ = vocabulary_stats(
        place, [by_y, swap(by_y, "tm", 1), by_x, swap(by_x, "tm", 1)], head
    )
    across = jnp.concatenate(across)
    third, _ = vocabulary_stats(place, [across, swap(across, "tm", 1)], head)
    stats = [first, second, third]

    every = exchange(
        spread_stats(place, slot_utt, stats, section_count, group_count, width_count), ALL
    )
    return hypothesis_scores(
        place, slot_utt, hyp_len, every, slot_count, hyp_count, section_count, width_count
    )


def near_device(
    frame_len,
    slot_utt,
    enc_in,
    ffn_up,
    ffn_down,
    kv_proj,
    hyp_state,
    hyp_tok,
    hyp_len,
    q_proj,
    o_proj,
    head,
):
    section_count = lax.axis_size("section")
    group_count = lax.axis_size("tm")
    width_count = lax.axis_size("mp")
    section_pos = lax.axis_index("section")
    group_pos = lax.axis_index("tm")
    width_pos = lax.axis_index("mp")
    head_devices = section_count * width_count
    all_devices = head_devices * group_count

    frame_rows, utterances, enc_width = enc_in.shape
    slot_count, hyp_count, positions, model_width = hyp_state.shape
    slot_tokens = hyp_count * positions
    share_rows = slot_tokens // head_devices
    vocab_start = (
        (section_pos * group_count + group_pos) * width_count + width_pos
    ) * head.shape[0]
    head_pos = section_pos * width_count + width_pos
    place = jnp.stack([section_pos, group_pos, width_pos, vocab_start, head_pos])
    place = place.astype(jnp.int32)

    parts, own_frames = ffn(place, enc_in, ffn_up, ffn_down, width_count)
    parts = exchange(parts, "mp")

    blocks = queries_of(
        place,
        slot_utt,
        hyp_len,
        place,
        hyp_state.reshape(slot_count, slot_tokens, model_width),
        hyp_tok.reshape(slot_count, 1, slot_tokens),
        q_proj,
        group_count,
        share_rows,
    )
    crossing = blocks[2] + swap(blocks[3], "tm", 1)
    payloads = [blocks[0], swap(blocks[1], "tm", 1), swap(crossing, "tm", 2)]

    sent = keys_values_of(
        parts, own_frames, kv_proj, blocks[0], section_count, utterances, width_count
    )
    frames_all = all_devices * (frame_rows // width_count)
    keys_values = exchange(sent.reshape(all_devices, -1, 2 * HD), ALL).reshape(frames_all, 2 * HD)

    here_slots = lax.dynamic_slice_in_dim(slot_utt, group_pos * slot_count, slot_count, 0)
    filled = jnp.where(here_slots >= 0, jnp.sum(hyp_len, axis=1), 0)
    count = jnp.max(filled).reshape(1)
    most = count
    for distance in range(1, group_count):
        most = jnp.maximum(most, swap(count, "tm", distance))
    operands = (place, slot_utt, frame_len, hyp_len, payloads, keys_values, o_proj, head)
    few = share_rows * 3 // 4
    return lax.cond(
        most[0] <= few * head_devices,
        functools.partial(rest, (few - few // 3, few // 3), slot_tokens),
        functools.partial(rest, (share_rows // 2, share_rows - share_rows // 2), slot_tokens),
        *operands,
    )


def general(
    frame_len,
    slot_utt,
    enc_in,
    ffn_up,
    ffn_down,
    kv_proj,
    hyp_state,
    hyp_tok,
    hyp_len,
    q_proj,
    o_proj,
    head,
):
    section_count = lax.axis_size("section")
    group_count = lax.axis_size("tm")
    width_count = lax.axis_size("mp")
    section_pos = lax.axis_index("section")
    group_pos = lax.axis_index("tm")
    width_pos = lax.axis_index("mp")
    head_devices = section_count * width_count
    head_pos = section_pos * width_count + width_pos
    all_devices = head_devices * group_count

    frame_rows, utterances, enc_width = enc_in.shape
    assert utterances == group_count
    slot_count, hyp_count, positions, model_width = hyp_state.shape
    slot_tokens = hyp_count * positions
    device_heads = q_proj.shape[1] // HD
    group_heads = NH // KVH
    frame_share = frame_rows // width_count
    share_rows = slot_tokens // head_devices
    here_slots = lax.dynamic_slice_in_dim(slot_utt, group_pos * slot_count, slot_count, 0)

    dec_rows = hyp_state.reshape(slot_count * slot_tokens, model_width).astype(jnp.float32)
    queries = jnp.dot(
        square_norm(dec_rows).astype(jnp.bfloat16), q_proj, preferred_element_type=jnp.float32
    ).astype(jnp.bfloat16)
    queries = queries.reshape(slot_count, slot_tokens, device_heads * HD)
    shares = lax.dynamic_slice_in_dim(
        hyp_state.reshape(slot_count, slot_tokens, model_width), head_pos * share_rows, share_rows, 1
    )

    def by_utterance(values):
        out = []
        for utterance in range(utterances):
            block = values[0]
            for slot in range(1, slot_count):
                block = jnp.where(here_slots[slot] == utterance, values[slot], block)
            out.append(block)
        return jnp.stack(out)

    own_slot = jnp.argmax(slot_utt == group_pos)
    from_group = own_slot // slot_count
    queries = lax.dynamic_index_in_dim(
        exchange(by_utterance(queries), "tm"), from_group, 0, keepdims=False
    )
    resid_rows = lax.dynamic_index_in_dim(
        exchange(by_utterance(shares), "tm"), from_group, 0, keepdims=False
    )
    slot_targets = lax.all_gather(
        hyp_tok.reshape(slot_count, slot_tokens), "tm", axis=0, tiled=True
    )
    utt_slots = jnp.argmax(slot_utt[None, :] == jnp.arange(utterances)[:, None], axis=1)
    targets = jnp.take(slot_targets, utt_slots, axis=0).reshape(utterances * slot_tokens)

    enc_flat = (
        enc_in.reshape(width_count, frame_share, utterances, enc_width)
        .transpose(0, 2, 1, 3)
        .reshape(frame_rows * utterances, enc_width)
    )
    share_count = frame_share * utterances
    enc_normed = layer_norm(enc_flat.astype(jnp.float32)).astype(jnp.bfloat16)
    enc_inner = jax.nn.gelu(
        jnp.dot(enc_normed, ffn_up, preferred_element_type=jnp.float32), approximate=False
    ).astype(jnp.bfloat16)
    enc_summed = scatter_sum(
        jnp.dot(enc_inner, ffn_down, preferred_element_type=jnp.float32).astype(jnp.bfloat16),
        "mp",
        width_count,
    )
    own_frames = lax.dynamic_slice_in_dim(enc_flat, width_pos * share_count, share_count, 0)
    enc_states = layer_norm(own_frames.astype(jnp.float32) + enc_summed).astype(jnp.bfloat16)
    keys_values = jnp.dot(enc_states, kv_proj, preferred_element_type=jnp.float32).astype(
        jnp.bfloat16
    )
    keys_values = keys_values.reshape(utterances, frame_share, 2, KVH, HD)
    sent = []
    for section in range(section_count):
        per_width = []
        for width in range(width_count):
            kv_head = (section * width_count + width) * device_heads // group_heads
            per_width.append(
                keys_values[:, :, :, kv_head].reshape(utterances, frame_share, 2 * HD)
            )
        sent.append(jnp.stack(per_width, axis=1))
    sent = jnp.stack(sent).reshape(all_devices, frame_share, 2 * HD)
    frames_all = all_devices * frame_share
    keys_values = exchange(sent, ALL).reshape(frames_all, 2 * HD)

    frame_limit = lax.dynamic_index_in_dim(frame_len, group_pos, 0, keepdims=False)
    queries = queries.reshape(slot_tokens, device_heads, HD)
    scores = jnp.einsum(
        "qhd,fd->hqf", queries, keys_values[:, :HD], preferred_element_type=jnp.float32
    ) / math.sqrt(HD)
    visible = jnp.arange(frames_all, dtype=jnp.int32) < frame_limit
    scores = jnp.where(visible[None, None, :], scores, -jnp.inf)
    weights = jax.nn.softmax(scores, axis=-1).astype(jnp.bfloat16)
    context = jnp.einsum(
        "hqf,fd->qhd", weights, keys_values[:, HD:], preferred_element_type=jnp.float32
    ).astype(jnp.bfloat16)
    partial = jnp.dot(
        context.reshape(slot_tokens, device_heads * HD), o_proj, preferred_element_type=jnp.float32
    ).astype(jnp.bfloat16)
    partial = scatter_sum(partial, "section", section_count).astype(jnp.bfloat16)
    attn_out = scatter_sum(partial, "mp", width_count)
    out_normed = square_norm(resid_rows.astype(jnp.float32) + attn_out).astype(jnp.bfloat16)

    hidden_rows = lax.all_gather(out_normed, ALL, axis=0, tiled=True)
    logits = lax.dot_general(
        hidden_rows, head, (((1,), (1,)), ((), ())), preferred_element_type=jnp.float32
    )
    vocab_rows = head.shape[0]
    vocab_start = (
        (section_pos * group_count + group_pos) * width_count + width_pos
    ) * vocab_rows
    target_rows = (
        targets.reshape(utterances, section_count, width_count, share_rows)
        .transpose(1, 0, 2, 3)
        .reshape(-1)
    )
    upper = jnp.max(logits, axis=1)
    totals = jnp.sum(jnp.exp(logits - upper[:, None]), axis=1)
    matches = (
        jnp.arange(vocab_rows, dtype=jnp.int32)[None, :] == (target_rows - vocab_start)[:, None]
    )
    target_logit = jnp.sum(jnp.where(matches, logits, 0.0), axis=1)

    stats = jnp.stack([upper, totals, target_logit])
    stats = stats.reshape(3, section_count, utterances, width_count, share_rows)
    stats = stats.transpose(2, 0, 1, 3, 4).reshape(utterances, 3, slot_tokens)
    by_slot = jnp.take(stats, jnp.maximum(slot_utt, 0), axis=0)
    by_group = by_slot.reshape(1, group_count, 1, slot_count, 3, slot_tokens)
    by_group = jnp.broadcast_to(
        by_group, (section_count, group_count, width_count, slot_count, 3, slot_tokens)
    ).reshape(all_devices, slot_count, 3, slot_tokens)
    every = exchange(by_group, ALL)
    peak = jnp.max(every[:, :, 0], axis=0)
    total = jnp.sum(every[:, :, 1] * jnp.exp(every[:, :, 0] - peak[None]), axis=0)
    picked = jnp.sum(every[:, :, 2], axis=0)
    token_logp = (picked - (peak + jnp.log(total))).reshape(slot_count, hyp_count, positions)
    valid = jnp.arange(positions, dtype=jnp.int32)[None, None, :] < hyp_len[:, :, None]
    summed = jnp.sum(jnp.where(valid, token_logp, 0.0), axis=-1) / hyp_len.astype(
        jnp.float32
    ) + math.log(V)
    return jnp.where(here_slots[:, None] >= 0, summed, 0.0)


def solution(mesh):
    in_specs = (
        P(),
        P(),
        P(("section", "tm"), None, None),
        P(None, "mp"),
        P("mp", None),
        P(),
        P("tm", None, None, None),
        P("tm", None, None),
        P("tm", None),
        P(None, ("section", "mp")),
        P(("section", "mp"), None),
        P(("section", "tm", "mp"), None),
    )
    out_specs = P("tm", None)
    near = dict(mesh.shape) == {"section": 2, "tm": 4, "mp": 4}
    per_device = near_device if near else general
    return jax.shard_map(
        per_device, mesh=mesh, in_specs=in_specs, out_specs=out_specs, check_vma=False
    )
```

```python
import functools
import math

import jax
import jax.numpy as jnp
from jax import lax
from jax.experimental import pallas as pl
from jax.experimental.pallas import tpu as pltpu
from jax.sharding import PartitionSpec as P

NH = 32
KVH = 4
HD = 128
V = 64000
ALL = ("section", "tm", "mp")
LANES = 128
FOLD = 4


def layer_norm(values):
    center = values - jnp.mean(values, axis=-1, keepdims=True)
    spread = jnp.mean(center * center, axis=-1, keepdims=True)
    return center * lax.rsqrt(spread + 1e-05)


def square_norm(values):
    return values * lax.rsqrt(jnp.mean(values * values, axis=-1, keepdims=True) + 1e-06)


def exchange(blocks, axis):
    return lax.all_to_all(blocks, axis, split_axis=0, concat_axis=0, tiled=True)


def scatter_sum(partial, axis, count):
    blocks = partial.reshape((count, partial.shape[0] // count) + partial.shape[1:])
    return jnp.sum(exchange(blocks, axis).astype(jnp.float32), axis=0)


def swap(values, axis, distance):
    pairs = [(i, i ^ distance) for i in range(lax.axis_size(axis))]
    return lax.ppermute(values, axis, pairs)


def whole(shape):
    return pl.BlockSpec(shape, lambda *_: (0,) * len(shape))


SCALARS = pl.BlockSpec(memory_space=pltpu.SMEM)


def dot(left, right):
    return jnp.dot(left, right, preferred_element_type=jnp.float32)


def dot_nt(left, right):
    return lax.dot_general(
        left, right, (((1,), (1,)), ((), ())), preferred_element_type=jnp.float32
    )


def start_copies(source_of, target_of, semaphores, count):
    copies = []
    for number in range(count):
        copy = pltpu.make_async_copy(
            source_of(number), target_of(number), semaphores.at[number]
        )
        copy.start()
        copies.append(copy)
    return copies


def ffn_kernel(tile, place_ref, x_ref, up_ref, down_ref, *refs):
    out_ref, own_ref, inputs, rows, up, down, x_sem, up_sem, down_sem = refs
    count, share, width = out_ref.shape
    tiles = up_ref.shape[1] // tile
    x_copy = start_copies(lambda i: x_ref, lambda i: inputs, x_sem, 1)[0]
    up_copies = start_copies(
        lambda i: up_ref.at[:, pl.ds(i * tile, tile)], lambda i: up.at[i], up_sem, tiles
    )
    x_copy.wait()
    rows[...] = inputs[...].astype(jnp.float32).reshape(rows.shape)
    start = pl.multiple_of(place_ref[2] * share, share)
    own_ref[...] = rows[pl.ds(start, share), :].astype(jnp.bfloat16)
    normed = layer_norm(rows[...]).astype(jnp.bfloat16)
    inner = []
    for number in range(tiles):
        up_copies[number].wait()
        if number == 0:
            down_copies = start_copies(
                lambda i: down_ref.at[pl.ds(i * tile, tile), :],
                lambda i: down.at[i],
                down_sem,
                tiles,
            )
        hidden = dot(normed, up[number])
        hidden = 0.5 * hidden * (1.0 + lax.erf(hidden * math.sqrt(0.5)))
        inner.append(hidden.astype(jnp.bfloat16))
    total = None
    for number in range(tiles):
        down_copies[number].wait()
        product = dot(inner[number], down[number])
        total = product if total is None else total + product
    for part in range(count):
        out_ref[part] = total[part * share : (part + 1) * share, :].astype(jnp.bfloat16)


def in_hbm(values):
    return pltpu.with_memory_space_constraint(values, pltpu.HBM)


ANYWHERE = pl.BlockSpec(memory_space=pl.ANY)
INSIDE = pl.BlockSpec(memory_space=pltpu.VMEM)


def ffn(place, enc_in, up, down, count):
    frames, utterances, width = enc_in.shape
    rows = frames * utterances
    share = rows // count
    tile = 256
    tiles = up.shape[1] // tile
    return pl.pallas_call(
        functools.partial(ffn_kernel, tile),
        in_specs=[SCALARS] + [ANYWHERE] * 3,
        out_specs=[INSIDE] * 2,
        out_shape=[
            jax.ShapeDtypeStruct((count, share, width), jnp.bfloat16),
            jax.ShapeDtypeStruct((share, width), jnp.bfloat16),
        ],
        scratch_shapes=[
            pltpu.VMEM(enc_in.shape, jnp.bfloat16),
            pltpu.VMEM((rows, width), jnp.float32),
            pltpu.VMEM((tiles, width, tile), jnp.bfloat16),
            pltpu.VMEM((tiles, tile, width), jnp.bfloat16),
            pltpu.SemaphoreType.DMA((1,)),
            pltpu.SemaphoreType.DMA((tiles,)),
            pltpu.SemaphoreType.DMA((tiles,)),
        ],
        cost_estimate=pl.CostEstimate(
            flops=4 * rows * width * up.shape[1],
            bytes_accessed=4 * width * up.shape[1],
            transcendentals=rows * up.shape[1],
        ),
        compiler_params=pltpu.CompilerParams(vmem_limit_bytes=24 << 20),
        name="encoder_ffn",
    )(place, in_hbm(enc_in), in_hbm(up), in_hbm(down))


def query_kernel(
    count, depth, place_ref, slot_ref, length_ref, after_ref, x_ref, tok_ref, w_ref, *refs
):
    outs, (states, weights, normed, total, shares, x_sem, w_sem) = refs[:count], refs[count:]
    slots, tokens, width = x_ref.shape
    hyps = length_ref.shape[1]
    positions = tokens // hyps
    columns = w_ref.shape[1]
    share = shares.shape[1] // 2
    parts = width // columns
    x_copies = start_copies(lambda i: x_ref.at[i], lambda i: states.at[i], x_sem, slots)
    w_copies = start_copies(
        lambda i: w_ref.at[pl.ds(i * depth, depth), :],
        lambda i: weights.at[i],
        w_sem,
        width // depth,
    )
    head_pos = place_ref[4]
    lane = lax.broadcasted_iota(jnp.int32, (1, tokens), 1)
    for slot in range(slots):
        order = jnp.full((1, tokens), -1, jnp.int32)
        start = jnp.int32(0)
        for hyp in range(hyps):
            length = length_ref[slot, hyp]
            inside = (lane >= hyp * positions) & (lane < hyp * positions + length)
            order = jnp.where(inside, lane - hyp * positions + start, order)
            start = start + length
        row = lax.broadcasted_iota(jnp.int32, (tokens, tokens), 0)
        move = jnp.where(order == row, 1.0, 0.0).astype(jnp.bfloat16)
        x_copies[slot].wait()
        ordered = dot(move, states[slot])
        normed[slot * tokens : (slot + 1) * tokens, :] = square_norm(ordered).astype(jnp.bfloat16)
        share_row = lax.broadcasted_iota(jnp.int32, (share, tokens), 0)
        chosen = order == share_row * (tokens // share) + head_pos
        mine = dot(jnp.where(chosen, 1.0, 0.0).astype(jnp.bfloat16), states[slot])
        shares[slot, :share, :] = mine.astype(jnp.bfloat16)
        target = jnp.sum(
            jnp.where(chosen, tok_ref[slot], 0), axis=1, keepdims=True, dtype=jnp.int32
        )
        coarse = target // 256
        cell = lax.broadcasted_iota(jnp.int32, (share, columns), 1)
        packed = jnp.where(cell == 0, coarse, jnp.where(cell == 1, target - coarse * 256, 0))
        shares[slot, share:, :columns] = packed.astype(jnp.float32).astype(jnp.bfloat16)
    for number in range(width // depth):
        w_copies[number].wait()
        product = dot(normed[:, number * depth : (number + 1) * depth], weights[number])
        if number == 0:
            total[...] = product
        else:
            total[...] += product
    group = place_ref[1]
    for distance in range(count):
        slot = jnp.int32(-1)
        for candidate in range(slots):
            holds = slot_ref[group * slots + candidate] == group ^ distance
            slot = jnp.where(holds, candidate, slot)
        out = outs[distance]

        @pl.when(slot < 0)
        def _(out=out):
            out[...] = jnp.zeros_like(out)

        @pl.when(slot >= 0)
        def _(out=out, slot=slot):
            start = pl.multiple_of(slot * tokens, tokens)
            out[:tokens, :] = total[pl.ds(start, tokens), :].astype(jnp.bfloat16)
            for part in range(parts):
                first = tokens + part * share
                out[first : first + share, :] = shares[
                    slot, :share, part * columns : (part + 1) * columns
                ]
            out[tokens + parts * share :, :] = shares[slot, share:, :columns]


def queries_of(place, slot_utt, lengths, after, states, targets, weights, count, share):
    slots, tokens, width = states.shape
    columns = weights.shape[1]
    depth = 1024
    rows = tokens + (width // columns + 1) * share
    block = jax.ShapeDtypeStruct((rows, columns), jnp.bfloat16)
    return pl.pallas_call(
        functools.partial(query_kernel, count, depth),
        in_specs=[SCALARS] * 3 + [ANYWHERE, ANYWHERE, INSIDE, ANYWHERE],
        out_specs=[INSIDE] * count,
        out_shape=[block] * count,
        scratch_shapes=[
            pltpu.VMEM(states.shape, jnp.bfloat16),
            pltpu.VMEM((width // depth, depth, columns), jnp.bfloat16),
            pltpu.VMEM((slots * tokens, width), jnp.bfloat16),
            pltpu.VMEM((slots * tokens, columns), jnp.float32),
            pltpu.VMEM((slots, 2 * share, width), jnp.bfloat16),
            pltpu.SemaphoreType.DMA((slots,)),
            pltpu.SemaphoreType.DMA((width // depth,)),
        ],
        cost_estimate=pl.CostEstimate(
            flops=2 * slots * tokens * width * columns,
            bytes_accessed=2 * width * (columns + slots * tokens),
            transcendentals=0,
        ),
        compiler_params=pltpu.CompilerParams(vmem_limit_bytes=32 << 20),
        name="hypothesis_queries",
    )(place, slot_utt, lengths, after, in_hbm(states), targets, in_hbm(weights))


def kv_kernel(sections, utterances, widths, *refs):
    parts_ref, own_ref, w_ref, after_ref, out_ref = refs
    rows = own_ref.shape[0]
    frames = rows // utterances
    total = own_ref[...].astype(jnp.float32)
    summed = parts_ref[0].astype(jnp.float32)
    for part in range(1, parts_ref.shape[0]):
        summed += parts_ref[part].astype(jnp.float32)
    states = layer_norm(total + summed).astype(jnp.bfloat16)
    to = lax.broadcasted_iota(jnp.int32, (rows, rows), 0)
    come = lax.broadcasted_iota(jnp.int32, (rows, rows), 1)
    move = jnp.where(come == to % frames * utterances + to // frames, 1.0, 0.0)
    states = dot(move.astype(jnp.bfloat16), states).astype(jnp.bfloat16)
    both = dot(states, w_ref[...])
    half = KVH * HD
    per_kv = sections * widths // KVH
    for section in range(sections):
        for utterance in range(utterances):
            for width in range(0, widths, per_kv):
                kv_head = (section * widths + width) // per_kv
                take = slice(utterance * frames, (utterance + 1) * frames)
                block = jnp.concatenate(
                    [
                        both[take, kv_head * HD : (kv_head + 1) * HD],
                        both[take, half + kv_head * HD : half + (kv_head + 1) * HD],
                    ],
                    axis=1,
                )
                start = ((section * utterances + utterance) * widths + width) * frames
                block = jnp.concatenate([block] * per_kv, axis=0).astype(jnp.bfloat16)
                out_ref[start : start + per_kv * frames, :] = block


def keys_values_of(parts, own, weights, after, sections, utterances, widths):
    rows = sections * widths * own.shape[0]
    return pl.pallas_call(
        functools.partial(kv_kernel, sections, utterances, widths),
        in_specs=[INSIDE] * 3 + [ANYWHERE],
        out_specs=INSIDE,
        out_shape=jax.ShapeDtypeStruct((rows, 2 * HD), jnp.bfloat16),
        cost_estimate=pl.CostEstimate(
            flops=2 * own.shape[0] * weights.shape[0] * weights.shape[1],
            bytes_accessed=2 * weights.shape[0] * weights.shape[1],
            transcendentals=0,
        ),
        compiler_params=pltpu.CompilerParams(vmem_limit_bytes=24 << 20),
        name="frame_keys_values",
    )(parts, own, weights, after)


def choice_of_payload(place_ref, slot_ref, slots):
    group = place_ref[1]
    source = jnp.int32(0)
    for slot in range(slot_ref.shape[0]):
        source = jnp.where(slot_ref[slot] == group, slot // slots, source)
    return jnp.minimum(source ^ group, 2)


def attention_kernel(count, slots, capacity, pieces, sections, widths, tile, *refs):
    place_ref, slot_ref, frame_ref = refs[:3]
    payloads, (kv_ref, w_ref) = refs[3 : 3 + count], refs[3 + count : 5 + count]
    outs = refs[5 + count : 5 + count + 2 * len(pieces)]
    weights, picked, context, w_sem = refs[5 + count + 2 * len(pieces) :]
    tokens, columns = capacity, w_ref.shape[0]
    tiles = w_ref.shape[1] // tile
    w_copies = start_copies(
        lambda i: w_ref.at[:, pl.ds(i * tile, tile)], lambda i: weights.at[i], w_sem, tiles
    )
    source = choice_of_payload(place_ref, slot_ref, slots)
    section_pos = place_ref[0]
    frame_limit = frame_ref[place_ref[1]]
    for distance in range(count):

        @pl.when(source == distance)
        def _(payload=payloads[distance]):
            picked[...] = payload[:tokens, :]

    keys = kv_ref[:, :HD]
    values = kv_ref[:, HD:]
    frames = kv_ref.shape[0]
    visible = lax.broadcasted_iota(jnp.int32, (tokens, frames), 1) < frame_limit
    for head in range(columns // HD):
        scores = dot_nt(picked[:, head * HD : (head + 1) * HD], keys) * (1.0 / math.sqrt(HD))
        scores = jnp.where(visible, scores, -jnp.inf)
        raised = jnp.exp(scores - jnp.max(scores, axis=1, keepdims=True))
        chances = (raised / jnp.sum(raised, axis=1, keepdims=True)).astype(jnp.bfloat16)
        context[:, head * HD : (head + 1) * HD] = dot(chances, values).astype(jnp.bfloat16)
    to = lax.broadcasted_iota(jnp.int32, (tokens, tokens), 0)
    come = lax.broadcasted_iota(jnp.int32, (tokens, tokens), 1)
    low_bit = place_ref[2] % 2
    size = widths * pieces[0]
    block = to % size // pieces[0]
    section = jnp.where(to < size, 1 - section_pos, section_pos)
    first_order = (to % pieces[0] * sections + section) * widths + block % 2 * 2 + block // 2
    at = to - 2 * size
    size = widths * pieces[1]
    block = at % size // pieces[1]
    low = jnp.where(at < size, 1 - low_bit, low_bit)
    row = pieces[0] + at % pieces[1]
    second_order = (row * sections + block // 2) * widths + block % 2 * 2 + low
    move = come == jnp.where(at < 0, first_order, second_order)
    ordered = dot(jnp.where(move, 1.0, 0.0).astype(jnp.bfloat16), context[...])
    ordered = ordered.astype(jnp.bfloat16)
    for number in range(tiles):
        w_copies[number].wait()
        product = dot(ordered, weights[number]).astype(jnp.bfloat16)
        first = 0
        for out in outs:
            out[:, number * tile : (number + 1) * tile] = product[first : first + out.shape[0], :]
            first += out.shape[0]


def attend(place, slot_utt, frame_len, payloads, keys_values, weights, pieces, sections, widths, slots):
    count = len(payloads)
    columns, width = weights.shape
    capacity = sum(pieces) * sections * widths
    tile = 1024
    tiles = width // tile
    shapes = [
        jax.ShapeDtypeStruct((piece * widths, width), jnp.bfloat16)
        for piece in pieces
        for _ in range(2)
    ]
    return pl.pallas_call(
        functools.partial(
            attention_kernel, count, slots, capacity, pieces, sections, widths, tile
        ),
        in_specs=[SCALARS] * 3 + [INSIDE] * (count + 1) + [ANYWHERE],
        out_specs=[INSIDE] * len(shapes),
        out_shape=shapes,
        scratch_shapes=[
            pltpu.VMEM((tiles, columns, tile), jnp.bfloat16),
            pltpu.VMEM((capacity, columns), jnp.bfloat16),
            pltpu.VMEM((capacity, columns), jnp.bfloat16),
            pltpu.SemaphoreType.DMA((tiles,)),
        ],
        cost_estimate=pl.CostEstimate(
            flops=2 * capacity * columns * (width + 2 * keys_values.shape[0]),
            bytes_accessed=2 * columns * width + 2 * capacity * width,
            transcendentals=capacity * keys_values.shape[0] * columns // HD,
        ),
        compiler_params=pltpu.CompilerParams(vmem_limit_bytes=24 << 20),
        name="attention_projection",
    )(place, slot_utt, frame_len, *payloads, keys_values, in_hbm(weights))


def fold_kernel(sides, joined, place_ref, *refs):
    count = len(sides)
    parts, outs = refs[: 2 * count], refs[2 * count :]
    first = 0
    for number, side in enumerate(sides):
        kept_ref, came_ref = parts[2 * number : 2 * number + 2]
        total = kept_ref[...].astype(jnp.float32) + came_ref[...].astype(jnp.float32)
        half = total.shape[0] // 2
        top, bottom = total[:half], total[half:]
        upper = side(place_ref) == 0
        kept = jnp.where(upper, top, bottom)
        sent = jnp.where(upper, bottom, top).astype(jnp.bfloat16)
        if joined:
            outs[0][first : first + half, :] = kept
            outs[1][first : first + half, :] = sent
            first += half
        else:
            outs[2 * number][...] = kept
            outs[2 * number + 1][...] = sent


def fold(place, parts, sides, joined):
    width = parts[0].shape[1]
    halves = [part.shape[0] // 2 for part in parts[::2]]
    if joined:
        halves = [sum(halves)]
    shapes = [
        jax.ShapeDtypeStruct((half, width), kind)
        for half in halves
        for kind in (jnp.float32, jnp.bfloat16)
    ]
    return pl.pallas_call(
        functools.partial(fold_kernel, sides, joined),
        in_specs=[SCALARS] + [INSIDE] * len(parts),
        out_specs=[INSIDE] * len(shapes),
        out_shape=shapes,
        compiler_params=pltpu.CompilerParams(vmem_limit_bytes=24 << 20),
        name="sum_phase",
    )(place, *parts)


def section_side(place_ref):
    return place_ref[0]


def low_side(place_ref):
    return place_ref[2] % 2


def high_side(place_ref):
    return place_ref[2] // 2


def norm_kernel(count, slots, tokens, place_ref, slot_ref, *refs):
    payloads, (kept, other) = refs[:count], refs[count : count + 2]
    out_ref, picked, total = refs[count + 2 :]
    rows, width = total.shape
    columns = picked.shape[1]
    share = picked.shape[0] // (width // columns + 1)
    source = choice_of_payload(place_ref, slot_ref, slots)
    for choice in range(count):

        @pl.when(source == choice)
        def _(payload=payloads[choice]):
            picked[...] = payload[tokens:, :]

    total[...] = kept[...] + other[...].astype(jnp.float32)
    for part in range(width // columns):
        take = slice(part * columns, (part + 1) * columns)
        total[:, take] += picked[part * share : part * share + rows, :].astype(jnp.float32)
    shape = out_ref.shape[:2]
    normed = square_norm(total[...]).reshape(*shape, width)
    out_ref[:, :, :width] = normed.astype(jnp.bfloat16)
    last = width // columns * share
    target = picked[last : last + rows, :LANES].astype(jnp.float32).reshape(*shape, LANES)
    out_ref[:, :, width:] = target.astype(jnp.bfloat16)


def normed_rows(place, slot_utt, payloads, blocks, tokens, slots):
    width = blocks[0].shape[1]
    rows = blocks[0].shape[0]
    columns = payloads[0].shape[1]
    return pl.pallas_call(
        functools.partial(norm_kernel, len(payloads), slots, tokens),
        in_specs=[SCALARS] * 2 + [INSIDE] * (len(payloads) + len(blocks)),
        out_specs=INSIDE,
        out_shape=jax.ShapeDtypeStruct((rows // FOLD, FOLD, width + LANES), jnp.bfloat16),
        scratch_shapes=[
            pltpu.VMEM((payloads[0].shape[0] - tokens, columns), jnp.bfloat16),
            pltpu.VMEM((rows, width), jnp.float32),
        ],
        compiler_params=pltpu.CompilerParams(vmem_limit_bytes=16 << 20),
        name="token_rows",
    )(place, slot_utt, *payloads, *blocks)


def vocabulary_kernel(tile, count, first_ref, *refs):
    sets, (head_ref, out_ref, rows_ref, stat) = refs[:count], refs[count:]
    vocab_rows, width = head_ref.shape
    share = sets[0].shape[0] * FOLD
    tokens = share * len(sets)
    cell = lax.broadcasted_iota(jnp.int32, (8, LANES), 1)
    take = jnp.where(cell == 0, 256.0, jnp.where(cell == 1, 1.0, 0.0)).astype(jnp.bfloat16)
    for number, rows in enumerate(sets):
        flat = rows[...].astype(jnp.float32).reshape(share, width + LANES)
        rows_ref[number * share : (number + 1) * share, :] = flat.astype(jnp.bfloat16)
    target = dot_nt(take, rows_ref[:, width:])[0:1, :].astype(jnp.int32) - first_ref[3]
    stat[0:1, :] = jnp.full((1, tokens), -jnp.inf, jnp.float32)
    stat[8:9, :] = jnp.zeros((1, tokens), jnp.float32)
    stat[16:17, :] = jnp.zeros((1, tokens), jnp.float32)

    @pl.loop(0, vocab_rows // tile)
    def _(step):
        start = pl.multiple_of(step * tile, tile)
        logits = dot_nt(head_ref[pl.ds(start, tile), :], rows_ref[:, :width])
        vocab = lax.broadcasted_iota(jnp.int32, logits.shape, 0) + start
        before = stat[0:1, :]
        upper = jnp.maximum(before, jnp.max(logits, axis=0, keepdims=True))
        stat[8:9, :] = stat[8:9, :] * jnp.exp(before - upper) + jnp.sum(
            jnp.exp(logits - upper), axis=0, keepdims=True
        )
        stat[16:17, :] += jnp.sum(jnp.where(vocab == target, logits, 0.0), axis=0, keepdims=True)
        stat[0:1, :] = upper

    for number in range(len(sets)):
        for row in range(3):
            out_ref[number, row : row + 1, :] = stat[
                8 * row : 8 * row + 1, number * share : (number + 1) * share
            ]


def vocabulary_stats(place, sets, head):
    share = sets[0].shape[0] * FOLD
    count = len(sets)
    width = head.shape[1]
    tokens = share * count
    return pl.pallas_call(
        functools.partial(vocabulary_kernel, head.shape[0] // 2, count),
        in_specs=[SCALARS] + [INSIDE] * (count + 1),
        out_specs=INSIDE,
        out_shape=jax.ShapeDtypeStruct((count, 8, share), jnp.float32),
        scratch_shapes=[
            pltpu.VMEM((tokens, width + LANES), jnp.bfloat16),
            pltpu.VMEM((24, tokens), jnp.float32),
        ],
        cost_estimate=pl.CostEstimate(
            flops=3 * tokens * head.shape[0] * width,
            bytes_accessed=2 * tokens * width,
            transcendentals=tokens * head.shape[0],
        ),
        compiler_params=pltpu.CompilerParams(vmem_limit_bytes=16 << 20),
        name="vocabulary_scores",
    )(place, *sets, pltpu.with_memory_space_constraint(head, pltpu.VMEM))


def spread_kernel(sections, groups, widths, place_ref, slot_ref, *refs):
    stats, (out_ref, table, block) = refs[:-3], refs[-3:]
    share = table.shape[2]
    first = 0
    for stat in stats:
        table[first : first + stat.shape[0]] = stat[...]
        first += stat.shape[0]
    slots = slot_ref.shape[0] // groups
    block[...] = jnp.zeros_like(block)
    for group in range(groups):
        for slot in range(slots):
            utterance = jnp.maximum(slot_ref[group * slots + slot], 0)
            for section in range(sections):
                at = (section ^ place_ref[0]) * groups + (utterance ^ place_ref[1])
                block[group, 3 * slot : 3 * slot + 3, section * share : (section + 1) * share] = (
                    table[at][0:3, :]
                )
    for section in range(sections):
        for group in range(groups):
            for width in range(widths):
                out_ref[(section * groups + group) * widths + width] = block[group]


def spread_stats(place, slot_utt, stats, sections, groups, widths):
    share = stats[0].shape[2]
    assert 3 * slot_utt.shape[0] // groups <= 8
    return pl.pallas_call(
        functools.partial(spread_kernel, sections, groups, widths),
        in_specs=[SCALARS] * 2 + [INSIDE] * len(stats),
        out_specs=INSIDE,
        out_shape=jax.ShapeDtypeStruct(
            (sections * groups * widths, 8, sections * share), jnp.float32
        ),
        scratch_shapes=[
            pltpu.VMEM((sections * groups, 8, share), jnp.float32),
            pltpu.VMEM((groups, 8, sections * share), jnp.float32),
        ],
        compiler_params=pltpu.CompilerParams(vmem_limit_bytes=16 << 20),
        name="statistics_by_group",
    )(place, slot_utt, *stats)


def score_kernel(sections, widths, place_ref, slot_ref, length_ref, every_ref, out_ref):
    slots, hyps = out_ref.shape
    lanes = every_ref.shape[2]
    share = lanes // sections // widths
    lane = lax.broadcasted_iota(jnp.int32, (1, lanes), 1)
    order = lane % share * (sections * widths) + lane // share
    column = lax.broadcasted_iota(jnp.int32, (1, hyps), 1)
    for slot in range(slots):
        upper = every_ref[:, 3 * slot, :]
        peak = jnp.max(upper, axis=0, keepdims=True)
        total = jnp.sum(
            every_ref[:, 3 * slot + 1, :] * jnp.exp(upper - peak), axis=0, keepdims=True
        )
        picked = jnp.sum(every_ref[:, 3 * slot + 2, :], axis=0, keepdims=True)
        logp = picked - (peak + jnp.log(total))
        scores = jnp.zeros((1, hyps), jnp.float32)
        start = jnp.int32(0)
        for hyp in range(hyps):
            length = length_ref[slot, hyp]
            valid = (order >= start) & (order < start + length)
            summed = jnp.sum(jnp.where(valid, logp, 0.0), axis=1, keepdims=True)
            mean = summed / jnp.full((1, 1), length, jnp.int32).astype(jnp.float32)
            scores = jnp.where(column == hyp, mean + math.log(V), scores)
            start = start + length
        filled = slot_ref[place_ref[1] * slots + slot] >= 0
        out_ref[slot : slot + 1, :] = jnp.where(filled, scores, 0.0)


def hypothesis_scores(place, slot_utt, lengths, every, slots, hyps, sections, widths):
    return pl.pallas_call(
        functools.partial(score_kernel, sections, widths),
        in_specs=[SCALARS] * 3 + [INSIDE],
        out_specs=INSIDE,
        out_shape=jax.ShapeDtypeStruct((slots, hyps), jnp.float32),
        compiler_params=pltpu.CompilerParams(vmem_limit_bytes=16 << 20),
        name="hypothesis_scores",
    )(place, slot_utt, lengths, every)


def rest(pieces, slot_tokens, place, slot_utt, frame_len, hyp_len, payloads, keys_values, o_proj, head):
    section_count = lax.axis_size("section")
    group_count = lax.axis_size("tm")
    width_count = lax.axis_size("mp")
    section_pos = lax.axis_index("section")
    width_pos = lax.axis_index("mp")
    slot_count, hyp_count = hyp_len.shape
    projected = attend(
        place,
        slot_utt,
        frame_len,
        payloads,
        keys_values,
        o_proj,
        pieces,
        section_count,
        width_count,
        slot_count,
    )

    kept, sent, other_kept, other_sent = fold(
        place,
        [projected[1], swap(projected[0], "section", 1), projected[3], swap(projected[2], "mp", 1)],
        [low_side, section_side],
        False,
    )
    kept, sent = fold(
        place,
        [kept, swap(sent, "mp", 1), other_kept, swap(other_sent, "section", 1)],
        [high_side, high_side],
        True,
    )
    out_rows = normed_rows(
        place, slot_utt, payloads, [kept, swap(sent, "mp", 2)], slot_tokens, slot_count
    )

    own = jnp.zeros((width_count, *out_rows.shape), jnp.bfloat16)
    for distance in range(width_count):
        block = swap(out_rows, "mp", distance) if distance else out_rows
        own = lax.dynamic_update_index_in_dim(own, block, width_pos ^ distance, 0)
    own = own.reshape(-1, *out_rows.shape[1:])
    half = own.shape[0] // 2
    by_x = swap(own, "section", 1)
    by_y = swap(own, "tm", 2)
    stats = [vocabulary_stats(place, [own, swap(own, "tm", 1)], head)]
    by_x, by_y, stats[0] = lax.optimization_barrier((by_x, by_y, stats[0]))
    across = [swap(by_x[:half], "tm", 2), swap(by_y[half:], "section", 1)]
    stats.append(
        vocabulary_stats(place, [by_y, swap(by_y, "tm", 1), by_x, swap(by_x, "tm", 1)], head)
    )
    *across, stats[1] = lax.optimization_barrier((*across, stats[1]))
    across = jnp.concatenate(across)
    stats.append(vocabulary_stats(place, [across, swap(across, "tm", 1)], head))

    every = exchange(
        spread_stats(place, slot_utt, stats, section_count, group_count, width_count), ALL
    )
    return hypothesis_scores(
        place, slot_utt, hyp_len, every, slot_count, hyp_count, section_count, width_count
    )


def near_device(
    frame_len,
    slot_utt,
    enc_in,
    ffn_up,
    ffn_down,
    kv_proj,
    hyp_state,
    hyp_tok,
    hyp_len,
    q_proj,
    o_proj,
    head,
):
    section_count = lax.axis_size("section")
    group_count = lax.axis_size("tm")
    width_count = lax.axis_size("mp")
    section_pos = lax.axis_index("section")
    group_pos = lax.axis_index("tm")
    width_pos = lax.axis_index("mp")
    head_devices = section_count * width_count
    all_devices = head_devices * group_count

    frame_rows, utterances, enc_width = enc_in.shape
    slot_count, hyp_count, positions, model_width = hyp_state.shape
    slot_tokens = hyp_count * positions
    share_rows = slot_tokens // head_devices
    vocab_start = (
        (section_pos * group_count + group_pos) * width_count + width_pos
    ) * head.shape[0]
    head_pos = section_pos * width_count + width_pos
    place = jnp.stack([section_pos, group_pos, width_pos, vocab_start, head_pos])
    place = place.astype(jnp.int32)

    parts, own_frames = ffn(place, enc_in, ffn_up, ffn_down, width_count)
    parts = exchange(parts, "mp")

    blocks = queries_of(
        place,
        slot_utt,
        hyp_len,
        place,
        hyp_state.reshape(slot_count, slot_tokens, model_width),
        hyp_tok.reshape(slot_count, 1, slot_tokens),
        q_proj,
        group_count,
        share_rows,
    )
    crossing = blocks[2] + swap(blocks[3], "tm", 1)
    payloads = [blocks[0], swap(blocks[1], "tm", 1), swap(crossing, "tm", 2)]

    sent = keys_values_of(
        parts, own_frames, kv_proj, blocks[0], section_count, utterances, width_count
    )
    frames_all = all_devices * (frame_rows // width_count)
    keys_values = exchange(sent.reshape(all_devices, -1, 2 * HD), ALL).reshape(frames_all, 2 * HD)

    here_slots = lax.dynamic_slice_in_dim(slot_utt, group_pos * slot_count, slot_count, 0)
    filled = jnp.where(here_slots >= 0, jnp.sum(hyp_len, axis=1), 0)
    count = jnp.max(filled).reshape(1)
    most = count
    for distance in range(1, group_count):
        most = jnp.maximum(most, swap(count, "tm", distance))
    operands = (place, slot_utt, frame_len, hyp_len, payloads, keys_values, o_proj, head)
    few = share_rows * 3 // 4
    return lax.cond(
        most[0] <= few * head_devices,
        functools.partial(rest, (few - few // 3, few // 3), slot_tokens),
        functools.partial(rest, (share_rows // 2, share_rows - share_rows // 2), slot_tokens),
        *operands,
    )


def general(
    frame_len,
    slot_utt,
    enc_in,
    ffn_up,
    ffn_down,
    kv_proj,
    hyp_state,
    hyp_tok,
    hyp_len,
    q_proj,
    o_proj,
    head,
):
    section_count = lax.axis_size("section")
    group_count = lax.axis_size("tm")
    width_count = lax.axis_size("mp")
    section_pos = lax.axis_index("section")
    group_pos = lax.axis_index("tm")
    width_pos = lax.axis_index("mp")
    head_devices = section_count * width_count
    head_pos = section_pos * width_count + width_pos
    all_devices = head_devices * group_count

    frame_rows, utterances, enc_width = enc_in.shape
    assert utterances == group_count
    slot_count, hyp_count, positions, model_width = hyp_state.shape
    slot_tokens = hyp_count * positions
    device_heads = q_proj.shape[1] // HD
    group_heads = NH // KVH
    frame_share = frame_rows // width_count
    share_rows = slot_tokens // head_devices
    here_slots = lax.dynamic_slice_in_dim(slot_utt, group_pos * slot_count, slot_count, 0)

    dec_rows = hyp_state.reshape(slot_count * slot_tokens, model_width).astype(jnp.float32)
    queries = jnp.dot(
        square_norm(dec_rows).astype(jnp.bfloat16), q_proj, preferred_element_type=jnp.float32
    ).astype(jnp.bfloat16)
    queries = queries.reshape(slot_count, slot_tokens, device_heads * HD)
    shares = lax.dynamic_slice_in_dim(
        hyp_state.reshape(slot_count, slot_tokens, model_width), head_pos * share_rows, share_rows, 1
    )

    def by_utterance(values):
        out = []
        for utterance in range(utterances):
            block = values[0]
            for slot in range(1, slot_count):
                block = jnp.where(here_slots[slot] == utterance, values[slot], block)
            out.append(block)
        return jnp.stack(out)

    own_slot = jnp.argmax(slot_utt == group_pos)
    from_group = own_slot // slot_count
    queries = lax.dynamic_index_in_dim(
        exchange(by_utterance(queries), "tm"), from_group, 0, keepdims=False
    )
    resid_rows = lax.dynamic_index_in_dim(
        exchange(by_utterance(shares), "tm"), from_group, 0, keepdims=False
    )
    slot_targets = lax.all_gather(
        hyp_tok.reshape(slot_count, slot_tokens), "tm", axis=0, tiled=True
    )
    utt_slots = jnp.argmax(slot_utt[None, :] == jnp.arange(utterances)[:, None], axis=1)
    targets = jnp.take(slot_targets, utt_slots, axis=0).reshape(utterances * slot_tokens)

    enc_flat = (
        enc_in.reshape(width_count, frame_share, utterances, enc_width)
        .transpose(0, 2, 1, 3)
        .reshape(frame_rows * utterances, enc_width)
    )
    share_count = frame_share * utterances
    enc_normed = layer_norm(enc_flat.astype(jnp.float32)).astype(jnp.bfloat16)
    enc_inner = jax.nn.gelu(
        jnp.dot(enc_normed, ffn_up, preferred_element_type=jnp.float32), approximate=False
    ).astype(jnp.bfloat16)
    enc_summed = scatter_sum(
        jnp.dot(enc_inner, ffn_down, preferred_element_type=jnp.float32).astype(jnp.bfloat16),
        "mp",
        width_count,
    )
    own_frames = lax.dynamic_slice_in_dim(enc_flat, width_pos * share_count, share_count, 0)
    enc_states = layer_norm(own_frames.astype(jnp.float32) + enc_summed).astype(jnp.bfloat16)
    keys_values = jnp.dot(enc_states, kv_proj, preferred_element_type=jnp.float32).astype(
        jnp.bfloat16
    )
    keys_values = keys_values.reshape(utterances, frame_share, 2, KVH, HD)
    sent = []
    for section in range(section_count):
        per_width = []
        for width in range(width_count):
            kv_head = (section * width_count + width) * device_heads // group_heads
            per_width.append(
                keys_values[:, :, :, kv_head].reshape(utterances, frame_share, 2 * HD)
            )
        sent.append(jnp.stack(per_width, axis=1))
    sent = jnp.stack(sent).reshape(all_devices, frame_share, 2 * HD)
    frames_all = all_devices * frame_share
    keys_values = exchange(sent, ALL).reshape(frames_all, 2 * HD)

    frame_limit = lax.dynamic_index_in_dim(frame_len, group_pos, 0, keepdims=False)
    queries = queries.reshape(slot_tokens, device_heads, HD)
    scores = jnp.einsum(
        "qhd,fd->hqf", queries, keys_values[:, :HD], preferred_element_type=jnp.float32
    ) / math.sqrt(HD)
    visible = jnp.arange(frames_all, dtype=jnp.int32) < frame_limit
    scores = jnp.where(visible[None, None, :], scores, -jnp.inf)
    weights = jax.nn.softmax(scores, axis=-1).astype(jnp.bfloat16)
    context = jnp.einsum(
        "hqf,fd->qhd", weights, keys_values[:, HD:], preferred_element_type=jnp.float32
    ).astype(jnp.bfloat16)
    partial = jnp.dot(
        context.reshape(slot_tokens, device_heads * HD), o_proj, preferred_element_type=jnp.float32
    ).astype(jnp.bfloat16)
    partial = scatter_sum(partial, "section", section_count).astype(jnp.bfloat16)
    attn_out = scatter_sum(partial, "mp", width_count)
    out_normed = square_norm(resid_rows.astype(jnp.float32) + attn_out).astype(jnp.bfloat16)

    hidden_rows = lax.all_gather(out_normed, ALL, axis=0, tiled=True)
    logits = lax.dot_general(
        hidden_rows, head, (((1,), (1,)), ((), ())), preferred_element_type=jnp.float32
    )
    vocab_rows = head.shape[0]
    vocab_start = (
        (section_pos * group_count + group_pos) * width_count + width_pos
    ) * vocab_rows
    target_rows = (
        targets.reshape(utterances, section_count, width_count, share_rows)
        .transpose(1, 0, 2, 3)
        .reshape(-1)
    )
    upper = jnp.max(logits, axis=1)
    totals = jnp.sum(jnp.exp(logits - upper[:, None]), axis=1)
    matches = (
        jnp.arange(vocab_rows, dtype=jnp.int32)[None, :] == (target_rows - vocab_start)[:, None]
    )
    target_logit = jnp.sum(jnp.where(matches, logits, 0.0), axis=1)

    stats = jnp.stack([upper, totals, target_logit])
    stats = stats.reshape(3, section_count, utterances, width_count, share_rows)
    stats = stats.transpose(2, 0, 1, 3, 4).reshape(utterances, 3, slot_tokens)
    by_slot = jnp.take(stats, jnp.maximum(slot_utt, 0), axis=0)
    by_group = by_slot.reshape(1, group_count, 1, slot_count, 3, slot_tokens)
    by_group = jnp.broadcast_to(
        by_group, (section_count, group_count, width_count, slot_count, 3, slot_tokens)
    ).reshape(all_devices, slot_count, 3, slot_tokens)
    every = exchange(by_group, ALL)
    peak = jnp.max(every[:, :, 0], axis=0)
    total = jnp.sum(every[:, :, 1] * jnp.exp(every[:, :, 0] - peak[None]), axis=0)
    picked = jnp.sum(every[:, :, 2], axis=0)
    token_logp = (picked - (peak + jnp.log(total))).reshape(slot_count, hyp_count, positions)
    valid = jnp.arange(positions, dtype=jnp.int32)[None, None, :] < hyp_len[:, :, None]
    summed = jnp.sum(jnp.where(valid, token_logp, 0.0), axis=-1) / hyp_len.astype(
        jnp.float32
    ) + math.log(V)
    return jnp.where(here_slots[:, None] >= 0, summed, 0.0)


def solution(mesh):
    in_specs = (
        P(),
        P(),
        P(("section", "tm"), None, None),
        P(None, "mp"),
        P("mp", None),
        P(),
        P("tm", None, None, None),
        P("tm", None, None),
        P("tm", None),
        P(None, ("section", "mp")),
        P(("section", "mp"), None),
        P(("section", "tm", "mp"), None),
    )
    out_specs = P("tm", None)
    near = dict(mesh.shape) == {"section": 2, "tm": 4, "mp": 4}
    per_device = near_device if near else general
    return jax.shard_map(
        per_device, mesh=mesh, in_specs=in_specs, out_specs=out_specs, check_vma=False
    )
```

```python
import functools
import math

import jax
import jax.numpy as jnp
from jax import lax
from jax.experimental import pallas as pl
from jax.experimental.pallas import tpu as pltpu
from jax.sharding import PartitionSpec as P

NH = 32
KVH = 4
HD = 128
V = 64000
ALL = ("section", "tm", "mp")
LANES = 128
FOLD = 4


def layer_norm(values):
    center = values - jnp.mean(values, axis=-1, keepdims=True)
    spread = jnp.mean(center * center, axis=-1, keepdims=True)
    return center * lax.rsqrt(spread + 1e-05)


def square_norm(values):
    return values * lax.rsqrt(jnp.mean(values * values, axis=-1, keepdims=True) + 1e-06)


def exchange(blocks, axis):
    return lax.all_to_all(blocks, axis, split_axis=0, concat_axis=0, tiled=True)


def scatter_sum(partial, axis, count):
    blocks = partial.reshape((count, partial.shape[0] // count) + partial.shape[1:])
    return jnp.sum(exchange(blocks, axis).astype(jnp.float32), axis=0)


def swap(values, axis, distance):
    pairs = [(i, i ^ distance) for i in range(lax.axis_size(axis))]
    return lax.ppermute(values, axis, pairs)


def whole(shape):
    return pl.BlockSpec(shape, lambda *_: (0,) * len(shape))


SCALARS = pl.BlockSpec(memory_space=pltpu.SMEM)


def dot(left, right):
    return jnp.dot(left, right, preferred_element_type=jnp.float32)


def dot_nt(left, right):
    return lax.dot_general(
        left, right, (((1,), (1,)), ((), ())), preferred_element_type=jnp.float32
    )


def start_copies(source_of, target_of, semaphores, count):
    copies = []
    for number in range(count):
        copy = pltpu.make_async_copy(
            source_of(number), target_of(number), semaphores.at[number]
        )
        copy.start()
        copies.append(copy)
    return copies


def ffn_kernel(tile, place_ref, x_ref, up_ref, down_ref, *refs):
    out_ref, own_ref, inputs, rows, up, down, x_sem, up_sem, down_sem = refs
    count, share, width = out_ref.shape
    tiles = up_ref.shape[1] // tile
    x_copy = start_copies(lambda i: x_ref, lambda i: inputs, x_sem, 1)[0]
    up_copies = start_copies(
        lambda i: up_ref.at[:, pl.ds(i * tile, tile)], lambda i: up.at[i], up_sem, tiles
    )
    x_copy.wait()
    rows[...] = inputs[...].astype(jnp.float32).reshape(rows.shape)
    start = pl.multiple_of(place_ref[2] * share, share)
    own_ref[...] = rows[pl.ds(start, share), :].astype(jnp.bfloat16)
    normed = layer_norm(rows[...]).astype(jnp.bfloat16)
    inner = []
    for number in range(tiles):
        up_copies[number].wait()
        if number == 0:
            down_copies = start_copies(
                lambda i: down_ref.at[pl.ds(i * tile, tile), :],
                lambda i: down.at[i],
                down_sem,
                tiles,
            )
        hidden = dot(normed, up[number])
        hidden = 0.5 * hidden * (1.0 + lax.erf(hidden * math.sqrt(0.5)))
        inner.append(hidden.astype(jnp.bfloat16))
    total = None
    for number in range(tiles):
        down_copies[number].wait()
        product = dot(inner[number], down[number])
        total = product if total is None else total + product
    for part in range(count):
        out_ref[part] = total[part * share : (part + 1) * share, :].astype(jnp.bfloat16)


def in_hbm(values):
    return pltpu.with_memory_space_constraint(values, pltpu.HBM)


ANYWHERE = pl.BlockSpec(memory_space=pl.ANY)
INSIDE = pl.BlockSpec(memory_space=pltpu.VMEM)


def ffn(place, enc_in, up, down, count):
    frames, utterances, width = enc_in.shape
    rows = frames * utterances
    share = rows // count
    tile = 256
    tiles = up.shape[1] // tile
    return pl.pallas_call(
        functools.partial(ffn_kernel, tile),
        in_specs=[SCALARS] + [ANYWHERE] * 3,
        out_specs=[INSIDE] * 2,
        out_shape=[
            jax.ShapeDtypeStruct((count, share, width), jnp.bfloat16),
            jax.ShapeDtypeStruct((share, width), jnp.bfloat16),
        ],
        scratch_shapes=[
            pltpu.VMEM(enc_in.shape, jnp.bfloat16),
            pltpu.VMEM((rows, width), jnp.float32),
            pltpu.VMEM((tiles, width, tile), jnp.bfloat16),
            pltpu.VMEM((tiles, tile, width), jnp.bfloat16),
            pltpu.SemaphoreType.DMA((1,)),
            pltpu.SemaphoreType.DMA((tiles,)),
            pltpu.SemaphoreType.DMA((tiles,)),
        ],
        cost_estimate=pl.CostEstimate(
            flops=4 * rows * width * up.shape[1],
            bytes_accessed=4 * width * up.shape[1],
            transcendentals=rows * up.shape[1],
        ),
        compiler_params=pltpu.CompilerParams(vmem_limit_bytes=24 << 20),
        name="encoder_ffn",
    )(place, in_hbm(enc_in), in_hbm(up), in_hbm(down))


def query_kernel(
    count, depth, place_ref, slot_ref, length_ref, after_ref, x_ref, tok_ref, w_ref, *refs
):
    outs, (states, weights, normed, total, shares, x_sem, w_sem) = refs[:count], refs[count:]
    slots, tokens, width = x_ref.shape
    hyps = length_ref.shape[1]
    positions = tokens // hyps
    columns = w_ref.shape[1]
    share = shares.shape[1] // 2
    parts = width // columns
    x_copies = start_copies(lambda i: x_ref.at[i], lambda i: states.at[i], x_sem, slots)
    w_copies = start_copies(
        lambda i: w_ref.at[pl.ds(i * depth, depth), :],
        lambda i: weights.at[i],
        w_sem,
        width // depth,
    )
    head_pos = place_ref[4]
    lane = lax.broadcasted_iota(jnp.int32, (1, tokens), 1)
    for slot in range(slots):
        order = jnp.full((1, tokens), -1, jnp.int32)
        start = jnp.int32(0)
        for hyp in range(hyps):
            length = length_ref[slot, hyp]
            inside = (lane >= hyp * positions) & (lane < hyp * positions + length)
            order = jnp.where(inside, lane - hyp * positions + start, order)
            start = start + length
        row = lax.broadcasted_iota(jnp.int32, (tokens, tokens), 0)
        move = jnp.where(order == row, 1.0, 0.0).astype(jnp.bfloat16)
        x_copies[slot].wait()
        ordered = dot(move, states[slot])
        normed[slot * tokens : (slot + 1) * tokens, :] = square_norm(ordered).astype(jnp.bfloat16)
        share_row = lax.broadcasted_iota(jnp.int32, (share, tokens), 0)
        chosen = order == share_row * (tokens // share) + head_pos
        mine = dot(jnp.where(chosen, 1.0, 0.0).astype(jnp.bfloat16), states[slot])
        shares[slot, :share, :] = mine.astype(jnp.bfloat16)
        target = jnp.sum(
            jnp.where(chosen, tok_ref[slot], 0), axis=1, keepdims=True, dtype=jnp.int32
        )
        coarse = target // 256
        cell = lax.broadcasted_iota(jnp.int32, (share, columns), 1)
        packed = jnp.where(cell == 0, coarse, jnp.where(cell == 1, target - coarse * 256, 0))
        shares[slot, share:, :columns] = packed.astype(jnp.float32).astype(jnp.bfloat16)
    for number in range(width // depth):
        w_copies[number].wait()
        product = dot(normed[:, number * depth : (number + 1) * depth], weights[number])
        if number == 0:
            total[...] = product
        else:
            total[...] += product
    group = place_ref[1]
    for distance in range(count):
        slot = jnp.int32(-1)
        for candidate in range(slots):
            holds = slot_ref[group * slots + candidate] == group ^ distance
            slot = jnp.where(holds, candidate, slot)
        out = outs[distance]

        @pl.when(slot < 0)
        def _(out=out):
            out[...] = jnp.zeros_like(out)

        @pl.when(slot >= 0)
        def _(out=out, slot=slot):
            start = pl.multiple_of(slot * tokens, tokens)
            out[:tokens, :] = total[pl.ds(start, tokens), :].astype(jnp.bfloat16)
            for part in range(parts):
                first = tokens + part * share
                out[first : first + share, :] = shares[
                    slot, :share, part * columns : (part + 1) * columns
                ]
            out[tokens + parts * share :, :] = shares[slot, share:, :columns]


def queries_of(place, slot_utt, lengths, after, states, targets, weights, count, share):
    slots, tokens, width = states.shape
    columns = weights.shape[1]
    depth = 1024
    rows = tokens + (width // columns + 1) * share
    block = jax.ShapeDtypeStruct((rows, columns), jnp.bfloat16)
    return pl.pallas_call(
        functools.partial(query_kernel, count, depth),
        in_specs=[SCALARS] * 3 + [ANYWHERE, ANYWHERE, INSIDE, ANYWHERE],
        out_specs=[INSIDE] * count,
        out_shape=[block] * count,
        scratch_shapes=[
            pltpu.VMEM(states.shape, jnp.bfloat16),
            pltpu.VMEM((width // depth, depth, columns), jnp.bfloat16),
            pltpu.VMEM((slots * tokens, width), jnp.bfloat16),
            pltpu.VMEM((slots * tokens, columns), jnp.float32),
            pltpu.VMEM((slots, 2 * share, width), jnp.bfloat16),
            pltpu.SemaphoreType.DMA((slots,)),
            pltpu.SemaphoreType.DMA((width // depth,)),
        ],
        cost_estimate=pl.CostEstimate(
            flops=2 * slots * tokens * width * columns,
            bytes_accessed=2 * width * (columns + slots * tokens),
            transcendentals=0,
        ),
        compiler_params=pltpu.CompilerParams(vmem_limit_bytes=32 << 20),
        name="hypothesis_queries",
    )(place, slot_utt, lengths, after, in_hbm(states), targets, in_hbm(weights))


def kv_kernel(sections, utterances, widths, *refs):
    parts_ref, own_ref, w_ref, after_ref, out_ref = refs
    rows = own_ref.shape[0]
    frames = rows // utterances
    total = own_ref[...].astype(jnp.float32)
    summed = parts_ref[0].astype(jnp.float32)
    for part in range(1, parts_ref.shape[0]):
        summed += parts_ref[part].astype(jnp.float32)
    states = layer_norm(total + summed).astype(jnp.bfloat16)
    to = lax.broadcasted_iota(jnp.int32, (rows, rows), 0)
    come = lax.broadcasted_iota(jnp.int32, (rows, rows), 1)
    move = jnp.where(come == to % frames * utterances + to // frames, 1.0, 0.0)
    states = dot(move.astype(jnp.bfloat16), states).astype(jnp.bfloat16)
    both = dot(states, w_ref[...])
    half = KVH * HD
    per_kv = sections * widths // KVH
    for section in range(sections):
        for utterance in range(utterances):
            for width in range(0, widths, per_kv):
                kv_head = (section * widths + width) // per_kv
                take = slice(utterance * frames, (utterance + 1) * frames)
                block = jnp.concatenate(
                    [
                        both[take, kv_head * HD : (kv_head + 1) * HD],
                        both[take, half + kv_head * HD : half + (kv_head + 1) * HD],
                    ],
                    axis=1,
                )
                start = ((section * utterances + utterance) * widths + width) * frames
                block = jnp.concatenate([block] * per_kv, axis=0).astype(jnp.bfloat16)
                out_ref[start : start + per_kv * frames, :] = block


def keys_values_of(parts, own, weights, after, sections, utterances, widths):
    rows = sections * widths * own.shape[0]
    return pl.pallas_call(
        functools.partial(kv_kernel, sections, utterances, widths),
        in_specs=[INSIDE] * 3 + [ANYWHERE],
        out_specs=INSIDE,
        out_shape=jax.ShapeDtypeStruct((rows, 2 * HD), jnp.bfloat16),
        cost_estimate=pl.CostEstimate(
            flops=2 * own.shape[0] * weights.shape[0] * weights.shape[1],
            bytes_accessed=2 * weights.shape[0] * weights.shape[1],
            transcendentals=0,
        ),
        compiler_params=pltpu.CompilerParams(vmem_limit_bytes=24 << 20),
        name="frame_keys_values",
    )(parts, own, weights, after)


def choice_of_payload(place_ref, slot_ref, slots):
    group = place_ref[1]
    source = jnp.int32(0)
    for slot in range(slot_ref.shape[0]):
        source = jnp.where(slot_ref[slot] == group, slot // slots, source)
    return jnp.minimum(source ^ group, 2)


def attention_kernel(count, slots, capacity, pieces, sections, widths, tile, *refs):
    place_ref, slot_ref, frame_ref = refs[:3]
    payloads, (kv_ref, w_ref) = refs[3 : 3 + count], refs[3 + count : 5 + count]
    outs = refs[5 + count : 5 + count + 2 * len(pieces)]
    weights, picked, context, w_sem = refs[5 + count + 2 * len(pieces) :]
    tokens, columns = capacity, w_ref.shape[0]
    tiles = w_ref.shape[1] // tile
    w_copies = start_copies(
        lambda i: w_ref.at[:, pl.ds(i * tile, tile)], lambda i: weights.at[i], w_sem, tiles
    )
    source = choice_of_payload(place_ref, slot_ref, slots)
    section_pos = place_ref[0]
    frame_limit = frame_ref[place_ref[1]]
    for distance in range(count):

        @pl.when(source == distance)
        def _(payload=payloads[distance]):
            picked[...] = payload[:tokens, :]

    keys = kv_ref[:, :HD]
    values = kv_ref[:, HD:]
    frames = kv_ref.shape[0]
    visible = lax.broadcasted_iota(jnp.int32, (tokens, frames), 1) < frame_limit
    for head in range(columns // HD):
        scores = dot_nt(picked[:, head * HD : (head + 1) * HD], keys) * (1.0 / math.sqrt(HD))
        scores = jnp.where(visible, scores, -jnp.inf)
        raised = jnp.exp(scores - jnp.max(scores, axis=1, keepdims=True))
        chances = (raised / jnp.sum(raised, axis=1, keepdims=True)).astype(jnp.bfloat16)
        context[:, head * HD : (head + 1) * HD] = dot(chances, values).astype(jnp.bfloat16)
    to = lax.broadcasted_iota(jnp.int32, (tokens, tokens), 0)
    come = lax.broadcasted_iota(jnp.int32, (tokens, tokens), 1)
    low_bit = place_ref[2] % 2
    size = widths * pieces[0]
    block = to % size // pieces[0]
    section = jnp.where(to < size, 1 - section_pos, section_pos)
    first_order = (to % pieces[0] * sections + section) * widths + block % 2 * 2 + block // 2
    at = to - 2 * size
    size = widths * pieces[1]
    block = at % size // pieces[1]
    low = jnp.where(at < size, 1 - low_bit, low_bit)
    row = pieces[0] + at % pieces[1]
    second_order = (row * sections + block // 2) * widths + block % 2 * 2 + low
    move = come == jnp.where(at < 0, first_order, second_order)
    ordered = dot(jnp.where(move, 1.0, 0.0).astype(jnp.bfloat16), context[...])
    ordered = ordered.astype(jnp.bfloat16)
    for number in range(tiles):
        w_copies[number].wait()
        product = dot(ordered, weights[number]).astype(jnp.bfloat16)
        first = 0
        for out in outs:
            out[:, number * tile : (number + 1) * tile] = product[first : first + out.shape[0], :]
            first += out.shape[0]


def attend(place, slot_utt, frame_len, payloads, keys_values, weights, pieces, sections, widths, slots):
    count = len(payloads)
    columns, width = weights.shape
    capacity = sum(pieces) * sections * widths
    tile = 1024
    tiles = width // tile
    shapes = [
        jax.ShapeDtypeStruct((piece * widths, width), jnp.bfloat16)
        for piece in pieces
        for _ in range(2)
    ]
    return pl.pallas_call(
        functools.partial(
            attention_kernel, count, slots, capacity, pieces, sections, widths, tile
        ),
        in_specs=[SCALARS] * 3 + [INSIDE] * (count + 1) + [ANYWHERE],
        out_specs=[INSIDE] * len(shapes),
        out_shape=shapes,
        scratch_shapes=[
            pltpu.VMEM((tiles, columns, tile), jnp.bfloat16),
            pltpu.VMEM((capacity, columns), jnp.bfloat16),
            pltpu.VMEM((capacity, columns), jnp.bfloat16),
            pltpu.SemaphoreType.DMA((tiles,)),
        ],
        cost_estimate=pl.CostEstimate(
            flops=2 * capacity * columns * (width + 2 * keys_values.shape[0]),
            bytes_accessed=2 * columns * width + 2 * capacity * width,
            transcendentals=capacity * keys_values.shape[0] * columns // HD,
        ),
        compiler_params=pltpu.CompilerParams(vmem_limit_bytes=24 << 20),
        name="attention_projection",
    )(place, slot_utt, frame_len, *payloads, keys_values, in_hbm(weights))


def fold_kernel(sides, joined, place_ref, *refs):
    count = len(sides)
    parts, outs = refs[: 2 * count], refs[2 * count :]
    first = 0
    for number, side in enumerate(sides):
        kept_ref, came_ref = parts[2 * number : 2 * number + 2]
        total = kept_ref[...].astype(jnp.float32) + came_ref[...].astype(jnp.float32)
        half = total.shape[0] // 2
        top, bottom = total[:half], total[half:]
        upper = side(place_ref) == 0
        kept = jnp.where(upper, top, bottom)
        sent = jnp.where(upper, bottom, top).astype(jnp.bfloat16)
        if joined:
            outs[0][first : first + half, :] = kept
            outs[1][first : first + half, :] = sent
            first += half
        else:
            outs[2 * number][...] = kept
            outs[2 * number + 1][...] = sent


def fold(place, parts, sides, joined):
    width = parts[0].shape[1]
    halves = [part.shape[0] // 2 for part in parts[::2]]
    if joined:
        halves = [sum(halves)]
    shapes = [
        jax.ShapeDtypeStruct((half, width), kind)
        for half in halves
        for kind in (jnp.float32, jnp.bfloat16)
    ]
    return pl.pallas_call(
        functools.partial(fold_kernel, sides, joined),
        in_specs=[SCALARS] + [INSIDE] * len(parts),
        out_specs=[INSIDE] * len(shapes),
        out_shape=shapes,
        compiler_params=pltpu.CompilerParams(vmem_limit_bytes=24 << 20),
        name="sum_phase",
    )(place, *parts)


def section_side(place_ref):
    return place_ref[0]


def low_side(place_ref):
    return place_ref[2] % 2


def high_side(place_ref):
    return place_ref[2] // 2


def norm_kernel(count, slots, tokens, place_ref, slot_ref, *refs):
    payloads, (kept, other) = refs[:count], refs[count : count + 2]
    out_ref, picked, total = refs[count + 2 :]
    rows, width = total.shape
    columns = picked.shape[1]
    share = picked.shape[0] // (width // columns + 1)
    source = choice_of_payload(place_ref, slot_ref, slots)
    for choice in range(count):

        @pl.when(source == choice)
        def _(payload=payloads[choice]):
            picked[...] = payload[tokens:, :]

    total[...] = kept[...] + other[...].astype(jnp.float32)
    for part in range(width // columns):
        take = slice(part * columns, (part + 1) * columns)
        total[:, take] += picked[part * share : part * share + rows, :].astype(jnp.float32)
    shape = out_ref.shape[:2]
    normed = square_norm(total[...]).reshape(*shape, width)
    out_ref[:, :, :width] = normed.astype(jnp.bfloat16)
    last = width // columns * share
    target = picked[last : last + rows, :LANES].astype(jnp.float32).reshape(*shape, LANES)
    out_ref[:, :, width:] = target.astype(jnp.bfloat16)


def normed_rows(place, slot_utt, payloads, blocks, tokens, slots):
    width = blocks[0].shape[1]
    rows = blocks[0].shape[0]
    columns = payloads[0].shape[1]
    return pl.pallas_call(
        functools.partial(norm_kernel, len(payloads), slots, tokens),
        in_specs=[SCALARS] * 2 + [INSIDE] * (len(payloads) + len(blocks)),
        out_specs=INSIDE,
        out_shape=jax.ShapeDtypeStruct((rows // FOLD, FOLD, width + LANES), jnp.bfloat16),
        scratch_shapes=[
            pltpu.VMEM((payloads[0].shape[0] - tokens, columns), jnp.bfloat16),
            pltpu.VMEM((rows, width), jnp.float32),
        ],
        compiler_params=pltpu.CompilerParams(vmem_limit_bytes=16 << 20),
        name="token_rows",
    )(place, slot_utt, *payloads, *blocks)


def vocabulary_kernel(tile, count, first_ref, *refs):
    sets, (head_ref, out_ref, rows_ref, stat) = refs[:count], refs[count:]
    vocab_rows, width = head_ref.shape
    share = sets[0].shape[0] * FOLD
    tokens = share * len(sets)
    cell = lax.broadcasted_iota(jnp.int32, (8, LANES), 1)
    take = jnp.where(cell == 0, 256.0, jnp.where(cell == 1, 1.0, 0.0)).astype(jnp.bfloat16)
    for number, rows in enumerate(sets):
        flat = rows[...].astype(jnp.float32).reshape(share, width + LANES)
        rows_ref[number * share : (number + 1) * share, :] = flat.astype(jnp.bfloat16)
    target = dot_nt(take, rows_ref[:, width:])[0:1, :].astype(jnp.int32) - first_ref[3]
    stat[0:1, :] = jnp.full((1, tokens), -jnp.inf, jnp.float32)
    stat[8:9, :] = jnp.zeros((1, tokens), jnp.float32)
    stat[16:17, :] = jnp.zeros((1, tokens), jnp.float32)

    for start in range(0, vocab_rows, tile):
        logits = dot_nt(head_ref[start : start + tile, :], rows_ref[:, :width])
        vocab = lax.broadcasted_iota(jnp.int32, logits.shape, 0) + start
        before = stat[0:1, :]
        upper = jnp.maximum(before, jnp.max(logits, axis=0, keepdims=True))
        stat[8:9, :] = stat[8:9, :] * jnp.exp(before - upper) + jnp.sum(
            jnp.exp(logits - upper), axis=0, keepdims=True
        )
        stat[16:17, :] += jnp.sum(jnp.where(vocab == target, logits, 0.0), axis=0, keepdims=True)
        stat[0:1, :] = upper

    for number in range(len(sets)):
        for row in range(3):
            out_ref[number, row : row + 1, :] = stat[
                8 * row : 8 * row + 1, number * share : (number + 1) * share
            ]


def vocabulary_stats(place, sets, head):
    share = sets[0].shape[0] * FOLD
    count = len(sets)
    width = head.shape[1]
    tokens = share * count
    return pl.pallas_call(
        functools.partial(vocabulary_kernel, head.shape[0], count),
        in_specs=[SCALARS] + [INSIDE] * (count + 1),
        out_specs=INSIDE,
        out_shape=jax.ShapeDtypeStruct((count, 8, share), jnp.float32),
        scratch_shapes=[
            pltpu.VMEM((tokens, width + LANES), jnp.bfloat16),
            pltpu.VMEM((24, tokens), jnp.float32),
        ],
        cost_estimate=pl.CostEstimate(
            flops=3 * tokens * head.shape[0] * width,
            bytes_accessed=2 * tokens * width,
            transcendentals=tokens * head.shape[0],
        ),
        compiler_params=pltpu.CompilerParams(vmem_limit_bytes=16 << 20),
        name="vocabulary_scores",
    )(place, *sets, pltpu.with_memory_space_constraint(head, pltpu.VMEM))


def zero_kernel(after_ref, head_ref, out_ref):
    out_ref[...] = jnp.zeros_like(out_ref)


def head_in_vmem(after, head):
    return pl.pallas_call(
        zero_kernel,
        in_specs=[ANYWHERE, INSIDE],
        out_specs=INSIDE,
        out_shape=jax.ShapeDtypeStruct((8, LANES), jnp.float32),
        compiler_params=pltpu.CompilerParams(vmem_limit_bytes=16 << 20),
        name="vocabulary_rows",
    )(after, pltpu.with_memory_space_constraint(head, pltpu.VMEM))


def spread_kernel(order, sections, groups, widths, place_ref, slot_ref, *refs):
    stats, (out_ref, table, block) = refs[:-3], refs[-3:]
    share = table.shape[2]
    for stat, places in zip(stats, order):
        for number, at in enumerate(places):
            table[at] = stat[number]
    slots = slot_ref.shape[0] // groups
    block[...] = jnp.zeros_like(block)
    for group in range(groups):
        for slot in range(slots):
            utterance = jnp.maximum(slot_ref[group * slots + slot], 0)
            for section in range(sections):
                at = (section ^ place_ref[0]) * groups + (utterance ^ place_ref[1])
                block[group, 3 * slot : 3 * slot + 3, section * share : (section + 1) * share] = (
                    table[at][0:3, :]
                )
    for section in range(sections):
        for group in range(groups):
            for width in range(widths):
                out_ref[(section * groups + group) * widths + width] = block[group]


def spread_stats(place, slot_utt, stats, order, sections, groups, widths):
    share = stats[0].shape[2]
    assert 3 * slot_utt.shape[0] // groups <= 8
    return pl.pallas_call(
        functools.partial(spread_kernel, order, sections, groups, widths),
        in_specs=[SCALARS] * 2 + [INSIDE] * len(stats),
        out_specs=INSIDE,
        out_shape=jax.ShapeDtypeStruct(
            (sections * groups * widths, 8, sections * share), jnp.float32
        ),
        scratch_shapes=[
            pltpu.VMEM((sections * groups, 8, share), jnp.float32),
            pltpu.VMEM((groups, 8, sections * share), jnp.float32),
        ],
        compiler_params=pltpu.CompilerParams(vmem_limit_bytes=16 << 20),
        name="statistics_by_group",
    )(place, slot_utt, *stats)


def score_kernel(sections, widths, place_ref, slot_ref, length_ref, every_ref, out_ref):
    slots, hyps = out_ref.shape
    lanes = every_ref.shape[2]
    share = lanes // sections // widths
    lane = lax.broadcasted_iota(jnp.int32, (1, lanes), 1)
    order = lane % share * (sections * widths) + lane // share
    column = lax.broadcasted_iota(jnp.int32, (1, hyps), 1)
    for slot in range(slots):
        upper = every_ref[:, 3 * slot, :]
        peak = jnp.max(upper, axis=0, keepdims=True)
        total = jnp.sum(
            every_ref[:, 3 * slot + 1, :] * jnp.exp(upper - peak), axis=0, keepdims=True
        )
        picked = jnp.sum(every_ref[:, 3 * slot + 2, :], axis=0, keepdims=True)
        logp = picked - (peak + jnp.log(total))
        scores = jnp.zeros((1, hyps), jnp.float32)
        start = jnp.int32(0)
        for hyp in range(hyps):
            length = length_ref[slot, hyp]
            valid = (order >= start) & (order < start + length)
            summed = jnp.sum(jnp.where(valid, logp, 0.0), axis=1, keepdims=True)
            mean = summed / jnp.full((1, 1), length, jnp.int32).astype(jnp.float32)
            scores = jnp.where(column == hyp, mean + math.log(V), scores)
            start = start + length
        filled = slot_ref[place_ref[1] * slots + slot] >= 0
        out_ref[slot : slot + 1, :] = jnp.where(filled, scores, 0.0)


def hypothesis_scores(place, slot_utt, lengths, every, slots, hyps, sections, widths):
    return pl.pallas_call(
        functools.partial(score_kernel, sections, widths),
        in_specs=[SCALARS] * 3 + [INSIDE],
        out_specs=INSIDE,
        out_shape=jax.ShapeDtypeStruct((slots, hyps), jnp.float32),
        compiler_params=pltpu.CompilerParams(vmem_limit_bytes=16 << 20),
        name="hypothesis_scores",
    )(place, slot_utt, lengths, every)


def rest(pieces, slot_tokens, place, slot_utt, frame_len, hyp_len, payloads, keys_values, o_proj, head):
    section_count = lax.axis_size("section")
    group_count = lax.axis_size("tm")
    width_count = lax.axis_size("mp")
    section_pos = lax.axis_index("section")
    width_pos = lax.axis_index("mp")
    slot_count, hyp_count = hyp_len.shape
    projected = attend(
        place,
        slot_utt,
        frame_len,
        payloads,
        keys_values,
        o_proj,
        pieces,
        section_count,
        width_count,
        slot_count,
    )

    kept, sent, other_kept, other_sent = fold(
        place,
        [projected[1], swap(projected[0], "section", 1), projected[3], swap(projected[2], "mp", 1)],
        [low_side, section_side],
        False,
    )
    kept, sent = fold(
        place,
        [kept, swap(sent, "mp", 1), other_kept, swap(other_sent, "section", 1)],
        [high_side, high_side],
        True,
    )
    out_rows = normed_rows(
        place, slot_utt, payloads, [kept, swap(sent, "mp", 2)], slot_tokens, slot_count
    )

    own = jnp.zeros((width_count, *out_rows.shape), jnp.bfloat16)
    for distance in range(width_count):
        block = swap(out_rows, "mp", distance) if distance else out_rows
        own = lax.dynamic_update_index_in_dim(own, block, width_pos ^ distance, 0)
    own = own.reshape(-1, *out_rows.shape[1:])
    half = own.shape[0] // 2
    by_x = swap(own, "section", 1)
    by_y = swap(own, "tm", 2)
    beside = swap(own, "tm", 1)
    by_x, by_y, _ = lax.optimization_barrier((by_x, by_y, head_in_vmem(beside, head)))
    across = [swap(by_x[:half], "tm", 2), swap(by_y[half:], "section", 1)]
    near = vocabulary_stats(place, [by_y, swap(by_y, "tm", 1), by_x, swap(by_x, "tm", 1)], head)
    *across, near = lax.optimization_barrier((*across, near))
    across = jnp.concatenate(across)
    far = vocabulary_stats(place, [across, swap(across, "tm", 1), own, beside], head)
    stats = [near, far]
    order = ((2, 3, 4, 5), (6, 7, 0, 1))

    every = exchange(
        spread_stats(place, slot_utt, stats, order, section_count, group_count, width_count), ALL
    )
    return hypothesis_scores(
        place, slot_utt, hyp_len, every, slot_count, hyp_count, section_count, width_count
    )


def near_device(
    frame_len,
    slot_utt,
    enc_in,
    ffn_up,
    ffn_down,
    kv_proj,
    hyp_state,
    hyp_tok,
    hyp_len,
    q_proj,
    o_proj,
    head,
):
    section_count = lax.axis_size("section")
    group_count = lax.axis_size("tm")
    width_count = lax.axis_size("mp")
    section_pos = lax.axis_index("section")
    group_pos = lax.axis_index("tm")
    width_pos = lax.axis_index("mp")
    head_devices = section_count * width_count
    all_devices = head_devices * group_count

    frame_rows, utterances, enc_width = enc_in.shape
    slot_count, hyp_count, positions, model_width = hyp_state.shape
    slot_tokens = hyp_count * positions
    share_rows = slot_tokens // head_devices
    vocab_start = (
        (section_pos * group_count + group_pos) * width_count + width_pos
    ) * head.shape[0]
    head_pos = section_pos * width_count + width_pos
    place = jnp.stack([section_pos, group_pos, width_pos, vocab_start, head_pos])
    place = place.astype(jnp.int32)

    parts, own_frames = ffn(place, enc_in, ffn_up, ffn_down, width_count)
    parts = exchange(parts, "mp")

    blocks = queries_of(
        place,
        slot_utt,
        hyp_len,
        place,
        hyp_state.reshape(slot_count, slot_tokens, model_width),
        hyp_tok.reshape(slot_count, 1, slot_tokens),
        q_proj,
        group_count,
        share_rows,
    )
    crossing = blocks[2] + swap(blocks[3], "tm", 1)
    payloads = [blocks[0], swap(blocks[1], "tm", 1), swap(crossing, "tm", 2)]

    sent = keys_values_of(
        parts, own_frames, kv_proj, blocks[0], section_count, utterances, width_count
    )
    frames_all = all_devices * (frame_rows // width_count)
    keys_values = exchange(sent.reshape(all_devices, -1, 2 * HD), ALL).reshape(frames_all, 2 * HD)

    here_slots = lax.dynamic_slice_in_dim(slot_utt, group_pos * slot_count, slot_count, 0)
    filled = jnp.where(here_slots >= 0, jnp.sum(hyp_len, axis=1), 0)
    count = jnp.max(filled).reshape(1)
    most = count
    for distance in range(1, group_count):
        most = jnp.maximum(most, swap(count, "tm", distance))
    operands = (place, slot_utt, frame_len, hyp_len, payloads, keys_values, o_proj, head)
    few = share_rows * 3 // 4
    return lax.cond(
        most[0] <= few * head_devices,
        functools.partial(rest, (few - few // 3, few // 3), slot_tokens),
        functools.partial(rest, (share_rows // 2, share_rows - share_rows // 2), slot_tokens),
        *operands,
    )


def general(
    frame_len,
    slot_utt,
    enc_in,
    ffn_up,
    ffn_down,
    kv_proj,
    hyp_state,
    hyp_tok,
    hyp_len,
    q_proj,
    o_proj,
    head,
):
    section_count = lax.axis_size("section")
    group_count = lax.axis_size("tm")
    width_count = lax.axis_size("mp")
    section_pos = lax.axis_index("section")
    group_pos = lax.axis_index("tm")
    width_pos = lax.axis_index("mp")
    head_devices = section_count * width_count
    head_pos = section_pos * width_count + width_pos
    all_devices = head_devices * group_count

    frame_rows, utterances, enc_width = enc_in.shape
    assert utterances == group_count
    slot_count, hyp_count, positions, model_width = hyp_state.shape
    slot_tokens = hyp_count * positions
    device_heads = q_proj.shape[1] // HD
    group_heads = NH // KVH
    frame_share = frame_rows // width_count
    share_rows = slot_tokens // head_devices
    here_slots = lax.dynamic_slice_in_dim(slot_utt, group_pos * slot_count, slot_count, 0)

    dec_rows = hyp_state.reshape(slot_count * slot_tokens, model_width).astype(jnp.float32)
    queries = jnp.dot(
        square_norm(dec_rows).astype(jnp.bfloat16), q_proj, preferred_element_type=jnp.float32
    ).astype(jnp.bfloat16)
    queries = queries.reshape(slot_count, slot_tokens, device_heads * HD)
    shares = lax.dynamic_slice_in_dim(
        hyp_state.reshape(slot_count, slot_tokens, model_width), head_pos * share_rows, share_rows, 1
    )

    def by_utterance(values):
        out = []
        for utterance in range(utterances):
            block = values[0]
            for slot in range(1, slot_count):
                block = jnp.where(here_slots[slot] == utterance, values[slot], block)
            out.append(block)
        return jnp.stack(out)

    own_slot = jnp.argmax(slot_utt == group_pos)
    from_group = own_slot // slot_count
    queries = lax.dynamic_index_in_dim(
        exchange(by_utterance(queries), "tm"), from_group, 0, keepdims=False
    )
    resid_rows = lax.dynamic_index_in_dim(
        exchange(by_utterance(shares), "tm"), from_group, 0, keepdims=False
    )
    slot_targets = lax.all_gather(
        hyp_tok.reshape(slot_count, slot_tokens), "tm", axis=0, tiled=True
    )
    utt_slots = jnp.argmax(slot_utt[None, :] == jnp.arange(utterances)[:, None], axis=1)
    targets = jnp.take(slot_targets, utt_slots, axis=0).reshape(utterances * slot_tokens)

    enc_flat = (
        enc_in.reshape(width_count, frame_share, utterances, enc_width)
        .transpose(0, 2, 1, 3)
        .reshape(frame_rows * utterances, enc_width)
    )
    share_count = frame_share * utterances
    enc_normed = layer_norm(enc_flat.astype(jnp.float32)).astype(jnp.bfloat16)
    enc_inner = jax.nn.gelu(
        jnp.dot(enc_normed, ffn_up, preferred_element_type=jnp.float32), approximate=False
    ).astype(jnp.bfloat16)
    enc_summed = scatter_sum(
        jnp.dot(enc_inner, ffn_down, preferred_element_type=jnp.float32).astype(jnp.bfloat16),
        "mp",
        width_count,
    )
    own_frames = lax.dynamic_slice_in_dim(enc_flat, width_pos * share_count, share_count, 0)
    enc_states = layer_norm(own_frames.astype(jnp.float32) + enc_summed).astype(jnp.bfloat16)
    keys_values = jnp.dot(enc_states, kv_proj, preferred_element_type=jnp.float32).astype(
        jnp.bfloat16
    )
    keys_values = keys_values.reshape(utterances, frame_share, 2, KVH, HD)
    sent = []
    for section in range(section_count):
        per_width = []
        for width in range(width_count):
            kv_head = (section * width_count + width) * device_heads // group_heads
            per_width.append(
                keys_values[:, :, :, kv_head].reshape(utterances, frame_share, 2 * HD)
            )
        sent.append(jnp.stack(per_width, axis=1))
    sent = jnp.stack(sent).reshape(all_devices, frame_share, 2 * HD)
    frames_all = all_devices * frame_share
    keys_values = exchange(sent, ALL).reshape(frames_all, 2 * HD)

    frame_limit = lax.dynamic_index_in_dim(frame_len, group_pos, 0, keepdims=False)
    queries = queries.reshape(slot_tokens, device_heads, HD)
    scores = jnp.einsum(
        "qhd,fd->hqf", queries, keys_values[:, :HD], preferred_element_type=jnp.float32
    ) / math.sqrt(HD)
    visible = jnp.arange(frames_all, dtype=jnp.int32) < frame_limit
    scores = jnp.where(visible[None, None, :], scores, -jnp.inf)
    weights = jax.nn.softmax(scores, axis=-1).astype(jnp.bfloat16)
    context = jnp.einsum(
        "hqf,fd->qhd", weights, keys_values[:, HD:], preferred_element_type=jnp.float32
    ).astype(jnp.bfloat16)
    partial = jnp.dot(
        context.reshape(slot_tokens, device_heads * HD), o_proj, preferred_element_type=jnp.float32
    ).astype(jnp.bfloat16)
    partial = scatter_sum(partial, "section", section_count).astype(jnp.bfloat16)
    attn_out = scatter_sum(partial, "mp", width_count)
    out_normed = square_norm(resid_rows.astype(jnp.float32) + attn_out).astype(jnp.bfloat16)

    hidden_rows = lax.all_gather(out_normed, ALL, axis=0, tiled=True)
    logits = lax.dot_general(
        hidden_rows, head, (((1,), (1,)), ((), ())), preferred_element_type=jnp.float32
    )
    vocab_rows = head.shape[0]
    vocab_start = (
        (section_pos * group_count + group_pos) * width_count + width_pos
    ) * vocab_rows
    target_rows = (
        targets.reshape(utterances, section_count, width_count, share_rows)
        .transpose(1, 0, 2, 3)
        .reshape(-1)
    )
    upper = jnp.max(logits, axis=1)
    totals = jnp.sum(jnp.exp(logits - upper[:, None]), axis=1)
    matches = (
        jnp.arange(vocab_rows, dtype=jnp.int32)[None, :] == (target_rows - vocab_start)[:, None]
    )
    target_logit = jnp.sum(jnp.where(matches, logits, 0.0), axis=1)

    stats = jnp.stack([upper, totals, target_logit])
    stats = stats.reshape(3, section_count, utterances, width_count, share_rows)
    stats = stats.transpose(2, 0, 1, 3, 4).reshape(utterances, 3, slot_tokens)
    by_slot = jnp.take(stats, jnp.maximum(slot_utt, 0), axis=0)
    by_group = by_slot.reshape(1, group_count, 1, slot_count, 3, slot_tokens)
    by_group = jnp.broadcast_to(
        by_group, (section_count, group_count, width_count, slot_count, 3, slot_tokens)
    ).reshape(all_devices, slot_count, 3, slot_tokens)
    every = exchange(by_group, ALL)
    peak = jnp.max(every[:, :, 0], axis=0)
    total = jnp.sum(every[:, :, 1] * jnp.exp(every[:, :, 0] - peak[None]), axis=0)
    picked = jnp.sum(every[:, :, 2], axis=0)
    token_logp = (picked - (peak + jnp.log(total))).reshape(slot_count, hyp_count, positions)
    valid = jnp.arange(positions, dtype=jnp.int32)[None, None, :] < hyp_len[:, :, None]
    summed = jnp.sum(jnp.where(valid, token_logp, 0.0), axis=-1) / hyp_len.astype(
        jnp.float32
    ) + math.log(V)
    return jnp.where(here_slots[:, None] >= 0, summed, 0.0)


def solution(mesh):
    in_specs = (
        P(),
        P(),
        P(("section", "tm"), None, None),
        P(None, "mp"),
        P("mp", None),
        P(),
        P("tm", None, None, None),
        P("tm", None, None),
        P("tm", None),
        P(None, ("section", "mp")),
        P(("section", "mp"), None),
        P(("section", "tm", "mp"), None),
    )
    out_specs = P("tm", None)
    near = dict(mesh.shape) == {"section": 2, "tm": 4, "mp": 4}
    per_device = near_device if near else general
    return jax.shard_map(
        per_device, mesh=mesh, in_specs=in_specs, out_specs=out_specs, check_vma=False
    )
```

```python
import functools
import math

import jax
import jax.numpy as jnp
from jax import lax
from jax.experimental import pallas as pl
from jax.experimental.pallas import tpu as pltpu
from jax.sharding import PartitionSpec as P

NH = 32
KVH = 4
HD = 128
V = 64000
ALL = ("section", "tm", "mp")
LANES = 128
FOLD = 4


def layer_norm(values):
    center = values - jnp.mean(values, axis=-1, keepdims=True)
    spread = jnp.mean(center * center, axis=-1, keepdims=True)
    return center * lax.rsqrt(spread + 1e-05)


def square_norm(values):
    return values * lax.rsqrt(jnp.mean(values * values, axis=-1, keepdims=True) + 1e-06)


def exchange(blocks, axis):
    return lax.all_to_all(blocks, axis, split_axis=0, concat_axis=0, tiled=True)


def scatter_sum(partial, axis, count):
    blocks = partial.reshape((count, partial.shape[0] // count) + partial.shape[1:])
    return jnp.sum(exchange(blocks, axis).astype(jnp.float32), axis=0)


def swap(values, axis, distance):
    pairs = [(i, i ^ distance) for i in range(lax.axis_size(axis))]
    return lax.ppermute(values, axis, pairs)


def whole(shape):
    return pl.BlockSpec(shape, lambda *_: (0,) * len(shape))


SCALARS = pl.BlockSpec(memory_space=pltpu.SMEM)


def dot(left, right):
    return jnp.dot(left, right, preferred_element_type=jnp.float32)


def dot_nt(left, right):
    return lax.dot_general(
        left, right, (((1,), (1,)), ((), ())), preferred_element_type=jnp.float32
    )


def start_copies(source_of, target_of, semaphores, count):
    copies = []
    for number in range(count):
        copy = pltpu.make_async_copy(
            source_of(number), target_of(number), semaphores.at[number]
        )
        copy.start()
        copies.append(copy)
    return copies


def ffn_kernel(tile, place_ref, x_ref, up_ref, down_ref, *refs):
    out_ref, own_ref, inputs, rows, up, down, x_sem, up_sem, down_sem = refs
    count, share, width = out_ref.shape
    tiles = up_ref.shape[1] // tile
    x_copy = start_copies(lambda i: x_ref, lambda i: inputs, x_sem, 1)[0]
    up_copies = start_copies(
        lambda i: up_ref.at[:, pl.ds(i * tile, tile)], lambda i: up.at[i], up_sem, tiles
    )
    x_copy.wait()
    rows[...] = inputs[...].astype(jnp.float32).reshape(rows.shape)
    start = pl.multiple_of(place_ref[2] * share, share)
    own_ref[...] = rows[pl.ds(start, share), :].astype(jnp.bfloat16)
    normed = layer_norm(rows[...]).astype(jnp.bfloat16)
    inner = []
    for number in range(tiles):
        up_copies[number].wait()
        if number == 0:
            down_copies = start_copies(
                lambda i: down_ref.at[pl.ds(i * tile, tile), :],
                lambda i: down.at[i],
                down_sem,
                tiles,
            )
        hidden = dot(normed, up[number])
        hidden = 0.5 * hidden * (1.0 + lax.erf(hidden * math.sqrt(0.5)))
        inner.append(hidden.astype(jnp.bfloat16))
    total = None
    for number in range(tiles):
        down_copies[number].wait()
        product = dot(inner[number], down[number])
        total = product if total is None else total + product
    for part in range(count):
        out_ref[part] = total[part * share : (part + 1) * share, :].astype(jnp.bfloat16)


def in_hbm(values):
    return pltpu.with_memory_space_constraint(values, pltpu.HBM)


ANYWHERE = pl.BlockSpec(memory_space=pl.ANY)
INSIDE = pl.BlockSpec(memory_space=pltpu.VMEM)


def ffn(place, enc_in, up, down, count):
    frames, utterances, width = enc_in.shape
    rows = frames * utterances
    share = rows // count
    tile = 256
    tiles = up.shape[1] // tile
    return pl.pallas_call(
        functools.partial(ffn_kernel, tile),
        in_specs=[SCALARS] + [ANYWHERE] * 3,
        out_specs=[INSIDE] * 2,
        out_shape=[
            jax.ShapeDtypeStruct((count, share, width), jnp.bfloat16),
            jax.ShapeDtypeStruct((share, width), jnp.bfloat16),
        ],
        scratch_shapes=[
            pltpu.VMEM(enc_in.shape, jnp.bfloat16),
            pltpu.VMEM((rows, width), jnp.float32),
            pltpu.VMEM((tiles, width, tile), jnp.bfloat16),
            pltpu.VMEM((tiles, tile, width), jnp.bfloat16),
            pltpu.SemaphoreType.DMA((1,)),
            pltpu.SemaphoreType.DMA((tiles,)),
            pltpu.SemaphoreType.DMA((tiles,)),
        ],
        cost_estimate=pl.CostEstimate(
            flops=4 * rows * width * up.shape[1],
            bytes_accessed=4 * width * up.shape[1],
            transcendentals=rows * up.shape[1],
        ),
        compiler_params=pltpu.CompilerParams(vmem_limit_bytes=24 << 20),
        name="encoder_ffn",
    )(place, in_hbm(enc_in), in_hbm(up), in_hbm(down))


def query_kernel(
    count, depth, place_ref, slot_ref, length_ref, after_ref, x_ref, tok_ref, w_ref, *refs
):
    outs, (states, weights, normed, total, shares, x_sem, w_sem) = refs[:count], refs[count:]
    slots, tokens, width = x_ref.shape
    hyps = length_ref.shape[1]
    positions = tokens // hyps
    columns = w_ref.shape[1]
    share = shares.shape[1] // 2
    parts = width // columns
    x_copies = start_copies(lambda i: x_ref.at[i], lambda i: states.at[i], x_sem, slots)
    w_copies = start_copies(
        lambda i: w_ref.at[pl.ds(i * depth, depth), :],
        lambda i: weights.at[i],
        w_sem,
        width // depth,
    )
    head_pos = place_ref[4]
    lane = lax.broadcasted_iota(jnp.int32, (1, tokens), 1)
    for slot in range(slots):
        order = jnp.full((1, tokens), -1, jnp.int32)
        start = jnp.int32(0)
        for hyp in range(hyps):
            length = length_ref[slot, hyp]
            inside = (lane >= hyp * positions) & (lane < hyp * positions + length)
            order = jnp.where(inside, lane - hyp * positions + start, order)
            start = start + length
        row = lax.broadcasted_iota(jnp.int32, (tokens, tokens), 0)
        move = jnp.where(order == row, 1.0, 0.0).astype(jnp.bfloat16)
        x_copies[slot].wait()
        ordered = dot(move, states[slot])
        normed[slot * tokens : (slot + 1) * tokens, :] = square_norm(ordered).astype(jnp.bfloat16)
        share_row = lax.broadcasted_iota(jnp.int32, (share, tokens), 0)
        chosen = order == share_row * (tokens // share) + head_pos
        mine = dot(jnp.where(chosen, 1.0, 0.0).astype(jnp.bfloat16), states[slot])
        shares[slot, :share, :] = mine.astype(jnp.bfloat16)
        target = jnp.sum(
            jnp.where(chosen, tok_ref[slot], 0), axis=1, keepdims=True, dtype=jnp.int32
        )
        coarse = target // 256
        cell = lax.broadcasted_iota(jnp.int32, (share, columns), 1)
        packed = jnp.where(cell == 0, coarse, jnp.where(cell == 1, target - coarse * 256, 0))
        shares[slot, share:, :columns] = packed.astype(jnp.float32).astype(jnp.bfloat16)
    for number in range(width // depth):
        w_copies[number].wait()
        product = dot(normed[:, number * depth : (number + 1) * depth], weights[number])
        if number == 0:
            total[...] = product
        else:
            total[...] += product
    group = place_ref[1]
    for distance in range(count):
        slot = jnp.int32(-1)
        for candidate in range(slots):
            holds = slot_ref[group * slots + candidate] == group ^ distance
            slot = jnp.where(holds, candidate, slot)
        out = outs[distance]

        @pl.when(slot < 0)
        def _(out=out):
            out[...] = jnp.zeros_like(out)

        @pl.when(slot >= 0)
        def _(out=out, slot=slot):
            start = pl.multiple_of(slot * tokens, tokens)
            out[:tokens, :] = total[pl.ds(start, tokens), :].astype(jnp.bfloat16)
            for part in range(parts):
                first = tokens + part * share
                out[first : first + share, :] = shares[
                    slot, :share, part * columns : (part + 1) * columns
                ]
            out[tokens + parts * share :, :] = shares[slot, share:, :columns]


def queries_of(place, slot_utt, lengths, after, states, targets, weights, count, share):
    slots, tokens, width = states.shape
    columns = weights.shape[1]
    depth = 1024
    rows = tokens + (width // columns + 1) * share
    block = jax.ShapeDtypeStruct((rows, columns), jnp.bfloat16)
    return pl.pallas_call(
        functools.partial(query_kernel, count, depth),
        in_specs=[SCALARS] * 3 + [ANYWHERE, ANYWHERE, INSIDE, ANYWHERE],
        out_specs=[INSIDE] * count,
        out_shape=[block] * count,
        scratch_shapes=[
            pltpu.VMEM(states.shape, jnp.bfloat16),
            pltpu.VMEM((width // depth, depth, columns), jnp.bfloat16),
            pltpu.VMEM((slots * tokens, width), jnp.bfloat16),
            pltpu.VMEM((slots * tokens, columns), jnp.float32),
            pltpu.VMEM((slots, 2 * share, width), jnp.bfloat16),
            pltpu.SemaphoreType.DMA((slots,)),
            pltpu.SemaphoreType.DMA((width // depth,)),
        ],
        cost_estimate=pl.CostEstimate(
            flops=2 * slots * tokens * width * columns,
            bytes_accessed=2 * width * (columns + slots * tokens),
            transcendentals=0,
        ),
        compiler_params=pltpu.CompilerParams(vmem_limit_bytes=32 << 20),
        name="hypothesis_queries",
    )(place, slot_utt, lengths, after, in_hbm(states), targets, in_hbm(weights))


def kv_kernel(sections, utterances, widths, *refs):
    parts_ref, own_ref, w_ref, after_ref, out_ref = refs
    rows = own_ref.shape[0]
    frames = rows // utterances
    total = own_ref[...].astype(jnp.float32)
    summed = parts_ref[0].astype(jnp.float32)
    for part in range(1, parts_ref.shape[0]):
        summed += parts_ref[part].astype(jnp.float32)
    states = layer_norm(total + summed).astype(jnp.bfloat16)
    to = lax.broadcasted_iota(jnp.int32, (rows, rows), 0)
    come = lax.broadcasted_iota(jnp.int32, (rows, rows), 1)
    move = jnp.where(come == to % frames * utterances + to // frames, 1.0, 0.0)
    states = dot(move.astype(jnp.bfloat16), states).astype(jnp.bfloat16)
    both = dot(states, w_ref[...])
    half = KVH * HD
    per_kv = sections * widths // KVH
    for section in range(sections):
        for utterance in range(utterances):
            for width in range(0, widths, per_kv):
                kv_head = (section * widths + width) // per_kv
                take = slice(utterance * frames, (utterance + 1) * frames)
                block = jnp.concatenate(
                    [
                        both[take, kv_head * HD : (kv_head + 1) * HD],
                        both[take, half + kv_head * HD : half + (kv_head + 1) * HD],
                    ],
                    axis=1,
                )
                start = ((section * utterances + utterance) * widths + width) * frames
                block = jnp.concatenate([block] * per_kv, axis=0).astype(jnp.bfloat16)
                out_ref[start : start + per_kv * frames, :] = block


def keys_values_of(parts, own, weights, after, sections, utterances, widths):
    rows = sections * widths * own.shape[0]
    return pl.pallas_call(
        functools.partial(kv_kernel, sections, utterances, widths),
        in_specs=[INSIDE] * 3 + [ANYWHERE],
        out_specs=INSIDE,
        out_shape=jax.ShapeDtypeStruct((rows, 2 * HD), jnp.bfloat16),
        cost_estimate=pl.CostEstimate(
            flops=2 * own.shape[0] * weights.shape[0] * weights.shape[1],
            bytes_accessed=2 * weights.shape[0] * weights.shape[1],
            transcendentals=0,
        ),
        compiler_params=pltpu.CompilerParams(vmem_limit_bytes=24 << 20),
        name="frame_keys_values",
    )(parts, own, weights, after)


def choice_of_payload(place_ref, slot_ref, slots):
    group = place_ref[1]
    source = jnp.int32(0)
    for slot in range(slot_ref.shape[0]):
        source = jnp.where(slot_ref[slot] == group, slot // slots, source)
    return jnp.minimum(source ^ group, 2)


def attention_kernel(count, slots, capacity, pieces, sections, widths, tile, *refs):
    place_ref, slot_ref, frame_ref = refs[:3]
    payloads, (kv_ref, w_ref) = refs[3 : 3 + count], refs[3 + count : 5 + count]
    outs = refs[5 + count : 5 + count + 2 * len(pieces)]
    weights, picked, context, w_sem = refs[5 + count + 2 * len(pieces) :]
    tokens, columns = capacity, w_ref.shape[0]
    tiles = w_ref.shape[1] // tile
    w_copies = start_copies(
        lambda i: w_ref.at[:, pl.ds(i * tile, tile)], lambda i: weights.at[i], w_sem, tiles
    )
    source = choice_of_payload(place_ref, slot_ref, slots)
    section_pos = place_ref[0]
    frame_limit = frame_ref[place_ref[1]]
    for distance in range(count):

        @pl.when(source == distance)
        def _(payload=payloads[distance]):
            picked[...] = payload[:tokens, :]

    keys = kv_ref[:, :HD]
    values = kv_ref[:, HD:]
    frames = kv_ref.shape[0]
    visible = lax.broadcasted_iota(jnp.int32, (tokens, frames), 1) < frame_limit
    for head in range(columns // HD):
        scores = dot_nt(picked[:, head * HD : (head + 1) * HD], keys) * (1.0 / math.sqrt(HD))
        scores = jnp.where(visible, scores, -jnp.inf)
        raised = jnp.exp(scores - jnp.max(scores, axis=1, keepdims=True))
        chances = (raised / jnp.sum(raised, axis=1, keepdims=True)).astype(jnp.bfloat16)
        context[:, head * HD : (head + 1) * HD] = dot(chances, values).astype(jnp.bfloat16)
    to = lax.broadcasted_iota(jnp.int32, (tokens, tokens), 0)
    come = lax.broadcasted_iota(jnp.int32, (tokens, tokens), 1)
    low_bit = place_ref[2] % 2
    size = widths * pieces[0]
    block = to % size // pieces[0]
    section = jnp.where(to < size, 1 - section_pos, section_pos)
    first_order = (to % pieces[0] * sections + section) * widths + block % 2 * 2 + block // 2
    at = to - 2 * size
    size = widths * pieces[1]
    block = at % size // pieces[1]
    low = jnp.where(at < size, 1 - low_bit, low_bit)
    row = pieces[0] + at % pieces[1]
    second_order = (row * sections + block // 2) * widths + block % 2 * 2 + low
    move = come == jnp.where(at < 0, first_order, second_order)
    ordered = dot(jnp.where(move, 1.0, 0.0).astype(jnp.bfloat16), context[...])
    ordered = ordered.astype(jnp.bfloat16)
    for number in range(tiles):
        w_copies[number].wait()
        product = dot(ordered, weights[number]).astype(jnp.bfloat16)
        first = 0
        for out in outs:
            out[:, number * tile : (number + 1) * tile] = product[first : first + out.shape[0], :]
            first += out.shape[0]


def attend(place, slot_utt, frame_len, payloads, keys_values, weights, pieces, sections, widths, slots):
    count = len(payloads)
    columns, width = weights.shape
    capacity = sum(pieces) * sections * widths
    tile = 1024
    tiles = width // tile
    shapes = [
        jax.ShapeDtypeStruct((piece * widths, width), jnp.bfloat16)
        for piece in pieces
        for _ in range(2)
    ]
    return pl.pallas_call(
        functools.partial(
            attention_kernel, count, slots, capacity, pieces, sections, widths, tile
        ),
        in_specs=[SCALARS] * 3 + [INSIDE] * (count + 1) + [ANYWHERE],
        out_specs=[INSIDE] * len(shapes),
        out_shape=shapes,
        scratch_shapes=[
            pltpu.VMEM((tiles, columns, tile), jnp.bfloat16),
            pltpu.VMEM((capacity, columns), jnp.bfloat16),
            pltpu.VMEM((capacity, columns), jnp.bfloat16),
            pltpu.SemaphoreType.DMA((tiles,)),
        ],
        cost_estimate=pl.CostEstimate(
            flops=2 * capacity * columns * (width + 2 * keys_values.shape[0]),
            bytes_accessed=2 * columns * width + 2 * capacity * width,
            transcendentals=capacity * keys_values.shape[0] * columns // HD,
        ),
        compiler_params=pltpu.CompilerParams(vmem_limit_bytes=24 << 20),
        name="attention_projection",
    )(place, slot_utt, frame_len, *payloads, keys_values, in_hbm(weights))


def fold_kernel(sides, joined, place_ref, *refs):
    count = len(sides)
    parts, outs = refs[: 2 * count], refs[2 * count :]
    first = 0
    for number, side in enumerate(sides):
        kept_ref, came_ref = parts[2 * number : 2 * number + 2]
        total = kept_ref[...].astype(jnp.float32) + came_ref[...].astype(jnp.float32)
        half = total.shape[0] // 2
        top, bottom = total[:half], total[half:]
        upper = side(place_ref) == 0
        kept = jnp.where(upper, top, bottom)
        sent = jnp.where(upper, bottom, top).astype(jnp.bfloat16)
        if joined:
            outs[0][first : first + half, :] = kept
            outs[1][first : first + half, :] = sent
            first += half
        else:
            outs[2 * number][...] = kept
            outs[2 * number + 1][...] = sent


def fold(place, parts, sides, joined):
    width = parts[0].shape[1]
    halves = [part.shape[0] // 2 for part in parts[::2]]
    if joined:
        halves = [sum(halves)]
    shapes = [
        jax.ShapeDtypeStruct((half, width), kind)
        for half in halves
        for kind in (jnp.float32, jnp.bfloat16)
    ]
    return pl.pallas_call(
        functools.partial(fold_kernel, sides, joined),
        in_specs=[SCALARS] + [INSIDE] * len(parts),
        out_specs=[INSIDE] * len(shapes),
        out_shape=shapes,
        compiler_params=pltpu.CompilerParams(vmem_limit_bytes=24 << 20),
        name="sum_phase",
    )(place, *parts)


def section_side(place_ref):
    return place_ref[0]


def low_side(place_ref):
    return place_ref[2] % 2


def high_side(place_ref):
    return place_ref[2] // 2


def norm_kernel(count, slots, tokens, place_ref, slot_ref, *refs):
    payloads, (kept, other) = refs[:count], refs[count : count + 2]
    out_ref, picked, total = refs[count + 2 :]
    rows, width = total.shape
    columns = picked.shape[1]
    share = picked.shape[0] // (width // columns + 1)
    source = choice_of_payload(place_ref, slot_ref, slots)
    for choice in range(count):

        @pl.when(source == choice)
        def _(payload=payloads[choice]):
            picked[...] = payload[tokens:, :]

    total[...] = kept[...] + other[...].astype(jnp.float32)
    for part in range(width // columns):
        take = slice(part * columns, (part + 1) * columns)
        total[:, take] += picked[part * share : part * share + rows, :].astype(jnp.float32)
    shape = out_ref.shape[:2]
    normed = square_norm(total[...]).reshape(*shape, width)
    out_ref[:, :, :width] = normed.astype(jnp.bfloat16)
    last = width // columns * share
    target = picked[last : last + rows, :LANES].astype(jnp.float32).reshape(*shape, LANES)
    out_ref[:, :, width:] = target.astype(jnp.bfloat16)


def normed_rows(place, slot_utt, payloads, blocks, tokens, slots):
    width = blocks[0].shape[1]
    rows = blocks[0].shape[0]
    columns = payloads[0].shape[1]
    return pl.pallas_call(
        functools.partial(norm_kernel, len(payloads), slots, tokens),
        in_specs=[SCALARS] * 2 + [INSIDE] * (len(payloads) + len(blocks)),
        out_specs=INSIDE,
        out_shape=jax.ShapeDtypeStruct((rows // FOLD, FOLD, width + LANES), jnp.bfloat16),
        scratch_shapes=[
            pltpu.VMEM((payloads[0].shape[0] - tokens, columns), jnp.bfloat16),
            pltpu.VMEM((rows, width), jnp.float32),
        ],
        compiler_params=pltpu.CompilerParams(vmem_limit_bytes=16 << 20),
        name="token_rows",
    )(place, slot_utt, *payloads, *blocks)


def vocabulary_kernel(tile, count, first_ref, after_ref, *refs):
    sets, (head_ref, out_ref, rows_ref, stat) = refs[:count], refs[count:]
    vocab_rows, width = head_ref.shape
    share = sets[0].shape[0] * FOLD
    tokens = share * len(sets)
    cell = lax.broadcasted_iota(jnp.int32, (8, LANES), 1)
    take = jnp.where(cell == 0, 256.0, jnp.where(cell == 1, 1.0, 0.0)).astype(jnp.bfloat16)
    for number, rows in enumerate(sets):
        flat = rows[...].astype(jnp.float32).reshape(share, width + LANES)
        rows_ref[number * share : (number + 1) * share, :] = flat.astype(jnp.bfloat16)
    target = dot_nt(take, rows_ref[:, width:])[0:1, :].astype(jnp.int32) - first_ref[3]
    stat[0:1, :] = jnp.full((1, tokens), -jnp.inf, jnp.float32)
    stat[8:9, :] = jnp.zeros((1, tokens), jnp.float32)
    stat[16:17, :] = jnp.zeros((1, tokens), jnp.float32)

    for start in range(0, vocab_rows, tile):
        logits = dot_nt(head_ref[start : start + tile, :], rows_ref[:, :width])
        vocab = lax.broadcasted_iota(jnp.int32, logits.shape, 0) + start
        before = stat[0:1, :]
        upper = jnp.maximum(before, jnp.max(logits, axis=0, keepdims=True))
        stat[8:9, :] = stat[8:9, :] * jnp.exp(before - upper) + jnp.sum(
            jnp.exp(logits - upper), axis=0, keepdims=True
        )
        stat[16:17, :] += jnp.sum(jnp.where(vocab == target, logits, 0.0), axis=0, keepdims=True)
        stat[0:1, :] = upper

    for number in range(len(sets)):
        for row in range(3):
            out_ref[number, row : row + 1, :] = stat[
                8 * row : 8 * row + 1, number * share : (number + 1) * share
            ]


def vocabulary_stats(place, after, sets, head):
    share = sets[0].shape[0] * FOLD
    count = len(sets)
    width = head.shape[1]
    tokens = share * count
    return pl.pallas_call(
        functools.partial(vocabulary_kernel, head.shape[0], count),
        in_specs=[SCALARS, ANYWHERE] + [INSIDE] * (count + 1),
        out_specs=INSIDE,
        out_shape=jax.ShapeDtypeStruct((count, 8, share), jnp.float32),
        scratch_shapes=[
            pltpu.VMEM((tokens, width + LANES), jnp.bfloat16),
            pltpu.VMEM((24, tokens), jnp.float32),
        ],
        cost_estimate=pl.CostEstimate(
            flops=3 * tokens * head.shape[0] * width,
            bytes_accessed=2 * tokens * width,
            transcendentals=tokens * head.shape[0],
        ),
        compiler_params=pltpu.CompilerParams(vmem_limit_bytes=16 << 20),
        name="vocabulary_scores",
    )(place, after, *sets, pltpu.with_memory_space_constraint(head, pltpu.VMEM))


def zero_kernel(after_ref, head_ref, out_ref):
    out_ref[...] = jnp.zeros_like(out_ref)


def head_in_vmem(after, head):
    return pl.pallas_call(
        zero_kernel,
        in_specs=[ANYWHERE, INSIDE],
        out_specs=INSIDE,
        out_shape=jax.ShapeDtypeStruct((8, LANES), jnp.float32),
        compiler_params=pltpu.CompilerParams(vmem_limit_bytes=16 << 20),
        name="vocabulary_rows",
    )(after, pltpu.with_memory_space_constraint(head, pltpu.VMEM))


def spread_kernel(order, sections, groups, widths, place_ref, slot_ref, *refs):
    stats, (out_ref, table, block) = refs[:-3], refs[-3:]
    share = table.shape[2]
    for stat, places in zip(stats, order):
        for number, at in enumerate(places):
            table[at] = stat[number]
    slots = slot_ref.shape[0] // groups
    block[...] = jnp.zeros_like(block)
    for group in range(groups):
        for slot in range(slots):
            utterance = jnp.maximum(slot_ref[group * slots + slot], 0)
            for section in range(sections):
                at = (section ^ place_ref[0]) * groups + (utterance ^ place_ref[1])
                block[group, 3 * slot : 3 * slot + 3, section * share : (section + 1) * share] = (
                    table[at][0:3, :]
                )
    for section in range(sections):
        for group in range(groups):
            for width in range(widths):
                out_ref[(section * groups + group) * widths + width] = block[group]


def spread_stats(place, slot_utt, stats, order, sections, groups, widths):
    share = stats[0].shape[2]
    assert 3 * slot_utt.shape[0] // groups <= 8
    return pl.pallas_call(
        functools.partial(spread_kernel, order, sections, groups, widths),
        in_specs=[SCALARS] * 2 + [INSIDE] * len(stats),
        out_specs=INSIDE,
        out_shape=jax.ShapeDtypeStruct(
            (sections * groups * widths, 8, sections * share), jnp.float32
        ),
        scratch_shapes=[
            pltpu.VMEM((sections * groups, 8, share), jnp.float32),
            pltpu.VMEM((groups, 8, sections * share), jnp.float32),
        ],
        compiler_params=pltpu.CompilerParams(vmem_limit_bytes=16 << 20),
        name="statistics_by_group",
    )(place, slot_utt, *stats)


def score_kernel(sections, widths, place_ref, slot_ref, length_ref, every_ref, out_ref):
    slots, hyps = out_ref.shape
    lanes = every_ref.shape[2]
    share = lanes // sections // widths
    lane = lax.broadcasted_iota(jnp.int32, (1, lanes), 1)
    order = lane % share * (sections * widths) + lane // share
    column = lax.broadcasted_iota(jnp.int32, (1, hyps), 1)
    for slot in range(slots):
        upper = every_ref[:, 3 * slot, :]
        peak = jnp.max(upper, axis=0, keepdims=True)
        total = jnp.sum(
            every_ref[:, 3 * slot + 1, :] * jnp.exp(upper - peak), axis=0, keepdims=True
        )
        picked = jnp.sum(every_ref[:, 3 * slot + 2, :], axis=0, keepdims=True)
        logp = picked - (peak + jnp.log(total))
        scores = jnp.zeros((1, hyps), jnp.float32)
        start = jnp.int32(0)
        for hyp in range(hyps):
            length = length_ref[slot, hyp]
            valid = (order >= start) & (order < start + length)
            summed = jnp.sum(jnp.where(valid, logp, 0.0), axis=1, keepdims=True)
            mean = summed / jnp.full((1, 1), length, jnp.int32).astype(jnp.float32)
            scores = jnp.where(column == hyp, mean + math.log(V), scores)
            start = start + length
        filled = slot_ref[place_ref[1] * slots + slot] >= 0
        out_ref[slot : slot + 1, :] = jnp.where(filled, scores, 0.0)


def hypothesis_scores(place, slot_utt, lengths, every, slots, hyps, sections, widths):
    return pl.pallas_call(
        functools.partial(score_kernel, sections, widths),
        in_specs=[SCALARS] * 3 + [INSIDE],
        out_specs=INSIDE,
        out_shape=jax.ShapeDtypeStruct((slots, hyps), jnp.float32),
        compiler_params=pltpu.CompilerParams(vmem_limit_bytes=16 << 20),
        name="hypothesis_scores",
    )(place, slot_utt, lengths, every)


def rest(pieces, slot_tokens, place, slot_utt, frame_len, hyp_len, payloads, keys_values, o_proj, head):
    section_count = lax.axis_size("section")
    group_count = lax.axis_size("tm")
    width_count = lax.axis_size("mp")
    section_pos = lax.axis_index("section")
    width_pos = lax.axis_index("mp")
    slot_count, hyp_count = hyp_len.shape
    projected = attend(
        place,
        slot_utt,
        frame_len,
        payloads,
        keys_values,
        o_proj,
        pieces,
        section_count,
        width_count,
        slot_count,
    )

    kept, sent, other_kept, other_sent = fold(
        place,
        [projected[1], swap(projected[0], "section", 1), projected[3], swap(projected[2], "mp", 1)],
        [low_side, section_side],
        False,
    )
    kept, sent = fold(
        place,
        [kept, swap(sent, "mp", 1), other_kept, swap(other_sent, "section", 1)],
        [high_side, high_side],
        True,
    )
    out_rows = normed_rows(
        place, slot_utt, payloads, [kept, swap(sent, "mp", 2)], slot_tokens, slot_count
    )

    own = jnp.zeros((width_count, *out_rows.shape), jnp.bfloat16)
    for distance in range(width_count):
        block = swap(out_rows, "mp", distance) if distance else out_rows
        own = lax.dynamic_update_index_in_dim(own, block, width_pos ^ distance, 0)
    own = own.reshape(-1, *out_rows.shape[1:])
    half = own.shape[0] // 2
    by_x = swap(own, "section", 1)
    by_y = swap(own, "tm", 2)
    beside = swap(own, "tm", 1)
    by_x, by_y, zeros = lax.optimization_barrier((by_x, by_y, head_in_vmem(beside, head)))
    across = [swap(by_x[:half], "tm", 2), swap(by_y[half:], "section", 1)]
    near = vocabulary_stats(
        place, zeros, [by_y, swap(by_y, "tm", 1), by_x, swap(by_x, "tm", 1)], head
    )
    *across, near = lax.optimization_barrier((*across, near))
    across = jnp.concatenate(across)
    far = vocabulary_stats(place, zeros, [across, swap(across, "tm", 1), own, beside], head)
    stats = [near, far]
    order = ((2, 3, 4, 5), (6, 7, 0, 1))

    every = exchange(
        spread_stats(place, slot_utt, stats, order, section_count, group_count, width_count), ALL
    )
    return hypothesis_scores(
        place, slot_utt, hyp_len, every, slot_count, hyp_count, section_count, width_count
    )


def near_device(
    frame_len,
    slot_utt,
    enc_in,
    ffn_up,
    ffn_down,
    kv_proj,
    hyp_state,
    hyp_tok,
    hyp_len,
    q_proj,
    o_proj,
    head,
):
    section_count = lax.axis_size("section")
    group_count = lax.axis_size("tm")
    width_count = lax.axis_size("mp")
    section_pos = lax.axis_index("section")
    group_pos = lax.axis_index("tm")
    width_pos = lax.axis_index("mp")
    head_devices = section_count * width_count
    all_devices = head_devices * group_count

    frame_rows, utterances, enc_width = enc_in.shape
    slot_count, hyp_count, positions, model_width = hyp_state.shape
    slot_tokens = hyp_count * positions
    share_rows = slot_tokens // head_devices
    vocab_start = (
        (section_pos * group_count + group_pos) * width_count + width_pos
    ) * head.shape[0]
    head_pos = section_pos * width_count + width_pos
    place = jnp.stack([section_pos, group_pos, width_pos, vocab_start, head_pos])
    place = place.astype(jnp.int32)

    parts, own_frames = ffn(place, enc_in, ffn_up, ffn_down, width_count)
    parts = exchange(parts, "mp")

    blocks = queries_of(
        place,
        slot_utt,
        hyp_len,
        place,
        hyp_state.reshape(slot_count, slot_tokens, model_width),
        hyp_tok.reshape(slot_count, 1, slot_tokens),
        q_proj,
        group_count,
        share_rows,
    )
    crossing = blocks[2] + swap(blocks[3], "tm", 1)
    payloads = [blocks[0], swap(blocks[1], "tm", 1), swap(crossing, "tm", 2)]

    sent = keys_values_of(
        parts, own_frames, kv_proj, blocks[0], section_count, utterances, width_count
    )
    frames_all = all_devices * (frame_rows // width_count)
    keys_values = exchange(sent.reshape(all_devices, -1, 2 * HD), ALL).reshape(frames_all, 2 * HD)

    here_slots = lax.dynamic_slice_in_dim(slot_utt, group_pos * slot_count, slot_count, 0)
    filled = jnp.where(here_slots >= 0, jnp.sum(hyp_len, axis=1), 0)
    count = jnp.max(filled).reshape(1)
    most = count
    for distance in range(1, group_count):
        most = jnp.maximum(most, swap(count, "tm", distance))
    operands = (place, slot_utt, frame_len, hyp_len, payloads, keys_values, o_proj, head)
    few = share_rows * 3 // 4
    return lax.cond(
        most[0] <= few * head_devices,
        functools.partial(rest, (few - few // 3, few // 3), slot_tokens),
        functools.partial(rest, (share_rows // 2, share_rows - share_rows // 2), slot_tokens),
        *operands,
    )


def general(
    frame_len,
    slot_utt,
    enc_in,
    ffn_up,
    ffn_down,
    kv_proj,
    hyp_state,
    hyp_tok,
    hyp_len,
    q_proj,
    o_proj,
    head,
):
    section_count = lax.axis_size("section")
    group_count = lax.axis_size("tm")
    width_count = lax.axis_size("mp")
    section_pos = lax.axis_index("section")
    group_pos = lax.axis_index("tm")
    width_pos = lax.axis_index("mp")
    head_devices = section_count * width_count
    head_pos = section_pos * width_count + width_pos
    all_devices = head_devices * group_count

    frame_rows, utterances, enc_width = enc_in.shape
    assert utterances == group_count
    slot_count, hyp_count, positions, model_width = hyp_state.shape
    slot_tokens = hyp_count * positions
    device_heads = q_proj.shape[1] // HD
    group_heads = NH // KVH
    frame_share = frame_rows // width_count
    share_rows = slot_tokens // head_devices
    here_slots = lax.dynamic_slice_in_dim(slot_utt, group_pos * slot_count, slot_count, 0)

    dec_rows = hyp_state.reshape(slot_count * slot_tokens, model_width).astype(jnp.float32)
    queries = jnp.dot(
        square_norm(dec_rows).astype(jnp.bfloat16), q_proj, preferred_element_type=jnp.float32
    ).astype(jnp.bfloat16)
    queries = queries.reshape(slot_count, slot_tokens, device_heads * HD)
    shares = lax.dynamic_slice_in_dim(
        hyp_state.reshape(slot_count, slot_tokens, model_width), head_pos * share_rows, share_rows, 1
    )

    def by_utterance(values):
        out = []
        for utterance in range(utterances):
            block = values[0]
            for slot in range(1, slot_count):
                block = jnp.where(here_slots[slot] == utterance, values[slot], block)
            out.append(block)
        return jnp.stack(out)

    own_slot = jnp.argmax(slot_utt == group_pos)
    from_group = own_slot // slot_count
    queries = lax.dynamic_index_in_dim(
        exchange(by_utterance(queries), "tm"), from_group, 0, keepdims=False
    )
    resid_rows = lax.dynamic_index_in_dim(
        exchange(by_utterance(shares), "tm"), from_group, 0, keepdims=False
    )
    slot_targets = lax.all_gather(
        hyp_tok.reshape(slot_count, slot_tokens), "tm", axis=0, tiled=True
    )
    utt_slots = jnp.argmax(slot_utt[None, :] == jnp.arange(utterances)[:, None], axis=1)
    targets = jnp.take(slot_targets, utt_slots, axis=0).reshape(utterances * slot_tokens)

    enc_flat = (
        enc_in.reshape(width_count, frame_share, utterances, enc_width)
        .transpose(0, 2, 1, 3)
        .reshape(frame_rows * utterances, enc_width)
    )
    share_count = frame_share * utterances
    enc_normed = layer_norm(enc_flat.astype(jnp.float32)).astype(jnp.bfloat16)
    enc_inner = jax.nn.gelu(
        jnp.dot(enc_normed, ffn_up, preferred_element_type=jnp.float32), approximate=False
    ).astype(jnp.bfloat16)
    enc_summed = scatter_sum(
        jnp.dot(enc_inner, ffn_down, preferred_element_type=jnp.float32).astype(jnp.bfloat16),
        "mp",
        width_count,
    )
    own_frames = lax.dynamic_slice_in_dim(enc_flat, width_pos * share_count, share_count, 0)
    enc_states = layer_norm(own_frames.astype(jnp.float32) + enc_summed).astype(jnp.bfloat16)
    keys_values = jnp.dot(enc_states, kv_proj, preferred_element_type=jnp.float32).astype(
        jnp.bfloat16
    )
    keys_values = keys_values.reshape(utterances, frame_share, 2, KVH, HD)
    sent = []
    for section in range(section_count):
        per_width = []
        for width in range(width_count):
            kv_head = (section * width_count + width) * device_heads // group_heads
            per_width.append(
                keys_values[:, :, :, kv_head].reshape(utterances, frame_share, 2 * HD)
            )
        sent.append(jnp.stack(per_width, axis=1))
    sent = jnp.stack(sent).reshape(all_devices, frame_share, 2 * HD)
    frames_all = all_devices * frame_share
    keys_values = exchange(sent, ALL).reshape(frames_all, 2 * HD)

    frame_limit = lax.dynamic_index_in_dim(frame_len, group_pos, 0, keepdims=False)
    queries = queries.reshape(slot_tokens, device_heads, HD)
    scores = jnp.einsum(
        "qhd,fd->hqf", queries, keys_values[:, :HD], preferred_element_type=jnp.float32
    ) / math.sqrt(HD)
    visible = jnp.arange(frames_all, dtype=jnp.int32) < frame_limit
    scores = jnp.where(visible[None, None, :], scores, -jnp.inf)
    weights = jax.nn.softmax(scores, axis=-1).astype(jnp.bfloat16)
    context = jnp.einsum(
        "hqf,fd->qhd", weights, keys_values[:, HD:], preferred_element_type=jnp.float32
    ).astype(jnp.bfloat16)
    partial = jnp.dot(
        context.reshape(slot_tokens, device_heads * HD), o_proj, preferred_element_type=jnp.float32
    ).astype(jnp.bfloat16)
    partial = scatter_sum(partial, "section", section_count).astype(jnp.bfloat16)
    attn_out = scatter_sum(partial, "mp", width_count)
    out_normed = square_norm(resid_rows.astype(jnp.float32) + attn_out).astype(jnp.bfloat16)

    hidden_rows = lax.all_gather(out_normed, ALL, axis=0, tiled=True)
    logits = lax.dot_general(
        hidden_rows, head, (((1,), (1,)), ((), ())), preferred_element_type=jnp.float32
    )
    vocab_rows = head.shape[0]
    vocab_start = (
        (section_pos * group_count + group_pos) * width_count + width_pos
    ) * vocab_rows
    target_rows = (
        targets.reshape(utterances, section_count, width_count, share_rows)
        .transpose(1, 0, 2, 3)
        .reshape(-1)
    )
    upper = jnp.max(logits, axis=1)
    totals = jnp.sum(jnp.exp(logits - upper[:, None]), axis=1)
    matches = (
        jnp.arange(vocab_rows, dtype=jnp.int32)[None, :] == (target_rows - vocab_start)[:, None]
    )
    target_logit = jnp.sum(jnp.where(matches, logits, 0.0), axis=1)

    stats = jnp.stack([upper, totals, target_logit])
    stats = stats.reshape(3, section_count, utterances, width_count, share_rows)
    stats = stats.transpose(2, 0, 1, 3, 4).reshape(utterances, 3, slot_tokens)
    by_slot = jnp.take(stats, jnp.maximum(slot_utt, 0), axis=0)
    by_group = by_slot.reshape(1, group_count, 1, slot_count, 3, slot_tokens)
    by_group = jnp.broadcast_to(
        by_group, (section_count, group_count, width_count, slot_count, 3, slot_tokens)
    ).reshape(all_devices, slot_count, 3, slot_tokens)
    every = exchange(by_group, ALL)
    peak = jnp.max(every[:, :, 0], axis=0)
    total = jnp.sum(every[:, :, 1] * jnp.exp(every[:, :, 0] - peak[None]), axis=0)
    picked = jnp.sum(every[:, :, 2], axis=0)
    token_logp = (picked - (peak + jnp.log(total))).reshape(slot_count, hyp_count, positions)
    valid = jnp.arange(positions, dtype=jnp.int32)[None, None, :] < hyp_len[:, :, None]
    summed = jnp.sum(jnp.where(valid, token_logp, 0.0), axis=-1) / hyp_len.astype(
        jnp.float32
    ) + math.log(V)
    return jnp.where(here_slots[:, None] >= 0, summed, 0.0)


def solution(mesh):
    in_specs = (
        P(),
        P(),
        P(("section", "tm"), None, None),
        P(None, "mp"),
        P("mp", None),
        P(),
        P("tm", None, None, None),
        P("tm", None, None),
        P("tm", None),
        P(None, ("section", "mp")),
        P(("section", "mp"), None),
        P(("section", "tm", "mp"), None),
    )
    out_specs = P("tm", None)
    near = dict(mesh.shape) == {"section": 2, "tm": 4, "mp": 4}
    per_device = near_device if near else general
    return jax.shard_map(
        per_device, mesh=mesh, in_specs=in_specs, out_specs=out_specs, check_vma=False
    )
```

```python
import functools
import math

import jax
import jax.numpy as jnp
from jax import lax
from jax.experimental import pallas as pl
from jax.experimental.pallas import tpu as pltpu
from jax.sharding import PartitionSpec as P

NH = 32
KVH = 4
HD = 128
V = 64000
ALL = ("section", "tm", "mp")
LANES = 128
FOLD = 4


def layer_norm(values):
    center = values - jnp.mean(values, axis=-1, keepdims=True)
    spread = jnp.mean(center * center, axis=-1, keepdims=True)
    return center * lax.rsqrt(spread + 1e-05)


def square_norm(values):
    return values * lax.rsqrt(jnp.mean(values * values, axis=-1, keepdims=True) + 1e-06)


def exchange(blocks, axis):
    return lax.all_to_all(blocks, axis, split_axis=0, concat_axis=0, tiled=True)


def scatter_sum(partial, axis, count):
    blocks = partial.reshape((count, partial.shape[0] // count) + partial.shape[1:])
    return jnp.sum(exchange(blocks, axis).astype(jnp.float32), axis=0)


def swap(values, axis, distance):
    pairs = [(i, i ^ distance) for i in range(lax.axis_size(axis))]
    return lax.ppermute(values, axis, pairs)


def whole(shape):
    return pl.BlockSpec(shape, lambda *_: (0,) * len(shape))


SCALARS = pl.BlockSpec(memory_space=pltpu.SMEM)


def dot(left, right):
    return jnp.dot(left, right, preferred_element_type=jnp.float32)


def dot_nt(left, right):
    return lax.dot_general(
        left, right, (((1,), (1,)), ((), ())), preferred_element_type=jnp.float32
    )


def start_copies(source_of, target_of, semaphores, count):
    copies = []
    for number in range(count):
        copy = pltpu.make_async_copy(
            source_of(number), target_of(number), semaphores.at[number]
        )
        copy.start()
        copies.append(copy)
    return copies


def ffn_kernel(tile, place_ref, x_ref, up_ref, down_ref, *refs):
    out_ref, own_ref, inputs, rows, up, down, x_sem, up_sem, down_sem = refs
    count, share, width = out_ref.shape
    tiles = up_ref.shape[1] // tile
    x_copy = start_copies(lambda i: x_ref, lambda i: inputs, x_sem, 1)[0]
    up_copies = start_copies(
        lambda i: up_ref.at[:, pl.ds(i * tile, tile)], lambda i: up.at[i], up_sem, tiles
    )
    x_copy.wait()
    rows[...] = inputs[...].astype(jnp.float32).reshape(rows.shape)
    start = pl.multiple_of(place_ref[2] * share, share)
    own_ref[...] = rows[pl.ds(start, share), :].astype(jnp.bfloat16)
    normed = layer_norm(rows[...]).astype(jnp.bfloat16)
    inner = []
    for number in range(tiles):
        up_copies[number].wait()
        if number == 0:
            down_copies = start_copies(
                lambda i: down_ref.at[pl.ds(i * tile, tile), :],
                lambda i: down.at[i],
                down_sem,
                tiles,
            )
        hidden = dot(normed, up[number])
        hidden = 0.5 * hidden * (1.0 + lax.erf(hidden * math.sqrt(0.5)))
        inner.append(hidden.astype(jnp.bfloat16))
    total = None
    for number in range(tiles):
        down_copies[number].wait()
        product = dot(inner[number], down[number])
        total = product if total is None else total + product
    for part in range(count):
        out_ref[part] = total[part * share : (part + 1) * share, :].astype(jnp.bfloat16)


def in_hbm(values):
    return pltpu.with_memory_space_constraint(values, pltpu.HBM)


ANYWHERE = pl.BlockSpec(memory_space=pl.ANY)
INSIDE = pl.BlockSpec(memory_space=pltpu.VMEM)


def ffn(place, enc_in, up, down, count):
    frames, utterances, width = enc_in.shape
    rows = frames * utterances
    share = rows // count
    tile = 256
    tiles = up.shape[1] // tile
    return pl.pallas_call(
        functools.partial(ffn_kernel, tile),
        in_specs=[SCALARS] + [ANYWHERE] * 3,
        out_specs=[INSIDE] * 2,
        out_shape=[
            jax.ShapeDtypeStruct((count, share, width), jnp.bfloat16),
            jax.ShapeDtypeStruct((share, width), jnp.bfloat16),
        ],
        scratch_shapes=[
            pltpu.VMEM(enc_in.shape, jnp.bfloat16),
            pltpu.VMEM((rows, width), jnp.float32),
            pltpu.VMEM((tiles, width, tile), jnp.bfloat16),
            pltpu.VMEM((tiles, tile, width), jnp.bfloat16),
            pltpu.SemaphoreType.DMA((1,)),
            pltpu.SemaphoreType.DMA((tiles,)),
            pltpu.SemaphoreType.DMA((tiles,)),
        ],
        cost_estimate=pl.CostEstimate(
            flops=4 * rows * width * up.shape[1],
            bytes_accessed=4 * width * up.shape[1],
            transcendentals=rows * up.shape[1],
        ),
        compiler_params=pltpu.CompilerParams(vmem_limit_bytes=24 << 20),
        name="encoder_ffn",
    )(place, in_hbm(enc_in), in_hbm(up), in_hbm(down))


def query_kernel(
    count, depth, place_ref, slot_ref, length_ref, after_ref, x_ref, tok_ref, w_ref, *refs
):
    outs, (states, weights, normed, total, shares, x_sem, w_sem) = refs[:count], refs[count:]
    slots, tokens, width = x_ref.shape
    hyps = length_ref.shape[1]
    positions = tokens // hyps
    columns = w_ref.shape[1]
    share = shares.shape[1] // 2
    parts = width // columns
    x_copies = start_copies(lambda i: x_ref.at[i], lambda i: states.at[i], x_sem, slots)
    w_copies = start_copies(
        lambda i: w_ref.at[pl.ds(i * depth, depth), :],
        lambda i: weights.at[i],
        w_sem,
        width // depth,
    )
    head_pos = place_ref[4]
    lane = lax.broadcasted_iota(jnp.int32, (1, tokens), 1)
    for slot in range(slots):
        order = jnp.full((1, tokens), -1, jnp.int32)
        start = jnp.int32(0)
        for hyp in range(hyps):
            length = length_ref[slot, hyp]
            inside = (lane >= hyp * positions) & (lane < hyp * positions + length)
            order = jnp.where(inside, lane - hyp * positions + start, order)
            start = start + length
        row = lax.broadcasted_iota(jnp.int32, (tokens, tokens), 0)
        move = jnp.where(order == row, 1.0, 0.0).astype(jnp.bfloat16)
        x_copies[slot].wait()
        ordered = dot(move, states[slot])
        normed[slot * tokens : (slot + 1) * tokens, :] = square_norm(ordered).astype(jnp.bfloat16)
        share_row = lax.broadcasted_iota(jnp.int32, (share, tokens), 0)
        chosen = order == share_row * (tokens // share) + head_pos
        mine = dot(jnp.where(chosen, 1.0, 0.0).astype(jnp.bfloat16), states[slot])
        shares[slot, :share, :] = mine.astype(jnp.bfloat16)
        target = jnp.sum(
            jnp.where(chosen, tok_ref[slot], 0), axis=1, keepdims=True, dtype=jnp.int32
        )
        coarse = target // 256
        cell = lax.broadcasted_iota(jnp.int32, (share, columns), 1)
        packed = jnp.where(cell == 0, coarse, jnp.where(cell == 1, target - coarse * 256, 0))
        shares[slot, share:, :columns] = packed.astype(jnp.float32).astype(jnp.bfloat16)
    for number in range(width // depth):
        w_copies[number].wait()
        product = dot(normed[:, number * depth : (number + 1) * depth], weights[number])
        if number == 0:
            total[...] = product
        else:
            total[...] += product
    group = place_ref[1]
    for distance in range(count):
        slot = jnp.int32(-1)
        for candidate in range(slots):
            holds = slot_ref[group * slots + candidate] == group ^ distance
            slot = jnp.where(holds, candidate, slot)
        out = outs[distance]

        @pl.when(slot < 0)
        def _(out=out):
            out[...] = jnp.zeros_like(out)

        @pl.when(slot >= 0)
        def _(out=out, slot=slot):
            start = pl.multiple_of(slot * tokens, tokens)
            out[:tokens, :] = total[pl.ds(start, tokens), :].astype(jnp.bfloat16)
            for part in range(parts):
                first = tokens + part * share
                out[first : first + share, :] = shares[
                    slot, :share, part * columns : (part + 1) * columns
                ]
            out[tokens + parts * share :, :] = shares[slot, share:, :columns]


def queries_of(place, slot_utt, lengths, after, states, targets, weights, count, share):
    slots, tokens, width = states.shape
    columns = weights.shape[1]
    depth = 1024
    rows = tokens + (width // columns + 1) * share
    block = jax.ShapeDtypeStruct((rows, columns), jnp.bfloat16)
    return pl.pallas_call(
        functools.partial(query_kernel, count, depth),
        in_specs=[SCALARS] * 3 + [ANYWHERE, ANYWHERE, INSIDE, ANYWHERE],
        out_specs=[INSIDE] * count,
        out_shape=[block] * count,
        scratch_shapes=[
            pltpu.VMEM(states.shape, jnp.bfloat16),
            pltpu.VMEM((width // depth, depth, columns), jnp.bfloat16),
            pltpu.VMEM((slots * tokens, width), jnp.bfloat16),
            pltpu.VMEM((slots * tokens, columns), jnp.float32),
            pltpu.VMEM((slots, 2 * share, width), jnp.bfloat16),
            pltpu.SemaphoreType.DMA((slots,)),
            pltpu.SemaphoreType.DMA((width // depth,)),
        ],
        cost_estimate=pl.CostEstimate(
            flops=2 * slots * tokens * width * columns,
            bytes_accessed=2 * width * (columns + slots * tokens),
            transcendentals=0,
        ),
        compiler_params=pltpu.CompilerParams(vmem_limit_bytes=32 << 20),
        name="hypothesis_queries",
    )(place, slot_utt, lengths, after, in_hbm(states), targets, in_hbm(weights))


def kv_kernel(sections, utterances, widths, *refs):
    parts_ref, own_ref, w_ref, after_ref, out_ref = refs
    rows = own_ref.shape[0]
    frames = rows // utterances
    total = own_ref[...].astype(jnp.float32)
    summed = parts_ref[0].astype(jnp.float32)
    for part in range(1, parts_ref.shape[0]):
        summed += parts_ref[part].astype(jnp.float32)
    states = layer_norm(total + summed).astype(jnp.bfloat16)
    to = lax.broadcasted_iota(jnp.int32, (rows, rows), 0)
    come = lax.broadcasted_iota(jnp.int32, (rows, rows), 1)
    move = jnp.where(come == to % frames * utterances + to // frames, 1.0, 0.0)
    states = dot(move.astype(jnp.bfloat16), states).astype(jnp.bfloat16)
    both = dot(states, w_ref[...])
    half = KVH * HD
    per_kv = sections * widths // KVH
    for section in range(sections):
        for utterance in range(utterances):
            for width in range(0, widths, per_kv):
                kv_head = (section * widths + width) // per_kv
                take = slice(utterance * frames, (utterance + 1) * frames)
                block = jnp.concatenate(
                    [
                        both[take, kv_head * HD : (kv_head + 1) * HD],
                        both[take, half + kv_head * HD : half + (kv_head + 1) * HD],
                    ],
                    axis=1,
                )
                start = ((section * utterances + utterance) * widths + width) * frames
                block = jnp.concatenate([block] * per_kv, axis=0).astype(jnp.bfloat16)
                out_ref[start : start + per_kv * frames, :] = block


def keys_values_of(parts, own, weights, after, sections, utterances, widths):
    rows = sections * widths * own.shape[0]
    return pl.pallas_call(
        functools.partial(kv_kernel, sections, utterances, widths),
        in_specs=[INSIDE] * 3 + [ANYWHERE],
        out_specs=INSIDE,
        out_shape=jax.ShapeDtypeStruct((rows, 2 * HD), jnp.bfloat16),
        cost_estimate=pl.CostEstimate(
            flops=2 * own.shape[0] * weights.shape[0] * weights.shape[1],
            bytes_accessed=2 * weights.shape[0] * weights.shape[1],
            transcendentals=0,
        ),
        compiler_params=pltpu.CompilerParams(vmem_limit_bytes=24 << 20),
        name="frame_keys_values",
    )(parts, own, weights, after)


def choice_of_payload(place_ref, slot_ref, slots):
    group = place_ref[1]
    source = jnp.int32(0)
    for slot in range(slot_ref.shape[0]):
        source = jnp.where(slot_ref[slot] == group, slot // slots, source)
    return jnp.minimum(source ^ group, 2)


def attention_kernel(count, slots, capacity, pieces, sections, widths, tile, *refs):
    place_ref, slot_ref, frame_ref = refs[:3]
    payloads, (kv_ref, w_ref) = refs[3 : 3 + count], refs[3 + count : 5 + count]
    outs = refs[5 + count : 5 + count + 2 * len(pieces)]
    weights, picked, context, w_sem = refs[5 + count + 2 * len(pieces) :]
    tokens, columns = capacity, w_ref.shape[0]
    tiles = w_ref.shape[1] // tile
    w_copies = start_copies(
        lambda i: w_ref.at[:, pl.ds(i * tile, tile)], lambda i: weights.at[i], w_sem, tiles
    )
    source = choice_of_payload(place_ref, slot_ref, slots)
    section_pos = place_ref[0]
    frame_limit = frame_ref[place_ref[1]]
    for distance in range(count):

        @pl.when(source == distance)
        def _(payload=payloads[distance]):
            picked[...] = payload[:tokens, :]

    keys = kv_ref[:, :HD]
    values = kv_ref[:, HD:]
    frames = kv_ref.shape[0]
    visible = lax.broadcasted_iota(jnp.int32, (tokens, frames), 1) < frame_limit
    for head in range(columns // HD):
        scores = dot_nt(picked[:, head * HD : (head + 1) * HD], keys) * (1.0 / math.sqrt(HD))
        scores = jnp.where(visible, scores, -jnp.inf)
        raised = jnp.exp(scores - jnp.max(scores, axis=1, keepdims=True))
        chances = (raised / jnp.sum(raised, axis=1, keepdims=True)).astype(jnp.bfloat16)
        context[:, head * HD : (head + 1) * HD] = dot(chances, values).astype(jnp.bfloat16)
    to = lax.broadcasted_iota(jnp.int32, (tokens, tokens), 0)
    come = lax.broadcasted_iota(jnp.int32, (tokens, tokens), 1)
    low_bit = place_ref[2] % 2
    size = widths * pieces[0]
    block = to % size // pieces[0]
    section = jnp.where(to < size, 1 - section_pos, section_pos)
    first_order = (to % pieces[0] * sections + section) * widths + block % 2 * 2 + block // 2
    at = to - 2 * size
    size = widths * pieces[1]
    block = at % size // pieces[1]
    low = jnp.where(at < size, 1 - low_bit, low_bit)
    row = pieces[0] + at % pieces[1]
    second_order = (row * sections + block // 2) * widths + block % 2 * 2 + low
    move = come == jnp.where(at < 0, first_order, second_order)
    ordered = dot(jnp.where(move, 1.0, 0.0).astype(jnp.bfloat16), context[...])
    ordered = ordered.astype(jnp.bfloat16)
    for number in range(tiles):
        w_copies[number].wait()
        product = dot(ordered, weights[number]).astype(jnp.bfloat16)
        first = 0
        for out in outs:
            out[:, number * tile : (number + 1) * tile] = product[first : first + out.shape[0], :]
            first += out.shape[0]


def attend(place, slot_utt, frame_len, payloads, keys_values, weights, pieces, sections, widths, slots):
    count = len(payloads)
    columns, width = weights.shape
    capacity = sum(pieces) * sections * widths
    tile = 1024
    tiles = width // tile
    shapes = [
        jax.ShapeDtypeStruct((piece * widths, width), jnp.bfloat16)
        for piece in pieces
        for _ in range(2)
    ]
    return pl.pallas_call(
        functools.partial(
            attention_kernel, count, slots, capacity, pieces, sections, widths, tile
        ),
        in_specs=[SCALARS] * 3 + [INSIDE] * (count + 1) + [ANYWHERE],
        out_specs=[INSIDE] * len(shapes),
        out_shape=shapes,
        scratch_shapes=[
            pltpu.VMEM((tiles, columns, tile), jnp.bfloat16),
            pltpu.VMEM((capacity, columns), jnp.bfloat16),
            pltpu.VMEM((capacity, columns), jnp.bfloat16),
            pltpu.SemaphoreType.DMA((tiles,)),
        ],
        cost_estimate=pl.CostEstimate(
            flops=2 * capacity * columns * (width + 2 * keys_values.shape[0]),
            bytes_accessed=2 * columns * width + 2 * capacity * width,
            transcendentals=capacity * keys_values.shape[0] * columns // HD,
        ),
        compiler_params=pltpu.CompilerParams(vmem_limit_bytes=24 << 20),
        name="attention_projection",
    )(place, slot_utt, frame_len, *payloads, keys_values, in_hbm(weights))


def fold_kernel(sides, joined, place_ref, *refs):
    count = len(sides)
    parts, outs = refs[: 2 * count], refs[2 * count :]
    first = 0
    for number, side in enumerate(sides):
        kept_ref, came_ref = parts[2 * number : 2 * number + 2]
        total = kept_ref[...].astype(jnp.float32) + came_ref[...].astype(jnp.float32)
        half = total.shape[0] // 2
        top, bottom = total[:half], total[half:]
        upper = side(place_ref) == 0
        kept = jnp.where(upper, top, bottom)
        sent = jnp.where(upper, bottom, top).astype(jnp.bfloat16)
        if joined:
            outs[0][first : first + half, :] = kept
            outs[1][first : first + half, :] = sent
            first += half
        else:
            outs[2 * number][...] = kept
            outs[2 * number + 1][...] = sent


def fold(place, parts, sides, joined):
    width = parts[0].shape[1]
    halves = [part.shape[0] // 2 for part in parts[::2]]
    if joined:
        halves = [sum(halves)]
    shapes = [
        jax.ShapeDtypeStruct((half, width), kind)
        for half in halves
        for kind in (jnp.float32, jnp.bfloat16)
    ]
    return pl.pallas_call(
        functools.partial(fold_kernel, sides, joined),
        in_specs=[SCALARS] + [INSIDE] * len(parts),
        out_specs=[INSIDE] * len(shapes),
        out_shape=shapes,
        compiler_params=pltpu.CompilerParams(vmem_limit_bytes=24 << 20),
        name="sum_phase",
    )(place, *parts)


def section_side(place_ref):
    return place_ref[0]


def low_side(place_ref):
    return place_ref[2] % 2


def high_side(place_ref):
    return place_ref[2] // 2


def norm_kernel(count, slots, tokens, place_ref, slot_ref, *refs):
    payloads, (kept, other) = refs[:count], refs[count : count + 2]
    out_ref, picked, total = refs[count + 2 :]
    rows, width = total.shape
    columns = picked.shape[1]
    share = picked.shape[0] // (width // columns + 1)
    source = choice_of_payload(place_ref, slot_ref, slots)
    for choice in range(count):

        @pl.when(source == choice)
        def _(payload=payloads[choice]):
            picked[...] = payload[tokens:, :]

    total[...] = kept[...] + other[...].astype(jnp.float32)
    for part in range(width // columns):
        take = slice(part * columns, (part + 1) * columns)
        total[:, take] += picked[part * share : part * share + rows, :].astype(jnp.float32)
    shape = out_ref.shape[:2]
    normed = square_norm(total[...]).reshape(*shape, width)
    out_ref[:, :, :width] = normed.astype(jnp.bfloat16)
    last = width // columns * share
    target = picked[last : last + rows, :LANES].astype(jnp.float32).reshape(*shape, LANES)
    out_ref[:, :, width:] = target.astype(jnp.bfloat16)


def normed_rows(place, slot_utt, payloads, blocks, tokens, slots):
    width = blocks[0].shape[1]
    rows = blocks[0].shape[0]
    columns = payloads[0].shape[1]
    return pl.pallas_call(
        functools.partial(norm_kernel, len(payloads), slots, tokens),
        in_specs=[SCALARS] * 2 + [INSIDE] * (len(payloads) + len(blocks)),
        out_specs=INSIDE,
        out_shape=jax.ShapeDtypeStruct((rows // FOLD, FOLD, width + LANES), jnp.bfloat16),
        scratch_shapes=[
            pltpu.VMEM((payloads[0].shape[0] - tokens, columns), jnp.bfloat16),
            pltpu.VMEM((rows, width), jnp.float32),
        ],
        compiler_params=pltpu.CompilerParams(vmem_limit_bytes=16 << 20),
        name="token_rows",
    )(place, slot_utt, *payloads, *blocks)


def vocabulary_kernel(tile, count, first_ref, after_ref, *refs):
    sets, (head_ref, out_ref, rows_ref, stat) = refs[:count], refs[count:]
    vocab_rows, width = head_ref.shape
    share = sets[0].shape[0] * FOLD
    tokens = share * len(sets)
    cell = lax.broadcasted_iota(jnp.int32, (8, LANES), 1)
    take = jnp.where(cell == 0, 256.0, jnp.where(cell == 1, 1.0, 0.0)).astype(jnp.bfloat16)
    for number, rows in enumerate(sets):
        flat = rows[...].astype(jnp.float32).reshape(share, width + LANES)
        rows_ref[number * share : (number + 1) * share, :] = flat.astype(jnp.bfloat16)
    target = dot_nt(take, rows_ref[:, width:])[0:1, :].astype(jnp.int32) - first_ref[3]
    stat[0:1, :] = jnp.full((1, tokens), -jnp.inf, jnp.float32)
    stat[8:9, :] = jnp.zeros((1, tokens), jnp.float32)
    stat[16:17, :] = jnp.zeros((1, tokens), jnp.float32)

    for start in range(0, vocab_rows, tile):
        logits = dot_nt(head_ref[start : start + tile, :], rows_ref[:, :width])
        vocab = lax.broadcasted_iota(jnp.int32, logits.shape, 0) + start
        before = stat[0:1, :]
        upper = jnp.maximum(before, jnp.max(logits, axis=0, keepdims=True))
        stat[8:9, :] = stat[8:9, :] * jnp.exp(before - upper) + jnp.sum(
            jnp.exp(logits - upper), axis=0, keepdims=True
        )
        stat[16:17, :] += jnp.sum(jnp.where(vocab == target, logits, 0.0), axis=0, keepdims=True)
        stat[0:1, :] = upper

    for number in range(len(sets)):
        for row in range(3):
            out_ref[number, row : row + 1, :] = stat[
                8 * row : 8 * row + 1, number * share : (number + 1) * share
            ]


def vocabulary_stats(place, after, sets, head):
    share = sets[0].shape[0] * FOLD
    count = len(sets)
    width = head.shape[1]
    tokens = share * count
    return pl.pallas_call(
        functools.partial(vocabulary_kernel, head.shape[0], count),
        in_specs=[SCALARS, ANYWHERE] + [INSIDE] * (count + 1),
        out_specs=INSIDE,
        out_shape=jax.ShapeDtypeStruct((count, 8, share), jnp.float32),
        scratch_shapes=[
            pltpu.VMEM((tokens, width + LANES), jnp.bfloat16),
            pltpu.VMEM((24, tokens), jnp.float32),
        ],
        cost_estimate=pl.CostEstimate(
            flops=3 * tokens * head.shape[0] * width,
            bytes_accessed=2 * tokens * width,
            transcendentals=tokens * head.shape[0],
        ),
        compiler_params=pltpu.CompilerParams(vmem_limit_bytes=16 << 20),
        name="vocabulary_scores",
    )(place, after, *sets, pltpu.with_memory_space_constraint(head, pltpu.VMEM))


def zero_kernel(after_ref, head_ref, out_ref):
    out_ref[...] = jnp.zeros_like(out_ref)


def head_in_vmem(after, head):
    return pl.pallas_call(
        zero_kernel,
        in_specs=[ANYWHERE, INSIDE],
        out_specs=INSIDE,
        out_shape=jax.ShapeDtypeStruct((8, LANES), jnp.float32),
        compiler_params=pltpu.CompilerParams(vmem_limit_bytes=16 << 20),
        name="vocabulary_rows",
    )(after, pltpu.with_memory_space_constraint(head, pltpu.VMEM))


def spread_kernel(order, sections, groups, widths, place_ref, slot_ref, *refs):
    stats, (out_ref, table, block) = refs[:-3], refs[-3:]
    share = table.shape[2]
    for stat, places in zip(stats, order):
        for number, at in enumerate(places):
            table[at] = stat[number]
    slots = slot_ref.shape[0] // groups
    block[...] = jnp.zeros_like(block)
    for group in range(groups):
        for slot in range(slots):
            utterance = jnp.maximum(slot_ref[group * slots + slot], 0)
            for section in range(sections):
                at = (section ^ place_ref[0]) * groups + (utterance ^ place_ref[1])
                block[group, 3 * slot : 3 * slot + 3, section * share : (section + 1) * share] = (
                    table[at][0:3, :]
                )
    for section in range(sections):
        for group in range(groups):
            for width in range(widths):
                out_ref[(section * groups + group) * widths + width] = block[group]


def spread_stats(place, slot_utt, stats, order, sections, groups, widths):
    share = stats[0].shape[2]
    assert 3 * slot_utt.shape[0] // groups <= 8
    return pl.pallas_call(
        functools.partial(spread_kernel, order, sections, groups, widths),
        in_specs=[SCALARS] * 2 + [INSIDE] * len(stats),
        out_specs=INSIDE,
        out_shape=jax.ShapeDtypeStruct(
            (sections * groups * widths, 8, sections * share), jnp.float32
        ),
        scratch_shapes=[
            pltpu.VMEM((sections * groups, 8, share), jnp.float32),
            pltpu.VMEM((groups, 8, sections * share), jnp.float32),
        ],
        compiler_params=pltpu.CompilerParams(vmem_limit_bytes=16 << 20),
        name="statistics_by_group",
    )(place, slot_utt, *stats)


def score_kernel(sections, widths, place_ref, slot_ref, length_ref, every_ref, out_ref):
    slots, hyps = out_ref.shape
    lanes = every_ref.shape[2]
    share = lanes // sections // widths
    lane = lax.broadcasted_iota(jnp.int32, (1, lanes), 1)
    order = lane % share * (sections * widths) + lane // share
    column = lax.broadcasted_iota(jnp.int32, (1, hyps), 1)
    for slot in range(slots):
        upper = every_ref[:, 3 * slot, :]
        peak = jnp.max(upper, axis=0, keepdims=True)
        total = jnp.sum(
            every_ref[:, 3 * slot + 1, :] * jnp.exp(upper - peak), axis=0, keepdims=True
        )
        picked = jnp.sum(every_ref[:, 3 * slot + 2, :], axis=0, keepdims=True)
        logp = picked - (peak + jnp.log(total))
        scores = jnp.zeros((1, hyps), jnp.float32)
        start = jnp.int32(0)
        for hyp in range(hyps):
            length = length_ref[slot, hyp]
            valid = (order >= start) & (order < start + length)
            summed = jnp.sum(jnp.where(valid, logp, 0.0), axis=1, keepdims=True)
            mean = summed / jnp.full((1, 1), length, jnp.int32).astype(jnp.float32)
            scores = jnp.where(column == hyp, mean + math.log(V), scores)
            start = start + length
        filled = slot_ref[place_ref[1] * slots + slot] >= 0
        out_ref[slot : slot + 1, :] = jnp.where(filled, scores, 0.0)


def hypothesis_scores(place, slot_utt, lengths, every, slots, hyps, sections, widths):
    return pl.pallas_call(
        functools.partial(score_kernel, sections, widths),
        in_specs=[SCALARS] * 3 + [INSIDE],
        out_specs=INSIDE,
        out_shape=pltpu.HBM((slots, hyps), jnp.float32),
        compiler_params=pltpu.CompilerParams(vmem_limit_bytes=16 << 20),
        name="hypothesis_scores",
    )(place, slot_utt, lengths, every)


def rest(pieces, slot_tokens, place, slot_utt, frame_len, hyp_len, payloads, keys_values, o_proj, head):
    section_count = lax.axis_size("section")
    group_count = lax.axis_size("tm")
    width_count = lax.axis_size("mp")
    section_pos = lax.axis_index("section")
    width_pos = lax.axis_index("mp")
    slot_count, hyp_count = hyp_len.shape
    projected = attend(
        place,
        slot_utt,
        frame_len,
        payloads,
        keys_values,
        o_proj,
        pieces,
        section_count,
        width_count,
        slot_count,
    )

    kept, sent, other_kept, other_sent = fold(
        place,
        [projected[1], swap(projected[0], "section", 1), projected[3], swap(projected[2], "mp", 1)],
        [low_side, section_side],
        False,
    )
    kept, sent = fold(
        place,
        [kept, swap(sent, "mp", 1), other_kept, swap(other_sent, "section", 1)],
        [high_side, high_side],
        True,
    )
    out_rows = normed_rows(
        place, slot_utt, payloads, [kept, swap(sent, "mp", 2)], slot_tokens, slot_count
    )

    own = jnp.zeros((width_count, *out_rows.shape), jnp.bfloat16)
    for distance in range(width_count):
        block = swap(out_rows, "mp", distance) if distance else out_rows
        own = lax.dynamic_update_index_in_dim(own, block, width_pos ^ distance, 0)
    own = own.reshape(-1, *out_rows.shape[1:])
    half = own.shape[0] // 2
    by_x = swap(own, "section", 1)
    by_y = swap(own, "tm", 2)
    beside = swap(own, "tm", 1)
    by_x, by_y, zeros = lax.optimization_barrier((by_x, by_y, head_in_vmem(beside, head)))
    across = [swap(by_x[:half], "tm", 2), swap(by_y[half:], "section", 1)]
    near = vocabulary_stats(
        place, zeros, [by_y, swap(by_y, "tm", 1), by_x, swap(by_x, "tm", 1)], head
    )
    *across, near = lax.optimization_barrier((*across, near))
    across = jnp.concatenate(across)
    far = vocabulary_stats(place, zeros, [across, swap(across, "tm", 1), own, beside], head)
    stats = [near, far]
    order = ((2, 3, 4, 5), (6, 7, 0, 1))

    every = exchange(
        spread_stats(place, slot_utt, stats, order, section_count, group_count, width_count), ALL
    )
    return hypothesis_scores(
        place, slot_utt, hyp_len, every, slot_count, hyp_count, section_count, width_count
    )


def near_device(
    frame_len,
    slot_utt,
    enc_in,
    ffn_up,
    ffn_down,
    kv_proj,
    hyp_state,
    hyp_tok,
    hyp_len,
    q_proj,
    o_proj,
    head,
):
    section_count = lax.axis_size("section")
    group_count = lax.axis_size("tm")
    width_count = lax.axis_size("mp")
    section_pos = lax.axis_index("section")
    group_pos = lax.axis_index("tm")
    width_pos = lax.axis_index("mp")
    head_devices = section_count * width_count
    all_devices = head_devices * group_count

    frame_rows, utterances, enc_width = enc_in.shape
    slot_count, hyp_count, positions, model_width = hyp_state.shape
    slot_tokens = hyp_count * positions
    share_rows = slot_tokens // head_devices
    vocab_start = (
        (section_pos * group_count + group_pos) * width_count + width_pos
    ) * head.shape[0]
    head_pos = section_pos * width_count + width_pos
    place = jnp.stack([section_pos, group_pos, width_pos, vocab_start, head_pos])
    place = place.astype(jnp.int32)

    parts, own_frames = ffn(place, enc_in, ffn_up, ffn_down, width_count)
    parts = exchange(parts, "mp")

    blocks = queries_of(
        place,
        slot_utt,
        hyp_len,
        place,
        hyp_state.reshape(slot_count, slot_tokens, model_width),
        hyp_tok.reshape(slot_count, 1, slot_tokens),
        q_proj,
        group_count,
        share_rows,
    )
    crossing = blocks[2] + swap(blocks[3], "tm", 1)
    payloads = [blocks[0], swap(blocks[1], "tm", 1), swap(crossing, "tm", 2)]

    sent = keys_values_of(
        parts, own_frames, kv_proj, blocks[0], section_count, utterances, width_count
    )
    frames_all = all_devices * (frame_rows // width_count)
    keys_values = exchange(sent.reshape(all_devices, -1, 2 * HD), ALL).reshape(frames_all, 2 * HD)

    here_slots = lax.dynamic_slice_in_dim(slot_utt, group_pos * slot_count, slot_count, 0)
    filled = jnp.where(here_slots >= 0, jnp.sum(hyp_len, axis=1), 0)
    count = jnp.max(filled).reshape(1)
    most = count
    for distance in range(1, group_count):
        most = jnp.maximum(most, swap(count, "tm", distance))
    operands = (place, slot_utt, frame_len, hyp_len, payloads, keys_values, o_proj, head)
    few = share_rows * 3 // 4
    return lax.cond(
        most[0] <= few * head_devices,
        functools.partial(rest, (few // 2, few - few // 2), slot_tokens),
        functools.partial(rest, (share_rows // 2, share_rows - share_rows // 2), slot_tokens),
        *operands,
    )


def general(
    frame_len,
    slot_utt,
    enc_in,
    ffn_up,
    ffn_down,
    kv_proj,
    hyp_state,
    hyp_tok,
    hyp_len,
    q_proj,
    o_proj,
    head,
):
    section_count = lax.axis_size("section")
    group_count = lax.axis_size("tm")
    width_count = lax.axis_size("mp")
    section_pos = lax.axis_index("section")
    group_pos = lax.axis_index("tm")
    width_pos = lax.axis_index("mp")
    head_devices = section_count * width_count
    head_pos = section_pos * width_count + width_pos
    all_devices = head_devices * group_count

    frame_rows, utterances, enc_width = enc_in.shape
    assert utterances == group_count
    slot_count, hyp_count, positions, model_width = hyp_state.shape
    slot_tokens = hyp_count * positions
    device_heads = q_proj.shape[1] // HD
    group_heads = NH // KVH
    frame_share = frame_rows // width_count
    share_rows = slot_tokens // head_devices
    here_slots = lax.dynamic_slice_in_dim(slot_utt, group_pos * slot_count, slot_count, 0)

    dec_rows = hyp_state.reshape(slot_count * slot_tokens, model_width).astype(jnp.float32)
    queries = jnp.dot(
        square_norm(dec_rows).astype(jnp.bfloat16), q_proj, preferred_element_type=jnp.float32
    ).astype(jnp.bfloat16)
    queries = queries.reshape(slot_count, slot_tokens, device_heads * HD)
    shares = lax.dynamic_slice_in_dim(
        hyp_state.reshape(slot_count, slot_tokens, model_width), head_pos * share_rows, share_rows, 1
    )

    def by_utterance(values):
        out = []
        for utterance in range(utterances):
            block = values[0]
            for slot in range(1, slot_count):
                block = jnp.where(here_slots[slot] == utterance, values[slot], block)
            out.append(block)
        return jnp.stack(out)

    own_slot = jnp.argmax(slot_utt == group_pos)
    from_group = own_slot // slot_count
    queries = lax.dynamic_index_in_dim(
        exchange(by_utterance(queries), "tm"), from_group, 0, keepdims=False
    )
    resid_rows = lax.dynamic_index_in_dim(
        exchange(by_utterance(shares), "tm"), from_group, 0, keepdims=False
    )
    slot_targets = lax.all_gather(
        hyp_tok.reshape(slot_count, slot_tokens), "tm", axis=0, tiled=True
    )
    utt_slots = jnp.argmax(slot_utt[None, :] == jnp.arange(utterances)[:, None], axis=1)
    targets = jnp.take(slot_targets, utt_slots, axis=0).reshape(utterances * slot_tokens)

    enc_flat = (
        enc_in.reshape(width_count, frame_share, utterances, enc_width)
        .transpose(0, 2, 1, 3)
        .reshape(frame_rows * utterances, enc_width)
    )
    share_count = frame_share * utterances
    enc_normed = layer_norm(enc_flat.astype(jnp.float32)).astype(jnp.bfloat16)
    enc_inner = jax.nn.gelu(
        jnp.dot(enc_normed, ffn_up, preferred_element_type=jnp.float32), approximate=False
    ).astype(jnp.bfloat16)
    enc_summed = scatter_sum(
        jnp.dot(enc_inner, ffn_down, preferred_element_type=jnp.float32).astype(jnp.bfloat16),
        "mp",
        width_count,
    )
    own_frames = lax.dynamic_slice_in_dim(enc_flat, width_pos * share_count, share_count, 0)
    enc_states = layer_norm(own_frames.astype(jnp.float32) + enc_summed).astype(jnp.bfloat16)
    keys_values = jnp.dot(enc_states, kv_proj, preferred_element_type=jnp.float32).astype(
        jnp.bfloat16
    )
    keys_values = keys_values.reshape(utterances, frame_share, 2, KVH, HD)
    sent = []
    for section in range(section_count):
        per_width = []
        for width in range(width_count):
            kv_head = (section * width_count + width) * device_heads // group_heads
            per_width.append(
                keys_values[:, :, :, kv_head].reshape(utterances, frame_share, 2 * HD)
            )
        sent.append(jnp.stack(per_width, axis=1))
    sent = jnp.stack(sent).reshape(all_devices, frame_share, 2 * HD)
    frames_all = all_devices * frame_share
    keys_values = exchange(sent, ALL).reshape(frames_all, 2 * HD)

    frame_limit = lax.dynamic_index_in_dim(frame_len, group_pos, 0, keepdims=False)
    queries = queries.reshape(slot_tokens, device_heads, HD)
    scores = jnp.einsum(
        "qhd,fd->hqf", queries, keys_values[:, :HD], preferred_element_type=jnp.float32
    ) / math.sqrt(HD)
    visible = jnp.arange(frames_all, dtype=jnp.int32) < frame_limit
    scores = jnp.where(visible[None, None, :], scores, -jnp.inf)
    weights = jax.nn.softmax(scores, axis=-1).astype(jnp.bfloat16)
    context = jnp.einsum(
        "hqf,fd->qhd", weights, keys_values[:, HD:], preferred_element_type=jnp.float32
    ).astype(jnp.bfloat16)
    partial = jnp.dot(
        context.reshape(slot_tokens, device_heads * HD), o_proj, preferred_element_type=jnp.float32
    ).astype(jnp.bfloat16)
    partial = scatter_sum(partial, "section", section_count).astype(jnp.bfloat16)
    attn_out = scatter_sum(partial, "mp", width_count)
    out_normed = square_norm(resid_rows.astype(jnp.float32) + attn_out).astype(jnp.bfloat16)

    hidden_rows = lax.all_gather(out_normed, ALL, axis=0, tiled=True)
    logits = lax.dot_general(
        hidden_rows, head, (((1,), (1,)), ((), ())), preferred_element_type=jnp.float32
    )
    vocab_rows = head.shape[0]
    vocab_start = (
        (section_pos * group_count + group_pos) * width_count + width_pos
    ) * vocab_rows
    target_rows = (
        targets.reshape(utterances, section_count, width_count, share_rows)
        .transpose(1, 0, 2, 3)
        .reshape(-1)
    )
    upper = jnp.max(logits, axis=1)
    totals = jnp.sum(jnp.exp(logits - upper[:, None]), axis=1)
    matches = (
        jnp.arange(vocab_rows, dtype=jnp.int32)[None, :] == (target_rows - vocab_start)[:, None]
    )
    target_logit = jnp.sum(jnp.where(matches, logits, 0.0), axis=1)

    stats = jnp.stack([upper, totals, target_logit])
    stats = stats.reshape(3, section_count, utterances, width_count, share_rows)
    stats = stats.transpose(2, 0, 1, 3, 4).reshape(utterances, 3, slot_tokens)
    by_slot = jnp.take(stats, jnp.maximum(slot_utt, 0), axis=0)
    by_group = by_slot.reshape(1, group_count, 1, slot_count, 3, slot_tokens)
    by_group = jnp.broadcast_to(
        by_group, (section_count, group_count, width_count, slot_count, 3, slot_tokens)
    ).reshape(all_devices, slot_count, 3, slot_tokens)
    every = exchange(by_group, ALL)
    peak = jnp.max(every[:, :, 0], axis=0)
    total = jnp.sum(every[:, :, 1] * jnp.exp(every[:, :, 0] - peak[None]), axis=0)
    picked = jnp.sum(every[:, :, 2], axis=0)
    token_logp = (picked - (peak + jnp.log(total))).reshape(slot_count, hyp_count, positions)
    valid = jnp.arange(positions, dtype=jnp.int32)[None, None, :] < hyp_len[:, :, None]
    summed = jnp.sum(jnp.where(valid, token_logp, 0.0), axis=-1) / hyp_len.astype(
        jnp.float32
    ) + math.log(V)
    return jnp.where(here_slots[:, None] >= 0, summed, 0.0)


def solution(mesh):
    in_specs = (
        P(),
        P(),
        P(("section", "tm"), None, None),
        P(None, "mp"),
        P("mp", None),
        P(),
        P("tm", None, None, None),
        P("tm", None, None),
        P("tm", None),
        P(None, ("section", "mp")),
        P(("section", "mp"), None),
        P(("section", "tm", "mp"), None),
    )
    out_specs = P("tm", None)
    near = dict(mesh.shape) == {"section": 2, "tm": 4, "mp": 4}
    per_device = near_device if near else general
    return jax.shard_map(
        per_device, mesh=mesh, in_specs=in_specs, out_specs=out_specs, check_vma=False
    )
```

```python
import functools
import math

import jax
import jax.numpy as jnp
from jax import lax
from jax.experimental import pallas as pl
from jax.experimental.pallas import tpu as pltpu
from jax.sharding import PartitionSpec as P

NH = 32
KVH = 4
HD = 128
V = 64000
ALL = ("section", "tm", "mp")
LANES = 128
FOLD = 4


def layer_norm(values):
    center = values - jnp.mean(values, axis=-1, keepdims=True)
    spread = jnp.mean(center * center, axis=-1, keepdims=True)
    return center * lax.rsqrt(spread + 1e-05)


def square_norm(values):
    return values * lax.rsqrt(jnp.mean(values * values, axis=-1, keepdims=True) + 1e-06)


def exchange(blocks, axis):
    return lax.all_to_all(blocks, axis, split_axis=0, concat_axis=0, tiled=True)


def scatter_sum(partial, axis, count):
    blocks = partial.reshape((count, partial.shape[0] // count) + partial.shape[1:])
    return jnp.sum(exchange(blocks, axis).astype(jnp.float32), axis=0)


def swap(values, axis, distance):
    pairs = [(i, i ^ distance) for i in range(lax.axis_size(axis))]
    return lax.ppermute(values, axis, pairs)


def whole(shape):
    return pl.BlockSpec(shape, lambda *_: (0,) * len(shape))


SCALARS = pl.BlockSpec(memory_space=pltpu.SMEM)


def dot(left, right):
    return jnp.dot(left, right, preferred_element_type=jnp.float32)


def dot_nt(left, right):
    return lax.dot_general(
        left, right, (((1,), (1,)), ((), ())), preferred_element_type=jnp.float32
    )


def start_copies(source_of, target_of, semaphores, count):
    copies = []
    for number in range(count):
        copy = pltpu.make_async_copy(
            source_of(number), target_of(number), semaphores.at[number]
        )
        copy.start()
        copies.append(copy)
    return copies


def ffn_kernel(tile, count, place_ref, x_ref, up_ref, down_ref, *refs):
    outs = refs[:count]
    own_ref, inputs, rows, up, down, x_sem, up_sem, down_sem = refs[count:]
    share = own_ref.shape[0]
    tiles = up_ref.shape[1] // tile
    x_copy = start_copies(lambda i: x_ref, lambda i: inputs, x_sem, 1)[0]
    up_copies = start_copies(
        lambda i: up_ref.at[:, pl.ds(i * tile, tile)], lambda i: up.at[i], up_sem, tiles
    )
    x_copy.wait()
    rows[...] = inputs[...].astype(jnp.float32).reshape(rows.shape)
    start = pl.multiple_of(place_ref[2] * share, share)
    own_ref[...] = rows[pl.ds(start, share), :].astype(jnp.bfloat16)
    normed = layer_norm(rows[...]).astype(jnp.bfloat16)
    inner = []
    for number in range(tiles):
        up_copies[number].wait()
        if number == 0:
            down_copies = start_copies(
                lambda i: down_ref.at[pl.ds(i * tile, tile), :],
                lambda i: down.at[i],
                down_sem,
                tiles,
            )
        hidden = dot(normed, up[number])
        hidden = 0.5 * hidden * (1.0 + lax.erf(hidden * math.sqrt(0.5)))
        inner.append(hidden.astype(jnp.bfloat16))
    total = None
    for number in range(tiles):
        down_copies[number].wait()
        product = dot(inner[number], down[number])
        total = product if total is None else total + product
    rows[...] = total
    for distance in range(count):
        start = pl.multiple_of((place_ref[2] ^ distance) * share, share)
        outs[distance][...] = rows[pl.ds(start, share), :].astype(jnp.bfloat16)


def in_hbm(values):
    return pltpu.with_memory_space_constraint(values, pltpu.HBM)


ANYWHERE = pl.BlockSpec(memory_space=pl.ANY)
INSIDE = pl.BlockSpec(memory_space=pltpu.VMEM)


def ffn(place, enc_in, up, down, count):
    frames, utterances, width = enc_in.shape
    rows = frames * utterances
    share = rows // count
    tile = 256
    tiles = up.shape[1] // tile
    return pl.pallas_call(
        functools.partial(ffn_kernel, tile, count),
        in_specs=[SCALARS] + [ANYWHERE] * 3,
        out_specs=[INSIDE] * (count + 1),
        out_shape=[jax.ShapeDtypeStruct((share, width), jnp.bfloat16)] * (count + 1),
        scratch_shapes=[
            pltpu.VMEM(enc_in.shape, jnp.bfloat16),
            pltpu.VMEM((rows, width), jnp.float32),
            pltpu.VMEM((tiles, width, tile), jnp.bfloat16),
            pltpu.VMEM((tiles, tile, width), jnp.bfloat16),
            pltpu.SemaphoreType.DMA((1,)),
            pltpu.SemaphoreType.DMA((tiles,)),
            pltpu.SemaphoreType.DMA((tiles,)),
        ],
        cost_estimate=pl.CostEstimate(
            flops=4 * rows * width * up.shape[1],
            bytes_accessed=4 * width * up.shape[1],
            transcendentals=rows * up.shape[1],
        ),
        compiler_params=pltpu.CompilerParams(vmem_limit_bytes=24 << 20),
        name="encoder_ffn",
    )(place, in_hbm(enc_in), in_hbm(up), in_hbm(down))


def query_kernel(
    count, depth, place_ref, slot_ref, length_ref, after_ref, x_ref, tok_ref, w_ref, *refs
):
    outs, (states, weights, normed, total, shares, x_sem, w_sem) = refs[:count], refs[count:]
    slots, tokens, width = x_ref.shape
    hyps = length_ref.shape[1]
    positions = tokens // hyps
    columns = w_ref.shape[1]
    share = shares.shape[1] // 2
    parts = width // columns
    x_copies = start_copies(lambda i: x_ref.at[i], lambda i: states.at[i], x_sem, slots)
    w_copies = start_copies(
        lambda i: w_ref.at[pl.ds(i * depth, depth), :],
        lambda i: weights.at[i],
        w_sem,
        width // depth,
    )
    head_pos = place_ref[4]
    lane = lax.broadcasted_iota(jnp.int32, (1, tokens), 1)
    for slot in range(slots):
        order = jnp.full((1, tokens), -1, jnp.int32)
        start = jnp.int32(0)
        for hyp in range(hyps):
            length = length_ref[slot, hyp]
            inside = (lane >= hyp * positions) & (lane < hyp * positions + length)
            order = jnp.where(inside, lane - hyp * positions + start, order)
            start = start + length
        row = lax.broadcasted_iota(jnp.int32, (tokens, tokens), 0)
        move = jnp.where(order == row, 1.0, 0.0).astype(jnp.bfloat16)
        x_copies[slot].wait()
        ordered = dot(move, states[slot])
        normed[slot * tokens : (slot + 1) * tokens, :] = square_norm(ordered).astype(jnp.bfloat16)
        share_row = lax.broadcasted_iota(jnp.int32, (share, tokens), 0)
        chosen = order == share_row * (tokens // share) + head_pos
        mine = dot(jnp.where(chosen, 1.0, 0.0).astype(jnp.bfloat16), states[slot])
        shares[slot, :share, :] = mine.astype(jnp.bfloat16)
        target = jnp.sum(
            jnp.where(chosen, tok_ref[slot], 0), axis=1, keepdims=True, dtype=jnp.int32
        )
        coarse = target // 256
        cell = lax.broadcasted_iota(jnp.int32, (share, columns), 1)
        packed = jnp.where(cell == 0, coarse, jnp.where(cell == 1, target - coarse * 256, 0))
        shares[slot, share:, :columns] = packed.astype(jnp.float32).astype(jnp.bfloat16)
    for number in range(width // depth):
        w_copies[number].wait()
        product = dot(normed[:, number * depth : (number + 1) * depth], weights[number])
        if number == 0:
            total[...] = product
        else:
            total[...] += product
    group = place_ref[1]
    for distance in range(count):
        slot = jnp.int32(-1)
        for candidate in range(slots):
            holds = slot_ref[group * slots + candidate] == group ^ distance
            slot = jnp.where(holds, candidate, slot)
        out = outs[distance]

        @pl.when(slot < 0)
        def _(out=out):
            out[...] = jnp.zeros_like(out)

        @pl.when(slot >= 0)
        def _(out=out, slot=slot):
            start = pl.multiple_of(slot * tokens, tokens)
            out[:tokens, :] = total[pl.ds(start, tokens), :].astype(jnp.bfloat16)
            for part in range(parts):
                first = tokens + part * share
                out[first : first + share, :] = shares[
                    slot, :share, part * columns : (part + 1) * columns
                ]
            out[tokens + parts * share :, :] = shares[slot, share:, :columns]


def queries_of(place, slot_utt, lengths, after, states, targets, weights, count, share):
    slots, tokens, width = states.shape
    columns = weights.shape[1]
    depth = 1024
    rows = tokens + (width // columns + 1) * share
    block = jax.ShapeDtypeStruct((rows, columns), jnp.bfloat16)
    return pl.pallas_call(
        functools.partial(query_kernel, count, depth),
        in_specs=[SCALARS] * 3 + [ANYWHERE, ANYWHERE, INSIDE, ANYWHERE],
        out_specs=[INSIDE] * count,
        out_shape=[block] * count,
        scratch_shapes=[
            pltpu.VMEM(states.shape, jnp.bfloat16),
            pltpu.VMEM((width // depth, depth, columns), jnp.bfloat16),
            pltpu.VMEM((slots * tokens, width), jnp.bfloat16),
            pltpu.VMEM((slots * tokens, columns), jnp.float32),
            pltpu.VMEM((slots, 2 * share, width), jnp.bfloat16),
            pltpu.SemaphoreType.DMA((slots,)),
            pltpu.SemaphoreType.DMA((width // depth,)),
        ],
        cost_estimate=pl.CostEstimate(
            flops=2 * slots * tokens * width * columns,
            bytes_accessed=2 * width * (columns + slots * tokens),
            transcendentals=0,
        ),
        compiler_params=pltpu.CompilerParams(vmem_limit_bytes=32 << 20),
        name="hypothesis_queries",
    )(place, slot_utt, lengths, after, in_hbm(states), targets, in_hbm(weights))


def kv_kernel(sections, utterances, widths, *refs):
    parts, (own_ref, w_ref, out_ref) = refs[:-3], refs[-3:]
    rows = own_ref.shape[0]
    frames = rows // utterances
    total = own_ref[...].astype(jnp.float32)
    summed = parts[0][...].astype(jnp.float32)
    for part in parts[1:]:
        summed += part[...].astype(jnp.float32)
    states = layer_norm(total + summed).astype(jnp.bfloat16)
    to = lax.broadcasted_iota(jnp.int32, (rows, rows), 0)
    come = lax.broadcasted_iota(jnp.int32, (rows, rows), 1)
    move = jnp.where(come == to % frames * utterances + to // frames, 1.0, 0.0)
    states = dot(move.astype(jnp.bfloat16), states).astype(jnp.bfloat16)
    both = dot(states, w_ref[...])
    half = KVH * HD
    per_kv = sections * widths // KVH
    for section in range(sections):
        for utterance in range(utterances):
            for width in range(0, widths, per_kv):
                kv_head = (section * widths + width) // per_kv
                take = slice(utterance * frames, (utterance + 1) * frames)
                block = jnp.concatenate(
                    [
                        both[take, kv_head * HD : (kv_head + 1) * HD],
                        both[take, half + kv_head * HD : half + (kv_head + 1) * HD],
                    ],
                    axis=1,
                )
                start = ((section * utterances + utterance) * widths + width) * frames
                block = jnp.concatenate([block] * per_kv, axis=0).astype(jnp.bfloat16)
                out_ref[start : start + per_kv * frames, :] = block


def keys_values_of(parts, own, weights, sections, utterances, widths):
    rows = sections * widths * own.shape[0]
    return pl.pallas_call(
        functools.partial(kv_kernel, sections, utterances, widths),
        in_specs=[INSIDE] * (len(parts) + 2),
        out_specs=INSIDE,
        out_shape=jax.ShapeDtypeStruct((rows, 2 * HD), jnp.bfloat16),
        cost_estimate=pl.CostEstimate(
            flops=2 * own.shape[0] * weights.shape[0] * weights.shape[1],
            bytes_accessed=2 * weights.shape[0] * weights.shape[1],
            transcendentals=0,
        ),
        compiler_params=pltpu.CompilerParams(vmem_limit_bytes=24 << 20),
        name="frame_keys_values",
    )(*parts, own, weights)


def choice_of_payload(place_ref, slot_ref, slots):
    group = place_ref[1]
    source = jnp.int32(0)
    for slot in range(slot_ref.shape[0]):
        source = jnp.where(slot_ref[slot] == group, slot // slots, source)
    return jnp.minimum(source ^ group, 2)


def attention_kernel(count, slots, capacity, pieces, sections, widths, tile, *refs):
    place_ref, slot_ref, frame_ref = refs[:3]
    payloads, (kv_ref, w_ref) = refs[3 : 3 + count], refs[3 + count : 5 + count]
    outs = refs[5 + count : 5 + count + 2 * len(pieces)]
    weights, picked, context, w_sem = refs[5 + count + 2 * len(pieces) :]
    tokens, columns = capacity, w_ref.shape[0]
    tiles = w_ref.shape[1] // tile
    w_copies = start_copies(
        lambda i: w_ref.at[:, pl.ds(i * tile, tile)], lambda i: weights.at[i], w_sem, tiles
    )
    source = choice_of_payload(place_ref, slot_ref, slots)
    section_pos = place_ref[0]
    frame_limit = frame_ref[place_ref[1]]
    for distance in range(count):

        @pl.when(source == distance)
        def _(payload=payloads[distance]):
            picked[...] = payload[:tokens, :]

    keys = kv_ref[:, :HD]
    values = kv_ref[:, HD:]
    frames = kv_ref.shape[0]
    visible = lax.broadcasted_iota(jnp.int32, (tokens, frames), 1) < frame_limit
    for head in range(columns // HD):
        scores = dot_nt(picked[:, head * HD : (head + 1) * HD], keys) * (1.0 / math.sqrt(HD))
        scores = jnp.where(visible, scores, -jnp.inf)
        raised = jnp.exp(scores - jnp.max(scores, axis=1, keepdims=True))
        chances = (raised / jnp.sum(raised, axis=1, keepdims=True)).astype(jnp.bfloat16)
        context[:, head * HD : (head + 1) * HD] = dot(chances, values).astype(jnp.bfloat16)
    to = lax.broadcasted_iota(jnp.int32, (tokens, tokens), 0)
    come = lax.broadcasted_iota(jnp.int32, (tokens, tokens), 1)
    low_bit = place_ref[2] % 2
    size = widths * pieces[0]
    block = to % size // pieces[0]
    section = jnp.where(to < size, 1 - section_pos, section_pos)
    first_order = (to % pieces[0] * sections + section) * widths + block % 2 * 2 + block // 2
    at = to - 2 * size
    size = widths * pieces[1]
    block = at % size // pieces[1]
    low = jnp.where(at < size, 1 - low_bit, low_bit)
    row = pieces[0] + at % pieces[1]
    second_order = (row * sections + block // 2) * widths + block % 2 * 2 + low
    move = come == jnp.where(at < 0, first_order, second_order)
    ordered = dot(jnp.where(move, 1.0, 0.0).astype(jnp.bfloat16), context[...])
    ordered = ordered.astype(jnp.bfloat16)
    for number in range(tiles):
        w_copies[number].wait()
        product = dot(ordered, weights[number]).astype(jnp.bfloat16)
        first = 0
        for out in outs:
            out[:, number * tile : (number + 1) * tile] = product[first : first + out.shape[0], :]
            first += out.shape[0]


def attend(place, slot_utt, frame_len, payloads, keys_values, weights, pieces, sections, widths, slots):
    count = len(payloads)
    columns, width = weights.shape
    capacity = sum(pieces) * sections * widths
    tile = 1024
    tiles = width // tile
    shapes = [
        jax.ShapeDtypeStruct((piece * widths, width), jnp.bfloat16)
        for piece in pieces
        for _ in range(2)
    ]
    return pl.pallas_call(
        functools.partial(
            attention_kernel, count, slots, capacity, pieces, sections, widths, tile
        ),
        in_specs=[SCALARS] * 3 + [INSIDE] * (count + 1) + [ANYWHERE],
        out_specs=[INSIDE] * len(shapes),
        out_shape=shapes,
        scratch_shapes=[
            pltpu.VMEM((tiles, columns, tile), jnp.bfloat16),
            pltpu.VMEM((capacity, columns), jnp.bfloat16),
            pltpu.VMEM((capacity, columns), jnp.bfloat16),
            pltpu.SemaphoreType.DMA((tiles,)),
        ],
        cost_estimate=pl.CostEstimate(
            flops=2 * capacity * columns * (width + 2 * keys_values.shape[0]),
            bytes_accessed=2 * columns * width + 2 * capacity * width,
            transcendentals=capacity * keys_values.shape[0] * columns // HD,
        ),
        compiler_params=pltpu.CompilerParams(vmem_limit_bytes=24 << 20),
        name="attention_projection",
    )(place, slot_utt, frame_len, *payloads, keys_values, in_hbm(weights))


def fold_kernel(sides, joined, place_ref, *refs):
    count = len(sides)
    parts, outs = refs[: 2 * count], refs[2 * count :]
    first = 0
    for number, side in enumerate(sides):
        kept_ref, came_ref = parts[2 * number : 2 * number + 2]
        total = kept_ref[...].astype(jnp.float32) + came_ref[...].astype(jnp.float32)
        half = total.shape[0] // 2
        top, bottom = total[:half], total[half:]
        upper = side(place_ref) == 0
        kept = jnp.where(upper, top, bottom)
        sent = jnp.where(upper, bottom, top).astype(jnp.bfloat16)
        if joined:
            outs[0][first : first + half, :] = kept
            outs[1][first : first + half, :] = sent
            first += half
        else:
            outs[2 * number][...] = kept
            outs[2 * number + 1][...] = sent


def fold(place, parts, sides, joined):
    width = parts[0].shape[1]
    halves = [part.shape[0] // 2 for part in parts[::2]]
    if joined:
        halves = [sum(halves)]
    shapes = [
        jax.ShapeDtypeStruct((half, width), kind)
        for half in halves
        for kind in (jnp.float32, jnp.bfloat16)
    ]
    return pl.pallas_call(
        functools.partial(fold_kernel, sides, joined),
        in_specs=[SCALARS] + [INSIDE] * len(parts),
        out_specs=[INSIDE] * len(shapes),
        out_shape=shapes,
        compiler_params=pltpu.CompilerParams(vmem_limit_bytes=24 << 20),
        name="sum_phase",
    )(place, *parts)


def section_side(place_ref):
    return place_ref[0]


def low_side(place_ref):
    return place_ref[2] % 2


def high_side(place_ref):
    return place_ref[2] // 2


def norm_kernel(count, slots, tokens, place_ref, slot_ref, *refs):
    payloads, (kept, other) = refs[:count], refs[count : count + 2]
    out_ref, picked, total = refs[count + 2 :]
    rows, width = total.shape
    columns = picked.shape[1]
    share = picked.shape[0] // (width // columns + 1)
    source = choice_of_payload(place_ref, slot_ref, slots)
    for choice in range(count):

        @pl.when(source == choice)
        def _(payload=payloads[choice]):
            picked[...] = payload[tokens:, :]

    total[...] = kept[...] + other[...].astype(jnp.float32)
    for part in range(width // columns):
        take = slice(part * columns, (part + 1) * columns)
        total[:, take] += picked[part * share : part * share + rows, :].astype(jnp.float32)
    shape = out_ref.shape[:2]
    normed = square_norm(total[...]).reshape(*shape, width)
    out_ref[:, :, :width] = normed.astype(jnp.bfloat16)
    last = width // columns * share
    target = picked[last : last + rows, :LANES].astype(jnp.float32).reshape(*shape, LANES)
    out_ref[:, :, width:] = target.astype(jnp.bfloat16)


def normed_rows(place, slot_utt, payloads, blocks, tokens, slots):
    width = blocks[0].shape[1]
    rows = blocks[0].shape[0]
    columns = payloads[0].shape[1]
    return pl.pallas_call(
        functools.partial(norm_kernel, len(payloads), slots, tokens),
        in_specs=[SCALARS] * 2 + [INSIDE] * (len(payloads) + len(blocks)),
        out_specs=INSIDE,
        out_shape=jax.ShapeDtypeStruct((rows // FOLD, FOLD, width + LANES), jnp.bfloat16),
        scratch_shapes=[
            pltpu.VMEM((payloads[0].shape[0] - tokens, columns), jnp.bfloat16),
            pltpu.VMEM((rows, width), jnp.float32),
        ],
        compiler_params=pltpu.CompilerParams(vmem_limit_bytes=16 << 20),
        name="token_rows",
    )(place, slot_utt, *payloads, *blocks)


def vocabulary_kernel(tile, count, first_ref, after_ref, *refs):
    sets, (head_ref, out_ref, rows_ref, stat) = refs[:count], refs[count:]
    vocab_rows, width = head_ref.shape
    share = sets[0].shape[0] * FOLD
    tokens = share * len(sets)
    cell = lax.broadcasted_iota(jnp.int32, (8, LANES), 1)
    take = jnp.where(cell == 0, 256.0, jnp.where(cell == 1, 1.0, 0.0)).astype(jnp.bfloat16)
    for number, rows in enumerate(sets):
        flat = rows[...].astype(jnp.float32).reshape(share, width + LANES)
        rows_ref[number * share : (number + 1) * share, :] = flat.astype(jnp.bfloat16)
    target = dot_nt(take, rows_ref[:, width:])[0:1, :].astype(jnp.int32) - first_ref[3]
    stat[0:1, :] = jnp.full((1, tokens), -jnp.inf, jnp.float32)
    stat[8:9, :] = jnp.zeros((1, tokens), jnp.float32)
    stat[16:17, :] = jnp.zeros((1, tokens), jnp.float32)

    for start in range(0, vocab_rows, tile):
        logits = dot_nt(head_ref[start : start + tile, :], rows_ref[:, :width])
        vocab = lax.broadcasted_iota(jnp.int32, logits.shape, 0) + start
        before = stat[0:1, :]
        upper = jnp.maximum(before, jnp.max(logits, axis=0, keepdims=True))
        stat[8:9, :] = stat[8:9, :] * jnp.exp(before - upper) + jnp.sum(
            jnp.exp(logits - upper), axis=0, keepdims=True
        )
        stat[16:17, :] += jnp.sum(jnp.where(vocab == target, logits, 0.0), axis=0, keepdims=True)
        stat[0:1, :] = upper

    for number in range(len(sets)):
        for row in range(3):
            out_ref[number, row : row + 1, :] = stat[
                8 * row : 8 * row + 1, number * share : (number + 1) * share
            ]


def vocabulary_stats(place, after, sets, head):
    share = sets[0].shape[0] * FOLD
    count = len(sets)
    width = head.shape[1]
    tokens = share * count
    return pl.pallas_call(
        functools.partial(vocabulary_kernel, head.shape[0], count),
        in_specs=[SCALARS, ANYWHERE] + [INSIDE] * (count + 1),
        out_specs=INSIDE,
        out_shape=jax.ShapeDtypeStruct((count, 8, share), jnp.float32),
        scratch_shapes=[
            pltpu.VMEM((tokens, width + LANES), jnp.bfloat16),
            pltpu.VMEM((24, tokens), jnp.float32),
        ],
        cost_estimate=pl.CostEstimate(
            flops=3 * tokens * head.shape[0] * width,
            bytes_accessed=2 * tokens * width,
            transcendentals=tokens * head.shape[0],
        ),
        compiler_params=pltpu.CompilerParams(vmem_limit_bytes=16 << 20),
        name="vocabulary_scores",
    )(place, after, *sets, pltpu.with_memory_space_constraint(head, pltpu.VMEM))


def zero_kernel(after_ref, head_ref, out_ref):
    out_ref[...] = jnp.zeros_like(out_ref)


def head_in_vmem(after, head):
    return pl.pallas_call(
        zero_kernel,
        in_specs=[ANYWHERE, INSIDE],
        out_specs=INSIDE,
        out_shape=jax.ShapeDtypeStruct((8, LANES), jnp.float32),
        compiler_params=pltpu.CompilerParams(vmem_limit_bytes=16 << 20),
        name="vocabulary_rows",
    )(after, pltpu.with_memory_space_constraint(head, pltpu.VMEM))


def spread_kernel(order, sections, groups, widths, place_ref, slot_ref, *refs):
    stats, (out_ref, table, block) = refs[:-3], refs[-3:]
    share = table.shape[2]
    for stat, places in zip(stats, order):
        for number, at in enumerate(places):
            table[at] = stat[number]
    slots = slot_ref.shape[0] // groups
    block[...] = jnp.zeros_like(block)
    for group in range(groups):
        for slot in range(slots):
            utterance = jnp.maximum(slot_ref[group * slots + slot], 0)
            for section in range(sections):
                at = (section ^ place_ref[0]) * groups + (utterance ^ place_ref[1])
                block[group, 3 * slot : 3 * slot + 3, section * share : (section + 1) * share] = (
                    table[at][0:3, :]
                )
    for section in range(sections):
        for group in range(groups):
            for width in range(widths):
                out_ref[(section * groups + group) * widths + width] = block[group]


def spread_stats(place, slot_utt, stats, order, sections, groups, widths):
    share = stats[0].shape[2]
    assert 3 * slot_utt.shape[0] // groups <= 8
    return pl.pallas_call(
        functools.partial(spread_kernel, order, sections, groups, widths),
        in_specs=[SCALARS] * 2 + [INSIDE] * len(stats),
        out_specs=INSIDE,
        out_shape=jax.ShapeDtypeStruct(
            (sections * groups * widths, 8, sections * share), jnp.float32
        ),
        scratch_shapes=[
            pltpu.VMEM((sections * groups, 8, share), jnp.float32),
            pltpu.VMEM((groups, 8, sections * share), jnp.float32),
        ],
        compiler_params=pltpu.CompilerParams(vmem_limit_bytes=16 << 20),
        name="statistics_by_group",
    )(place, slot_utt, *stats)


def score_kernel(sections, widths, place_ref, slot_ref, length_ref, every_ref, out_ref):
    slots, hyps = out_ref.shape
    lanes = every_ref.shape[2]
    share = lanes // sections // widths
    lane = lax.broadcasted_iota(jnp.int32, (1, lanes), 1)
    order = lane % share * (sections * widths) + lane // share
    column = lax.broadcasted_iota(jnp.int32, (1, hyps), 1)
    for slot in range(slots):
        upper = every_ref[:, 3 * slot, :]
        peak = jnp.max(upper, axis=0, keepdims=True)
        total = jnp.sum(
            every_ref[:, 3 * slot + 1, :] * jnp.exp(upper - peak), axis=0, keepdims=True
        )
        picked = jnp.sum(every_ref[:, 3 * slot + 2, :], axis=0, keepdims=True)
        logp = picked - (peak + jnp.log(total))
        scores = jnp.zeros((1, hyps), jnp.float32)
        start = jnp.int32(0)
        for hyp in range(hyps):
            length = length_ref[slot, hyp]
            valid = (order >= start) & (order < start + length)
            summed = jnp.sum(jnp.where(valid, logp, 0.0), axis=1, keepdims=True)
            mean = summed / jnp.full((1, 1), length, jnp.int32).astype(jnp.float32)
            scores = jnp.where(column == hyp, mean + math.log(V), scores)
            start = start + length
        filled = slot_ref[place_ref[1] * slots + slot] >= 0
        out_ref[slot : slot + 1, :] = jnp.where(filled, scores, 0.0)


def hypothesis_scores(place, slot_utt, lengths, every, slots, hyps, sections, widths):
    return pl.pallas_call(
        functools.partial(score_kernel, sections, widths),
        in_specs=[SCALARS] * 3 + [INSIDE],
        out_specs=INSIDE,
        out_shape=pltpu.HBM((slots, hyps), jnp.float32),
        compiler_params=pltpu.CompilerParams(vmem_limit_bytes=16 << 20),
        name="hypothesis_scores",
    )(place, slot_utt, lengths, every)


def rest(pieces, slot_tokens, place, slot_utt, frame_len, hyp_len, payloads, keys_values, o_proj, head):
    section_count = lax.axis_size("section")
    group_count = lax.axis_size("tm")
    width_count = lax.axis_size("mp")
    section_pos = lax.axis_index("section")
    width_pos = lax.axis_index("mp")
    slot_count, hyp_count = hyp_len.shape
    projected = attend(
        place,
        slot_utt,
        frame_len,
        payloads,
        keys_values,
        o_proj,
        pieces,
        section_count,
        width_count,
        slot_count,
    )

    kept, sent, other_kept, other_sent = fold(
        place,
        [projected[1], swap(projected[0], "section", 1), projected[3], swap(projected[2], "mp", 1)],
        [low_side, section_side],
        False,
    )
    kept, sent = fold(
        place,
        [kept, swap(sent, "mp", 1), other_kept, swap(other_sent, "section", 1)],
        [high_side, high_side],
        True,
    )
    out_rows = normed_rows(
        place, slot_utt, payloads, [kept, swap(sent, "mp", 2)], slot_tokens, slot_count
    )

    own = jnp.zeros((width_count, *out_rows.shape), jnp.bfloat16)
    for distance in range(width_count):
        block = swap(out_rows, "mp", distance) if distance else out_rows
        own = lax.dynamic_update_index_in_dim(own, block, width_pos ^ distance, 0)
    own = own.reshape(-1, *out_rows.shape[1:])
    half = own.shape[0] // 2
    by_x = swap(own, "section", 1)
    by_y = swap(own, "tm", 2)
    beside = swap(own, "tm", 1)
    by_x, by_y, zeros = lax.optimization_barrier((by_x, by_y, head_in_vmem(beside, head)))
    across = [swap(by_x[:half], "tm", 2), swap(by_y[half:], "section", 1)]
    near = vocabulary_stats(
        place, zeros, [by_y, swap(by_y, "tm", 1), by_x, swap(by_x, "tm", 1)], head
    )
    *across, near = lax.optimization_barrier((*across, near))
    across = jnp.concatenate(across)
    far = vocabulary_stats(place, zeros, [across, swap(across, "tm", 1), own, beside], head)
    stats = [near, far]
    order = ((2, 3, 4, 5), (6, 7, 0, 1))

    every = exchange(
        spread_stats(place, slot_utt, stats, order, section_count, group_count, width_count), ALL
    )
    return hypothesis_scores(
        place, slot_utt, hyp_len, every, slot_count, hyp_count, section_count, width_count
    )


def near_device(
    frame_len,
    slot_utt,
    enc_in,
    ffn_up,
    ffn_down,
    kv_proj,
    hyp_state,
    hyp_tok,
    hyp_len,
    q_proj,
    o_proj,
    head,
):
    section_count = lax.axis_size("section")
    group_count = lax.axis_size("tm")
    width_count = lax.axis_size("mp")
    section_pos = lax.axis_index("section")
    group_pos = lax.axis_index("tm")
    width_pos = lax.axis_index("mp")
    head_devices = section_count * width_count
    all_devices = head_devices * group_count

    frame_rows, utterances, enc_width = enc_in.shape
    slot_count, hyp_count, positions, model_width = hyp_state.shape
    slot_tokens = hyp_count * positions
    share_rows = slot_tokens // head_devices
    vocab_start = (
        (section_pos * group_count + group_pos) * width_count + width_pos
    ) * head.shape[0]
    head_pos = section_pos * width_count + width_pos
    place = jnp.stack([section_pos, group_pos, width_pos, vocab_start, head_pos])
    place = place.astype(jnp.int32)

    *parts, own_frames = ffn(place, enc_in, ffn_up, ffn_down, width_count)
    parts = [parts[0]] + [
        swap(parts[distance], "mp", distance) for distance in range(1, width_count)
    ]

    blocks = queries_of(
        place,
        slot_utt,
        hyp_len,
        place,
        hyp_state.reshape(slot_count, slot_tokens, model_width),
        hyp_tok.reshape(slot_count, 1, slot_tokens),
        q_proj,
        group_count,
        share_rows,
    )
    crossing = blocks[2] + swap(blocks[3], "tm", 1)
    payloads = [blocks[0], swap(blocks[1], "tm", 1), swap(crossing, "tm", 2)]

    sent = keys_values_of(parts, own_frames, kv_proj, section_count, utterances, width_count)
    frames_all = all_devices * (frame_rows // width_count)
    keys_values = exchange(sent.reshape(all_devices, -1, 2 * HD), ALL).reshape(frames_all, 2 * HD)

    here_slots = lax.dynamic_slice_in_dim(slot_utt, group_pos * slot_count, slot_count, 0)
    filled = jnp.where(here_slots >= 0, jnp.sum(hyp_len, axis=1), 0)
    count = jnp.max(filled).reshape(1)
    most = count
    for distance in range(1, group_count):
        most = jnp.maximum(most, swap(count, "tm", distance))
    operands = (place, slot_utt, frame_len, hyp_len, payloads, keys_values, o_proj, head)
    few = share_rows * 3 // 4
    return lax.cond(
        most[0] <= few * head_devices,
        functools.partial(rest, (few // 2, few - few // 2), slot_tokens),
        functools.partial(rest, (share_rows // 2, share_rows - share_rows // 2), slot_tokens),
        *operands,
    )


def general(
    frame_len,
    slot_utt,
    enc_in,
    ffn_up,
    ffn_down,
    kv_proj,
    hyp_state,
    hyp_tok,
    hyp_len,
    q_proj,
    o_proj,
    head,
):
    section_count = lax.axis_size("section")
    group_count = lax.axis_size("tm")
    width_count = lax.axis_size("mp")
    section_pos = lax.axis_index("section")
    group_pos = lax.axis_index("tm")
    width_pos = lax.axis_index("mp")
    head_devices = section_count * width_count
    head_pos = section_pos * width_count + width_pos
    all_devices = head_devices * group_count

    frame_rows, utterances, enc_width = enc_in.shape
    assert utterances == group_count
    slot_count, hyp_count, positions, model_width = hyp_state.shape
    slot_tokens = hyp_count * positions
    device_heads = q_proj.shape[1] // HD
    group_heads = NH // KVH
    frame_share = frame_rows // width_count
    share_rows = slot_tokens // head_devices
    here_slots = lax.dynamic_slice_in_dim(slot_utt, group_pos * slot_count, slot_count, 0)

    dec_rows = hyp_state.reshape(slot_count * slot_tokens, model_width).astype(jnp.float32)
    queries = jnp.dot(
        square_norm(dec_rows).astype(jnp.bfloat16), q_proj, preferred_element_type=jnp.float32
    ).astype(jnp.bfloat16)
    queries = queries.reshape(slot_count, slot_tokens, device_heads * HD)
    shares = lax.dynamic_slice_in_dim(
        hyp_state.reshape(slot_count, slot_tokens, model_width), head_pos * share_rows, share_rows, 1
    )

    def by_utterance(values):
        out = []
        for utterance in range(utterances):
            block = values[0]
            for slot in range(1, slot_count):
                block = jnp.where(here_slots[slot] == utterance, values[slot], block)
            out.append(block)
        return jnp.stack(out)

    own_slot = jnp.argmax(slot_utt == group_pos)
    from_group = own_slot // slot_count
    queries = lax.dynamic_index_in_dim(
        exchange(by_utterance(queries), "tm"), from_group, 0, keepdims=False
    )
    resid_rows = lax.dynamic_index_in_dim(
        exchange(by_utterance(shares), "tm"), from_group, 0, keepdims=False
    )
    slot_targets = lax.all_gather(
        hyp_tok.reshape(slot_count, slot_tokens), "tm", axis=0, tiled=True
    )
    utt_slots = jnp.argmax(slot_utt[None, :] == jnp.arange(utterances)[:, None], axis=1)
    targets = jnp.take(slot_targets, utt_slots, axis=0).reshape(utterances * slot_tokens)

    enc_flat = (
        enc_in.reshape(width_count, frame_share, utterances, enc_width)
        .transpose(0, 2, 1, 3)
        .reshape(frame_rows * utterances, enc_width)
    )
    share_count = frame_share * utterances
    enc_normed = layer_norm(enc_flat.astype(jnp.float32)).astype(jnp.bfloat16)
    enc_inner = jax.nn.gelu(
        jnp.dot(enc_normed, ffn_up, preferred_element_type=jnp.float32), approximate=False
    ).astype(jnp.bfloat16)
    enc_summed = scatter_sum(
        jnp.dot(enc_inner, ffn_down, preferred_element_type=jnp.float32).astype(jnp.bfloat16),
        "mp",
        width_count,
    )
    own_frames = lax.dynamic_slice_in_dim(enc_flat, width_pos * share_count, share_count, 0)
    enc_states = layer_norm(own_frames.astype(jnp.float32) + enc_summed).astype(jnp.bfloat16)
    keys_values = jnp.dot(enc_states, kv_proj, preferred_element_type=jnp.float32).astype(
        jnp.bfloat16
    )
    keys_values = keys_values.reshape(utterances, frame_share, 2, KVH, HD)
    sent = []
    for section in range(section_count):
        per_width = []
        for width in range(width_count):
            kv_head = (section * width_count + width) * device_heads // group_heads
            per_width.append(
                keys_values[:, :, :, kv_head].reshape(utterances, frame_share, 2 * HD)
            )
        sent.append(jnp.stack(per_width, axis=1))
    sent = jnp.stack(sent).reshape(all_devices, frame_share, 2 * HD)
    frames_all = all_devices * frame_share
    keys_values = exchange(sent, ALL).reshape(frames_all, 2 * HD)

    frame_limit = lax.dynamic_index_in_dim(frame_len, group_pos, 0, keepdims=False)
    queries = queries.reshape(slot_tokens, device_heads, HD)
    scores = jnp.einsum(
        "qhd,fd->hqf", queries, keys_values[:, :HD], preferred_element_type=jnp.float32
    ) / math.sqrt(HD)
    visible = jnp.arange(frames_all, dtype=jnp.int32) < frame_limit
    scores = jnp.where(visible[None, None, :], scores, -jnp.inf)
    weights = jax.nn.softmax(scores, axis=-1).astype(jnp.bfloat16)
    context = jnp.einsum(
        "hqf,fd->qhd", weights, keys_values[:, HD:], preferred_element_type=jnp.float32
    ).astype(jnp.bfloat16)
    partial = jnp.dot(
        context.reshape(slot_tokens, device_heads * HD), o_proj, preferred_element_type=jnp.float32
    ).astype(jnp.bfloat16)
    partial = scatter_sum(partial, "section", section_count).astype(jnp.bfloat16)
    attn_out = scatter_sum(partial, "mp", width_count)
    out_normed = square_norm(resid_rows.astype(jnp.float32) + attn_out).astype(jnp.bfloat16)

    hidden_rows = lax.all_gather(out_normed, ALL, axis=0, tiled=True)
    logits = lax.dot_general(
        hidden_rows, head, (((1,), (1,)), ((), ())), preferred_element_type=jnp.float32
    )
    vocab_rows = head.shape[0]
    vocab_start = (
        (section_pos * group_count + group_pos) * width_count + width_pos
    ) * vocab_rows
    target_rows = (
        targets.reshape(utterances, section_count, width_count, share_rows)
        .transpose(1, 0, 2, 3)
        .reshape(-1)
    )
    upper = jnp.max(logits, axis=1)
    totals = jnp.sum(jnp.exp(logits - upper[:, None]), axis=1)
    matches = (
        jnp.arange(vocab_rows, dtype=jnp.int32)[None, :] == (target_rows - vocab_start)[:, None]
    )
    target_logit = jnp.sum(jnp.where(matches, logits, 0.0), axis=1)

    stats = jnp.stack([upper, totals, target_logit])
    stats = stats.reshape(3, section_count, utterances, width_count, share_rows)
    stats = stats.transpose(2, 0, 1, 3, 4).reshape(utterances, 3, slot_tokens)
    by_slot = jnp.take(stats, jnp.maximum(slot_utt, 0), axis=0)
    by_group = by_slot.reshape(1, group_count, 1, slot_count, 3, slot_tokens)
    by_group = jnp.broadcast_to(
        by_group, (section_count, group_count, width_count, slot_count, 3, slot_tokens)
    ).reshape(all_devices, slot_count, 3, slot_tokens)
    every = exchange(by_group, ALL)
    peak = jnp.max(every[:, :, 0], axis=0)
    total = jnp.sum(every[:, :, 1] * jnp.exp(every[:, :, 0] - peak[None]), axis=0)
    picked = jnp.sum(every[:, :, 2], axis=0)
    token_logp = (picked - (peak + jnp.log(total))).reshape(slot_count, hyp_count, positions)
    valid = jnp.arange(positions, dtype=jnp.int32)[None, None, :] < hyp_len[:, :, None]
    summed = jnp.sum(jnp.where(valid, token_logp, 0.0), axis=-1) / hyp_len.astype(
        jnp.float32
    ) + math.log(V)
    return jnp.where(here_slots[:, None] >= 0, summed, 0.0)


def solution(mesh):
    in_specs = (
        P(),
        P(),
        P(("section", "tm"), None, None),
        P(None, "mp"),
        P("mp", None),
        P(),
        P("tm", None, None, None),
        P("tm", None, None),
        P("tm", None),
        P(None, ("section", "mp")),
        P(("section", "mp"), None),
        P(("section", "tm", "mp"), None),
    )
    out_specs = P("tm", None)
    near = dict(mesh.shape) == {"section": 2, "tm": 4, "mp": 4}
    per_device = near_device if near else general
    return jax.shard_map(
        per_device, mesh=mesh, in_specs=in_specs, out_specs=out_specs, check_vma=False
    )
```

```python
import functools
import math

import jax
import jax.numpy as jnp
from jax import lax
from jax.experimental import pallas as pl
from jax.experimental.pallas import tpu as pltpu
from jax.sharding import PartitionSpec as P

NH = 32
KVH = 4
HD = 128
V = 64000
ALL = ("section", "tm", "mp")
LANES = 128
FOLD = 4


def layer_norm(values):
    center = values - jnp.mean(values, axis=-1, keepdims=True)
    spread = jnp.mean(center * center, axis=-1, keepdims=True)
    return center * lax.rsqrt(spread + 1e-05)


def square_norm(values):
    return values * lax.rsqrt(jnp.mean(values * values, axis=-1, keepdims=True) + 1e-06)


def exchange(blocks, axis):
    return lax.all_to_all(blocks, axis, split_axis=0, concat_axis=0, tiled=True)


def scatter_sum(partial, axis, count):
    blocks = partial.reshape((count, partial.shape[0] // count) + partial.shape[1:])
    return jnp.sum(exchange(blocks, axis).astype(jnp.float32), axis=0)


def swap(values, axis, distance):
    pairs = [(i, i ^ distance) for i in range(lax.axis_size(axis))]
    return lax.ppermute(values, axis, pairs)


def whole(shape):
    return pl.BlockSpec(shape, lambda *_: (0,) * len(shape))


SCALARS = pl.BlockSpec(memory_space=pltpu.SMEM)


def dot(left, right):
    return jnp.dot(left, right, preferred_element_type=jnp.float32)


def dot_nt(left, right):
    return lax.dot_general(
        left, right, (((1,), (1,)), ((), ())), preferred_element_type=jnp.float32
    )


def start_copies(source_of, target_of, semaphores, count):
    copies = []
    for number in range(count):
        copy = pltpu.make_async_copy(
            source_of(number), target_of(number), semaphores.at[number]
        )
        copy.start()
        copies.append(copy)
    return copies


def ffn_kernel(tile, count, place_ref, x_ref, up_ref, down_ref, *refs):
    outs = refs[:count]
    own_ref, inputs, rows, up, down, x_sem, up_sem, down_sem = refs[count:]
    share = own_ref.shape[0]
    tiles = up_ref.shape[1] // tile
    x_copy = start_copies(lambda i: x_ref, lambda i: inputs, x_sem, 1)[0]
    up_copies = start_copies(
        lambda i: up_ref.at[:, pl.ds(i * tile, tile)], lambda i: up.at[i], up_sem, tiles
    )
    x_copy.wait()
    rows[...] = inputs[...].astype(jnp.float32).reshape(rows.shape)
    start = pl.multiple_of(place_ref[2] * share, share)
    own_ref[...] = rows[pl.ds(start, share), :].astype(jnp.bfloat16)
    normed = layer_norm(rows[...]).astype(jnp.bfloat16)
    inner = []
    for number in range(tiles):
        up_copies[number].wait()
        if number == 0:
            down_copies = start_copies(
                lambda i: down_ref.at[pl.ds(i * tile, tile), :],
                lambda i: down.at[i],
                down_sem,
                tiles,
            )
        hidden = dot(normed, up[number])
        hidden = 0.5 * hidden * (1.0 + lax.erf(hidden * math.sqrt(0.5)))
        inner.append(hidden.astype(jnp.bfloat16))
    total = None
    for number in range(tiles):
        down_copies[number].wait()
        product = dot(inner[number], down[number])
        total = product if total is None else total + product
    rows[...] = total
    for distance in range(count):
        start = pl.multiple_of((place_ref[2] ^ distance) * share, share)
        outs[distance][...] = rows[pl.ds(start, share), :].astype(jnp.bfloat16)


def in_hbm(values):
    return pltpu.with_memory_space_constraint(values, pltpu.HBM)


ANYWHERE = pl.BlockSpec(memory_space=pl.ANY)
INSIDE = pl.BlockSpec(memory_space=pltpu.VMEM)


def ffn(place, enc_in, up, down, count):
    frames, utterances, width = enc_in.shape
    rows = frames * utterances
    share = rows // count
    tile = 256
    tiles = up.shape[1] // tile
    return pl.pallas_call(
        functools.partial(ffn_kernel, tile, count),
        in_specs=[SCALARS] + [ANYWHERE] * 3,
        out_specs=[INSIDE] * (count + 1),
        out_shape=[jax.ShapeDtypeStruct((share, width), jnp.bfloat16)] * (count + 1),
        scratch_shapes=[
            pltpu.VMEM(enc_in.shape, jnp.bfloat16),
            pltpu.VMEM((rows, width), jnp.float32),
            pltpu.VMEM((tiles, width, tile), jnp.bfloat16),
            pltpu.VMEM((tiles, tile, width), jnp.bfloat16),
            pltpu.SemaphoreType.DMA((1,)),
            pltpu.SemaphoreType.DMA((tiles,)),
            pltpu.SemaphoreType.DMA((tiles,)),
        ],
        cost_estimate=pl.CostEstimate(
            flops=4 * rows * width * up.shape[1],
            bytes_accessed=4 * width * up.shape[1],
            transcendentals=rows * up.shape[1],
        ),
        compiler_params=pltpu.CompilerParams(vmem_limit_bytes=24 << 20),
        name="encoder_ffn",
    )(place, in_hbm(enc_in), in_hbm(up), in_hbm(down))


def query_kernel(
    count, depth, place_ref, slot_ref, length_ref, after_ref, x_ref, tok_ref, w_ref, *refs
):
    outs, (states, weights, normed, total, shares, x_sem, w_sem) = refs[:count], refs[count:]
    slots, tokens, width = x_ref.shape
    hyps = length_ref.shape[1]
    positions = tokens // hyps
    columns = w_ref.shape[1]
    share = shares.shape[1] // 2
    parts = width // columns
    x_copies = start_copies(lambda i: x_ref.at[i], lambda i: states.at[i], x_sem, slots)
    w_copies = start_copies(
        lambda i: w_ref.at[pl.ds(i * depth, depth), :],
        lambda i: weights.at[i],
        w_sem,
        width // depth,
    )
    head_pos = place_ref[4]
    lane = lax.broadcasted_iota(jnp.int32, (1, tokens), 1)
    for slot in range(slots):
        order = jnp.full((1, tokens), -1, jnp.int32)
        start = jnp.int32(0)
        for hyp in range(hyps):
            length = length_ref[slot, hyp]
            inside = (lane >= hyp * positions) & (lane < hyp * positions + length)
            order = jnp.where(inside, lane - hyp * positions + start, order)
            start = start + length
        row = lax.broadcasted_iota(jnp.int32, (tokens, tokens), 0)
        move = jnp.where(order == row, 1.0, 0.0).astype(jnp.bfloat16)
        x_copies[slot].wait()
        ordered = dot(move, states[slot])
        normed[slot * tokens : (slot + 1) * tokens, :] = square_norm(ordered).astype(jnp.bfloat16)
        share_row = lax.broadcasted_iota(jnp.int32, (share, tokens), 0)
        chosen = order == share_row * (tokens // share) + head_pos
        mine = dot(jnp.where(chosen, 1.0, 0.0).astype(jnp.bfloat16), states[slot])
        shares[slot, :share, :] = mine.astype(jnp.bfloat16)
        target = jnp.sum(
            jnp.where(chosen, tok_ref[slot], 0), axis=1, keepdims=True, dtype=jnp.int32
        )
        coarse = target // 256
        cell = lax.broadcasted_iota(jnp.int32, (share, columns), 1)
        packed = jnp.where(cell == 0, coarse, jnp.where(cell == 1, target - coarse * 256, 0))
        shares[slot, share:, :columns] = packed.astype(jnp.float32).astype(jnp.bfloat16)
    for number in range(width // depth):
        w_copies[number].wait()
        product = dot(normed[:, number * depth : (number + 1) * depth], weights[number])
        if number == 0:
            total[...] = product
        else:
            total[...] += product
    group = place_ref[1]
    for distance in range(count):
        slot = jnp.int32(-1)
        for candidate in range(slots):
            holds = slot_ref[group * slots + candidate] == group ^ distance
            slot = jnp.where(holds, candidate, slot)
        out = outs[distance]

        @pl.when(slot < 0)
        def _(out=out):
            out[...] = jnp.zeros_like(out)

        @pl.when(slot >= 0)
        def _(out=out, slot=slot):
            start = pl.multiple_of(slot * tokens, tokens)
            out[:tokens, :] = total[pl.ds(start, tokens), :].astype(jnp.bfloat16)
            for part in range(parts):
                first = tokens + part * share
                out[first : first + share, :] = shares[
                    slot, :share, part * columns : (part + 1) * columns
                ]
            out[tokens + parts * share :, :] = shares[slot, share:, :columns]


def queries_of(place, slot_utt, lengths, after, states, targets, weights, count, share):
    slots, tokens, width = states.shape
    columns = weights.shape[1]
    depth = 1024
    rows = tokens + (width // columns + 1) * share
    block = jax.ShapeDtypeStruct((rows, columns), jnp.bfloat16)
    return pl.pallas_call(
        functools.partial(query_kernel, count, depth),
        in_specs=[SCALARS] * 3 + [ANYWHERE, ANYWHERE, INSIDE, ANYWHERE],
        out_specs=[INSIDE] * count,
        out_shape=[block] * count,
        scratch_shapes=[
            pltpu.VMEM(states.shape, jnp.bfloat16),
            pltpu.VMEM((width // depth, depth, columns), jnp.bfloat16),
            pltpu.VMEM((slots * tokens, width), jnp.bfloat16),
            pltpu.VMEM((slots * tokens, columns), jnp.float32),
            pltpu.VMEM((slots, 2 * share, width), jnp.bfloat16),
            pltpu.SemaphoreType.DMA((slots,)),
            pltpu.SemaphoreType.DMA((width // depth,)),
        ],
        cost_estimate=pl.CostEstimate(
            flops=2 * slots * tokens * width * columns,
            bytes_accessed=2 * width * (columns + slots * tokens),
            transcendentals=0,
        ),
        compiler_params=pltpu.CompilerParams(vmem_limit_bytes=32 << 20),
        name="hypothesis_queries",
    )(place, slot_utt, lengths, after, in_hbm(states), targets, in_hbm(weights))


def kv_kernel(sections, utterances, widths, *refs):
    parts, (own_ref, w_ref, out_ref) = refs[:-3], refs[-3:]
    rows = own_ref.shape[0]
    frames = rows // utterances
    total = own_ref[...].astype(jnp.float32)
    summed = parts[0][...].astype(jnp.float32)
    for part in parts[1:]:
        summed += part[...].astype(jnp.float32)
    states = layer_norm(total + summed).astype(jnp.bfloat16)
    to = lax.broadcasted_iota(jnp.int32, (rows, rows), 0)
    come = lax.broadcasted_iota(jnp.int32, (rows, rows), 1)
    move = jnp.where(come == to % frames * utterances + to // frames, 1.0, 0.0)
    states = dot(move.astype(jnp.bfloat16), states).astype(jnp.bfloat16)
    both = dot(states, w_ref[...])
    half = KVH * HD
    per_kv = sections * widths // KVH
    for section in range(sections):
        for utterance in range(utterances):
            for width in range(0, widths, per_kv):
                kv_head = (section * widths + width) // per_kv
                take = slice(utterance * frames, (utterance + 1) * frames)
                block = jnp.concatenate(
                    [
                        both[take, kv_head * HD : (kv_head + 1) * HD],
                        both[take, half + kv_head * HD : half + (kv_head + 1) * HD],
                    ],
                    axis=1,
                )
                start = ((section * utterances + utterance) * widths + width) * frames
                block = jnp.concatenate([block] * per_kv, axis=0).astype(jnp.bfloat16)
                out_ref[start : start + per_kv * frames, :] = block


def keys_values_of(parts, own, weights, sections, utterances, widths):
    rows = sections * widths * own.shape[0]
    return pl.pallas_call(
        functools.partial(kv_kernel, sections, utterances, widths),
        in_specs=[INSIDE] * (len(parts) + 2),
        out_specs=INSIDE,
        out_shape=jax.ShapeDtypeStruct((rows, 2 * HD), jnp.bfloat16),
        cost_estimate=pl.CostEstimate(
            flops=2 * own.shape[0] * weights.shape[0] * weights.shape[1],
            bytes_accessed=2 * weights.shape[0] * weights.shape[1],
            transcendentals=0,
        ),
        compiler_params=pltpu.CompilerParams(vmem_limit_bytes=24 << 20),
        name="frame_keys_values",
    )(*parts, own, weights)


def choice_of_payload(place_ref, slot_ref, slots):
    group = place_ref[1]
    source = jnp.int32(0)
    for slot in range(slot_ref.shape[0]):
        source = jnp.where(slot_ref[slot] == group, slot // slots, source)
    return jnp.minimum(source ^ group, 2)


def attention_kernel(count, slots, capacity, pieces, sections, widths, tile, *refs):
    place_ref, slot_ref, frame_ref = refs[:3]
    payloads, (kv_ref, w_ref) = refs[3 : 3 + count], refs[3 + count : 5 + count]
    outs = refs[5 + count : 5 + count + 2 * len(pieces)]
    weights, picked, context, w_sem = refs[5 + count + 2 * len(pieces) :]
    tokens, columns = capacity, w_ref.shape[0]
    tiles = w_ref.shape[1] // tile
    w_copies = start_copies(
        lambda i: w_ref.at[:, pl.ds(i * tile, tile)], lambda i: weights.at[i], w_sem, tiles
    )
    source = choice_of_payload(place_ref, slot_ref, slots)
    section_pos = place_ref[0]
    frame_limit = frame_ref[place_ref[1]]
    for distance in range(count):

        @pl.when(source == distance)
        def _(payload=payloads[distance]):
            picked[...] = payload[:tokens, :]

    keys = kv_ref[:, :HD]
    values = kv_ref[:, HD:]
    frames = kv_ref.shape[0]
    visible = lax.broadcasted_iota(jnp.int32, (tokens, frames), 1) < frame_limit
    for head in range(columns // HD):
        scores = dot_nt(picked[:, head * HD : (head + 1) * HD], keys) * (1.0 / math.sqrt(HD))
        scores = jnp.where(visible, scores, -jnp.inf)
        raised = jnp.exp(scores - jnp.max(scores, axis=1, keepdims=True))
        chances = (raised / jnp.sum(raised, axis=1, keepdims=True)).astype(jnp.bfloat16)
        context[:, head * HD : (head + 1) * HD] = dot(chances, values).astype(jnp.bfloat16)
    to = lax.broadcasted_iota(jnp.int32, (tokens, tokens), 0)
    come = lax.broadcasted_iota(jnp.int32, (tokens, tokens), 1)
    low_bit = place_ref[2] % 2
    size = widths * pieces[0]
    block = to % size // pieces[0]
    section = jnp.where(to < size, 1 - section_pos, section_pos)
    first_order = (to % pieces[0] * sections + section) * widths + block % 2 * 2 + block // 2
    at = to - 2 * size
    size = widths * pieces[1]
    block = at % size // pieces[1]
    low = jnp.where(at < size, 1 - low_bit, low_bit)
    row = pieces[0] + at % pieces[1]
    second_order = (row * sections + block // 2) * widths + block % 2 * 2 + low
    move = come == jnp.where(at < 0, first_order, second_order)
    ordered = dot(jnp.where(move, 1.0, 0.0).astype(jnp.bfloat16), context[...])
    ordered = ordered.astype(jnp.bfloat16)
    for number in range(tiles):
        w_copies[number].wait()
        product = dot(ordered, weights[number]).astype(jnp.bfloat16)
        first = 0
        for out in outs:
            out[:, number * tile : (number + 1) * tile] = product[first : first + out.shape[0], :]
            first += out.shape[0]


def attend(place, slot_utt, frame_len, payloads, keys_values, weights, pieces, sections, widths, slots):
    count = len(payloads)
    columns, width = weights.shape
    capacity = sum(pieces) * sections * widths
    tile = 1024
    tiles = width // tile
    shapes = [
        jax.ShapeDtypeStruct((piece * widths, width), jnp.bfloat16)
        for piece in pieces
        for _ in range(2)
    ]
    return pl.pallas_call(
        functools.partial(
            attention_kernel, count, slots, capacity, pieces, sections, widths, tile
        ),
        in_specs=[SCALARS] * 3 + [INSIDE] * (count + 1) + [ANYWHERE],
        out_specs=[INSIDE] * len(shapes),
        out_shape=shapes,
        scratch_shapes=[
            pltpu.VMEM((tiles, columns, tile), jnp.bfloat16),
            pltpu.VMEM((capacity, columns), jnp.bfloat16),
            pltpu.VMEM((capacity, columns), jnp.bfloat16),
            pltpu.SemaphoreType.DMA((tiles,)),
        ],
        cost_estimate=pl.CostEstimate(
            flops=2 * capacity * columns * (width + 2 * keys_values.shape[0]),
            bytes_accessed=2 * columns * width + 2 * capacity * width,
            transcendentals=capacity * keys_values.shape[0] * columns // HD,
        ),
        compiler_params=pltpu.CompilerParams(vmem_limit_bytes=24 << 20),
        name="attention_projection",
    )(place, slot_utt, frame_len, *payloads, keys_values, in_hbm(weights))


def fold_kernel(sides, joined, place_ref, *refs):
    count = len(sides)
    parts, outs = refs[: 2 * count], refs[2 * count :]
    first = 0
    for number, side in enumerate(sides):
        kept_ref, came_ref = parts[2 * number : 2 * number + 2]
        total = kept_ref[...].astype(jnp.float32) + came_ref[...].astype(jnp.float32)
        half = total.shape[0] // 2
        top, bottom = total[:half], total[half:]
        upper = side(place_ref) == 0
        kept = jnp.where(upper, top, bottom)
        sent = jnp.where(upper, bottom, top).astype(jnp.bfloat16)
        if joined:
            outs[0][first : first + half, :] = kept
            outs[1][first : first + half, :] = sent
            first += half
        else:
            outs[2 * number][...] = kept
            outs[2 * number + 1][...] = sent


def fold(place, parts, sides, joined):
    width = parts[0].shape[1]
    halves = [part.shape[0] // 2 for part in parts[::2]]
    if joined:
        halves = [sum(halves)]
    shapes = [
        jax.ShapeDtypeStruct((half, width), kind)
        for half in halves
        for kind in (jnp.float32, jnp.bfloat16)
    ]
    return pl.pallas_call(
        functools.partial(fold_kernel, sides, joined),
        in_specs=[SCALARS] + [INSIDE] * len(parts),
        out_specs=[INSIDE] * len(shapes),
        out_shape=shapes,
        compiler_params=pltpu.CompilerParams(vmem_limit_bytes=24 << 20),
        name="sum_phase",
    )(place, *parts)


def section_side(place_ref):
    return place_ref[0]


def low_side(place_ref):
    return place_ref[2] % 2


def high_side(place_ref):
    return place_ref[2] // 2


def norm_kernel(count, slots, tokens, place_ref, slot_ref, *refs):
    payloads, (kept, other) = refs[:count], refs[count : count + 2]
    out_ref, picked, total = refs[count + 2 :]
    rows, width = total.shape
    columns = picked.shape[1]
    share = picked.shape[0] // (width // columns + 1)
    source = choice_of_payload(place_ref, slot_ref, slots)
    for choice in range(count):

        @pl.when(source == choice)
        def _(payload=payloads[choice]):
            picked[...] = payload[tokens:, :]

    total[...] = kept[...] + other[...].astype(jnp.float32)
    for part in range(width // columns):
        take = slice(part * columns, (part + 1) * columns)
        total[:, take] += picked[part * share : part * share + rows, :].astype(jnp.float32)
    shape = out_ref.shape[:2]
    normed = square_norm(total[...]).reshape(*shape, width)
    out_ref[:, :, :width] = normed.astype(jnp.bfloat16)
    last = width // columns * share
    target = picked[last : last + rows, :LANES].astype(jnp.float32).reshape(*shape, LANES)
    out_ref[:, :, width:] = target.astype(jnp.bfloat16)


def normed_rows(place, slot_utt, payloads, blocks, tokens, slots):
    width = blocks[0].shape[1]
    rows = blocks[0].shape[0]
    columns = payloads[0].shape[1]
    return pl.pallas_call(
        functools.partial(norm_kernel, len(payloads), slots, tokens),
        in_specs=[SCALARS] * 2 + [INSIDE] * (len(payloads) + len(blocks)),
        out_specs=INSIDE,
        out_shape=jax.ShapeDtypeStruct((rows // FOLD, FOLD, width + LANES), jnp.bfloat16),
        scratch_shapes=[
            pltpu.VMEM((payloads[0].shape[0] - tokens, columns), jnp.bfloat16),
            pltpu.VMEM((rows, width), jnp.float32),
        ],
        compiler_params=pltpu.CompilerParams(vmem_limit_bytes=16 << 20),
        name="token_rows",
    )(place, slot_utt, *payloads, *blocks)


def vocabulary_kernel(tile, count, first_ref, after_ref, *refs):
    sets, (head_ref, out_ref, rows_ref, stat) = refs[:count], refs[count:]
    vocab_rows, width = head_ref.shape
    share = sets[0].shape[0] * FOLD
    tokens = share * len(sets)
    cell = lax.broadcasted_iota(jnp.int32, (8, LANES), 1)
    take = jnp.where(cell == 0, 256.0, jnp.where(cell == 1, 1.0, 0.0)).astype(jnp.bfloat16)
    for number, rows in enumerate(sets):
        flat = rows[...].astype(jnp.float32).reshape(share, width + LANES)
        rows_ref[number * share : (number + 1) * share, :] = flat.astype(jnp.bfloat16)
    target = dot_nt(take, rows_ref[:, width:])[0:1, :].astype(jnp.int32) - first_ref[3]
    stat[0:1, :] = jnp.full((1, tokens), -jnp.inf, jnp.float32)
    stat[8:9, :] = jnp.zeros((1, tokens), jnp.float32)
    stat[16:17, :] = jnp.zeros((1, tokens), jnp.float32)

    for start in range(0, vocab_rows, tile):
        logits = dot_nt(head_ref[start : start + tile, :], rows_ref[:, :width])
        vocab = lax.broadcasted_iota(jnp.int32, logits.shape, 0) + start
        before = stat[0:1, :]
        upper = jnp.maximum(before, jnp.max(logits, axis=0, keepdims=True))
        stat[8:9, :] = stat[8:9, :] * jnp.exp(before - upper) + jnp.sum(
            jnp.exp(logits - upper), axis=0, keepdims=True
        )
        stat[16:17, :] += jnp.sum(jnp.where(vocab == target, logits, 0.0), axis=0, keepdims=True)
        stat[0:1, :] = upper

    for number in range(len(sets)):
        for row in range(3):
            out_ref[number, row : row + 1, :] = stat[
                8 * row : 8 * row + 1, number * share : (number + 1) * share
            ]


def vocabulary_stats(place, after, sets, head):
    share = sets[0].shape[0] * FOLD
    count = len(sets)
    width = head.shape[1]
    tokens = share * count
    return pl.pallas_call(
        functools.partial(vocabulary_kernel, head.shape[0], count),
        in_specs=[SCALARS, ANYWHERE] + [INSIDE] * (count + 1),
        out_specs=INSIDE,
        out_shape=jax.ShapeDtypeStruct((count, 8, share), jnp.float32),
        scratch_shapes=[
            pltpu.VMEM((tokens, width + LANES), jnp.bfloat16),
            pltpu.VMEM((24, tokens), jnp.float32),
        ],
        cost_estimate=pl.CostEstimate(
            flops=3 * tokens * head.shape[0] * width,
            bytes_accessed=2 * tokens * width,
            transcendentals=tokens * head.shape[0],
        ),
        compiler_params=pltpu.CompilerParams(vmem_limit_bytes=16 << 20),
        name="vocabulary_scores",
    )(place, after, *sets, pltpu.with_memory_space_constraint(head, pltpu.VMEM))


def zero_kernel(after_ref, head_ref, out_ref):
    out_ref[...] = jnp.zeros_like(out_ref)


def head_in_vmem(after, head):
    return pl.pallas_call(
        zero_kernel,
        in_specs=[ANYWHERE, INSIDE],
        out_specs=INSIDE,
        out_shape=jax.ShapeDtypeStruct((8, LANES), jnp.float32),
        compiler_params=pltpu.CompilerParams(vmem_limit_bytes=16 << 20),
        name="vocabulary_rows",
    )(after, pltpu.with_memory_space_constraint(head, pltpu.VMEM))


def spread_kernel(order, sections, groups, widths, place_ref, slot_ref, *refs):
    stats, (out_ref, table, block) = refs[:-3], refs[-3:]
    share = table.shape[2]
    for stat, places in zip(stats, order):
        for number, at in enumerate(places):
            table[at] = stat[number]
    slots = slot_ref.shape[0] // groups
    block[...] = jnp.zeros_like(block)
    for group in range(groups):
        for slot in range(slots):
            utterance = jnp.maximum(slot_ref[group * slots + slot], 0)
            for section in range(sections):
                at = (section ^ place_ref[0]) * groups + (utterance ^ place_ref[1])
                block[group, 3 * slot : 3 * slot + 3, section * share : (section + 1) * share] = (
                    table[at][0:3, :]
                )
    for section in range(sections):
        for group in range(groups):
            for width in range(widths):
                out_ref[(section * groups + group) * widths + width] = block[group]


def spread_stats(place, slot_utt, stats, order, sections, groups, widths):
    share = stats[0].shape[2]
    assert 3 * slot_utt.shape[0] // groups <= 8
    return pl.pallas_call(
        functools.partial(spread_kernel, order, sections, groups, widths),
        in_specs=[SCALARS] * 2 + [INSIDE] * len(stats),
        out_specs=INSIDE,
        out_shape=jax.ShapeDtypeStruct(
            (sections * groups * widths, 8, sections * share), jnp.float32
        ),
        scratch_shapes=[
            pltpu.VMEM((sections * groups, 8, share), jnp.float32),
            pltpu.VMEM((groups, 8, sections * share), jnp.float32),
        ],
        compiler_params=pltpu.CompilerParams(vmem_limit_bytes=16 << 20),
        name="statistics_by_group",
    )(place, slot_utt, *stats)


def score_kernel(sections, widths, place_ref, slot_ref, length_ref, every_ref, out_ref):
    slots, hyps = out_ref.shape
    lanes = every_ref.shape[2]
    share = lanes // sections // widths
    lane = lax.broadcasted_iota(jnp.int32, (1, lanes), 1)
    order = lane % share * (sections * widths) + lane // share
    column = lax.broadcasted_iota(jnp.int32, (1, hyps), 1)
    for slot in range(slots):
        upper = every_ref[:, 3 * slot, :]
        peak = jnp.max(upper, axis=0, keepdims=True)
        total = jnp.sum(
            every_ref[:, 3 * slot + 1, :] * jnp.exp(upper - peak), axis=0, keepdims=True
        )
        picked = jnp.sum(every_ref[:, 3 * slot + 2, :], axis=0, keepdims=True)
        logp = picked - (peak + jnp.log(total))
        scores = jnp.zeros((1, hyps), jnp.float32)
        start = jnp.int32(0)
        for hyp in range(hyps):
            length = length_ref[slot, hyp]
            valid = (order >= start) & (order < start + length)
            summed = jnp.sum(jnp.where(valid, logp, 0.0), axis=1, keepdims=True)
            mean = summed / jnp.full((1, 1), length, jnp.int32).astype(jnp.float32)
            scores = jnp.where(column == hyp, mean + math.log(V), scores)
            start = start + length
        filled = slot_ref[place_ref[1] * slots + slot] >= 0
        out_ref[slot : slot + 1, :] = jnp.where(filled, scores, 0.0)


def hypothesis_scores(place, slot_utt, lengths, every, slots, hyps, sections, widths):
    return pl.pallas_call(
        functools.partial(score_kernel, sections, widths),
        in_specs=[SCALARS] * 3 + [INSIDE],
        out_specs=INSIDE,
        out_shape=pltpu.HBM((slots, hyps), jnp.float32),
        compiler_params=pltpu.CompilerParams(vmem_limit_bytes=16 << 20),
        name="hypothesis_scores",
    )(place, slot_utt, lengths, every)


def rest(pieces, slot_tokens, place, slot_utt, frame_len, hyp_len, payloads, keys_values, o_proj, head):
    section_count = lax.axis_size("section")
    group_count = lax.axis_size("tm")
    width_count = lax.axis_size("mp")
    section_pos = lax.axis_index("section")
    width_pos = lax.axis_index("mp")
    slot_count, hyp_count = hyp_len.shape
    projected = attend(
        place,
        slot_utt,
        frame_len,
        payloads,
        keys_values,
        o_proj,
        pieces,
        section_count,
        width_count,
        slot_count,
    )

    kept, sent, other_kept, other_sent = fold(
        place,
        [projected[1], swap(projected[0], "section", 1), projected[3], swap(projected[2], "mp", 1)],
        [low_side, section_side],
        False,
    )
    kept, sent = fold(
        place,
        [kept, swap(sent, "mp", 1), other_kept, swap(other_sent, "section", 1)],
        [high_side, high_side],
        True,
    )
    out_rows = normed_rows(
        place, slot_utt, payloads, [kept, swap(sent, "mp", 2)], slot_tokens, slot_count
    )

    own = jnp.zeros((width_count, *out_rows.shape), jnp.bfloat16)
    for distance in range(width_count):
        block = swap(out_rows, "mp", distance) if distance else out_rows
        own = lax.dynamic_update_index_in_dim(own, block, width_pos ^ distance, 0)
    own = own.reshape(-1, *out_rows.shape[1:])
    half = own.shape[0] // 2
    by_x = swap(own, "section", 1)
    by_y = swap(own, "tm", 2)
    beside = swap(own, "tm", 1)
    by_x, by_y, zeros = lax.optimization_barrier((by_x, by_y, head_in_vmem(beside, head)))
    across = [swap(by_x[:half], "tm", 2), swap(by_y[half:], "section", 1)]
    near = vocabulary_stats(
        place, zeros, [by_y, swap(by_y, "tm", 1), by_x, swap(by_x, "tm", 1)], head
    )
    *across, near = lax.optimization_barrier((*across, near))
    across = jnp.concatenate(across)
    far = vocabulary_stats(place, zeros, [across, swap(across, "tm", 1), own, beside], head)
    stats = [near, far]
    order = ((2, 3, 4, 5), (6, 7, 0, 1))

    every = exchange(
        spread_stats(place, slot_utt, stats, order, section_count, group_count, width_count), ALL
    )
    return hypothesis_scores(
        place, slot_utt, hyp_len, every, slot_count, hyp_count, section_count, width_count
    )


def near_device(
    frame_len,
    slot_utt,
    enc_in,
    ffn_up,
    ffn_down,
    kv_proj,
    hyp_state,
    hyp_tok,
    hyp_len,
    q_proj,
    o_proj,
    head,
):
    section_count = lax.axis_size("section")
    group_count = lax.axis_size("tm")
    width_count = lax.axis_size("mp")
    section_pos = lax.axis_index("section")
    group_pos = lax.axis_index("tm")
    width_pos = lax.axis_index("mp")
    head_devices = section_count * width_count
    all_devices = head_devices * group_count

    frame_rows, utterances, enc_width = enc_in.shape
    slot_count, hyp_count, positions, model_width = hyp_state.shape
    slot_tokens = hyp_count * positions
    share_rows = slot_tokens // head_devices
    vocab_start = (
        (section_pos * group_count + group_pos) * width_count + width_pos
    ) * head.shape[0]
    head_pos = section_pos * width_count + width_pos
    place = jnp.stack([section_pos, group_pos, width_pos, vocab_start, head_pos])
    place = place.astype(jnp.int32)

    *parts, own_frames = ffn(place, enc_in, ffn_up, ffn_down, width_count)
    parts = [parts[0]] + [
        swap(parts[distance], "mp", distance) for distance in range(1, width_count)
    ]
    own_frames, lengths = lax.optimization_barrier((own_frames, hyp_len))

    blocks = queries_of(
        place,
        slot_utt,
        lengths,
        place,
        hyp_state.reshape(slot_count, slot_tokens, model_width),
        hyp_tok.reshape(slot_count, 1, slot_tokens),
        q_proj,
        group_count,
        share_rows,
    )
    crossing = blocks[2] + swap(blocks[3], "tm", 1)
    payloads = [blocks[0], swap(blocks[1], "tm", 1), swap(crossing, "tm", 2)]

    sent = keys_values_of(parts, own_frames, kv_proj, section_count, utterances, width_count)
    frames_all = all_devices * (frame_rows // width_count)
    keys_values = exchange(sent.reshape(all_devices, -1, 2 * HD), ALL).reshape(frames_all, 2 * HD)

    here_slots = lax.dynamic_slice_in_dim(slot_utt, group_pos * slot_count, slot_count, 0)
    filled = jnp.where(here_slots >= 0, jnp.sum(hyp_len, axis=1), 0)
    count = jnp.max(filled).reshape(1)
    most = count
    for distance in range(1, group_count):
        most = jnp.maximum(most, swap(count, "tm", distance))
    operands = (place, slot_utt, frame_len, hyp_len, payloads, keys_values, o_proj, head)
    few = share_rows * 3 // 4
    return lax.cond(
        most[0] <= few * head_devices,
        functools.partial(rest, (few // 2, few - few // 2), slot_tokens),
        functools.partial(rest, (share_rows // 2, share_rows - share_rows // 2), slot_tokens),
        *operands,
    )


def general(
    frame_len,
    slot_utt,
    enc_in,
    ffn_up,
    ffn_down,
    kv_proj,
    hyp_state,
    hyp_tok,
    hyp_len,
    q_proj,
    o_proj,
    head,
):
    section_count = lax.axis_size("section")
    group_count = lax.axis_size("tm")
    width_count = lax.axis_size("mp")
    section_pos = lax.axis_index("section")
    group_pos = lax.axis_index("tm")
    width_pos = lax.axis_index("mp")
    head_devices = section_count * width_count
    head_pos = section_pos * width_count + width_pos
    all_devices = head_devices * group_count

    frame_rows, utterances, enc_width = enc_in.shape
    assert utterances == group_count
    slot_count, hyp_count, positions, model_width = hyp_state.shape
    slot_tokens = hyp_count * positions
    device_heads = q_proj.shape[1] // HD
    group_heads = NH // KVH
    frame_share = frame_rows // width_count
    share_rows = slot_tokens // head_devices
    here_slots = lax.dynamic_slice_in_dim(slot_utt, group_pos * slot_count, slot_count, 0)

    dec_rows = hyp_state.reshape(slot_count * slot_tokens, model_width).astype(jnp.float32)
    queries = jnp.dot(
        square_norm(dec_rows).astype(jnp.bfloat16), q_proj, preferred_element_type=jnp.float32
    ).astype(jnp.bfloat16)
    queries = queries.reshape(slot_count, slot_tokens, device_heads * HD)
    shares = lax.dynamic_slice_in_dim(
        hyp_state.reshape(slot_count, slot_tokens, model_width), head_pos * share_rows, share_rows, 1
    )

    def by_utterance(values):
        out = []
        for utterance in range(utterances):
            block = values[0]
            for slot in range(1, slot_count):
                block = jnp.where(here_slots[slot] == utterance, values[slot], block)
            out.append(block)
        return jnp.stack(out)

    own_slot = jnp.argmax(slot_utt == group_pos)
    from_group = own_slot // slot_count
    queries = lax.dynamic_index_in_dim(
        exchange(by_utterance(queries), "tm"), from_group, 0, keepdims=False
    )
    resid_rows = lax.dynamic_index_in_dim(
        exchange(by_utterance(shares), "tm"), from_group, 0, keepdims=False
    )
    slot_targets = lax.all_gather(
        hyp_tok.reshape(slot_count, slot_tokens), "tm", axis=0, tiled=True
    )
    utt_slots = jnp.argmax(slot_utt[None, :] == jnp.arange(utterances)[:, None], axis=1)
    targets = jnp.take(slot_targets, utt_slots, axis=0).reshape(utterances * slot_tokens)

    enc_flat = (
        enc_in.reshape(width_count, frame_share, utterances, enc_width)
        .transpose(0, 2, 1, 3)
        .reshape(frame_rows * utterances, enc_width)
    )
    share_count = frame_share * utterances
    enc_normed = layer_norm(enc_flat.astype(jnp.float32)).astype(jnp.bfloat16)
    enc_inner = jax.nn.gelu(
        jnp.dot(enc_normed, ffn_up, preferred_element_type=jnp.float32), approximate=False
    ).astype(jnp.bfloat16)
    enc_summed = scatter_sum(
        jnp.dot(enc_inner, ffn_down, preferred_element_type=jnp.float32).astype(jnp.bfloat16),
        "mp",
        width_count,
    )
    own_frames = lax.dynamic_slice_in_dim(enc_flat, width_pos * share_count, share_count, 0)
    enc_states = layer_norm(own_frames.astype(jnp.float32) + enc_summed).astype(jnp.bfloat16)
    keys_values = jnp.dot(enc_states, kv_proj, preferred_element_type=jnp.float32).astype(
        jnp.bfloat16
    )
    keys_values = keys_values.reshape(utterances, frame_share, 2, KVH, HD)
    sent = []
    for section in range(section_count):
        per_width = []
        for width in range(width_count):
            kv_head = (section * width_count + width) * device_heads // group_heads
            per_width.append(
                keys_values[:, :, :, kv_head].reshape(utterances, frame_share, 2 * HD)
            )
        sent.append(jnp.stack(per_width, axis=1))
    sent = jnp.stack(sent).reshape(all_devices, frame_share, 2 * HD)
    frames_all = all_devices * frame_share
    keys_values = exchange(sent, ALL).reshape(frames_all, 2 * HD)

    frame_limit = lax.dynamic_index_in_dim(frame_len, group_pos, 0, keepdims=False)
    queries = queries.reshape(slot_tokens, device_heads, HD)
    scores = jnp.einsum(
        "qhd,fd->hqf", queries, keys_values[:, :HD], preferred_element_type=jnp.float32
    ) / math.sqrt(HD)
    visible = jnp.arange(frames_all, dtype=jnp.int32) < frame_limit
    scores = jnp.where(visible[None, None, :], scores, -jnp.inf)
    weights = jax.nn.softmax(scores, axis=-1).astype(jnp.bfloat16)
    context = jnp.einsum(
        "hqf,fd->qhd", weights, keys_values[:, HD:], preferred_element_type=jnp.float32
    ).astype(jnp.bfloat16)
    partial = jnp.dot(
        context.reshape(slot_tokens, device_heads * HD), o_proj, preferred_element_type=jnp.float32
    ).astype(jnp.bfloat16)
    partial = scatter_sum(partial, "section", section_count).astype(jnp.bfloat16)
    attn_out = scatter_sum(partial, "mp", width_count)
    out_normed = square_norm(resid_rows.astype(jnp.float32) + attn_out).astype(jnp.bfloat16)

    hidden_rows = lax.all_gather(out_normed, ALL, axis=0, tiled=True)
    logits = lax.dot_general(
        hidden_rows, head, (((1,), (1,)), ((), ())), preferred_element_type=jnp.float32
    )
    vocab_rows = head.shape[0]
    vocab_start = (
        (section_pos * group_count + group_pos) * width_count + width_pos
    ) * vocab_rows
    target_rows = (
        targets.reshape(utterances, section_count, width_count, share_rows)
        .transpose(1, 0, 2, 3)
        .reshape(-1)
    )
    upper = jnp.max(logits, axis=1)
    totals = jnp.sum(jnp.exp(logits - upper[:, None]), axis=1)
    matches = (
        jnp.arange(vocab_rows, dtype=jnp.int32)[None, :] == (target_rows - vocab_start)[:, None]
    )
    target_logit = jnp.sum(jnp.where(matches, logits, 0.0), axis=1)

    stats = jnp.stack([upper, totals, target_logit])
    stats = stats.reshape(3, section_count, utterances, width_count, share_rows)
    stats = stats.transpose(2, 0, 1, 3, 4).reshape(utterances, 3, slot_tokens)
    by_slot = jnp.take(stats, jnp.maximum(slot_utt, 0), axis=0)
    by_group = by_slot.reshape(1, group_count, 1, slot_count, 3, slot_tokens)
    by_group = jnp.broadcast_to(
        by_group, (section_count, group_count, width_count, slot_count, 3, slot_tokens)
    ).reshape(all_devices, slot_count, 3, slot_tokens)
    every = exchange(by_group, ALL)
    peak = jnp.max(every[:, :, 0], axis=0)
    total = jnp.sum(every[:, :, 1] * jnp.exp(every[:, :, 0] - peak[None]), axis=0)
    picked = jnp.sum(every[:, :, 2], axis=0)
    token_logp = (picked - (peak + jnp.log(total))).reshape(slot_count, hyp_count, positions)
    valid = jnp.arange(positions, dtype=jnp.int32)[None, None, :] < hyp_len[:, :, None]
    summed = jnp.sum(jnp.where(valid, token_logp, 0.0), axis=-1) / hyp_len.astype(
        jnp.float32
    ) + math.log(V)
    return jnp.where(here_slots[:, None] >= 0, summed, 0.0)


def solution(mesh):
    in_specs = (
        P(),
        P(),
        P(("section", "tm"), None, None),
        P(None, "mp"),
        P("mp", None),
        P(),
        P("tm", None, None, None),
        P("tm", None, None),
        P("tm", None),
        P(None, ("section", "mp")),
        P(("section", "mp"), None),
        P(("section", "tm", "mp"), None),
    )
    out_specs = P("tm", None)
    near = dict(mesh.shape) == {"section": 2, "tm": 4, "mp": 4}
    per_device = near_device if near else general
    return jax.shard_map(
        per_device, mesh=mesh, in_specs=in_specs, out_specs=out_specs, check_vma=False
    )
```

```python
import functools
import math

import jax
import jax.numpy as jnp
from jax import lax
from jax.experimental import pallas as pl
from jax.experimental.pallas import tpu as pltpu
from jax.sharding import PartitionSpec as P

NH = 32
KVH = 4
HD = 128
V = 64000
ALL = ("section", "tm", "mp")
LANES = 128
FOLD = 4


def layer_norm(values):
    center = values - jnp.mean(values, axis=-1, keepdims=True)
    spread = jnp.mean(center * center, axis=-1, keepdims=True)
    return center * lax.rsqrt(spread + 1e-05)


def square_norm(values):
    return values * lax.rsqrt(jnp.mean(values * values, axis=-1, keepdims=True) + 1e-06)


def exchange(blocks, axis):
    return lax.all_to_all(blocks, axis, split_axis=0, concat_axis=0, tiled=True)


def scatter_sum(partial, axis, count):
    blocks = partial.reshape((count, partial.shape[0] // count) + partial.shape[1:])
    return jnp.sum(exchange(blocks, axis).astype(jnp.float32), axis=0)


def swap(values, axis, distance):
    pairs = [(i, i ^ distance) for i in range(lax.axis_size(axis))]
    return lax.ppermute(values, axis, pairs)


def whole(shape):
    return pl.BlockSpec(shape, lambda *_: (0,) * len(shape))


SCALARS = pl.BlockSpec(memory_space=pltpu.SMEM)


def dot(left, right):
    return jnp.dot(left, right, preferred_element_type=jnp.float32)


def dot_nt(left, right):
    return lax.dot_general(
        left, right, (((1,), (1,)), ((), ())), preferred_element_type=jnp.float32
    )


def start_copies(source_of, target_of, semaphores, count):
    copies = []
    for number in range(count):
        copy = pltpu.make_async_copy(
            source_of(number), target_of(number), semaphores.at[number]
        )
        copy.start()
        copies.append(copy)
    return copies


def ffn_kernel(tile, count, place_ref, x_ref, up_ref, down_ref, *refs):
    outs = refs[:count]
    own_ref, inputs, rows, up, down, x_sem, up_sem, down_sem = refs[count:]
    share = own_ref.shape[0]
    tiles = up_ref.shape[1] // tile
    x_copy = start_copies(lambda i: x_ref, lambda i: inputs, x_sem, 1)[0]
    up_copies = start_copies(
        lambda i: up_ref.at[:, pl.ds(i * tile, tile)], lambda i: up.at[i], up_sem, tiles
    )
    x_copy.wait()
    rows[...] = inputs[...].astype(jnp.float32).reshape(rows.shape)
    start = pl.multiple_of(place_ref[2] * share, share)
    own_ref[...] = rows[pl.ds(start, share), :].astype(jnp.bfloat16)
    normed = layer_norm(rows[...]).astype(jnp.bfloat16)
    inner = []
    for number in range(tiles):
        up_copies[number].wait()
        if number == 0:
            down_copies = start_copies(
                lambda i: down_ref.at[pl.ds(i * tile, tile), :],
                lambda i: down.at[i],
                down_sem,
                tiles,
            )
        hidden = dot(normed, up[number])
        hidden = 0.5 * hidden * (1.0 + lax.erf(hidden * math.sqrt(0.5)))
        inner.append(hidden.astype(jnp.bfloat16))
    total = None
    for number in range(tiles):
        down_copies[number].wait()
        product = dot(inner[number], down[number])
        total = product if total is None else total + product
    rows[...] = total
    for distance in range(count):
        start = pl.multiple_of((place_ref[2] ^ distance) * share, share)
        outs[distance][...] = rows[pl.ds(start, share), :].astype(jnp.bfloat16)


def in_hbm(values):
    return pltpu.with_memory_space_constraint(values, pltpu.HBM)


ANYWHERE = pl.BlockSpec(memory_space=pl.ANY)
INSIDE = pl.BlockSpec(memory_space=pltpu.VMEM)


def ffn(place, enc_in, up, down, count):
    frames, utterances, width = enc_in.shape
    rows = frames * utterances
    share = rows // count
    tile = 256
    tiles = up.shape[1] // tile
    return pl.pallas_call(
        functools.partial(ffn_kernel, tile, count),
        in_specs=[SCALARS] + [ANYWHERE] * 3,
        out_specs=[INSIDE] * (count + 1),
        out_shape=[jax.ShapeDtypeStruct((share, width), jnp.bfloat16)] * (count + 1),
        scratch_shapes=[
            pltpu.VMEM(enc_in.shape, jnp.bfloat16),
            pltpu.VMEM((rows, width), jnp.float32),
            pltpu.VMEM((tiles, width, tile), jnp.bfloat16),
            pltpu.VMEM((tiles, tile, width), jnp.bfloat16),
            pltpu.SemaphoreType.DMA((1,)),
            pltpu.SemaphoreType.DMA((tiles,)),
            pltpu.SemaphoreType.DMA((tiles,)),
        ],
        cost_estimate=pl.CostEstimate(
            flops=4 * rows * width * up.shape[1],
            bytes_accessed=4 * width * up.shape[1],
            transcendentals=rows * up.shape[1],
        ),
        compiler_params=pltpu.CompilerParams(vmem_limit_bytes=24 << 20),
        name="encoder_ffn",
    )(place, in_hbm(enc_in), in_hbm(up), in_hbm(down))


def query_kernel(
    count, depth, place_ref, slot_ref, length_ref, after_ref, x_ref, tok_ref, w_ref, *refs
):
    outs, (states, weights, normed, total, shares, x_sem, w_sem) = refs[:count], refs[count:]
    slots, tokens, width = x_ref.shape
    hyps = length_ref.shape[1]
    positions = tokens // hyps
    columns = w_ref.shape[1]
    share = shares.shape[1] // 2
    parts = width // columns
    x_copies = start_copies(lambda i: x_ref.at[i], lambda i: states.at[i], x_sem, slots)
    w_copies = start_copies(
        lambda i: w_ref.at[pl.ds(i * depth, depth), :],
        lambda i: weights.at[i],
        w_sem,
        width // depth,
    )
    head_pos = place_ref[4]
    lane = lax.broadcasted_iota(jnp.int32, (1, tokens), 1)
    for slot in range(slots):
        order = jnp.full((1, tokens), -1, jnp.int32)
        start = jnp.int32(0)
        for hyp in range(hyps):
            length = length_ref[slot, hyp]
            inside = (lane >= hyp * positions) & (lane < hyp * positions + length)
            order = jnp.where(inside, lane - hyp * positions + start, order)
            start = start + length
        row = lax.broadcasted_iota(jnp.int32, (tokens, tokens), 0)
        move = jnp.where(order == row, 1.0, 0.0).astype(jnp.bfloat16)
        x_copies[slot].wait()
        ordered = dot(move, states[slot])
        normed[slot * tokens : (slot + 1) * tokens, :] = square_norm(ordered).astype(jnp.bfloat16)
        share_row = lax.broadcasted_iota(jnp.int32, (share, tokens), 0)
        chosen = order == share_row * (tokens // share) + head_pos
        mine = dot(jnp.where(chosen, 1.0, 0.0).astype(jnp.bfloat16), states[slot])
        shares[slot, :share, :] = mine.astype(jnp.bfloat16)
        target = jnp.sum(
            jnp.where(chosen, tok_ref[slot], 0), axis=1, keepdims=True, dtype=jnp.int32
        )
        coarse = target // 256
        cell = lax.broadcasted_iota(jnp.int32, (share, columns), 1)
        packed = jnp.where(cell == 0, coarse, jnp.where(cell == 1, target - coarse * 256, 0))
        shares[slot, share:, :columns] = packed.astype(jnp.float32).astype(jnp.bfloat16)
    for number in range(width // depth):
        w_copies[number].wait()
        product = dot(normed[:, number * depth : (number + 1) * depth], weights[number])
        if number == 0:
            total[...] = product
        else:
            total[...] += product
    group = place_ref[1]
    for distance in range(count):
        slot = jnp.int32(-1)
        for candidate in range(slots):
            holds = slot_ref[group * slots + candidate] == group ^ distance
            slot = jnp.where(holds, candidate, slot)
        out = outs[distance]

        @pl.when(slot < 0)
        def _(out=out):
            out[...] = jnp.zeros_like(out)

        @pl.when(slot >= 0)
        def _(out=out, slot=slot):
            start = pl.multiple_of(slot * tokens, tokens)
            out[:tokens, :] = total[pl.ds(start, tokens), :].astype(jnp.bfloat16)
            for part in range(parts):
                first = tokens + part * share
                out[first : first + share, :] = shares[
                    slot, :share, part * columns : (part + 1) * columns
                ]
            out[tokens + parts * share :, :] = shares[slot, share:, :columns]


def queries_of(place, slot_utt, lengths, after, states, targets, weights, count, share):
    slots, tokens, width = states.shape
    columns = weights.shape[1]
    depth = 1024
    rows = tokens + (width // columns + 1) * share
    block = jax.ShapeDtypeStruct((rows, columns), jnp.bfloat16)
    return pl.pallas_call(
        functools.partial(query_kernel, count, depth),
        in_specs=[SCALARS] * 3 + [ANYWHERE, ANYWHERE, INSIDE, ANYWHERE],
        out_specs=[INSIDE] * count,
        out_shape=[block] * count,
        scratch_shapes=[
            pltpu.VMEM(states.shape, jnp.bfloat16),
            pltpu.VMEM((width // depth, depth, columns), jnp.bfloat16),
            pltpu.VMEM((slots * tokens, width), jnp.bfloat16),
            pltpu.VMEM((slots * tokens, columns), jnp.float32),
            pltpu.VMEM((slots, 2 * share, width), jnp.bfloat16),
            pltpu.SemaphoreType.DMA((slots,)),
            pltpu.SemaphoreType.DMA((width // depth,)),
        ],
        cost_estimate=pl.CostEstimate(
            flops=2 * slots * tokens * width * columns,
            bytes_accessed=2 * width * (columns + slots * tokens),
            transcendentals=0,
        ),
        compiler_params=pltpu.CompilerParams(vmem_limit_bytes=32 << 20),
        name="hypothesis_queries",
    )(place, slot_utt, lengths, after, in_hbm(states), targets, in_hbm(weights))


def kv_kernel(sections, utterances, widths, *refs):
    parts, (own_ref, w_ref, out_ref) = refs[:-3], refs[-3:]
    rows = own_ref.shape[0]
    frames = rows // utterances
    total = own_ref[...].astype(jnp.float32)
    summed = parts[0][...].astype(jnp.float32)
    for part in parts[1:]:
        summed += part[...].astype(jnp.float32)
    states = layer_norm(total + summed).astype(jnp.bfloat16)
    to = lax.broadcasted_iota(jnp.int32, (rows, rows), 0)
    come = lax.broadcasted_iota(jnp.int32, (rows, rows), 1)
    move = jnp.where(come == to % frames * utterances + to // frames, 1.0, 0.0)
    states = dot(move.astype(jnp.bfloat16), states).astype(jnp.bfloat16)
    both = dot(states, w_ref[...])
    half = KVH * HD
    per_kv = sections * widths // KVH
    for section in range(sections):
        for utterance in range(utterances):
            for width in range(0, widths, per_kv):
                kv_head = (section * widths + width) // per_kv
                take = slice(utterance * frames, (utterance + 1) * frames)
                block = jnp.concatenate(
                    [
                        both[take, kv_head * HD : (kv_head + 1) * HD],
                        both[take, half + kv_head * HD : half + (kv_head + 1) * HD],
                    ],
                    axis=1,
                )
                start = ((section * utterances + utterance) * widths + width) * frames
                block = jnp.concatenate([block] * per_kv, axis=0).astype(jnp.bfloat16)
                out_ref[start : start + per_kv * frames, :] = block


def keys_values_of(parts, own, weights, sections, utterances, widths):
    rows = sections * widths * own.shape[0]
    return pl.pallas_call(
        functools.partial(kv_kernel, sections, utterances, widths),
        in_specs=[INSIDE] * (len(parts) + 2),
        out_specs=INSIDE,
        out_shape=jax.ShapeDtypeStruct((rows, 2 * HD), jnp.bfloat16),
        cost_estimate=pl.CostEstimate(
            flops=2 * own.shape[0] * weights.shape[0] * weights.shape[1],
            bytes_accessed=2 * weights.shape[0] * weights.shape[1],
            transcendentals=0,
        ),
        compiler_params=pltpu.CompilerParams(vmem_limit_bytes=24 << 20),
        name="frame_keys_values",
    )(*parts, own, weights)


def choice_of_payload(place_ref, slot_ref, slots):
    group = place_ref[1]
    source = jnp.int32(0)
    for slot in range(slot_ref.shape[0]):
        source = jnp.where(slot_ref[slot] == group, slot // slots, source)
    return jnp.minimum(source ^ group, 2)


def attention_kernel(count, slots, capacity, pieces, sections, widths, tile, *refs):
    place_ref, slot_ref, frame_ref = refs[:3]
    payloads, (kv_ref, w_ref) = refs[3 : 3 + count], refs[3 + count : 5 + count]
    outs = refs[5 + count : 5 + count + 2 * len(pieces)]
    weights, picked, context, w_sem = refs[5 + count + 2 * len(pieces) :]
    tokens, columns = capacity, w_ref.shape[0]
    tiles = w_ref.shape[1] // tile
    w_copies = start_copies(
        lambda i: w_ref.at[:, pl.ds(i * tile, tile)], lambda i: weights.at[i], w_sem, tiles
    )
    source = choice_of_payload(place_ref, slot_ref, slots)
    section_pos = place_ref[0]
    frame_limit = frame_ref[place_ref[1]]
    for distance in range(count):

        @pl.when(source == distance)
        def _(payload=payloads[distance]):
            picked[...] = payload[:tokens, :]

    keys = kv_ref[:, :HD]
    values = kv_ref[:, HD:]
    frames = kv_ref.shape[0]
    visible = lax.broadcasted_iota(jnp.int32, (tokens, frames), 1) < frame_limit
    for head in range(columns // HD):
        scores = dot_nt(picked[:, head * HD : (head + 1) * HD], keys) * (1.0 / math.sqrt(HD))
        scores = jnp.where(visible, scores, -jnp.inf)
        raised = jnp.exp(scores - jnp.max(scores, axis=1, keepdims=True))
        chances = (raised / jnp.sum(raised, axis=1, keepdims=True)).astype(jnp.bfloat16)
        context[:, head * HD : (head + 1) * HD] = dot(chances, values).astype(jnp.bfloat16)
    to = lax.broadcasted_iota(jnp.int32, (tokens, tokens), 0)
    come = lax.broadcasted_iota(jnp.int32, (tokens, tokens), 1)
    low_bit = place_ref[2] % 2
    size = widths * pieces[0]
    block = to % size // pieces[0]
    section = jnp.where(to < size, 1 - section_pos, section_pos)
    first_order = (to % pieces[0] * sections + section) * widths + block % 2 * 2 + block // 2
    at = to - 2 * size
    size = widths * pieces[1]
    block = at % size // pieces[1]
    low = jnp.where(at < size, 1 - low_bit, low_bit)
    row = pieces[0] + at % pieces[1]
    second_order = (row * sections + block // 2) * widths + block % 2 * 2 + low
    move = come == jnp.where(at < 0, first_order, second_order)
    ordered = dot(jnp.where(move, 1.0, 0.0).astype(jnp.bfloat16), context[...])
    ordered = ordered.astype(jnp.bfloat16)
    for number in range(tiles):
        w_copies[number].wait()
        product = dot(ordered, weights[number]).astype(jnp.bfloat16)
        first = 0
        for out in outs:
            out[:, number * tile : (number + 1) * tile] = product[first : first + out.shape[0], :]
            first += out.shape[0]


def attend(place, slot_utt, frame_len, payloads, keys_values, weights, pieces, sections, widths, slots):
    count = len(payloads)
    columns, width = weights.shape
    capacity = sum(pieces) * sections * widths
    tile = 1024
    tiles = width // tile
    shapes = [
        jax.ShapeDtypeStruct((piece * widths, width), jnp.bfloat16)
        for piece in pieces
        for _ in range(2)
    ]
    return pl.pallas_call(
        functools.partial(
            attention_kernel, count, slots, capacity, pieces, sections, widths, tile
        ),
        in_specs=[SCALARS] * 3 + [INSIDE] * (count + 1) + [ANYWHERE],
        out_specs=[INSIDE] * len(shapes),
        out_shape=shapes,
        scratch_shapes=[
            pltpu.VMEM((tiles, columns, tile), jnp.bfloat16),
            pltpu.VMEM((capacity, columns), jnp.bfloat16),
            pltpu.VMEM((capacity, columns), jnp.bfloat16),
            pltpu.SemaphoreType.DMA((tiles,)),
        ],
        cost_estimate=pl.CostEstimate(
            flops=2 * capacity * columns * (width + 2 * keys_values.shape[0]),
            bytes_accessed=2 * columns * width + 2 * capacity * width,
            transcendentals=capacity * keys_values.shape[0] * columns // HD,
        ),
        compiler_params=pltpu.CompilerParams(vmem_limit_bytes=24 << 20),
        name="attention_projection",
    )(place, slot_utt, frame_len, *payloads, keys_values, in_hbm(weights))


def fold_kernel(sides, joined, place_ref, *refs):
    count = len(sides)
    parts, outs = refs[: 2 * count], refs[2 * count :]
    first = 0
    for number, side in enumerate(sides):
        kept_ref, came_ref = parts[2 * number : 2 * number + 2]
        total = kept_ref[...].astype(jnp.float32) + came_ref[...].astype(jnp.float32)
        half = total.shape[0] // 2
        top, bottom = total[:half], total[half:]
        upper = side(place_ref) == 0
        kept = jnp.where(upper, top, bottom)
        sent = jnp.where(upper, bottom, top).astype(jnp.bfloat16)
        if joined:
            outs[0][first : first + half, :] = kept
            outs[1][first : first + half, :] = sent
            first += half
        else:
            outs[2 * number][...] = kept
            outs[2 * number + 1][...] = sent


def fold(place, parts, sides, joined):
    width = parts[0].shape[1]
    halves = [part.shape[0] // 2 for part in parts[::2]]
    if joined:
        halves = [sum(halves)]
    shapes = [
        jax.ShapeDtypeStruct((half, width), kind)
        for half in halves
        for kind in (jnp.float32, jnp.bfloat16)
    ]
    return pl.pallas_call(
        functools.partial(fold_kernel, sides, joined),
        in_specs=[SCALARS] + [INSIDE] * len(parts),
        out_specs=[INSIDE] * len(shapes),
        out_shape=shapes,
        compiler_params=pltpu.CompilerParams(vmem_limit_bytes=24 << 20),
        name="sum_phase",
    )(place, *parts)


def section_side(place_ref):
    return place_ref[0]


def low_side(place_ref):
    return place_ref[2] % 2


def high_side(place_ref):
    return place_ref[2] // 2


def norm_kernel(count, slots, tokens, place_ref, slot_ref, *refs):
    payloads, (kept, other) = refs[:count], refs[count : count + 2]
    out_ref, picked, total = refs[count + 2 :]
    rows, width = total.shape
    columns = picked.shape[1]
    share = picked.shape[0] // (width // columns + 1)
    source = choice_of_payload(place_ref, slot_ref, slots)
    for choice in range(count):

        @pl.when(source == choice)
        def _(payload=payloads[choice]):
            picked[...] = payload[tokens:, :]

    total[...] = kept[...] + other[...].astype(jnp.float32)
    for part in range(width // columns):
        take = slice(part * columns, (part + 1) * columns)
        total[:, take] += picked[part * share : part * share + rows, :].astype(jnp.float32)
    shape = out_ref.shape[:2]
    normed = square_norm(total[...]).reshape(*shape, width)
    out_ref[:, :, :width] = normed.astype(jnp.bfloat16)
    last = width // columns * share
    target = picked[last : last + rows, :LANES].astype(jnp.float32).reshape(*shape, LANES)
    out_ref[:, :, width:] = target.astype(jnp.bfloat16)


def normed_rows(place, slot_utt, payloads, blocks, tokens, slots):
    width = blocks[0].shape[1]
    rows = blocks[0].shape[0]
    columns = payloads[0].shape[1]
    return pl.pallas_call(
        functools.partial(norm_kernel, len(payloads), slots, tokens),
        in_specs=[SCALARS] * 2 + [INSIDE] * (len(payloads) + len(blocks)),
        out_specs=INSIDE,
        out_shape=jax.ShapeDtypeStruct((rows // FOLD, FOLD, width + LANES), jnp.bfloat16),
        scratch_shapes=[
            pltpu.VMEM((payloads[0].shape[0] - tokens, columns), jnp.bfloat16),
            pltpu.VMEM((rows, width), jnp.float32),
        ],
        compiler_params=pltpu.CompilerParams(vmem_limit_bytes=16 << 20),
        name="token_rows",
    )(place, slot_utt, *payloads, *blocks)


def vocabulary_kernel(tile, count, first_ref, after_ref, *refs):
    sets, (head_ref, out_ref, rows_ref, stat) = refs[:count], refs[count:]
    vocab_rows, width = head_ref.shape
    share = sets[0].shape[0] * FOLD
    tokens = share * len(sets)
    cell = lax.broadcasted_iota(jnp.int32, (8, LANES), 1)
    take = jnp.where(cell == 0, 256.0, jnp.where(cell == 1, 1.0, 0.0)).astype(jnp.bfloat16)
    for number, rows in enumerate(sets):
        flat = rows[...].astype(jnp.float32).reshape(share, width + LANES)
        rows_ref[number * share : (number + 1) * share, :] = flat.astype(jnp.bfloat16)
    target = dot_nt(take, rows_ref[:, width:])[0:1, :].astype(jnp.int32) - first_ref[3]
    stat[0:1, :] = jnp.full((1, tokens), -jnp.inf, jnp.float32)
    stat[8:9, :] = jnp.zeros((1, tokens), jnp.float32)
    stat[16:17, :] = jnp.zeros((1, tokens), jnp.float32)

    for start in range(0, vocab_rows, tile):
        logits = dot_nt(head_ref[start : start + tile, :], rows_ref[:, :width])
        vocab = lax.broadcasted_iota(jnp.int32, logits.shape, 0) + start
        before = stat[0:1, :]
        upper = jnp.maximum(before, jnp.max(logits, axis=0, keepdims=True))
        stat[8:9, :] = stat[8:9, :] * jnp.exp(before - upper) + jnp.sum(
            jnp.exp(logits - upper), axis=0, keepdims=True
        )
        stat[16:17, :] += jnp.sum(jnp.where(vocab == target, logits, 0.0), axis=0, keepdims=True)
        stat[0:1, :] = upper

    for number in range(len(sets)):
        for row in range(3):
            out_ref[number, row : row + 1, :] = stat[
                8 * row : 8 * row + 1, number * share : (number + 1) * share
            ]


def vocabulary_stats(place, after, sets, head):
    share = sets[0].shape[0] * FOLD
    count = len(sets)
    width = head.shape[1]
    tokens = share * count
    return pl.pallas_call(
        functools.partial(vocabulary_kernel, head.shape[0], count),
        in_specs=[SCALARS, ANYWHERE] + [INSIDE] * (count + 1),
        out_specs=INSIDE,
        out_shape=jax.ShapeDtypeStruct((count, 8, share), jnp.float32),
        scratch_shapes=[
            pltpu.VMEM((tokens, width + LANES), jnp.bfloat16),
            pltpu.VMEM((24, tokens), jnp.float32),
        ],
        cost_estimate=pl.CostEstimate(
            flops=3 * tokens * head.shape[0] * width,
            bytes_accessed=2 * tokens * width,
            transcendentals=tokens * head.shape[0],
        ),
        compiler_params=pltpu.CompilerParams(vmem_limit_bytes=16 << 20),
        name="vocabulary_scores",
    )(place, after, *sets, pltpu.with_memory_space_constraint(head, pltpu.VMEM))


def zero_kernel(after_ref, head_ref, out_ref):
    out_ref[...] = jnp.zeros_like(out_ref)


def head_in_vmem(after, head):
    return pl.pallas_call(
        zero_kernel,
        in_specs=[ANYWHERE, INSIDE],
        out_specs=INSIDE,
        out_shape=jax.ShapeDtypeStruct((8, LANES), jnp.float32),
        compiler_params=pltpu.CompilerParams(vmem_limit_bytes=16 << 20),
        name="vocabulary_rows",
    )(after, pltpu.with_memory_space_constraint(head, pltpu.VMEM))


def spread_kernel(order, sections, groups, widths, place_ref, slot_ref, *refs):
    stats, (out_ref, table, block) = refs[:-3], refs[-3:]
    share = table.shape[2]
    for stat, places in zip(stats, order):
        for number, at in enumerate(places):
            table[at] = stat[number]
    slots = slot_ref.shape[0] // groups
    block[...] = jnp.zeros_like(block)
    for group in range(groups):
        for slot in range(slots):
            utterance = jnp.maximum(slot_ref[group * slots + slot], 0)
            for section in range(sections):
                at = (section ^ place_ref[0]) * groups + (utterance ^ place_ref[1])
                block[group, 3 * slot : 3 * slot + 3, section * share : (section + 1) * share] = (
                    table[at][0:3, :]
                )
    for section in range(sections):
        for group in range(groups):
            for width in range(widths):
                out_ref[(section * groups + group) * widths + width] = block[group]


def spread_stats(place, slot_utt, stats, order, sections, groups, widths):
    share = stats[0].shape[2]
    assert 3 * slot_utt.shape[0] // groups <= 8
    return pl.pallas_call(
        functools.partial(spread_kernel, order, sections, groups, widths),
        in_specs=[SCALARS] * 2 + [INSIDE] * len(stats),
        out_specs=INSIDE,
        out_shape=jax.ShapeDtypeStruct(
            (sections * groups * widths, 8, sections * share), jnp.float32
        ),
        scratch_shapes=[
            pltpu.VMEM((sections * groups, 8, share), jnp.float32),
            pltpu.VMEM((groups, 8, sections * share), jnp.float32),
        ],
        compiler_params=pltpu.CompilerParams(vmem_limit_bytes=16 << 20),
        name="statistics_by_group",
    )(place, slot_utt, *stats)


def score_kernel(sections, widths, place_ref, slot_ref, length_ref, every_ref, out_ref):
    slots, hyps = out_ref.shape
    lanes = every_ref.shape[2]
    share = lanes // sections // widths
    lane = lax.broadcasted_iota(jnp.int32, (1, lanes), 1)
    order = lane % share * (sections * widths) + lane // share
    column = lax.broadcasted_iota(jnp.int32, (1, hyps), 1)
    for slot in range(slots):
        upper = every_ref[:, 3 * slot, :]
        peak = jnp.max(upper, axis=0, keepdims=True)
        total = jnp.sum(
            every_ref[:, 3 * slot + 1, :] * jnp.exp(upper - peak), axis=0, keepdims=True
        )
        picked = jnp.sum(every_ref[:, 3 * slot + 2, :], axis=0, keepdims=True)
        logp = picked - (peak + jnp.log(total))
        scores = jnp.zeros((1, hyps), jnp.float32)
        start = jnp.int32(0)
        for hyp in range(hyps):
            length = length_ref[slot, hyp]
            valid = (order >= start) & (order < start + length)
            summed = jnp.sum(jnp.where(valid, logp, 0.0), axis=1, keepdims=True)
            mean = summed / jnp.full((1, 1), length, jnp.int32).astype(jnp.float32)
            scores = jnp.where(column == hyp, mean + math.log(V), scores)
            start = start + length
        filled = slot_ref[place_ref[1] * slots + slot] >= 0
        out_ref[slot : slot + 1, :] = jnp.where(filled, scores, 0.0)


def hypothesis_scores(place, slot_utt, lengths, every, slots, hyps, sections, widths):
    return pl.pallas_call(
        functools.partial(score_kernel, sections, widths),
        in_specs=[SCALARS] * 3 + [INSIDE],
        out_specs=INSIDE,
        out_shape=pltpu.HBM((slots, hyps), jnp.float32),
        compiler_params=pltpu.CompilerParams(vmem_limit_bytes=16 << 20),
        name="hypothesis_scores",
    )(place, slot_utt, lengths, every)


def rest(pieces, slot_tokens, place, slot_utt, frame_len, hyp_len, payloads, keys_values, o_proj, head):
    section_count = lax.axis_size("section")
    group_count = lax.axis_size("tm")
    width_count = lax.axis_size("mp")
    section_pos = lax.axis_index("section")
    width_pos = lax.axis_index("mp")
    slot_count, hyp_count = hyp_len.shape
    projected = attend(
        place,
        slot_utt,
        frame_len,
        payloads,
        keys_values,
        o_proj,
        pieces,
        section_count,
        width_count,
        slot_count,
    )

    kept, sent, other_kept, other_sent = fold(
        place,
        [projected[1], swap(projected[0], "section", 1), projected[3], swap(projected[2], "mp", 1)],
        [low_side, section_side],
        False,
    )
    kept, sent = fold(
        place,
        [kept, swap(sent, "mp", 1), other_kept, swap(other_sent, "section", 1)],
        [high_side, high_side],
        True,
    )
    out_rows = normed_rows(
        place, slot_utt, payloads, [kept, swap(sent, "mp", 2)], slot_tokens, slot_count
    )

    own = jnp.zeros((width_count, *out_rows.shape), jnp.bfloat16)
    for distance in range(width_count):
        block = swap(out_rows, "mp", distance) if distance else out_rows
        own = lax.dynamic_update_index_in_dim(own, block, width_pos ^ distance, 0)
    own = own.reshape(-1, *out_rows.shape[1:])
    half = own.shape[0] // 2
    by_x = swap(own, "section", 1)
    by_y = swap(own, "tm", 2)
    beside = swap(own, "tm", 1)
    by_x, by_y, zeros = lax.optimization_barrier((by_x, by_y, head_in_vmem(beside, head)))
    across = [swap(by_x[:half], "tm", 2), swap(by_y[half:], "section", 1)]
    near = vocabulary_stats(
        place, zeros, [by_y, swap(by_y, "tm", 1), by_x, swap(by_x, "tm", 1)], head
    )
    *across, near = lax.optimization_barrier((*across, near))
    across = jnp.concatenate(across)
    far = vocabulary_stats(place, zeros, [across, swap(across, "tm", 1), own, beside], head)
    stats = [near, far]
    order = ((2, 3, 4, 5), (6, 7, 0, 1))

    every = exchange(
        spread_stats(place, slot_utt, stats, order, section_count, group_count, width_count), ALL
    )
    return hypothesis_scores(
        place, slot_utt, hyp_len, every, slot_count, hyp_count, section_count, width_count
    )


def near_device(
    frame_len,
    slot_utt,
    enc_in,
    ffn_up,
    ffn_down,
    kv_proj,
    hyp_state,
    hyp_tok,
    hyp_len,
    q_proj,
    o_proj,
    head,
):
    section_count = lax.axis_size("section")
    group_count = lax.axis_size("tm")
    width_count = lax.axis_size("mp")
    section_pos = lax.axis_index("section")
    group_pos = lax.axis_index("tm")
    width_pos = lax.axis_index("mp")
    head_devices = section_count * width_count
    all_devices = head_devices * group_count

    frame_rows, utterances, enc_width = enc_in.shape
    slot_count, hyp_count, positions, model_width = hyp_state.shape
    slot_tokens = hyp_count * positions
    share_rows = slot_tokens // head_devices
    vocab_start = (
        (section_pos * group_count + group_pos) * width_count + width_pos
    ) * head.shape[0]
    head_pos = section_pos * width_count + width_pos
    place = jnp.stack([section_pos, group_pos, width_pos, vocab_start, head_pos])
    place = place.astype(jnp.int32)

    *parts, own_frames = ffn(place, enc_in, ffn_up, ffn_down, width_count)
    parts = [parts[0]] + [
        swap(parts[distance], "mp", distance) for distance in range(1, width_count)
    ]
    own_frames, lengths = lax.optimization_barrier((own_frames, hyp_len))

    blocks = queries_of(
        place,
        slot_utt,
        lengths,
        place,
        hyp_state.reshape(slot_count, slot_tokens, model_width),
        hyp_tok.reshape(slot_count, 1, slot_tokens),
        q_proj,
        group_count,
        share_rows,
    )
    crossing = blocks[2] + swap(blocks[3], "tm", 1)
    payloads = [blocks[0], swap(blocks[1], "tm", 1), swap(crossing, "tm", 2)]

    here_slots = lax.dynamic_slice_in_dim(slot_utt, group_pos * slot_count, slot_count, 0)
    filled = jnp.where(here_slots >= 0, jnp.sum(hyp_len, axis=1), 0)
    count = jnp.max(filled).reshape(1)
    most = count
    for distance in range(1, group_count):
        most = jnp.maximum(most, swap(count, "tm", distance))
    own_frames, most = lax.optimization_barrier((own_frames, most))
    sent = keys_values_of(parts, own_frames, kv_proj, section_count, utterances, width_count)
    frames_all = all_devices * (frame_rows // width_count)
    keys_values = exchange(sent.reshape(all_devices, -1, 2 * HD), ALL).reshape(frames_all, 2 * HD)

    operands = (place, slot_utt, frame_len, hyp_len, payloads, keys_values, o_proj, head)
    few = share_rows * 3 // 4
    return lax.cond(
        most[0] <= few * head_devices,
        functools.partial(rest, (few // 2, few - few // 2), slot_tokens),
        functools.partial(rest, (share_rows // 2, share_rows - share_rows // 2), slot_tokens),
        *operands,
    )


def general(
    frame_len,
    slot_utt,
    enc_in,
    ffn_up,
    ffn_down,
    kv_proj,
    hyp_state,
    hyp_tok,
    hyp_len,
    q_proj,
    o_proj,
    head,
):
    section_count = lax.axis_size("section")
    group_count = lax.axis_size("tm")
    width_count = lax.axis_size("mp")
    section_pos = lax.axis_index("section")
    group_pos = lax.axis_index("tm")
    width_pos = lax.axis_index("mp")
    head_devices = section_count * width_count
    head_pos = section_pos * width_count + width_pos
    all_devices = head_devices * group_count

    frame_rows, utterances, enc_width = enc_in.shape
    assert utterances == group_count
    slot_count, hyp_count, positions, model_width = hyp_state.shape
    slot_tokens = hyp_count * positions
    device_heads = q_proj.shape[1] // HD
    group_heads = NH // KVH
    frame_share = frame_rows // width_count
    share_rows = slot_tokens // head_devices
    here_slots = lax.dynamic_slice_in_dim(slot_utt, group_pos * slot_count, slot_count, 0)

    dec_rows = hyp_state.reshape(slot_count * slot_tokens, model_width).astype(jnp.float32)
    queries = jnp.dot(
        square_norm(dec_rows).astype(jnp.bfloat16), q_proj, preferred_element_type=jnp.float32
    ).astype(jnp.bfloat16)
    queries = queries.reshape(slot_count, slot_tokens, device_heads * HD)
    shares = lax.dynamic_slice_in_dim(
        hyp_state.reshape(slot_count, slot_tokens, model_width), head_pos * share_rows, share_rows, 1
    )

    def by_utterance(values):
        out = []
        for utterance in range(utterances):
            block = values[0]
            for slot in range(1, slot_count):
                block = jnp.where(here_slots[slot] == utterance, values[slot], block)
            out.append(block)
        return jnp.stack(out)

    own_slot = jnp.argmax(slot_utt == group_pos)
    from_group = own_slot // slot_count
    queries = lax.dynamic_index_in_dim(
        exchange(by_utterance(queries), "tm"), from_group, 0, keepdims=False
    )
    resid_rows = lax.dynamic_index_in_dim(
        exchange(by_utterance(shares), "tm"), from_group, 0, keepdims=False
    )
    slot_targets = lax.all_gather(
        hyp_tok.reshape(slot_count, slot_tokens), "tm", axis=0, tiled=True
    )
    utt_slots = jnp.argmax(slot_utt[None, :] == jnp.arange(utterances)[:, None], axis=1)
    targets = jnp.take(slot_targets, utt_slots, axis=0).reshape(utterances * slot_tokens)

    enc_flat = (
        enc_in.reshape(width_count, frame_share, utterances, enc_width)
        .transpose(0, 2, 1, 3)
        .reshape(frame_rows * utterances, enc_width)
    )
    share_count = frame_share * utterances
    enc_normed = layer_norm(enc_flat.astype(jnp.float32)).astype(jnp.bfloat16)
    enc_inner = jax.nn.gelu(
        jnp.dot(enc_normed, ffn_up, preferred_element_type=jnp.float32), approximate=False
    ).astype(jnp.bfloat16)
    enc_summed = scatter_sum(
        jnp.dot(enc_inner, ffn_down, preferred_element_type=jnp.float32).astype(jnp.bfloat16),
        "mp",
        width_count,
    )
    own_frames = lax.dynamic_slice_in_dim(enc_flat, width_pos * share_count, share_count, 0)
    enc_states = layer_norm(own_frames.astype(jnp.float32) + enc_summed).astype(jnp.bfloat16)
    keys_values = jnp.dot(enc_states, kv_proj, preferred_element_type=jnp.float32).astype(
        jnp.bfloat16
    )
    keys_values = keys_values.reshape(utterances, frame_share, 2, KVH, HD)
    sent = []
    for section in range(section_count):
        per_width = []
        for width in range(width_count):
            kv_head = (section * width_count + width) * device_heads // group_heads
            per_width.append(
                keys_values[:, :, :, kv_head].reshape(utterances, frame_share, 2 * HD)
            )
        sent.append(jnp.stack(per_width, axis=1))
    sent = jnp.stack(sent).reshape(all_devices, frame_share, 2 * HD)
    frames_all = all_devices * frame_share
    keys_values = exchange(sent, ALL).reshape(frames_all, 2 * HD)

    frame_limit = lax.dynamic_index_in_dim(frame_len, group_pos, 0, keepdims=False)
    queries = queries.reshape(slot_tokens, device_heads, HD)
    scores = jnp.einsum(
        "qhd,fd->hqf", queries, keys_values[:, :HD], preferred_element_type=jnp.float32
    ) / math.sqrt(HD)
    visible = jnp.arange(frames_all, dtype=jnp.int32) < frame_limit
    scores = jnp.where(visible[None, None, :], scores, -jnp.inf)
    weights = jax.nn.softmax(scores, axis=-1).astype(jnp.bfloat16)
    context = jnp.einsum(
        "hqf,fd->qhd", weights, keys_values[:, HD:], preferred_element_type=jnp.float32
    ).astype(jnp.bfloat16)
    partial = jnp.dot(
        context.reshape(slot_tokens, device_heads * HD), o_proj, preferred_element_type=jnp.float32
    ).astype(jnp.bfloat16)
    partial = scatter_sum(partial, "section", section_count).astype(jnp.bfloat16)
    attn_out = scatter_sum(partial, "mp", width_count)
    out_normed = square_norm(resid_rows.astype(jnp.float32) + attn_out).astype(jnp.bfloat16)

    hidden_rows = lax.all_gather(out_normed, ALL, axis=0, tiled=True)
    logits = lax.dot_general(
        hidden_rows, head, (((1,), (1,)), ((), ())), preferred_element_type=jnp.float32
    )
    vocab_rows = head.shape[0]
    vocab_start = (
        (section_pos * group_count + group_pos) * width_count + width_pos
    ) * vocab_rows
    target_rows = (
        targets.reshape(utterances, section_count, width_count, share_rows)
        .transpose(1, 0, 2, 3)
        .reshape(-1)
    )
    upper = jnp.max(logits, axis=1)
    totals = jnp.sum(jnp.exp(logits - upper[:, None]), axis=1)
    matches = (
        jnp.arange(vocab_rows, dtype=jnp.int32)[None, :] == (target_rows - vocab_start)[:, None]
    )
    target_logit = jnp.sum(jnp.where(matches, logits, 0.0), axis=1)

    stats = jnp.stack([upper, totals, target_logit])
    stats = stats.reshape(3, section_count, utterances, width_count, share_rows)
    stats = stats.transpose(2, 0, 1, 3, 4).reshape(utterances, 3, slot_tokens)
    by_slot = jnp.take(stats, jnp.maximum(slot_utt, 0), axis=0)
    by_group = by_slot.reshape(1, group_count, 1, slot_count, 3, slot_tokens)
    by_group = jnp.broadcast_to(
        by_group, (section_count, group_count, width_count, slot_count, 3, slot_tokens)
    ).reshape(all_devices, slot_count, 3, slot_tokens)
    every = exchange(by_group, ALL)
    peak = jnp.max(every[:, :, 0], axis=0)
    total = jnp.sum(every[:, :, 1] * jnp.exp(every[:, :, 0] - peak[None]), axis=0)
    picked = jnp.sum(every[:, :, 2], axis=0)
    token_logp = (picked - (peak + jnp.log(total))).reshape(slot_count, hyp_count, positions)
    valid = jnp.arange(positions, dtype=jnp.int32)[None, None, :] < hyp_len[:, :, None]
    summed = jnp.sum(jnp.where(valid, token_logp, 0.0), axis=-1) / hyp_len.astype(
        jnp.float32
    ) + math.log(V)
    return jnp.where(here_slots[:, None] >= 0, summed, 0.0)


def solution(mesh):
    in_specs = (
        P(),
        P(),
        P(("section", "tm"), None, None),
        P(None, "mp"),
        P("mp", None),
        P(),
        P("tm", None, None, None),
        P("tm", None, None),
        P("tm", None),
        P(None, ("section", "mp")),
        P(("section", "mp"), None),
        P(("section", "tm", "mp"), None),
    )
    out_specs = P("tm", None)
    near = dict(mesh.shape) == {"section": 2, "tm": 4, "mp": 4}
    per_device = near_device if near else general
    return jax.shard_map(
        per_device, mesh=mesh, in_specs=in_specs, out_specs=out_specs, check_vma=False
    )
```
